32 devices in a mesh: path: 2 (over core), frames: 16 (over z, y, x).
Axes of the slice: x: 2, y: 2, z: 4, core: 2. Of those that a mesh axis runs over, the one named last changes fastest.
Arguments:
- slow_input: bfloat16 [512, 14, 14, 1024], P(('path', 'frames'))
- fast_input: bfloat16 [2048, 14, 14, 128], P(('path', 'frames'))
- clip_offset: int32 [512], P(('path', 'frames')), may hold values from 0 to 256, as said below
- fill: int32 [512], P(('path', 'frames')), may hold values from 0 to 1, as said below
- w_fast_in: bfloat16 [128, 32], replicated, may hold values from -0.5 to 0.5
- w_fast_mid: bfloat16 [3, 32, 32], replicated, may hold values from -0.625 to 0.625
- w_fast_out: bfloat16 [32, 128], replicated, may hold values from -1 to 1
- w_lateral: bfloat16 [5, 128, 256], replicated, may hold values from -0.25 to 0.25
- w_slow_in: bfloat16 [1280, 256], replicated, may hold values from -0.15625 to 0.15625
- w_slow_mid: bfloat16 [3, 3, 256, 256], replicated, may hold values from -0.125 to 0.125
- w_slow_out: bfloat16 [256, 1024], replicated, may hold values from -0.375 to 0.375
- w_shortcut: bfloat16 [1280, 1024], replicated, may hold values from -0.15625 to 0.15625
- gains: float32 [3008], replicated, may hold values from 0.25 to 1.75
- biases: float32 [3008], replicated, may hold values from -3 to 3
- slow_cot: bfloat16 [512, 14, 14, 1024], P(('path', 'frames')), may hold values from -6 to 6
- fast_cot: bfloat16 [2048, 14, 14, 128], P(('path', 'frames')), may hold values from -6 to 6
Outputs:
- slow_output: bfloat16 [512, 14, 14, 1024], P(('path', 'frames'))
- fast_output: bfloat16 [2048, 14, 14, 128], P(('path', 'frames'))
- slow_input_grad: bfloat16 [512, 14, 14, 1024], P(('path', 'frames'))
- fast_input_grad: bfloat16 [2048, 14, 14, 128], P(('path', 'frames'))
- w_fast_in_grad: float32 [128, 32], replicated
- w_fast_mid_grad: float32 [3, 32, 32], replicated
- w_fast_out_grad: float32 [32, 128], replicated
- w_lateral_grad: float32 [5, 128, 256], replicated
- w_slow_in_grad: float32 [1280, 256], replicated
- w_slow_mid_grad: float32 [3, 3, 256, 256], replicated
- w_slow_out_grad: float32 [256, 1024], replicated
- w_shortcut_grad: float32 [1280, 1024], replicated
- gains_grad: float32 [3008], replicated
- biases_grad: float32 [3008], replicated
The draws below stay inside these ranges and needn't reach their ends.
Inputs may be any that keep to these rules, and one draw needn't show every extreme that they name: clip_offset[t] is t minus the first slow frame of t's clip; it is 0 exactly where a clip begins, always at t = 0 and never at a t > 0 with t % 16 == 0; the first clip holds the slow frames 0 to 256 and the next begins right after it. fill[0] = 1.
All inputs are finite; a program needn't handle non-finite values.
Results may differ from the reference program's by a relative error of at most 0.0075.
The reference program's roundings to bfloat16 on the way count: a program that leaves them out, or rounds other values in their place, can miss the bound.
Values may be sent and summed in bfloat16 or wider, within the bound.
A program may use at most 320 MiB of HBM per device.

```python
import jax
import jax.numpy as jnp
from jax import lax

C_SLOW = 1024
C_FAST = 128
IN_SLOW = 256
IN_FAST = 32
C_LAT = 256
SIDE = 14
FRAMES_DEV = 16
SLOW_FRAMES = 512
FAST_FRAMES = 2048
C_CAT = 1280
NORMS = 3008


def activation_field(key, frames, channels, ramp_top, mean_spread):
    key_scale, key_mean, key_normal = jax.random.split(key, 3)
    channel_scale = jnp.exp(jax.random.uniform(key_scale, (channels,), jnp.float32, jnp.log(0.4), jnp.log(2.5)))
    channel_mean = jax.random.uniform(key_mean, (channels,), jnp.float32, -mean_spread, mean_spread)
    normal_part = jnp.clip(jax.random.normal(key_normal, (frames, SIDE, SIDE, channels), jnp.float32), -4.0, 4.0)
    noise_part = normal_part
    position = jnp.arange(frames, dtype=jnp.float32) / (frames - 1)
    frame_scale = ramp_top ** position
    return (noise_part + channel_mean) * channel_scale * frame_scale[:, None, None, None]


def draw_slow_input(key, part):
    key = jax.random.fold_in(key, 3)
    field = activation_field(key, SLOW_FRAMES, C_SLOW, 3.0, 0.5)
    return (0.2 * field).astype(jnp.bfloat16)


def draw_fast_input(key, part):
    key = jax.random.fold_in(key, 4)
    field = activation_field(key, FAST_FRAMES, C_FAST, 3.0, 0.5)
    return field.astype(jnp.bfloat16)


def draw_clip_offset(key, part):
    key = jax.random.fold_in(key, 11)
    position = jnp.arange(SLOW_FRAMES, dtype=jnp.int32)
    first_end = SLOW_FRAMES // 2 + 1
    lottery = jax.random.randint(key, (SLOW_FRAMES,), 0, 8)
    free_begin = (lottery == 0) & (position % FRAMES_DEV != 0) & (position > first_end)
    begins = free_begin | (position == 0) | (position == first_end)
    latest = lax.cummax(jnp.where(begins, position, 0), axis=0)
    return (position - latest).astype(jnp.int32)


def draw_fill(key, part):
    key = jax.random.fold_in(key, 12)
    position = jnp.arange(SLOW_FRAMES, dtype=jnp.int32)
    lottery = jax.random.randint(key, (SLOW_FRAMES,), 0, 8)
    filled = (lottery != 0) | (position == 0)
    return filled.astype(jnp.int32)


def steps_of(key, shape, pieces, smallest, high):
    def one(dim, blocks):
        draws = jax.random.uniform(jax.random.fold_in(jax.random.fold_in(key, 6), dim), (blocks,), jnp.float32, smallest / len(pieces), high / len(pieces))
        return jnp.repeat(jnp.exp(draws), shape[dim] // blocks).reshape((-1,) + (1,) * (len(shape) - dim - 1))

    loudness = one(*pieces[0])
    for cut in pieces[1:]:
        loudness = loudness * one(*cut)
    return loudness


def centred(rng, dims, scale, reach, cuts=(), kind=jnp.bfloat16):
    gain = steps_of(rng, dims, cuts, -0.22, 0.18) if cuts else 1.0
    entries = jax.random.normal(rng, dims, jnp.float32) * scale * gain
    return jnp.minimum(jnp.maximum(entries, -reach), reach).astype(kind)


def setup_inputs(seed: int = 0) -> dict:
    streams_of = jax.random.split(jax.random.key(seed), 17)
    slow_input = draw_slow_input(jax.random.fold_in(streams_of[16], 71), 0)
    fast_input = draw_fast_input(jax.random.fold_in(streams_of[16], 71), 0)
    clip_offset = draw_clip_offset(jax.random.fold_in(streams_of[16], 71), 0)
    fill = draw_fill(jax.random.fold_in(streams_of[16], 71), 0)
    w_fast_in = centred(streams_of[4], (C_FAST, IN_FAST), C_FAST ** -0.5, 0.5)
    w_fast_mid = centred(streams_of[5], (3, IN_FAST, IN_FAST), (3 * IN_FAST) ** -0.5, 0.625)
    w_fast_out = centred(streams_of[6], (IN_FAST, C_FAST), IN_FAST ** -0.5, 1.0)
    w_lateral = centred(streams_of[7], (5, C_FAST, C_LAT), (5 * C_FAST) ** -0.5, 0.25)
    w_slow_in = centred(streams_of[8], (C_CAT, IN_SLOW), C_CAT ** -0.5, 0.15625)
    w_slow_mid = centred(streams_of[9], (3, 3, IN_SLOW, IN_SLOW), (9 * IN_SLOW) ** -0.5, 0.125)
    w_slow_out = centred(streams_of[10], (IN_SLOW, C_SLOW), IN_SLOW ** -0.5, 0.375)
    w_shortcut = centred(streams_of[11], (C_CAT, C_SLOW), C_CAT ** -0.5, 0.15625)
    gains = jnp.clip(1.0 + 0.15 * jax.random.normal(streams_of[12], (NORMS,), jnp.float32), 0.25, 1.75)
    biases = centred(streams_of[13], (NORMS,), 0.5, 3.0, (), jnp.float32)
    slow_cot = centred(streams_of[14], (SLOW_FRAMES, SIDE, SIDE, C_SLOW), 1.0, 6.0, ((0, 32),))
    fast_cot = centred(streams_of[15], (FAST_FRAMES, SIDE, SIDE, C_FAST), 1.0, 6.0, ((0, 32),))
    return {"slow_input": slow_input, "fast_input": fast_input, "clip_offset": clip_offset, "fill": fill, "w_fast_in": w_fast_in, "w_fast_mid": w_fast_mid, "w_fast_out": w_fast_out, "w_lateral": w_lateral, "w_slow_in": w_slow_in, "w_slow_mid": w_slow_mid, "w_slow_out": w_slow_out, "w_shortcut": w_shortcut, "gains": gains, "biases": biases, "slow_cot": slow_cot, "fast_cot": fast_cot}


norm_eps = 1e-05

@jax.custom_vjp
def low(v):
    return lax.optimization_barrier(v.astype(jnp.bfloat16)).astype(jnp.float32)

@jax.custom_vjp
def low_back(v):
    return v

def low_keep(v):
    return (low(v), None)

def low_pass(kept, grad):
    return (grad,)

def back_keep(v):
    return (v, None)

def back_low(kept, grad):
    return (low(grad),)
low.defvjp(low_keep, low_pass)
low_back.defvjp(back_keep, back_low)

def project(inputs, matrix):
    return jnp.einsum('fpc,cd->fpd', inputs, matrix, precision=lax.Precision.HIGHEST)

def forward(slow_x, fast_x, w_fast_in, w_fast_mid, w_fast_out, w_lateral, w_slow_in, w_slow_mid, w_slow_out, w_shortcut, gains, biases, clip_offset, fill):
    frames = slow_x.shape[0]
    grid_side = slow_x.shape[1]
    pixels = grid_side * grid_side
    c_slow = slow_x.shape[3]
    fast_frames = fast_x.shape[0]
    c_fast = fast_x.shape[3]
    in_fast = w_fast_in.shape[1]
    in_slow = w_slow_in.shape[1]
    c_lat = w_lateral.shape[2]
    widths = [in_fast, in_fast, c_fast, c_lat, in_slow, in_slow, c_slow, c_slow]
    bounds = [0]
    for seg_width in widths:
        bounds.append(bounds[-1] + seg_width)
    fill_value = fill.astype(jnp.float32)
    slow_weight = fill_value[:, None, None]
    fast_weight = jnp.repeat(fill_value, 4)[:, None, None]
    slow_count = jnp.sum(fill_value) * pixels
    fast_count = 4.0 * slow_count

    def normalize(inputs, segment, weight, total_count):
        average = lax.optimization_barrier(jnp.sum(inputs * weight, axis=(0, 1))) / total_count
        centered = inputs - average
        spread = lax.optimization_barrier(jnp.sum(centered * centered * weight, axis=(0, 1))) / total_count
        gain_part = gains[bounds[segment]:bounds[segment + 1]]
        bias_part = biases[bounds[segment]:bounds[segment + 1]]
        return centered * lax.rsqrt(spread + norm_eps) * gain_part + bias_part
    within = (clip_offset >= 1).astype(jnp.float32)
    quarter = jnp.arange(4)
    prev_link = jnp.where(quarter[None, :] > 0, 1.0, within[:, None]).reshape(fast_frames)
    next_link = jnp.concatenate([prev_link[1:], jnp.zeros((1,), jnp.float32)])
    fast_rows = fast_x.reshape(fast_frames, pixels, c_fast)
    fa_conv = low_back(project(fast_rows, w_fast_in))
    fa_act = low(jax.nn.silu(normalize(fa_conv, 0, fast_weight, fast_count)))
    zero_frame = jnp.zeros_like(fa_act[:1])
    before_tap = jnp.concatenate([zero_frame, fa_act[:-1]], axis=0) * prev_link[:, None, None]
    after_tap = jnp.concatenate([fa_act[1:], zero_frame], axis=0) * next_link[:, None, None]
    fb_conv = low_back(project(before_tap, w_fast_mid[0]) + project(fa_act, w_fast_mid[1]) + project(after_tap, w_fast_mid[2]))
    fb_act = low(jax.nn.silu(normalize(fb_conv, 1, fast_weight, fast_count)))
    fc_conv = low_back(project(fb_act, w_fast_out))
    fast_out = jax.nn.silu(normalize(fc_conv, 2, fast_weight, fast_count) + fast_rows) * fast_weight
    groups = fast_rows.reshape(frames, 4, pixels, c_fast)
    earlier = jnp.concatenate([jnp.zeros_like(groups[:1]), groups[:-1]], axis=0)[:, 2:4] * within[:, None, None, None]
    lat_conv = project(earlier[:, 0], w_lateral[0]) + project(earlier[:, 1], w_lateral[1])
    lat_conv = lat_conv + project(groups[:, 0], w_lateral[2]) + project(groups[:, 1], w_lateral[3]) + project(groups[:, 2], w_lateral[4])
    lat_conv = low_back(lat_conv)
    lat_act = low(jax.nn.silu(normalize(lat_conv, 3, slow_weight, slow_count)))
    joined = jnp.concatenate([slow_x.reshape(frames, pixels, c_slow), lat_act], axis=2)
    sa_conv = low_back(project(joined, w_slow_in))
    sa_act = low(jax.nn.silu(normalize(sa_conv, 4, slow_weight, slow_count)))
    padded_grid = jnp.pad(sa_act.reshape(frames, grid_side, grid_side, in_slow), ((0, 0), (1, 1), (1, 1), (0, 0)))
    sb_conv = jnp.zeros((frames, grid_side, grid_side, in_slow), jnp.float32)
    for row_step in range(3):
        for col_step in range(3):
            window = padded_grid[:, row_step:row_step + grid_side, col_step:col_step + grid_side]
            sb_conv = sb_conv + jnp.einsum('fhwc,cd->fhwd', window, w_slow_mid[row_step, col_step], precision=lax.Precision.HIGHEST)
    sb_conv = low_back(sb_conv.reshape(frames, pixels, in_slow))
    sb_act = low(jax.nn.silu(normalize(sb_conv, 5, slow_weight, slow_count)))
    sc_conv = low_back(project(sb_act, w_slow_out))
    sp_conv = low_back(project(joined, w_shortcut))
    slow_pre = normalize(sc_conv, 6, slow_weight, slow_count) + normalize(sp_conv, 7, slow_weight, slow_count)
    slow_out = jax.nn.silu(slow_pre) * slow_weight
    return (slow_out.reshape(slow_x.shape), fast_out.reshape(fast_x.shape))

def reference(slow_input, fast_input, clip_offset, fill, w_fast_in, w_fast_mid, w_fast_out, w_lateral, w_slow_in, w_slow_mid, w_slow_out, w_shortcut, gains, biases, slow_cot, fast_cot):
    floats = (slow_input.astype(jnp.float32), fast_input.astype(jnp.float32), w_fast_in.astype(jnp.float32), w_fast_mid.astype(jnp.float32), w_fast_out.astype(jnp.float32), w_lateral.astype(jnp.float32), w_slow_in.astype(jnp.float32), w_slow_mid.astype(jnp.float32), w_slow_out.astype(jnp.float32), w_shortcut.astype(jnp.float32), gains.astype(jnp.float32), biases.astype(jnp.float32))

    def forward_all(slow_x, fast_x, wa, wb, wc, wd, we, wf, wg, wh, gain_all, bias_all):
        return forward(slow_x, fast_x, wa, wb, wc, wd, we, wf, wg, wh, gain_all, bias_all, clip_offset, fill)
    outputs, pullback = jax.vjp(forward_all, *floats)
    gradients = pullback((slow_cot.astype(jnp.float32), fast_cot.astype(jnp.float32)))
    return (outputs[0].astype(jnp.bfloat16), outputs[1].astype(jnp.bfloat16), gradients[0].astype(jnp.bfloat16), gradients[1].astype(jnp.bfloat16), gradients[2], gradients[3], gradients[4], gradients[5], gradients[6], gradients[7], gradients[8], gradients[9], gradients[10], gradients[11])
```

```python
import functools

import jax
import jax.numpy as jnp
from jax import lax
from jax.experimental import pallas as pl
from jax.experimental.pallas import tpu as pltpu
from jax.sharding import PartitionSpec as P

norm_eps = 1e-05
F32 = jnp.float32
BF16 = jnp.bfloat16
MESH = pl.DeviceIdType.MESH
AXES = ("path", "frames")
STEPS = 7
LANES = 128
VMEM_LIMIT = 56 * 1024 * 1024


def dot(a, b):
    return jnp.dot(a, b, preferred_element_type=F32)


def dot_nt(a, b):
    return lax.dot_general(a, b, (((1,), (1,)), ((), ())), preferred_element_type=F32)


def dot_tn(a, b):
    return lax.dot_general(a, b, (((0,), (0,)), ((), ())), preferred_element_type=F32)


def sig(v):
    return 0.5 * jnp.tanh(0.5 * v) + 0.5


def slope(v):
    s = sig(v)
    return s + (v * s) * (1.0 - s)


def rows(ref, slab, first, count):
    parts = [ref[slab, first + j : first + j + 1, :] for j in range(count)]
    return parts[0] if count == 1 else jnp.concatenate(parts, axis=1)


def put_rows(ref, first, value):
    for j in range(value.shape[1] // LANES):
        ref[first + j : first + j + 1, :] = value[:, j * LANES : (j + 1) * LANES]


def zero_ref(ref):
    ref[...] = jnp.zeros(ref.shape, ref.dtype)


def spread_add(step, z, mean_ref, m2_ref, cols=slice(None)):
    count = z.shape[0]
    mean = jnp.sum(z, axis=0) * (1.0 / count)
    d = z - mean
    m2 = jnp.sum(d * d, axis=0)
    first = step == 0
    old_mean = jnp.where(first, 0.0, mean_ref[:, cols])
    old_m2 = jnp.where(first, 0.0, m2_ref[:, cols])
    done = jnp.full((1, z.shape[-1]), step, jnp.int32).astype(F32)
    share = 1.0 / (done + 1.0)
    delta = mean - old_mean
    mean_ref[:, cols] = old_mean + delta * share
    m2_ref[:, cols] = old_m2 + m2 + delta * delta * (done * share * count)


def spread_end(mean_ref, m2_ref, fill, positions):
    filled = jnp.sum(fill, axis=0, keepdims=True)
    mean = jnp.sum(fill * mean_ref[...], axis=0, keepdims=True) / jnp.maximum(filled, 1.0)
    d = mean_ref[...] - mean
    m2 = jnp.sum(fill * (m2_ref[...] + positions * (d * d)), axis=0, keepdims=True)
    return mean, m2


def sum_add(step, value, ref, cols=slice(None)):
    ref[:, cols] = jnp.where(step == 0, 0.0, ref[:, cols]) + jnp.sum(value, axis=0)


def sum_end(ref):
    return jnp.sum(ref[...], axis=0, keepdims=True)


def pad8(n):
    return -(-n // 8) * 8


def exchange_kernel(cfg, *refs):
    fwd, bwd, n_coefs, has_up, has_down = cfg
    nf = sum(c[2] for c in fwd)
    nb = max((c[6] + c[4] for c in bwd), default=0)
    nn = sum(c[4] for c in bwd)
    n_row = 2 * nf + nb
    it = iter(refs)
    stats_ref, gb_ref = next(it), next(it)
    coef_refs = [next(it) for _ in range(n_coefs)]
    up_ref = next(it) if has_up else None
    down_ref = next(it) if has_down else None
    coef_out = next(it) if nf else None
    pq_out = next(it) if nb else None
    from_prev = next(it) if has_up else None
    from_next = next(it) if has_down else None
    slots1, slots2, mid, tot, send1, recv1, send2, recv2 = (next(it) for _ in range(8))
    if has_up:
        up_land, up_sems = next(it), next(it)
    if has_down:
        down_land, down_sems = next(it), next(it)

    paths, length = lax.axis_size("path"), lax.axis_size("frames")
    near = 4
    g1, g2 = paths * near, length // near
    me_p, me_f = lax.axis_index("path"), lax.axis_index("frames")
    me = me_p * length + me_f
    total = paths * length
    r1 = me_p * near + lax.rem(me_f, near)
    r2 = lax.div(me_f, near)

    def peer1(k):
        r = lax.rem(r1 + k, g1)
        return (lax.div(r, near), r2 * near + lax.rem(r, near))

    def peer2(k):
        r = lax.rem(r2 + k, g2)
        return (me_p, r * near + lax.rem(me_f, near))

    def split(index):
        return (lax.div(index, length), lax.rem(index, length))

    nxt, prv = split(lax.rem(me + 1, total)), split(lax.rem(me + total - 1, total))

    barrier = pltpu.get_barrier_semaphore()
    greeted = 0
    for k in range(1, g1):
        pl.semaphore_signal(barrier, inc=1, device_id=peer1(k), device_id_type=MESH)
        greeted += 1
    for k in range(1, g2):
        pl.semaphore_signal(barrier, inc=1, device_id=peer2(k), device_id_type=MESH)
        greeted += 1
    if has_up or has_down:
        pl.semaphore_signal(barrier, inc=1, device_id=nxt, device_id_type=MESH)
        pl.semaphore_signal(barrier, inc=1, device_id=prv, device_id_type=MESH)
        greeted += 2
    pl.semaphore_wait(barrier, greeted)

    halos = []
    copies = []
    for k in range(1, g1):
        copies.append(
            pltpu.make_async_remote_copy(
                src_ref=stats_ref,
                dst_ref=slots1.at[r1],
                send_sem=send1.at[k],
                recv_sem=recv1.at[k],
                device_id=peer1(k),
                device_id_type=MESH,
            )
        )
        copies[-1].start()
    if has_up:
        halos.append(
            pltpu.make_async_remote_copy(
                src_ref=up_ref,
                dst_ref=up_land,
                send_sem=up_sems.at[0],
                recv_sem=up_sems.at[1],
                device_id=nxt,
                device_id_type=MESH,
            )
        )
        halos[-1].start()
    if has_down:
        halos.append(
            pltpu.make_async_remote_copy(
                src_ref=down_ref,
                dst_ref=down_land,
                send_sem=down_sems.at[0],
                recv_sem=down_sems.at[1],
                device_id=prv,
                device_id_type=MESH,
            )
        )
        halos[-1].start()
    slots1[r1] = stats_ref[...]
    for c in copies:
        c.wait_recv()

    def combine(slots, count, out):
        if nf:
            n = slots[0, n_row : n_row + 1, :]
            for g in range(1, count):
                n = n + slots[g, n_row : n_row + 1, :]
            acc = slots[0, n_row : n_row + 1, :] * slots[0, 0:nf, :]
            for g in range(1, count):
                acc = acc + slots[g, n_row : n_row + 1, :] * slots[g, 0:nf, :]
            mean = acc / jnp.maximum(n, 1.0)
            m2 = None
            for g in range(count):
                d = slots[g, 0:nf, :] - mean
                part = slots[g, nf : 2 * nf, :] + slots[g, n_row : n_row + 1, :] * (d * d)
                m2 = part if m2 is None else m2 + part
            out[0:nf, :] = mean
            out[nf : 2 * nf, :] = m2
            out[n_row : n_row + 1, :] = n
        if nb:
            acc = slots[0, 2 * nf : n_row, :]
            for g in range(1, count):
                acc = acc + slots[g, 2 * nf : n_row, :]
            out[2 * nf : n_row, :] = acc

    zero_ref(mid)
    combine(slots1, g1, mid)
    copies2 = []
    for k in range(1, g2):
        copies2.append(
            pltpu.make_async_remote_copy(
                src_ref=mid,
                dst_ref=slots2.at[r2],
                send_sem=send2.at[k],
                recv_sem=recv2.at[k],
                device_id=peer2(k),
                device_id_type=MESH,
            )
        )
        copies2[-1].start()
    slots2[r2] = mid[...]
    for c in copies2:
        c.wait_recv()
    combine(slots2, g2, tot)

    def lanes4(v):
        w = v + pltpu.roll(v, 64, 1)
        return w + pltpu.roll(w, 32, 1)

    at = 0
    for kind, g_row, count in fwd:
        n = tot[n_row : n_row + 1, :]
        mean = tot[at : at + count, :]
        m2 = tot[nf + at : nf + at + count, :]
        if kind == "lane4":
            whole = lanes4(mean) * 0.25
            d = mean - whole
            var = lanes4(m2 + n * (d * d)) / (4.0 * n)
            mean = whole
        elif kind == "row4":
            whole = jnp.sum(mean, axis=0, keepdims=True) * 0.25
            d = mean - whole
            var = jnp.sum(m2 + n * (d * d), axis=0, keepdims=True) / (4.0 * n)
            var = jnp.broadcast_to(var, (count, LANES))
            mean = jnp.broadcast_to(whole, (count, LANES))
        else:
            var = m2 / n
        inv = lax.rsqrt(var + norm_eps)
        scale = inv * gb_ref[0, g_row : g_row + count, :]
        coef_out[0, at : at + count, :] = scale
        coef_out[1, at : at + count, :] = gb_ref[1, g_row : g_row + count, :] - mean * scale
        coef_out[2, at : at + count, :] = inv
        coef_out[3, at : at + count, :] = mean * inv
        coef_out[4, at : at + count, :] = jnp.broadcast_to(n, (count, LANES))
        at += count
    at = 0
    for kind, coef, row, _, count, db_at, dg_at in bwd:
        db = tot[2 * nf + db_at : 2 * nf + db_at + count, :]
        dg = tot[2 * nf + dg_at : 2 * nf + dg_at + count, :]
        c = coef_refs[coef]
        scale, inv = c[0, row : row + count, :], c[2, row : row + count, :]
        mi, n = c[3, row : row + count, :], c[4, row : row + count, :]
        if kind == "lane4":
            db, dg, n = lanes4(db), lanes4(dg), 4.0 * n
        elif kind == "row4":
            db = jnp.broadcast_to(jnp.sum(db, axis=0, keepdims=True), (count, LANES))
            dg = jnp.broadcast_to(jnp.sum(dg, axis=0, keepdims=True), (count, LANES))
            n = 4.0 * n
        pq_out[0, at : at + count, :] = scale / n * (db - mi * dg)
        pq_out[1, at : at + count, :] = scale / n * inv * dg
        pq_out[2, at : at + count, :] = db
        pq_out[3, at : at + count, :] = dg
        at += count

    for c in halos:
        c.wait()
    if has_up:
        from_prev[...] = up_land[...]
    if has_down:
        from_next[...] = down_land[...]
    for c in copies:
        c.wait_send()
    for c in copies2:
        c.wait_send()


def exchange(mesh_sizes, cid, stats, gb, fwd=(), bwd=(), coefs=(), up=None, down=None):
    paths, length = mesh_sizes
    g1, g2 = paths * 4, length // 4
    nf = sum(c[2] for c in fwd)
    nn = sum(c[4] for c in bwd)
    r = stats.shape[0]
    vm = pl.BlockSpec(memory_space=pltpu.VMEM)
    operands = [stats, gb, *coefs]
    outs = []
    if nf:
        outs.append(jax.ShapeDtypeStruct((5, nf, LANES), F32))
    if nn:
        outs.append(jax.ShapeDtypeStruct((4, nn, LANES), F32))
    scratch = [
        pltpu.VMEM((g1, r, LANES), F32),
        pltpu.VMEM((g2, r, LANES), F32),
        pltpu.VMEM((r, LANES), F32),
        pltpu.VMEM((r, LANES), F32),
        pltpu.SemaphoreType.DMA((g1,)),
        pltpu.SemaphoreType.DMA((g1,)),
        pltpu.SemaphoreType.DMA((g2,)),
        pltpu.SemaphoreType.DMA((g2,)),
    ]
    for halo in (up, down):
        if halo is not None:
            operands.append(halo)
            outs.append(jax.ShapeDtypeStruct(halo.shape, halo.dtype))
            scratch += [pltpu.VMEM(halo.shape, halo.dtype), pltpu.SemaphoreType.DMA((2,))]
    cfg = (fwd, bwd, len(coefs), up is not None, down is not None)
    return pl.pallas_call(
        functools.partial(exchange_kernel, cfg),
        out_shape=outs,
        in_specs=[vm] * len(operands),
        out_specs=[vm] * len(outs),
        scratch_shapes=scratch,
        compiler_params=pltpu.CompilerParams(collective_id=cid, has_side_effects=True),
        name=f"exchange_{cid}",
    )(*operands)


def call(kernel, ins, outs, scratch=(), name=None):
    return pl.pallas_call(
        kernel,
        grid=(STEPS,),
        in_specs=[pl.BlockSpec(b, m) for _, b, m in ins],
        out_specs=[pl.BlockSpec(b, m) for _, _, b, m in outs],
        out_shape=[jax.ShapeDtypeStruct(s, d) for s, d, _, _ in outs],
        scratch_shapes=list(scratch),
        compiler_params=pltpu.CompilerParams(
            dimension_semantics=("arbitrary",), vmem_limit_bytes=VMEM_LIMIT
        ),
        name=name,
    )(*[a for a, _, _ in ins])


def whole(array):
    zeros = (0,) * array.ndim
    return (array, array.shape, lambda i: zeros)


def blocked(array, axis, size):
    block = array.shape[:axis] + (size,) + array.shape[axis + 1 :]
    return (array, block, lambda i: tuple(i if d == axis else 0 for d in range(array.ndim)))


def out_whole(shape, dtype):
    zeros = (0,) * len(shape)
    return (shape, dtype, shape, lambda i: zeros)


def out_blocked(shape, dtype, axis, size):
    block = shape[:axis] + (size,) + shape[axis + 1 :]
    return (shape, dtype, block, lambda i: tuple(i if d == axis else 0 for d in range(len(shape))))


def flat(value):
    return value.reshape(-1, value.shape[-1])


def spread_rows(ref, index, count, height):
    return [jnp.broadcast_to(ref[(*index, slice(p, p + 1))], (height, ref.shape[-1])) for p in range(count)]


def k_first(x_ref, tail_ref, m16_ref, m64_ref, wfa_ref, wlat_ref,
            fa_ref, lat_ref, taps_ref, st_ref, up_ref, down_ref, xs, fm, fv, lm, lv):
    i = pl.program_id(0)
    x = x_ref[...]
    s_n, p_n, f_n, _ = x.shape
    packed = jnp.concatenate([flat(x[s]) for s in range(s_n)], axis=1)
    fa = dot(packed, wfa_ref[...])
    fa_ref[...] = fa.reshape(fa_ref.shape)
    zero_ref(up_ref)
    zero_ref(down_ref)
    for p in range(p_n):
        down_ref[0, p : p + 1, :] = fa[p * f_n : p * f_n + 1, :]
        up_ref[0, p : p + 1, :] = fa[p * f_n + f_n - 1 : p * f_n + f_n, :]
    spread_add(i, fa.reshape(p_n, f_n, LANES), fm, fv)

    xs[...] = flat(x).astype(F32)
    n = xs.shape[0] // 4
    quarter = [xs[pl.ds(k, n, stride=4), :] for k in range(4)]
    t_n = f_n // 4
    first = lax.broadcasted_iota(jnp.int32, (n // t_n, t_n, LANES), 1) == 0
    link = m16_ref[1:2]
    taps = []
    for k in range(2):
        halo = jnp.concatenate(
            [
                jnp.broadcast_to(tail_ref[0, s, p : p + 1, k * LANES : (k + 1) * LANES], (t_n, LANES))
                for s in range(s_n)
                for p in range(p_n)
            ],
            axis=0,
        )
        moved = pltpu.roll(quarter[2 + k], 1, 0).reshape(n // t_n, t_n, LANES)
        taps.append(flat(jnp.where(first, halo.reshape(moved.shape), moved) * link))
    taps = jnp.concatenate([*taps, *quarter[:3]], axis=1).astype(BF16)
    taps_ref[...] = taps.reshape(taps_ref.shape)
    lat = dot(taps, wlat_ref[...])
    lat_ref[...] = lat.reshape(lat_ref.shape)
    spread_add(i, lat.reshape(n // t_n, t_n, lat.shape[1]), lm, lv)

    @pl.when(i == STEPS - 1)
    def _():
        zero_ref(st_ref)
        fill = m16_ref[0, :, 0:1]
        mean, m2 = spread_end(fm, fv, m64_ref[0, :, 0:1], STEPS * p_n)
        put_rows(st_ref, 0, mean)
        put_rows(st_ref, 3, m2)
        mean, m2 = spread_end(lm, lv, fill, STEPS * p_n * s_n)
        put_rows(st_ref, 1, mean)
        put_rows(st_ref, 4, m2)
        put_rows(st_ref, 6, count_row(m16_ref, STEPS * p_n * s_n))


def count_row(m16_ref, positions):
    return jnp.sum(m16_ref[0], axis=0, keepdims=True) * float(positions)


def shifted(value, first_rows, last_rows, f_n):
    n = value.shape[0]
    shape = (n // f_n, f_n, value.shape[1])
    place = lax.broadcasted_iota(jnp.int32, shape, 1)
    before = jnp.where(place == 0, first_rows, pltpu.roll(value, 1, 0).reshape(shape))
    after = jnp.where(place == f_n - 1, last_rows, pltpu.roll(value, n - 1, 0).reshape(shape))
    return before, after


def k_join(x_ref, lat_ref, fa_ref, hp_ref, hn_ref, c1_ref, m16_ref, m64_ref, wj_ref, wmid_ref,
           lact_ref, ftap_ref, sa_ref, sp_ref, fb_ref, st_ref, am, av, pm, pv, bm, bv):
    i = pl.program_id(0)
    s_n, p_n, t_n, c_slow = x_ref.shape
    c_lat = lat_ref.shape[-1]
    v = flat(lat_ref[...]) * rows(c1_ref, 0, 1, 2) + rows(c1_ref, 1, 1, 2)
    lact = (v * sig(v)).astype(BF16)
    lact_ref[...] = lact.reshape(lact_ref.shape)
    joined = jnp.concatenate([flat(x_ref[...]), lact], axis=1)
    wide = c_lat
    for n in range(wj_ref.shape[1] // wide):
        z = dot(joined, wj_ref[:, n * wide : (n + 1) * wide])
        z4 = z.reshape(s_n, p_n, t_n, wide)
        z3 = z.reshape(s_n * p_n, t_n, wide)
        if n == 0:
            sa_ref[...] = z4
            spread_add(i, z3, am, av)
        else:
            cols = slice((n - 1) * wide, n * wide)
            sp_ref[:, :, :, cols] = z4
            spread_add(i, z3, pm, pv, cols)

    f_n = fa_ref.shape[1]
    scale, shift = rows(c1_ref, 0, 0, 1), rows(c1_ref, 1, 0, 1)

    def act(z):
        w = z * scale + shift
        return (w * sig(w)).astype(BF16).astype(F32)

    fact = act(flat(fa_ref[...]))
    ends = []
    for ref in (hp_ref, hn_ref):
        small = act(ref[0])
        ends.append(
            jnp.concatenate(
                [jnp.broadcast_to(small[p : p + 1, :], (f_n, LANES)) for p in range(p_n)], axis=0
            ).reshape(p_n, f_n, LANES)
        )
    before, after = shifted(fact, ends[0], ends[1], f_n)
    ftap = jnp.concatenate(
        [flat(before * m64_ref[1:2]), fact, flat(after * m64_ref[2:3])], axis=1
    ).astype(BF16)
    ftap_ref[...] = ftap.reshape(ftap_ref.shape)
    fb = dot(ftap, wmid_ref[...])
    fb_ref[...] = fb.reshape(fb_ref.shape)
    spread_add(i, fb.reshape(p_n, f_n, LANES), bm, bv)

    @pl.when(i == STEPS - 1)
    def _():
        zero_ref(st_ref)
        fill = m16_ref[0, :, 0:1]
        positions = STEPS * p_n * s_n
        mean, m2 = spread_end(bm, bv, m64_ref[0, :, 0:1], STEPS * p_n)
        put_rows(st_ref, 0, mean)
        put_rows(st_ref, 11, m2)
        mean, m2 = spread_end(am, av, fill, positions)
        put_rows(st_ref, 1, mean)
        put_rows(st_ref, 12, m2)
        mean, m2 = spread_end(pm, pv, fill, positions)
        put_rows(st_ref, 3, mean)
        put_rows(st_ref, 14, m2)
        put_rows(st_ref, 22, count_row(m16_ref, positions))


def k_spatial(sa_ref, fb_ref, c2_ref, m16_ref, m64_ref, wsp_ref, wout_ref,
              pad_ref, sb_ref, fact_ref, st_ref, sm, sv, cm, cv):
    i = pl.program_id(0)
    h_n, w_n, t_n, c = sa_ref.shape

    @pl.when(i == 0)
    def _():
        scale, shift = rows(c2_ref, 0, 1, 2), rows(c2_ref, 1, 1, 2)
        zero_ref(pad_ref)

        @pl.loop(0, h_n)
        def _(h):
            v = flat(sa_ref[h]) * scale + shift
            pad_ref[h + 1, 1 : w_n + 1] = (v * sig(v)).astype(BF16).reshape(w_n, t_n, c)

    per = h_n // STEPS
    h0 = i * per
    acc = None
    for a in range(3):
        for b in range(3):
            k = 3 * a + b
            part = dot(flat(pad_ref[pl.ds(h0 + a, per), b : b + w_n].reshape(per * w_n, t_n, c)), wsp_ref[k])
            acc = part if acc is None else acc + part
    sb_ref[...] = acc.reshape(sb_ref.shape)
    spread_add(i, acc.reshape(per * w_n, t_n, acc.shape[1]), sm, sv)

    p_n, f_n, _ = fb_ref.shape
    v = flat(fb_ref[...]) * rows(c2_ref, 0, 0, 1) + rows(c2_ref, 1, 0, 1)
    fact = (v * sig(v)).astype(BF16)
    fact_ref[...] = fact.reshape(fact_ref.shape)
    fc = dot(fact, wout_ref[...])
    spread_add(i, fc.reshape(p_n, f_n, fc.shape[1]), cm, cv)

    @pl.when(i == STEPS - 1)
    def _():
        zero_ref(st_ref)
        mean, m2 = spread_end(cm, cv, m64_ref[0, :, 0:1], STEPS * p_n)
        put_rows(st_ref, 0, mean)
        put_rows(st_ref, 6, m2)
        mean, m2 = spread_end(sm, sv, m16_ref[0, :, 0:1], h_n * w_n)
        put_rows(st_ref, 4, mean)
        put_rows(st_ref, 10, m2)
        put_rows(st_ref, 12, count_row(m16_ref, h_n * w_n))


def k_expand(sb_ref, fact_ref, x_ref, cot_ref, c3_ref, m16_ref, m64_ref, wso_ref, wout_ref,
             sact_ref, fout_ref, df_ref, st_ref, cm, cv, s1, s2):
    i = pl.program_id(0)
    s_n, p_n, t_n, c = sb_ref.shape
    v = flat(sb_ref[...]) * rows(c3_ref, 0, 4, 2) + rows(c3_ref, 1, 4, 2)
    sact = (v * sig(v)).astype(BF16)
    sact_ref[...] = sact.reshape(sact_ref.shape)
    wide = 256
    for n in range(wso_ref.shape[1] // wide):
        cols = slice(n * wide, (n + 1) * wide)
        z = dot(sact, wso_ref[:, cols])
        spread_add(i, z.reshape(s_n * p_n, t_n, wide), cm, cv, cols)

    f_n = fact_ref.shape[1]
    fc = dot(flat(fact_ref[...]), wout_ref[...])
    fill = m64_ref[0:1]
    for s in range(s_n):
        cols = slice(s * LANES, (s + 1) * LANES)
        z = fc[:, cols].reshape(p_n, f_n, LANES)
        unit = z * rows(c3_ref, 2, s, 1) - rows(c3_ref, 3, s, 1)
        pre = z * rows(c3_ref, 0, s, 1) + rows(c3_ref, 1, s, 1) + x_ref[s].astype(F32)
        g = sig(pre)
        y = pre * g
        fout_ref[s] = (y * fill).astype(BF16)
        d = cot_ref[s].astype(F32) * fill * (g + y * (1.0 - g))
        df_ref[:, :, cols] = d
        sum_add(i, d, s1, cols)
        sum_add(i, d * unit, s2, cols)

    @pl.when(i == STEPS - 1)
    def _():
        zero_ref(st_ref)
        positions = STEPS * p_n * s_n
        mean, m2 = spread_end(cm, cv, m16_ref[0, :, 0:1], positions)
        put_rows(st_ref, 0, mean)
        put_rows(st_ref, 8, m2)
        put_rows(st_ref, 16, sum_end(s1))
        put_rows(st_ref, 20, sum_end(s2))
        put_rows(st_ref, 24, count_row(m16_ref, positions))


def back_norm(scale, p, q, dy, z, fill):
    return scale * dy - fill * (p + z * q)


def k_out(sact_ref, sp_ref, cot_ref, df_ref, fact_ref, fb_ref, c2_ref, c3_ref, c4_ref, q4_ref,
          m16_ref, m64_ref, wso_ref, wout_ref,
          out_ref, dy_ref, dfb_ref, gout_ref, up_ref, down_ref, st_ref, s1, s2, s3, t1, t2):
    i = pl.program_id(0)
    s_n, p_n, t_n, _ = sact_ref.shape
    sact = flat(sact_ref[...])
    fill = m16_ref[0:1, :, 0:1]
    wide = 256
    for n in range(wso_ref.shape[1] // wide):
        cols = slice(n * wide, (n + 1) * wide)
        shape = (s_n * p_n, t_n, wide)
        sc = dot(sact, wso_ref[:, cols]).reshape(shape)
        sp = sp_ref[:, :, :, cols].reshape(shape)
        u6 = sc * rows(c4_ref, 2, 2 * n, 2) - rows(c4_ref, 3, 2 * n, 2)
        u7 = sp * rows(c2_ref, 2, 3 + 2 * n, 2) - rows(c2_ref, 3, 3 + 2 * n, 2)
        pre = (
            sc * rows(c4_ref, 0, 2 * n, 2)
            + sp * rows(c2_ref, 0, 3 + 2 * n, 2)
            + (rows(c4_ref, 1, 2 * n, 2) + rows(c2_ref, 1, 3 + 2 * n, 2))
        )
        g = sig(pre)
        y = pre * g
        out_ref[:, :, :, cols] = (y * fill).astype(BF16).reshape(s_n, p_n, t_n, wide)
        d = cot_ref[:, :, :, cols].reshape(shape).astype(F32) * fill * (g + y * (1.0 - g))
        dy_ref[:, :, :, cols] = d.reshape(s_n, p_n, t_n, wide)
        sum_add(i, d, s1, cols)
        sum_add(i, d * u6, s2, cols)
        sum_add(i, d * u7, s3, cols)

    f_n = fact_ref.shape[1]
    fact = flat(fact_ref[...])
    fc = dot(fact, wout_ref[...])
    fill4 = m64_ref[0:1]
    parts = []
    for s in range(s_n):
        cols = slice(s * LANES, (s + 1) * LANES)
        d = back_norm(
            rows(c3_ref, 0, s, 1), rows(q4_ref, 0, s, 1), rows(q4_ref, 1, s, 1),
            df_ref[:, :, cols], fc[:, cols].reshape(p_n, f_n, LANES), fill4,
        )
        parts.append(flat(d).astype(BF16))
    dfc = jnp.concatenate(parts, axis=1)
    gout_ref[...] = jnp.where(i == 0, 0.0, gout_ref[...]) + dot_tn(fact, dfc)
    z = fb_ref[...]
    back = dot_nt(dfc, wout_ref[...]).reshape(p_n, f_n, LANES) * slope(
        z * rows(c2_ref, 0, 0, 1) + rows(c2_ref, 1, 0, 1)
    )
    dfb_ref[...] = back
    sum_add(i, back, t1)
    sum_add(i, back * (z * rows(c2_ref, 2, 0, 1) - rows(c2_ref, 3, 0, 1)), t2)
    for k, value in enumerate((back, z)):
        value = flat(value)
        for p in range(p_n):
            down_ref[0, k, p : p + 1, :] = value[p * f_n : p * f_n + 1, :]
            up_ref[0, k, p : p + 1, :] = value[p * f_n + f_n - 1 : p * f_n + f_n, :]
        down_ref[0, k, p_n : p_n + 1, :] = m64_ref[0, 0:1, :]
        up_ref[0, k, p_n : p_n + 1, :] = m64_ref[0, f_n - 1 : f_n, :]

    @pl.when(i == STEPS - 1)
    def _():
        zero_ref(st_ref)
        put_rows(st_ref, 0, sum_end(s1))
        put_rows(st_ref, 8, sum_end(s2))
        put_rows(st_ref, 16, sum_end(s3))
        put_rows(st_ref, 24, sum_end(t1))
        put_rows(st_ref, 25, sum_end(t2))


def k_back_out(dy_ref, sp_ref, sact_ref, sb_ref, dfb_ref, fb_ref, fa_ref, ftap_ref, hp_ref, hn_ref,
               c1_ref, c2_ref, c3_ref, c4_ref, q5_ref, m16_ref, m64_ref, wso_ref, wback_ref,
               dsc_ref, dsp_ref, dsb_ref, dfa_ref, gmid_ref, st_ref, s1, s2, t1, t2):
    i = pl.program_id(0)
    s_n, p_n, t_n, c = sb_ref.shape
    sact = flat(sact_ref[...])
    fill = m16_ref[0:1, :, 0:1]
    wide = 256
    back = None
    for n in range(wso_ref.shape[1] // wide):
        cols = slice(n * wide, (n + 1) * wide)
        shape = (s_n * p_n, t_n, wide)
        d = dy_ref[:, :, :, cols].reshape(shape)
        sc = dot(sact, wso_ref[:, cols]).reshape(shape)
        dsc = back_norm(rows(c4_ref, 0, 2 * n, 2), rows(q5_ref, 0, 2 * n, 2), rows(q5_ref, 1, 2 * n, 2), d, sc, fill)
        dsc = dsc.astype(BF16)
        dsc_ref[:, :, :, cols] = dsc.reshape(s_n, p_n, t_n, wide)
        sp = sp_ref[:, :, :, cols].reshape(shape)
        dsp = back_norm(
            rows(c2_ref, 0, 3 + 2 * n, 2), rows(q5_ref, 0, 8 + 2 * n, 2), rows(q5_ref, 1, 8 + 2 * n, 2), d, sp, fill
        )
        dsp_ref[:, :, :, cols] = dsp.astype(BF16).reshape(s_n, p_n, t_n, wide)
        part = dot_nt(flat(dsc), wso_ref[:, cols])
        back = part if back is None else back + part
    z = sb_ref[...].reshape(s_n * p_n, t_n, c)
    back = back.reshape(z.shape) * slope(z * rows(c3_ref, 0, 4, 2) + rows(c3_ref, 1, 4, 2))
    dsb_ref[...] = back.reshape(dsb_ref.shape)
    sum_add(i, back, s1)
    sum_add(i, back * (z * rows(c3_ref, 2, 4, 2) - rows(c3_ref, 3, 4, 2)), s2)

    f_n = fb_ref.shape[1]
    scale, p_row, q_row = rows(c2_ref, 0, 0, 1), rows(q5_ref, 0, 16, 1), rows(q5_ref, 1, 16, 1)
    dfb = back_norm(scale, p_row, q_row, dfb_ref[...], fb_ref[...], m64_ref[0:1])
    dfb_low = flat(dfb).astype(BF16)
    gmid_ref[...] = jnp.where(i == 0, 0.0, gmid_ref[...]) + dot_tn(dfb_low, flat(ftap_ref[...]))
    own = dfb_low.astype(F32)
    ends = []
    for ref in (hp_ref, hn_ref):
        small = back_norm(scale, p_row, q_row, ref[0, 0], ref[0, 1], ref[0, 0, p_n : p_n + 1, :])
        small = small.astype(BF16).astype(F32)
        ends.append(
            jnp.concatenate(
                [jnp.broadcast_to(small[p : p + 1, :], (f_n, LANES)) for p in range(p_n)], axis=0
            ).reshape(p_n, f_n, LANES)
        )
    before, after = shifted(own, ends[0], ends[1], f_n)
    taps = jnp.concatenate(
        [flat(after * m64_ref[2:3]), own, flat(before * m64_ref[1:2])], axis=1
    ).astype(BF16)
    z = fa_ref[...]
    back = dot(taps, wback_ref[...]).reshape(z.shape) * slope(
        z * rows(c1_ref, 0, 0, 1) + rows(c1_ref, 1, 0, 1)
    )
    dfa_ref[...] = back
    sum_add(i, back, t1)
    sum_add(i, back * (z * rows(c1_ref, 2, 0, 1) - rows(c1_ref, 3, 0, 1)), t2)

    @pl.when(i == STEPS - 1)
    def _():
        zero_ref(st_ref)
        put_rows(st_ref, 0, sum_end(s1))
        put_rows(st_ref, 2, sum_end(s2))
        put_rows(st_ref, 4, sum_end(t1))
        put_rows(st_ref, 5, sum_end(t2))


def k_back_spatial(dsb_ref, sb_ref, sa_ref, x_ref, dfa_ref, fa_ref, c1_ref, c2_ref, c3_ref, q6_ref,
                   m16_ref, m64_ref, wsp_ref,
                   pad_ref, dsa_ref, dlow_ref, gin_ref, st_ref, s1, s2):
    i = pl.program_id(0)
    h_n, w_n, t_n, c = sb_ref.shape

    @pl.when(i == 0)
    def _():
        scale = rows(c3_ref, 0, 4, 2)
        p_row, q_row = rows(q6_ref, 0, 0, 2), rows(q6_ref, 1, 0, 2)
        zero_ref(pad_ref)

        @pl.loop(0, h_n)
        def _(h):
            d = back_norm(scale, p_row, q_row, dsb_ref[h], sb_ref[h], m16_ref[0:1, :, 0:1])
            pad_ref[h + 1, 1 : w_n + 1] = d.astype(BF16)

    per = h_n // STEPS
    h0 = i * per
    acc = None
    for a in range(3):
        for b in range(3):
            k = 3 * a + b
            block = pad_ref[pl.ds(h0 + 2 - a, per), 2 - b : 2 - b + w_n]
            part = dot_nt(flat(block), wsp_ref[k])
            acc = part if acc is None else acc + part
    z = sa_ref[...].reshape(per * w_n, t_n, c)
    back = acc.reshape(z.shape) * slope(z * rows(c2_ref, 0, 1, 2) + rows(c2_ref, 1, 1, 2))
    dsa_ref[...] = back.reshape(dsa_ref.shape)
    sum_add(i, back, s1)
    sum_add(i, back * (z * rows(c2_ref, 2, 1, 2) - rows(c2_ref, 3, 1, 2)), s2)

    low = back_norm(
        rows(c1_ref, 0, 0, 1), rows(q6_ref, 0, 2, 1), rows(q6_ref, 1, 2, 1), dfa_ref[...], fa_ref[...], m64_ref[0:1]
    ).astype(BF16)
    dlow_ref[...] = low
    packed = jnp.concatenate([flat(x_ref[s]) for s in range(x_ref.shape[0])], axis=1)
    gin_ref[...] = jnp.where(i == 0, 0.0, gin_ref[...]) + dot_tn(flat(low), packed)

    @pl.when(i == STEPS - 1)
    def _():
        zero_ref(st_ref)
        put_rows(st_ref, 0, sum_end(s1))
        put_rows(st_ref, 2, sum_end(s2))


def k_back_join(dsa_ref, sa_ref, dsp_ref, lat_ref, c1_ref, c2_ref, q7_ref, m16_ref, wj_ref,
                low_ref, gx_ref, dlat_ref, down_ref, st_ref, s1, s2):
    i = pl.program_id(0)
    s_n, p_n, t_n, c = sa_ref.shape
    shape = (s_n * p_n, t_n, c)
    low = back_norm(
        rows(c2_ref, 0, 1, 2), rows(q7_ref, 0, 0, 2), rows(q7_ref, 1, 0, 2),
        dsa_ref[...].reshape(shape), sa_ref[...].reshape(shape), m16_ref[0:1, :, 0:1],
    ).astype(BF16)
    low_ref[...] = low.reshape(low_ref.shape)
    both = jnp.concatenate([flat(low), flat(dsp_ref[...])], axis=1)
    wide = 256
    blocks = wj_ref.shape[0] // wide
    for n in range(blocks):
        d = dot_nt(both, wj_ref[n * wide : (n + 1) * wide, :])
        if n < blocks - 1:
            gx_ref[:, :, :, n * wide : (n + 1) * wide] = d.astype(BF16).reshape(s_n, p_n, t_n, wide)
    z = lat_ref[...].reshape(shape)
    back = d.reshape(shape) * slope(z * rows(c1_ref, 0, 1, 2) + rows(c1_ref, 1, 1, 2))
    dlat_ref[...] = back.reshape(dlat_ref.shape)
    sum_add(i, back, s1)
    sum_add(i, back * (z * rows(c1_ref, 2, 1, 2) - rows(c1_ref, 3, 1, 2)), s2)
    fill = jnp.broadcast_to(m16_ref[0, 0:1, 0:1], (1, c))
    for k, value in enumerate((flat(back), flat(z))):
        for s in range(s_n):
            for p in range(p_n):
                r = (s * p_n + p) * t_n
                down_ref[0, k, s, p : p + 1, :] = value[r : r + 1, :]
            down_ref[0, k, s, p_n : p_n + 1, :] = fill

    @pl.when(i == STEPS - 1)
    def _():
        zero_ref(st_ref)
        put_rows(st_ref, 0, sum_end(s1))
        put_rows(st_ref, 2, sum_end(s2))


def k_last(dlat_ref, lat_ref, taps_ref, hn_ref, df_ref, dlow_ref, c1_ref, q8_ref, m16_ref,
           wlat_ref, wfa_ref, gx_ref, glat_ref, gs):
    i = pl.program_id(0)
    s_n, p_n, t_n, c = lat_ref.shape
    shape = (s_n * p_n, t_n, c)
    scale, p_row, q_row = rows(c1_ref, 0, 1, 2), rows(q8_ref, 0, 0, 2), rows(q8_ref, 1, 0, 2)
    low = flat(
        back_norm(scale, p_row, q_row, dlat_ref[...].reshape(shape), lat_ref[...].reshape(shape), m16_ref[0:1, :, 0:1])
    ).astype(BF16)
    glat_ref[...] = jnp.where(i == 0, 0.0, glat_ref[...]) + dot_tn(low, flat(taps_ref[...]))
    ends = []
    for s in range(s_n):
        small = back_norm(
            scale, p_row, q_row, hn_ref[0, 0, s], hn_ref[0, 1, s], hn_ref[0, 0, s, p_n : p_n + 1, :]
        )
        small = small.astype(BF16).astype(F32)
        ends += [jnp.broadcast_to(small[p : p + 1, :], (t_n, c)) for p in range(p_n)]
    ends = jnp.concatenate(ends, axis=0).reshape(shape)
    n = low.shape[0]
    moved = pltpu.roll(low.astype(F32), n - 1, 0).reshape(shape)
    place = lax.broadcasted_iota(jnp.int32, shape, 1)
    following = flat(jnp.where(place == t_n - 1, ends, moved) * m16_ref[2:3, :, 0:1]).astype(BF16)
    own = dot_nt(low, wlat_ref[2 * LANES : 5 * LANES, :])
    late = dot_nt(following, wlat_ref[0 : 2 * LANES, :])
    gs[pl.ds(0, n, stride=4), :] = own[:, 0:LANES]
    gs[pl.ds(1, n, stride=4), :] = own[:, LANES : 2 * LANES]
    gs[pl.ds(2, n, stride=4), :] = own[:, 2 * LANES :] + late[:, 0:LANES]
    gs[pl.ds(3, n, stride=4), :] = late[:, LANES:]
    back = dot_nt(flat(dlow_ref[...]), wfa_ref[...])
    for s in range(s_n):
        cols = slice(s * LANES, (s + 1) * LANES)
        total = flat(df_ref[:, :, cols]) + back[:, cols] + gs[s * n : (s + 1) * n, :]
        gx_ref[s] = total.astype(BF16).reshape(gx_ref.shape[1:])


def blockdiag(matrix, count):
    a, b = matrix.shape
    eye = jnp.eye(count, dtype=matrix.dtype)
    return (eye[:, None, :, None] * matrix[None, :, None, :]).reshape(count * a, count * b)


def fold_diag(value, count, a, b):
    blocks = value.reshape(count, a, count, b)
    return sum(blocks[s, :, s, :] for s in range(count))


def per_device(slow_input, fast_input, clip_offset, fill, w_fast_in, w_fast_mid, w_fast_out, w_lateral,
               w_slow_in, w_slow_mid, w_slow_out, w_shortcut, gains, biases, slow_cot, fast_cot):
    sizes = (lax.axis_size("path"), lax.axis_size("frames"))
    total = sizes[0] * sizes[1]
    me = lax.axis_index("path") * sizes[1] + lax.axis_index("frames")
    t_n, side, _, c_slow = slow_input.shape
    f_n, c_fast = fast_input.shape[0], fast_input.shape[3]
    in_fast, in_slow, c_lat = w_fast_in.shape[1], w_slow_in.shape[1], w_lateral.shape[2]
    pixels = side * side
    groups = LANES // in_fast
    inner = pixels // groups
    p_n = inner // STEPS

    def slow_view(a):
        return jnp.transpose(a, (1, 2, 0, 3)).reshape(groups, inner, t_n, a.shape[3])

    def fast_view(a):
        return jnp.transpose(a, (1, 2, 0, 3)).reshape(groups, inner, f_n, a.shape[3])

    def unview(a):
        return jnp.transpose(a.reshape(side, side, a.shape[2], a.shape[3]), (2, 0, 1, 3))

    x_slow, cot_slow = slow_view(slow_input), slow_view(slow_cot)
    x_fast, cot_fast = fast_view(fast_input), fast_view(fast_cot)

    filled = fill.astype(F32)
    link = (clip_offset >= 1).astype(F32)
    next_link = jnp.concatenate([link[1:], (me < total - 1).astype(F32)[None]])
    m16 = jnp.broadcast_to(jnp.stack([filled, link, next_link])[:, :, None], (3, t_n, LANES))
    ones = jnp.ones((t_n, 3), F32)
    before = jnp.concatenate([link[:, None], ones], axis=1).reshape(f_n)
    after = jnp.concatenate([ones, next_link[:, None]], axis=1).reshape(f_n)
    m64 = jnp.broadcast_to(jnp.stack([jnp.repeat(filled, 4), before, after])[:, :, None], (3, f_n, LANES))

    def norm_rows(a):
        at = [0]
        for w in (in_fast, in_fast, c_fast, c_lat, in_slow, in_slow, c_slow, c_slow):
            at.append(at[-1] + w)
        seg = [a[at[k] : at[k + 1]] for k in range(8)]
        return jnp.concatenate(
            [seg[0]] * groups + [seg[1]] * groups + [seg[2]] * groups + seg[3:]
        ).reshape(-1, LANES)

    gb = jnp.stack([norm_rows(gains), norm_rows(biases)])

    tail = x_fast.reshape(pixels, f_n, c_fast)[:, f_n - 2 :].reshape(groups, STEPS, p_n, 2 * c_fast)
    ups = [(k, k + 1) for k in range(total - 1)]
    tail = lax.ppermute(tail, AXES, ups)
    tail = jnp.pad(jnp.transpose(tail, (1, 0, 2, 3)).astype(F32), ((0, 0), (0, 0), (0, 8 - p_n), (0, 0)))

    wfa = blockdiag(w_fast_in, groups)
    wmid = jnp.concatenate([blockdiag(w_fast_mid[k], groups) for k in range(3)], axis=0)
    wback = jnp.concatenate([blockdiag(w_fast_mid[k].T, groups) for k in range(3)], axis=0)
    wout = blockdiag(w_fast_out, groups)
    wlat = w_lateral.reshape(-1, c_lat)
    wj = jnp.concatenate([w_slow_in, w_shortcut], axis=1)
    wsp = w_slow_mid.reshape(9, in_slow, in_slow)

    sl = (groups, inner, t_n)
    fp = (inner, f_n)

    def slow_out(width, dtype):
        return out_blocked(sl + (width,), dtype, 1, p_n)

    def fast_out(width, dtype):
        return out_blocked(fp + (width,), dtype, 0, p_n)

    def sb_(a):
        return blocked(a, 1, p_n)

    def fb_(a):
        return blocked(a, 0, p_n)

    def stat(n):
        return out_whole((pad8(n), LANES), F32)

    def acc(rows_n, width, count):
        return [pltpu.VMEM((rows_n, width), F32)] * count

    halo_small = out_blocked((STEPS, 8, LANES), F32, 0, 1)

    fa, lat, taps, st, up, down = call(
        k_first,
        [sb_(x_fast), blocked(tail, 0, 1), whole(m16), whole(m64), whole(wfa), whole(wlat)],
        [fast_out(LANES, F32), slow_out(c_lat, F32), slow_out(5 * c_fast, BF16), stat(7), halo_small, halo_small],
        [pltpu.VMEM((groups * p_n * f_n, c_fast), F32), *acc(f_n, LANES, 2), *acc(t_n, c_lat, 2)],
        "first",
    )
    c1, hp, hn = exchange(sizes, 1, st, gb, fwd=(("lane4", 0, 1), ("plain", 6, 2)), up=up, down=down)

    lact, ftap, sa, sp, fb, st = call(
        k_join,
        [sb_(x_slow), sb_(lat), fb_(fa), blocked(hp, 0, 1), blocked(hn, 0, 1), whole(c1), whole(m16), whole(m64),
         whole(wj), whole(wmid)],
        [slow_out(c_lat, BF16), fast_out(3 * LANES, BF16), slow_out(in_slow, F32), slow_out(c_slow, F32),
         fast_out(LANES, F32), stat(23)],
        [*acc(t_n, in_slow, 2), *acc(t_n, c_slow, 2), *acc(f_n, LANES, 2)],
        "join",
    )
    (c2,) = exchange(sizes, 2, st, gb, fwd=(("lane4", 1, 1), ("plain", 8, 2), ("plain", 20, 8)))

    rows_n = side // STEPS
    pad, sb, fact, st = call(
        k_spatial,
        [whole(sa.reshape(side, side, t_n, in_slow)),
         fb_(fb), whole(c2), whole(m16), whole(m64), whole(wsp), whole(wout)],
        [out_whole((side + 2, side + 2, t_n, in_slow), BF16),
         out_blocked((side, side, t_n, in_slow), F32, 0, rows_n), fast_out(LANES, BF16), stat(13)],
        [*acc(t_n, in_slow, 2), *acc(f_n, groups * c_fast, 2)],
        "spatial",
    )
    (c3,) = exchange(sizes, 3, st, gb, fwd=(("row4", 2, 4), ("plain", 10, 2)))

    sb4 = sb.reshape(sl + (in_slow,))
    sact, fast_y, df, st = call(
        k_expand,
        [sb_(sb4), fb_(fact), sb_(x_fast), sb_(cot_fast), whole(c3), whole(m16), whole(m64), whole(w_slow_out), whole(wout)],
        [slow_out(in_slow, BF16), out_blocked((groups, inner, f_n, c_fast), BF16, 1, p_n),
         fast_out(groups * c_fast, F32), stat(25)],
        [*acc(t_n, c_slow, 2), *acc(f_n, groups * c_fast, 2)],
        "expand",
    )
    c4, q4 = exchange(sizes, 4, st, gb, fwd=(("plain", 12, 8),), bwd=(("row4", 0, 0, 2, 4, 0, 4),), coefs=(c3,))

    halo_pair = out_blocked((STEPS, 2, 8, LANES), F32, 0, 1)
    slow_y, dy, dfb, g_fout, up, down, st = call(
        k_out,
        [sb_(sact), sb_(sp), sb_(cot_slow), fb_(df), fb_(fact), fb_(fb), whole(c2), whole(c3), whole(c4), whole(q4),
         whole(m16), whole(m64), whole(w_slow_out), whole(wout)],
        [slow_out(c_slow, BF16), slow_out(c_slow, F32), fast_out(LANES, F32),
         out_whole((LANES, groups * c_fast), F32), halo_pair, halo_pair, stat(26)],
        [*acc(t_n, c_slow, 3), *acc(f_n, LANES, 2)],
        "out",
    )
    q5, hp, hn = exchange(
        sizes, 5, st, gb,
        bwd=(("plain", 0, 0, 12, 8, 0, 8), ("plain", 1, 3, 20, 8, 0, 16), ("lane4", 1, 0, 1, 1, 24, 25)),
        coefs=(c4, c2), up=up, down=down,
    )

    dsc, dsp, dsb, dfa, g_fmid, st = call(
        k_back_out,
        [sb_(dy), sb_(sp), sb_(sact), sb_(sb4), fb_(dfb), fb_(fb), fb_(fa), fb_(ftap), blocked(hp, 0, 1), blocked(hn, 0, 1),
         whole(c1), whole(c2), whole(c3), whole(c4), whole(q5), whole(m16), whole(m64), whole(w_slow_out), whole(wback)],
        [slow_out(c_slow, BF16), slow_out(c_slow, BF16), slow_out(in_slow, F32), fast_out(LANES, F32),
         out_whole((LANES, 3 * LANES), F32), stat(6)],
        [*acc(t_n, in_slow, 2), *acc(f_n, LANES, 2)],
        "back_out",
    )
    (q6,) = exchange(
        sizes, 6, st, gb, bwd=(("plain", 0, 4, 10, 2, 0, 2), ("lane4", 1, 0, 0, 1, 4, 5)), coefs=(c3, c1)
    )

    grid = (side, side, t_n, in_slow)
    dpad, dsa, dfa_low, g_fin, st = call(
        k_back_spatial,
        [whole(dsb.reshape(grid)), whole(sb), blocked(sa.reshape(grid), 0, rows_n), sb_(x_fast), fb_(dfa), fb_(fa),
         whole(c1), whole(c2), whole(c3), whole(q6), whole(m16), whole(m64), whole(wsp)],
        [out_whole((side + 2, side + 2, t_n, in_slow), BF16), out_blocked(grid, F32, 0, rows_n), fast_out(LANES, BF16),
         out_whole((LANES, groups * c_fast), F32), stat(4)],
        [*acc(t_n, in_slow, 2)],
        "back_spatial",
    )
    (q7,) = exchange(sizes, 7, st, gb, bwd=(("plain", 0, 1, 8, 2, 0, 2),), coefs=(c2,))

    dsa_low, slow_gx, dlat, down, st = call(
        k_back_join,
        [sb_(dsa.reshape(sl + (in_slow,))), sb_(sa), sb_(dsp), sb_(lat), whole(c1), whole(c2), whole(q7), whole(m16), whole(wj)],
        [slow_out(in_slow, BF16), slow_out(c_slow, BF16), slow_out(c_lat, F32),
         out_blocked((STEPS, 2, groups, 8, c_lat), F32, 0, 1), stat(4)],
        [*acc(t_n, c_lat, 2)],
        "back_join",
    )
    q8, hn = exchange(sizes, 8, st, gb, bwd=(("plain", 0, 1, 6, 2, 0, 2),), coefs=(c1,), down=down)

    fast_gx, g_lat = call(
        k_last,
        [sb_(dlat), sb_(lat), sb_(taps), blocked(hn, 0, 1), fb_(df), fb_(dfa_low), whole(c1), whole(q8), whole(m16),
         whole(wlat), whole(wfa)],
        [out_blocked((groups, inner, f_n, c_fast), BF16, 1, p_n), out_whole((c_lat, 5 * c_fast), F32)],
        [pltpu.VMEM((groups * p_n * f_n, c_fast), F32)],
        "last",
    )

    def wgrad(a, b):
        return dot_tn(a.reshape(-1, a.shape[-1]), b.reshape(-1, b.shape[-1]))

    g_sout = wgrad(sact, dsc)
    g_short = jnp.concatenate([wgrad(x_slow, dsp), wgrad(lact, dsp)], axis=0)
    g_sin = jnp.concatenate([wgrad(x_slow, dsa_low), wgrad(lact, dsa_low)], axis=0)
    patches = jnp.concatenate(
        [pad[a : a + side, b : b + side] for a in range(3) for b in range(3)], axis=3
    )
    g_smid = wgrad(patches, dpad[1 : side + 1, 1 : side + 1]).reshape(w_slow_mid.shape)
    g_fin = fold_diag(g_fin, groups, in_fast, c_fast).T
    g_fmid = jnp.stack(
        [fold_diag(g_fmid[:, k * LANES : (k + 1) * LANES], groups, in_fast, in_fast).T for k in range(3)]
    )
    g_fout = fold_diag(g_fout, groups, in_fast, c_fast)
    g_lat = g_lat.T.reshape(w_lateral.shape)
    grads = lax.psum((g_fin, g_fmid, g_fout, g_lat, g_sin, g_smid, g_sout, g_short), AXES)

    def norm_grads(slab):
        def row(q, at, n):
            return q[slab, at : at + n].reshape(-1)

        return jnp.concatenate(
            [row(q6, 2, 1)[:in_fast], row(q5, 16, 1)[:in_fast], row(q4, 0, 1), row(q8, 0, 2), row(q7, 0, 2),
             row(q6, 0, 2), row(q5, 0, 8), row(q5, 8, 8)]
        )

    return (
        unview(slow_y),
        unview(fast_y),
        unview(slow_gx),
        unview(fast_gx),
        *grads,
        norm_grads(3),
        norm_grads(2),
    )


def solution(mesh):
    frames = P(("path", "frames"), None, None, None)
    in_specs = (frames, frames, P(AXES), P(AXES), *([P()] * 10), frames, frames)
    out_specs = (*([frames] * 4), *([P()] * 10))
    return jax.shard_map(per_device, mesh=mesh, in_specs=in_specs, out_specs=out_specs, check_vma=False)
```

```python
import functools

import jax
import jax.numpy as jnp
from jax import lax
from jax.experimental import pallas as pl
from jax.experimental.pallas import tpu as pltpu
from jax.sharding import PartitionSpec as P

norm_eps = 1e-05
F32 = jnp.float32
BF16 = jnp.bfloat16
MESH = pl.DeviceIdType.MESH
AXES = ("path", "frames")
STEPS = 7
LANES = 128
VMEM_LIMIT = 56 * 1024 * 1024


def dot(a, b):
    return jnp.dot(a, b, preferred_element_type=F32)


def dot_nt(a, b):
    return lax.dot_general(a, b, (((1,), (1,)), ((), ())), preferred_element_type=F32)


def dot_tn(a, b):
    return lax.dot_general(a, b, (((0,), (0,)), ((), ())), preferred_element_type=F32)


def sig(v):
    return 0.5 * jnp.tanh(0.5 * v) + 0.5


def slope(v):
    s = sig(v)
    return s + (v * s) * (1.0 - s)


def rows(ref, slab, first, count):
    parts = [ref[slab, first + j : first + j + 1, :] for j in range(count)]
    return parts[0] if count == 1 else jnp.concatenate(parts, axis=1)


def put_rows(ref, first, value):
    for j in range(value.shape[1] // LANES):
        ref[first + j : first + j + 1, :] = value[:, j * LANES : (j + 1) * LANES]


def zero_ref(ref):
    ref[...] = jnp.zeros(ref.shape, ref.dtype)


def spread_add(step, z, mean_ref, m2_ref, cols=slice(None)):
    count = z.shape[0]
    mean = jnp.sum(z, axis=0) * (1.0 / count)
    d = z - mean
    m2 = jnp.sum(d * d, axis=0)
    first = step == 0
    old_mean = jnp.where(first, 0.0, mean_ref[:, cols])
    old_m2 = jnp.where(first, 0.0, m2_ref[:, cols])
    done = jnp.full((1, z.shape[-1]), step, jnp.int32).astype(F32)
    share = 1.0 / (done + 1.0)
    delta = mean - old_mean
    mean_ref[:, cols] = old_mean + delta * share
    m2_ref[:, cols] = old_m2 + m2 + delta * delta * (done * share * count)


def spread_end(mean_ref, m2_ref, fill, positions):
    filled = jnp.sum(fill, axis=0, keepdims=True)
    mean = jnp.sum(fill * mean_ref[...], axis=0, keepdims=True) / jnp.maximum(filled, 1.0)
    d = mean_ref[...] - mean
    m2 = jnp.sum(fill * (m2_ref[...] + positions * (d * d)), axis=0, keepdims=True)
    return mean, m2


def sum_add(step, value, ref, cols=slice(None)):
    ref[:, cols] = jnp.where(step == 0, 0.0, ref[:, cols]) + jnp.sum(value, axis=0)


def sum_end(ref):
    return jnp.sum(ref[...], axis=0, keepdims=True)


def pad8(n):
    return -(-n // 8) * 8


def exchange_kernel(cfg, *refs):
    fwd, bwd, n_coefs, has_up, has_down = cfg
    nf = sum(c[2] for c in fwd)
    nb = max((c[6] + c[4] for c in bwd), default=0)
    nn = sum(c[4] for c in bwd)
    n_row = 2 * nf + nb
    it = iter(refs)
    stats_ref, gb_ref = next(it), next(it)
    coef_refs = [next(it) for _ in range(n_coefs)]
    up_ref = next(it) if has_up else None
    down_ref = next(it) if has_down else None
    coef_out = next(it) if nf else None
    pq_out = next(it) if nb else None
    from_prev = next(it) if has_up else None
    from_next = next(it) if has_down else None
    slots1, slots2, mid, tot, send1, recv1, send2, recv2 = (next(it) for _ in range(8))
    if has_up:
        up_land, up_sems = next(it), next(it)
    if has_down:
        down_land, down_sems = next(it), next(it)

    paths, length = lax.axis_size("path"), lax.axis_size("frames")
    near = 4
    g1, g2 = paths * near, length // near
    me_p, me_f = lax.axis_index("path"), lax.axis_index("frames")
    me = me_p * length + me_f
    total = paths * length
    r1 = me_p * near + lax.rem(me_f, near)
    r2 = lax.div(me_f, near)

    def peer1(k):
        r = lax.rem(r1 + k, g1)
        return (lax.div(r, near), r2 * near + lax.rem(r, near))

    def peer2(k):
        r = lax.rem(r2 + k, g2)
        return (me_p, r * near + lax.rem(me_f, near))

    def split(index):
        return (lax.div(index, length), lax.rem(index, length))

    nxt, prv = split(lax.rem(me + 1, total)), split(lax.rem(me + total - 1, total))

    barrier = pltpu.get_barrier_semaphore()
    greeted = 0
    for k in range(1, g1):
        pl.semaphore_signal(barrier, inc=1, device_id=peer1(k), device_id_type=MESH)
        greeted += 1
    for k in range(1, g2):
        pl.semaphore_signal(barrier, inc=1, device_id=peer2(k), device_id_type=MESH)
        greeted += 1
    if has_up or has_down:
        pl.semaphore_signal(barrier, inc=1, device_id=nxt, device_id_type=MESH)
        pl.semaphore_signal(barrier, inc=1, device_id=prv, device_id_type=MESH)
        greeted += 2
    pl.semaphore_wait(barrier, greeted)

    halos = []
    copies = []
    for k in range(1, g1):
        copies.append(
            pltpu.make_async_remote_copy(
                src_ref=stats_ref,
                dst_ref=slots1.at[r1],
                send_sem=send1.at[k],
                recv_sem=recv1.at[k],
                device_id=peer1(k),
                device_id_type=MESH,
            )
        )
        copies[-1].start()
    if has_up:
        halos.append(
            pltpu.make_async_remote_copy(
                src_ref=up_ref,
                dst_ref=up_land,
                send_sem=up_sems.at[0],
                recv_sem=up_sems.at[1],
                device_id=nxt,
                device_id_type=MESH,
            )
        )
        halos[-1].start()
    if has_down:
        halos.append(
            pltpu.make_async_remote_copy(
                src_ref=down_ref,
                dst_ref=down_land,
                send_sem=down_sems.at[0],
                recv_sem=down_sems.at[1],
                device_id=prv,
                device_id_type=MESH,
            )
        )
        halos[-1].start()
    slots1[r1] = stats_ref[...]
    for c in copies:
        c.wait_recv()

    def combine(slots, count, out):
        if nf:
            n = slots[0, n_row : n_row + 1, :]
            for g in range(1, count):
                n = n + slots[g, n_row : n_row + 1, :]
            acc = slots[0, n_row : n_row + 1, :] * slots[0, 0:nf, :]
            for g in range(1, count):
                acc = acc + slots[g, n_row : n_row + 1, :] * slots[g, 0:nf, :]
            mean = acc / jnp.maximum(n, 1.0)
            m2 = None
            for g in range(count):
                d = slots[g, 0:nf, :] - mean
                part = slots[g, nf : 2 * nf, :] + slots[g, n_row : n_row + 1, :] * (d * d)
                m2 = part if m2 is None else m2 + part
            out[0:nf, :] = mean
            out[nf : 2 * nf, :] = m2
            out[n_row : n_row + 1, :] = n
        if nb:
            acc = slots[0, 2 * nf : n_row, :]
            for g in range(1, count):
                acc = acc + slots[g, 2 * nf : n_row, :]
            out[2 * nf : n_row, :] = acc

    zero_ref(mid)
    combine(slots1, g1, mid)
    copies2 = []
    for k in range(1, g2):
        copies2.append(
            pltpu.make_async_remote_copy(
                src_ref=mid,
                dst_ref=slots2.at[r2],
                send_sem=send2.at[k],
                recv_sem=recv2.at[k],
                device_id=peer2(k),
                device_id_type=MESH,
            )
        )
        copies2[-1].start()
    slots2[r2] = mid[...]
    for c in copies2:
        c.wait_recv()
    combine(slots2, g2, tot)

    def lanes4(v):
        w = v + pltpu.roll(v, 64, 1)
        return w + pltpu.roll(w, 32, 1)

    at = 0
    for kind, g_row, count in fwd:
        n = tot[n_row : n_row + 1, :]
        mean = tot[at : at + count, :]
        m2 = tot[nf + at : nf + at + count, :]
        if kind == "lane4":
            whole = lanes4(mean) * 0.25
            d = mean - whole
            var = lanes4(m2 + n * (d * d)) / (4.0 * n)
            mean = whole
        elif kind == "row4":
            whole = jnp.sum(mean, axis=0, keepdims=True) * 0.25
            d = mean - whole
            var = jnp.sum(m2 + n * (d * d), axis=0, keepdims=True) / (4.0 * n)
            var = jnp.broadcast_to(var, (count, LANES))
            mean = jnp.broadcast_to(whole, (count, LANES))
        else:
            var = m2 / n
        inv = lax.rsqrt(var + norm_eps)
        scale = inv * gb_ref[0, g_row : g_row + count, :]
        coef_out[0, at : at + count, :] = scale
        coef_out[1, at : at + count, :] = gb_ref[1, g_row : g_row + count, :] - mean * scale
        coef_out[2, at : at + count, :] = inv
        coef_out[3, at : at + count, :] = mean * inv
        coef_out[4, at : at + count, :] = jnp.broadcast_to(n, (count, LANES))
        at += count
    at = 0
    for kind, coef, row, _, count, db_at, dg_at in bwd:
        db = tot[2 * nf + db_at : 2 * nf + db_at + count, :]
        dg = tot[2 * nf + dg_at : 2 * nf + dg_at + count, :]
        c = coef_refs[coef]
        scale, inv = c[0, row : row + count, :], c[2, row : row + count, :]
        mi, n = c[3, row : row + count, :], c[4, row : row + count, :]
        if kind == "lane4":
            db, dg, n = lanes4(db), lanes4(dg), 4.0 * n
        elif kind == "row4":
            db = jnp.broadcast_to(jnp.sum(db, axis=0, keepdims=True), (count, LANES))
            dg = jnp.broadcast_to(jnp.sum(dg, axis=0, keepdims=True), (count, LANES))
            n = 4.0 * n
        pq_out[0, at : at + count, :] = scale / n * (db - mi * dg)
        pq_out[1, at : at + count, :] = scale / n * inv * dg
        pq_out[2, at : at + count, :] = db
        pq_out[3, at : at + count, :] = dg
        at += count

    for c in halos:
        c.wait()
    if has_up:
        from_prev[...] = up_land[...]
    if has_down:
        from_next[...] = down_land[...]
    for c in copies:
        c.wait_send()
    for c in copies2:
        c.wait_send()


def exchange(mesh_sizes, cid, stats, gb, fwd=(), bwd=(), coefs=(), up=None, down=None):
    paths, length = mesh_sizes
    g1, g2 = paths * 4, length // 4
    nf = sum(c[2] for c in fwd)
    nn = sum(c[4] for c in bwd)
    r = stats.shape[0]
    vm = pl.BlockSpec(memory_space=pltpu.VMEM)
    operands = [stats, gb, *coefs]
    outs = []
    if nf:
        outs.append(jax.ShapeDtypeStruct((5, nf, LANES), F32))
    if nn:
        outs.append(jax.ShapeDtypeStruct((4, nn, LANES), F32))
    scratch = [
        pltpu.VMEM((g1, r, LANES), F32),
        pltpu.VMEM((g2, r, LANES), F32),
        pltpu.VMEM((r, LANES), F32),
        pltpu.VMEM((r, LANES), F32),
        pltpu.SemaphoreType.DMA((g1,)),
        pltpu.SemaphoreType.DMA((g1,)),
        pltpu.SemaphoreType.DMA((g2,)),
        pltpu.SemaphoreType.DMA((g2,)),
    ]
    for halo in (up, down):
        if halo is not None:
            operands.append(halo)
            outs.append(jax.ShapeDtypeStruct(halo.shape, halo.dtype))
            scratch += [pltpu.VMEM(halo.shape, halo.dtype), pltpu.SemaphoreType.DMA((2,))]
    cfg = (fwd, bwd, len(coefs), up is not None, down is not None)
    return pl.pallas_call(
        functools.partial(exchange_kernel, cfg),
        out_shape=outs,
        in_specs=[vm] * len(operands),
        out_specs=[vm] * len(outs),
        scratch_shapes=scratch,
        compiler_params=pltpu.CompilerParams(collective_id=cid, has_side_effects=True),
        name=f"exchange_{cid}",
    )(*operands)


def call(kernel, ins, outs, scratch=(), name=None):
    return pl.pallas_call(
        kernel,
        grid=(STEPS,),
        in_specs=[pl.BlockSpec(b, m) for _, b, m in ins],
        out_specs=[pl.BlockSpec(b, m) for _, _, b, m in outs],
        out_shape=[jax.ShapeDtypeStruct(s, d) for s, d, _, _ in outs],
        scratch_shapes=list(scratch),
        compiler_params=pltpu.CompilerParams(
            dimension_semantics=("arbitrary",), vmem_limit_bytes=VMEM_LIMIT
        ),
        name=name,
    )(*[a for a, _, _ in ins])


def whole(array):
    zeros = (0,) * array.ndim
    return (array, array.shape, lambda i: zeros)


def blocked(array, axis, size):
    block = array.shape[:axis] + (size,) + array.shape[axis + 1 :]
    return (array, block, lambda i: tuple(i if d == axis else 0 for d in range(array.ndim)))


def out_whole(shape, dtype):
    zeros = (0,) * len(shape)
    return (shape, dtype, shape, lambda i: zeros)


def out_blocked(shape, dtype, axis, size):
    block = shape[:axis] + (size,) + shape[axis + 1 :]
    return (shape, dtype, block, lambda i: tuple(i if d == axis else 0 for d in range(len(shape))))


def flat(value):
    return value.reshape(-1, value.shape[-1])


def spread_rows(ref, index, count, height):
    return [jnp.broadcast_to(ref[(*index, slice(p, p + 1))], (height, ref.shape[-1])) for p in range(count)]


def k_first(x_ref, tail_ref, m16_ref, m64_ref, wfa_ref, wlat_ref,
            fa_ref, lat_ref, taps_ref, st_ref, up_ref, down_ref, xs, fm, fv, lm, lv):
    i = pl.program_id(0)
    x = x_ref[...]
    s_n, p_n, f_n, _ = x.shape
    packed = jnp.concatenate([flat(x[s]) for s in range(s_n)], axis=1)
    fa = dot_nt(packed, wfa_ref[...])
    fa_ref[...] = fa.reshape(fa_ref.shape)
    zero_ref(up_ref)
    zero_ref(down_ref)
    for p in range(p_n):
        down_ref[0, p : p + 1, :] = fa[p * f_n : p * f_n + 1, :]
        up_ref[0, p : p + 1, :] = fa[p * f_n + f_n - 1 : p * f_n + f_n, :]
    spread_add(i, fa.reshape(p_n, f_n, LANES), fm, fv)

    xs[...] = flat(x).astype(F32)
    n = xs.shape[0] // 4
    quarter = [xs[pl.ds(k, n, stride=4), :] for k in range(4)]
    t_n = f_n // 4
    first = lax.broadcasted_iota(jnp.int32, (n // t_n, t_n, LANES), 1) == 0
    link = m16_ref[1:2]
    taps = []
    for k in range(2):
        halo = jnp.concatenate(
            [
                jnp.broadcast_to(tail_ref[0, s, p : p + 1, k * LANES : (k + 1) * LANES], (t_n, LANES))
                for s in range(s_n)
                for p in range(p_n)
            ],
            axis=0,
        )
        moved = pltpu.roll(quarter[2 + k], 1, 0).reshape(n // t_n, t_n, LANES)
        taps.append(flat(jnp.where(first, halo.reshape(moved.shape), moved) * link))
    taps = jnp.concatenate([*taps, *quarter[:3]], axis=1).astype(BF16)
    taps_ref[...] = taps.reshape(taps_ref.shape)
    lat = dot(taps, wlat_ref[...])
    lat_ref[...] = lat.reshape(lat_ref.shape)
    spread_add(i, lat.reshape(n // t_n, t_n, lat.shape[1]), lm, lv)

    @pl.when(i == STEPS - 1)
    def _():
        zero_ref(st_ref)
        fill = m16_ref[0, :, 0:1]
        mean, m2 = spread_end(fm, fv, m64_ref[0, :, 0:1], STEPS * p_n)
        put_rows(st_ref, 0, mean)
        put_rows(st_ref, 3, m2)
        mean, m2 = spread_end(lm, lv, fill, STEPS * p_n * s_n)
        put_rows(st_ref, 1, mean)
        put_rows(st_ref, 4, m2)
        put_rows(st_ref, 6, count_row(m16_ref, STEPS * p_n * s_n))


def count_row(m16_ref, positions):
    return jnp.sum(m16_ref[0], axis=0, keepdims=True) * float(positions)


def shifted(value, first_rows, last_rows, f_n):
    n = value.shape[0]
    shape = (n // f_n, f_n, value.shape[1])
    place = lax.broadcasted_iota(jnp.int32, shape, 1)
    before = jnp.where(place == 0, first_rows, pltpu.roll(value, 1, 0).reshape(shape))
    after = jnp.where(place == f_n - 1, last_rows, pltpu.roll(value, n - 1, 0).reshape(shape))
    return before, after


def k_join(x_ref, lat_ref, fa_ref, hp_ref, hn_ref, c1_ref, m16_ref, m64_ref, win_ref, wsc_ref, wmid_ref,
           lact_ref, ftap_ref, sa_ref, sp_ref, fb_ref, st_ref, am, av, pm, pv, bm, bv):
    i = pl.program_id(0)
    s_n, p_n, t_n, c_slow = x_ref.shape
    c_lat = lat_ref.shape[-1]
    v = flat(lat_ref[...]) * rows(c1_ref, 0, 1, 2) + rows(c1_ref, 1, 1, 2)
    lact = (v * sig(v)).astype(BF16)
    lact_ref[...] = lact.reshape(lact_ref.shape)
    joined = jnp.concatenate([flat(x_ref[...]), lact], axis=1)
    wide = c_lat
    for n in range(1 + wsc_ref.shape[1] // wide):
        z = dot(joined, win_ref[...] if n == 0 else wsc_ref[:, (n - 1) * wide : n * wide])
        z4 = z.reshape(s_n, p_n, t_n, wide)
        z3 = z.reshape(s_n * p_n, t_n, wide)
        if n == 0:
            sa_ref[...] = z4
            spread_add(i, z3, am, av)
        else:
            cols = slice((n - 1) * wide, n * wide)
            sp_ref[:, :, :, cols] = z4
            spread_add(i, z3, pm, pv, cols)

    f_n = fa_ref.shape[1]
    scale, shift = rows(c1_ref, 0, 0, 1), rows(c1_ref, 1, 0, 1)

    def act(z):
        w = z * scale + shift
        return (w * sig(w)).astype(BF16).astype(F32)

    fact = act(flat(fa_ref[...]))
    ends = []
    for ref in (hp_ref, hn_ref):
        small = act(ref[0])
        ends.append(
            jnp.concatenate(
                [jnp.broadcast_to(small[p : p + 1, :], (f_n, LANES)) for p in range(p_n)], axis=0
            ).reshape(p_n, f_n, LANES)
        )
    before, after = shifted(fact, ends[0], ends[1], f_n)
    ftap = jnp.concatenate(
        [flat(before * m64_ref[1:2]), fact, flat(after * m64_ref[2:3])], axis=1
    ).astype(BF16)
    ftap_ref[...] = ftap.reshape(ftap_ref.shape)
    fb = dot(ftap, wmid_ref[...])
    fb_ref[...] = fb.reshape(fb_ref.shape)
    spread_add(i, fb.reshape(p_n, f_n, LANES), bm, bv)

    @pl.when(i == STEPS - 1)
    def _():
        zero_ref(st_ref)
        fill = m16_ref[0, :, 0:1]
        positions = STEPS * p_n * s_n
        mean, m2 = spread_end(bm, bv, m64_ref[0, :, 0:1], STEPS * p_n)
        put_rows(st_ref, 0, mean)
        put_rows(st_ref, 11, m2)
        mean, m2 = spread_end(am, av, fill, positions)
        put_rows(st_ref, 1, mean)
        put_rows(st_ref, 12, m2)
        mean, m2 = spread_end(pm, pv, fill, positions)
        put_rows(st_ref, 3, mean)
        put_rows(st_ref, 14, m2)
        put_rows(st_ref, 22, count_row(m16_ref, positions))


def k_spatial(sa_ref, fb_ref, c2_ref, m16_ref, m64_ref, wsp_ref, wout_ref,
              pad_ref, sb_ref, fact_ref, st_ref, sm, sv, cm, cv):
    i = pl.program_id(0)
    h_n, w_n, t_n, c = sa_ref.shape

    @pl.when(i == 0)
    def _():
        scale, shift = rows(c2_ref, 0, 1, 2), rows(c2_ref, 1, 1, 2)
        zero_ref(pad_ref)

        @pl.loop(0, h_n)
        def _(h):
            v = flat(sa_ref[h]) * scale + shift
            pad_ref[h + 1, 1 : w_n + 1] = (v * sig(v)).astype(BF16).reshape(w_n, t_n, c)

    per = h_n // STEPS
    h0 = i * per
    acc = None
    for a in range(3):
        for b in range(3):
            k = 3 * a + b
            part = dot(flat(pad_ref[pl.ds(h0 + a, per), b : b + w_n].reshape(per * w_n, t_n, c)), wsp_ref[k])
            acc = part if acc is None else acc + part
    sb_ref[...] = acc.reshape(sb_ref.shape)
    spread_add(i, acc.reshape(per * w_n, t_n, acc.shape[1]), sm, sv)

    p_n, f_n, _ = fb_ref.shape
    v = flat(fb_ref[...]) * rows(c2_ref, 0, 0, 1) + rows(c2_ref, 1, 0, 1)
    fact = (v * sig(v)).astype(BF16)
    fact_ref[...] = fact.reshape(fact_ref.shape)
    fc = dot(fact, wout_ref[...])
    spread_add(i, fc.reshape(p_n, f_n, fc.shape[1]), cm, cv)

    @pl.when(i == STEPS - 1)
    def _():
        zero_ref(st_ref)
        mean, m2 = spread_end(cm, cv, m64_ref[0, :, 0:1], STEPS * p_n)
        put_rows(st_ref, 0, mean)
        put_rows(st_ref, 6, m2)
        mean, m2 = spread_end(sm, sv, m16_ref[0, :, 0:1], h_n * w_n)
        put_rows(st_ref, 4, mean)
        put_rows(st_ref, 10, m2)
        put_rows(st_ref, 12, count_row(m16_ref, h_n * w_n))


def k_expand(sb_ref, fact_ref, x_ref, cot_ref, c3_ref, m16_ref, m64_ref, wso_ref, wout_ref,
             sact_ref, fout_ref, df_ref, st_ref, cm, cv, s1, s2):
    i = pl.program_id(0)
    s_n, p_n, t_n, c = sb_ref.shape
    v = flat(sb_ref[...]) * rows(c3_ref, 0, 4, 2) + rows(c3_ref, 1, 4, 2)
    sact = (v * sig(v)).astype(BF16)
    sact_ref[...] = sact.reshape(sact_ref.shape)
    wide = 256
    for n in range(wso_ref.shape[1] // wide):
        cols = slice(n * wide, (n + 1) * wide)
        z = dot(sact, wso_ref[:, cols])
        spread_add(i, z.reshape(s_n * p_n, t_n, wide), cm, cv, cols)

    f_n = fact_ref.shape[1]
    fc = dot(flat(fact_ref[...]), wout_ref[...])
    fill = m64_ref[0:1]
    for s in range(s_n):
        cols = slice(s * LANES, (s + 1) * LANES)
        z = fc[:, cols].reshape(p_n, f_n, LANES)
        unit = z * rows(c3_ref, 2, s, 1) - rows(c3_ref, 3, s, 1)
        pre = z * rows(c3_ref, 0, s, 1) + rows(c3_ref, 1, s, 1) + x_ref[s].astype(F32)
        g = sig(pre)
        y = pre * g
        fout_ref[s] = (y * fill).astype(BF16)
        d = cot_ref[s].astype(F32) * fill * (g + y * (1.0 - g))
        df_ref[:, :, cols] = d
        sum_add(i, d, s1, cols)
        sum_add(i, d * unit, s2, cols)

    @pl.when(i == STEPS - 1)
    def _():
        zero_ref(st_ref)
        positions = STEPS * p_n * s_n
        mean, m2 = spread_end(cm, cv, m16_ref[0, :, 0:1], positions)
        put_rows(st_ref, 0, mean)
        put_rows(st_ref, 8, m2)
        put_rows(st_ref, 16, sum_end(s1))
        put_rows(st_ref, 20, sum_end(s2))
        put_rows(st_ref, 24, count_row(m16_ref, positions))


def back_norm(scale, p, q, dy, z, fill):
    return scale * dy - fill * (p + z * q)


def k_out(sact_ref, sp_ref, cot_ref, df_ref, fact_ref, fb_ref, c2_ref, c3_ref, c4_ref, q4_ref,
          m16_ref, m64_ref, wso_ref, wout_ref,
          out_ref, dy_ref, dfb_ref, gout_ref, up_ref, down_ref, st_ref, s1, s2, s3, t1, t2, gout):
    i = pl.program_id(0)
    s_n, p_n, t_n, _ = sact_ref.shape
    sact = flat(sact_ref[...])
    fill = m16_ref[0:1, :, 0:1]
    wide = 256
    for n in range(wso_ref.shape[1] // wide):
        cols = slice(n * wide, (n + 1) * wide)
        shape = (s_n * p_n, t_n, wide)
        sc = dot(sact, wso_ref[:, cols]).reshape(shape)
        sp = sp_ref[:, :, :, cols].reshape(shape)
        u6 = sc * rows(c4_ref, 2, 2 * n, 2) - rows(c4_ref, 3, 2 * n, 2)
        u7 = sp * rows(c2_ref, 2, 3 + 2 * n, 2) - rows(c2_ref, 3, 3 + 2 * n, 2)
        pre = (
            sc * rows(c4_ref, 0, 2 * n, 2)
            + sp * rows(c2_ref, 0, 3 + 2 * n, 2)
            + (rows(c4_ref, 1, 2 * n, 2) + rows(c2_ref, 1, 3 + 2 * n, 2))
        )
        g = sig(pre)
        y = pre * g
        out_ref[:, :, :, cols] = (y * fill).astype(BF16).reshape(s_n, p_n, t_n, wide)
        d = cot_ref[:, :, :, cols].reshape(shape).astype(F32) * fill * (g + y * (1.0 - g))
        dy_ref[:, :, :, cols] = d.reshape(s_n, p_n, t_n, wide)
        sum_add(i, d, s1, cols)
        sum_add(i, d * u6, s2, cols)
        sum_add(i, d * u7, s3, cols)

    f_n = fact_ref.shape[1]
    fact = flat(fact_ref[...])
    fc = dot(fact, wout_ref[...])
    fill4 = m64_ref[0:1]
    parts = []
    for s in range(s_n):
        cols = slice(s * LANES, (s + 1) * LANES)
        d = back_norm(
            rows(c3_ref, 0, s, 1), rows(q4_ref, 0, s, 1), rows(q4_ref, 1, s, 1),
            df_ref[:, :, cols], fc[:, cols].reshape(p_n, f_n, LANES), fill4,
        )
        parts.append(flat(d).astype(BF16))
    dfc = jnp.concatenate(parts, axis=1)
    add_to(i, gout, dot_tn(fact, dfc))
    z = fb_ref[...]
    back = dot_nt(dfc, wout_ref[...]).reshape(p_n, f_n, LANES) * slope(
        z * rows(c2_ref, 0, 0, 1) + rows(c2_ref, 1, 0, 1)
    )
    dfb_ref[...] = back
    sum_add(i, back, t1)
    sum_add(i, back * (z * rows(c2_ref, 2, 0, 1) - rows(c2_ref, 3, 0, 1)), t2)
    for k, value in enumerate((back, z)):
        value = flat(value)
        for p in range(p_n):
            down_ref[0, k, p : p + 1, :] = value[p * f_n : p * f_n + 1, :]
            up_ref[0, k, p : p + 1, :] = value[p * f_n + f_n - 1 : p * f_n + f_n, :]
        down_ref[0, k, p_n : p_n + 1, :] = m64_ref[0, 0:1, :]
        up_ref[0, k, p_n : p_n + 1, :] = m64_ref[0, f_n - 1 : f_n, :]

    @pl.when(i == STEPS - 1)
    def _():
        zero_ref(st_ref)
        put_rows(st_ref, 0, sum_end(s1))
        put_rows(st_ref, 8, sum_end(s2))
        put_rows(st_ref, 16, sum_end(s3))
        put_rows(st_ref, 24, sum_end(t1))
        put_rows(st_ref, 25, sum_end(t2))
        gout_ref[...] = fold_wide(gout, s_n)


def add_to(step, ref, value):
    ref[...] = jnp.where(step == 0, 0.0, ref[...]) + value


def fold_wide(ref, count):
    a = ref.shape[0] // count
    return sum(ref[s * a : (s + 1) * a, s * LANES : (s + 1) * LANES] for s in range(count))


def fold_lanes(value, count):
    a = value.shape[0] // count
    parts = [value[s * a : (s + 1) * a, :] for s in range(count)]
    return sum(p if s == 0 else pltpu.roll(p, LANES - s * a, 1) for s, p in enumerate(parts))


def k_back_out(x_ref, lact_ref, dy_ref, sp_ref, sact_ref, sb_ref, dfb_ref, fb_ref, fa_ref, ftap_ref, hp_ref, hn_ref,
               c1_ref, c2_ref, c3_ref, c4_ref, q5_ref, m16_ref, m64_ref, wso_ref, wback_ref,
               gw_ref, dsp_ref, dsb_ref, dfa_ref, gmid_ref, st_ref, s1, s2, t1, t2, gsc, gso, gmid):
    i = pl.program_id(0)
    s_n, p_n, t_n, c = sb_ref.shape
    sact = flat(sact_ref[...])
    fill = m16_ref[0:1, :, 0:1]
    wide = 256
    back = None
    turned = jnp.concatenate([flat(x_ref[...]), flat(lact_ref[...])], axis=1).T
    sact_turned = sact.T
    for n in range(wso_ref.shape[1] // wide):
        cols = slice(n * wide, (n + 1) * wide)
        shape = (s_n * p_n, t_n, wide)
        d = dy_ref[:, :, :, cols].reshape(shape)
        sc = dot(sact, wso_ref[:, cols]).reshape(shape)
        dsc = back_norm(rows(c4_ref, 0, 2 * n, 2), rows(q5_ref, 0, 2 * n, 2), rows(q5_ref, 1, 2 * n, 2), d, sc, fill)
        dsc = flat(dsc.astype(BF16))
        old = jnp.where(i == 0, 0.0, gso[:, cols])
        gso[:, cols] = old + dot(sact_turned, dsc)
        sp = sp_ref[:, :, :, cols].reshape(shape)
        dsp = back_norm(
            rows(c2_ref, 0, 3 + 2 * n, 2), rows(q5_ref, 0, 8 + 2 * n, 2), rows(q5_ref, 1, 8 + 2 * n, 2), d, sp, fill
        )
        dsp = flat(dsp.astype(BF16))
        dsp_ref[:, :, :, cols] = dsp.reshape(s_n, p_n, t_n, wide)
        old = jnp.where(i == 0, 0.0, gsc[:, cols])
        gsc[:, cols] = old + dot(turned, dsp)
        part = dot_nt(dsc, wso_ref[:, cols])
        back = part if back is None else back + part
    z = sb_ref[...].reshape(s_n * p_n, t_n, c)
    back = back.reshape(z.shape) * slope(z * rows(c3_ref, 0, 4, 2) + rows(c3_ref, 1, 4, 2))
    dsb_ref[...] = back.reshape(dsb_ref.shape)
    sum_add(i, back, s1)
    sum_add(i, back * (z * rows(c3_ref, 2, 4, 2) - rows(c3_ref, 3, 4, 2)), s2)

    f_n = fb_ref.shape[1]
    scale, p_row, q_row = rows(c2_ref, 0, 0, 1), rows(q5_ref, 0, 16, 1), rows(q5_ref, 1, 16, 1)
    dfb = back_norm(scale, p_row, q_row, dfb_ref[...], fb_ref[...], m64_ref[0:1])
    dfb_low = flat(dfb).astype(BF16)
    add_to(i, gmid, dot_tn(dfb_low, flat(ftap_ref[...])))
    own = dfb_low.astype(F32)
    ends = []
    for ref in (hp_ref, hn_ref):
        small = back_norm(scale, p_row, q_row, ref[0, 0], ref[0, 1], ref[0, 0, p_n : p_n + 1, :])
        small = small.astype(BF16).astype(F32)
        ends.append(
            jnp.concatenate(
                [jnp.broadcast_to(small[p : p + 1, :], (f_n, LANES)) for p in range(p_n)], axis=0
            ).reshape(p_n, f_n, LANES)
        )
    before, after = shifted(own, ends[0], ends[1], f_n)
    taps = jnp.concatenate(
        [flat(after * m64_ref[2:3]), own, flat(before * m64_ref[1:2])], axis=1
    ).astype(BF16)
    z = fa_ref[...]
    back = dot(taps, wback_ref[...]).reshape(z.shape) * slope(
        z * rows(c1_ref, 0, 0, 1) + rows(c1_ref, 1, 0, 1)
    )
    dfa_ref[...] = back
    sum_add(i, back, t1)
    sum_add(i, back * (z * rows(c1_ref, 2, 0, 1) - rows(c1_ref, 3, 0, 1)), t2)

    @pl.when(i == STEPS - 1)
    def _():
        zero_ref(st_ref)
        put_rows(st_ref, 0, sum_end(s1))
        put_rows(st_ref, 2, sum_end(s2))
        put_rows(st_ref, 4, sum_end(t1))
        put_rows(st_ref, 5, sum_end(t2))
        for k in range(3):
            gmid_ref[k * 32 : (k + 1) * 32, :] = fold_lanes(gmid[:, k * LANES : (k + 1) * LANES], s_n)
        tall, low_tall = gsc.shape[0], gso.shape[0]
        blocks = gsc.shape[1] // wide
        for n in range(blocks):
            cols = slice(n * wide, (n + 1) * wide)
            gw_ref[n * tall : (n + 1) * tall, :] = gsc[:, cols].astype(BF16)
            at = blocks * tall + n * low_tall
            gw_ref[at : at + low_tall, :] = gso[:, cols].astype(BF16)


def k_back_spatial(dsb_ref, sb_ref, sa_ref, spad_ref, x_ref, dfa_ref, fa_ref, gout_ref, gmid_ref, c1_ref, c2_ref, c3_ref, q6_ref,
                   m16_ref, m64_ref, wsp_ref,
                   dsa_ref, dlow_ref, gw_ref, gf_ref, st_ref, s1, s2, pad_ref, gsp, gin):
    i = pl.program_id(0)
    h_n, w_n, t_n, c = sb_ref.shape

    @pl.when(i == 0)
    def _():
        scale = rows(c3_ref, 0, 4, 2)
        p_row, q_row = rows(q6_ref, 0, 0, 2), rows(q6_ref, 1, 0, 2)
        zero_ref(pad_ref)

        @pl.loop(0, h_n)
        def _(h):
            d = back_norm(scale, p_row, q_row, dsb_ref[h], sb_ref[h], m16_ref[0:1, :, 0:1])
            pad_ref[h + 1, 1 : w_n + 1] = d.astype(BF16)

    per = h_n // STEPS
    h0 = i * per
    acc = None
    turned = flat(pad_ref[pl.ds(h0 + 1, per), 1 : w_n + 1]).T
    for a in range(3):
        for b in range(3):
            k = 3 * a + b
            patch = flat(spad_ref[pl.ds(h0 + a, per), b : b + w_n])
            cols = slice(k * c, (k + 1) * c)
            gsp[:, cols] = jnp.where(i == 0, 0.0, gsp[:, cols]) + dot(turned, patch)
            block = pad_ref[pl.ds(h0 + 2 - a, per), 2 - b : 2 - b + w_n]
            part = dot_nt(flat(block), wsp_ref[k])
            acc = part if acc is None else acc + part
    z = sa_ref[...].reshape(per * w_n, t_n, c)
    back = acc.reshape(z.shape) * slope(z * rows(c2_ref, 0, 1, 2) + rows(c2_ref, 1, 1, 2))
    dsa_ref[...] = back.reshape(dsa_ref.shape)
    sum_add(i, back, s1)
    sum_add(i, back * (z * rows(c2_ref, 2, 1, 2) - rows(c2_ref, 3, 1, 2)), s2)

    low = back_norm(
        rows(c1_ref, 0, 0, 1), rows(q6_ref, 0, 2, 1), rows(q6_ref, 1, 2, 1), dfa_ref[...], fa_ref[...], m64_ref[0:1]
    ).astype(BF16)
    dlow_ref[...] = low
    packed = jnp.concatenate([flat(x_ref[s]) for s in range(x_ref.shape[0])], axis=1)
    add_to(i, gin, dot_tn(flat(low), packed))

    @pl.when(i == STEPS - 1)
    def _():
        zero_ref(st_ref)
        put_rows(st_ref, 0, sum_end(s1))
        put_rows(st_ref, 2, sum_end(s2))
        for k in range(9):
            gw_ref[k * c : (k + 1) * c, :] = gsp[:, k * c : (k + 1) * c].T.astype(BF16)
        gf_ref[0:32, 0:LANES] = fold_wide(gin, x_ref.shape[0])
        gf_ref[0:32, LANES:] = gout_ref[...]
        gf_ref[32:64, 0:LANES] = gmid_ref[0:32, :]
        gf_ref[32:64, LANES:] = gmid_ref[32:64, :]
        gf_ref[64:96, 0:LANES] = gmid_ref[64:96, :]
        gf_ref[64:96, LANES:] = jnp.zeros((32, LANES), F32)


def k_back_join(x_ref, lact_ref, dsa_ref, sa_ref, dsp_ref, lat_ref, c1_ref, c2_ref, q7_ref, m16_ref, win_ref, wsc_ref,
                gw_ref, gx_ref, dlat_ref, down_ref, st_ref, s1, s2, gsi):
    i = pl.program_id(0)
    s_n, p_n, t_n, c = sa_ref.shape
    shape = (s_n * p_n, t_n, c)
    low = back_norm(
        rows(c2_ref, 0, 1, 2), rows(q7_ref, 0, 0, 2), rows(q7_ref, 1, 0, 2),
        dsa_ref[...].reshape(shape), sa_ref[...].reshape(shape), m16_ref[0:1, :, 0:1],
    ).astype(BF16)
    low = flat(low)
    dsp = flat(dsp_ref[...])
    turned = low.T
    wide = 256
    blocks = win_ref.shape[0] // wide
    for n in range(blocks):
        part = slice(n * wide, (n + 1) * wide)
        joined = flat(x_ref[:, :, :, part] if n < blocks - 1 else lact_ref[...])
        gsi[:, part] = jnp.where(i == 0, 0.0, gsi[:, part]) + dot(turned, joined)
        d = dot_nt(dsp, wsc_ref[part, :]) + dot_nt(low, win_ref[part, :])
        if n < blocks - 1:
            gx_ref[:, :, :, n * wide : (n + 1) * wide] = d.astype(BF16).reshape(s_n, p_n, t_n, wide)
    z = lat_ref[...].reshape(shape)
    back = d.reshape(shape) * slope(z * rows(c1_ref, 0, 1, 2) + rows(c1_ref, 1, 1, 2))
    dlat_ref[...] = back.reshape(dlat_ref.shape)
    sum_add(i, back, s1)
    sum_add(i, back * (z * rows(c1_ref, 2, 1, 2) - rows(c1_ref, 3, 1, 2)), s2)
    fill = jnp.broadcast_to(m16_ref[0, 0:1, 0:1], (1, c))
    for k, value in enumerate((flat(back), flat(z))):
        for s in range(s_n):
            for p in range(p_n):
                r = (s * p_n + p) * t_n
                down_ref[0, k, s, p : p + 1, :] = value[r : r + 1, :]
            down_ref[0, k, s, p_n : p_n + 1, :] = fill

    @pl.when(i == STEPS - 1)
    def _():
        zero_ref(st_ref)
        put_rows(st_ref, 0, sum_end(s1))
        put_rows(st_ref, 2, sum_end(s2))
        for n in range(blocks):
            part = slice(n * wide, (n + 1) * wide)
            gw_ref[part, :] = gsi[:, part].T.astype(BF16)


def k_last(dlat_ref, lat_ref, taps_ref, hn_ref, df_ref, dlow_ref, c1_ref, q8_ref, m16_ref,
           wlat_ref, wfa_ref, gx_ref, gw_ref, gs, glat):
    i = pl.program_id(0)
    s_n, p_n, t_n, c = lat_ref.shape
    shape = (s_n * p_n, t_n, c)
    scale, p_row, q_row = rows(c1_ref, 0, 1, 2), rows(q8_ref, 0, 0, 2), rows(q8_ref, 1, 0, 2)
    low = flat(
        back_norm(scale, p_row, q_row, dlat_ref[...].reshape(shape), lat_ref[...].reshape(shape), m16_ref[0:1, :, 0:1])
    ).astype(BF16)
    add_to(i, glat, dot_tn(low, flat(taps_ref[...])))
    ends = []
    for s in range(s_n):
        small = back_norm(
            scale, p_row, q_row, hn_ref[0, 0, s], hn_ref[0, 1, s], hn_ref[0, 0, s, p_n : p_n + 1, :]
        )
        small = small.astype(BF16).astype(F32)
        ends += [jnp.broadcast_to(small[p : p + 1, :], (t_n, c)) for p in range(p_n)]
    ends = jnp.concatenate(ends, axis=0).reshape(shape)
    n = low.shape[0]
    moved = pltpu.roll(low.astype(F32), n - 1, 0).reshape(shape)
    place = lax.broadcasted_iota(jnp.int32, shape, 1)
    following = flat(jnp.where(place == t_n - 1, ends, moved) * m16_ref[2:3, :, 0:1]).astype(BF16)
    own = dot_nt(low, wlat_ref[2 * LANES : 5 * LANES, :])
    late = dot_nt(following, wlat_ref[0 : 2 * LANES, :])
    gs[pl.ds(0, n, stride=4), :] = own[:, 0:LANES]
    gs[pl.ds(1, n, stride=4), :] = own[:, LANES : 2 * LANES]
    gs[pl.ds(2, n, stride=4), :] = own[:, 2 * LANES :] + late[:, 0:LANES]
    gs[pl.ds(3, n, stride=4), :] = late[:, LANES:]
    back = dot(flat(dlow_ref[...]), wfa_ref[...])
    for s in range(s_n):
        cols = slice(s * LANES, (s + 1) * LANES)
        total = flat(df_ref[:, :, cols]) + back[:, cols] + gs[s * n : (s + 1) * n, :]
        gx_ref[s] = total.astype(BF16).reshape(gx_ref.shape[1:])

    @pl.when(i == STEPS - 1)
    def _():
        for k in range(glat.shape[1] // LANES):
            part = slice(k * LANES, (k + 1) * LANES)
            gw_ref[part, :] = glat[:, part].T.astype(BF16)


def each(first, last, body):
    def step(k, carry):
        body(k)
        return carry
    lax.fori_loop(first, last, step, 0)


NEAR = 4


def reduce_kernel(cfg, *refs):
    offsets, heights, ch, far = cfg
    n_in = len(offsets)
    ins = refs[:n_in]
    (out_ref, x, land_a, buf_b, land_b, buf_c, land_c, acc,
     sem_a, sem_b, sem_c, sem_d, sem_e, sem_f) = refs[n_in:]
    me_p, me_f = lax.axis_index("path"), lax.axis_index("frames")
    me_q, me_r = lax.rem(me_f, NEAR), lax.div(me_f, NEAR)
    other = 1 - me_p

    def at(path, q, r):
        return pl.ds(pl.multiple_of(((path * NEAR + q) * far + r) * ch, 16), ch)

    def q_of(k):
        return lax.rem(me_q + k, NEAR)

    def r_of(k):
        return lax.rem(me_r + k, far)

    barrier = pltpu.get_barrier_semaphore()
    pl.semaphore_signal(barrier, inc=1, device_id=(other, me_f), device_id_type=MESH)
    each(1, NEAR, lambda k: pl.semaphore_signal(
        barrier, inc=1, device_id=(me_p, me_r * NEAR + q_of(k)), device_id_type=MESH))
    each(1, far, lambda k: pl.semaphore_signal(
        barrier, inc=1, device_id=(me_p, r_of(k) * NEAR + me_q), device_id_type=MESH))
    end = 0
    for ref, off, height in zip(ins, offsets, heights):
        x[off : off + height, :] = ref[...].astype(BF16)
        end = off + height
    if end < x.shape[0]:
        x[end:, :] = jnp.zeros((x.shape[0] - end, x.shape[1]), BF16)
    pl.semaphore_wait(barrier, NEAR + far - 1)

    def copy(src, dst, sem, index, device):
        return pltpu.make_async_remote_copy(
            src_ref=src, dst_ref=dst, send_sem=sem.at[(0, *index)], recv_sem=sem.at[(1, *index)],
            device_id=device, device_id_type=MESH)

    sibling = (other, me_f)

    def pair(k, m):
        return copy(x.at[at(other, q_of(k), r_of(m + 1))], land_a.at[k, m], sem_a, (k, m), sibling)

    def plane(k, m):
        return copy(buf_b.at[k, m], land_b.at[k, m], sem_b, (k, m), (me_p, me_r * NEAR + q_of(k)))

    def line(m):
        return copy(buf_c.at[m], land_c.at[m], sem_c, (m,), (me_p, r_of(m + 1) * NEAR + me_q))

    def own(q, r):
        return out_ref.at[at(me_p, q, r)]

    def line_back(k):
        return copy(own(me_q, me_r), own(me_q, me_r), sem_d, (k,), (me_p, r_of(k) * NEAR + me_q))

    def plane_back(k, m):
        part = own(me_q, r_of(far - m))
        return copy(part, part, sem_e, (k, m), (me_p, me_r * NEAR + q_of(k)))

    def pair_back(k, m):
        part = own(q_of(NEAR - k), r_of(far - m))
        return copy(part, part, sem_f, (k, m), sibling)

    def both(body, first=0):
        each(0, far, lambda m: each(first, NEAR, lambda k: body(k, m)))

    def start_pair(m):
        each(1, NEAR, lambda k: pair(k, m).start())
        pair(0, m).start()

    each(0, far, start_pair)

    def add_pair(k, m):
        pair(k, m).wait_recv()
        buf_b[k, m] = (x[at(me_p, q_of(k), r_of(m + 1)), :].astype(F32) + land_a[k, m].astype(F32)).astype(BF16)
        plane(k, m).start()

    both(add_pair, 1)

    def add_plane(m):
        pair(0, m).wait_recv()
        acc[...] = x[at(me_p, me_q, r_of(m + 1)), :].astype(F32) + land_a[0, m].astype(F32)

        def more(k):
            plane(k, m).wait_recv()
            acc[...] += land_b[k, m].astype(F32)

        each(1, NEAR, more)

    def send_line(m):
        add_plane(m)
        buf_c[m] = acc[...].astype(BF16)
        line(m).start()

    each(0, far - 1, send_line)
    add_plane(far - 1)

    def add_line(m):
        line(m).wait_recv()
        acc[...] += land_c[m].astype(F32)

    each(0, far - 1, add_line)
    out_ref[at(me_p, me_q, me_r), :] = acc[...].astype(BF16)
    each(1, far, lambda k: line_back(k).start())

    def share(m):
        each(1, NEAR, lambda k: plane_back(k, m).start())
        pair_back(0, m).start()

    share(0)

    def relay(m):
        line_back(m).wait_recv()
        share(m)

    each(1, far, relay)

    def hand_on(k, m):
        plane_back(k, m).wait_recv()
        pair_back(k, m).start()

    both(hand_on, 1)
    both(lambda k, m: pair_back(k, m).wait())
    both(lambda k, m: pair(k, m).wait_send())
    both(lambda k, m: plane(k, m).wait_send(), 1)
    each(0, far - 1, lambda m: line(m).wait_send())
    each(1, far, lambda k: line_back(k).wait_send())
    both(lambda k, m: plane_back(k, m).wait_send(), 1)


def reduce_all(sizes, cid, parts):
    paths, length = sizes
    far = length // NEAR
    unit = 16 * paths * length
    heights = tuple(p.shape[0] for p in parts)
    offsets = tuple(sum(heights[:k]) for k in range(len(parts)))
    total = -(-sum(heights) // unit) * unit
    ch = total // (paths * length)
    vm = pl.BlockSpec(memory_space=pltpu.VMEM)
    width = parts[0].shape[1]
    quad = pltpu.VMEM((NEAR, far, ch, width), BF16)
    single = pltpu.VMEM((far, ch, width), BF16)
    out = pl.pallas_call(
        functools.partial(reduce_kernel, (offsets, heights, ch, far)),
        out_shape=jax.ShapeDtypeStruct((total, width), BF16),
        in_specs=[vm] * len(parts),
        out_specs=vm,
        scratch_shapes=[
            pltpu.VMEM((total, width), BF16), quad, quad, quad, single, single,
            pltpu.VMEM((ch, width), F32),
            *[pltpu.SemaphoreType.DMA((2, NEAR, far))] * 2,
            *[pltpu.SemaphoreType.DMA((2, far))] * 2,
            *[pltpu.SemaphoreType.DMA((2, NEAR, far))] * 2,
        ],
        compiler_params=pltpu.CompilerParams(collective_id=cid, has_side_effects=True, vmem_limit_bytes=VMEM_LIMIT),
        name=f"reduce_{cid}",
    )(*parts)
    return [out[o : o + h] for o, h in zip(offsets, heights)]


def k_prep(x_hbm, fill_ref, clip_ref, norm_ref, wfi_ref, wfm_ref, wfo_ref,
           tail_ref, gb_ref, m16_ref, m64_ref, wfa_ref, wmid_ref, wback_ref, wout_ref,
           near, rows_f, sent, land, sems, local):
    length = lax.axis_size("frames")
    total = lax.axis_size("path") * length
    me = lax.axis_index("path") * length + lax.axis_index("frames")

    def place(index):
        return (lax.div(index, length), lax.rem(index, length))

    nxt, prv = place(lax.rem(me + 1, total)), place(lax.rem(me + total - 1, total))
    barrier = pltpu.get_barrier_semaphore()
    pl.semaphore_signal(barrier, inc=1, device_id=nxt, device_id_type=MESH)
    pl.semaphore_signal(barrier, inc=1, device_id=prv, device_id_type=MESH)
    s_n, inner, t_n, c = near.shape
    f_n = x_hbm.shape[2]
    fetch = pltpu.make_async_copy(x_hbm.at[:, :, pl.ds(f_n - t_n, t_n), :], near, local)
    fetch.start()
    fetch.wait()
    p_n = inner // STEPS
    rows_f[...] = near[...].reshape(rows_f.shape).astype(F32)
    zero_ref(sent)
    count = s_n * inner
    for k in range(2):
        line = rows_f[pl.ds(t_n - 2 + k, count, stride=t_n), :]
        for s in range(s_n):
            for step in range(STEPS):
                at = s * inner + step * p_n
                sent[step, s, 0:p_n, k * c : (k + 1) * c] = line[at : at + p_n, :]
    pl.semaphore_wait(barrier, 2)
    copy = pltpu.make_async_remote_copy(
        src_ref=sent, dst_ref=land, send_sem=sems.at[0], recv_sem=sems.at[1], device_id=nxt, device_id_type=MESH
    )
    copy.start()

    lane = lax.broadcasted_iota(jnp.int32, (1, LANES), 1)
    for k in range(2):
        half = pltpu.roll(norm_ref[k], LANES // 2, 1)
        main = jnp.where(lane < LANES // 2, half[0:23], half[1:24])
        for j in range(2):
            v = jnp.where(lane // 32 == j, norm_ref[k, 0:1, :], 0.0)
            v = v + pltpu.roll(v, 64, 1)
            gb_ref[k, j : j + 1, :] = v + pltpu.roll(v, 32, 1)
        for j in range(4):
            gb_ref[k, 2 + j : 3 + j, :] = main[0:1]
        gb_ref[k, 6:28, :] = main[1:23]
        gb_ref[k, 28:32, :] = jnp.zeros((4, LANES), F32)

    def row(value):
        return jnp.full((1, LANES), value, F32)

    last = jnp.where(me < total - 1, 1.0, 0.0)
    link = [jnp.where(clip_ref[t] >= 1, 1.0, 0.0) for t in range(t_n)]
    for t in range(t_n):
        filled = row(fill_ref[t].astype(F32))
        after = row(link[t + 1] if t + 1 < t_n else last)
        m16_ref[0, t : t + 1, :] = filled
        m16_ref[1, t : t + 1, :] = row(link[t])
        m16_ref[2, t : t + 1, :] = after
        m64_ref[0, 4 * t : 4 * t + 4, :] = jnp.broadcast_to(filled, (4, LANES))
        m64_ref[1, 4 * t : 4 * t + 1, :] = row(link[t])
        m64_ref[1, 4 * t + 1 : 4 * t + 4, :] = jnp.ones((3, LANES), F32)
        m64_ref[2, 4 * t : 4 * t + 3, :] = jnp.ones((3, LANES), F32)
        m64_ref[2, 4 * t + 3 : 4 * t + 4, :] = after

    zero_ref(wfa_ref)
    zero_ref(wout_ref)
    a = wfi_ref.shape[0]
    for s in range(s_n):
        wfa_ref[s * a : (s + 1) * a, s * LANES : (s + 1) * LANES] = wfi_ref[...]
        wout_ref[s * a : (s + 1) * a, s * LANES : (s + 1) * LANES] = wfo_ref[...]
    tall = (LANES, a)
    spread = (lax.broadcasted_iota(jnp.int32, tall, 0) % a == lax.broadcasted_iota(jnp.int32, tall, 1)).astype(BF16)
    square = (LANES, LANES)
    diag = lax.broadcasted_iota(jnp.int32, square, 0) // a == lax.broadcasted_iota(jnp.int32, square, 1) // a
    for k in range(3):
        left = dot(spread, wfm_ref[k]).astype(BF16)
        wmid_ref[k * LANES : (k + 1) * LANES, :] = jnp.where(diag, dot_nt(left, spread), 0.0).astype(BF16)
        right = dot_nt(spread, wfm_ref[k]).astype(BF16)
        wback_ref[k * LANES : (k + 1) * LANES, :] = jnp.where(diag, dot_nt(right, spread), 0.0).astype(BF16)
    copy.wait()
    tail_ref[...] = land[...]


def prepare(x_fast, fill, clip_offset, norms, w_fast_in, w_fast_mid, w_fast_out):
    s_n, inner, f_n, c = x_fast.shape
    t_n = fill.shape[0]
    p_n = inner // STEPS
    vm = pl.BlockSpec(memory_space=pltpu.VMEM)
    sm = pl.BlockSpec(memory_space=pltpu.SMEM)
    tail = (STEPS, s_n, 8, 2 * c)
    outs = [(tail, F32), ((2, 32, LANES), F32), ((3, t_n, LANES), F32), ((3, f_n, LANES), F32),
            ((LANES, s_n * c), BF16), ((3 * LANES, LANES), BF16), ((3 * LANES, LANES), BF16), ((LANES, s_n * c), BF16)]
    return pl.pallas_call(
        k_prep,
        out_shape=[jax.ShapeDtypeStruct(s, d) for s, d in outs],
        in_specs=[pl.BlockSpec(memory_space=pl.ANY), sm, sm, vm, vm, vm, vm],
        out_specs=[vm] * len(outs),
        scratch_shapes=[
            pltpu.VMEM((s_n, inner, t_n, c), BF16),
            pltpu.VMEM((s_n * inner * t_n, c), F32),
            pltpu.VMEM(tail, F32),
            pltpu.VMEM(tail, F32),
            pltpu.SemaphoreType.DMA((2,)),
            pltpu.SemaphoreType.DMA,
        ],
        compiler_params=pltpu.CompilerParams(collective_id=10, has_side_effects=True, vmem_limit_bytes=VMEM_LIMIT),
        name="prepare",
    )(x_fast, fill, clip_offset, norms, w_fast_in.T, w_fast_mid, w_fast_out)


def per_device(slow_input, fast_input, clip_offset, fill, w_fast_in, w_fast_mid, w_fast_out, w_lateral,
               w_slow_in, w_slow_mid, w_slow_out, w_shortcut, gains, biases, slow_cot, fast_cot):
    sizes = (lax.axis_size("path"), lax.axis_size("frames"))
    t_n, side, _, c_slow = slow_input.shape
    f_n, c_fast = fast_input.shape[0], fast_input.shape[3]
    in_fast, in_slow, c_lat = w_fast_in.shape[1], w_slow_in.shape[1], w_lateral.shape[2]
    pixels = side * side
    groups = LANES // in_fast
    inner = pixels // groups
    p_n = inner // STEPS

    def slow_view(a):
        return jnp.transpose(a, (1, 2, 0, 3)).reshape(groups, inner, t_n, a.shape[3])

    def fast_view(a):
        return jnp.transpose(a, (1, 2, 0, 3)).reshape(groups, inner, f_n, a.shape[3])

    def unview(a):
        return jnp.transpose(a.reshape(side, side, a.shape[2], a.shape[3]), (2, 0, 1, 3))

    x_slow, cot_slow = slow_view(slow_input), slow_view(slow_cot)
    x_fast, cot_fast = fast_view(fast_input), fast_view(fast_cot)

    norms = jnp.stack([gains, biases])
    norms = jnp.pad(norms, ((0, 0), (0, -norms.shape[1] % (8 * LANES)))).reshape(2, -1, LANES)
    tail, gb, m16, m64, wfa, wmid, wback, wout = prepare(
        x_fast, fill, clip_offset, norms, w_fast_in, w_fast_mid, w_fast_out
    )
    wlat = w_lateral.reshape(-1, c_lat)
    wsp = w_slow_mid.reshape(9, in_slow, in_slow)

    sl = (groups, inner, t_n)
    fp = (inner, f_n)

    def slow_out(width, dtype):
        return out_blocked(sl + (width,), dtype, 1, p_n)

    def fast_out(width, dtype):
        return out_blocked(fp + (width,), dtype, 0, p_n)

    def sb_(a):
        return blocked(a, 1, p_n)

    def fb_(a):
        return blocked(a, 0, p_n)

    def stat(n):
        return out_whole((pad8(n), LANES), F32)

    def acc(rows_n, width, count):
        return [pltpu.VMEM((rows_n, width), F32)] * count

    halo_small = out_blocked((STEPS, 8, LANES), F32, 0, 1)

    fa, lat, taps, st, up, down = call(
        k_first,
        [sb_(x_fast), blocked(tail, 0, 1), whole(m16), whole(m64), whole(wfa), whole(wlat)],
        [fast_out(LANES, F32), slow_out(c_lat, F32), slow_out(5 * c_fast, BF16), stat(7), halo_small, halo_small],
        [pltpu.VMEM((groups * p_n * f_n, c_fast), F32), *acc(f_n, LANES, 2), *acc(t_n, c_lat, 2)],
        "first",
    )
    c1, hp, hn = exchange(sizes, 1, st, gb, fwd=(("lane4", 0, 1), ("plain", 6, 2)), up=up, down=down)

    lact, ftap, sa, sp, fb, st = call(
        k_join,
        [sb_(x_slow), sb_(lat), fb_(fa), blocked(hp, 0, 1), blocked(hn, 0, 1), whole(c1), whole(m16), whole(m64),
         whole(w_slow_in), whole(w_shortcut), whole(wmid)],
        [slow_out(c_lat, BF16), fast_out(3 * LANES, BF16), slow_out(in_slow, F32), slow_out(c_slow, F32),
         fast_out(LANES, F32), stat(23)],
        [*acc(t_n, in_slow, 2), *acc(t_n, c_slow, 2), *acc(f_n, LANES, 2)],
        "join",
    )
    (c2,) = exchange(sizes, 2, st, gb, fwd=(("lane4", 1, 1), ("plain", 8, 2), ("plain", 20, 8)))

    rows_n = side // STEPS
    pad, sb, fact, st = call(
        k_spatial,
        [whole(sa.reshape(side, side, t_n, in_slow)),
         fb_(fb), whole(c2), whole(m16), whole(m64), whole(wsp), whole(wout)],
        [out_whole((side + 2, side + 2, t_n, in_slow), BF16),
         out_blocked((side, side, t_n, in_slow), F32, 0, rows_n), fast_out(LANES, BF16), stat(13)],
        [*acc(t_n, in_slow, 2), *acc(f_n, groups * c_fast, 2)],
        "spatial",
    )
    (c3,) = exchange(sizes, 3, st, gb, fwd=(("row4", 2, 4), ("plain", 10, 2)))

    sb4 = sb.reshape(sl + (in_slow,))
    sact, fast_y, df, st = call(
        k_expand,
        [sb_(sb4), fb_(fact), sb_(x_fast), sb_(cot_fast), whole(c3), whole(m16), whole(m64), whole(w_slow_out), whole(wout)],
        [slow_out(in_slow, BF16), out_blocked((groups, inner, f_n, c_fast), BF16, 1, p_n),
         fast_out(groups * c_fast, F32), stat(25)],
        [*acc(t_n, c_slow, 2), *acc(f_n, groups * c_fast, 2)],
        "expand",
    )
    c4, q4 = exchange(sizes, 4, st, gb, fwd=(("plain", 12, 8),), bwd=(("row4", 0, 0, 2, 4, 0, 4),), coefs=(c3,))

    halo_pair = out_blocked((STEPS, 2, 8, LANES), F32, 0, 1)
    slow_y, dy, dfb, g_fout, up, down, st = call(
        k_out,
        [sb_(sact), sb_(sp), sb_(cot_slow), fb_(df), fb_(fact), fb_(fb), whole(c2), whole(c3), whole(c4), whole(q4),
         whole(m16), whole(m64), whole(w_slow_out), whole(wout)],
        [slow_out(c_slow, BF16), slow_out(c_slow, F32), fast_out(LANES, F32),
         out_whole((in_fast, c_fast), F32), halo_pair, halo_pair, stat(26)],
        [*acc(t_n, c_slow, 3), *acc(f_n, LANES, 2), *acc(LANES, groups * c_fast, 1)],
        "out",
    )
    q5, hp, hn = exchange(
        sizes, 5, st, gb,
        bwd=(("plain", 0, 0, 12, 8, 0, 8), ("plain", 1, 3, 20, 8, 0, 16), ("lane4", 1, 0, 1, 1, 24, 25)),
        coefs=(c4, c2), up=up, down=down,
    )

    c_cat = w_slow_in.shape[0]
    gw_out, dsp, dsb, dfa, g_fmid, st = call(
        k_back_out,
        [sb_(x_slow), sb_(lact), sb_(dy), sb_(sp), sb_(sact), sb_(sb4), fb_(dfb), fb_(fb), fb_(fa), fb_(ftap), blocked(hp, 0, 1), blocked(hn, 0, 1),
         whole(c1), whole(c2), whole(c3), whole(c4), whole(q5), whole(m16), whole(m64), whole(w_slow_out), whole(wback)],
        [out_whole(((c_cat + in_slow) * c_slow // in_slow, in_slow), BF16), slow_out(c_slow, BF16),
         slow_out(in_slow, F32), fast_out(LANES, F32), out_whole((3 * in_fast, LANES), F32), stat(6)],
        [*acc(t_n, in_slow, 2), *acc(f_n, LANES, 2), *acc(c_cat, c_slow, 1), *acc(in_slow, c_slow, 1),
         *acc(LANES, 3 * LANES, 1)],
        "back_out",
    )
    (q6,) = exchange(
        sizes, 6, st, gb, bwd=(("plain", 0, 4, 10, 2, 0, 2), ("lane4", 1, 0, 0, 1, 4, 5)), coefs=(c3, c1)
    )

    grid = (side, side, t_n, in_slow)
    dsa, dfa_low, gw_mid, gw_fast, st = call(
        k_back_spatial,
        [whole(dsb.reshape(grid)), whole(sb), blocked(sa.reshape(grid), 0, rows_n), whole(pad), sb_(x_fast), fb_(dfa), fb_(fa),
         whole(g_fout), whole(g_fmid), whole(c1), whole(c2), whole(c3), whole(q6), whole(m16), whole(m64), whole(wsp)],
        [out_blocked(grid, F32, 0, rows_n), fast_out(LANES, BF16), out_whole((9 * in_slow, in_slow), BF16),
         out_whole((3 * in_fast, 2 * LANES), F32), stat(4)],
        [*acc(t_n, in_slow, 2), pltpu.VMEM((side + 2, side + 2, t_n, in_slow), BF16), *acc(in_slow, 9 * in_slow, 1),
         *acc(LANES, groups * c_fast, 1)],
        "back_spatial",
    )
    (q7,) = exchange(sizes, 7, st, gb, bwd=(("plain", 0, 1, 8, 2, 0, 2),), coefs=(c2,))

    gw_in, slow_gx, dlat, down, st = call(
        k_back_join,
        [sb_(x_slow), sb_(lact), sb_(dsa.reshape(sl + (in_slow,))), sb_(sa), sb_(dsp), sb_(lat), whole(c1), whole(c2), whole(q7), whole(m16),
         whole(w_slow_in), whole(w_shortcut)],
        [out_whole((c_cat, in_slow), BF16), slow_out(c_slow, BF16), slow_out(c_lat, F32),
         out_blocked((STEPS, 2, groups, 8, c_lat), F32, 0, 1), stat(4)],
        [*acc(t_n, c_lat, 2), *acc(in_slow, c_cat, 1)],
        "back_join",
    )
    q8, hn = exchange(sizes, 8, st, gb, bwd=(("plain", 0, 1, 6, 2, 0, 2),), coefs=(c1,), down=down)

    fast_gx, gw_lat = call(
        k_last,
        [sb_(dlat), sb_(lat), sb_(taps), blocked(hn, 0, 1), fb_(df), fb_(dfa_low), whole(c1), whole(q8), whole(m16),
         whole(wlat), whole(wfa)],
        [out_blocked((groups, inner, f_n, c_fast), BF16, 1, p_n), out_whole((5 * c_fast, c_lat), BF16)],
        [pltpu.VMEM((groups * p_n * f_n, c_fast), F32), *acc(c_lat, 5 * c_fast, 1)],
        "last",
    )

    gw_out, gw_mid, gw_in, gw_lat, gw_fast = [
        g.astype(F32) for g in reduce_all(sizes, 9, [gw_out, gw_mid, gw_in, gw_lat, gw_fast])
    ]
    blocks = c_slow // in_slow
    g_short, g_sout = [
        jnp.transpose(g.reshape(blocks, -1, in_slow), (1, 0, 2)).reshape(-1, c_slow)
        for g in (gw_out[: blocks * c_cat], gw_out[blocks * c_cat :])
    ]
    taps_t = [gw_fast[in_fast : 2 * in_fast, :in_fast], gw_fast[in_fast : 2 * in_fast, c_fast : c_fast + in_fast],
              gw_fast[2 * in_fast :, :in_fast]]
    grads = (
        gw_fast[:in_fast, :c_fast].T,
        jnp.transpose(jnp.stack(taps_t), (0, 2, 1)),
        gw_fast[:in_fast, c_fast:],
        gw_lat.reshape(w_lateral.shape),
        gw_in,
        gw_mid.reshape(w_slow_mid.shape),
        g_sout,
        g_short,
    )

    def norm_grads(slab):
        def row(q, at, n):
            return q[slab, at : at + n].reshape(-1)

        return jnp.concatenate(
            [row(q6, 2, 1)[:in_fast], row(q5, 16, 1)[:in_fast], row(q4, 0, 1), row(q8, 0, 2), row(q7, 0, 2),
             row(q6, 0, 2), row(q5, 0, 8), row(q5, 8, 8)]
        )

    return (
        unview(slow_y),
        unview(fast_y),
        unview(slow_gx),
        unview(fast_gx),
        *grads,
        norm_grads(3),
        norm_grads(2),
    )


def solution(mesh):
    frames = P(("path", "frames"), None, None, None)
    in_specs = (frames, frames, P(AXES), P(AXES), *([P()] * 10), frames, frames)
    out_specs = (*([frames] * 4), *([P()] * 10))
    return jax.shard_map(per_device, mesh=mesh, in_specs=in_specs, out_specs=out_specs, check_vma=False)
```

```python
import functools

import jax
import jax.numpy as jnp
from jax import lax
from jax.experimental import pallas as pl
from jax.experimental.pallas import tpu as pltpu
from jax.sharding import PartitionSpec as P

norm_eps = 1e-05
F32 = jnp.float32
BF16 = jnp.bfloat16
MESH = pl.DeviceIdType.MESH
AXES = ("path", "frames")
STEPS = 7
LANES = 128
VMEM_LIMIT = 56 * 1024 * 1024


def dot(a, b):
    return jnp.dot(a, b, preferred_element_type=F32)


def dot_nt(a, b):
    return lax.dot_general(a, b, (((1,), (1,)), ((), ())), preferred_element_type=F32)


def dot_tn(a, b):
    return lax.dot_general(a, b, (((0,), (0,)), ((), ())), preferred_element_type=F32)


def sig(v):
    return 0.5 * jnp.tanh(0.5 * v) + 0.5


def slope(v):
    s = sig(v)
    return s + (v * s) * (1.0 - s)


def rows(ref, slab, first, count):
    parts = [ref[slab, first + j : first + j + 1, :] for j in range(count)]
    return parts[0] if count == 1 else jnp.concatenate(parts, axis=1)


def put_rows(ref, first, value):
    for j in range(value.shape[1] // LANES):
        ref[first + j : first + j + 1, :] = value[:, j * LANES : (j + 1) * LANES]


def zero_ref(ref):
    ref[...] = jnp.zeros(ref.shape, ref.dtype)


def spread_add(step, z, mean_ref, m2_ref, cols=slice(None)):
    count = z.shape[0]
    mean = jnp.sum(z, axis=0) * (1.0 / count)
    d = z - mean
    m2 = jnp.sum(d * d, axis=0)
    first = step == 0
    old_mean = jnp.where(first, 0.0, mean_ref[:, cols])
    old_m2 = jnp.where(first, 0.0, m2_ref[:, cols])
    done = jnp.full((1, z.shape[-1]), step, jnp.int32).astype(F32)
    share = 1.0 / (done + 1.0)
    delta = mean - old_mean
    mean_ref[:, cols] = old_mean + delta * share
    m2_ref[:, cols] = old_m2 + m2 + delta * delta * (done * share * count)


def spread_end(mean_ref, m2_ref, fill, positions):
    filled = jnp.sum(fill, axis=0, keepdims=True)
    mean = jnp.sum(fill * mean_ref[...], axis=0, keepdims=True) / jnp.maximum(filled, 1.0)
    d = mean_ref[...] - mean
    m2 = jnp.sum(fill * (m2_ref[...] + positions * (d * d)), axis=0, keepdims=True)
    return mean, m2


def sum_add(step, value, ref, cols=slice(None)):
    ref[:, cols] = jnp.where(step == 0, 0.0, ref[:, cols]) + jnp.sum(value, axis=0)


def sum_end(ref):
    return jnp.sum(ref[...], axis=0, keepdims=True)


def pad8(n):
    return -(-n // 8) * 8


def exchange_peers(cfg):
    paths, length = lax.axis_size("path"), lax.axis_size("frames")
    near = 4
    g1, g2 = paths * near, length // near
    me_p, me_f = lax.axis_index("path"), lax.axis_index("frames")
    me = me_p * length + me_f
    total = paths * length
    r1 = me_p * near + lax.rem(me_f, near)
    r2 = lax.div(me_f, near)

    def peer1(k):
        r = lax.rem(r1 + k, g1)
        return (lax.div(r, near), r2 * near + lax.rem(r, near))

    def peer2(k):
        r = lax.rem(r2 + k, g2)
        return (me_p, r * near + lax.rem(me_f, near))

    def split(index):
        return (lax.div(index, length), lax.rem(index, length))

    nxt, prv = split(lax.rem(me + 1, total)), split(lax.rem(me + total - 1, total))
    return g1, g2, r1, r2, peer1, peer2, nxt, prv


def exchange_hello(cfg):
    g1, g2, _, _, peer1, peer2, nxt, prv = exchange_peers(cfg)
    peers = [peer1(k) for k in range(1, g1)] + [peer2(k) for k in range(1, g2)]
    if cfg.up or cfg.down:
        peers += [nxt, prv]
    for peer in peers:
        pl.semaphore_signal(pltpu.get_barrier_semaphore(), inc=1, device_id=peer, device_id_type=MESH)
    return len(peers)


def exchange_run(cfg, ins, outs, scratch, meanwhile=None):
    fwd, bwd = cfg.fwd, cfg.bwd
    nf = sum(c[2] for c in fwd)
    nb = max((c[6] + c[4] for c in bwd), default=0)
    n_row = 2 * nf + nb
    stats_ref, up_ref, down_ref = scratch[:3]
    gb_ref, *coef_refs = ins
    outs = list(outs)
    coef_out = outs.pop(0) if nf else None
    pq_out = outs.pop(0) if nb else None
    from_prev = outs.pop(0) if cfg.up else None
    from_next = outs.pop(0) if cfg.down else None
    slots1, slots2, mid, tot, send1, recv1, send2, recv2, up_land, up_sems, down_land, down_sems = scratch[3:]
    g1, g2, r1, r2, peer1, peer2, nxt, prv = exchange_peers(cfg)

    halos = []
    copies = []
    for k in range(1, g1):
        copies.append(
            pltpu.make_async_remote_copy(
                src_ref=stats_ref,
                dst_ref=slots1.at[r1],
                send_sem=send1.at[k],
                recv_sem=recv1.at[k],
                device_id=peer1(k),
                device_id_type=MESH,
            )
        )
        copies[-1].start()
    for used, src, land, sems, peer in (
        (cfg.up, up_ref, up_land, up_sems, nxt),
        (cfg.down, down_ref, down_land, down_sems, prv),
    ):
        if used:
            halos.append(
                pltpu.make_async_remote_copy(
                    src_ref=src,
                    dst_ref=land,
                    send_sem=sems.at[0],
                    recv_sem=sems.at[1],
                    device_id=peer,
                    device_id_type=MESH,
                )
            )
            halos[-1].start()
    slots1[r1] = stats_ref[...]
    if meanwhile is not None:
        meanwhile()
    for c in copies:
        c.wait_recv()

    def combine(slots, count, out):
        if nf:
            n = slots[0, n_row : n_row + 1, :]
            for g in range(1, count):
                n = n + slots[g, n_row : n_row + 1, :]
            acc = slots[0, n_row : n_row + 1, :] * slots[0, 0:nf, :]
            for g in range(1, count):
                acc = acc + slots[g, n_row : n_row + 1, :] * slots[g, 0:nf, :]
            mean = acc / jnp.maximum(n, 1.0)
            m2 = None
            for g in range(count):
                d = slots[g, 0:nf, :] - mean
                part = slots[g, nf : 2 * nf, :] + slots[g, n_row : n_row + 1, :] * (d * d)
                m2 = part if m2 is None else m2 + part
            out[0:nf, :] = mean
            out[nf : 2 * nf, :] = m2
            out[n_row : n_row + 1, :] = n
        if nb:
            acc = slots[0, 2 * nf : n_row, :]
            for g in range(1, count):
                acc = acc + slots[g, 2 * nf : n_row, :]
            out[2 * nf : n_row, :] = acc

    zero_ref(mid)
    combine(slots1, g1, mid)
    copies2 = []
    for k in range(1, g2):
        copies2.append(
            pltpu.make_async_remote_copy(
                src_ref=mid,
                dst_ref=slots2.at[r2],
                send_sem=send2.at[k],
                recv_sem=recv2.at[k],
                device_id=peer2(k),
                device_id_type=MESH,
            )
        )
        copies2[-1].start()
    slots2[r2] = mid[...]
    for c in copies2:
        c.wait_recv()
    combine(slots2, g2, tot)

    def lanes4(v):
        w = v + pltpu.roll(v, 64, 1)
        return w + pltpu.roll(w, 32, 1)

    at = 0
    for kind, g_row, count in fwd:
        n = tot[n_row : n_row + 1, :]
        mean = tot[at : at + count, :]
        m2 = tot[nf + at : nf + at + count, :]
        if kind == "lane4":
            whole = lanes4(mean) * 0.25
            d = mean - whole
            var = lanes4(m2 + n * (d * d)) / (4.0 * n)
            mean = whole
        elif kind == "row4":
            whole = jnp.sum(mean, axis=0, keepdims=True) * 0.25
            d = mean - whole
            var = jnp.sum(m2 + n * (d * d), axis=0, keepdims=True) / (4.0 * n)
            var = jnp.broadcast_to(var, (count, LANES))
            mean = jnp.broadcast_to(whole, (count, LANES))
        else:
            var = m2 / n
        inv = lax.rsqrt(var + norm_eps)
        scale = inv * gb_ref[0, g_row : g_row + count, :]
        coef_out[0, at : at + count, :] = scale
        coef_out[1, at : at + count, :] = gb_ref[1, g_row : g_row + count, :] - mean * scale
        coef_out[2, at : at + count, :] = inv
        coef_out[3, at : at + count, :] = mean * inv
        coef_out[4, at : at + count, :] = jnp.broadcast_to(n, (count, LANES))
        at += count
    at = 0
    for kind, coef, row, _, count, db_at, dg_at in bwd:
        db = tot[2 * nf + db_at : 2 * nf + db_at + count, :]
        dg = tot[2 * nf + dg_at : 2 * nf + dg_at + count, :]
        c = coef_refs[coef]
        scale, inv = c[0, row : row + count, :], c[2, row : row + count, :]
        mi, n = c[3, row : row + count, :], c[4, row : row + count, :]
        if kind == "lane4":
            db, dg, n = lanes4(db), lanes4(dg), 4.0 * n
        elif kind == "row4":
            db = jnp.broadcast_to(jnp.sum(db, axis=0, keepdims=True), (count, LANES))
            dg = jnp.broadcast_to(jnp.sum(dg, axis=0, keepdims=True), (count, LANES))
            n = 4.0 * n
        pq_out[0, at : at + count, :] = scale / n * (db - mi * dg)
        pq_out[1, at : at + count, :] = scale / n * inv * dg
        pq_out[2, at : at + count, :] = db
        pq_out[3, at : at + count, :] = dg
        at += count

    for c in halos:
        c.wait()
    if cfg.up:
        from_prev[...] = up_land[...]
    if cfg.down:
        from_next[...] = down_land[...]
    for c in copies:
        c.wait_send()
    for c in copies2:
        c.wait_send()


class Exchange:
    def __init__(self, sizes, cid, rows_n, fwd=(), bwd=(), up=None, down=None):
        self.cid, self.fwd, self.bwd, self.up, self.down = cid, fwd, bwd, up, down
        g1, g2, r = sizes[0] * 4, sizes[1] // 4, pad8(rows_n)
        self.outs = []
        nf, nn = sum(c[2] for c in fwd), sum(c[4] for c in bwd)
        if nf:
            self.outs.append(((5, nf, LANES), F32))
        if nn:
            self.outs.append(((4, nn, LANES), F32))
        self.outs += [(h, F32) for h in (up, down) if h]
        none = (8, LANES)
        self.stats = (r, LANES)
        self.work = [
            pltpu.VMEM((g1, r, LANES), F32),
            pltpu.VMEM((g2, r, LANES), F32),
            pltpu.VMEM((r, LANES), F32),
            pltpu.VMEM((r, LANES), F32),
            pltpu.SemaphoreType.DMA((g1,)),
            pltpu.SemaphoreType.DMA((g1,)),
            pltpu.SemaphoreType.DMA((g2,)),
            pltpu.SemaphoreType.DMA((g2,)),
            pltpu.VMEM(up or none, F32),
            pltpu.SemaphoreType.DMA((2,)),
            pltpu.VMEM(down or none, F32),
            pltpu.SemaphoreType.DMA((2,)),
        ]
        self.local = [pltpu.VMEM(self.stats, F32), pltpu.VMEM(up or none, F32), pltpu.VMEM(down or none, F32)]


def exchange_alone(ex, stats, gb, coefs=(), up=None, down=None):
    vm = pl.BlockSpec(memory_space=pltpu.VMEM)
    operands = [stats, gb, *coefs] + [h for h in (up, down) if h is not None]
    n_in, n_out = len(operands), len(ex.outs)

    def kernel(*refs):
        ins, outs, work = refs[:n_in], refs[n_in : n_in + n_out], refs[n_in + n_out :]
        count = exchange_hello(ex)
        pl.semaphore_wait(pltpu.get_barrier_semaphore(), count)
        halos = list(ins[2 + len(coefs) :])
        up_ref = halos.pop(0) if ex.up else None
        down_ref = halos.pop(0) if ex.down else None
        exchange_run(ex, ins[1 : 2 + len(coefs)], outs, [ins[0], up_ref, down_ref, *work])

    return pl.pallas_call(
        kernel,
        out_shape=[jax.ShapeDtypeStruct(s, d) for s, d in ex.outs],
        in_specs=[vm] * n_in,
        out_specs=[vm] * n_out,
        scratch_shapes=ex.work,
        compiler_params=pltpu.CompilerParams(collective_id=ex.cid, has_side_effects=True),
        name=f"exchange_{ex.cid}",
    )(*operands)


STAT, UP, DOWN = "stat", "up", "down"


def call(kernel, ins, outs, scratch=(), name=None, ex=None, ex_ins=()):
    real = [o for o in outs if not isinstance(o, str)]
    extra_in = [whole(a) for a in ex_ins]
    extra_out = [out_whole(s, d) for s, d in ex.outs] if ex else []
    all_in, all_out = [*ins, *extra_in], [*real, *extra_out]
    local = [*ex.local, *ex.work] if ex else []
    sizes = [len(ins), len(extra_in), len(real), len(extra_out), len(scratch), len(local)]
    ends = [sum(sizes[: k + 1]) for k in range(len(sizes))]

    def body(*refs):
        k_in, x_in, k_out, x_out, k_scr, x_scr = (refs[e - n : e] for e, n in zip(ends, sizes))
        if ex is None:
            kernel(*k_in, *k_out, *k_scr)
            return
        i = pl.program_id(0)

        @pl.when(i == 0)
        def _():
            exchange_hello(ex)

        named = {STAT: x_scr[0]}
        if ex.up:
            named[UP] = x_scr[1].at[pl.ds(i, 1)]
        if ex.down:
            named[DOWN] = x_scr[2].at[pl.ds(i, 1)]
        it = iter(k_out)
        late = kernel(*k_in, *[named[o] if isinstance(o, str) else next(it) for o in outs], *k_scr)

        @pl.when(i == STEPS - 1)
        def _():
            pl.semaphore_wait(pltpu.get_barrier_semaphore(), len_peers(ex))
            exchange_run(ex, x_in, x_out, x_scr, late)

    params = {"collective_id": ex.cid, "has_side_effects": True} if ex else {}
    return pl.pallas_call(
        body,
        grid=(STEPS,),
        in_specs=[pl.BlockSpec(b, m) for _, b, m in all_in],
        out_specs=[pl.BlockSpec(b, m) for _, _, b, m in all_out],
        out_shape=[jax.ShapeDtypeStruct(s, d) for s, d, _, _ in all_out],
        scratch_shapes=[*scratch, *local],
        compiler_params=pltpu.CompilerParams(
            dimension_semantics=("arbitrary",), vmem_limit_bytes=VMEM_LIMIT, **params
        ),
        name=name,
    )(*[a for a, _, _ in all_in])


def len_peers(ex):
    paths, length = lax.axis_size("path"), lax.axis_size("frames")
    return paths * 4 - 1 + length // 4 - 1 + (2 if ex.up or ex.down else 0)


def whole(array):
    zeros = (0,) * array.ndim
    return (array, array.shape, lambda i: zeros)


def blocked(array, axis, size):
    block = array.shape[:axis] + (size,) + array.shape[axis + 1 :]
    return (array, block, lambda i: tuple(i if d == axis else 0 for d in range(array.ndim)))


def out_whole(shape, dtype):
    zeros = (0,) * len(shape)
    return (shape, dtype, shape, lambda i: zeros)


def out_blocked(shape, dtype, axis, size):
    block = shape[:axis] + (size,) + shape[axis + 1 :]
    return (shape, dtype, block, lambda i: tuple(i if d == axis else 0 for d in range(len(shape))))


def flat(value):
    return value.reshape(-1, value.shape[-1])


def spread_rows(ref, index, count, height):
    return [jnp.broadcast_to(ref[(*index, slice(p, p + 1))], (height, ref.shape[-1])) for p in range(count)]


def k_first(x_ref, tail_ref, m16_ref, m64_ref, wfa_ref, wlat_ref,
            fa_ref, lat_ref, taps_ref, st_ref, up_ref, down_ref, xs, fm, fv, lm, lv):
    i = pl.program_id(0)
    x = x_ref[...]
    s_n, p_n, f_n, _ = x.shape
    packed = jnp.concatenate([flat(x[s]) for s in range(s_n)], axis=1)
    fa = dot_nt(packed, wfa_ref[...])
    fa_ref[...] = fa.reshape(fa_ref.shape)
    zero_ref(up_ref)
    zero_ref(down_ref)
    for p in range(p_n):
        down_ref[0, p : p + 1, :] = fa[p * f_n : p * f_n + 1, :]
        up_ref[0, p : p + 1, :] = fa[p * f_n + f_n - 1 : p * f_n + f_n, :]
    spread_add(i, fa.reshape(p_n, f_n, LANES), fm, fv)

    xs[...] = flat(x).astype(F32)
    n = xs.shape[0] // 4
    quarter = [xs[pl.ds(k, n, stride=4), :] for k in range(4)]
    t_n = f_n // 4
    first = lax.broadcasted_iota(jnp.int32, (n // t_n, t_n, LANES), 1) == 0
    link = m16_ref[1:2]
    taps = []
    for k in range(2):
        halo = jnp.concatenate(
            [
                jnp.broadcast_to(tail_ref[0, s, p : p + 1, k * LANES : (k + 1) * LANES], (t_n, LANES))
                for s in range(s_n)
                for p in range(p_n)
            ],
            axis=0,
        )
        moved = pltpu.roll(quarter[2 + k], 1, 0).reshape(n // t_n, t_n, LANES)
        taps.append(flat(jnp.where(first, halo.reshape(moved.shape), moved) * link))
    taps = jnp.concatenate([*taps, *quarter[:3]], axis=1).astype(BF16)
    taps_ref[...] = taps.reshape(taps_ref.shape)
    lat = dot(taps, wlat_ref[...])
    lat_ref[...] = lat.reshape(lat_ref.shape)
    spread_add(i, lat.reshape(n // t_n, t_n, lat.shape[1]), lm, lv)

    @pl.when(i == STEPS - 1)
    def _():
        zero_ref(st_ref)
        fill = m16_ref[0, :, 0:1]
        mean, m2 = spread_end(fm, fv, m64_ref[0, :, 0:1], STEPS * p_n)
        put_rows(st_ref, 0, mean)
        put_rows(st_ref, 3, m2)
        mean, m2 = spread_end(lm, lv, fill, STEPS * p_n * s_n)
        put_rows(st_ref, 1, mean)
        put_rows(st_ref, 4, m2)
        put_rows(st_ref, 6, count_row(m16_ref, STEPS * p_n * s_n))


def count_row(m16_ref, positions):
    return jnp.sum(m16_ref[0], axis=0, keepdims=True) * float(positions)


def shifted(value, first_rows, last_rows, f_n):
    n = value.shape[0]
    shape = (n // f_n, f_n, value.shape[1])
    place = lax.broadcasted_iota(jnp.int32, shape, 1)
    before = jnp.where(place == 0, first_rows, pltpu.roll(value, 1, 0).reshape(shape))
    after = jnp.where(place == f_n - 1, last_rows, pltpu.roll(value, n - 1, 0).reshape(shape))
    return before, after


def k_join(x_ref, lat_ref, fa_ref, hp_ref, hn_ref, c1_ref, m16_ref, m64_ref, win_ref, wsc_ref, wmid_ref,
           lact_ref, ftap_ref, sa_ref, sp_ref, fb_ref, st_ref, am, av, pm, pv, bm, bv):
    i = pl.program_id(0)
    s_n, p_n, t_n, c_slow = x_ref.shape
    c_lat = lat_ref.shape[-1]
    v = flat(lat_ref[...]) * rows(c1_ref, 0, 1, 2) + rows(c1_ref, 1, 1, 2)
    lact = (v * sig(v)).astype(BF16)
    lact_ref[...] = lact.reshape(lact_ref.shape)
    joined = jnp.concatenate([flat(x_ref[...]), lact], axis=1)
    wide = c_lat
    for n in range(1 + wsc_ref.shape[1] // wide):
        z = dot(joined, win_ref[...] if n == 0 else wsc_ref[:, (n - 1) * wide : n * wide])
        z4 = z.reshape(s_n, p_n, t_n, wide)
        z3 = z.reshape(s_n * p_n, t_n, wide)
        if n == 0:
            sa_ref[...] = z4
            spread_add(i, z3, am, av)
        else:
            cols = slice((n - 1) * wide, n * wide)
            sp_ref[:, :, :, cols] = z4
            spread_add(i, z3, pm, pv, cols)

    f_n = fa_ref.shape[1]
    scale, shift = rows(c1_ref, 0, 0, 1), rows(c1_ref, 1, 0, 1)

    def act(z):
        w = z * scale + shift
        return (w * sig(w)).astype(BF16).astype(F32)

    fact = act(flat(fa_ref[...]))
    ends = []
    for ref in (hp_ref, hn_ref):
        small = act(ref[0])
        ends.append(
            jnp.concatenate(
                [jnp.broadcast_to(small[p : p + 1, :], (f_n, LANES)) for p in range(p_n)], axis=0
            ).reshape(p_n, f_n, LANES)
        )
    before, after = shifted(fact, ends[0], ends[1], f_n)
    ftap = jnp.concatenate(
        [flat(before * m64_ref[1:2]), fact, flat(after * m64_ref[2:3])], axis=1
    ).astype(BF16)
    ftap_ref[...] = ftap.reshape(ftap_ref.shape)
    fb = dot(ftap, wmid_ref[...])
    fb_ref[...] = fb.reshape(fb_ref.shape)
    spread_add(i, fb.reshape(p_n, f_n, LANES), bm, bv)

    @pl.when(i == STEPS - 1)
    def _():
        zero_ref(st_ref)
        fill = m16_ref[0, :, 0:1]
        positions = STEPS * p_n * s_n
        mean, m2 = spread_end(bm, bv, m64_ref[0, :, 0:1], STEPS * p_n)
        put_rows(st_ref, 0, mean)
        put_rows(st_ref, 11, m2)
        mean, m2 = spread_end(am, av, fill, positions)
        put_rows(st_ref, 1, mean)
        put_rows(st_ref, 12, m2)
        mean, m2 = spread_end(pm, pv, fill, positions)
        put_rows(st_ref, 3, mean)
        put_rows(st_ref, 14, m2)
        put_rows(st_ref, 22, count_row(m16_ref, positions))


def k_spatial(sa_ref, fb_ref, c2_ref, m16_ref, m64_ref, wsp_ref, wout_ref,
              pad_ref, sb_ref, fact_ref, st_ref, sm, sv, cm, cv):
    i = pl.program_id(0)
    h_n, w_n, t_n, c = sa_ref.shape

    @pl.when(i == 0)
    def _():
        scale, shift = rows(c2_ref, 0, 1, 2), rows(c2_ref, 1, 1, 2)
        zero_ref(pad_ref)

        @pl.loop(0, h_n)
        def _(h):
            v = flat(sa_ref[h]) * scale + shift
            pad_ref[h + 1, 1 : w_n + 1] = (v * sig(v)).astype(BF16).reshape(w_n, t_n, c)

    per = h_n // STEPS
    h0 = i * per
    acc = None
    for a in range(3):
        for b in range(3):
            k = 3 * a + b
            part = dot(flat(pad_ref[pl.ds(h0 + a, per), b : b + w_n].reshape(per * w_n, t_n, c)), wsp_ref[k])
            acc = part if acc is None else acc + part
    sb_ref[...] = acc.reshape(sb_ref.shape)
    spread_add(i, acc.reshape(per * w_n, t_n, acc.shape[1]), sm, sv)

    p_n, f_n, _ = fb_ref.shape
    v = flat(fb_ref[...]) * rows(c2_ref, 0, 0, 1) + rows(c2_ref, 1, 0, 1)
    fact = (v * sig(v)).astype(BF16)
    fact_ref[...] = fact.reshape(fact_ref.shape)
    fc = dot(fact, wout_ref[...])
    spread_add(i, fc.reshape(p_n, f_n, fc.shape[1]), cm, cv)

    @pl.when(i == STEPS - 1)
    def _():
        zero_ref(st_ref)
        mean, m2 = spread_end(cm, cv, m64_ref[0, :, 0:1], STEPS * p_n)
        put_rows(st_ref, 0, mean)
        put_rows(st_ref, 6, m2)
        mean, m2 = spread_end(sm, sv, m16_ref[0, :, 0:1], h_n * w_n)
        put_rows(st_ref, 4, mean)
        put_rows(st_ref, 10, m2)
        put_rows(st_ref, 12, count_row(m16_ref, h_n * w_n))


def k_expand(sb_ref, fact_ref, x_ref, cot_ref, c3_ref, m16_ref, m64_ref, wso_ref, wout_ref,
             sact_ref, fout_ref, df_ref, st_ref, cm, cv, s1, s2):
    i = pl.program_id(0)
    s_n, p_n, t_n, c = sb_ref.shape
    v = flat(sb_ref[...]) * rows(c3_ref, 0, 4, 2) + rows(c3_ref, 1, 4, 2)
    sact = (v * sig(v)).astype(BF16)
    sact_ref[...] = sact.reshape(sact_ref.shape)
    wide = 256
    for n in range(wso_ref.shape[1] // wide):
        cols = slice(n * wide, (n + 1) * wide)
        z = dot(sact, wso_ref[:, cols])
        spread_add(i, z.reshape(s_n * p_n, t_n, wide), cm, cv, cols)

    f_n = fact_ref.shape[1]
    fc = dot(flat(fact_ref[...]), wout_ref[...])
    fill = m64_ref[0:1]
    for s in range(s_n):
        cols = slice(s * LANES, (s + 1) * LANES)
        z = fc[:, cols].reshape(p_n, f_n, LANES)
        unit = z * rows(c3_ref, 2, s, 1) - rows(c3_ref, 3, s, 1)
        pre = z * rows(c3_ref, 0, s, 1) + rows(c3_ref, 1, s, 1) + x_ref[s].astype(F32)
        g = sig(pre)
        y = pre * g
        fout_ref[s] = (y * fill).astype(BF16)
        d = cot_ref[s].astype(F32) * fill * (g + y * (1.0 - g))
        df_ref[:, :, cols] = d
        sum_add(i, d, s1, cols)
        sum_add(i, d * unit, s2, cols)

    @pl.when(i == STEPS - 1)
    def _():
        zero_ref(st_ref)
        positions = STEPS * p_n * s_n
        mean, m2 = spread_end(cm, cv, m16_ref[0, :, 0:1], positions)
        put_rows(st_ref, 0, mean)
        put_rows(st_ref, 8, m2)
        put_rows(st_ref, 16, sum_end(s1))
        put_rows(st_ref, 20, sum_end(s2))
        put_rows(st_ref, 24, count_row(m16_ref, positions))


def back_norm(scale, p, q, dy, z, fill):
    return scale * dy - fill * (p + z * q)


def k_out(sact_ref, sp_ref, cot_ref, df_ref, fact_ref, fb_ref, c2_ref, c3_ref, c4_ref, q4_ref,
          m16_ref, m64_ref, wso_ref, wout_ref,
          out_ref, dy_ref, dfb_ref, gout_ref, up_ref, down_ref, st_ref, s1, s2, s3, t1, t2, gout):
    i = pl.program_id(0)
    s_n, p_n, t_n, _ = sact_ref.shape
    sact = flat(sact_ref[...])
    fill = m16_ref[0:1, :, 0:1]
    wide = 256
    for n in range(wso_ref.shape[1] // wide):
        cols = slice(n * wide, (n + 1) * wide)
        shape = (s_n * p_n, t_n, wide)
        sc = dot(sact, wso_ref[:, cols]).reshape(shape)
        sp = sp_ref[:, :, :, cols].reshape(shape)
        u6 = sc * rows(c4_ref, 2, 2 * n, 2) - rows(c4_ref, 3, 2 * n, 2)
        u7 = sp * rows(c2_ref, 2, 3 + 2 * n, 2) - rows(c2_ref, 3, 3 + 2 * n, 2)
        pre = (
            sc * rows(c4_ref, 0, 2 * n, 2)
            + sp * rows(c2_ref, 0, 3 + 2 * n, 2)
            + (rows(c4_ref, 1, 2 * n, 2) + rows(c2_ref, 1, 3 + 2 * n, 2))
        )
        g = sig(pre)
        y = pre * g
        out_ref[:, :, :, cols] = (y * fill).astype(BF16).reshape(s_n, p_n, t_n, wide)
        d = cot_ref[:, :, :, cols].reshape(shape).astype(F32) * fill * (g + y * (1.0 - g))
        dy_ref[:, :, :, cols] = d.reshape(s_n, p_n, t_n, wide)
        sum_add(i, d, s1, cols)
        sum_add(i, d * u6, s2, cols)
        sum_add(i, d * u7, s3, cols)

    f_n = fact_ref.shape[1]
    fact = flat(fact_ref[...])
    fc = dot(fact, wout_ref[...])
    fill4 = m64_ref[0:1]
    parts = []
    for s in range(s_n):
        cols = slice(s * LANES, (s + 1) * LANES)
        d = back_norm(
            rows(c3_ref, 0, s, 1), rows(q4_ref, 0, s, 1), rows(q4_ref, 1, s, 1),
            df_ref[:, :, cols], fc[:, cols].reshape(p_n, f_n, LANES), fill4,
        )
        parts.append(flat(d).astype(BF16))
    dfc = jnp.concatenate(parts, axis=1)
    add_to(i, gout, dot_tn(fact, dfc))
    z = fb_ref[...]
    back = dot_nt(dfc, wout_ref[...]).reshape(p_n, f_n, LANES) * slope(
        z * rows(c2_ref, 0, 0, 1) + rows(c2_ref, 1, 0, 1)
    )
    dfb_ref[...] = back
    sum_add(i, back, t1)
    sum_add(i, back * (z * rows(c2_ref, 2, 0, 1) - rows(c2_ref, 3, 0, 1)), t2)
    for k, value in enumerate((back, z)):
        value = flat(value)
        for p in range(p_n):
            down_ref[0, k, p : p + 1, :] = value[p * f_n : p * f_n + 1, :]
            up_ref[0, k, p : p + 1, :] = value[p * f_n + f_n - 1 : p * f_n + f_n, :]
        down_ref[0, k, p_n : p_n + 1, :] = m64_ref[0, 0:1, :]
        up_ref[0, k, p_n : p_n + 1, :] = m64_ref[0, f_n - 1 : f_n, :]

    @pl.when(i == STEPS - 1)
    def _():
        zero_ref(st_ref)
        put_rows(st_ref, 0, sum_end(s1))
        put_rows(st_ref, 8, sum_end(s2))
        put_rows(st_ref, 16, sum_end(s3))
        put_rows(st_ref, 24, sum_end(t1))
        put_rows(st_ref, 25, sum_end(t2))
        gout_ref[...] = fold_wide(gout, s_n)


def add_to(step, ref, value):
    ref[...] = jnp.where(step == 0, 0.0, ref[...]) + value


def fold_wide(ref, count):
    a = ref.shape[0] // count
    return sum(ref[s * a : (s + 1) * a, s * LANES : (s + 1) * LANES] for s in range(count))


def fold_lanes(value, count):
    a = value.shape[0] // count
    parts = [value[s * a : (s + 1) * a, :] for s in range(count)]
    return sum(p if s == 0 else pltpu.roll(p, LANES - s * a, 1) for s, p in enumerate(parts))


def k_back_out(x_ref, lact_ref, dy_ref, sp_ref, sact_ref, sb_ref, dfb_ref, fb_ref, fa_ref, ftap_ref, hp_ref, hn_ref,
               c1_ref, c2_ref, c3_ref, c4_ref, q5_ref, m16_ref, m64_ref, wso_ref, wback_ref,
               gw_ref, dsp_ref, dsb_ref, dfa_ref, gmid_ref, st_ref, s1, s2, t1, t2, gsc, gso, gmid):
    i = pl.program_id(0)
    s_n, p_n, t_n, c = sb_ref.shape
    sact = flat(sact_ref[...])
    fill = m16_ref[0:1, :, 0:1]
    wide = 256
    back = None
    turned = jnp.concatenate([flat(x_ref[...]), flat(lact_ref[...])], axis=1).T
    sact_turned = sact.T
    for n in range(wso_ref.shape[1] // wide):
        cols = slice(n * wide, (n + 1) * wide)
        shape = (s_n * p_n, t_n, wide)
        d = dy_ref[:, :, :, cols].reshape(shape)
        sc = dot(sact, wso_ref[:, cols]).reshape(shape)
        dsc = back_norm(rows(c4_ref, 0, 2 * n, 2), rows(q5_ref, 0, 2 * n, 2), rows(q5_ref, 1, 2 * n, 2), d, sc, fill)
        dsc = flat(dsc.astype(BF16))
        old = jnp.where(i == 0, 0.0, gso[:, cols])
        gso[:, cols] = old + dot(sact_turned, dsc)
        sp = sp_ref[:, :, :, cols].reshape(shape)
        dsp = back_norm(
            rows(c2_ref, 0, 3 + 2 * n, 2), rows(q5_ref, 0, 8 + 2 * n, 2), rows(q5_ref, 1, 8 + 2 * n, 2), d, sp, fill
        )
        dsp = flat(dsp.astype(BF16))
        dsp_ref[:, :, :, cols] = dsp.reshape(s_n, p_n, t_n, wide)
        old = jnp.where(i == 0, 0.0, gsc[:, cols])
        gsc[:, cols] = old + dot(turned, dsp)
        part = dot_nt(dsc, wso_ref[:, cols])
        back = part if back is None else back + part
    z = sb_ref[...].reshape(s_n * p_n, t_n, c)
    back = back.reshape(z.shape) * slope(z * rows(c3_ref, 0, 4, 2) + rows(c3_ref, 1, 4, 2))
    dsb_ref[...] = back.reshape(dsb_ref.shape)
    sum_add(i, back, s1)
    sum_add(i, back * (z * rows(c3_ref, 2, 4, 2) - rows(c3_ref, 3, 4, 2)), s2)

    f_n = fb_ref.shape[1]
    scale, p_row, q_row = rows(c2_ref, 0, 0, 1), rows(q5_ref, 0, 16, 1), rows(q5_ref, 1, 16, 1)
    dfb = back_norm(scale, p_row, q_row, dfb_ref[...], fb_ref[...], m64_ref[0:1])
    dfb_low = flat(dfb).astype(BF16)
    add_to(i, gmid, dot_tn(dfb_low, flat(ftap_ref[...])))
    own = dfb_low.astype(F32)
    ends = []
    for ref in (hp_ref, hn_ref):
        small = back_norm(scale, p_row, q_row, ref[0, 0], ref[0, 1], ref[0, 0, p_n : p_n + 1, :])
        small = small.astype(BF16).astype(F32)
        ends.append(
            jnp.concatenate(
                [jnp.broadcast_to(small[p : p + 1, :], (f_n, LANES)) for p in range(p_n)], axis=0
            ).reshape(p_n, f_n, LANES)
        )
    before, after = shifted(own, ends[0], ends[1], f_n)
    taps = jnp.concatenate(
        [flat(after * m64_ref[2:3]), own, flat(before * m64_ref[1:2])], axis=1
    ).astype(BF16)
    z = fa_ref[...]
    back = dot(taps, wback_ref[...]).reshape(z.shape) * slope(
        z * rows(c1_ref, 0, 0, 1) + rows(c1_ref, 1, 0, 1)
    )
    dfa_ref[...] = back
    sum_add(i, back, t1)
    sum_add(i, back * (z * rows(c1_ref, 2, 0, 1) - rows(c1_ref, 3, 0, 1)), t2)

    @pl.when(i == STEPS - 1)
    def _():
        zero_ref(st_ref)
        put_rows(st_ref, 0, sum_end(s1))
        put_rows(st_ref, 2, sum_end(s2))
        put_rows(st_ref, 4, sum_end(t1))
        put_rows(st_ref, 5, sum_end(t2))

    def late():
        for k in range(3):
            gmid_ref[k * 32 : (k + 1) * 32, :] = fold_lanes(gmid[:, k * LANES : (k + 1) * LANES], s_n)
        tall, low_tall = gsc.shape[0], gso.shape[0]
        blocks = gsc.shape[1] // wide
        for n in range(blocks):
            cols = slice(n * wide, (n + 1) * wide)
            gw_ref[n * tall : (n + 1) * tall, :] = gsc[:, cols].astype(BF16)
            at = blocks * tall + n * low_tall
            gw_ref[at : at + low_tall, :] = gso[:, cols].astype(BF16)

    return late


def k_back_spatial(dsb_ref, sb_ref, sa_ref, spad_ref, x_ref, dfa_ref, fa_ref, gout_ref, gmid_ref, c1_ref, c2_ref, c3_ref, q6_ref,
                   m16_ref, m64_ref, wsp_ref,
                   dsa_ref, dlow_ref, gw_ref, gf_ref, st_ref, s1, s2, pad_ref, gsp, gin):
    i = pl.program_id(0)
    h_n, w_n, t_n, c = sb_ref.shape

    @pl.when(i == 0)
    def _():
        scale = rows(c3_ref, 0, 4, 2)
        p_row, q_row = rows(q6_ref, 0, 0, 2), rows(q6_ref, 1, 0, 2)
        zero_ref(pad_ref)

        @pl.loop(0, h_n)
        def _(h):
            d = back_norm(scale, p_row, q_row, dsb_ref[h], sb_ref[h], m16_ref[0:1, :, 0:1])
            pad_ref[h + 1, 1 : w_n + 1] = d.astype(BF16)

    per = h_n // STEPS
    h0 = i * per
    acc = None
    turned = flat(pad_ref[pl.ds(h0 + 1, per), 1 : w_n + 1]).T
    for a in range(3):
        for b in range(3):
            k = 3 * a + b
            patch = flat(spad_ref[pl.ds(h0 + a, per), b : b + w_n])
            cols = slice(k * c, (k + 1) * c)
            gsp[:, cols] = jnp.where(i == 0, 0.0, gsp[:, cols]) + dot(turned, patch)
            block = pad_ref[pl.ds(h0 + 2 - a, per), 2 - b : 2 - b + w_n]
            part = dot_nt(flat(block), wsp_ref[k])
            acc = part if acc is None else acc + part
    z = sa_ref[...].reshape(per * w_n, t_n, c)
    back = acc.reshape(z.shape) * slope(z * rows(c2_ref, 0, 1, 2) + rows(c2_ref, 1, 1, 2))
    dsa_ref[...] = back.reshape(dsa_ref.shape)
    sum_add(i, back, s1)
    sum_add(i, back * (z * rows(c2_ref, 2, 1, 2) - rows(c2_ref, 3, 1, 2)), s2)

    low = back_norm(
        rows(c1_ref, 0, 0, 1), rows(q6_ref, 0, 2, 1), rows(q6_ref, 1, 2, 1), dfa_ref[...], fa_ref[...], m64_ref[0:1]
    ).astype(BF16)
    dlow_ref[...] = low
    packed = jnp.concatenate([flat(x_ref[s]) for s in range(x_ref.shape[0])], axis=1)
    add_to(i, gin, dot_tn(flat(low), packed))

    @pl.when(i == STEPS - 1)
    def _():
        zero_ref(st_ref)
        put_rows(st_ref, 0, sum_end(s1))
        put_rows(st_ref, 2, sum_end(s2))

    def late():
        for k in range(9):
            gw_ref[k * c : (k + 1) * c, :] = gsp[:, k * c : (k + 1) * c].T.astype(BF16)
        gf_ref[0:32, 0:LANES] = fold_wide(gin, x_ref.shape[0])
        gf_ref[0:32, LANES:] = gout_ref[...]
        gf_ref[32:64, 0:LANES] = gmid_ref[0:32, :]
        gf_ref[32:64, LANES:] = gmid_ref[32:64, :]
        gf_ref[64:96, 0:LANES] = gmid_ref[64:96, :]
        gf_ref[64:96, LANES:] = jnp.zeros((32, LANES), F32)

    return late


def k_back_join(x_ref, lact_ref, dsa_ref, sa_ref, dsp_ref, lat_ref, c1_ref, c2_ref, q7_ref, m16_ref, win_ref, wsc_ref,
                gw_ref, gx_ref, dlat_ref, down_ref, st_ref, s1, s2, gsi):
    i = pl.program_id(0)
    s_n, p_n, t_n, c = sa_ref.shape
    shape = (s_n * p_n, t_n, c)
    low = back_norm(
        rows(c2_ref, 0, 1, 2), rows(q7_ref, 0, 0, 2), rows(q7_ref, 1, 0, 2),
        dsa_ref[...].reshape(shape), sa_ref[...].reshape(shape), m16_ref[0:1, :, 0:1],
    ).astype(BF16)
    low = flat(low)
    dsp = flat(dsp_ref[...])
    turned = low.T
    wide = 256
    blocks = win_ref.shape[0] // wide
    for n in range(blocks):
        part = slice(n * wide, (n + 1) * wide)
        joined = flat(x_ref[:, :, :, part] if n < blocks - 1 else lact_ref[...])
        gsi[:, part] = jnp.where(i == 0, 0.0, gsi[:, part]) + dot(turned, joined)
        d = dot_nt(dsp, wsc_ref[part, :]) + dot_nt(low, win_ref[part, :])
        if n < blocks - 1:
            gx_ref[:, :, :, n * wide : (n + 1) * wide] = d.astype(BF16).reshape(s_n, p_n, t_n, wide)
    z = lat_ref[...].reshape(shape)
    back = d.reshape(shape) * slope(z * rows(c1_ref, 0, 1, 2) + rows(c1_ref, 1, 1, 2))
    dlat_ref[...] = back.reshape(dlat_ref.shape)
    sum_add(i, back, s1)
    sum_add(i, back * (z * rows(c1_ref, 2, 1, 2) - rows(c1_ref, 3, 1, 2)), s2)
    fill = jnp.broadcast_to(m16_ref[0, 0:1, 0:1], (1, c))
    for k, value in enumerate((flat(back), flat(z))):
        for s in range(s_n):
            for p in range(p_n):
                r = (s * p_n + p) * t_n
                down_ref[0, k, s, p : p + 1, :] = value[r : r + 1, :]
            down_ref[0, k, s, p_n : p_n + 1, :] = fill

    @pl.when(i == STEPS - 1)
    def _():
        zero_ref(st_ref)
        put_rows(st_ref, 0, sum_end(s1))
        put_rows(st_ref, 2, sum_end(s2))
        for n in range(blocks):
            part = slice(n * wide, (n + 1) * wide)
            gw_ref[part, :] = gsi[:, part].T.astype(BF16)


def k_last(dlat_ref, lat_ref, taps_ref, hn_ref, df_ref, dlow_ref, c1_ref, q8_ref, m16_ref,
           wlat_ref, wfa_ref, gx_ref, gw_ref, gs, glat):
    i = pl.program_id(0)
    s_n, p_n, t_n, c = lat_ref.shape
    shape = (s_n * p_n, t_n, c)
    scale, p_row, q_row = rows(c1_ref, 0, 1, 2), rows(q8_ref, 0, 0, 2), rows(q8_ref, 1, 0, 2)
    low = flat(
        back_norm(scale, p_row, q_row, dlat_ref[...].reshape(shape), lat_ref[...].reshape(shape), m16_ref[0:1, :, 0:1])
    ).astype(BF16)
    add_to(i, glat, dot_tn(low, flat(taps_ref[...])))
    ends = []
    for s in range(s_n):
        small = back_norm(
            scale, p_row, q_row, hn_ref[0, 0, s], hn_ref[0, 1, s], hn_ref[0, 0, s, p_n : p_n + 1, :]
        )
        small = small.astype(BF16).astype(F32)
        ends += [jnp.broadcast_to(small[p : p + 1, :], (t_n, c)) for p in range(p_n)]
    ends = jnp.concatenate(ends, axis=0).reshape(shape)
    n = low.shape[0]
    moved = pltpu.roll(low.astype(F32), n - 1, 0).reshape(shape)
    place = lax.broadcasted_iota(jnp.int32, shape, 1)
    following = flat(jnp.where(place == t_n - 1, ends, moved) * m16_ref[2:3, :, 0:1]).astype(BF16)
    own = dot_nt(low, wlat_ref[2 * LANES : 5 * LANES, :])
    late = dot_nt(following, wlat_ref[0 : 2 * LANES, :])
    gs[pl.ds(0, n, stride=4), :] = own[:, 0:LANES]
    gs[pl.ds(1, n, stride=4), :] = own[:, LANES : 2 * LANES]
    gs[pl.ds(2, n, stride=4), :] = own[:, 2 * LANES :] + late[:, 0:LANES]
    gs[pl.ds(3, n, stride=4), :] = late[:, LANES:]
    back = dot(flat(dlow_ref[...]), wfa_ref[...])
    for s in range(s_n):
        cols = slice(s * LANES, (s + 1) * LANES)
        total = flat(df_ref[:, :, cols]) + back[:, cols] + gs[s * n : (s + 1) * n, :]
        gx_ref[s] = total.astype(BF16).reshape(gx_ref.shape[1:])

    @pl.when(i == STEPS - 1)
    def _():
        for k in range(glat.shape[1] // LANES):
            part = slice(k * LANES, (k + 1) * LANES)
            gw_ref[part, :] = glat[:, part].T.astype(BF16)


def each(first, last, body):
    def step(k, carry):
        body(k)
        return carry
    lax.fori_loop(first, last, step, 0)


NEAR = 4


def reduce_kernel(cfg, *refs):
    offsets, heights, ch, far = cfg
    n_in = len(offsets)
    ins = refs[:n_in]
    (out_ref, x, land_a, buf_b, land_b, buf_c, land_c, acc,
     sem_a, sem_b, sem_c, sem_d, sem_e, sem_f) = refs[n_in:]
    me_p, me_f = lax.axis_index("path"), lax.axis_index("frames")
    me_q, me_r = lax.rem(me_f, NEAR), lax.div(me_f, NEAR)
    other = 1 - me_p

    def at(path, q, r):
        return pl.ds(pl.multiple_of(((path * NEAR + q) * far + r) * ch, 16), ch)

    def q_of(k):
        return lax.rem(me_q + k, NEAR)

    def r_of(k):
        return lax.rem(me_r + k, far)

    barrier = pltpu.get_barrier_semaphore()
    pl.semaphore_signal(barrier, inc=1, device_id=(other, me_f), device_id_type=MESH)
    each(1, NEAR, lambda k: pl.semaphore_signal(
        barrier, inc=1, device_id=(me_p, me_r * NEAR + q_of(k)), device_id_type=MESH))
    each(1, far, lambda k: pl.semaphore_signal(
        barrier, inc=1, device_id=(me_p, r_of(k) * NEAR + me_q), device_id_type=MESH))
    end = 0
    for ref, off, height in zip(ins, offsets, heights):
        x[off : off + height, :] = ref[...].astype(BF16)
        end = off + height
    if end < x.shape[0]:
        x[end:, :] = jnp.zeros((x.shape[0] - end, x.shape[1]), BF16)
    pl.semaphore_wait(barrier, NEAR + far - 1)

    def copy(src, dst, sem, index, device):
        return pltpu.make_async_remote_copy(
            src_ref=src, dst_ref=dst, send_sem=sem.at[(0, *index)], recv_sem=sem.at[(1, *index)],
            device_id=device, device_id_type=MESH)

    sibling = (other, me_f)

    def pair(k, m):
        return copy(x.at[at(other, q_of(k), r_of(m + 1))], land_a.at[k, m], sem_a, (k, m), sibling)

    def plane(k, m):
        return copy(buf_b.at[k, m], land_b.at[k, m], sem_b, (k, m), (me_p, me_r * NEAR + q_of(k)))

    def line(m):
        return copy(buf_c.at[m], land_c.at[m], sem_c, (m,), (me_p, r_of(m + 1) * NEAR + me_q))

    def own(q, r):
        return out_ref.at[at(me_p, q, r)]

    def line_back(k):
        return copy(own(me_q, me_r), own(me_q, me_r), sem_d, (k,), (me_p, r_of(k) * NEAR + me_q))

    def plane_back(k, m):
        part = own(me_q, r_of(far - m))
        return copy(part, part, sem_e, (k, m), (me_p, me_r * NEAR + q_of(k)))

    def pair_back(k, m):
        part = own(q_of(NEAR - k), r_of(far - m))
        return copy(part, part, sem_f, (k, m), sibling)

    def both(body, first=0):
        each(0, far, lambda m: each(first, NEAR, lambda k: body(k, m)))

    def start_pair(m):
        each(1, NEAR, lambda k: pair(k, m).start())
        pair(0, m).start()

    each(0, far, start_pair)

    def add_pair(k, m):
        pair(k, m).wait_recv()
        buf_b[k, m] = (x[at(me_p, q_of(k), r_of(m + 1)), :].astype(F32) + land_a[k, m].astype(F32)).astype(BF16)
        plane(k, m).start()

    both(add_pair, 1)

    def add_plane(m):
        pair(0, m).wait_recv()
        acc[...] = x[at(me_p, me_q, r_of(m + 1)), :].astype(F32) + land_a[0, m].astype(F32)

        def more(k):
            plane(k, m).wait_recv()
            acc[...] += land_b[k, m].astype(F32)

        each(1, NEAR, more)

    def send_line(m):
        add_plane(m)
        buf_c[m] = acc[...].astype(BF16)
        line(m).start()

    each(0, far - 1, send_line)
    add_plane(far - 1)

    def add_line(m):
        line(m).wait_recv()
        acc[...] += land_c[m].astype(F32)

    each(0, far - 1, add_line)
    out_ref[at(me_p, me_q, me_r), :] = acc[...].astype(BF16)
    each(1, far, lambda k: line_back(k).start())

    def share(m):
        each(1, NEAR, lambda k: plane_back(k, m).start())
        pair_back(0, m).start()

    share(0)

    def relay(m):
        line_back(m).wait_recv()
        share(m)

    each(1, far, relay)

    def hand_on(k, m):
        plane_back(k, m).wait_recv()
        pair_back(k, m).start()

    both(hand_on, 1)
    both(lambda k, m: pair_back(k, m).wait())
    both(lambda k, m: pair(k, m).wait_send())
    both(lambda k, m: plane(k, m).wait_send(), 1)
    each(0, far - 1, lambda m: line(m).wait_send())
    each(1, far, lambda k: line_back(k).wait_send())
    both(lambda k, m: plane_back(k, m).wait_send(), 1)


def reduce_all(sizes, cid, parts):
    paths, length = sizes
    far = length // NEAR
    unit = 16 * paths * length
    heights = tuple(p.shape[0] for p in parts)
    offsets = tuple(sum(heights[:k]) for k in range(len(parts)))
    total = -(-sum(heights) // unit) * unit
    ch = total // (paths * length)
    vm = pl.BlockSpec(memory_space=pltpu.VMEM)
    width = parts[0].shape[1]
    quad = pltpu.VMEM((NEAR, far, ch, width), BF16)
    single = pltpu.VMEM((far, ch, width), BF16)
    out = pl.pallas_call(
        functools.partial(reduce_kernel, (offsets, heights, ch, far)),
        out_shape=jax.ShapeDtypeStruct((total, width), BF16),
        in_specs=[vm] * len(parts),
        out_specs=vm,
        scratch_shapes=[
            pltpu.VMEM((total, width), BF16), quad, quad, quad, single, single,
            pltpu.VMEM((ch, width), F32),
            *[pltpu.SemaphoreType.DMA((2, NEAR, far))] * 2,
            *[pltpu.SemaphoreType.DMA((2, far))] * 2,
            *[pltpu.SemaphoreType.DMA((2, NEAR, far))] * 2,
        ],
        compiler_params=pltpu.CompilerParams(collective_id=cid, has_side_effects=True, vmem_limit_bytes=VMEM_LIMIT),
        name=f"reduce_{cid}",
    )(*parts)
    return out


def k_unpack(pieces, src_ref, *refs):
    n_out = len(refs) - 4
    outs, (low, wide, sem_in, sem_out) = refs[:n_out], refs[n_out:]

    def fetch(k):
        row, height = pieces[k][:2]
        part = pl.ds(row, height)
        return pltpu.make_async_copy(src_ref.at[part], low.at[part], sem_in.at[k])

    def store(k):
        row, height, out, col = pieces[k]
        part = outs[out] if col is None else outs[out].at[:, pl.ds(col, src_ref.shape[1])]
        return pltpu.make_async_copy(wide.at[pl.ds(row, height)], part, sem_out.at[k])

    for k in range(len(pieces)):
        fetch(k).start()
    for k, (row, height, _, _) in enumerate(pieces):
        fetch(k).wait()
        wide[row : row + height, :] = low[row : row + height, :].astype(F32)
        store(k).start()
    for k in range(len(pieces)):
        store(k).wait()


def unpack(reduced, pieces, shapes):
    hbm = pl.BlockSpec(memory_space=pl.ANY)
    return pl.pallas_call(
        functools.partial(k_unpack, pieces),
        out_shape=[jax.ShapeDtypeStruct(s, F32) for s in shapes],
        in_specs=[hbm],
        out_specs=[hbm] * len(shapes),
        scratch_shapes=[
            pltpu.VMEM(reduced.shape, BF16),
            pltpu.VMEM(reduced.shape, F32),
            pltpu.SemaphoreType.DMA((len(pieces),)),
            pltpu.SemaphoreType.DMA((len(pieces),)),
        ],
        compiler_params=pltpu.CompilerParams(vmem_limit_bytes=VMEM_LIMIT),
        name="unpack",
    )(reduced)


def k_prep(x_hbm, fill_ref, clip_ref, norm_ref, wfi_ref, wfm_ref, wfo_ref,
           tail_ref, gb_ref, m16_ref, m64_ref, wfa_ref, wmid_ref, wback_ref, wout_ref,
           near, rows_f, sent, land, sems, local):
    length = lax.axis_size("frames")
    total = lax.axis_size("path") * length
    me = lax.axis_index("path") * length + lax.axis_index("frames")

    def place(index):
        return (lax.div(index, length), lax.rem(index, length))

    nxt, prv = place(lax.rem(me + 1, total)), place(lax.rem(me + total - 1, total))
    barrier = pltpu.get_barrier_semaphore()
    pl.semaphore_signal(barrier, inc=1, device_id=nxt, device_id_type=MESH)
    pl.semaphore_signal(barrier, inc=1, device_id=prv, device_id_type=MESH)
    s_n, inner, t_n, c = near.shape
    f_n = x_hbm.shape[2]
    fetch = pltpu.make_async_copy(x_hbm.at[:, :, pl.ds(f_n - t_n, t_n), :], near, local)
    fetch.start()
    fetch.wait()
    p_n = inner // STEPS
    rows_f[...] = near[...].reshape(rows_f.shape).astype(F32)
    zero_ref(sent)
    count = s_n * inner
    for k in range(2):
        line = rows_f[pl.ds(t_n - 2 + k, count, stride=t_n), :]
        for s in range(s_n):
            for step in range(STEPS):
                at = s * inner + step * p_n
                sent[step, s, 0:p_n, k * c : (k + 1) * c] = line[at : at + p_n, :]
    pl.semaphore_wait(barrier, 2)
    copy = pltpu.make_async_remote_copy(
        src_ref=sent, dst_ref=land, send_sem=sems.at[0], recv_sem=sems.at[1], device_id=nxt, device_id_type=MESH
    )
    copy.start()

    lane = lax.broadcasted_iota(jnp.int32, (1, LANES), 1)
    for k in range(2):
        half = pltpu.roll(norm_ref[k], LANES // 2, 1)
        main = jnp.where(lane < LANES // 2, half[0:23], half[1:24])
        for j in range(2):
            v = jnp.where(lane // 32 == j, norm_ref[k, 0:1, :], 0.0)
            v = v + pltpu.roll(v, 64, 1)
            gb_ref[k, j : j + 1, :] = v + pltpu.roll(v, 32, 1)
        for j in range(4):
            gb_ref[k, 2 + j : 3 + j, :] = main[0:1]
        gb_ref[k, 6:28, :] = main[1:23]
        gb_ref[k, 28:32, :] = jnp.zeros((4, LANES), F32)

    def row(value):
        return jnp.full((1, LANES), value, F32)

    last = jnp.where(me < total - 1, 1.0, 0.0)
    link = [jnp.where(clip_ref[t] >= 1, 1.0, 0.0) for t in range(t_n)]
    for t in range(t_n):
        filled = row(fill_ref[t].astype(F32))
        after = row(link[t + 1] if t + 1 < t_n else last)
        m16_ref[0, t : t + 1, :] = filled
        m16_ref[1, t : t + 1, :] = row(link[t])
        m16_ref[2, t : t + 1, :] = after
        m64_ref[0, 4 * t : 4 * t + 4, :] = jnp.broadcast_to(filled, (4, LANES))
        m64_ref[1, 4 * t : 4 * t + 1, :] = row(link[t])
        m64_ref[1, 4 * t + 1 : 4 * t + 4, :] = jnp.ones((3, LANES), F32)
        m64_ref[2, 4 * t : 4 * t + 3, :] = jnp.ones((3, LANES), F32)
        m64_ref[2, 4 * t + 3 : 4 * t + 4, :] = after

    zero_ref(wfa_ref)
    zero_ref(wout_ref)
    a = wfi_ref.shape[0]
    for s in range(s_n):
        wfa_ref[s * a : (s + 1) * a, s * LANES : (s + 1) * LANES] = wfi_ref[...]
        wout_ref[s * a : (s + 1) * a, s * LANES : (s + 1) * LANES] = wfo_ref[...]
    tall = (LANES, a)
    spread = (lax.broadcasted_iota(jnp.int32, tall, 0) % a == lax.broadcasted_iota(jnp.int32, tall, 1)).astype(BF16)
    square = (LANES, LANES)
    diag = lax.broadcasted_iota(jnp.int32, square, 0) // a == lax.broadcasted_iota(jnp.int32, square, 1) // a
    for k in range(3):
        left = dot(spread, wfm_ref[k]).astype(BF16)
        wmid_ref[k * LANES : (k + 1) * LANES, :] = jnp.where(diag, dot_nt(left, spread), 0.0).astype(BF16)
        right = dot_nt(spread, wfm_ref[k]).astype(BF16)
        wback_ref[k * LANES : (k + 1) * LANES, :] = jnp.where(diag, dot_nt(right, spread), 0.0).astype(BF16)
    copy.wait()
    tail_ref[...] = land[...]


def prepare(x_fast, fill, clip_offset, norms, w_fast_in, w_fast_mid, w_fast_out):
    s_n, inner, f_n, c = x_fast.shape
    t_n = fill.shape[0]
    p_n = inner // STEPS
    vm = pl.BlockSpec(memory_space=pltpu.VMEM)
    sm = pl.BlockSpec(memory_space=pltpu.SMEM)
    tail = (STEPS, s_n, 8, 2 * c)
    outs = [(tail, F32), ((2, 32, LANES), F32), ((3, t_n, LANES), F32), ((3, f_n, LANES), F32),
            ((LANES, s_n * c), BF16), ((3 * LANES, LANES), BF16), ((3 * LANES, LANES), BF16), ((LANES, s_n * c), BF16)]
    return pl.pallas_call(
        k_prep,
        out_shape=[jax.ShapeDtypeStruct(s, d) for s, d in outs],
        in_specs=[pl.BlockSpec(memory_space=pl.ANY), sm, sm, vm, vm, vm, vm],
        out_specs=[vm] * len(outs),
        scratch_shapes=[
            pltpu.VMEM((s_n, inner, t_n, c), BF16),
            pltpu.VMEM((s_n * inner * t_n, c), F32),
            pltpu.VMEM(tail, F32),
            pltpu.VMEM(tail, F32),
            pltpu.SemaphoreType.DMA((2,)),
            pltpu.SemaphoreType.DMA,
        ],
        compiler_params=pltpu.CompilerParams(collective_id=10, has_side_effects=True, vmem_limit_bytes=VMEM_LIMIT),
        name="prepare",
    )(x_fast, fill, clip_offset, norms, w_fast_in.T, w_fast_mid, w_fast_out)


def per_device(slow_input, fast_input, clip_offset, fill, w_fast_in, w_fast_mid, w_fast_out, w_lateral,
               w_slow_in, w_slow_mid, w_slow_out, w_shortcut, gains, biases, slow_cot, fast_cot):
    sizes = (lax.axis_size("path"), lax.axis_size("frames"))
    t_n, side, _, c_slow = slow_input.shape
    f_n, c_fast = fast_input.shape[0], fast_input.shape[3]
    in_fast, in_slow, c_lat = w_fast_in.shape[1], w_slow_in.shape[1], w_lateral.shape[2]
    pixels = side * side
    groups = LANES // in_fast
    inner = pixels // groups
    p_n = inner // STEPS

    def slow_view(a):
        return jnp.transpose(a, (1, 2, 0, 3)).reshape(groups, inner, t_n, a.shape[3])

    def fast_view(a):
        return jnp.transpose(a, (1, 2, 0, 3)).reshape(groups, inner, f_n, a.shape[3])

    def unview(a):
        return jnp.transpose(a.reshape(side, side, a.shape[2], a.shape[3]), (2, 0, 1, 3))

    x_slow, cot_slow = slow_view(slow_input), slow_view(slow_cot)
    x_fast, cot_fast = fast_view(fast_input), fast_view(fast_cot)

    norms = jnp.stack([gains, biases])
    norms = jnp.pad(norms, ((0, 0), (0, -norms.shape[1] % (8 * LANES)))).reshape(2, -1, LANES)
    tail, gb, m16, m64, wfa, wmid, wback, wout = prepare(
        x_fast, fill, clip_offset, norms, w_fast_in, w_fast_mid, w_fast_out
    )
    wlat = w_lateral.reshape(-1, c_lat)
    wsp = w_slow_mid.reshape(9, in_slow, in_slow)

    sl = (groups, inner, t_n)
    fp = (inner, f_n)

    def slow_out(width, dtype):
        return out_blocked(sl + (width,), dtype, 1, p_n)

    def fast_out(width, dtype):
        return out_blocked(fp + (width,), dtype, 0, p_n)

    def sb_(a):
        return blocked(a, 1, p_n)

    def fb_(a):
        return blocked(a, 0, p_n)

    def stat(n):
        return out_whole((pad8(n), LANES), F32)

    def acc(rows_n, width, count):
        return [pltpu.VMEM((rows_n, width), F32)] * count

    small = (STEPS, 8, LANES)

    fa, lat, taps, c1, hp, hn = call(
        k_first,
        [sb_(x_fast), blocked(tail, 0, 1), whole(m16), whole(m64), whole(wfa), whole(wlat)],
        [fast_out(LANES, F32), slow_out(c_lat, F32), slow_out(5 * c_fast, BF16), STAT, UP, DOWN],
        [pltpu.VMEM((groups * p_n * f_n, c_fast), F32), *acc(f_n, LANES, 2), *acc(t_n, c_lat, 2)],
        "first",
        Exchange(sizes, 1, 7, fwd=(("lane4", 0, 1), ("plain", 6, 2)), up=small, down=small),
        [gb],
    )

    lact, ftap, sa, sp, fb, c2 = call(
        k_join,
        [sb_(x_slow), sb_(lat), fb_(fa), blocked(hp, 0, 1), blocked(hn, 0, 1), whole(c1), whole(m16), whole(m64),
         whole(w_slow_in), whole(w_shortcut), whole(wmid)],
        [slow_out(c_lat, BF16), fast_out(3 * LANES, BF16), slow_out(in_slow, F32), slow_out(c_slow, F32),
         fast_out(LANES, F32), STAT],
        [*acc(t_n, in_slow, 2), *acc(t_n, c_slow, 2), *acc(f_n, LANES, 2)],
        "join",
        Exchange(sizes, 2, 23, fwd=(("lane4", 1, 1), ("plain", 8, 2), ("plain", 20, 8))),
        [gb],
    )

    rows_n = side // STEPS
    pad, sb, fact, c3 = call(
        k_spatial,
        [whole(sa.reshape(side, side, t_n, in_slow)),
         fb_(fb), whole(c2), whole(m16), whole(m64), whole(wsp), whole(wout)],
        [out_whole((side + 2, side + 2, t_n, in_slow), BF16),
         out_blocked((side, side, t_n, in_slow), F32, 0, rows_n), fast_out(LANES, BF16), STAT],
        [*acc(t_n, in_slow, 2), *acc(f_n, groups * c_fast, 2)],
        "spatial",
        Exchange(sizes, 3, 13, fwd=(("row4", 2, 4), ("plain", 10, 2))),
        [gb],
    )

    sb4 = sb.reshape(sl + (in_slow,))
    sact, fast_y, df, st = call(
        k_expand,
        [sb_(sb4), fb_(fact), sb_(x_fast), sb_(cot_fast), whole(c3), whole(m16), whole(m64), whole(w_slow_out), whole(wout)],
        [slow_out(in_slow, BF16), out_blocked((groups, inner, f_n, c_fast), BF16, 1, p_n),
         fast_out(groups * c_fast, F32), stat(25)],
        [*acc(t_n, c_slow, 2), *acc(f_n, groups * c_fast, 2)],
        "expand",
    )
    c4, q4 = exchange_alone(
        Exchange(sizes, 4, 25, fwd=(("plain", 12, 8),), bwd=(("row4", 0, 0, 2, 4, 0, 4),)), st, gb, [c3]
    )

    halo_pair = out_blocked((STEPS, 2, 8, LANES), F32, 0, 1)
    slow_y, dy, dfb, g_fout, up, down, st = call(
        k_out,
        [sb_(sact), sb_(sp), sb_(cot_slow), fb_(df), fb_(fact), fb_(fb), whole(c2), whole(c3), whole(c4), whole(q4),
         whole(m16), whole(m64), whole(w_slow_out), whole(wout)],
        [slow_out(c_slow, BF16), slow_out(c_slow, F32), fast_out(LANES, F32),
         out_whole((in_fast, c_fast), F32), halo_pair, halo_pair, stat(26)],
        [*acc(t_n, c_slow, 3), *acc(f_n, LANES, 2), *acc(LANES, groups * c_fast, 1)],
        "out",
    )
    pair = (STEPS, 2, 8, LANES)
    ex5 = Exchange(
        sizes, 5, 26,
        bwd=(("plain", 0, 0, 12, 8, 0, 8), ("plain", 1, 3, 20, 8, 0, 16), ("lane4", 1, 0, 1, 1, 24, 25)),
        up=pair, down=pair,
    )
    q5, hp, hn = exchange_alone(ex5, st, gb, [c4, c2], up, down)

    c_cat = w_slow_in.shape[0]
    gw_out, dsp, dsb, dfa, g_fmid, q6 = call(
        k_back_out,
        [sb_(x_slow), sb_(lact), sb_(dy), sb_(sp), sb_(sact), sb_(sb4), fb_(dfb), fb_(fb), fb_(fa), fb_(ftap), blocked(hp, 0, 1), blocked(hn, 0, 1),
         whole(c1), whole(c2), whole(c3), whole(c4), whole(q5), whole(m16), whole(m64), whole(w_slow_out), whole(wback)],
        [out_whole(((c_cat + in_slow) * c_slow // in_slow, in_slow), BF16), slow_out(c_slow, BF16),
         slow_out(in_slow, F32), fast_out(LANES, F32), out_whole((3 * in_fast, LANES), F32), STAT],
        [*acc(t_n, in_slow, 2), *acc(f_n, LANES, 2), *acc(c_cat, c_slow, 1), *acc(in_slow, c_slow, 1),
         *acc(LANES, 3 * LANES, 1)],
        "back_out",
        Exchange(sizes, 6, 6, bwd=(("plain", 0, 4, 10, 2, 0, 2), ("lane4", 1, 0, 0, 1, 4, 5))),
        [gb, c3, c1],
    )

    grid = (side, side, t_n, in_slow)
    dsa, dfa_low, gw_mid, gw_fast, q7 = call(
        k_back_spatial,
        [whole(dsb.reshape(grid)), whole(sb), blocked(sa.reshape(grid), 0, rows_n), whole(pad), sb_(x_fast), fb_(dfa), fb_(fa),
         whole(g_fout), whole(g_fmid), whole(c1), whole(c2), whole(c3), whole(q6), whole(m16), whole(m64), whole(wsp)],
        [out_blocked(grid, F32, 0, rows_n), fast_out(LANES, BF16), out_whole((9 * in_slow, in_slow), BF16),
         out_whole((3 * in_fast, 2 * LANES), F32), STAT],
        [*acc(t_n, in_slow, 2), pltpu.VMEM((side + 2, side + 2, t_n, in_slow), BF16), *acc(in_slow, 9 * in_slow, 1),
         *acc(LANES, groups * c_fast, 1)],
        "back_spatial",
        Exchange(sizes, 7, 4, bwd=(("plain", 0, 1, 8, 2, 0, 2),)),
        [gb, c2],
    )

    gw_in, slow_gx, dlat, down, st = call(
        k_back_join,
        [sb_(x_slow), sb_(lact), sb_(dsa.reshape(sl + (in_slow,))), sb_(sa), sb_(dsp), sb_(lat), whole(c1), whole(c2), whole(q7), whole(m16),
         whole(w_slow_in), whole(w_shortcut)],
        [out_whole((c_cat, in_slow), BF16), slow_out(c_slow, BF16), slow_out(c_lat, F32),
         out_blocked((STEPS, 2, groups, 8, c_lat), F32, 0, 1), stat(4)],
        [*acc(t_n, c_lat, 2), *acc(in_slow, c_cat, 1)],
        "back_join",
    )
    ex8 = Exchange(sizes, 8, 4, bwd=(("plain", 0, 1, 6, 2, 0, 2),), down=down.shape)
    q8, hn = exchange_alone(ex8, st, gb, [c1], None, down)

    fast_gx, gw_lat = call(
        k_last,
        [sb_(dlat), sb_(lat), sb_(taps), blocked(hn, 0, 1), fb_(df), fb_(dfa_low), whole(c1), whole(q8), whole(m16),
         whole(wlat), whole(wfa)],
        [out_blocked((groups, inner, f_n, c_fast), BF16, 1, p_n), out_whole((5 * c_fast, c_lat), BF16)],
        [pltpu.VMEM((groups * p_n * f_n, c_fast), F32), *acc(c_lat, 5 * c_fast, 1)],
        "last",
    )

    reduced = reduce_all(sizes, 9, [gw_out, gw_mid, gw_in, gw_lat, gw_fast])
    blocks = c_slow // in_slow
    pieces, at = [], 0
    for out, tall in ((0, c_cat), (1, in_slow)):
        for n in range(blocks):
            pieces.append((at, tall, out, n * in_slow))
            at += tall
    for out, tall in ((2, gw_mid.shape[0]), (3, c_cat), (4, gw_lat.shape[0]), (5, gw_fast.shape[0])):
        pieces.append((at, tall, out, None))
        at += tall
    g_short, g_sout, gw_mid, gw_in, gw_lat, gw_fast = unpack(
        reduced, tuple(pieces),
        [(c_cat, c_slow), (in_slow, c_slow), gw_mid.shape, (c_cat, in_slow), gw_lat.shape, gw_fast.shape],
    )
    taps_t = [gw_fast[in_fast : 2 * in_fast, :in_fast], gw_fast[in_fast : 2 * in_fast, c_fast : c_fast + in_fast],
              gw_fast[2 * in_fast :, :in_fast]]
    grads = (
        gw_fast[:in_fast, :c_fast].T,
        jnp.transpose(jnp.stack(taps_t), (0, 2, 1)),
        gw_fast[:in_fast, c_fast:],
        gw_lat.reshape(w_lateral.shape),
        gw_in,
        gw_mid.reshape(w_slow_mid.shape),
        g_sout,
        g_short,
    )

    def norm_grads(slab):
        def row(q, at, n):
            return q[slab, at : at + n].reshape(-1)

        return jnp.concatenate(
            [row(q6, 2, 1)[:in_fast], row(q5, 16, 1)[:in_fast], row(q4, 0, 1), row(q8, 0, 2), row(q7, 0, 2),
             row(q6, 0, 2), row(q5, 0, 8), row(q5, 8, 8)]
        )

    return (
        unview(slow_y),
        unview(fast_y),
        unview(slow_gx),
        unview(fast_gx),
        *grads,
        norm_grads(3),
        norm_grads(2),
    )


def solution(mesh):
    frames = P(("path", "frames"), None, None, None)
    in_specs = (frames, frames, P(AXES), P(AXES), *([P()] * 10), frames, frames)
    out_specs = (*([frames] * 4), *([P()] * 10))
    return jax.shard_map(per_device, mesh=mesh, in_specs=in_specs, out_specs=out_specs, check_vma=False)
```

```python
import functools

import jax
import jax.numpy as jnp
from jax import lax
from jax.experimental import pallas as pl
from jax.experimental.pallas import tpu as pltpu
from jax.sharding import PartitionSpec as P

norm_eps = 1e-05
F32 = jnp.float32
BF16 = jnp.bfloat16
MESH = pl.DeviceIdType.MESH
AXES = ("path", "frames")
STEPS = 7
LANES = 128
VMEM_LIMIT = 56 * 1024 * 1024


def dot(a, b):
    return jnp.dot(a, b, preferred_element_type=F32)


def dot_nt(a, b):
    return lax.dot_general(a, b, (((1,), (1,)), ((), ())), preferred_element_type=F32)


def dot_tn(a, b):
    return lax.dot_general(a, b, (((0,), (0,)), ((), ())), preferred_element_type=F32)


def sig(v):
    return 0.5 * jnp.tanh(0.5 * v) + 0.5


def slope(v):
    s = sig(v)
    return s + (v * s) * (1.0 - s)


def rows(ref, slab, first, count):
    parts = [ref[slab, first + j : first + j + 1, :] for j in range(count)]
    return parts[0] if count == 1 else jnp.concatenate(parts, axis=1)


def put_rows(ref, first, value):
    for j in range(value.shape[1] // LANES):
        ref[first + j : first + j + 1, :] = value[:, j * LANES : (j + 1) * LANES]


def zero_ref(ref):
    ref[...] = jnp.zeros(ref.shape, ref.dtype)


def spread_add(step, z, mean_ref, m2_ref, cols=slice(None)):
    count = z.shape[0]
    mean = jnp.sum(z, axis=0) * (1.0 / count)
    d = z - mean
    m2 = jnp.sum(d * d, axis=0)
    first = step == 0
    old_mean = jnp.where(first, 0.0, mean_ref[:, cols])
    old_m2 = jnp.where(first, 0.0, m2_ref[:, cols])
    done = jnp.full((1, z.shape[-1]), step, jnp.int32).astype(F32)
    share = 1.0 / (done + 1.0)
    delta = mean - old_mean
    mean_ref[:, cols] = old_mean + delta * share
    m2_ref[:, cols] = old_m2 + m2 + delta * delta * (done * share * count)


def spread_end(mean_ref, m2_ref, fill, positions):
    filled = jnp.sum(fill, axis=0, keepdims=True)
    mean = jnp.sum(fill * mean_ref[...], axis=0, keepdims=True) / jnp.maximum(filled, 1.0)
    d = mean_ref[...] - mean
    m2 = jnp.sum(fill * (m2_ref[...] + positions * (d * d)), axis=0, keepdims=True)
    return mean, m2


def sum_add(step, value, ref, cols=slice(None)):
    ref[:, cols] = jnp.where(step == 0, 0.0, ref[:, cols]) + jnp.sum(value, axis=0)


def sum_end(ref):
    return jnp.sum(ref[...], axis=0, keepdims=True)


def pad8(n):
    return -(-n // 8) * 8


def exchange_peers(cfg):
    paths, length = lax.axis_size("path"), lax.axis_size("frames")
    near = 4
    g1, g2 = paths * near, length // near
    me_p, me_f = lax.axis_index("path"), lax.axis_index("frames")
    me = me_p * length + me_f
    total = paths * length
    r1 = me_p * near + lax.rem(me_f, near)
    r2 = lax.div(me_f, near)

    def peer1(k):
        r = lax.rem(r1 + k, g1)
        return (lax.div(r, near), r2 * near + lax.rem(r, near))

    def peer2(k):
        r = lax.rem(r2 + k, g2)
        return (me_p, r * near + lax.rem(me_f, near))

    def split(index):
        return (lax.div(index, length), lax.rem(index, length))

    nxt, prv = split(lax.rem(me + 1, total)), split(lax.rem(me + total - 1, total))
    return g1, g2, r1, r2, peer1, peer2, nxt, prv


def exchange_hello(cfg):
    g1, g2, _, _, peer1, peer2, nxt, prv = exchange_peers(cfg)
    peers = [peer1(k) for k in range(1, g1)] + [peer2(k) for k in range(1, g2)]
    if cfg.greets:
        peers += [nxt, prv]
    for peer in peers:
        pl.semaphore_signal(pltpu.get_barrier_semaphore(), inc=1, device_id=peer, device_id_type=MESH)
    return len(peers)


def exchange_run(cfg, ins, outs, scratch, meanwhile=None, post=None):
    fwd, bwd = cfg.fwd, cfg.bwd
    nf = sum(c[2] for c in fwd)
    nb = max((c[6] + c[4] for c in bwd), default=0)
    n_row = 2 * nf + nb
    stats_ref, up_ref, down_ref = scratch[:3]
    gb_ref, *coef_refs = ins
    outs = list(outs)
    coef_out = outs.pop(0) if nf else None
    pq_out = outs.pop(0) if nb else None
    from_prev = outs.pop(0) if cfg.up else None
    from_next = outs.pop(0) if cfg.down else None
    slots1, slots2, mid, tot, send1, recv1, send2, recv2, up_land, up_sems, down_land, down_sems = scratch[3:15]
    g1, g2, r1, r2, peer1, peer2, nxt, prv = exchange_peers(cfg)

    halos = []
    copies = []
    for k in range(1, g1):
        copies.append(
            pltpu.make_async_remote_copy(
                src_ref=stats_ref,
                dst_ref=slots1.at[r1],
                send_sem=send1.at[k],
                recv_sem=recv1.at[k],
                device_id=peer1(k),
                device_id_type=MESH,
            )
        )
        copies[-1].start()
    for used, src, land, sems, peer in (
        (cfg.up, up_ref, up_land, up_sems, nxt),
        (cfg.down, down_ref, down_land, down_sems, prv),
    ):
        if used:
            halos.append(
                pltpu.make_async_remote_copy(
                    src_ref=src,
                    dst_ref=land,
                    send_sem=sems.at[0],
                    recv_sem=sems.at[1],
                    device_id=peer,
                    device_id_type=MESH,
                )
            )
            halos[-1].start()
    slots1[r1] = stats_ref[...]
    if meanwhile is not None:
        meanwhile()
    for c in copies:
        c.wait_recv()

    def combine(slots, count, out):
        if nf:
            n = slots[0, n_row : n_row + 1, :]
            for g in range(1, count):
                n = n + slots[g, n_row : n_row + 1, :]
            acc = slots[0, n_row : n_row + 1, :] * slots[0, 0:nf, :]
            for g in range(1, count):
                acc = acc + slots[g, n_row : n_row + 1, :] * slots[g, 0:nf, :]
            mean = acc / jnp.maximum(n, 1.0)
            m2 = None
            for g in range(count):
                d = slots[g, 0:nf, :] - mean
                part = slots[g, nf : 2 * nf, :] + slots[g, n_row : n_row + 1, :] * (d * d)
                m2 = part if m2 is None else m2 + part
            out[0:nf, :] = mean
            out[nf : 2 * nf, :] = m2
            out[n_row : n_row + 1, :] = n
        if nb:
            acc = slots[0, 2 * nf : n_row, :]
            for g in range(1, count):
                acc = acc + slots[g, 2 * nf : n_row, :]
            out[2 * nf : n_row, :] = acc

    zero_ref(mid)
    combine(slots1, g1, mid)
    copies2 = []
    for k in range(1, g2):
        copies2.append(
            pltpu.make_async_remote_copy(
                src_ref=mid,
                dst_ref=slots2.at[r2],
                send_sem=send2.at[k],
                recv_sem=recv2.at[k],
                device_id=peer2(k),
                device_id_type=MESH,
            )
        )
        copies2[-1].start()
    slots2[r2] = mid[...]
    for c in copies2:
        c.wait_recv()
    combine(slots2, g2, tot)

    def lanes4(v):
        w = v + pltpu.roll(v, 64, 1)
        return w + pltpu.roll(w, 32, 1)

    at = 0
    for kind, g_row, count in fwd:
        n = tot[n_row : n_row + 1, :]
        mean = tot[at : at + count, :]
        m2 = tot[nf + at : nf + at + count, :]
        if kind == "lane4":
            whole = lanes4(mean) * 0.25
            d = mean - whole
            var = lanes4(m2 + n * (d * d)) / (4.0 * n)
            mean = whole
        elif kind == "row4":
            whole = jnp.sum(mean, axis=0, keepdims=True) * 0.25
            d = mean - whole
            var = jnp.sum(m2 + n * (d * d), axis=0, keepdims=True) / (4.0 * n)
            var = jnp.broadcast_to(var, (count, LANES))
            mean = jnp.broadcast_to(whole, (count, LANES))
        else:
            var = m2 / n
        inv = lax.rsqrt(var + norm_eps)
        scale = inv * gb_ref[0, g_row : g_row + count, :]
        coef_out[0, at : at + count, :] = scale
        coef_out[1, at : at + count, :] = gb_ref[1, g_row : g_row + count, :] - mean * scale
        coef_out[2, at : at + count, :] = inv
        coef_out[3, at : at + count, :] = mean * inv
        coef_out[4, at : at + count, :] = jnp.broadcast_to(n, (count, LANES))
        at += count
    at = 0
    for kind, coef, row, _, count, db_at, dg_at in bwd:
        db = tot[2 * nf + db_at : 2 * nf + db_at + count, :]
        dg = tot[2 * nf + dg_at : 2 * nf + dg_at + count, :]
        c = coef_refs[coef]
        scale, inv = c[0, row : row + count, :], c[2, row : row + count, :]
        mi, n = c[3, row : row + count, :], c[4, row : row + count, :]
        if kind == "lane4":
            db, dg, n = lanes4(db), lanes4(dg), 4.0 * n
        elif kind == "row4":
            db = jnp.broadcast_to(jnp.sum(db, axis=0, keepdims=True), (count, LANES))
            dg = jnp.broadcast_to(jnp.sum(dg, axis=0, keepdims=True), (count, LANES))
            n = 4.0 * n
        pq_out[0, at : at + count, :] = scale / n * (db - mi * dg)
        pq_out[1, at : at + count, :] = scale / n * inv * dg
        pq_out[2, at : at + count, :] = db
        pq_out[3, at : at + count, :] = dg
        at += count

    if cfg.post:
        post_sent, post_land, post_sems = scratch[15:]
        post(pq_out, post_sent)
        late = pltpu.make_async_remote_copy(
            src_ref=post_sent,
            dst_ref=post_land,
            send_sem=post_sems.at[0],
            recv_sem=post_sems.at[1],
            device_id=prv,
            device_id_type=MESH,
        )
        late.start()
        late.wait()
        outs.pop(0)[...] = post_land[...]
    for c in halos:
        c.wait()
    if cfg.up:
        from_prev[...] = up_land[...]
    if cfg.down:
        from_next[...] = down_land[...]
    for c in copies:
        c.wait_send()
    for c in copies2:
        c.wait_send()


class Exchange:
    def __init__(self, sizes, cid, rows_n, fwd=(), bwd=(), up=None, down=None, post=None):
        self.cid, self.fwd, self.bwd, self.up, self.down, self.post = cid, fwd, bwd, up, down, post
        self.greets = bool(up or down or post)
        g1, g2, r = sizes[0] * 4, sizes[1] // 4, pad8(rows_n)
        self.outs = []
        nf, nn = sum(c[2] for c in fwd), sum(c[4] for c in bwd)
        if nf:
            self.outs.append(((5, nf, LANES), F32))
        if nn:
            self.outs.append(((4, nn, LANES), F32))
        self.outs += [(h, F32) for h in (up, down) if h]
        if post:
            self.outs.append((post, BF16))
        none = (8, LANES)
        self.stats = (r, LANES)
        self.work = [
            pltpu.VMEM((g1, r, LANES), F32),
            pltpu.VMEM((g2, r, LANES), F32),
            pltpu.VMEM((r, LANES), F32),
            pltpu.VMEM((r, LANES), F32),
            pltpu.SemaphoreType.DMA((g1,)),
            pltpu.SemaphoreType.DMA((g1,)),
            pltpu.SemaphoreType.DMA((g2,)),
            pltpu.SemaphoreType.DMA((g2,)),
            pltpu.VMEM(up or none, F32),
            pltpu.SemaphoreType.DMA((2,)),
            pltpu.VMEM(down or none, F32),
            pltpu.SemaphoreType.DMA((2,)),
        ]
        if post:
            self.work += [pltpu.VMEM(post, BF16), pltpu.VMEM(post, BF16), pltpu.SemaphoreType.DMA((2,))]
        self.local = [pltpu.VMEM(self.stats, F32), pltpu.VMEM(up or none, F32), pltpu.VMEM(down or none, F32)]


def exchange_alone(ex, stats, gb, coefs=(), up=None, down=None):
    vm = pl.BlockSpec(memory_space=pltpu.VMEM)
    operands = [stats, gb, *coefs] + [h for h in (up, down) if h is not None]
    n_in, n_out = len(operands), len(ex.outs)

    def kernel(*refs):
        ins, outs, work = refs[:n_in], refs[n_in : n_in + n_out], refs[n_in + n_out :]
        count = exchange_hello(ex)
        pl.semaphore_wait(pltpu.get_barrier_semaphore(), count)
        halos = list(ins[2 + len(coefs) :])
        up_ref = halos.pop(0) if ex.up else None
        down_ref = halos.pop(0) if ex.down else None
        exchange_run(ex, ins[1 : 2 + len(coefs)], outs, [ins[0], up_ref, down_ref, *work])

    return pl.pallas_call(
        kernel,
        out_shape=[jax.ShapeDtypeStruct(s, d) for s, d in ex.outs],
        in_specs=[vm] * n_in,
        out_specs=[vm] * n_out,
        scratch_shapes=ex.work,
        compiler_params=pltpu.CompilerParams(collective_id=ex.cid, has_side_effects=True),
        name=f"exchange_{ex.cid}",
    )(*operands)


STAT, UP, DOWN = "stat", "up", "down"


def call(kernel, ins, outs, scratch=(), name=None, ex=None, ex_ins=()):
    real = [o for o in outs if not isinstance(o, str)]
    extra_in = [whole(a) for a in ex_ins]
    extra_out = [out_whole(s, d) for s, d in ex.outs] if ex else []
    all_in, all_out = [*ins, *extra_in], [*real, *extra_out]
    local = [*ex.local, *ex.work] if ex else []
    sizes = [len(ins), len(extra_in), len(real), len(extra_out), len(scratch), len(local)]
    ends = [sum(sizes[: k + 1]) for k in range(len(sizes))]

    def body(*refs):
        k_in, x_in, k_out, x_out, k_scr, x_scr = (refs[e - n : e] for e, n in zip(ends, sizes))
        if ex is None:
            kernel(*k_in, *k_out, *k_scr)
            return
        i = pl.program_id(0)

        @pl.when(i == 0)
        def _():
            exchange_hello(ex)

        named = {STAT: x_scr[0]}
        if ex.up:
            named[UP] = x_scr[1].at[pl.ds(i, 1)]
        if ex.down:
            named[DOWN] = x_scr[2].at[pl.ds(i, 1)]
        it = iter(k_out)
        late = kernel(*k_in, *[named[o] if isinstance(o, str) else next(it) for o in outs], *k_scr)

        @pl.when(i == STEPS - 1)
        def _():
            pl.semaphore_wait(pltpu.get_barrier_semaphore(), len_peers(ex))
            exchange_run(ex, x_in, x_out, x_scr, late)

    params = {"collective_id": ex.cid, "has_side_effects": True} if ex else {}
    return pl.pallas_call(
        body,
        grid=(STEPS,),
        in_specs=[pl.BlockSpec(b, m) for _, b, m in all_in],
        out_specs=[pl.BlockSpec(b, m) for _, _, b, m in all_out],
        out_shape=[jax.ShapeDtypeStruct(s, d) for s, d, _, _ in all_out],
        scratch_shapes=[*scratch, *local],
        compiler_params=pltpu.CompilerParams(
            dimension_semantics=("arbitrary",), vmem_limit_bytes=VMEM_LIMIT, **params
        ),
        name=name,
    )(*[a for a, _, _ in all_in])


def len_peers(ex):
    paths, length = lax.axis_size("path"), lax.axis_size("frames")
    return paths * 4 - 1 + length // 4 - 1 + (2 if ex.greets else 0)


def whole(array):
    zeros = (0,) * array.ndim
    return (array, array.shape, lambda i: zeros)


def blocked(array, axis, size):
    block = array.shape[:axis] + (size,) + array.shape[axis + 1 :]
    return (array, block, lambda i: tuple(i if d == axis else 0 for d in range(array.ndim)))


def out_whole(shape, dtype):
    zeros = (0,) * len(shape)
    return (shape, dtype, shape, lambda i: zeros)


def out_blocked(shape, dtype, axis, size):
    block = shape[:axis] + (size,) + shape[axis + 1 :]
    return (shape, dtype, block, lambda i: tuple(i if d == axis else 0 for d in range(len(shape))))


def flat(value):
    return value.reshape(-1, value.shape[-1])


def spread_rows(ref, index, count, height):
    return [jnp.broadcast_to(ref[(*index, slice(p, p + 1))], (height, ref.shape[-1])) for p in range(count)]


def k_first(x_ref, tail_ref, m16_ref, m64_ref, wfa_ref, wlat_ref,
            fa_ref, lat_ref, taps_ref, st_ref, up_ref, down_ref, xs, fm, fv, lm, lv):
    i = pl.program_id(0)
    x = x_ref[...]
    s_n, p_n, f_n, _ = x.shape
    packed = jnp.concatenate([flat(x[s]) for s in range(s_n)], axis=1)
    fa = dot_nt(packed, wfa_ref[...])
    fa_ref[...] = fa.reshape(fa_ref.shape)
    zero_ref(up_ref)
    zero_ref(down_ref)
    for p in range(p_n):
        down_ref[0, p : p + 1, :] = fa[p * f_n : p * f_n + 1, :]
        up_ref[0, p : p + 1, :] = fa[p * f_n + f_n - 1 : p * f_n + f_n, :]
    spread_add(i, fa.reshape(p_n, f_n, LANES), fm, fv)

    xs[...] = flat(x).astype(F32)
    n = xs.shape[0] // 4
    quarter = [xs[pl.ds(k, n, stride=4), :] for k in range(4)]
    t_n = f_n // 4
    first = lax.broadcasted_iota(jnp.int32, (n // t_n, t_n, LANES), 1) == 0
    link = m16_ref[1:2]
    taps = []
    for k in range(2):
        halo = jnp.concatenate(
            [
                jnp.broadcast_to(tail_ref[0, s, p : p + 1, k * LANES : (k + 1) * LANES], (t_n, LANES))
                for s in range(s_n)
                for p in range(p_n)
            ],
            axis=0,
        )
        moved = pltpu.roll(quarter[2 + k], 1, 0).reshape(n // t_n, t_n, LANES)
        taps.append(flat(jnp.where(first, halo.reshape(moved.shape), moved) * link))
    taps = jnp.concatenate([*taps, *quarter[:3]], axis=1).astype(BF16)
    taps_ref[...] = taps.reshape(taps_ref.shape)
    lat = dot(taps, wlat_ref[...])
    lat_ref[...] = lat.reshape(lat_ref.shape)
    spread_add(i, lat.reshape(n // t_n, t_n, lat.shape[1]), lm, lv)

    @pl.when(i == STEPS - 1)
    def _():
        zero_ref(st_ref)
        fill = m16_ref[0, :, 0:1]
        mean, m2 = spread_end(fm, fv, m64_ref[0, :, 0:1], STEPS * p_n)
        put_rows(st_ref, 0, mean)
        put_rows(st_ref, 3, m2)
        mean, m2 = spread_end(lm, lv, fill, STEPS * p_n * s_n)
        put_rows(st_ref, 1, mean)
        put_rows(st_ref, 4, m2)
        put_rows(st_ref, 6, count_row(m16_ref, STEPS * p_n * s_n))


def count_row(m16_ref, positions):
    return jnp.sum(m16_ref[0], axis=0, keepdims=True) * float(positions)


def shifted(value, first_rows, last_rows, f_n):
    n = value.shape[0]
    shape = (n // f_n, f_n, value.shape[1])
    place = lax.broadcasted_iota(jnp.int32, shape, 1)
    before = jnp.where(place == 0, first_rows, pltpu.roll(value, 1, 0).reshape(shape))
    after = jnp.where(place == f_n - 1, last_rows, pltpu.roll(value, n - 1, 0).reshape(shape))
    return before, after


def k_join(x_ref, lat_ref, fa_ref, hp_ref, hn_ref, c1_ref, m16_ref, m64_ref, win_ref, wsc_ref, wmid_ref,
           lact_ref, ftap_ref, sa_ref, sp_ref, fb_ref, st_ref, am, av, pm, pv, bm, bv):
    i = pl.program_id(0)
    s_n, p_n, t_n, c_slow = x_ref.shape
    c_lat = lat_ref.shape[-1]
    v = flat(lat_ref[...]) * rows(c1_ref, 0, 1, 2) + rows(c1_ref, 1, 1, 2)
    lact = (v * sig(v)).astype(BF16)
    lact_ref[...] = lact.reshape(lact_ref.shape)
    joined = jnp.concatenate([flat(x_ref[...]), lact], axis=1)
    wide = c_lat
    for n in range(1 + wsc_ref.shape[1] // wide):
        z = dot(joined, win_ref[...] if n == 0 else wsc_ref[:, (n - 1) * wide : n * wide])
        z4 = z.reshape(s_n, p_n, t_n, wide)
        z3 = z.reshape(s_n * p_n, t_n, wide)
        if n == 0:
            sa_ref[...] = z4
            spread_add(i, z3, am, av)
        else:
            cols = slice((n - 1) * wide, n * wide)
            sp_ref[:, :, :, cols] = z4
            spread_add(i, z3, pm, pv, cols)

    f_n = fa_ref.shape[1]
    scale, shift = rows(c1_ref, 0, 0, 1), rows(c1_ref, 1, 0, 1)

    def act(z):
        w = z * scale + shift
        return (w * sig(w)).astype(BF16).astype(F32)

    fact = act(flat(fa_ref[...]))
    ends = []
    for ref in (hp_ref, hn_ref):
        small = act(ref[0])
        ends.append(
            jnp.concatenate(
                [jnp.broadcast_to(small[p : p + 1, :], (f_n, LANES)) for p in range(p_n)], axis=0
            ).reshape(p_n, f_n, LANES)
        )
    before, after = shifted(fact, ends[0], ends[1], f_n)
    ftap = jnp.concatenate(
        [flat(before * m64_ref[1:2]), fact, flat(after * m64_ref[2:3])], axis=1
    ).astype(BF16)
    ftap_ref[...] = ftap.reshape(ftap_ref.shape)
    fb = dot(ftap, wmid_ref[...])
    fb_ref[...] = fb.reshape(fb_ref.shape)
    spread_add(i, fb.reshape(p_n, f_n, LANES), bm, bv)

    @pl.when(i == STEPS - 1)
    def _():
        zero_ref(st_ref)
        fill = m16_ref[0, :, 0:1]
        positions = STEPS * p_n * s_n
        mean, m2 = spread_end(bm, bv, m64_ref[0, :, 0:1], STEPS * p_n)
        put_rows(st_ref, 0, mean)
        put_rows(st_ref, 11, m2)
        mean, m2 = spread_end(am, av, fill, positions)
        put_rows(st_ref, 1, mean)
        put_rows(st_ref, 12, m2)
        mean, m2 = spread_end(pm, pv, fill, positions)
        put_rows(st_ref, 3, mean)
        put_rows(st_ref, 14, m2)
        put_rows(st_ref, 22, count_row(m16_ref, positions))


def k_spatial(sa_ref, fb_ref, c2_ref, m16_ref, m64_ref, wsp_ref, wout_ref,
              pad_ref, sb_ref, fact_ref, st_ref, sm, sv, cm, cv):
    i = pl.program_id(0)
    h_n, w_n, t_n, c = sa_ref.shape

    @pl.when(i == 0)
    def _():
        scale, shift = rows(c2_ref, 0, 1, 2), rows(c2_ref, 1, 1, 2)
        zero_ref(pad_ref)

        @pl.loop(0, h_n)
        def _(h):
            v = flat(sa_ref[h]) * scale + shift
            pad_ref[h + 1, 1 : w_n + 1] = (v * sig(v)).astype(BF16).reshape(w_n, t_n, c)

    per = h_n // STEPS
    h0 = i * per
    acc = None
    for a in range(3):
        for b in range(3):
            k = 3 * a + b
            part = dot(flat(pad_ref[pl.ds(h0 + a, per), b : b + w_n].reshape(per * w_n, t_n, c)), wsp_ref[k])
            acc = part if acc is None else acc + part
    sb_ref[...] = acc.reshape(sb_ref.shape)
    spread_add(i, acc.reshape(per * w_n, t_n, acc.shape[1]), sm, sv)

    p_n, f_n, _ = fb_ref.shape
    v = flat(fb_ref[...]) * rows(c2_ref, 0, 0, 1) + rows(c2_ref, 1, 0, 1)
    fact = (v * sig(v)).astype(BF16)
    fact_ref[...] = fact.reshape(fact_ref.shape)
    fc = dot(fact, wout_ref[...])
    spread_add(i, fc.reshape(p_n, f_n, fc.shape[1]), cm, cv)

    @pl.when(i == STEPS - 1)
    def _():
        zero_ref(st_ref)
        mean, m2 = spread_end(cm, cv, m64_ref[0, :, 0:1], STEPS * p_n)
        put_rows(st_ref, 0, mean)
        put_rows(st_ref, 6, m2)
        mean, m2 = spread_end(sm, sv, m16_ref[0, :, 0:1], h_n * w_n)
        put_rows(st_ref, 4, mean)
        put_rows(st_ref, 10, m2)
        put_rows(st_ref, 12, count_row(m16_ref, h_n * w_n))


def k_expand(sb_ref, fact_ref, x_ref, cot_ref, c3_ref, m16_ref, m64_ref, wso_ref, wout_ref,
             sact_ref, fout_ref, df_ref, st_ref, cm, cv, s1, s2):
    i = pl.program_id(0)
    s_n, p_n, t_n, c = sb_ref.shape
    v = flat(sb_ref[...]) * rows(c3_ref, 0, 4, 2) + rows(c3_ref, 1, 4, 2)
    sact = (v * sig(v)).astype(BF16)
    sact_ref[...] = sact.reshape(sact_ref.shape)
    wide = 256
    for n in range(wso_ref.shape[1] // wide):
        cols = slice(n * wide, (n + 1) * wide)
        z = dot(sact, wso_ref[:, cols])
        spread_add(i, z.reshape(s_n * p_n, t_n, wide), cm, cv, cols)

    f_n = fact_ref.shape[1]
    fc = dot(flat(fact_ref[...]), wout_ref[...])
    fill = m64_ref[0:1]
    for s in range(s_n):
        cols = slice(s * LANES, (s + 1) * LANES)
        z = fc[:, cols].reshape(p_n, f_n, LANES)
        unit = z * rows(c3_ref, 2, s, 1) - rows(c3_ref, 3, s, 1)
        pre = z * rows(c3_ref, 0, s, 1) + rows(c3_ref, 1, s, 1) + x_ref[s].astype(F32)
        g = sig(pre)
        y = pre * g
        fout_ref[s] = (y * fill).astype(BF16)
        d = cot_ref[s].astype(F32) * fill * (g + y * (1.0 - g))
        df_ref[:, :, cols] = d
        sum_add(i, d, s1, cols)
        sum_add(i, d * unit, s2, cols)

    @pl.when(i == STEPS - 1)
    def _():
        zero_ref(st_ref)
        positions = STEPS * p_n * s_n
        mean, m2 = spread_end(cm, cv, m16_ref[0, :, 0:1], positions)
        put_rows(st_ref, 0, mean)
        put_rows(st_ref, 8, m2)
        put_rows(st_ref, 16, sum_end(s1))
        put_rows(st_ref, 20, sum_end(s2))
        put_rows(st_ref, 24, count_row(m16_ref, positions))


def back_norm(scale, p, q, dy, z, fill):
    return scale * dy - fill * (p + z * q)


def k_out(sact_ref, sp_ref, cot_ref, df_ref, fact_ref, fb_ref, c2_ref, c3_ref, c4_ref, q4_ref,
          m16_ref, m64_ref, wso_ref, wout_ref,
          out_ref, dy_ref, dfb_ref, gout_ref, up_ref, down_ref, st_ref, s1, s2, s3, t1, t2, gout):
    i = pl.program_id(0)
    s_n, p_n, t_n, _ = sact_ref.shape
    sact = flat(sact_ref[...])
    fill = m16_ref[0:1, :, 0:1]
    wide = 256
    for n in range(wso_ref.shape[1] // wide):
        cols = slice(n * wide, (n + 1) * wide)
        shape = (s_n * p_n, t_n, wide)
        sc = dot(sact, wso_ref[:, cols]).reshape(shape)
        sp = sp_ref[:, :, :, cols].reshape(shape)
        u6 = sc * rows(c4_ref, 2, 2 * n, 2) - rows(c4_ref, 3, 2 * n, 2)
        u7 = sp * rows(c2_ref, 2, 3 + 2 * n, 2) - rows(c2_ref, 3, 3 + 2 * n, 2)
        pre = (
            sc * rows(c4_ref, 0, 2 * n, 2)
            + sp * rows(c2_ref, 0, 3 + 2 * n, 2)
            + (rows(c4_ref, 1, 2 * n, 2) + rows(c2_ref, 1, 3 + 2 * n, 2))
        )
        g = sig(pre)
        y = pre * g
        out_ref[:, :, :, cols] = (y * fill).astype(BF16).reshape(s_n, p_n, t_n, wide)
        d = cot_ref[:, :, :, cols].reshape(shape).astype(F32) * fill * (g + y * (1.0 - g))
        dy_ref[:, :, :, cols] = d.reshape(s_n, p_n, t_n, wide)
        sum_add(i, d, s1, cols)
        sum_add(i, d * u6, s2, cols)
        sum_add(i, d * u7, s3, cols)

    f_n = fact_ref.shape[1]
    fact = flat(fact_ref[...])
    fc = dot(fact, wout_ref[...])
    fill4 = m64_ref[0:1]
    parts = []
    for s in range(s_n):
        cols = slice(s * LANES, (s + 1) * LANES)
        d = back_norm(
            rows(c3_ref, 0, s, 1), rows(q4_ref, 0, s, 1), rows(q4_ref, 1, s, 1),
            df_ref[:, :, cols], fc[:, cols].reshape(p_n, f_n, LANES), fill4,
        )
        parts.append(flat(d).astype(BF16))
    dfc = jnp.concatenate(parts, axis=1)
    add_to(i, gout, dot_tn(fact, dfc))
    z = fb_ref[...]
    back = dot_nt(dfc, wout_ref[...]).reshape(p_n, f_n, LANES) * slope(
        z * rows(c2_ref, 0, 0, 1) + rows(c2_ref, 1, 0, 1)
    )
    dfb_ref[...] = back
    sum_add(i, back, t1)
    sum_add(i, back * (z * rows(c2_ref, 2, 0, 1) - rows(c2_ref, 3, 0, 1)), t2)
    for k, value in enumerate((back, z)):
        value = flat(value)
        for p in range(p_n):
            down_ref[0, k, p : p + 1, :] = value[p * f_n : p * f_n + 1, :]
            up_ref[0, k, p : p + 1, :] = value[p * f_n + f_n - 1 : p * f_n + f_n, :]
        down_ref[0, k, p_n : p_n + 1, :] = m64_ref[0, 0:1, :]
        up_ref[0, k, p_n : p_n + 1, :] = m64_ref[0, f_n - 1 : f_n, :]

    @pl.when(i == STEPS - 1)
    def _():
        zero_ref(st_ref)
        put_rows(st_ref, 0, sum_end(s1))
        put_rows(st_ref, 8, sum_end(s2))
        put_rows(st_ref, 16, sum_end(s3))
        put_rows(st_ref, 24, sum_end(t1))
        put_rows(st_ref, 25, sum_end(t2))
        gout_ref[...] = fold_wide(gout, s_n)


def add_to(step, ref, value):
    ref[...] = jnp.where(step == 0, 0.0, ref[...]) + value


def fold_wide(ref, count):
    a = ref.shape[0] // count
    return sum(ref[s * a : (s + 1) * a, s * LANES : (s + 1) * LANES] for s in range(count))


def fold_lanes(value, count):
    a = value.shape[0] // count
    parts = [value[s * a : (s + 1) * a, :] for s in range(count)]
    return sum(p if s == 0 else pltpu.roll(p, LANES - s * a, 1) for s, p in enumerate(parts))


def k_back_out(x_ref, lact_ref, dy_ref, sp_ref, sact_ref, sb_ref, dfb_ref, fb_ref, fa_ref, ftap_ref, hp_ref, hn_ref,
               c1_ref, c2_ref, c3_ref, c4_ref, q5_ref, m16_ref, m64_ref, wso_ref, wback_ref,
               gw_ref, gs_ref, dsp_ref, dsb_ref, dfa_ref, gmid_ref, st_ref, s1, s2, t1, t2, gsc, gso, gmid):
    i = pl.program_id(0)
    s_n, p_n, t_n, c = sb_ref.shape
    sact = flat(sact_ref[...])
    fill = m16_ref[0:1, :, 0:1]
    wide = 256
    back = None
    turned = jnp.concatenate([flat(x_ref[...]), flat(lact_ref[...])], axis=1).T
    sact_turned = sact.T
    for n in range(wso_ref.shape[1] // wide):
        cols = slice(n * wide, (n + 1) * wide)
        shape = (s_n * p_n, t_n, wide)
        d = dy_ref[:, :, :, cols].reshape(shape)
        sc = dot(sact, wso_ref[:, cols]).reshape(shape)
        dsc = back_norm(rows(c4_ref, 0, 2 * n, 2), rows(q5_ref, 0, 2 * n, 2), rows(q5_ref, 1, 2 * n, 2), d, sc, fill)
        dsc = flat(dsc.astype(BF16))
        old = jnp.where(i == 0, 0.0, gso[:, cols])
        gso[:, cols] = old + dot(sact_turned, dsc)
        sp = sp_ref[:, :, :, cols].reshape(shape)
        dsp = back_norm(
            rows(c2_ref, 0, 3 + 2 * n, 2), rows(q5_ref, 0, 8 + 2 * n, 2), rows(q5_ref, 1, 8 + 2 * n, 2), d, sp, fill
        )
        dsp = flat(dsp.astype(BF16))
        dsp_ref[:, :, :, cols] = dsp.reshape(s_n, p_n, t_n, wide)
        old = jnp.where(i == 0, 0.0, gsc[:, cols])
        gsc[:, cols] = old + dot(turned, dsp)
        part = dot_nt(dsc, wso_ref[:, cols])
        back = part if back is None else back + part
    z = sb_ref[...].reshape(s_n * p_n, t_n, c)
    back = back.reshape(z.shape) * slope(z * rows(c3_ref, 0, 4, 2) + rows(c3_ref, 1, 4, 2))
    dsb_ref[...] = back.reshape(dsb_ref.shape)
    sum_add(i, back, s1)
    sum_add(i, back * (z * rows(c3_ref, 2, 4, 2) - rows(c3_ref, 3, 4, 2)), s2)

    f_n = fb_ref.shape[1]
    scale, p_row, q_row = rows(c2_ref, 0, 0, 1), rows(q5_ref, 0, 16, 1), rows(q5_ref, 1, 16, 1)
    dfb = back_norm(scale, p_row, q_row, dfb_ref[...], fb_ref[...], m64_ref[0:1])
    dfb_low = flat(dfb).astype(BF16)
    add_to(i, gmid, dot_tn(dfb_low, flat(ftap_ref[...])))
    own = dfb_low.astype(F32)
    ends = []
    for ref in (hp_ref, hn_ref):
        small = back_norm(scale, p_row, q_row, ref[0, 0], ref[0, 1], ref[0, 0, p_n : p_n + 1, :])
        small = small.astype(BF16).astype(F32)
        ends.append(
            jnp.concatenate(
                [jnp.broadcast_to(small[p : p + 1, :], (f_n, LANES)) for p in range(p_n)], axis=0
            ).reshape(p_n, f_n, LANES)
        )
    before, after = shifted(own, ends[0], ends[1], f_n)
    taps = jnp.concatenate(
        [flat(after * m64_ref[2:3]), own, flat(before * m64_ref[1:2])], axis=1
    ).astype(BF16)
    z = fa_ref[...]
    back = dot(taps, wback_ref[...]).reshape(z.shape) * slope(
        z * rows(c1_ref, 0, 0, 1) + rows(c1_ref, 1, 0, 1)
    )
    dfa_ref[...] = back
    sum_add(i, back, t1)
    sum_add(i, back * (z * rows(c1_ref, 2, 0, 1) - rows(c1_ref, 3, 0, 1)), t2)

    @pl.when(i == STEPS - 1)
    def _():
        zero_ref(st_ref)
        put_rows(st_ref, 0, sum_end(s1))
        put_rows(st_ref, 2, sum_end(s2))
        put_rows(st_ref, 4, sum_end(t1))
        put_rows(st_ref, 5, sum_end(t2))

    def late():
        for k in range(3):
            gmid_ref[k * 32 : (k + 1) * 32, :] = fold_lanes(gmid[:, k * LANES : (k + 1) * LANES], s_n)
        tall, low_tall = gsc.shape[0], gso.shape[0]
        blocks = gsc.shape[1] // wide
        for n in range(blocks):
            cols = slice(n * wide, (n + 1) * wide)
            gw_ref[n * tall : (n + 1) * tall, :] = gsc[:, cols].astype(BF16)
            gs_ref[n * low_tall : (n + 1) * low_tall, :] = gso[:, cols].astype(BF16)
        if blocks * tall < gw_ref.shape[0]:
            gw_ref[blocks * tall :, :] = jnp.zeros((gw_ref.shape[0] - blocks * tall, wide), BF16)

    return late


def k_slow_grad(x_ref, lact_ref, low_ref, dsp_ref, win_ref, wsc_ref, gx_ref, gw_ref, gsi):
    i = pl.program_id(0)
    s_n, p_n, t_n, c = low_ref.shape
    low, dsp = flat(low_ref[...]), flat(dsp_ref[...])
    turned = low.T
    blocks = gx_ref.shape[-1] // c
    for n in range(blocks + 1):
        part = slice(n * c, (n + 1) * c)
        joined = flat(x_ref[:, :, :, part] if n < blocks else lact_ref[...])
        gsi[:, part] = jnp.where(i == 0, 0.0, gsi[:, part]) + dot(turned, joined)
        if n < blocks:
            d = dot_nt(dsp, wsc_ref[part, :]) + dot_nt(low, win_ref[part, :])
            gx_ref[:, :, :, part] = d.astype(BF16).reshape(s_n, p_n, t_n, c)

    @pl.when(i == STEPS - 1)
    def _():
        for n in range(blocks + 1):
            part = slice(n * c, (n + 1) * c)
            gw_ref[part, :] = gsi[:, part].T.astype(BF16)


def k_fast_grad(dlat_ref, lat_ref, taps_ref, hn_ref, df_ref, dlow_ref, c1_ref, q8_ref, m16_ref, wlat_ref, wfa_ref,
                gx_ref, gw_ref, gs, glat):
    i = pl.program_id(0)
    s_n, p_n, t_n, c = lat_ref.shape
    shape = (s_n * p_n, t_n, c)
    scale, p_row, q_row = rows(c1_ref, 0, 1, 2), rows(q8_ref, 0, 0, 2), rows(q8_ref, 1, 0, 2)
    low = flat(
        back_norm(scale, p_row, q_row, dlat_ref[...].reshape(shape), lat_ref[...].reshape(shape), m16_ref[0:1, :, 0:1])
    ).astype(BF16)
    add_to(i, glat, dot_tn(low, flat(taps_ref[...])))

    @pl.when(i == STEPS - 1)
    def _():
        for k in range(glat.shape[1] // LANES):
            part = slice(k * LANES, (k + 1) * LANES)
            gw_ref[part, :] = glat[:, part].T.astype(BF16)

    small = hn_ref[0].astype(F32)
    ends = [
        jnp.broadcast_to(small[s * 8 + p : s * 8 + p + 1, :], (t_n, c)) for s in range(s_n) for p in range(p_n)
    ]
    ends = jnp.concatenate(ends, axis=0).reshape(shape)
    n = low.shape[0]
    moved = pltpu.roll(low.astype(F32), n - 1, 0).reshape(shape)
    place = lax.broadcasted_iota(jnp.int32, shape, 1)
    following = flat(jnp.where(place == t_n - 1, ends, moved) * m16_ref[2:3, :, 0:1]).astype(BF16)
    own = dot_nt(low, wlat_ref[2 * LANES : 5 * LANES, :])
    late = dot_nt(following, wlat_ref[0 : 2 * LANES, :])
    gs[pl.ds(0, n, stride=4), :] = own[:, 0:LANES]
    gs[pl.ds(1, n, stride=4), :] = own[:, LANES : 2 * LANES]
    gs[pl.ds(2, n, stride=4), :] = own[:, 2 * LANES :] + late[:, 0:LANES]
    gs[pl.ds(3, n, stride=4), :] = late[:, LANES:]
    back = dot(flat(dlow_ref[...]), wfa_ref[...])
    for s in range(s_n):
        cols = slice(s * LANES, (s + 1) * LANES)
        total = flat(df_ref[:, :, cols]) + back[:, cols] + gs[s * n : (s + 1) * n, :]
        gx_ref[s] = total.astype(BF16).reshape(gx_ref.shape[1:])


def each(first, last, body):
    def step(k, carry):
        body(k)
        return carry
    lax.fori_loop(first, last, step, 0)


NEAR = 4


class Cube:
    def __init__(self, ch, far):
        self.ch, self.far = ch, far
        self.p, self.f = lax.axis_index("path"), lax.axis_index("frames")
        self.q, self.r = lax.rem(self.f, NEAR), lax.div(self.f, NEAR)
        self.sibling = (1 - self.p, self.f)

    def q_of(self, k):
        return lax.rem(self.q + k, NEAR)

    def r_of(self, k):
        return lax.rem(self.r + k, self.far)

    def plane(self, k):
        return (self.p, self.r * NEAR + self.q_of(k))

    def line(self, k):
        return (self.p, self.r_of(k) * NEAR + self.q)

    def at(self, path, q, r):
        return pl.ds(pl.multiple_of(((path * NEAR + q) * self.far + r) * self.ch, 16), self.ch)


def remote(src, dst, sem, index, device):
    return pltpu.make_async_remote_copy(
        src_ref=src, dst_ref=dst, send_sem=sem.at[(0, *index)], recv_sem=sem.at[(1, *index)],
        device_id=device, device_id_type=MESH)


def rows_for(sizes, n):
    unit = 16 * sizes[0] * sizes[1]
    return -(-n // unit) * unit


class Stream:
    def __init__(self, sizes, rows_n, width):
        self.sizes, self.rows_n, self.width = sizes, rows_n, width
        self.far = sizes[1] // NEAR
        self.ch = rows_n // (sizes[0] * sizes[1])
        self.chunk = (self.ch, width)
        self.near_shape = (self.far, *self.chunk)
        quad = pltpu.VMEM((NEAR, *self.near_shape), BF16)
        quad_sems, line_sems = pltpu.SemaphoreType.DMA((2, NEAR, self.far)), pltpu.SemaphoreType.DMA((2, self.far))
        self.near_scratch = [quad, quad, quad, pltpu.VMEM(self.chunk, F32), quad_sems, quad_sems]
        self.line_scratch = [pltpu.VMEM(self.near_shape, BF16), pltpu.VMEM(self.chunk, F32), line_sems]
        self.share_scratch = [line_sems, quad_sems, quad_sems, pltpu.SemaphoreType.DMA]


class Near:
    def __init__(self, stream, x, out, scratch):
        self.x, self.out, self.far, self.c = x, out, stream.far, Cube(stream.ch, stream.far)
        self.land_a, self.buf_b, self.land_b, self.acc, self.sem_a, self.sem_b = scratch

    def pair(self, k, m):
        c = self.c
        return remote(self.x.at[c.at(1 - c.p, c.q_of(k), c.r_of(m + 1))], self.land_a.at[k, m], self.sem_a, (k, m), c.sibling)

    def plane(self, k, m):
        return remote(self.buf_b.at[k, m], self.land_b.at[k, m], self.sem_b, (k, m), self.c.plane(k))

    def start(self):
        def one(m):
            each(1, NEAR, lambda k: self.pair(k, m).start())
            self.pair(0, m).start()

        each(0, self.far, one)

    def add_pair(self, first, last):
        c = self.c

        def one(k, m):
            self.pair(k, m).wait_recv()
            mine = self.x[c.at(c.p, c.q_of(k), c.r_of(m + 1)), :]
            self.buf_b[k, m] = (mine.astype(F32) + self.land_a[k, m].astype(F32)).astype(BF16)
            self.plane(k, m).start()

        each(first, last, lambda m: each(1, NEAR, lambda k: one(k, m)))

    def add_plane(self, first, last, then=None):
        c = self.c

        def one(m):
            self.pair(0, m).wait_recv()
            self.acc[...] = self.x[c.at(c.p, c.q, c.r_of(m + 1)), :].astype(F32) + self.land_a[0, m].astype(F32)

            def more(k):
                self.plane(k, m).wait_recv()
                self.acc[...] += self.land_b[k, m].astype(F32)

            each(1, NEAR, more)
            self.out[m] = self.acc[...].astype(BF16)
            if then is not None:
                then(m)

        each(first, last, one)

    def end(self):
        each(0, self.far, lambda m: each(0, NEAR, lambda k: self.pair(k, m).wait_send()))
        each(0, self.far, lambda m: each(1, NEAR, lambda k: self.plane(k, m).wait_send()))


class Line:
    def __init__(self, stream, near, scratch):
        self.near, self.far, self.c = near, stream.far, Cube(stream.ch, stream.far)
        self.land, self.acc, self.sem = scratch

    def line(self, m):
        return remote(self.near.at[m], self.land.at[m], self.sem, (m,), self.c.line(m + 1))

    def start(self, first, last):
        each(first, min(last, self.far - 1), lambda m: self.line(m).start())

    def total(self):
        self.acc[...] = self.near[self.far - 1].astype(F32)

        def one(m):
            self.line(m).wait_recv()
            self.acc[...] += self.land[m].astype(F32)

        each(0, self.far - 1, one)
        return self.acc[...].astype(BF16)

    def end(self):
        each(0, self.far - 1, lambda m: self.line(m).wait_send())


class Share:
    def __init__(self, stream, res, out, scratch):
        self.res, self.out, self.far, self.c = res, out, stream.far, Cube(stream.ch, stream.far)
        self.sem_d, self.sem_e, self.sem_f, self.sem_own = scratch

    def own(self):
        return self.out.at[self.c.at(self.c.p, self.c.q, self.c.r)]

    def keep(self):
        return pltpu.make_async_copy(self.res, self.own(), self.sem_own)

    def line_back(self, k):
        return remote(self.res, self.own(), self.sem_d, (k,), self.c.line(k))

    def part(self, q, m):
        return self.out.at[self.c.at(self.c.p, q, self.c.r_of(self.far - m))]

    def plane_back(self, k, m, src=None):
        dst = self.part(self.c.q, m)
        return remote(dst if src is None else src, dst, self.sem_e, (k, m), self.c.plane(k))

    def pair_back(self, k, m, src=None):
        dst = self.part(self.c.q_of(NEAR - k), m)
        return remote(dst if src is None else src, dst, self.sem_f, (k, m), self.c.sibling)

    def start_line(self):
        each(1, self.far, lambda k: self.line_back(k).start())

    def start_plane(self):
        each(1, NEAR, lambda k: self.plane_back(k, 0, self.res).start())
        self.pair_back(0, 0, self.res).start()
        self.keep().start()

    def relay(self, first, last):
        def one(m):
            self.line_back(m).wait_recv()
            each(1, NEAR, lambda k: self.plane_back(k, m).start())
            self.pair_back(0, m).start()

        each(first, last, one)

    def hand_on(self, first, last):
        def one(k, m):
            self.plane_back(k, m).wait_recv()
            self.pair_back(k, m).start()

        each(first, last, lambda m: each(1, NEAR, lambda k: one(k, m)))

    def end(self):
        each(0, self.far, lambda m: each(0, NEAR, lambda k: self.pair_back(k, m).wait()))
        self.keep().wait()
        each(1, self.far, lambda k: self.line_back(k).wait_send())
        each(0, self.far, lambda m: each(1, NEAR, lambda k: self.plane_back(k, m).wait_send()))


def k_tail(cfg, *refs):
    st_a, st_b, ex7, ex8, side = cfg
    it = iter(refs)

    def take(n):
        return [next(it) for _ in range(n)]

    hbm = take(13)
    gb, c1, c2, c3, q6, m16, m64, g_fout, g_fmid = take(9)
    low_out, dlow_out, dlat_out, gf, q7, q8, hn, res_a, near_b = take(9)
    local = take(13)
    gw_a, dsb, sb, spad, wsp, sa, x_fast, dfa, fa, w_in, w_sc, dsp, lat = local
    pad, gsp, gin, low, dlow, gw_b, near_a, ends, s1, s2, t1, t2, sems, out_sems = take(14)
    near1, line1, near2 = take(len(st_a.near_scratch)), take(len(st_a.line_scratch)), take(len(st_b.near_scratch))
    scr7 = take(len(ex7.local) + len(ex7.work))
    scr8 = take(len(ex8.local) + len(ex8.work))
    n_in = w_in.shape[0]
    srcs = list(hbm)
    for k in (9, 10):
        srcs[k] = hbm[k].at[pl.ds(hbm[k].shape[0] - n_in, n_in)]
    loads = [pltpu.make_async_copy(src, dst, sems.at[k]) for k, (src, dst) in enumerate(zip(srcs, local))]
    count = exchange_hello(ex8)
    for load in loads:
        load.start()
    near = Near(st_a, gw_a, near_a, near1)
    line = Line(st_a, near_a, line1)
    near_two = Near(st_b, gw_b, near_b, near2)
    far = st_a.far
    t_n, c = pad.shape[2], pad.shape[3]
    wide = side * t_n
    per = side // STEPS
    fill = m16[0:1, :, 0:1]

    def waits(*names):
        for k in names:
            loads[k].wait()

    waits(1, 2)
    scale, p_row, q_row = rows(c3, 0, 4, 2), rows(q6, 0, 0, 2), rows(q6, 1, 0, 2)
    zero_ref(pad)

    def fill_pad(h):
        part = pl.ds(h * wide, wide)
        d = back_norm(
            scale, p_row, q_row, dsb[part].reshape(side, t_n, c), sb[part].reshape(side, t_n, c), fill
        )
        pad[h + 1, 1 : side + 1] = d.astype(BF16)

    each(0, side, fill_pad)
    waits(0)
    pl.semaphore_wait(pltpu.get_barrier_semaphore(), count)
    near.start()
    waits(3, 4, 5, 6, 7, 8)
    f_n = x_fast.shape[2]
    p_n = x_fast.shape[1] // STEPS

    def spatial(i):
        h0 = i * per
        turned = flat(pad[pl.ds(h0 + 1, per), 1 : side + 1]).T
        acc = None
        for a in range(3):
            for b in range(3):
                k = 3 * a + b
                patch = flat(spad[pl.ds(h0 + a, per), b : b + side])
                cols = slice(k * c, (k + 1) * c)
                gsp[:, cols] = jnp.where(i == 0, 0.0, gsp[:, cols]) + dot(turned, patch)
                block = pad[pl.ds(h0 + 2 - a, per), 2 - b : 2 - b + side]
                part = dot_nt(flat(block), wsp[k])
                acc = part if acc is None else acc + part
        span = pl.ds(i * per * wide, per * wide)
        z = sa[span]
        back = acc * slope(z * rows(c2, 0, 1, 2) + rows(c2, 1, 1, 2))
        dsb[span] = back
        unit = z * rows(c2, 2, 1, 2) - rows(c2, 3, 1, 2)
        sum_add(i, back.reshape(per * side, t_n, c), s1)
        sum_add(i, (back * unit).reshape(per * side, t_n, c), s2)
        f_span = pl.ds(i * p_n, p_n)
        small = back_norm(
            rows(c1, 0, 0, 1), rows(q6, 0, 2, 1), rows(q6, 1, 2, 1), dfa[f_span], fa[f_span], m64[0:1]
        ).astype(BF16)
        dlow[f_span] = small
        packed = jnp.concatenate([flat(x_fast[s, f_span]) for s in range(x_fast.shape[0])], axis=1)
        add_to(i, gin, dot_tn(flat(small), packed))
        pl.when(i == 0)(lambda: near.add_pair(0, far // 2))
        pl.when(i == 1)(lambda: near.add_pair(far // 2, far))

    each(0, STEPS, spatial)
    stats = scr7[0]
    zero_ref(stats)
    put_rows(stats, 0, sum_end(s1))
    put_rows(stats, 2, sum_end(s2))
    stores = [pltpu.make_async_copy(dlow, dlow_out, out_sems.at[0])]
    stores[0].start()

    def late():
        for k in range(9):
            gw_b[k * c : (k + 1) * c, :] = gsp[:, k * c : (k + 1) * c].T.astype(BF16)
        if 9 * c < gw_b.shape[0]:
            gw_b[9 * c :, :] = jnp.zeros((gw_b.shape[0] - 9 * c, c), BF16)
        n = g_fout.shape[0]
        gf[0:n, 0:LANES] = fold_wide(gin, x_fast.shape[0])
        gf[0:n, LANES:] = g_fout[...]
        gf[n : 2 * n, 0:LANES] = g_fmid[0:n, :]
        gf[n : 2 * n, LANES:] = g_fmid[n : 2 * n, :]
        gf[2 * n :, 0:LANES] = g_fmid[2 * n :, :]
        gf[2 * n :, LANES:] = jnp.zeros((n, LANES), F32)

    exchange_run(ex7, [gb, c2], [q7], scr7, late)
    near_two.start()
    near.add_plane(0, far - 1, lambda m: line.line(m).start())
    near.add_plane(far - 1, far)
    waits(9, 10, 11, 12)
    scale7, p7, q7_row = rows(c2, 0, 1, 2), rows(q7, 0, 0, 2), rows(q7, 1, 0, 2)
    block = per * wide

    def join(i):
        span = pl.ds(i * block, block)
        shape = (per * side, t_n, c)
        d = back_norm(scale7, p7, q7_row, dsb[span].reshape(shape), sa[span].reshape(shape), fill)
        small = flat(d).astype(BF16)
        low[span] = small
        d = dot_nt(dsp[span], w_sc[...]) + dot_nt(small, w_in[...])
        z = lat[span]
        back = d * slope(z * rows(c1, 0, 1, 2) + rows(c1, 1, 1, 2))
        sb[span] = back
        unit = z * rows(c1, 2, 1, 2) - rows(c1, 3, 1, 2)
        sum_add(i, back.reshape(shape), t1)
        sum_add(i, (back * unit).reshape(shape), t2)
        pl.when(i == 2)(lambda: near_two.add_pair(0, far))

    each(0, STEPS, join)
    stores.append(pltpu.make_async_copy(low, low_out, out_sems.at[1]))
    stores.append(pltpu.make_async_copy(sb, dlat_out, out_sems.at[2]))
    stores[1].start()
    stores[2].start()
    stats = scr8[0]
    zero_ref(stats)
    put_rows(stats, 0, sum_end(t1))
    put_rows(stats, 2, sum_end(t2))

    def post(q, sent):
        zero_ref(ends)
        for s in range(x_fast.shape[0]):
            for step in range(STEPS):
                for p in range(p_n):
                    at = ((s * STEPS + step) * p_n + p) * t_n
                    ends[0, step, s * 8 + p : s * 8 + p + 1, :] = sb[at : at + 1, :]
                    ends[1, step, s * 8 + p : s * 8 + p + 1, :] = lat[at : at + 1, :]
        d = back_norm(rows(c1, 0, 1, 2), rows(q, 0, 0, 2), rows(q, 1, 0, 2), ends[0], ends[1], m16[0, 0:1, 0:1])
        sent[...] = d.astype(BF16)

    exchange_run(ex8, [gb, c1], [q8, hn], scr8, None, post)
    res_a[...] = line.total()
    near_two.add_plane(0, far)
    for store in stores:
        store.wait()
    line.end()
    near.end()
    near_two.end()


def back_tail(st_a, st_b, ex7, ex8, hbm, small, side, t_n, c):
    vm, anywhere = pl.BlockSpec(memory_space=pltpu.VMEM), pl.BlockSpec(memory_space=pl.ANY)
    inner, f_n = hbm[7].shape[:2]
    n = side * side * t_n
    outs = [((n, c), BF16), ((inner, f_n, LANES), BF16), ((n, c), F32), (small[-1].shape[0:1] + (2 * LANES,), F32),
            *ex7.outs, *ex8.outs, (st_a.chunk, BF16), (st_b.near_shape, BF16)]
    local = [pltpu.VMEM((c,) + a.shape[1:] if k in (9, 10) else a.shape, a.dtype) for k, a in enumerate(hbm)]
    width = hbm[6].shape[0] * hbm[6].shape[3]
    scratch = [
        pltpu.VMEM((side + 2, side + 2, t_n, c), BF16), pltpu.VMEM((c, 9 * c), F32), pltpu.VMEM((LANES, width), F32),
        pltpu.VMEM((n, c), BF16), pltpu.VMEM((inner, f_n, LANES), BF16), pltpu.VMEM((st_b.rows_n, c), BF16),
        pltpu.VMEM(st_a.near_shape, BF16), pltpu.VMEM((2, *ex8.post), F32), *[pltpu.VMEM((t_n, c), F32)] * 4,
        pltpu.SemaphoreType.DMA((len(hbm),)), pltpu.SemaphoreType.DMA((3,)),
        *st_a.near_scratch, *st_a.line_scratch, *st_b.near_scratch, *ex7.local, *ex7.work, *ex8.local, *ex8.work,
    ]
    return pl.pallas_call(
        functools.partial(k_tail, (st_a, st_b, ex7, ex8, side)),
        out_shape=[jax.ShapeDtypeStruct(s, d) for s, d in outs],
        in_specs=[anywhere] * len(hbm) + [vm] * len(small),
        out_specs=[anywhere] * 3 + [vm] * (len(outs) - 3),
        scratch_shapes=[*local, *scratch],
        compiler_params=pltpu.CompilerParams(collective_id=ex8.cid, has_side_effects=True, vmem_limit_bytes=VMEM_LIMIT),
        name="tail",
    )(*hbm, *small)


def final_kernel(cfg, *refs):
    first, second, third, both, offsets, heights = cfg
    n = len(offsets)
    (res_a, near_b), ins, (out_a, out_bc), refs = refs[:2], refs[2 : 2 + n], refs[2 + n : 4 + n], refs[4 + n :]
    x, near_c, res = refs[:3]
    at = [3]

    def take(scratch):
        at[0] += len(scratch)
        return refs[at[0] - len(scratch) : at[0]]

    far = first.far
    share_a = Share(first, res_a, out_a, take(first.share_scratch))
    line_b = Line(second, near_b, take(second.line_scratch))
    near = Near(third, x, near_c, take(third.near_scratch))
    line_c = Line(third, near_c, take(third.line_scratch))
    share = Share(both, res, out_bc, take(both.share_scratch))

    c = near.c
    barrier = pltpu.get_barrier_semaphore()

    def greet(device):
        pl.semaphore_signal(barrier, inc=1, device_id=device, device_id_type=MESH)

    greet(c.sibling)
    each(1, NEAR, lambda k: greet(c.plane(k)))
    each(1, far, lambda k: greet(c.line(k)))
    end = 0
    for ref, off, height in zip(ins, offsets, heights):
        x[off : off + height, :] = ref[...].astype(BF16)
        end = off + height
    if end < x.shape[0]:
        x[end:, :] = jnp.zeros((x.shape[0] - end, x.shape[1]), BF16)
    pl.semaphore_wait(barrier, NEAR + far - 1)

    near.start()
    line_b.start(0, far)
    share_a.start_line()
    near.add_pair(0, far)
    share_a.start_plane()
    res[0 : second.ch, :] = line_b.total()
    near.add_plane(0, far - 1, lambda m: line_c.line(m).start())
    near.add_plane(far - 1, far)
    share_a.relay(1, far)
    res[second.ch :, :] = line_c.total()
    share.start_line()
    share.start_plane()
    share_a.hand_on(0, far)
    share.relay(1, far)
    share.hand_on(0, far)
    share_a.end()
    share.end()
    line_b.end()
    line_c.end()
    near.end()


def final_sum(sizes, cid, first, second, res_a, near_b, parts):
    width = res_a.shape[1]
    heights = tuple(p.shape[0] for p in parts)
    offsets = tuple(sum(heights[:k]) for k in range(len(parts)))
    third = Stream(sizes, rows_for(sizes, sum(heights)), width)
    both = Stream(sizes, second.rows_n + third.rows_n, width)
    vm, hbm = pl.BlockSpec(memory_space=pltpu.VMEM), pl.BlockSpec(memory_space=pl.ANY)
    out_a, out_bc = pl.pallas_call(
        functools.partial(final_kernel, (first, second, third, both, offsets, heights)),
        out_shape=[jax.ShapeDtypeStruct((s.rows_n, width), BF16) for s in (first, both)],
        in_specs=[vm] * (2 + len(parts)),
        out_specs=[hbm] * 2,
        scratch_shapes=[
            pltpu.VMEM((third.rows_n, width), BF16), pltpu.VMEM(third.near_shape, BF16), pltpu.VMEM(both.chunk, BF16),
            *first.share_scratch, *second.line_scratch, *third.near_scratch, *third.line_scratch, *both.share_scratch,
        ],
        compiler_params=pltpu.CompilerParams(collective_id=cid, has_side_effects=True, vmem_limit_bytes=VMEM_LIMIT),
        name="final_sum",
    )(res_a, near_b, *parts)
    return out_a, out_bc.reshape(-1, both.ch, width), third


def k_unpack(pieces, cut, *refs):
    (src_a, src_b), outs, (low_a, low_b, low_c, wide, sem_a, sem_b, sem_out) = refs[:2], refs[2:-7], refs[-7:]
    lows = (low_a, low_b, low_c)
    flats = [low_a, low_b.reshape(-1, low_b.shape[-1]), low_c.reshape(-1, low_c.shape[-1])]
    starts = [sum(p[2] for p in pieces[:k]) for k in range(len(pieces))]

    def fetch_a(k):
        _, row, height, _, _ = pieces[k]
        return pltpu.make_async_copy(src_a.at[pl.ds(row, height)], low_a.at[pl.ds(row, height)], sem_a.at[k])

    def fetch_b(k):
        part = src_b.at[:, pl.ds(0, cut)] if k == 1 else src_b.at[:, pl.ds(cut, src_b.shape[1] - cut)]
        return pltpu.make_async_copy(part, lows[k], sem_b.at[k])

    def store(k):
        _, _, height, out, col = pieces[k]
        part = outs[out] if col is None else outs[out].at[:, pl.ds(col, wide.shape[1])]
        return pltpu.make_async_copy(wide.at[pl.ds(starts[k], height)], part, sem_out.at[k])

    for k, piece in enumerate(pieces):
        if piece[0] == 0:
            fetch_a(k).start()
    for k in (1, 2):
        fetch_b(k).start()
    seen = 0
    for k, (src, row, height, _, _) in enumerate(pieces):
        if src == 0:
            fetch_a(k).wait()
        elif src != seen:
            fetch_b(src).wait()
            seen = src
        wide[starts[k] : starts[k] + height, :] = flats[src][row : row + height, :].astype(F32)
        store(k).start()
    for k in range(len(pieces)):
        store(k).wait()


def unpack(src_a, src_b, cut, pieces, shapes):
    hbm = pl.BlockSpec(memory_space=pl.ANY)
    n, _, width = src_b.shape
    return pl.pallas_call(
        functools.partial(k_unpack, pieces, cut),
        out_shape=[jax.ShapeDtypeStruct(s, F32) for s in shapes],
        in_specs=[hbm] * 2,
        out_specs=[hbm] * len(shapes),
        scratch_shapes=[
            pltpu.VMEM(src_a.shape, BF16),
            pltpu.VMEM((n, cut, width), BF16),
            pltpu.VMEM((n, src_b.shape[1] - cut, width), BF16),
            pltpu.VMEM((sum(p[2] for p in pieces), width), F32),
            pltpu.SemaphoreType.DMA((len(pieces),)),
            pltpu.SemaphoreType.DMA((3,)),
            pltpu.SemaphoreType.DMA((len(pieces),)),
        ],
        compiler_params=pltpu.CompilerParams(vmem_limit_bytes=VMEM_LIMIT),
        name="unpack",
    )(src_a, src_b)


def k_prep(x_hbm, fill_ref, clip_ref, norm_ref, wfi_ref, wfm_ref, wfo_ref,
           tail_ref, gb_ref, m16_ref, m64_ref, wfa_ref, wmid_ref, wback_ref, wout_ref,
           near, rows_f, sent, land, sems, local):
    length = lax.axis_size("frames")
    total = lax.axis_size("path") * length
    me = lax.axis_index("path") * length + lax.axis_index("frames")

    def place(index):
        return (lax.div(index, length), lax.rem(index, length))

    nxt, prv = place(lax.rem(me + 1, total)), place(lax.rem(me + total - 1, total))
    barrier = pltpu.get_barrier_semaphore()
    pl.semaphore_signal(barrier, inc=1, device_id=nxt, device_id_type=MESH)
    pl.semaphore_signal(barrier, inc=1, device_id=prv, device_id_type=MESH)
    s_n, inner, t_n, c = near.shape
    f_n = x_hbm.shape[2]
    fetch = pltpu.make_async_copy(x_hbm.at[:, :, pl.ds(f_n - t_n, t_n), :], near, local)
    fetch.start()
    fetch.wait()
    p_n = inner // STEPS
    rows_f[...] = near[...].reshape(rows_f.shape).astype(F32)
    zero_ref(sent)
    count = s_n * inner
    for k in range(2):
        line = rows_f[pl.ds(t_n - 2 + k, count, stride=t_n), :]
        for s in range(s_n):
            for step in range(STEPS):
                at = s * inner + step * p_n
                sent[step, s, 0:p_n, k * c : (k + 1) * c] = line[at : at + p_n, :]
    pl.semaphore_wait(barrier, 2)
    copy = pltpu.make_async_remote_copy(
        src_ref=sent, dst_ref=land, send_sem=sems.at[0], recv_sem=sems.at[1], device_id=nxt, device_id_type=MESH
    )
    copy.start()

    lane = lax.broadcasted_iota(jnp.int32, (1, LANES), 1)
    for k in range(2):
        half = pltpu.roll(norm_ref[k], LANES // 2, 1)
        main = jnp.where(lane < LANES // 2, half[0:23], half[1:24])
        for j in range(2):
            v = jnp.where(lane // 32 == j, norm_ref[k, 0:1, :], 0.0)
            v = v + pltpu.roll(v, 64, 1)
            gb_ref[k, j : j + 1, :] = v + pltpu.roll(v, 32, 1)
        for j in range(4):
            gb_ref[k, 2 + j : 3 + j, :] = main[0:1]
        gb_ref[k, 6:28, :] = main[1:23]
        gb_ref[k, 28:32, :] = jnp.zeros((4, LANES), F32)

    def row(value):
        return jnp.full((1, LANES), value, F32)

    last = jnp.where(me < total - 1, 1.0, 0.0)
    link = [jnp.where(clip_ref[t] >= 1, 1.0, 0.0) for t in range(t_n)]
    for t in range(t_n):
        filled = row(fill_ref[t].astype(F32))
        after = row(link[t + 1] if t + 1 < t_n else last)
        m16_ref[0, t : t + 1, :] = filled
        m16_ref[1, t : t + 1, :] = row(link[t])
        m16_ref[2, t : t + 1, :] = after
        m64_ref[0, 4 * t : 4 * t + 4, :] = jnp.broadcast_to(filled, (4, LANES))
        m64_ref[1, 4 * t : 4 * t + 1, :] = row(link[t])
        m64_ref[1, 4 * t + 1 : 4 * t + 4, :] = jnp.ones((3, LANES), F32)
        m64_ref[2, 4 * t : 4 * t + 3, :] = jnp.ones((3, LANES), F32)
        m64_ref[2, 4 * t + 3 : 4 * t + 4, :] = after

    zero_ref(wfa_ref)
    zero_ref(wout_ref)
    a = wfi_ref.shape[0]
    for s in range(s_n):
        wfa_ref[s * a : (s + 1) * a, s * LANES : (s + 1) * LANES] = wfi_ref[...]
        wout_ref[s * a : (s + 1) * a, s * LANES : (s + 1) * LANES] = wfo_ref[...]
    tall = (LANES, a)
    spread = (lax.broadcasted_iota(jnp.int32, tall, 0) % a == lax.broadcasted_iota(jnp.int32, tall, 1)).astype(BF16)
    square = (LANES, LANES)
    diag = lax.broadcasted_iota(jnp.int32, square, 0) // a == lax.broadcasted_iota(jnp.int32, square, 1) // a
    for k in range(3):
        left = dot(spread, wfm_ref[k]).astype(BF16)
        wmid_ref[k * LANES : (k + 1) * LANES, :] = jnp.where(diag, dot_nt(left, spread), 0.0).astype(BF16)
        right = dot_nt(spread, wfm_ref[k]).astype(BF16)
        wback_ref[k * LANES : (k + 1) * LANES, :] = jnp.where(diag, dot_nt(right, spread), 0.0).astype(BF16)
    copy.wait()
    tail_ref[...] = land[...]


def prepare(x_fast, fill, clip_offset, norms, w_fast_in, w_fast_mid, w_fast_out):
    s_n, inner, f_n, c = x_fast.shape
    t_n = fill.shape[0]
    p_n = inner // STEPS
    vm = pl.BlockSpec(memory_space=pltpu.VMEM)
    sm = pl.BlockSpec(memory_space=pltpu.SMEM)
    tail = (STEPS, s_n, 8, 2 * c)
    outs = [(tail, F32), ((2, 32, LANES), F32), ((3, t_n, LANES), F32), ((3, f_n, LANES), F32),
            ((LANES, s_n * c), BF16), ((3 * LANES, LANES), BF16), ((3 * LANES, LANES), BF16), ((LANES, s_n * c), BF16)]
    return pl.pallas_call(
        k_prep,
        out_shape=[jax.ShapeDtypeStruct(s, d) for s, d in outs],
        in_specs=[pl.BlockSpec(memory_space=pl.ANY), sm, sm, vm, vm, vm, vm],
        out_specs=[vm] * len(outs),
        scratch_shapes=[
            pltpu.VMEM((s_n, inner, t_n, c), BF16),
            pltpu.VMEM((s_n * inner * t_n, c), F32),
            pltpu.VMEM(tail, F32),
            pltpu.VMEM(tail, F32),
            pltpu.SemaphoreType.DMA((2,)),
            pltpu.SemaphoreType.DMA,
        ],
        compiler_params=pltpu.CompilerParams(collective_id=10, has_side_effects=True, vmem_limit_bytes=VMEM_LIMIT),
        name="prepare",
    )(x_fast, fill, clip_offset, norms, w_fast_in.T, w_fast_mid, w_fast_out)


def per_device(slow_input, fast_input, clip_offset, fill, w_fast_in, w_fast_mid, w_fast_out, w_lateral,
               w_slow_in, w_slow_mid, w_slow_out, w_shortcut, gains, biases, slow_cot, fast_cot):
    sizes = (lax.axis_size("path"), lax.axis_size("frames"))
    t_n, side, _, c_slow = slow_input.shape
    f_n, c_fast = fast_input.shape[0], fast_input.shape[3]
    in_fast, in_slow, c_lat = w_fast_in.shape[1], w_slow_in.shape[1], w_lateral.shape[2]
    pixels = side * side
    groups = LANES // in_fast
    inner = pixels // groups
    p_n = inner // STEPS

    def slow_view(a):
        return jnp.transpose(a, (1, 2, 0, 3)).reshape(groups, inner, t_n, a.shape[3])

    def fast_view(a):
        return jnp.transpose(a, (1, 2, 0, 3)).reshape(groups, inner, f_n, a.shape[3])

    def unview(a):
        return jnp.transpose(a.reshape(side, side, a.shape[2], a.shape[3]), (2, 0, 1, 3))

    x_slow, cot_slow = slow_view(slow_input), slow_view(slow_cot)
    x_fast, cot_fast = fast_view(fast_input), fast_view(fast_cot)

    norms = jnp.stack([gains, biases])
    norms = jnp.pad(norms, ((0, 0), (0, -norms.shape[1] % (8 * LANES)))).reshape(2, -1, LANES)
    tail, gb, m16, m64, wfa, wmid, wback, wout = prepare(
        x_fast, fill, clip_offset, norms, w_fast_in, w_fast_mid, w_fast_out
    )
    wlat = w_lateral.reshape(-1, c_lat)
    wsp = w_slow_mid.reshape(9, in_slow, in_slow)

    sl = (groups, inner, t_n)
    fp = (inner, f_n)

    def slow_out(width, dtype):
        return out_blocked(sl + (width,), dtype, 1, p_n)

    def fast_out(width, dtype):
        return out_blocked(fp + (width,), dtype, 0, p_n)

    def sb_(a):
        return blocked(a, 1, p_n)

    def fb_(a):
        return blocked(a, 0, p_n)

    def stat(n):
        return out_whole((pad8(n), LANES), F32)

    def acc(rows_n, width, count):
        return [pltpu.VMEM((rows_n, width), F32)] * count

    small = (STEPS, 8, LANES)

    fa, lat, taps, c1, hp, hn = call(
        k_first,
        [sb_(x_fast), blocked(tail, 0, 1), whole(m16), whole(m64), whole(wfa), whole(wlat)],
        [fast_out(LANES, F32), slow_out(c_lat, F32), slow_out(5 * c_fast, BF16), STAT, UP, DOWN],
        [pltpu.VMEM((groups * p_n * f_n, c_fast), F32), *acc(f_n, LANES, 2), *acc(t_n, c_lat, 2)],
        "first",
        Exchange(sizes, 1, 7, fwd=(("lane4", 0, 1), ("plain", 6, 2)), up=small, down=small),
        [gb],
    )

    lact, ftap, sa, sp, fb, c2 = call(
        k_join,
        [sb_(x_slow), sb_(lat), fb_(fa), blocked(hp, 0, 1), blocked(hn, 0, 1), whole(c1), whole(m16), whole(m64),
         whole(w_slow_in), whole(w_shortcut), whole(wmid)],
        [slow_out(c_lat, BF16), fast_out(3 * LANES, BF16), slow_out(in_slow, F32), slow_out(c_slow, F32),
         fast_out(LANES, F32), STAT],
        [*acc(t_n, in_slow, 2), *acc(t_n, c_slow, 2), *acc(f_n, LANES, 2)],
        "join",
        Exchange(sizes, 2, 23, fwd=(("lane4", 1, 1), ("plain", 8, 2), ("plain", 20, 8))),
        [gb],
    )

    rows_n = side // STEPS
    pad, sb, fact, c3 = call(
        k_spatial,
        [whole(sa.reshape(side, side, t_n, in_slow)),
         fb_(fb), whole(c2), whole(m16), whole(m64), whole(wsp), whole(wout)],
        [out_whole((side + 2, side + 2, t_n, in_slow), BF16),
         out_blocked((side, side, t_n, in_slow), F32, 0, rows_n), fast_out(LANES, BF16), STAT],
        [*acc(t_n, in_slow, 2), *acc(f_n, groups * c_fast, 2)],
        "spatial",
        Exchange(sizes, 3, 13, fwd=(("row4", 2, 4), ("plain", 10, 2))),
        [gb],
    )

    sb4 = sb.reshape(sl + (in_slow,))
    sact, fast_y, df, st = call(
        k_expand,
        [sb_(sb4), fb_(fact), sb_(x_fast), sb_(cot_fast), whole(c3), whole(m16), whole(m64), whole(w_slow_out), whole(wout)],
        [slow_out(in_slow, BF16), out_blocked((groups, inner, f_n, c_fast), BF16, 1, p_n),
         fast_out(groups * c_fast, F32), stat(25)],
        [*acc(t_n, c_slow, 2), *acc(f_n, groups * c_fast, 2)],
        "expand",
    )
    c4, q4 = exchange_alone(
        Exchange(sizes, 4, 25, fwd=(("plain", 12, 8),), bwd=(("row4", 0, 0, 2, 4, 0, 4),)), st, gb, [c3]
    )

    halo_pair = out_blocked((STEPS, 2, 8, LANES), F32, 0, 1)
    slow_y, dy, dfb, g_fout, up, down, st = call(
        k_out,
        [sb_(sact), sb_(sp), sb_(cot_slow), fb_(df), fb_(fact), fb_(fb), whole(c2), whole(c3), whole(c4), whole(q4),
         whole(m16), whole(m64), whole(w_slow_out), whole(wout)],
        [slow_out(c_slow, BF16), slow_out(c_slow, F32), fast_out(LANES, F32),
         out_whole((in_fast, c_fast), F32), halo_pair, halo_pair, stat(26)],
        [*acc(t_n, c_slow, 3), *acc(f_n, LANES, 2), *acc(LANES, groups * c_fast, 1)],
        "out",
    )
    pair = (STEPS, 2, 8, LANES)
    ex5 = Exchange(
        sizes, 5, 26,
        bwd=(("plain", 0, 0, 12, 8, 0, 8), ("plain", 1, 3, 20, 8, 0, 16), ("lane4", 1, 0, 1, 1, 24, 25)),
        up=pair, down=pair,
    )
    q5, hp, hn = exchange_alone(ex5, st, gb, [c4, c2], up, down)

    c_cat = w_slow_in.shape[0]
    width = in_slow
    stream_a = Stream(sizes, rows_for(sizes, c_cat * c_slow // width), width)
    stream_b = Stream(sizes, rows_for(sizes, 9 * in_slow), width)
    gw_short, gw_sout, dsp, dsb, dfa, g_fmid, q6 = call(
        k_back_out,
        [sb_(x_slow), sb_(lact), sb_(dy), sb_(sp), sb_(sact), sb_(sb4), fb_(dfb), fb_(fb), fb_(fa), fb_(ftap), blocked(hp, 0, 1), blocked(hn, 0, 1),
         whole(c1), whole(c2), whole(c3), whole(c4), whole(q5), whole(m16), whole(m64), whole(w_slow_out), whole(wback)],
        [out_whole((stream_a.rows_n, width), BF16), out_whole((c_slow, width), BF16), slow_out(c_slow, BF16),
         slow_out(in_slow, F32), fast_out(LANES, F32), out_whole((3 * in_fast, LANES), F32), STAT],
        [*acc(t_n, in_slow, 2), *acc(f_n, LANES, 2), *acc(c_cat, c_slow, 1), *acc(in_slow, c_slow, 1),
         *acc(LANES, 3 * LANES, 1)],
        "back_out",
        Exchange(sizes, 6, 6, bwd=(("plain", 0, 4, 10, 2, 0, 2), ("lane4", 1, 0, 0, 1, 4, 5))),
        [gb, c3, c1],
    )

    def rows2(a):
        return a.reshape(-1, a.shape[-1])

    dsa_low, dfa_low, dlat, gw_fast, q7, q8, hn, res_a, near_b = back_tail(
        stream_a, stream_b,
        Exchange(sizes, 7, 4, bwd=(("plain", 0, 1, 8, 2, 0, 2),)),
        Exchange(sizes, 7, 4, bwd=(("plain", 0, 1, 6, 2, 0, 2),), post=(STEPS, groups * 8, c_lat)),
        [gw_short, rows2(dsb), rows2(sb), pad, wsp, rows2(sa), x_fast, dfa, fa, w_slow_in, w_shortcut, rows2(dsp), rows2(lat)],
        [gb, c1, c2, c3, q6, m16, m64, g_fout, g_fmid],
        side, t_n, in_slow,
    )
    slow_gx, gw_in = call(
        k_slow_grad,
        [sb_(x_slow), sb_(lact), sb_(dsa_low.reshape(sl + (in_slow,))), sb_(dsp), whole(w_slow_in), whole(w_shortcut)],
        [slow_out(c_slow, BF16), out_whole((c_cat, in_slow), BF16)], acc(in_slow, c_cat, 1), "slow_grad",
    )
    fast_gx, gw_lat = call(
        k_fast_grad,
        [sb_(dlat.reshape(sl + (c_lat,))), sb_(lat), sb_(taps), blocked(hn, 0, 1), fb_(df), fb_(dfa_low), whole(c1), whole(q8),
         whole(m16), whole(wlat), whole(wfa)],
        [out_blocked((groups, inner, f_n, c_fast), BF16, 1, p_n), out_whole((5 * c_fast, c_lat), BF16)],
        [pltpu.VMEM((groups * p_n * f_n, c_fast), F32), *acc(c_lat, 5 * c_fast, 1)],
        "fast_grad",
    )
    sum_a, sum_bc, _ = final_sum(sizes, 9, stream_a, stream_b, res_a, near_b, [gw_sout, gw_in, gw_lat, gw_fast])
    blocks = c_slow // in_slow
    pieces = [(0, n * c_cat, c_cat, 0, n * width) for n in range(blocks)]
    pieces.append((1, 0, 9 * in_slow, 2, None))
    at = 0
    for n in range(blocks):
        pieces.append((2, at, in_slow, 1, n * width))
        at += in_slow
    for out, tall in ((3, c_cat), (4, gw_lat.shape[0]), (5, gw_fast.shape[0])):
        pieces.append((2, at, tall, out, None))
        at += tall
    g_short, g_sout, gw_mid, gw_in, gw_lat, gw_fast = unpack(
        sum_a, sum_bc, stream_b.ch, tuple(pieces),
        [(c_cat, c_slow), (in_slow, c_slow), (9 * in_slow, width), (c_cat, in_slow), gw_lat.shape, gw_fast.shape],
    )
    taps_t = [gw_fast[in_fast : 2 * in_fast, :in_fast], gw_fast[in_fast : 2 * in_fast, c_fast : c_fast + in_fast],
              gw_fast[2 * in_fast :, :in_fast]]
    grads = (
        gw_fast[:in_fast, :c_fast].T,
        jnp.transpose(jnp.stack(taps_t), (0, 2, 1)),
        gw_fast[:in_fast, c_fast:],
        gw_lat.reshape(w_lateral.shape),
        gw_in,
        gw_mid.reshape(w_slow_mid.shape),
        g_sout,
        g_short,
    )

    def norm_grads(slab):
        def row(q, at, n):
            return q[slab, at : at + n].reshape(-1)

        return jnp.concatenate(
            [row(q6, 2, 1)[:in_fast], row(q5, 16, 1)[:in_fast], row(q4, 0, 1), row(q8, 0, 2), row(q7, 0, 2),
             row(q6, 0, 2), row(q5, 0, 8), row(q5, 8, 8)]
        )

    return (
        unview(slow_y),
        unview(fast_y),
        unview(slow_gx),
        unview(fast_gx),
        *grads,
        norm_grads(3),
        norm_grads(2),
    )


def solution(mesh):
    frames = P(("path", "frames"), None, None, None)
    in_specs = (frames, frames, P(AXES), P(AXES), *([P()] * 10), frames, frames)
    out_specs = (*([frames] * 4), *([P()] * 10))
    return jax.shard_map(per_device, mesh=mesh, in_specs=in_specs, out_specs=out_specs, check_vma=False)
```

```python
import functools

import jax
import jax.numpy as jnp
from jax import lax
from jax.experimental import pallas as pl
from jax.experimental.pallas import tpu as pltpu
from jax.sharding import PartitionSpec as P

norm_eps = 1e-05
F32 = jnp.float32
BF16 = jnp.bfloat16
MESH = pl.DeviceIdType.MESH
AXES = ("path", "frames")
STEPS = 7
LANES = 128
VMEM_LIMIT = 56 * 1024 * 1024


def dot(a, b):
    return jnp.dot(a, b, preferred_element_type=F32)


def dot_nt(a, b):
    return lax.dot_general(a, b, (((1,), (1,)), ((), ())), preferred_element_type=F32)


def dot_tn(a, b):
    return lax.dot_general(a, b, (((0,), (0,)), ((), ())), preferred_element_type=F32)


def sig(v):
    return 0.5 * jnp.tanh(0.5 * v) + 0.5


def slope(v):
    s = sig(v)
    return s + (v * s) * (1.0 - s)


def rows(ref, slab, first, count):
    parts = [ref[slab, first + j : first + j + 1, :] for j in range(count)]
    return parts[0] if count == 1 else jnp.concatenate(parts, axis=1)


def put_rows(ref, first, value):
    for j in range(value.shape[1] // LANES):
        ref[first + j : first + j + 1, :] = value[:, j * LANES : (j + 1) * LANES]


def zero_ref(ref):
    ref[...] = jnp.zeros(ref.shape, ref.dtype)


def spread_add(step, z, mean_ref, m2_ref, cols=slice(None)):
    count = z.shape[0]
    mean = jnp.sum(z, axis=0) * (1.0 / count)
    d = z - mean
    m2 = jnp.sum(d * d, axis=0)
    first = step == 0
    old_mean = jnp.where(first, 0.0, mean_ref[:, cols])
    old_m2 = jnp.where(first, 0.0, m2_ref[:, cols])
    done = jnp.full((1, z.shape[-1]), step, jnp.int32).astype(F32)
    share = 1.0 / (done + 1.0)
    delta = mean - old_mean
    mean_ref[:, cols] = old_mean + delta * share
    m2_ref[:, cols] = old_m2 + m2 + delta * delta * (done * share * count)


def spread_end(mean_ref, m2_ref, fill, positions):
    filled = jnp.sum(fill, axis=0, keepdims=True)
    mean = jnp.sum(fill * mean_ref[...], axis=0, keepdims=True) / jnp.maximum(filled, 1.0)
    d = mean_ref[...] - mean
    m2 = jnp.sum(fill * (m2_ref[...] + positions * (d * d)), axis=0, keepdims=True)
    return mean, m2


def sum_add(step, value, ref, cols=slice(None)):
    ref[:, cols] = jnp.where(step == 0, 0.0, ref[:, cols]) + jnp.sum(value, axis=0)


def sum_end(ref):
    return jnp.sum(ref[...], axis=0, keepdims=True)


def pad8(n):
    return -(-n // 8) * 8


def exchange_peers(cfg):
    paths, length = lax.axis_size("path"), lax.axis_size("frames")
    near = 4
    g1, g2 = paths * near, length // near
    me_p, me_f = lax.axis_index("path"), lax.axis_index("frames")
    me = me_p * length + me_f
    total = paths * length
    r1 = me_p * near + lax.rem(me_f, near)
    r2 = lax.div(me_f, near)

    def peer1(k):
        r = lax.rem(r1 + k, g1)
        return (lax.div(r, near), r2 * near + lax.rem(r, near))

    def peer2(k):
        r = lax.rem(r2 + k, g2)
        return (me_p, r * near + lax.rem(me_f, near))

    def split(index):
        return (lax.div(index, length), lax.rem(index, length))

    nxt, prv = split(lax.rem(me + 1, total)), split(lax.rem(me + total - 1, total))
    return g1, g2, r1, r2, peer1, peer2, nxt, prv


def exchange_hello(cfg):
    g1, g2, _, _, peer1, peer2, nxt, prv = exchange_peers(cfg)
    peers = [peer1(k) for k in range(1, g1)] + [peer2(k) for k in range(1, g2)]
    if cfg.greets:
        peers += [nxt, prv]
    for peer in peers:
        pl.semaphore_signal(pltpu.get_barrier_semaphore(), inc=1, device_id=peer, device_id_type=MESH)
    return len(peers)


def exchange_run(cfg, ins, outs, scratch, meanwhile=None, post=None):
    fwd, bwd = cfg.fwd, cfg.bwd
    nf = sum(c[2] for c in fwd)
    nb = max((c[6] + c[4] for c in bwd), default=0)
    n_row = 2 * nf + nb
    stats_ref, up_ref, down_ref = scratch[:3]
    gb_ref, *coef_refs = ins
    outs = list(outs)
    coef_out = outs.pop(0) if nf else None
    pq_out = outs.pop(0) if nb else None
    from_prev = outs.pop(0) if cfg.up else None
    from_next = outs.pop(0) if cfg.down else None
    slots1, slots2, mid, tot, send1, recv1, send2, recv2, up_land, up_sems, down_land, down_sems = scratch[3:15]
    g1, g2, r1, r2, peer1, peer2, nxt, prv = exchange_peers(cfg)

    halos = []
    copies = []
    for k in range(1, g1):
        copies.append(
            pltpu.make_async_remote_copy(
                src_ref=stats_ref,
                dst_ref=slots1.at[r1],
                send_sem=send1.at[k],
                recv_sem=recv1.at[k],
                device_id=peer1(k),
                device_id_type=MESH,
            )
        )
        copies[-1].start()
    for used, src, land, sems, peer in (
        (cfg.up, up_ref, up_land, up_sems, nxt),
        (cfg.down, down_ref, down_land, down_sems, prv),
    ):
        if used:
            halos.append(
                pltpu.make_async_remote_copy(
                    src_ref=src,
                    dst_ref=land,
                    send_sem=sems.at[0],
                    recv_sem=sems.at[1],
                    device_id=peer,
                    device_id_type=MESH,
                )
            )
            halos[-1].start()
    slots1[r1] = stats_ref[...]
    if meanwhile is not None:
        meanwhile()
    for c in copies:
        c.wait_recv()

    def combine(slots, count, out):
        if nf:
            n = slots[0, n_row : n_row + 1, :]
            for g in range(1, count):
                n = n + slots[g, n_row : n_row + 1, :]
            acc = slots[0, n_row : n_row + 1, :] * slots[0, 0:nf, :]
            for g in range(1, count):
                acc = acc + slots[g, n_row : n_row + 1, :] * slots[g, 0:nf, :]
            mean = acc / jnp.maximum(n, 1.0)
            m2 = None
            for g in range(count):
                d = slots[g, 0:nf, :] - mean
                part = slots[g, nf : 2 * nf, :] + slots[g, n_row : n_row + 1, :] * (d * d)
                m2 = part if m2 is None else m2 + part
            out[0:nf, :] = mean
            out[nf : 2 * nf, :] = m2
            out[n_row : n_row + 1, :] = n
        if nb:
            acc = slots[0, 2 * nf : n_row, :]
            for g in range(1, count):
                acc = acc + slots[g, 2 * nf : n_row, :]
            out[2 * nf : n_row, :] = acc

    zero_ref(mid)
    combine(slots1, g1, mid)
    copies2 = []
    for k in range(1, g2):
        copies2.append(
            pltpu.make_async_remote_copy(
                src_ref=mid,
                dst_ref=slots2.at[r2],
                send_sem=send2.at[k],
                recv_sem=recv2.at[k],
                device_id=peer2(k),
                device_id_type=MESH,
            )
        )
        copies2[-1].start()
    slots2[r2] = mid[...]
    for c in copies2:
        c.wait_recv()
    combine(slots2, g2, tot)

    def lanes4(v):
        w = v + pltpu.roll(v, 64, 1)
        return w + pltpu.roll(w, 32, 1)

    at = 0
    for kind, g_row, count in fwd:
        n = tot[n_row : n_row + 1, :]
        mean = tot[at : at + count, :]
        m2 = tot[nf + at : nf + at + count, :]
        if kind == "lane4":
            whole = lanes4(mean) * 0.25
            d = mean - whole
            var = lanes4(m2 + n * (d * d)) / (4.0 * n)
            mean = whole
        elif kind == "row4":
            whole = jnp.sum(mean, axis=0, keepdims=True) * 0.25
            d = mean - whole
            var = jnp.sum(m2 + n * (d * d), axis=0, keepdims=True) / (4.0 * n)
            var = jnp.broadcast_to(var, (count, LANES))
            mean = jnp.broadcast_to(whole, (count, LANES))
        else:
            var = m2 / n
        inv = lax.rsqrt(var + norm_eps)
        scale = inv * gb_ref[0, g_row : g_row + count, :]
        coef_out[0, at : at + count, :] = scale
        coef_out[1, at : at + count, :] = gb_ref[1, g_row : g_row + count, :] - mean * scale
        coef_out[2, at : at + count, :] = inv
        coef_out[3, at : at + count, :] = mean * inv
        coef_out[4, at : at + count, :] = jnp.broadcast_to(n, (count, LANES))
        at += count
    at = 0
    for kind, coef, row, _, count, db_at, dg_at in bwd:
        db = tot[2 * nf + db_at : 2 * nf + db_at + count, :]
        dg = tot[2 * nf + dg_at : 2 * nf + dg_at + count, :]
        c = coef_refs[coef]
        scale, inv = c[0, row : row + count, :], c[2, row : row + count, :]
        mi, n = c[3, row : row + count, :], c[4, row : row + count, :]
        if kind == "lane4":
            db, dg, n = lanes4(db), lanes4(dg), 4.0 * n
        elif kind == "row4":
            db = jnp.broadcast_to(jnp.sum(db, axis=0, keepdims=True), (count, LANES))
            dg = jnp.broadcast_to(jnp.sum(dg, axis=0, keepdims=True), (count, LANES))
            n = 4.0 * n
        pq_out[0, at : at + count, :] = scale / n * (db - mi * dg)
        pq_out[1, at : at + count, :] = scale / n * inv * dg
        pq_out[2, at : at + count, :] = db
        pq_out[3, at : at + count, :] = dg
        at += count

    if cfg.post:
        post_sent, post_land, post_sems = scratch[15:]
        post(pq_out, post_sent)
        late = pltpu.make_async_remote_copy(
            src_ref=post_sent,
            dst_ref=post_land,
            send_sem=post_sems.at[0],
            recv_sem=post_sems.at[1],
            device_id=prv,
            device_id_type=MESH,
        )
        late.start()
        late.wait()
        outs.pop(0)[...] = post_land[...]
    for c in halos:
        c.wait()
    if cfg.up:
        from_prev[...] = up_land[...]
    if cfg.down:
        from_next[...] = down_land[...]
    for c in copies:
        c.wait_send()
    for c in copies2:
        c.wait_send()


class Exchange:
    def __init__(self, sizes, cid, rows_n, fwd=(), bwd=(), up=None, down=None, post=None):
        self.cid, self.fwd, self.bwd, self.up, self.down, self.post = cid, fwd, bwd, up, down, post
        self.greets = bool(up or down or post)
        g1, g2, r = sizes[0] * 4, sizes[1] // 4, pad8(rows_n)
        self.outs = []
        nf, nn = sum(c[2] for c in fwd), sum(c[4] for c in bwd)
        if nf:
            self.outs.append(((5, nf, LANES), F32))
        if nn:
            self.outs.append(((4, nn, LANES), F32))
        self.outs += [(h, F32) for h in (up, down) if h]
        if post:
            self.outs.append((post, BF16))
        none = (8, LANES)
        self.stats = (r, LANES)
        self.work = [
            pltpu.VMEM((g1, r, LANES), F32),
            pltpu.VMEM((g2, r, LANES), F32),
            pltpu.VMEM((r, LANES), F32),
            pltpu.VMEM((r, LANES), F32),
            pltpu.SemaphoreType.DMA((g1,)),
            pltpu.SemaphoreType.DMA((g1,)),
            pltpu.SemaphoreType.DMA((g2,)),
            pltpu.SemaphoreType.DMA((g2,)),
            pltpu.VMEM(up or none, F32),
            pltpu.SemaphoreType.DMA((2,)),
            pltpu.VMEM(down or none, F32),
            pltpu.SemaphoreType.DMA((2,)),
        ]
        if post:
            self.work += [pltpu.VMEM(post, BF16), pltpu.VMEM(post, BF16), pltpu.SemaphoreType.DMA((2,))]
        self.local = [pltpu.VMEM(self.stats, F32), pltpu.VMEM(up or none, F32), pltpu.VMEM(down or none, F32)]


STAT, UP, DOWN = "stat", "up", "down"


def call(kernel, ins, outs, scratch=(), name=None, ex=None, ex_ins=(), pre=None, pre_ins=()):
    real = [o for o in outs if not isinstance(o, str)]
    given = ins
    ins = [a for a in given if not isinstance(a, int)]
    extra_in = [whole(a) for a in (*ex_ins, *pre_ins)]
    extra_out = [out_whole(s, d) for s, d in ex.outs] if ex else []
    local = [*ex.local, *ex.work] if ex else []
    n_local = len(local)
    if pre:
        extra_out.append(out_whole(*pre.outs[0]))
        local += [*pre.work, *[pltpu.VMEM(shape, d) for shape, d in pre.outs[1:]]]
    all_in, all_out = [*ins, *extra_in], [*real, *extra_out]
    sizes = [len(ins), len(extra_in), len(real), len(extra_out), len(scratch), len(local)]
    ends = [sum(sizes[: k + 1]) for k in range(len(sizes))]

    def body(*refs):
        k_in, x_in, k_out, x_out, k_scr, x_scr = (refs[e - n : e] for e, n in zip(ends, sizes))
        if ex is None:
            kernel(*k_in, *k_out, *k_scr)
            return
        i = pl.program_id(0)

        p_ins, p_outs, p_scr = x_in[len(ex_ins) :], [], x_scr[n_local:]
        x_in, x_scr = x_in[: len(ex_ins)], x_scr[:n_local]
        if pre:
            n = len(pre.work)
            p_outs = [x_out[-1], *p_scr[n:]]
            x_out = x_out[:-1]

        @pl.when(i == 0)
        def _():
            exchange_hello(pre or ex)
            if pre:
                pl.semaphore_wait(pltpu.get_barrier_semaphore(), len_peers(pre))
                exchange_run(pre, p_ins[3:], p_outs, [*p_ins[:3], *p_scr[:n]])

        if pre:
            it_in = iter(k_in)
            views = [p_outs[0], *[o.at[pl.ds(i, 1)] for o in p_outs[1:]]]
            k_in = [views[a] if isinstance(a, int) else next(it_in) for a in given]
        named = {STAT: x_scr[0]}
        if ex.up:
            named[UP] = x_scr[1].at[pl.ds(i, 1)]
        if ex.down:
            named[DOWN] = x_scr[2].at[pl.ds(i, 1)]
        it = iter(k_out)
        late = kernel(*k_in, *[named[o] if isinstance(o, str) else next(it) for o in outs], *k_scr)

        @pl.when(i == STEPS - 1)
        def _():
            if not pre:
                pl.semaphore_wait(pltpu.get_barrier_semaphore(), len_peers(ex))
            exchange_run(ex, x_in, x_out, x_scr, late)

    params = {"collective_id": ex.cid, "has_side_effects": True} if ex else {}
    return pl.pallas_call(
        body,
        grid=(STEPS,),
        in_specs=[pl.BlockSpec(b, m) for _, b, m in all_in],
        out_specs=[pl.BlockSpec(b, m) for _, _, b, m in all_out],
        out_shape=[jax.ShapeDtypeStruct(s, d) for s, d, _, _ in all_out],
        scratch_shapes=[*scratch, *local],
        compiler_params=pltpu.CompilerParams(
            dimension_semantics=("arbitrary",), vmem_limit_bytes=VMEM_LIMIT, **params
        ),
        name=name,
    )(*[a for a, _, _ in all_in])


def len_peers(ex):
    paths, length = lax.axis_size("path"), lax.axis_size("frames")
    return paths * 4 - 1 + length // 4 - 1 + (2 if ex.greets else 0)


def whole(array):
    zeros = (0,) * array.ndim
    return (array, array.shape, lambda i: zeros)


def blocked(array, axis, size):
    block = array.shape[:axis] + (size,) + array.shape[axis + 1 :]
    return (array, block, lambda i: tuple(i if d == axis else 0 for d in range(array.ndim)))


def out_whole(shape, dtype):
    zeros = (0,) * len(shape)
    return (shape, dtype, shape, lambda i: zeros)


def out_blocked(shape, dtype, axis, size):
    block = shape[:axis] + (size,) + shape[axis + 1 :]
    return (shape, dtype, block, lambda i: tuple(i if d == axis else 0 for d in range(len(shape))))


def flat(value):
    return value.reshape(-1, value.shape[-1])


def spread_rows(ref, index, count, height):
    return [jnp.broadcast_to(ref[(*index, slice(p, p + 1))], (height, ref.shape[-1])) for p in range(count)]


def k_first(i, x_ref, tail_ref, m16_ref, m64_ref, wfa_ref, wlat_ref,
            fa_ref, lat_ref, taps_ref, st_ref, up_ref, down_ref, xs, fm, fv, lm, lv):
    x = x_ref[...]
    s_n, p_n, f_n, _ = x.shape
    packed = jnp.concatenate([flat(x[s]) for s in range(s_n)], axis=1)
    fa = dot_nt(packed, wfa_ref[...])
    fa_ref[...] = fa.reshape(fa_ref.shape)
    zero_ref(up_ref)
    zero_ref(down_ref)
    for p in range(p_n):
        down_ref[0, p : p + 1, :] = fa[p * f_n : p * f_n + 1, :]
        up_ref[0, p : p + 1, :] = fa[p * f_n + f_n - 1 : p * f_n + f_n, :]
    spread_add(i, fa.reshape(p_n, f_n, LANES), fm, fv)

    xs[...] = flat(x).astype(F32)
    n = xs.shape[0] // 4
    quarter = [xs[pl.ds(k, n, stride=4), :] for k in range(4)]
    t_n = f_n // 4
    first = lax.broadcasted_iota(jnp.int32, (n // t_n, t_n, LANES), 1) == 0
    link = m16_ref[1:2]
    taps = []
    for k in range(2):
        halo = jnp.concatenate(
            [
                jnp.broadcast_to(tail_ref[0, s, p : p + 1, k * LANES : (k + 1) * LANES], (t_n, LANES))
                for s in range(s_n)
                for p in range(p_n)
            ],
            axis=0,
        )
        moved = pltpu.roll(quarter[2 + k], 1, 0).reshape(n // t_n, t_n, LANES)
        taps.append(flat(jnp.where(first, halo.reshape(moved.shape), moved) * link))
    taps = jnp.concatenate([*taps, *quarter[:3]], axis=1).astype(BF16)
    taps_ref[...] = taps.reshape(taps_ref.shape)
    lat = dot(taps, wlat_ref[...])
    lat_ref[...] = lat.reshape(lat_ref.shape)
    spread_add(i, lat.reshape(n // t_n, t_n, lat.shape[1]), lm, lv)

    @pl.when(i == STEPS - 1)
    def _():
        zero_ref(st_ref)
        fill = m16_ref[0, :, 0:1]
        mean, m2 = spread_end(fm, fv, m64_ref[0, :, 0:1], STEPS * p_n)
        put_rows(st_ref, 0, mean)
        put_rows(st_ref, 3, m2)
        mean, m2 = spread_end(lm, lv, fill, STEPS * p_n * s_n)
        put_rows(st_ref, 1, mean)
        put_rows(st_ref, 4, m2)
        put_rows(st_ref, 6, count_row(m16_ref, STEPS * p_n * s_n))


def count_row(m16_ref, positions):
    return jnp.sum(m16_ref[0], axis=0, keepdims=True) * float(positions)


def shifted(value, first_rows, last_rows, f_n):
    n = value.shape[0]
    shape = (n // f_n, f_n, value.shape[1])
    place = lax.broadcasted_iota(jnp.int32, shape, 1)
    before = jnp.where(place == 0, first_rows, pltpu.roll(value, 1, 0).reshape(shape))
    after = jnp.where(place == f_n - 1, last_rows, pltpu.roll(value, n - 1, 0).reshape(shape))
    return before, after


def k_join(i, x_ref, lat_ref, fa_ref, hp_ref, hn_ref, c1_ref, m16_ref, m64_ref, win_ref, wsc_ref, wmid_ref,
           lact_ref, ftap_ref, sa_ref, sp_ref, fb_ref, st_ref, am, av, pm, pv, bm, bv):
    s_n, p_n, t_n, c_slow = x_ref.shape
    c_lat = lat_ref.shape[-1]
    v = flat(lat_ref[...]) * rows(c1_ref, 0, 1, 2) + rows(c1_ref, 1, 1, 2)
    lact = (v * sig(v)).astype(BF16)
    lact_ref[...] = lact.reshape(lact_ref.shape)
    joined = jnp.concatenate([flat(x_ref[...]), lact], axis=1)
    wide = c_lat
    for n in range(1 + wsc_ref.shape[1] // wide):
        z = dot(joined, win_ref[...] if n == 0 else wsc_ref[:, (n - 1) * wide : n * wide])
        z4 = z.reshape(s_n, p_n, t_n, wide)
        z3 = z.reshape(s_n * p_n, t_n, wide)
        if n == 0:
            sa_ref[...] = z4
            spread_add(i, z3, am, av)
        else:
            cols = slice((n - 1) * wide, n * wide)
            sp_ref[:, :, :, cols] = z4
            spread_add(i, z3, pm, pv, cols)

    f_n = fa_ref.shape[1]
    scale, shift = rows(c1_ref, 0, 0, 1), rows(c1_ref, 1, 0, 1)

    def act(z):
        w = z * scale + shift
        return (w * sig(w)).astype(BF16).astype(F32)

    fact = act(flat(fa_ref[...]))
    ends = []
    for ref in (hp_ref, hn_ref):
        small = act(ref[0])
        ends.append(
            jnp.concatenate(
                [jnp.broadcast_to(small[p : p + 1, :], (f_n, LANES)) for p in range(p_n)], axis=0
            ).reshape(p_n, f_n, LANES)
        )
    before, after = shifted(fact, ends[0], ends[1], f_n)
    ftap = jnp.concatenate(
        [flat(before * m64_ref[1:2]), fact, flat(after * m64_ref[2:3])], axis=1
    ).astype(BF16)
    ftap_ref[...] = ftap.reshape(ftap_ref.shape)
    fb = dot(ftap, wmid_ref[...])
    fb_ref[...] = fb.reshape(fb_ref.shape)
    spread_add(i, fb.reshape(p_n, f_n, LANES), bm, bv)

    @pl.when(i == STEPS - 1)
    def _():
        zero_ref(st_ref)
        fill = m16_ref[0, :, 0:1]
        positions = STEPS * p_n * s_n
        mean, m2 = spread_end(bm, bv, m64_ref[0, :, 0:1], STEPS * p_n)
        put_rows(st_ref, 0, mean)
        put_rows(st_ref, 11, m2)
        mean, m2 = spread_end(am, av, fill, positions)
        put_rows(st_ref, 1, mean)
        put_rows(st_ref, 12, m2)
        mean, m2 = spread_end(pm, pv, fill, positions)
        put_rows(st_ref, 3, mean)
        put_rows(st_ref, 14, m2)
        put_rows(st_ref, 22, count_row(m16_ref, positions))


def k_spatial(i, sa_ref, fb_ref, c2_ref, m16_ref, m64_ref, wsp_ref, wout_ref,
              pad_ref, sb_ref, fact_ref, st_ref, sm, sv, cm, cv):
    h_n, w_n, t_n, c = sa_ref.shape

    @pl.when(i == 0)
    def _():
        scale, shift = rows(c2_ref, 0, 1, 2), rows(c2_ref, 1, 1, 2)
        zero_ref(pad_ref)

        @pl.loop(0, h_n)
        def _(h):
            v = flat(sa_ref[h]) * scale + shift
            pad_ref[h + 1, 1 : w_n + 1] = (v * sig(v)).astype(BF16).reshape(w_n, t_n, c)

    per = h_n // STEPS
    h0 = i * per
    acc = None
    for a in range(3):
        for b in range(3):
            k = 3 * a + b
            part = dot(flat(pad_ref[pl.ds(h0 + a, per), b : b + w_n].reshape(per * w_n, t_n, c)), wsp_ref[k])
            acc = part if acc is None else acc + part
    sb_ref[...] = acc.reshape(sb_ref.shape)
    spread_add(i, acc.reshape(per * w_n, t_n, acc.shape[1]), sm, sv)

    p_n, f_n, _ = fb_ref.shape
    v = flat(fb_ref[...]) * rows(c2_ref, 0, 0, 1) + rows(c2_ref, 1, 0, 1)
    fact = (v * sig(v)).astype(BF16)
    fact_ref[...] = fact.reshape(fact_ref.shape)
    fc = dot(fact, wout_ref[...])
    spread_add(i, fc.reshape(p_n, f_n, fc.shape[1]), cm, cv)

    @pl.when(i == STEPS - 1)
    def _():
        zero_ref(st_ref)
        mean, m2 = spread_end(cm, cv, m64_ref[0, :, 0:1], STEPS * p_n)
        put_rows(st_ref, 0, mean)
        put_rows(st_ref, 6, m2)
        mean, m2 = spread_end(sm, sv, m16_ref[0, :, 0:1], h_n * w_n)
        put_rows(st_ref, 4, mean)
        put_rows(st_ref, 10, m2)
        put_rows(st_ref, 12, count_row(m16_ref, h_n * w_n))


def k_expand(i, sb_ref, fact_ref, x_ref, cot_ref, c3_ref, m16_ref, m64_ref, wso_ref, wout_ref,
             sact_ref, fout_ref, df_ref, st_ref, cm, cv, s1, s2):
    s_n, p_n, t_n = x_ref.shape[0], fact_ref.shape[0], sb_ref.shape[-2]
    v = flat(sb_ref[...]) * rows(c3_ref, 0, 4, 2) + rows(c3_ref, 1, 4, 2)
    sact = (v * sig(v)).astype(BF16)
    sact_ref[...] = sact.reshape(sact_ref.shape)
    wide = 256
    for n in range(wso_ref.shape[1] // wide):
        cols = slice(n * wide, (n + 1) * wide)
        z = dot(sact, wso_ref[:, cols])
        spread_add(i, z.reshape(s_n * p_n, t_n, wide), cm, cv, cols)

    f_n = fact_ref.shape[1]
    fc = dot(flat(fact_ref[...]), wout_ref[...])
    fill = m64_ref[0:1]
    for s in range(s_n):
        cols = slice(s * LANES, (s + 1) * LANES)
        z = fc[:, cols].reshape(p_n, f_n, LANES)
        unit = z * rows(c3_ref, 2, s, 1) - rows(c3_ref, 3, s, 1)
        pre = z * rows(c3_ref, 0, s, 1) + rows(c3_ref, 1, s, 1) + x_ref[s].astype(F32)
        g = sig(pre)
        y = pre * g
        fout_ref[s] = (y * fill).astype(BF16)
        d = cot_ref[s].astype(F32) * fill * (g + y * (1.0 - g))
        df_ref[:, :, cols] = d
        sum_add(i, d, s1, cols)
        sum_add(i, d * unit, s2, cols)

    @pl.when(i == STEPS - 1)
    def _():
        zero_ref(st_ref)
        positions = STEPS * p_n * s_n
        mean, m2 = spread_end(cm, cv, m16_ref[0, :, 0:1], positions)
        put_rows(st_ref, 0, mean)
        put_rows(st_ref, 8, m2)
        put_rows(st_ref, 16, sum_end(s1))
        put_rows(st_ref, 20, sum_end(s2))
        put_rows(st_ref, 24, count_row(m16_ref, positions))


def run_resident(kernel, ex_list, hbm, small, locals_, outs, scratch, name):
    vm, anywhere = pl.BlockSpec(memory_space=pltpu.VMEM), pl.BlockSpec(memory_space=pl.ANY)
    for ex in ex_list:
        outs = [*outs, *[(shape, dtype, False) for shape, dtype in ex.outs]]
    work = [w for ex in ex_list for w in (*ex.local, *ex.work)]
    sizes = [len(hbm), len(small), len(outs), len(hbm), len(locals_), len(scratch), 1]
    ends = [sum(sizes[: k + 1]) for k in range(len(sizes))]

    def body(*refs):
        h, sm, o, loaded, kept, scr, (sems,) = (refs[e - n : e] for e, n in zip(ends, sizes))
        rest, at = [], ends[-1]
        for ex in ex_list:
            n = len(ex.local) + len(ex.work)
            rest.append(refs[at : at + n])
            at += n
        loads = [pltpu.make_async_copy(a, b, sems.at[k]) for k, (a, b) in enumerate(zip(h, loaded))]
        greeter = max(ex_list, key=lambda ex: ex.greets)
        count = exchange_hello(greeter)
        for load in loads:
            load.start()
        kernel(loads, lambda: pl.semaphore_wait(pltpu.get_barrier_semaphore(), count), loaded, sm, kept, scr, o, rest)

    return pl.pallas_call(
        body,
        out_shape=[jax.ShapeDtypeStruct(shape, dtype) for shape, dtype, _ in outs],
        in_specs=[anywhere] * len(hbm) + [vm] * len(small),
        out_specs=[anywhere if stays else vm for _, _, stays in outs],
        scratch_shapes=[
            *[pltpu.VMEM(a.shape, a.dtype) for a in hbm], *[pltpu.VMEM(*k) for k in locals_], *scratch,
            pltpu.SemaphoreType.DMA((len(hbm),)), *work,
        ],
        compiler_params=pltpu.CompilerParams(
            collective_id=ex_list[0].cid, has_side_effects=True, vmem_limit_bytes=VMEM_LIMIT
        ),
        name=name,
    )(*hbm, *small)


def stores_of(pairs, sems):
    return [pltpu.make_async_copy(a, b, sems.at[k]) for k, (a, b) in enumerate(pairs)]


def k_front(exs, loads, met, loaded, small, kept, scratch, outs, work):
    x_fast, wlat, x_slow, w_in, w_sc = loaded
    tail_ref, gb, m16, m64, wfa, wmid = small
    fa, lat, taps, lact, ftap, sa, sp, fb = kept
    xs, fm, fv, lm, lv, am, av, pm, pv, bm, bv, sems, sp_sems = scratch
    big, (c1, hp, hn, c2) = outs[:8], outs[8:]
    p_n = fa.shape[0] // STEPS
    copies = dict(zip((0, 1, 2, 3, 4, 5, 7), stores_of([p for k, p in enumerate(zip(kept, big)) if k != 6], sems)))
    st1, up, down = work[0][:3]
    loads[0].wait()
    loads[1].wait()

    def first(i):
        part, one = pl.ds(i * p_n, p_n), pl.ds(i, 1)
        k_first(i, x_fast.at[:, part], tail_ref.at[one], m16, m64, wfa, wlat, fa.at[part], lat.at[:, part],
                taps.at[:, part], st1, up.at[one], down.at[one], xs, fm, fv, lm, lv)

    each(0, STEPS, first)
    met()
    for k in (0, 1, 2):
        copies[k].start()
    exchange_run(exs[0], [gb], [c1, hp, hn], work[0])
    for k in (2, 3, 4):
        loads[k].wait()

    def store_sp(i):
        part = pl.ds(i * p_n, p_n)
        return pltpu.make_async_copy(sp.at[:, part], big[6].at[:, part], sp_sems.at[i])

    def join(i):
        part, one = pl.ds(i * p_n, p_n), pl.ds(i, 1)
        k_join(i, x_slow.at[:, part], lat.at[:, part], fa.at[part], hp.at[one], hn.at[one], c1, m16, m64, w_in, w_sc, wmid,
               lact.at[:, part], ftap.at[part], sa.at[:, part], sp.at[:, part], fb.at[part], work[1][0],
               am, av, pm, pv, bm, bv)
        store_sp(i).start()

    each(0, STEPS, join)
    for k in (3, 4, 5, 7):
        copies[k].start()
    exchange_run(exs[1], [gb], [c2], work[1])
    each(0, STEPS, lambda i: store_sp(i).wait())
    for k in (0, 1, 2, 3, 4, 5, 7):
        copies[k].wait()


def k_middle(exs, loads, met, loaded, small, kept, scratch, outs, work):
    sa, fb, wsp, wso, x_fast, cot = loaded
    gb, c2, m16, m64, wout = small
    pad, sb, fact, sact, fast_y, df = kept
    sm, sv, cm, cv, em, ev, s1, s2, sems, y_sems, df_sems = scratch
    big, (c3, c4, q4) = outs[:6], outs[6:]
    p_n = fb.shape[0] // STEPS
    rows_n = sb.shape[0] // STEPS
    copies = stores_of(list(zip(kept, big))[:4], sems)
    for k in (0, 1, 2):
        loads[k].wait()

    def spatial(i):
        part, span = pl.ds(i * p_n, p_n), pl.ds(i * rows_n, rows_n)
        k_spatial(i, sa, fb.at[part], c2, m16, m64, wsp, wout, pad, sb.at[span], fact.at[part], work[0][0], sm, sv, cm, cv)

    each(0, STEPS, spatial)
    met()
    for k in (0, 1, 2):
        copies[k].start()
    exchange_run(exs[0], [gb], [c3], work[0])
    for k in (3, 4, 5):
        loads[k].wait()

    def y_store(i):
        part = pl.ds(i * p_n, p_n)
        return pltpu.make_async_copy(fast_y.at[:, part], big[4].at[:, part], y_sems.at[i])

    def df_store(i):
        part = pl.ds(i * p_n, p_n)
        return pltpu.make_async_copy(df.at[part], big[5].at[part], df_sems.at[i])

    def expand(i):
        part, span = pl.ds(i * p_n, p_n), pl.ds(i * rows_n, rows_n)
        k_expand(i, sb.at[span], fact.at[part], x_fast.at[:, part], cot.at[:, part], c3, m16, m64, wso, wout,
                 sact.at[span], fast_y.at[:, part], df.at[part], work[1][0], em, ev, s1, s2)
        y_store(i).start()
        df_store(i).start()

    each(0, STEPS, expand)
    copies[3].start()
    exchange_run(exs[1], [gb, c3], [c4, q4], work[1])
    each(0, STEPS, lambda i: y_store(i).wait())
    each(0, STEPS, lambda i: df_store(i).wait())
    for copy in copies:
        copy.wait()


def back_norm(scale, p, q, dy, z, fill):
    return scale * dy - fill * (p + z * q)


def k_out(sact_ref, sp_ref, cot_ref, df_ref, fact_ref, fb_ref, c2_ref, c3_ref, c4_ref, q4_ref,
          m16_ref, m64_ref, wso_ref, wout_ref,
          out_ref, dy_ref, dfb_ref, gout_ref, up_ref, down_ref, st_ref, s1, s2, s3, t1, t2, gout):
    i = pl.program_id(0)
    s_n, p_n, t_n, _ = sact_ref.shape
    sact = flat(sact_ref[...])
    fill = m16_ref[0:1, :, 0:1]
    wide = 256
    for n in range(wso_ref.shape[1] // wide):
        cols = slice(n * wide, (n + 1) * wide)
        shape = (s_n * p_n, t_n, wide)
        sc = dot(sact, wso_ref[:, cols]).reshape(shape)
        sp = sp_ref[:, :, :, cols].reshape(shape)
        u6 = sc * rows(c4_ref, 2, 2 * n, 2) - rows(c4_ref, 3, 2 * n, 2)
        u7 = sp * rows(c2_ref, 2, 3 + 2 * n, 2) - rows(c2_ref, 3, 3 + 2 * n, 2)
        pre = (
            sc * rows(c4_ref, 0, 2 * n, 2)
            + sp * rows(c2_ref, 0, 3 + 2 * n, 2)
            + (rows(c4_ref, 1, 2 * n, 2) + rows(c2_ref, 1, 3 + 2 * n, 2))
        )
        g = sig(pre)
        y = pre * g
        out_ref[:, :, :, cols] = (y * fill).astype(BF16).reshape(s_n, p_n, t_n, wide)
        d = cot_ref[:, :, :, cols].reshape(shape).astype(F32) * fill * (g + y * (1.0 - g))
        dy_ref[:, :, :, cols] = d.reshape(s_n, p_n, t_n, wide)
        sum_add(i, d, s1, cols)
        sum_add(i, d * u6, s2, cols)
        sum_add(i, d * u7, s3, cols)

    f_n = fact_ref.shape[1]
    fact = flat(fact_ref[...])
    fc = dot(fact, wout_ref[...])
    fill4 = m64_ref[0:1]
    parts = []
    for s in range(s_n):
        cols = slice(s * LANES, (s + 1) * LANES)
        d = back_norm(
            rows(c3_ref, 0, s, 1), rows(q4_ref, 0, s, 1), rows(q4_ref, 1, s, 1),
            df_ref[:, :, cols], fc[:, cols].reshape(p_n, f_n, LANES), fill4,
        )
        parts.append(flat(d).astype(BF16))
    dfc = jnp.concatenate(parts, axis=1)
    add_to(i, gout, dot_tn(fact, dfc))
    z = fb_ref[...]
    back = dot_nt(dfc, wout_ref[...]).reshape(p_n, f_n, LANES) * slope(
        z * rows(c2_ref, 0, 0, 1) + rows(c2_ref, 1, 0, 1)
    )
    dfb_ref[...] = back
    sum_add(i, back, t1)
    sum_add(i, back * (z * rows(c2_ref, 2, 0, 1) - rows(c2_ref, 3, 0, 1)), t2)
    for k, value in enumerate((back, z)):
        value = flat(value)
        for p in range(p_n):
            down_ref[0, k, p : p + 1, :] = value[p * f_n : p * f_n + 1, :]
            up_ref[0, k, p : p + 1, :] = value[p * f_n + f_n - 1 : p * f_n + f_n, :]
        down_ref[0, k, p_n : p_n + 1, :] = m64_ref[0, 0:1, :]
        up_ref[0, k, p_n : p_n + 1, :] = m64_ref[0, f_n - 1 : f_n, :]

    @pl.when(i == STEPS - 1)
    def _():
        zero_ref(st_ref)
        put_rows(st_ref, 0, sum_end(s1))
        put_rows(st_ref, 8, sum_end(s2))
        put_rows(st_ref, 16, sum_end(s3))
        put_rows(st_ref, 24, sum_end(t1))
        put_rows(st_ref, 25, sum_end(t2))
        gout_ref[...] = fold_wide(gout, s_n)


def add_to(step, ref, value):
    ref[...] = jnp.where(step == 0, 0.0, ref[...]) + value


def fold_wide(ref, count):
    a = ref.shape[0] // count
    return sum(ref[s * a : (s + 1) * a, s * LANES : (s + 1) * LANES] for s in range(count))


def fold_lanes(value, count):
    a = value.shape[0] // count
    parts = [value[s * a : (s + 1) * a, :] for s in range(count)]
    return sum(p if s == 0 else pltpu.roll(p, LANES - s * a, 1) for s, p in enumerate(parts))


def k_back_out(x_ref, lact_ref, dy_ref, sp_ref, sact_ref, sb_ref, dfb_ref, fb_ref, fa_ref, ftap_ref, hp_ref, hn_ref,
               c1_ref, c2_ref, c3_ref, c4_ref, q5_ref, m16_ref, m64_ref, wso_ref, wback_ref,
               gw_ref, gs_ref, dsp_ref, dsb_ref, dfa_ref, gmid_ref, st_ref, s1, s2, t1, t2, gsc, gso, gmid):
    i = pl.program_id(0)
    s_n, p_n, t_n, c = sb_ref.shape
    sact = flat(sact_ref[...])
    fill = m16_ref[0:1, :, 0:1]
    wide = 256
    back = None
    turned = jnp.concatenate([flat(x_ref[...]), flat(lact_ref[...])], axis=1).T
    sact_turned = sact.T
    for n in range(wso_ref.shape[1] // wide):
        cols = slice(n * wide, (n + 1) * wide)
        shape = (s_n * p_n, t_n, wide)
        d = dy_ref[:, :, :, cols].reshape(shape)
        sc = dot(sact, wso_ref[:, cols]).reshape(shape)
        dsc = back_norm(rows(c4_ref, 0, 2 * n, 2), rows(q5_ref, 0, 2 * n, 2), rows(q5_ref, 1, 2 * n, 2), d, sc, fill)
        dsc = flat(dsc.astype(BF16))
        old = jnp.where(i == 0, 0.0, gso[:, cols])
        gso[:, cols] = old + dot(sact_turned, dsc)
        sp = sp_ref[:, :, :, cols].reshape(shape)
        dsp = back_norm(
            rows(c2_ref, 0, 3 + 2 * n, 2), rows(q5_ref, 0, 8 + 2 * n, 2), rows(q5_ref, 1, 8 + 2 * n, 2), d, sp, fill
        )
        dsp = flat(dsp.astype(BF16))
        dsp_ref[:, :, :, cols] = dsp.reshape(s_n, p_n, t_n, wide)
        old = jnp.where(i == 0, 0.0, gsc[:, cols])
        gsc[:, cols] = old + dot(turned, dsp)
        part = dot_nt(dsc, wso_ref[:, cols])
        back = part if back is None else back + part
    z = sb_ref[...].reshape(s_n * p_n, t_n, c)
    back = back.reshape(z.shape) * slope(z * rows(c3_ref, 0, 4, 2) + rows(c3_ref, 1, 4, 2))
    dsb_ref[...] = back.reshape(dsb_ref.shape)
    sum_add(i, back, s1)
    sum_add(i, back * (z * rows(c3_ref, 2, 4, 2) - rows(c3_ref, 3, 4, 2)), s2)

    f_n = fb_ref.shape[1]
    scale, p_row, q_row = rows(c2_ref, 0, 0, 1), rows(q5_ref, 0, 16, 1), rows(q5_ref, 1, 16, 1)
    dfb = back_norm(scale, p_row, q_row, dfb_ref[...], fb_ref[...], m64_ref[0:1])
    dfb_low = flat(dfb).astype(BF16)
    add_to(i, gmid, dot_tn(dfb_low, flat(ftap_ref[...])))
    own = dfb_low.astype(F32)
    ends = []
    for ref in (hp_ref, hn_ref):
        small = back_norm(scale, p_row, q_row, ref[0, 0], ref[0, 1], ref[0, 0, p_n : p_n + 1, :])
        small = small.astype(BF16).astype(F32)
        ends.append(
            jnp.concatenate(
                [jnp.broadcast_to(small[p : p + 1, :], (f_n, LANES)) for p in range(p_n)], axis=0
            ).reshape(p_n, f_n, LANES)
        )
    before, after = shifted(own, ends[0], ends[1], f_n)
    taps = jnp.concatenate(
        [flat(after * m64_ref[2:3]), own, flat(before * m64_ref[1:2])], axis=1
    ).astype(BF16)
    z = fa_ref[...]
    back = dot(taps, wback_ref[...]).reshape(z.shape) * slope(
        z * rows(c1_ref, 0, 0, 1) + rows(c1_ref, 1, 0, 1)
    )
    dfa_ref[...] = back
    sum_add(i, back, t1)
    sum_add(i, back * (z * rows(c1_ref, 2, 0, 1) - rows(c1_ref, 3, 0, 1)), t2)

    @pl.when(i == STEPS - 1)
    def _():
        zero_ref(st_ref)
        put_rows(st_ref, 0, sum_end(s1))
        put_rows(st_ref, 2, sum_end(s2))
        put_rows(st_ref, 4, sum_end(t1))
        put_rows(st_ref, 5, sum_end(t2))

    def late():
        for k in range(3):
            gmid_ref[k * 32 : (k + 1) * 32, :] = fold_lanes(gmid[:, k * LANES : (k + 1) * LANES], s_n)
        tall, low_tall = gsc.shape[0], gso.shape[0]
        blocks = gsc.shape[1] // wide
        for n in range(blocks):
            cols = slice(n * wide, (n + 1) * wide)
            gw_ref[n * tall : (n + 1) * tall, :] = gsc[:, cols].astype(BF16)
            gs_ref[n * low_tall : (n + 1) * low_tall, :] = gso[:, cols].astype(BF16)
        if blocks * tall < gw_ref.shape[0]:
            gw_ref[blocks * tall :, :] = jnp.zeros((gw_ref.shape[0] - blocks * tall, wide), BF16)

    return late


def k_slow_grad(x_ref, lact_ref, low_ref, dsp_ref, win_ref, wsc_ref, gx_ref, gw_ref, gsi):
    i = pl.program_id(0)
    s_n, p_n, t_n, c = low_ref.shape
    low, dsp = flat(low_ref[...]), flat(dsp_ref[...])
    turned = low.T
    blocks = gx_ref.shape[-1] // c
    for n in range(blocks + 1):
        part = slice(n * c, (n + 1) * c)
        joined = flat(x_ref[:, :, :, part] if n < blocks else lact_ref[...])
        gsi[:, part] = jnp.where(i == 0, 0.0, gsi[:, part]) + dot(turned, joined)
        if n < blocks:
            d = dot_nt(dsp, wsc_ref[part, :]) + dot_nt(low, win_ref[part, :])
            gx_ref[:, :, :, part] = d.astype(BF16).reshape(s_n, p_n, t_n, c)

    @pl.when(i == STEPS - 1)
    def _():
        for n in range(blocks + 1):
            part = slice(n * c, (n + 1) * c)
            gw_ref[part, :] = gsi[:, part].T.astype(BF16)


def k_fast_grad(dlat_ref, lat_ref, taps_ref, hn_ref, df_ref, dlow_ref, c1_ref, q8_ref, m16_ref, wlat_ref, wfa_ref,
                gx_ref, gw_ref, gs, glat):
    i = pl.program_id(0)
    s_n, p_n, t_n, c = lat_ref.shape
    shape = (s_n * p_n, t_n, c)
    scale, p_row, q_row = rows(c1_ref, 0, 1, 2), rows(q8_ref, 0, 0, 2), rows(q8_ref, 1, 0, 2)
    low = flat(
        back_norm(scale, p_row, q_row, dlat_ref[...].reshape(shape), lat_ref[...].reshape(shape), m16_ref[0:1, :, 0:1])
    ).astype(BF16)
    add_to(i, glat, dot_tn(low, flat(taps_ref[...])))

    @pl.when(i == STEPS - 1)
    def _():
        for k in range(glat.shape[1] // LANES):
            part = slice(k * LANES, (k + 1) * LANES)
            gw_ref[part, :] = glat[:, part].T.astype(BF16)

    small = hn_ref[0].astype(F32)
    ends = [
        jnp.broadcast_to(small[s * 8 + p : s * 8 + p + 1, :], (t_n, c)) for s in range(s_n) for p in range(p_n)
    ]
    ends = jnp.concatenate(ends, axis=0).reshape(shape)
    n = low.shape[0]
    moved = pltpu.roll(low.astype(F32), n - 1, 0).reshape(shape)
    place = lax.broadcasted_iota(jnp.int32, shape, 1)
    following = flat(jnp.where(place == t_n - 1, ends, moved) * m16_ref[2:3, :, 0:1]).astype(BF16)
    own = dot_nt(low, wlat_ref[2 * LANES : 5 * LANES, :])
    late = dot_nt(following, wlat_ref[0 : 2 * LANES, :])
    gs[pl.ds(0, n, stride=4), :] = own[:, 0:LANES]
    gs[pl.ds(1, n, stride=4), :] = own[:, LANES : 2 * LANES]
    gs[pl.ds(2, n, stride=4), :] = own[:, 2 * LANES :] + late[:, 0:LANES]
    gs[pl.ds(3, n, stride=4), :] = late[:, LANES:]
    back = dot(flat(dlow_ref[...]), wfa_ref[...])
    for s in range(s_n):
        cols = slice(s * LANES, (s + 1) * LANES)
        total = flat(df_ref[:, :, cols]) + back[:, cols] + gs[s * n : (s + 1) * n, :]
        gx_ref[s] = total.astype(BF16).reshape(gx_ref.shape[1:])


def each(first, last, body):
    def step(k, carry):
        body(k)
        return carry
    lax.fori_loop(first, last, step, 0)


NEAR = 4


class Cube:
    def __init__(self, ch, far):
        self.ch, self.far = ch, far
        self.p, self.f = lax.axis_index("path"), lax.axis_index("frames")
        self.q, self.r = lax.rem(self.f, NEAR), lax.div(self.f, NEAR)
        self.sibling = (1 - self.p, self.f)

    def q_of(self, k):
        low = (self.q % 2 + k % 2) % 2
        return (self.q // 2 + k // 2) % 2 * 2 + low

    def r_of(self, k):
        return lax.rem(self.r + k, self.far)

    def plane(self, k):
        return (self.p, self.r * NEAR + self.q_of(k))

    def line(self, k):
        return (self.p, self.r_of(k) * NEAR + self.q)

    def at(self, path, q, r):
        return pl.ds(pl.multiple_of(((path * NEAR + q) * self.far + r) * self.ch, 16), self.ch)


def remote(src, dst, sem, index, device):
    return pltpu.make_async_remote_copy(
        src_ref=src, dst_ref=dst, send_sem=sem.at[(0, *index)], recv_sem=sem.at[(1, *index)],
        device_id=device, device_id_type=MESH)


def rows_for(sizes, n):
    unit = 16 * sizes[0] * sizes[1]
    return -(-n // unit) * unit


class Stream:
    def __init__(self, sizes, rows_n, width):
        self.sizes, self.rows_n, self.width = sizes, rows_n, width
        self.far = sizes[1] // NEAR
        self.ch = rows_n // (sizes[0] * sizes[1])
        self.chunk = (self.ch, width)
        self.near_shape = (self.far, *self.chunk)
        quad = pltpu.VMEM((NEAR, *self.near_shape), BF16)
        quad_sems, line_sems = pltpu.SemaphoreType.DMA((2, NEAR, self.far)), pltpu.SemaphoreType.DMA((2, self.far))
        self.near_scratch = [quad, quad, quad, pltpu.VMEM(self.chunk, F32), quad_sems, quad_sems]
        self.line_scratch = [pltpu.VMEM(self.near_shape, BF16), pltpu.VMEM(self.chunk, F32), line_sems]
        self.share_scratch = [line_sems, quad_sems, quad_sems, pltpu.SemaphoreType.DMA]


class Near:
    def __init__(self, stream, x, out, scratch):
        self.x, self.out, self.far, self.c = x, out, stream.far, Cube(stream.ch, stream.far)
        self.land_a, self.buf_b, self.land_b, self.acc, self.sem_a, self.sem_b = scratch

    def pair(self, k, m):
        c = self.c
        return remote(self.x.at[c.at(1 - c.p, c.q_of(k), c.r_of(m + 1))], self.land_a.at[k, m], self.sem_a, (k, m), c.sibling)

    def plane(self, k, m):
        return remote(self.buf_b.at[k, m], self.land_b.at[k, m], self.sem_b, (k, m), self.c.plane(k))

    def start(self):
        def one(m):
            each(1, NEAR, lambda k: self.pair(k, m).start())
            self.pair(0, m).start()

        each(0, self.far, one)

    def add_pair(self, first, last):
        c = self.c

        def one(k, m):
            self.pair(k, m).wait_recv()
            mine = self.x[c.at(c.p, c.q_of(k), c.r_of(m + 1)), :]
            self.buf_b[k, m] = (mine.astype(F32) + self.land_a[k, m].astype(F32)).astype(BF16)
            self.plane(k, m).start()

        each(first, last, lambda m: each(1, NEAR, lambda k: one(k, m)))

    def add_plane(self, first, last, then=None):
        c = self.c

        def one(m):
            self.pair(0, m).wait_recv()
            self.acc[...] = self.x[c.at(c.p, c.q, c.r_of(m + 1)), :].astype(F32) + self.land_a[0, m].astype(F32)

            def more(k):
                self.plane(k, m).wait_recv()
                self.acc[...] += self.land_b[k, m].astype(F32)

            each(1, NEAR, more)
            self.out[m] = self.acc[...].astype(BF16)
            if then is not None:
                then(m)

        each(first, last, one)

    def end(self):
        each(0, self.far, lambda m: each(0, NEAR, lambda k: self.pair(k, m).wait_send()))
        each(0, self.far, lambda m: each(1, NEAR, lambda k: self.plane(k, m).wait_send()))


class Line:
    def __init__(self, stream, near, scratch):
        self.near, self.far, self.c = near, stream.far, Cube(stream.ch, stream.far)
        self.land, self.acc, self.sem = scratch

    def line(self, m):
        return remote(self.near.at[m], self.land.at[m], self.sem, (m,), self.c.line(m + 1))

    def start(self, first, last):
        each(first, min(last, self.far - 1), lambda m: self.line(m).start())

    def total(self):
        self.acc[...] = self.near[self.far - 1].astype(F32)

        def one(m):
            self.line(m).wait_recv()
            self.acc[...] += self.land[m].astype(F32)

        each(0, self.far - 1, one)
        return self.acc[...].astype(BF16)

    def end(self):
        each(0, self.far - 1, lambda m: self.line(m).wait_send())


class Share:
    def __init__(self, stream, res, out, scratch):
        self.res, self.out, self.far, self.c = res, out, stream.far, Cube(stream.ch, stream.far)
        self.cut = stream.ch // 32 * 16
        self.sem_d, self.sem_e, self.sem_f, self.sem_own = scratch

    def own(self):
        return self.out.at[self.c.at(self.c.p, self.c.q, self.c.r)]

    def keep(self):
        return pltpu.make_async_copy(self.res, self.own(), self.sem_own)

    def line_back(self, k):
        return remote(self.res, self.own(), self.sem_d, (k,), self.c.line(k))

    def part(self, q, m):
        return self.out.at[self.c.at(self.c.p, q, self.c.r_of(self.far - m))]

    def plane_back(self, k, m, src=None):
        dst = self.part(self.c.q, m)
        return remote(dst if src is None else src, dst, self.sem_e, (k, m), self.c.plane(k))

    def pair_back(self, k, m, src=None):
        dst = self.part(self.c.q_of(k), m)
        return remote(dst if src is None else src, dst, self.sem_f, (k, m), self.c.sibling)

    def start_line(self):
        each(1, self.far, lambda k: self.line_back(k).start())

    def half(self, k, m):
        c, cut = self.c, self.cut
        start = ((c.p * NEAR + c.q_of(k)) * self.far + c.r_of(self.far - m)) * c.ch
        rows_n = cut if k == 1 else c.ch - cut
        part = self.out.at[pl.ds(pl.multiple_of(start + (0 if k == 1 else cut), 16), rows_n)]
        return remote(part, part, self.sem_e, (3 if k == 1 else 0, m), c.plane(3 - k))

    def start_plane(self):
        each(1, NEAR - 1, lambda k: self.plane_back(k, 0, self.res).start())
        self.pair_back(0, 0, self.res).start()
        self.keep().start()

    def relay(self, first, last):
        def one(m):
            self.line_back(m).wait_recv()
            each(1, NEAR - 1, lambda k: self.plane_back(k, m).start())
            self.pair_back(0, m).start()

        each(first, last, one)

    def hand_on(self, first, last):
        def one(m):
            for k in (1, 2):
                self.plane_back(k, m).wait_recv()
                self.half(k, m).start()
                self.pair_back(k, m).start()

        each(first, last, one)

    def hand_across(self, first, last):
        def one(m):
            for k in (1, 2):
                self.half(k, m).wait_recv()
            self.pair_back(3, m).start()

        each(first, last, one)

    def end(self):
        each(0, self.far, lambda m: each(0, NEAR, lambda k: self.pair_back(k, m).wait()))
        self.keep().wait()
        each(1, self.far, lambda k: self.line_back(k).wait_send())
        each(0, self.far, lambda m: each(1, NEAR - 1, lambda k: self.plane_back(k, m).wait_send()))

        def sent(m):
            for k in (1, 2):
                self.half(k, m).wait_send()

        each(0, self.far, sent)


def k_tail(cfg, *refs):
    st_a, st_b, ex7, ex8, side = cfg
    it = iter(refs)

    def take(n):
        return [next(it) for _ in range(n)]

    hbm = take(13)
    gb, c1, c2, c3, q6, m16, m64, g_fout, g_fmid = take(9)
    low_out, dlow_out, dlat_out, gf, q7, q8, hn, res_a, near_b = take(9)
    local = take(13)
    gw_a, dsb, sb, spad, wsp, sa, x_fast, dfa, fa, w_in, w_sc, dsp, lat = local
    pad, gsp, gin, low, dlow, gw_b, near_a, ends, s1, s2, t1, t2, sems, out_sems = take(14)
    near1, line1, near2 = take(len(st_a.near_scratch)), take(len(st_a.line_scratch)), take(len(st_b.near_scratch))
    scr7 = take(len(ex7.local) + len(ex7.work))
    scr8 = take(len(ex8.local) + len(ex8.work))
    n_in = w_in.shape[0]
    srcs = list(hbm)
    for k in (9, 10):
        srcs[k] = hbm[k].at[pl.ds(hbm[k].shape[0] - n_in, n_in)]
    loads = [pltpu.make_async_copy(src, dst, sems.at[k]) for k, (src, dst) in enumerate(zip(srcs, local))]
    count = exchange_hello(ex8)
    for load in loads:
        load.start()
    near = Near(st_a, gw_a, near_a, near1)
    line = Line(st_a, near_a, line1)
    near_two = Near(st_b, gw_b, near_b, near2)
    far = st_a.far
    t_n, c = pad.shape[2], pad.shape[3]
    wide = side * t_n
    per = side // STEPS
    fill = m16[0:1, :, 0:1]

    def waits(*names):
        for k in names:
            loads[k].wait()

    waits(1, 2)
    scale, p_row, q_row = rows(c3, 0, 4, 2), rows(q6, 0, 0, 2), rows(q6, 1, 0, 2)
    zero_ref(pad)

    def fill_pad(h):
        part = pl.ds(h * wide, wide)
        d = back_norm(
            scale, p_row, q_row, dsb[part].reshape(side, t_n, c), sb[part].reshape(side, t_n, c), fill
        )
        pad[h + 1, 1 : side + 1] = d.astype(BF16)

    each(0, side, fill_pad)
    waits(0)
    pl.semaphore_wait(pltpu.get_barrier_semaphore(), count)
    near.start()
    waits(3, 4, 5, 6, 7, 8)
    f_n = x_fast.shape[2]
    p_n = x_fast.shape[1] // STEPS

    def spatial(i):
        h0 = i * per
        turned = flat(pad[pl.ds(h0 + 1, per), 1 : side + 1]).T
        acc = None
        for a in range(3):
            for b in range(3):
                k = 3 * a + b
                patch = flat(spad[pl.ds(h0 + a, per), b : b + side])
                cols = slice(k * c, (k + 1) * c)
                gsp[:, cols] = jnp.where(i == 0, 0.0, gsp[:, cols]) + dot(turned, patch)
                block = pad[pl.ds(h0 + 2 - a, per), 2 - b : 2 - b + side]
                part = dot_nt(flat(block), wsp[k])
                acc = part if acc is None else acc + part
        span = pl.ds(i * per * wide, per * wide)
        z = sa[span]
        back = acc * slope(z * rows(c2, 0, 1, 2) + rows(c2, 1, 1, 2))
        dsb[span] = back
        unit = z * rows(c2, 2, 1, 2) - rows(c2, 3, 1, 2)
        sum_add(i, back.reshape(per * side, t_n, c), s1)
        sum_add(i, (back * unit).reshape(per * side, t_n, c), s2)
        f_span = pl.ds(i * p_n, p_n)
        small = back_norm(
            rows(c1, 0, 0, 1), rows(q6, 0, 2, 1), rows(q6, 1, 2, 1), dfa[f_span], fa[f_span], m64[0:1]
        ).astype(BF16)
        dlow[f_span] = small
        packed = jnp.concatenate([flat(x_fast[s, f_span]) for s in range(x_fast.shape[0])], axis=1)
        add_to(i, gin, dot_tn(flat(small), packed))
        pl.when(i == 0)(lambda: near.add_pair(0, far // 2))
        pl.when(i == 1)(lambda: near.add_pair(far // 2, far))

    each(0, STEPS, spatial)
    stats = scr7[0]
    zero_ref(stats)
    put_rows(stats, 0, sum_end(s1))
    put_rows(stats, 2, sum_end(s2))
    stores = [pltpu.make_async_copy(dlow, dlow_out, out_sems.at[0])]
    stores[0].start()

    def late():
        for k in range(9):
            gw_b[k * c : (k + 1) * c, :] = gsp[:, k * c : (k + 1) * c].T.astype(BF16)
        if 9 * c < gw_b.shape[0]:
            gw_b[9 * c :, :] = jnp.zeros((gw_b.shape[0] - 9 * c, c), BF16)
        n = g_fout.shape[0]
        gf[0:n, 0:LANES] = fold_wide(gin, x_fast.shape[0])
        gf[0:n, LANES:] = g_fout[...]
        gf[n : 2 * n, 0:LANES] = g_fmid[0:n, :]
        gf[n : 2 * n, LANES:] = g_fmid[n : 2 * n, :]
        gf[2 * n :, 0:LANES] = g_fmid[2 * n :, :]
        gf[2 * n :, LANES:] = jnp.zeros((n, LANES), F32)

    exchange_run(ex7, [gb, c2], [q7], scr7, late)
    near_two.start()
    near.add_plane(0, far - 1, lambda m: line.line(m).start())
    near.add_plane(far - 1, far)
    waits(9, 10, 11, 12)
    scale7, p7, q7_row = rows(c2, 0, 1, 2), rows(q7, 0, 0, 2), rows(q7, 1, 0, 2)
    block = per * wide

    def join(i):
        span = pl.ds(i * block, block)
        shape = (per * side, t_n, c)
        d = back_norm(scale7, p7, q7_row, dsb[span].reshape(shape), sa[span].reshape(shape), fill)
        small = flat(d).astype(BF16)
        low[span] = small
        d = dot_nt(dsp[span], w_sc[...]) + dot_nt(small, w_in[...])
        z = lat[span]
        back = d * slope(z * rows(c1, 0, 1, 2) + rows(c1, 1, 1, 2))
        sb[span] = back
        unit = z * rows(c1, 2, 1, 2) - rows(c1, 3, 1, 2)
        sum_add(i, back.reshape(shape), t1)
        sum_add(i, (back * unit).reshape(shape), t2)
        pl.when(i == 2)(lambda: near_two.add_pair(0, far))

    each(0, STEPS, join)
    stores.append(pltpu.make_async_copy(low, low_out, out_sems.at[1]))
    stores.append(pltpu.make_async_copy(sb, dlat_out, out_sems.at[2]))
    stores[1].start()
    stores[2].start()
    stats = scr8[0]
    zero_ref(stats)
    put_rows(stats, 0, sum_end(t1))
    put_rows(stats, 2, sum_end(t2))

    def post(q, sent):
        zero_ref(ends)
        for s in range(x_fast.shape[0]):
            for step in range(STEPS):
                for p in range(p_n):
                    at = ((s * STEPS + step) * p_n + p) * t_n
                    ends[0, step, s * 8 + p : s * 8 + p + 1, :] = sb[at : at + 1, :]
                    ends[1, step, s * 8 + p : s * 8 + p + 1, :] = lat[at : at + 1, :]
        d = back_norm(rows(c1, 0, 1, 2), rows(q, 0, 0, 2), rows(q, 1, 0, 2), ends[0], ends[1], m16[0, 0:1, 0:1])
        sent[...] = d.astype(BF16)

    exchange_run(ex8, [gb, c1], [q8, hn], scr8, None, post)
    res_a[...] = line.total()
    near_two.add_plane(0, far)
    for store in stores:
        store.wait()
    line.end()
    near.end()
    near_two.end()


def back_tail(st_a, st_b, ex7, ex8, hbm, small, side, t_n, c):
    vm, anywhere = pl.BlockSpec(memory_space=pltpu.VMEM), pl.BlockSpec(memory_space=pl.ANY)
    inner, f_n = hbm[7].shape[:2]
    n = side * side * t_n
    outs = [((n, c), BF16), ((inner, f_n, LANES), BF16), ((n, c), F32), (small[-1].shape[0:1] + (2 * LANES,), F32),
            *ex7.outs, *ex8.outs, (st_a.chunk, BF16), (st_b.near_shape, BF16)]
    local = [pltpu.VMEM((c,) + a.shape[1:] if k in (9, 10) else a.shape, a.dtype) for k, a in enumerate(hbm)]
    width = hbm[6].shape[0] * hbm[6].shape[3]
    scratch = [
        pltpu.VMEM((side + 2, side + 2, t_n, c), BF16), pltpu.VMEM((c, 9 * c), F32), pltpu.VMEM((LANES, width), F32),
        pltpu.VMEM((n, c), BF16), pltpu.VMEM((inner, f_n, LANES), BF16), pltpu.VMEM((st_b.rows_n, c), BF16),
        pltpu.VMEM(st_a.near_shape, BF16), pltpu.VMEM((2, *ex8.post), F32), *[pltpu.VMEM((t_n, c), F32)] * 4,
        pltpu.SemaphoreType.DMA((len(hbm),)), pltpu.SemaphoreType.DMA((3,)),
        *st_a.near_scratch, *st_a.line_scratch, *st_b.near_scratch, *ex7.local, *ex7.work, *ex8.local, *ex8.work,
    ]
    return pl.pallas_call(
        functools.partial(k_tail, (st_a, st_b, ex7, ex8, side)),
        out_shape=[jax.ShapeDtypeStruct(s, d) for s, d in outs],
        in_specs=[anywhere] * len(hbm) + [vm] * len(small),
        out_specs=[anywhere] * 3 + [vm] * (len(outs) - 3),
        scratch_shapes=[*local, *scratch],
        compiler_params=pltpu.CompilerParams(collective_id=ex8.cid, has_side_effects=True, vmem_limit_bytes=VMEM_LIMIT),
        name="tail",
    )(*hbm, *small)


def final_kernel(cfg, *refs):
    first, second, third, both, offsets, heights = cfg
    n = len(offsets)
    (res_a, near_b), ins, (out_a, out_bc), refs = refs[:2], refs[2 : 2 + n], refs[2 + n : 4 + n], refs[4 + n :]
    x, near_c, res = refs[:3]
    at = [3]

    def take(scratch):
        at[0] += len(scratch)
        return refs[at[0] - len(scratch) : at[0]]

    far = first.far
    share_a = Share(first, res_a, out_a, take(first.share_scratch))
    line_b = Line(second, near_b, take(second.line_scratch))
    near = Near(third, x, near_c, take(third.near_scratch))
    line_c = Line(third, near_c, take(third.line_scratch))
    share = Share(both, res, out_bc, take(both.share_scratch))

    c = near.c
    barrier = pltpu.get_barrier_semaphore()

    def greet(device):
        pl.semaphore_signal(barrier, inc=1, device_id=device, device_id_type=MESH)

    greet(c.sibling)
    each(1, NEAR, lambda k: greet(c.plane(k)))
    each(1, far, lambda k: greet(c.line(k)))
    end = 0
    for ref, off, height in zip(ins, offsets, heights):
        x[off : off + height, :] = ref[...].astype(BF16)
        end = off + height
    if end < x.shape[0]:
        x[end:, :] = jnp.zeros((x.shape[0] - end, x.shape[1]), BF16)
    pl.semaphore_wait(barrier, NEAR + far - 1)

    near.start()
    line_b.start(0, far)
    share_a.start_line()
    near.add_pair(0, far)
    share_a.start_plane()
    res[0 : second.ch, :] = line_b.total()
    near.add_plane(0, far - 1, lambda m: line_c.line(m).start())
    near.add_plane(far - 1, far)
    share_a.relay(1, far)
    res[second.ch :, :] = line_c.total()
    share.start_line()
    share.start_plane()
    share_a.hand_on(0, far)
    share.relay(1, far)
    share_a.hand_across(0, far)
    share.hand_on(0, far)
    share.hand_across(0, far)
    share_a.end()
    share.end()
    line_b.end()
    line_c.end()
    near.end()


def final_sum(sizes, cid, first, second, res_a, near_b, parts):
    width = res_a.shape[1]
    heights = tuple(p.shape[0] for p in parts)
    offsets = tuple(sum(heights[:k]) for k in range(len(parts)))
    third = Stream(sizes, rows_for(sizes, sum(heights)), width)
    both = Stream(sizes, second.rows_n + third.rows_n, width)
    vm, hbm = pl.BlockSpec(memory_space=pltpu.VMEM), pl.BlockSpec(memory_space=pl.ANY)
    out_a, out_bc = pl.pallas_call(
        functools.partial(final_kernel, (first, second, third, both, offsets, heights)),
        out_shape=[jax.ShapeDtypeStruct((s.rows_n, width), BF16) for s in (first, both)],
        in_specs=[vm] * (2 + len(parts)),
        out_specs=[hbm] * 2,
        scratch_shapes=[
            pltpu.VMEM((third.rows_n, width), BF16), pltpu.VMEM(third.near_shape, BF16), pltpu.VMEM(both.chunk, BF16),
            *first.share_scratch, *second.line_scratch, *third.near_scratch, *third.line_scratch, *both.share_scratch,
        ],
        compiler_params=pltpu.CompilerParams(collective_id=cid, has_side_effects=True, vmem_limit_bytes=VMEM_LIMIT),
        name="final_sum",
    )(res_a, near_b, *parts)
    return out_a, out_bc.reshape(-1, both.ch, width), third


def k_unpack(pieces, cut, *refs):
    (src_a, src_b, q4, q5, q6, q7, q8), refs = refs[:7], refs[7:]
    outs, (low_a, low_b, low_c, wide, line, sem_a, sem_b, sem_out) = refs[:-8], refs[-8:]
    outs, (gains_out, biases_out, in_out, mid_out, out_out) = outs[:-5], outs[-5:]
    lows = (low_a, low_b, low_c)
    flats = [low_a, low_b.reshape(-1, low_b.shape[-1]), low_c.reshape(-1, low_c.shape[-1])]
    starts = [sum(p[2] for p in pieces[:k]) for k in range(len(pieces))]

    def fetch_a(k):
        _, row, height, _, _ = pieces[k]
        return pltpu.make_async_copy(src_a.at[pl.ds(row, height)], low_a.at[pl.ds(row, height)], sem_a.at[k])

    def fetch_b(k):
        part = src_b.at[:, pl.ds(0, cut)] if k == 1 else src_b.at[:, pl.ds(cut, src_b.shape[1] - cut)]
        return pltpu.make_async_copy(part, lows[k], sem_b.at[k])

    def store(k):
        _, _, height, out, col = pieces[k]
        part = outs[out] if col is None else outs[out].at[:, pl.ds(col, wide.shape[1])]
        return pltpu.make_async_copy(wide.at[pl.ds(starts[k], height)], part, sem_out.at[k])

    for k, piece in enumerate(pieces):
        if piece[0] == 0:
            fetch_a(k).start()
    for k in (1, 2):
        fetch_b(k).start()
    seen = 0
    for k, (src, row, height, _, _) in enumerate(pieces):
        if src == 0:
            fetch_a(k).wait()
        elif src != seen:
            fetch_b(src).wait()
            seen = src
        wide[starts[k] : starts[k] + height, :] = flats[src][row : row + height, :].astype(F32)
        store(k).start()
    lane = lax.broadcasted_iota(jnp.int32, (1, LANES), 1)
    left = lane < LANES // 2
    for slab, out in ((3, gains_out), (2, biases_out)):
        at = 0
        for q, first, count in ((q4, 0, 1), (q8, 0, 2), (q7, 0, 2), (q6, 0, 2), (q5, 0, 16)):
            line[at : at + count, :] = q[slab, first : first + count, :]
            at += count
        half = pltpu.roll(line[0:at, :], LANES // 2, 1)
        head = jnp.where(lane < LANES // 4, q6[slab, 2:3, :], q5[slab, 16:17, :])
        out[0:1, :] = jnp.where(left, head, half[0:1])
        out[1:at, :] = jnp.where(left, half[0 : at - 1], half[1:at])
        out[at : at + 1, :] = jnp.where(left, half[at - 1 : at], 0.0)
    a = in_out.shape[0]
    last = sum(p[2] for p in pieces if p[0] == 2)
    small = flats[2][last : last + 3 * a, :]
    in_out[...] = small[0:a, 0:LANES].astype(F32)
    out_out[...] = small[0:a, LANES:].astype(F32)
    eye = (lax.broadcasted_iota(jnp.int32, (a, a), 0) == lax.broadcasted_iota(jnp.int32, (a, a), 1)).astype(BF16)
    for k, (row, col) in enumerate(((a, 0), (a, LANES), (2 * a, 0))):
        mid_out[k] = dot_tn(small[row : row + a, col : col + LANES], eye)[0:a, :]
    for k in range(len(pieces)):
        store(k).wait()


def unpack(src_a, src_b, cut, pieces, shapes, small_shapes, norm_sums):
    hbm, vm = pl.BlockSpec(memory_space=pl.ANY), pl.BlockSpec(memory_space=pltpu.VMEM)
    n, _, width = src_b.shape
    return pl.pallas_call(
        functools.partial(k_unpack, pieces, cut),
        out_shape=[jax.ShapeDtypeStruct(s, F32) for s in (*shapes, *small_shapes)],
        in_specs=[hbm] * 2 + [vm] * len(norm_sums),
        out_specs=[hbm] * len(shapes) + [vm] * len(small_shapes),
        scratch_shapes=[
            pltpu.VMEM(src_a.shape, BF16),
            pltpu.VMEM((n, cut, width), BF16),
            pltpu.VMEM((n, src_b.shape[1] - cut, width), BF16),
            pltpu.VMEM((sum(p[2] for p in pieces), width), F32),
            pltpu.VMEM((24, LANES), F32),
            pltpu.SemaphoreType.DMA((len(pieces),)),
            pltpu.SemaphoreType.DMA((3,)),
            pltpu.SemaphoreType.DMA((len(pieces),)),
        ],
        compiler_params=pltpu.CompilerParams(vmem_limit_bytes=VMEM_LIMIT),
        name="unpack",
    )(src_a, src_b, *norm_sums)


def k_prep(x_hbm, fill_ref, clip_ref, norm_ref, wfi_ref, wfm_ref, wfo_ref,
           tail_ref, gb_ref, m16_ref, m64_ref, wfa_ref, wmid_ref, wback_ref, wout_ref,
           near, rows_f, sent, land, sems, local):
    length = lax.axis_size("frames")
    total = lax.axis_size("path") * length
    me = lax.axis_index("path") * length + lax.axis_index("frames")

    def place(index):
        return (lax.div(index, length), lax.rem(index, length))

    nxt, prv = place(lax.rem(me + 1, total)), place(lax.rem(me + total - 1, total))
    barrier = pltpu.get_barrier_semaphore()
    pl.semaphore_signal(barrier, inc=1, device_id=nxt, device_id_type=MESH)
    pl.semaphore_signal(barrier, inc=1, device_id=prv, device_id_type=MESH)
    s_n, inner, t_n, c = near.shape
    f_n = x_hbm.shape[2]
    fetch = pltpu.make_async_copy(x_hbm.at[:, :, pl.ds(f_n - t_n, t_n), :], near, local)
    fetch.start()
    fetch.wait()
    p_n = inner // STEPS
    rows_f[...] = near[...].reshape(rows_f.shape).astype(F32)
    zero_ref(sent)
    count = s_n * inner
    for k in range(2):
        line = rows_f[pl.ds(t_n - 2 + k, count, stride=t_n), :]
        for s in range(s_n):
            for step in range(STEPS):
                at = s * inner + step * p_n
                sent[step, s, 0:p_n, k * c : (k + 1) * c] = line[at : at + p_n, :]
    pl.semaphore_wait(barrier, 2)
    copy = pltpu.make_async_remote_copy(
        src_ref=sent, dst_ref=land, send_sem=sems.at[0], recv_sem=sems.at[1], device_id=nxt, device_id_type=MESH
    )
    copy.start()

    lane = lax.broadcasted_iota(jnp.int32, (1, LANES), 1)
    for k in range(2):
        half = pltpu.roll(norm_ref[k], LANES // 2, 1)
        main = jnp.where(lane < LANES // 2, half[0:23], half[1:24])
        for j in range(2):
            v = jnp.where(lane // 32 == j, norm_ref[k, 0:1, :], 0.0)
            v = v + pltpu.roll(v, 64, 1)
            gb_ref[k, j : j + 1, :] = v + pltpu.roll(v, 32, 1)
        for j in range(4):
            gb_ref[k, 2 + j : 3 + j, :] = main[0:1]
        gb_ref[k, 6:28, :] = main[1:23]
        gb_ref[k, 28:32, :] = jnp.zeros((4, LANES), F32)

    def row(value):
        return jnp.full((1, LANES), value, F32)

    last = jnp.where(me < total - 1, 1.0, 0.0)
    link = [jnp.where(clip_ref[t] >= 1, 1.0, 0.0) for t in range(t_n)]
    for t in range(t_n):
        filled = row(fill_ref[t].astype(F32))
        after = row(link[t + 1] if t + 1 < t_n else last)
        m16_ref[0, t : t + 1, :] = filled
        m16_ref[1, t : t + 1, :] = row(link[t])
        m16_ref[2, t : t + 1, :] = after
        m64_ref[0, 4 * t : 4 * t + 4, :] = jnp.broadcast_to(filled, (4, LANES))
        m64_ref[1, 4 * t : 4 * t + 1, :] = row(link[t])
        m64_ref[1, 4 * t + 1 : 4 * t + 4, :] = jnp.ones((3, LANES), F32)
        m64_ref[2, 4 * t : 4 * t + 3, :] = jnp.ones((3, LANES), F32)
        m64_ref[2, 4 * t + 3 : 4 * t + 4, :] = after

    zero_ref(wfa_ref)
    zero_ref(wout_ref)
    a = wfi_ref.shape[0]
    for s in range(s_n):
        wfa_ref[s * a : (s + 1) * a, s * LANES : (s + 1) * LANES] = wfi_ref[...]
        wout_ref[s * a : (s + 1) * a, s * LANES : (s + 1) * LANES] = wfo_ref[...]
    tall = (LANES, a)
    spread = (lax.broadcasted_iota(jnp.int32, tall, 0) % a == lax.broadcasted_iota(jnp.int32, tall, 1)).astype(BF16)
    square = (LANES, LANES)
    diag = lax.broadcasted_iota(jnp.int32, square, 0) // a == lax.broadcasted_iota(jnp.int32, square, 1) // a
    for k in range(3):
        left = dot(spread, wfm_ref[k]).astype(BF16)
        wmid_ref[k * LANES : (k + 1) * LANES, :] = jnp.where(diag, dot_nt(left, spread), 0.0).astype(BF16)
        right = dot_nt(spread, wfm_ref[k]).astype(BF16)
        wback_ref[k * LANES : (k + 1) * LANES, :] = jnp.where(diag, dot_nt(right, spread), 0.0).astype(BF16)
    copy.wait()
    tail_ref[...] = land[...]


def prepare(x_fast, fill, clip_offset, norms, w_fast_in, w_fast_mid, w_fast_out):
    s_n, inner, f_n, c = x_fast.shape
    t_n = fill.shape[0]
    p_n = inner // STEPS
    vm = pl.BlockSpec(memory_space=pltpu.VMEM)
    sm = pl.BlockSpec(memory_space=pltpu.SMEM)
    tail = (STEPS, s_n, 8, 2 * c)
    outs = [(tail, F32), ((2, 32, LANES), F32), ((3, t_n, LANES), F32), ((3, f_n, LANES), F32),
            ((LANES, s_n * c), BF16), ((3 * LANES, LANES), BF16), ((3 * LANES, LANES), BF16), ((LANES, s_n * c), BF16)]
    return pl.pallas_call(
        k_prep,
        out_shape=[jax.ShapeDtypeStruct(s, d) for s, d in outs],
        in_specs=[pl.BlockSpec(memory_space=pl.ANY), sm, sm, vm, vm, vm, vm],
        out_specs=[vm] * len(outs),
        scratch_shapes=[
            pltpu.VMEM((s_n, inner, t_n, c), BF16),
            pltpu.VMEM((s_n * inner * t_n, c), F32),
            pltpu.VMEM(tail, F32),
            pltpu.VMEM(tail, F32),
            pltpu.SemaphoreType.DMA((2,)),
            pltpu.SemaphoreType.DMA,
        ],
        compiler_params=pltpu.CompilerParams(collective_id=10, has_side_effects=True, vmem_limit_bytes=VMEM_LIMIT),
        name="prepare",
    )(x_fast, fill, clip_offset, norms, w_fast_in.T, w_fast_mid, w_fast_out)


def per_device(slow_input, fast_input, clip_offset, fill, w_fast_in, w_fast_mid, w_fast_out, w_lateral,
               w_slow_in, w_slow_mid, w_slow_out, w_shortcut, gains, biases, slow_cot, fast_cot):
    sizes = (lax.axis_size("path"), lax.axis_size("frames"))
    t_n, side, _, c_slow = slow_input.shape
    f_n, c_fast = fast_input.shape[0], fast_input.shape[3]
    in_fast, in_slow, c_lat = w_fast_in.shape[1], w_slow_in.shape[1], w_lateral.shape[2]
    pixels = side * side
    groups = LANES // in_fast
    inner = pixels // groups
    p_n = inner // STEPS

    def slow_view(a):
        return jnp.transpose(a, (1, 2, 0, 3)).reshape(groups, inner, t_n, a.shape[3])

    def fast_view(a):
        return jnp.transpose(a, (1, 2, 0, 3)).reshape(groups, inner, f_n, a.shape[3])

    def unview(a):
        return jnp.transpose(a.reshape(side, side, a.shape[2], a.shape[3]), (2, 0, 1, 3))

    x_slow, cot_slow = slow_view(slow_input), slow_view(slow_cot)
    x_fast, cot_fast = fast_view(fast_input), fast_view(fast_cot)

    norms = jnp.stack([gains, biases])
    norms = jnp.pad(norms, ((0, 0), (0, -norms.shape[1] % (8 * LANES)))).reshape(2, -1, LANES)
    tail, gb, m16, m64, wfa, wmid, wback, wout = prepare(
        x_fast, fill, clip_offset, norms, w_fast_in, w_fast_mid, w_fast_out
    )
    wlat = w_lateral.reshape(-1, c_lat)
    wsp = w_slow_mid.reshape(9, in_slow, in_slow)

    sl = (groups, inner, t_n)
    fp = (inner, f_n)

    def slow_out(width, dtype):
        return out_blocked(sl + (width,), dtype, 1, p_n)

    def fast_out(width, dtype):
        return out_blocked(fp + (width,), dtype, 0, p_n)

    def sb_(a):
        return blocked(a, 1, p_n)

    def fb_(a):
        return blocked(a, 0, p_n)

    def stat(n):
        return out_whole((pad8(n), LANES), F32)

    def acc(rows_n, width, count):
        return [pltpu.VMEM((rows_n, width), F32)] * count

    small = (STEPS, 8, LANES)

    sems7 = pltpu.SemaphoreType.DMA((STEPS,))
    exs = [
        Exchange(sizes, 1, 7, fwd=(("lane4", 0, 1), ("plain", 6, 2)), up=small, down=small),
        Exchange(sizes, 1, 23, fwd=(("lane4", 1, 1), ("plain", 8, 2), ("plain", 20, 8))),
    ]
    kept = [
        (fp + (LANES,), F32), (sl + (c_lat,), F32), (sl + (5 * c_fast,), BF16), (sl + (c_lat,), BF16),
        (fp + (3 * LANES,), BF16), (sl + (in_slow,), F32), (sl + (c_slow,), F32), (fp + (LANES,), F32),
    ]
    fa, lat, taps, lact, ftap, sa, sp, fb, c1, hp, hn, c2 = run_resident(
        functools.partial(k_front, exs), exs,
        [x_fast, wlat, x_slow, w_slow_in, w_shortcut], [tail, gb, m16, m64, wfa, wmid],
        kept, [(*k, True) for k in kept],
        [pltpu.VMEM((groups * p_n * f_n, c_fast), F32), *acc(f_n, LANES, 2), *acc(t_n, c_lat, 2), *acc(t_n, in_slow, 2),
         *acc(t_n, c_slow, 2), *acc(f_n, LANES, 2), pltpu.SemaphoreType.DMA((8,)), sems7],
        "front",
    )

    exs = [
        Exchange(sizes, 3, 13, fwd=(("row4", 2, 4), ("plain", 10, 2))),
        Exchange(sizes, 3, 25, fwd=(("plain", 12, 8),), bwd=(("row4", 0, 0, 2, 4, 0, 4),)),
    ]
    kept = [
        ((side + 2, side + 2, t_n, in_slow), BF16), ((pixels, t_n, in_slow), F32), (fp + (LANES,), BF16),
        ((pixels, t_n, in_slow), BF16), ((groups, inner, f_n, c_fast), BF16), (fp + (groups * c_fast,), F32),
    ]
    pad, sb, fact, sact, fast_y, df, c3, c4, q4 = run_resident(
        functools.partial(k_middle, exs), exs,
        [sa.reshape(side, side, t_n, in_slow), fb, wsp, w_slow_out, x_fast, cot_fast], [gb, c2, m16, m64, wout],
        kept, [(*k, True) for k in kept],
        [*acc(t_n, in_slow, 2), *acc(f_n, groups * c_fast, 2), *acc(t_n, c_slow, 2), *acc(f_n, groups * c_fast, 2),
         pltpu.SemaphoreType.DMA((4,)), sems7, sems7],
        "middle",
    )
    sb4, sact = sb.reshape(sl + (in_slow,)), sact.reshape(sl + (in_slow,))

    halo_pair = out_blocked((STEPS, 2, 8, LANES), F32, 0, 1)
    slow_y, dy, dfb, g_fout, up, down, st = call(
        k_out,
        [sb_(sact), sb_(sp), sb_(cot_slow), fb_(df), fb_(fact), fb_(fb), whole(c2), whole(c3), whole(c4), whole(q4),
         whole(m16), whole(m64), whole(w_slow_out), whole(wout)],
        [slow_out(c_slow, BF16), slow_out(c_slow, F32), fast_out(LANES, F32),
         out_whole((in_fast, c_fast), F32), halo_pair, halo_pair, stat(26)],
        [*acc(t_n, c_slow, 3), *acc(f_n, LANES, 2), *acc(LANES, groups * c_fast, 1)],
        "out",
    )
    pair = (STEPS, 2, 8, LANES)
    ex5 = Exchange(
        sizes, 6, 26,
        bwd=(("plain", 0, 0, 12, 8, 0, 8), ("plain", 1, 3, 20, 8, 0, 16), ("lane4", 1, 0, 1, 1, 24, 25)),
        up=pair, down=pair,
    )
    c_cat = w_slow_in.shape[0]
    width = in_slow
    stream_a = Stream(sizes, rows_for(sizes, c_cat * c_slow // width), width)
    stream_b = Stream(sizes, rows_for(sizes, 9 * in_slow), width)
    gw_short, gw_sout, dsp, dsb, dfa, g_fmid, q6, q5 = call(
        k_back_out,
        [sb_(x_slow), sb_(lact), sb_(dy), sb_(sp), sb_(sact), sb_(sb4), fb_(dfb), fb_(fb), fb_(fa), fb_(ftap), 1, 2,
         whole(c1), whole(c2), whole(c3), whole(c4), 0, whole(m16), whole(m64), whole(w_slow_out), whole(wback)],
        [out_whole((stream_a.rows_n, width), BF16), out_whole((c_slow, width), BF16), slow_out(c_slow, BF16),
         slow_out(in_slow, F32), fast_out(LANES, F32), out_whole((3 * in_fast, LANES), F32), STAT],
        [*acc(t_n, in_slow, 2), *acc(f_n, LANES, 2), *acc(c_cat, c_slow, 1), *acc(in_slow, c_slow, 1),
         *acc(LANES, 3 * LANES, 1)],
        "back_out",
        Exchange(sizes, 6, 6, bwd=(("plain", 0, 4, 10, 2, 0, 2), ("lane4", 1, 0, 0, 1, 4, 5))),
        [gb, c3, c1],
        ex5,
        [st, up, down, gb, c4, c2],
    )

    def rows2(a):
        return a.reshape(-1, a.shape[-1])

    dsa_low, dfa_low, dlat, gw_fast, q7, q8, hn, res_a, near_b = back_tail(
        stream_a, stream_b,
        Exchange(sizes, 7, 4, bwd=(("plain", 0, 1, 8, 2, 0, 2),)),
        Exchange(sizes, 7, 4, bwd=(("plain", 0, 1, 6, 2, 0, 2),), post=(STEPS, groups * 8, c_lat)),
        [gw_short, rows2(dsb), rows2(sb4), pad, wsp, rows2(sa), x_fast, dfa, fa, w_slow_in, w_shortcut, rows2(dsp), rows2(lat)],
        [gb, c1, c2, c3, q6, m16, m64, g_fout, g_fmid],
        side, t_n, in_slow,
    )
    slow_gx, gw_in = call(
        k_slow_grad,
        [sb_(x_slow), sb_(lact), sb_(dsa_low.reshape(sl + (in_slow,))), sb_(dsp), whole(w_slow_in), whole(w_shortcut)],
        [slow_out(c_slow, BF16), out_whole((c_cat, in_slow), BF16)], acc(in_slow, c_cat, 1), "slow_grad",
    )
    fast_gx, gw_lat = call(
        k_fast_grad,
        [sb_(dlat.reshape(sl + (c_lat,))), sb_(lat), sb_(taps), blocked(hn, 0, 1), fb_(df), fb_(dfa_low), whole(c1), whole(q8),
         whole(m16), whole(wlat), whole(wfa)],
        [out_blocked((groups, inner, f_n, c_fast), BF16, 1, p_n), out_whole((5 * c_fast, c_lat), BF16)],
        [pltpu.VMEM((groups * p_n * f_n, c_fast), F32), *acc(c_lat, 5 * c_fast, 1)],
        "fast_grad",
    )
    sum_a, sum_bc, _ = final_sum(sizes, 9, stream_a, stream_b, res_a, near_b, [gw_sout, gw_in, gw_lat, gw_fast])
    blocks = c_slow // in_slow
    pieces = [(0, n * c_cat, c_cat, 0, n * width) for n in range(blocks)]
    pieces.append((1, 0, 9 * in_slow, 2, None))
    at = 0
    for n in range(blocks):
        pieces.append((2, at, in_slow, 1, n * width))
        at += in_slow
    for out, tall in ((3, c_cat), (4, gw_lat.shape[0])):
        pieces.append((2, at, tall, out, None))
        at += tall
    norm_rows = -(-gains.shape[0] // LANES)
    g_short, g_sout, gw_mid, gw_in, gw_lat, gains_grad, biases_grad, g_fin, g_fmid, g_fout = unpack(
        sum_a, sum_bc, stream_b.ch, tuple(pieces),
        [(c_cat, c_slow), (in_slow, c_slow), (9 * in_slow, width), (c_cat, in_slow), gw_lat.shape],
        [(norm_rows, LANES), (norm_rows, LANES), (in_fast, c_fast), w_fast_mid.shape, (in_fast, c_fast)],
        [q4, q5, q6, q7, q8],
    )
    grads = (
        g_fin.T,
        g_fmid,
        g_fout,
        gw_lat.reshape(w_lateral.shape),
        gw_in,
        gw_mid.reshape(w_slow_mid.shape),
        g_sout,
        g_short,
    )
    return (
        unview(slow_y),
        unview(fast_y),
        unview(slow_gx),
        unview(fast_gx),
        *grads,
        gains_grad.reshape(-1)[: gains.shape[0]],
        biases_grad.reshape(-1)[: biases.shape[0]],
    )


def solution(mesh):
    frames = P(("path", "frames"), None, None, None)
    in_specs = (frames, frames, P(AXES), P(AXES), *([P()] * 10), frames, frames)
    out_specs = (*([frames] * 4), *([P()] * 10))
    return jax.shard_map(per_device, mesh=mesh, in_specs=in_specs, out_specs=out_specs, check_vma=False)
```

```python
import functools

import jax
import jax.numpy as jnp
from jax import lax
from jax.experimental import pallas as pl
from jax.experimental.pallas import tpu as pltpu
from jax.sharding import PartitionSpec as P

norm_eps = 1e-05
F32 = jnp.float32
BF16 = jnp.bfloat16
MESH = pl.DeviceIdType.MESH
AXES = ("path", "frames")
STEPS = 7
LANES = 128
VMEM_LIMIT = 60 * 1024 * 1024


def dot(a, b):
    return jnp.dot(a, b, preferred_element_type=F32)


def dot_nt(a, b):
    return lax.dot_general(a, b, (((1,), (1,)), ((), ())), preferred_element_type=F32)


def dot_tn(a, b):
    return lax.dot_general(a, b, (((0,), (0,)), ((), ())), preferred_element_type=F32)


def sig(v):
    return 0.5 * jnp.tanh(0.5 * v) + 0.5


def slope(v):
    s = sig(v)
    return s + (v * s) * (1.0 - s)


def rows(ref, slab, first, count):
    parts = [ref[slab, first + j : first + j + 1, :] for j in range(count)]
    return parts[0] if count == 1 else jnp.concatenate(parts, axis=1)


def put_rows(ref, first, value):
    for j in range(value.shape[1] // LANES):
        ref[first + j : first + j + 1, :] = value[:, j * LANES : (j + 1) * LANES]


def zero_ref(ref):
    ref[...] = jnp.zeros(ref.shape, ref.dtype)


def spread_add(step, z, mean_ref, m2_ref, cols=slice(None)):
    count = z.shape[0]
    mean = jnp.sum(z, axis=0) * (1.0 / count)
    d = z - mean
    m2 = jnp.sum(d * d, axis=0)
    first = step == 0
    old_mean = jnp.where(first, 0.0, mean_ref[:, cols])
    old_m2 = jnp.where(first, 0.0, m2_ref[:, cols])
    done = jnp.full((1, z.shape[-1]), step, jnp.int32).astype(F32)
    share = 1.0 / (done + 1.0)
    delta = mean - old_mean
    mean_ref[:, cols] = old_mean + delta * share
    m2_ref[:, cols] = old_m2 + m2 + delta * delta * (done * share * count)


def spread_end(mean_ref, m2_ref, fill, positions):
    filled = jnp.sum(fill, axis=0, keepdims=True)
    mean = jnp.sum(fill * mean_ref[...], axis=0, keepdims=True) / jnp.maximum(filled, 1.0)
    d = mean_ref[...] - mean
    m2 = jnp.sum(fill * (m2_ref[...] + positions * (d * d)), axis=0, keepdims=True)
    return mean, m2


def sum_add(step, value, ref, cols=slice(None)):
    ref[:, cols] = jnp.where(step == 0, 0.0, ref[:, cols]) + jnp.sum(value, axis=0)


def sum_end(ref):
    return jnp.sum(ref[...], axis=0, keepdims=True)


def pad8(n):
    return -(-n // 8) * 8


def exchange_peers(cfg):
    paths, length = lax.axis_size("path"), lax.axis_size("frames")
    near = 4
    g1, g2 = paths * near, length // near
    me_p, me_f = lax.axis_index("path"), lax.axis_index("frames")
    me = me_p * length + me_f
    total = paths * length
    r1 = me_p * near + lax.rem(me_f, near)
    r2 = lax.div(me_f, near)

    def peer1(k):
        r = lax.rem(r1 + k, g1)
        return (lax.div(r, near), r2 * near + lax.rem(r, near))

    def peer2(k):
        r = lax.rem(r2 + k, g2)
        return (me_p, r * near + lax.rem(me_f, near))

    def split(index):
        return (lax.div(index, length), lax.rem(index, length))

    nxt, prv = split(lax.rem(me + 1, total)), split(lax.rem(me + total - 1, total))
    return g1, g2, r1, r2, peer1, peer2, nxt, prv


def exchange_hello(cfg):
    g1, g2, _, _, peer1, peer2, nxt, prv = exchange_peers(cfg)
    peers = [peer1(k) for k in range(1, g1)] + [peer2(k) for k in range(1, g2)]
    if cfg.greets:
        peers += [nxt, prv]
    for peer in peers:
        pl.semaphore_signal(pltpu.get_barrier_semaphore(), inc=1, device_id=peer, device_id_type=MESH)
    return len(peers)


def exchange_run(cfg, ins, outs, scratch, meanwhile=None, post=None, after=None):
    fwd, bwd = cfg.fwd, cfg.bwd
    nf = sum(c[2] for c in fwd)
    nb = max((c[6] + c[4] for c in bwd), default=0)
    n_row = 2 * nf + nb
    stats_ref, up_ref, down_ref = scratch[:3]
    gb_ref, *coef_refs = ins
    outs = list(outs)
    coef_out = outs.pop(0) if nf else None
    pq_out = outs.pop(0) if nb else None
    from_prev = outs.pop(0) if cfg.up else None
    from_next = outs.pop(0) if cfg.down else None
    slots1, slots2, mid, tot, send1, recv1, send2, recv2, up_land, up_sems, down_land, down_sems = scratch[3:15]
    g1, g2, r1, r2, peer1, peer2, nxt, prv = exchange_peers(cfg)

    halos = []
    copies = []
    for k in range(1, g1):
        copies.append(
            pltpu.make_async_remote_copy(
                src_ref=stats_ref,
                dst_ref=slots1.at[r1],
                send_sem=send1.at[k],
                recv_sem=recv1.at[k],
                device_id=peer1(k),
                device_id_type=MESH,
            )
        )
        copies[-1].start()
    for used, src, land, sems, peer in (
        (cfg.up, up_ref, up_land, up_sems, nxt),
        (cfg.down, down_ref, down_land, down_sems, prv),
    ):
        if used:
            halos.append(
                pltpu.make_async_remote_copy(
                    src_ref=src,
                    dst_ref=land,
                    send_sem=sems.at[0],
                    recv_sem=sems.at[1],
                    device_id=peer,
                    device_id_type=MESH,
                )
            )
            halos[-1].start()
    slots1[r1] = stats_ref[...]
    if meanwhile is not None:
        meanwhile()
    for c in copies:
        c.wait_recv()

    def combine(slots, count, out):
        if nf:
            n = slots[0, n_row : n_row + 1, :]
            for g in range(1, count):
                n = n + slots[g, n_row : n_row + 1, :]
            acc = slots[0, n_row : n_row + 1, :] * slots[0, 0:nf, :]
            for g in range(1, count):
                acc = acc + slots[g, n_row : n_row + 1, :] * slots[g, 0:nf, :]
            mean = acc / jnp.maximum(n, 1.0)
            m2 = None
            for g in range(count):
                d = slots[g, 0:nf, :] - mean
                part = slots[g, nf : 2 * nf, :] + slots[g, n_row : n_row + 1, :] * (d * d)
                m2 = part if m2 is None else m2 + part
            out[0:nf, :] = mean
            out[nf : 2 * nf, :] = m2
            out[n_row : n_row + 1, :] = n
        if nb:
            acc = slots[0, 2 * nf : n_row, :]
            for g in range(1, count):
                acc = acc + slots[g, 2 * nf : n_row, :]
            out[2 * nf : n_row, :] = acc

    zero_ref(mid)
    combine(slots1, g1, mid)
    copies2 = []
    for k in range(1, g2):
        copies2.append(
            pltpu.make_async_remote_copy(
                src_ref=mid,
                dst_ref=slots2.at[r2],
                send_sem=send2.at[k],
                recv_sem=recv2.at[k],
                device_id=peer2(k),
                device_id_type=MESH,
            )
        )
        copies2[-1].start()
    slots2[r2] = mid[...]
    for c in copies2:
        c.wait_recv()
    combine(slots2, g2, tot)

    def lanes4(v):
        w = v + pltpu.roll(v, 64, 1)
        return w + pltpu.roll(w, 32, 1)

    at = 0
    for kind, g_row, count in fwd:
        n = tot[n_row : n_row + 1, :]
        mean = tot[at : at + count, :]
        m2 = tot[nf + at : nf + at + count, :]
        if kind == "lane4":
            whole = lanes4(mean) * 0.25
            d = mean - whole
            var = lanes4(m2 + n * (d * d)) / (4.0 * n)
            mean = whole
        elif kind == "row4":
            whole = jnp.sum(mean, axis=0, keepdims=True) * 0.25
            d = mean - whole
            var = jnp.sum(m2 + n * (d * d), axis=0, keepdims=True) / (4.0 * n)
            var = jnp.broadcast_to(var, (count, LANES))
            mean = jnp.broadcast_to(whole, (count, LANES))
        else:
            var = m2 / n
        inv = lax.rsqrt(var + norm_eps)
        scale = inv * gb_ref[0, g_row : g_row + count, :]
        coef_out[0, at : at + count, :] = scale
        coef_out[1, at : at + count, :] = gb_ref[1, g_row : g_row + count, :] - mean * scale
        coef_out[2, at : at + count, :] = inv
        coef_out[3, at : at + count, :] = mean * inv
        coef_out[4, at : at + count, :] = jnp.broadcast_to(n, (count, LANES))
        at += count
    at = 0
    for kind, coef, row, _, count, db_at, dg_at in bwd:
        db = tot[2 * nf + db_at : 2 * nf + db_at + count, :]
        dg = tot[2 * nf + dg_at : 2 * nf + dg_at + count, :]
        c = coef_refs[coef]
        scale, inv = c[0, row : row + count, :], c[2, row : row + count, :]
        mi, n = c[3, row : row + count, :], c[4, row : row + count, :]
        if kind == "lane4":
            db, dg, n = lanes4(db), lanes4(dg), 4.0 * n
        elif kind == "row4":
            db = jnp.broadcast_to(jnp.sum(db, axis=0, keepdims=True), (count, LANES))
            dg = jnp.broadcast_to(jnp.sum(dg, axis=0, keepdims=True), (count, LANES))
            n = 4.0 * n
        pq_out[0, at : at + count, :] = scale / n * (db - mi * dg)
        pq_out[1, at : at + count, :] = scale / n * inv * dg
        pq_out[2, at : at + count, :] = db
        pq_out[3, at : at + count, :] = dg
        at += count

    if cfg.post:
        post_sent, post_land, post_sems = scratch[15:]
        post(pq_out, post_sent)
        late = pltpu.make_async_remote_copy(
            src_ref=post_sent,
            dst_ref=post_land,
            send_sem=post_sems.at[0],
            recv_sem=post_sems.at[1],
            device_id=prv,
            device_id_type=MESH,
        )
        late.start()
        if after is not None:
            after()
        late.wait()
        outs.pop(0)[...] = post_land[...]
    for c in halos:
        c.wait()
    if cfg.up:
        from_prev[...] = up_land[...]
    if cfg.down:
        from_next[...] = down_land[...]
    for c in copies:
        c.wait_send()
    for c in copies2:
        c.wait_send()


class Exchange:
    def __init__(self, sizes, cid, rows_n, fwd=(), bwd=(), up=None, down=None, post=None):
        self.cid, self.fwd, self.bwd, self.up, self.down, self.post = cid, fwd, bwd, up, down, post
        self.greets = bool(up or down or post)
        g1, g2, r = sizes[0] * 4, sizes[1] // 4, pad8(rows_n)
        self.outs = []
        nf, nn = sum(c[2] for c in fwd), sum(c[4] for c in bwd)
        if nf:
            self.outs.append(((5, nf, LANES), F32))
        if nn:
            self.outs.append(((4, nn, LANES), F32))
        self.outs += [(h, F32) for h in (up, down) if h]
        if post:
            self.outs.append((post, BF16))
        none = (8, LANES)
        self.stats = (r, LANES)
        self.work = [
            pltpu.VMEM((g1, r, LANES), F32),
            pltpu.VMEM((g2, r, LANES), F32),
            pltpu.VMEM((r, LANES), F32),
            pltpu.VMEM((r, LANES), F32),
            pltpu.SemaphoreType.DMA((g1,)),
            pltpu.SemaphoreType.DMA((g1,)),
            pltpu.SemaphoreType.DMA((g2,)),
            pltpu.SemaphoreType.DMA((g2,)),
            pltpu.VMEM(up or none, F32),
            pltpu.SemaphoreType.DMA((2,)),
            pltpu.VMEM(down or none, F32),
            pltpu.SemaphoreType.DMA((2,)),
        ]
        if post:
            self.work += [pltpu.VMEM(post, BF16), pltpu.VMEM(post, BF16), pltpu.SemaphoreType.DMA((2,))]
        self.local = [pltpu.VMEM(self.stats, F32), pltpu.VMEM(up or none, F32), pltpu.VMEM(down or none, F32)]


STAT, UP, DOWN = "stat", "up", "down"


def call(kernel, ins, outs, scratch=(), name=None, ex=None, ex_ins=(), pre=None, pre_ins=()):
    real = [o for o in outs if not isinstance(o, str)]
    given = ins
    ins = [a for a in given if not isinstance(a, int)]
    extra_in = [whole(a) for a in (*ex_ins, *pre_ins)]
    extra_out = [out_whole(s, d) for s, d in ex.outs] if ex else []
    local = [*ex.local, *ex.work] if ex else []
    n_local = len(local)
    if pre:
        extra_out.append(out_whole(*pre.outs[0]))
        local += [*pre.work, *[pltpu.VMEM(shape, d) for shape, d in pre.outs[1:]]]
    all_in, all_out = [*ins, *extra_in], [*real, *extra_out]
    sizes = [len(ins), len(extra_in), len(real), len(extra_out), len(scratch), len(local)]
    ends = [sum(sizes[: k + 1]) for k in range(len(sizes))]

    def body(*refs):
        k_in, x_in, k_out, x_out, k_scr, x_scr = (refs[e - n : e] for e, n in zip(ends, sizes))
        if ex is None:
            kernel(*k_in, *k_out, *k_scr)
            return
        i = pl.program_id(0)

        p_ins, p_outs, p_scr = x_in[len(ex_ins) :], [], x_scr[n_local:]
        x_in, x_scr = x_in[: len(ex_ins)], x_scr[:n_local]
        if pre:
            n = len(pre.work)
            p_outs = [x_out[-1], *p_scr[n:]]
            x_out = x_out[:-1]

        @pl.when(i == 0)
        def _():
            exchange_hello(pre or ex)
            if pre:
                pl.semaphore_wait(pltpu.get_barrier_semaphore(), len_peers(pre))
                exchange_run(pre, p_ins[3:], p_outs, [*p_ins[:3], *p_scr[:n]])

        if pre:
            it_in = iter(k_in)
            views = [p_outs[0], *[o.at[pl.ds(i, 1)] for o in p_outs[1:]]]
            k_in = [views[a] if isinstance(a, int) else next(it_in) for a in given]
        named = {STAT: x_scr[0]}
        if ex.up:
            named[UP] = x_scr[1].at[pl.ds(i, 1)]
        if ex.down:
            named[DOWN] = x_scr[2].at[pl.ds(i, 1)]
        it = iter(k_out)
        late = kernel(*k_in, *[named[o] if isinstance(o, str) else next(it) for o in outs], *k_scr)

        @pl.when(i == STEPS - 1)
        def _():
            if not pre:
                pl.semaphore_wait(pltpu.get_barrier_semaphore(), len_peers(ex))
            exchange_run(ex, x_in, x_out, x_scr, late)

    params = {"collective_id": ex.cid, "has_side_effects": True} if ex else {}
    return pl.pallas_call(
        body,
        grid=(STEPS,),
        in_specs=[pl.BlockSpec(b, m) for _, b, m in all_in],
        out_specs=[pl.BlockSpec(b, m) for _, _, b, m in all_out],
        out_shape=[jax.ShapeDtypeStruct(s, d) for s, d, _, _ in all_out],
        scratch_shapes=[*scratch, *local],
        compiler_params=pltpu.CompilerParams(
            dimension_semantics=("arbitrary",), vmem_limit_bytes=VMEM_LIMIT, **params
        ),
        name=name,
    )(*[a for a, _, _ in all_in])


def len_peers(ex):
    paths, length = lax.axis_size("path"), lax.axis_size("frames")
    return paths * 4 - 1 + length // 4 - 1 + (2 if ex.greets else 0)


def whole(array):
    zeros = (0,) * array.ndim
    return (array, array.shape, lambda i: zeros)


def blocked(array, axis, size):
    block = array.shape[:axis] + (size,) + array.shape[axis + 1 :]
    return (array, block, lambda i: tuple(i if d == axis else 0 for d in range(array.ndim)))


def out_whole(shape, dtype):
    zeros = (0,) * len(shape)
    return (shape, dtype, shape, lambda i: zeros)


def out_blocked(shape, dtype, axis, size):
    block = shape[:axis] + (size,) + shape[axis + 1 :]
    return (shape, dtype, block, lambda i: tuple(i if d == axis else 0 for d in range(len(shape))))


def flat(value):
    return value.reshape(-1, value.shape[-1])


def spread_rows(ref, index, count, height):
    return [jnp.broadcast_to(ref[(*index, slice(p, p + 1))], (height, ref.shape[-1])) for p in range(count)]


def k_first(i, x_ref, tail_ref, m16_ref, m64_ref, wfa_ref, wlat_ref,
            fa_ref, lat_ref, taps_ref, st_ref, up_ref, down_ref, xs, fm, fv, lm, lv):
    x = x_ref[...]
    s_n, p_n, f_n, _ = x.shape
    packed = jnp.concatenate([flat(x[s]) for s in range(s_n)], axis=1)
    fa = dot_nt(packed, wfa_ref[...])
    fa_ref[...] = fa.reshape(fa_ref.shape)
    zero_ref(up_ref)
    zero_ref(down_ref)
    for p in range(p_n):
        down_ref[0, p : p + 1, :] = fa[p * f_n : p * f_n + 1, :]
        up_ref[0, p : p + 1, :] = fa[p * f_n + f_n - 1 : p * f_n + f_n, :]
    spread_add(i, fa.reshape(p_n, f_n, LANES), fm, fv)

    xs[...] = flat(x).astype(F32)
    n = xs.shape[0] // 4
    quarter = [xs[pl.ds(k, n, stride=4), :] for k in range(4)]
    t_n = f_n // 4
    first = lax.broadcasted_iota(jnp.int32, (n // t_n, t_n, LANES), 1) == 0
    link = m16_ref[1:2]
    tail = tail_ref[0].astype(F32)
    taps = []
    for k in range(2):
        halo = jnp.concatenate(
            [
                jnp.broadcast_to(tail[s * 8 + p : s * 8 + p + 1, k * LANES : (k + 1) * LANES], (t_n, LANES))
                for s in range(s_n)
                for p in range(p_n)
            ],
            axis=0,
        )
        moved = pltpu.roll(quarter[2 + k], 1, 0).reshape(n // t_n, t_n, LANES)
        taps.append(flat(jnp.where(first, halo.reshape(moved.shape), moved) * link))
    taps = jnp.concatenate([*taps, *quarter[:3]], axis=1).astype(BF16)
    taps_ref[...] = taps.reshape(taps_ref.shape)
    lat = dot(taps, wlat_ref[...])
    lat_ref[...] = lat.reshape(lat_ref.shape)
    spread_add(i, lat.reshape(n // t_n, t_n, lat.shape[1]), lm, lv)

    @pl.when(i == STEPS - 1)
    def _():
        zero_ref(st_ref)
        fill = m16_ref[0, :, 0:1]
        mean, m2 = spread_end(fm, fv, m64_ref[0, :, 0:1], STEPS * p_n)
        put_rows(st_ref, 0, mean)
        put_rows(st_ref, 3, m2)
        mean, m2 = spread_end(lm, lv, fill, STEPS * p_n * s_n)
        put_rows(st_ref, 1, mean)
        put_rows(st_ref, 4, m2)
        put_rows(st_ref, 6, count_row(m16_ref, STEPS * p_n * s_n))


def count_row(m16_ref, positions):
    return jnp.sum(m16_ref[0], axis=0, keepdims=True) * float(positions)


def shifted(value, first_rows, last_rows, f_n):
    n = value.shape[0]
    shape = (n // f_n, f_n, value.shape[1])
    place = lax.broadcasted_iota(jnp.int32, shape, 1)
    before = jnp.where(place == 0, first_rows, pltpu.roll(value, 1, 0).reshape(shape))
    after = jnp.where(place == f_n - 1, last_rows, pltpu.roll(value, n - 1, 0).reshape(shape))
    return before, after


def k_join(i, x_ref, lat_ref, fa_ref, hp_ref, hn_ref, c1_ref, m16_ref, m64_ref, win_ref, wsc_ref, wmid_ref,
           lact_ref, ftap_ref, sa_ref, sp_ref, fb_ref, st_ref, am, av, pm, pv, bm, bv):
    s_n, p_n, t_n, c_slow = x_ref.shape
    c_lat = lat_ref.shape[-1]
    v = flat(lat_ref[...]) * rows(c1_ref, 0, 1, 2) + rows(c1_ref, 1, 1, 2)
    lact = (v * sig(v)).astype(BF16)
    lact_ref[...] = lact.reshape(lact_ref.shape)
    joined = jnp.concatenate([flat(x_ref[...]), lact], axis=1)
    wide = c_lat
    for n in range(1 + wsc_ref.shape[1] // wide):
        z = dot(joined, win_ref[...] if n == 0 else wsc_ref[:, (n - 1) * wide : n * wide])
        z4 = z.reshape(s_n, p_n, t_n, wide)
        z3 = z.reshape(s_n * p_n, t_n, wide)
        if n == 0:
            sa_ref[...] = z4
            spread_add(i, z3, am, av)
        else:
            cols = slice((n - 1) * wide, n * wide)
            sp_ref[:, :, :, cols] = z4
            spread_add(i, z3, pm, pv, cols)

    f_n = fa_ref.shape[1]
    scale, shift = rows(c1_ref, 0, 0, 1), rows(c1_ref, 1, 0, 1)

    def act(z):
        w = z * scale + shift
        return (w * sig(w)).astype(BF16).astype(F32)

    fact = act(flat(fa_ref[...]))
    ends = []
    for ref in (hp_ref, hn_ref):
        small = act(ref[0])
        ends.append(
            jnp.concatenate(
                [jnp.broadcast_to(small[p : p + 1, :], (f_n, LANES)) for p in range(p_n)], axis=0
            ).reshape(p_n, f_n, LANES)
        )
    before, after = shifted(fact, ends[0], ends[1], f_n)
    ftap = jnp.concatenate(
        [flat(before * m64_ref[1:2]), fact, flat(after * m64_ref[2:3])], axis=1
    ).astype(BF16)
    ftap_ref[...] = ftap.reshape(ftap_ref.shape)
    fb = dot(ftap, wmid_ref[...])
    fb_ref[...] = fb.reshape(fb_ref.shape)
    spread_add(i, fb.reshape(p_n, f_n, LANES), bm, bv)

    @pl.when(i == STEPS - 1)
    def _():
        zero_ref(st_ref)
        fill = m16_ref[0, :, 0:1]
        positions = STEPS * p_n * s_n
        mean, m2 = spread_end(bm, bv, m64_ref[0, :, 0:1], STEPS * p_n)
        put_rows(st_ref, 0, mean)
        put_rows(st_ref, 11, m2)
        mean, m2 = spread_end(am, av, fill, positions)
        put_rows(st_ref, 1, mean)
        put_rows(st_ref, 12, m2)
        mean, m2 = spread_end(pm, pv, fill, positions)
        put_rows(st_ref, 3, mean)
        put_rows(st_ref, 14, m2)
        put_rows(st_ref, 22, count_row(m16_ref, positions))


def k_spatial(i, sa_ref, fb_ref, c2_ref, m16_ref, m64_ref, wsp_ref, wout_ref,
              pad_ref, sb_ref, fact_ref, st_ref, sm, sv, cm, cv):
    h_n, w_n, t_n, c = sa_ref.shape

    @pl.when(i == 0)
    def _():
        scale, shift = rows(c2_ref, 0, 1, 2), rows(c2_ref, 1, 1, 2)
        zero_ref(pad_ref)

        @pl.loop(0, h_n)
        def _(h):
            v = flat(sa_ref[h]) * scale + shift
            pad_ref[h + 1, 1 : w_n + 1] = (v * sig(v)).astype(BF16).reshape(w_n, t_n, c)

    per = h_n // STEPS
    h0 = i * per
    patches = [flat(pad_ref[pl.ds(h0 + a, per), b : b + w_n]) for a in range(3) for b in range(3)]
    acc = dot(jnp.concatenate(patches, axis=1), wsp_ref[...])
    sb_ref[...] = acc.reshape(sb_ref.shape)
    spread_add(i, acc.reshape(per * w_n, t_n, acc.shape[1]), sm, sv)

    p_n, f_n, _ = fb_ref.shape
    v = flat(fb_ref[...]) * rows(c2_ref, 0, 0, 1) + rows(c2_ref, 1, 0, 1)
    fact = (v * sig(v)).astype(BF16)
    fact_ref[...] = fact.reshape(fact_ref.shape)
    fc = dot(fact, wout_ref[...])
    spread_add(i, fc.reshape(p_n, f_n, fc.shape[1]), cm, cv)

    @pl.when(i == STEPS - 1)
    def _():
        zero_ref(st_ref)
        mean, m2 = spread_end(cm, cv, m64_ref[0, :, 0:1], STEPS * p_n)
        put_rows(st_ref, 0, mean)
        put_rows(st_ref, 6, m2)
        mean, m2 = spread_end(sm, sv, m16_ref[0, :, 0:1], h_n * w_n)
        put_rows(st_ref, 4, mean)
        put_rows(st_ref, 10, m2)
        put_rows(st_ref, 12, count_row(m16_ref, h_n * w_n))


def k_expand(i, sb_ref, fact_ref, x_ref, cot_ref, c3_ref, m16_ref, m64_ref, wso_ref, wout_ref,
             sact_ref, fout_ref, df_ref, st_ref, cm, cv, s1, s2):
    s_n, p_n, t_n = x_ref.shape[0], fact_ref.shape[0], sb_ref.shape[-2]
    v = flat(sb_ref[...]) * rows(c3_ref, 0, 4, 2) + rows(c3_ref, 1, 4, 2)
    sact = (v * sig(v)).astype(BF16)
    sact_ref[...] = sact.reshape(sact_ref.shape)
    wide = 256
    for n in range(wso_ref.shape[1] // wide):
        cols = slice(n * wide, (n + 1) * wide)
        z = dot(sact, wso_ref[:, cols])
        spread_add(i, z.reshape(s_n * p_n, t_n, wide), cm, cv, cols)

    f_n = fact_ref.shape[1]
    fc = dot(flat(fact_ref[...]), wout_ref[...])
    fill = m64_ref[0:1]
    for s in range(s_n):
        cols = slice(s * LANES, (s + 1) * LANES)
        z = fc[:, cols].reshape(p_n, f_n, LANES)
        unit = z * rows(c3_ref, 2, s, 1) - rows(c3_ref, 3, s, 1)
        pre = z * rows(c3_ref, 0, s, 1) + rows(c3_ref, 1, s, 1) + x_ref[s].astype(F32)
        g = sig(pre)
        y = pre * g
        fout_ref[s] = (y * fill).astype(BF16)
        d = cot_ref[s].astype(F32) * fill * (g + y * (1.0 - g))
        df_ref[:, :, cols] = d
        sum_add(i, d, s1, cols)
        sum_add(i, d * unit, s2, cols)

    @pl.when(i == STEPS - 1)
    def _():
        zero_ref(st_ref)
        positions = STEPS * p_n * s_n
        mean, m2 = spread_end(cm, cv, m16_ref[0, :, 0:1], positions)
        put_rows(st_ref, 0, mean)
        put_rows(st_ref, 8, m2)
        put_rows(st_ref, 16, sum_end(s1))
        put_rows(st_ref, 20, sum_end(s2))
        put_rows(st_ref, 24, count_row(m16_ref, positions))


def run_resident(kernel, ex_list, hbm, small, locals_, outs, scratch, name, scalars=0):
    vm, anywhere = pl.BlockSpec(memory_space=pltpu.VMEM), pl.BlockSpec(memory_space=pl.ANY)
    for ex in ex_list:
        outs = [*outs, *[(shape, dtype, False) for shape, dtype in ex.outs]]
    work = [w for ex in ex_list for w in (*ex.local, *ex.work)]
    sizes = [len(hbm), len(small), len(outs), len(hbm), len(locals_), len(scratch), 1]
    ends = [sum(sizes[: k + 1]) for k in range(len(sizes))]

    def body(*refs):
        h, sm, o, loaded, kept, scr, (sems,) = (refs[e - n : e] for e, n in zip(ends, sizes))
        rest, at = [], ends[-1]
        for ex in ex_list:
            n = len(ex.local) + len(ex.work)
            rest.append(refs[at : at + n])
            at += n
        loads = [pltpu.make_async_copy(a, b, sems.at[k]) for k, (a, b) in enumerate(zip(h, loaded))]
        greeter = max(ex_list, key=lambda ex: ex.greets)
        count = exchange_hello(greeter)
        for load in loads:
            load.start()
        kernel(loads, lambda: pl.semaphore_wait(pltpu.get_barrier_semaphore(), count), loaded, sm, kept, scr, o, rest)

    return pl.pallas_call(
        body,
        out_shape=[jax.ShapeDtypeStruct(shape, dtype) for shape, dtype, _ in outs],
        in_specs=[anywhere] * len(hbm) + [pl.BlockSpec(memory_space=pltpu.SMEM)] * scalars + [vm] * (len(small) - scalars),
        out_specs=[anywhere if stays else vm for _, _, stays in outs],
        scratch_shapes=[
            *[pltpu.VMEM(a.shape, a.dtype) for a in hbm], *[pltpu.VMEM(*k) for k in locals_], *scratch,
            pltpu.SemaphoreType.DMA((len(hbm),)), *work,
        ],
        compiler_params=pltpu.CompilerParams(
            collective_id=ex_list[0].cid, has_side_effects=True, vmem_limit_bytes=VMEM_LIMIT
        ),
        name=name,
    )(*hbm, *small)


def stores_of(pairs, sems):
    return [pltpu.make_async_copy(a, b, sems.at[k]) for k, (a, b) in enumerate(pairs)]


def k_front(exs, loads, met, loaded, small, kept, scratch, outs, work):
    x_fast, wlat, x_slow, w_in, w_sc = loaded
    fa, lat, taps, lact, ftap, sa, sp, fb = kept
    xs, fm, fv, lm, lv, am, av, pm, pv, bm, bv, sems, sp_sems, ends_f, sent, sent_low, tail_ref, tail_sems = scratch
    big, ready, (c1, hp, hn, c2) = outs[:8], outs[8:15], outs[15:]
    gb, m16, m64, wfa, wmid, wback, wout = ready
    p_n = fa.shape[0] // STEPS
    copies = dict(zip((0, 1, 2, 3, 4, 5, 7), stores_of([p for k, p in enumerate(zip(kept, big)) if k != 6], sems)))
    st1, up, down = work[0][:3]
    loads[0].wait()
    s_n, inner, f_n, ch = x_fast.shape
    t_n = lat.shape[2]
    ends_f[...] = flat(x_fast[:, :, f_n - t_n : f_n, :]).astype(F32)
    zero_ref(sent)
    for k in range(2):
        lines = ends_f[pl.ds(t_n - 2 + k, s_n * inner, stride=t_n), :]
        for s in range(s_n):
            for step in range(STEPS):
                at = s * inner + step * p_n
                sent[step, s * 8 : s * 8 + p_n, k * ch : (k + 1) * ch] = lines[at : at + p_n, :]
    sent_low[...] = sent[...].astype(BF16)
    met()
    nxt = exchange_peers(exs[0])[6]
    halo = pltpu.make_async_remote_copy(
        src_ref=sent_low, dst_ref=tail_ref, send_sem=tail_sems.at[0], recv_sem=tail_sems.at[1],
        device_id=nxt, device_id_type=MESH,
    )
    halo.start()
    small_set_up(*small, *ready, s_n, t_n)
    loads[1].wait()
    halo.wait()

    def first(i):
        part, one = pl.ds(i * p_n, p_n), pl.ds(i, 1)
        k_first(i, x_fast.at[:, part], tail_ref.at[one], m16, m64, wfa, wlat, fa.at[part], lat.at[:, part],
                taps.at[:, part], st1, up.at[one], down.at[one], xs, fm, fv, lm, lv)

    each(0, STEPS, first)
    for k in (0, 1, 2):
        copies[k].start()
    exchange_run(exs[0], [gb], [c1, hp, hn], work[0])
    for k in (2, 3, 4):
        loads[k].wait()

    def store_sp(i):
        part = pl.ds(i * p_n, p_n)
        return pltpu.make_async_copy(sp.at[:, part], big[6].at[:, part], sp_sems.at[i])

    def join(i):
        part, one = pl.ds(i * p_n, p_n), pl.ds(i, 1)
        k_join(i, x_slow.at[:, part], lat.at[:, part], fa.at[part], hp.at[one], hn.at[one], c1, m16, m64, w_in, w_sc, wmid,
               lact.at[:, part], ftap.at[part], sa.at[:, part], sp.at[:, part], fb.at[part], work[1][0],
               am, av, pm, pv, bm, bv)
        store_sp(i).start()

    each(0, STEPS, join)
    for k in (3, 4, 5, 7):
        copies[k].start()
    exchange_run(exs[1], [gb], [c2], work[1])
    each(0, STEPS, lambda i: store_sp(i).wait())
    for k in (0, 1, 2, 3, 4, 5, 7):
        copies[k].wait()


def k_middle(exs, loads, met, loaded, small, kept, scratch, outs, work):
    sa, fb, wsp, wso, x_fast, cot = loaded
    gb, c2, m16, m64, wout = small
    pad, sb, fact, sact, fast_y, df = kept
    sm, sv, cm, cv, em, ev, s1, s2, sems, y_sems, df_sems = scratch
    big, (c3, c4, q4) = outs[:6], outs[6:]
    p_n = fb.shape[0] // STEPS
    rows_n = sb.shape[0] // STEPS
    copies = stores_of(list(zip(kept, big))[:4], sems)
    for k in (0, 1, 2):
        loads[k].wait()

    def spatial(i):
        part, span = pl.ds(i * p_n, p_n), pl.ds(i * rows_n, rows_n)
        k_spatial(i, sa, fb.at[part], c2, m16, m64, wsp, wout, pad, sb.at[span], fact.at[part], work[0][0], sm, sv, cm, cv)

    each(0, STEPS, spatial)
    met()
    for k in (0, 1, 2):
        copies[k].start()
    exchange_run(exs[0], [gb], [c3], work[0])
    for k in (3, 4, 5):
        loads[k].wait()

    def y_store(i):
        part = pl.ds(i * p_n, p_n)
        return pltpu.make_async_copy(fast_y.at[:, part], big[4].at[:, part], y_sems.at[i])

    def df_store(i):
        part = pl.ds(i * p_n, p_n)
        return pltpu.make_async_copy(df.at[part], big[5].at[part], df_sems.at[i])

    def expand(i):
        part, span = pl.ds(i * p_n, p_n), pl.ds(i * rows_n, rows_n)
        k_expand(i, sb.at[span], fact.at[part], x_fast.at[:, part], cot.at[:, part], c3, m16, m64, wso, wout,
                 sact.at[span], fast_y.at[:, part], df.at[part], work[1][0], em, ev, s1, s2)
        y_store(i).start()
        df_store(i).start()

    each(0, STEPS, expand)
    copies[3].start()
    exchange_run(exs[1], [gb, c3], [c4, q4], work[1])
    each(0, STEPS, lambda i: y_store(i).wait())
    each(0, STEPS, lambda i: df_store(i).wait())
    for copy in copies:
        copy.wait()


def back_norm(scale, p, q, dy, z, fill):
    return scale * dy - fill * (p + z * q)


def k_out(sact_ref, sp_ref, cot_ref, df_ref, fact_ref, fb_ref, c2_ref, c3_ref, c4_ref, q4_ref,
          m16_ref, m64_ref, wso_ref, wout_ref,
          out_ref, dy_ref, dfb_ref, gout_ref, up_ref, down_ref, st_ref, s1, s2, s3, t1, t2, gout):
    i = pl.program_id(0)
    s_n, p_n, t_n, _ = sact_ref.shape
    sact = flat(sact_ref[...])
    fill = m16_ref[0:1, :, 0:1]
    wide = 256
    for n in range(wso_ref.shape[1] // wide):
        cols = slice(n * wide, (n + 1) * wide)
        shape = (s_n * p_n, t_n, wide)
        sc = dot(sact, wso_ref[:, cols]).reshape(shape)
        sp = sp_ref[:, :, :, cols].reshape(shape)
        u6 = sc * rows(c4_ref, 2, 2 * n, 2) - rows(c4_ref, 3, 2 * n, 2)
        u7 = sp * rows(c2_ref, 2, 3 + 2 * n, 2) - rows(c2_ref, 3, 3 + 2 * n, 2)
        pre = (
            sc * rows(c4_ref, 0, 2 * n, 2)
            + sp * rows(c2_ref, 0, 3 + 2 * n, 2)
            + (rows(c4_ref, 1, 2 * n, 2) + rows(c2_ref, 1, 3 + 2 * n, 2))
        )
        g = sig(pre)
        y = pre * g
        out_ref[:, :, :, cols] = (y * fill).astype(BF16).reshape(s_n, p_n, t_n, wide)
        d = cot_ref[:, :, :, cols].reshape(shape).astype(F32) * fill * (g + y * (1.0 - g))
        dy_ref[:, :, :, cols] = d.reshape(s_n, p_n, t_n, wide)
        sum_add(i, d, s1, cols)
        sum_add(i, d * u6, s2, cols)
        sum_add(i, d * u7, s3, cols)

    f_n = fact_ref.shape[1]
    fact = flat(fact_ref[...])
    fc = dot(fact, wout_ref[...])
    fill4 = m64_ref[0:1]
    parts = []
    for s in range(s_n):
        cols = slice(s * LANES, (s + 1) * LANES)
        d = back_norm(
            rows(c3_ref, 0, s, 1), rows(q4_ref, 0, s, 1), rows(q4_ref, 1, s, 1),
            df_ref[:, :, cols], fc[:, cols].reshape(p_n, f_n, LANES), fill4,
        )
        parts.append(flat(d).astype(BF16))
    dfc = jnp.concatenate(parts, axis=1)
    add_to(i, gout, dot_tn(fact, dfc))
    z = fb_ref[...]
    back = dot_nt(dfc, wout_ref[...]).reshape(p_n, f_n, LANES) * slope(
        z * rows(c2_ref, 0, 0, 1) + rows(c2_ref, 1, 0, 1)
    )
    dfb_ref[...] = back
    sum_add(i, back, t1)
    sum_add(i, back * (z * rows(c2_ref, 2, 0, 1) - rows(c2_ref, 3, 0, 1)), t2)
    for k, value in enumerate((back, z)):
        value = flat(value)
        for p in range(p_n):
            down_ref[0, k, p : p + 1, :] = value[p * f_n : p * f_n + 1, :]
            up_ref[0, k, p : p + 1, :] = value[p * f_n + f_n - 1 : p * f_n + f_n, :]
        down_ref[0, k, p_n : p_n + 1, :] = m64_ref[0, 0:1, :]
        up_ref[0, k, p_n : p_n + 1, :] = m64_ref[0, f_n - 1 : f_n, :]

    @pl.when(i == STEPS - 1)
    def _():
        zero_ref(st_ref)
        put_rows(st_ref, 0, sum_end(s1))
        put_rows(st_ref, 8, sum_end(s2))
        put_rows(st_ref, 16, sum_end(s3))
        put_rows(st_ref, 24, sum_end(t1))
        put_rows(st_ref, 25, sum_end(t2))
        gout_ref[...] = fold_wide(gout, s_n)


def add_to(step, ref, value):
    ref[...] = jnp.where(step == 0, 0.0, ref[...]) + value


def fold_wide(ref, count):
    a = ref.shape[0] // count
    return sum(ref[s * a : (s + 1) * a, s * LANES : (s + 1) * LANES] for s in range(count))


def fold_lanes(value, count):
    a = value.shape[0] // count
    parts = [value[s * a : (s + 1) * a, :] for s in range(count)]
    return sum(p if s == 0 else pltpu.roll(p, LANES - s * a, 1) for s, p in enumerate(parts))


def k_back_out(x_ref, lact_ref, dy_ref, sp_ref, sact_ref, sb_ref, dfb_ref, fb_ref, fa_ref, ftap_ref, hp_ref, hn_ref,
               c1_ref, c2_ref, c3_ref, c4_ref, q5_ref, m16_ref, m64_ref, wso_ref, wback_ref,
               gw_ref, gs_ref, dsp_ref, dsb_ref, dfa_ref, gmid_ref, st_ref, s1, s2, t1, t2, gsc, gso, gmid):
    i = pl.program_id(0)
    s_n, p_n, t_n, c = sb_ref.shape
    sact = flat(sact_ref[...])
    fill = m16_ref[0:1, :, 0:1]
    wide = 256
    dscs = []
    turned = jnp.concatenate([flat(x_ref[...]), flat(lact_ref[...])], axis=1).T
    sact_turned = sact.T
    for n in range(wso_ref.shape[1] // wide):
        cols = slice(n * wide, (n + 1) * wide)
        shape = (s_n * p_n, t_n, wide)
        d = dy_ref[:, :, :, cols].reshape(shape)
        sc = dot(sact, wso_ref[:, cols]).reshape(shape)
        dsc = back_norm(rows(c4_ref, 0, 2 * n, 2), rows(q5_ref, 0, 2 * n, 2), rows(q5_ref, 1, 2 * n, 2), d, sc, fill)
        dsc = flat(dsc.astype(BF16))
        old = jnp.where(i == 0, 0.0, gso[:, cols])
        gso[:, cols] = old + dot(sact_turned, dsc)
        sp = sp_ref[:, :, :, cols].reshape(shape)
        dsp = back_norm(
            rows(c2_ref, 0, 3 + 2 * n, 2), rows(q5_ref, 0, 8 + 2 * n, 2), rows(q5_ref, 1, 8 + 2 * n, 2), d, sp, fill
        )
        dsp = flat(dsp.astype(BF16))
        dsp_ref[:, :, :, cols] = dsp.reshape(s_n, p_n, t_n, wide)
        old = jnp.where(i == 0, 0.0, gsc[:, cols])
        gsc[:, cols] = old + dot(turned, dsp)
        dscs.append(dsc)
    z = sb_ref[...].reshape(s_n * p_n, t_n, c)
    back = dot_nt(jnp.concatenate(dscs, axis=1), wso_ref[...])
    back = back.reshape(z.shape) * slope(z * rows(c3_ref, 0, 4, 2) + rows(c3_ref, 1, 4, 2))
    dsb_ref[...] = back.reshape(dsb_ref.shape)
    sum_add(i, back, s1)
    sum_add(i, back * (z * rows(c3_ref, 2, 4, 2) - rows(c3_ref, 3, 4, 2)), s2)

    f_n = fb_ref.shape[1]
    scale, p_row, q_row = rows(c2_ref, 0, 0, 1), rows(q5_ref, 0, 16, 1), rows(q5_ref, 1, 16, 1)
    dfb = back_norm(scale, p_row, q_row, dfb_ref[...], fb_ref[...], m64_ref[0:1])
    dfb_low = flat(dfb).astype(BF16)
    add_to(i, gmid, dot_tn(dfb_low, flat(ftap_ref[...])))
    own = dfb_low.astype(F32)
    ends = []
    for ref in (hp_ref, hn_ref):
        small = back_norm(scale, p_row, q_row, ref[0, 0], ref[0, 1], ref[0, 0, p_n : p_n + 1, :])
        small = small.astype(BF16).astype(F32)
        ends.append(
            jnp.concatenate(
                [jnp.broadcast_to(small[p : p + 1, :], (f_n, LANES)) for p in range(p_n)], axis=0
            ).reshape(p_n, f_n, LANES)
        )
    before, after = shifted(own, ends[0], ends[1], f_n)
    taps = jnp.concatenate(
        [flat(after * m64_ref[2:3]), own, flat(before * m64_ref[1:2])], axis=1
    ).astype(BF16)
    z = fa_ref[...]
    back = dot(taps, wback_ref[...]).reshape(z.shape) * slope(
        z * rows(c1_ref, 0, 0, 1) + rows(c1_ref, 1, 0, 1)
    )
    dfa_ref[...] = back
    sum_add(i, back, t1)
    sum_add(i, back * (z * rows(c1_ref, 2, 0, 1) - rows(c1_ref, 3, 0, 1)), t2)

    @pl.when(i == STEPS - 1)
    def _():
        zero_ref(st_ref)
        put_rows(st_ref, 0, sum_end(s1))
        put_rows(st_ref, 2, sum_end(s2))
        put_rows(st_ref, 4, sum_end(t1))
        put_rows(st_ref, 5, sum_end(t2))

    def late():
        for k in range(3):
            gmid_ref[k * 32 : (k + 1) * 32, :] = fold_lanes(gmid[:, k * LANES : (k + 1) * LANES], s_n)
        tall, low_tall = gsc.shape[0], gso.shape[0]
        blocks = gsc.shape[1] // wide
        for n in range(blocks):
            cols = slice(n * wide, (n + 1) * wide)
            gw_ref[n * tall : (n + 1) * tall, :] = gsc[:, cols].astype(BF16)
            gs_ref[n * low_tall : (n + 1) * low_tall, :] = gso[:, cols].astype(BF16)
        if blocks * tall < gw_ref.shape[0]:
            gw_ref[blocks * tall :, :] = jnp.zeros((gw_ref.shape[0] - blocks * tall, wide), BF16)

    return late


def slow_grad(low, dsp, w_in, w_sc, out):
    s_n, p_n, t_n, c = low.shape
    small, d_sp = flat(low[...]), flat(dsp[...])
    for n in range(out.shape[-1] // c):
        part = slice(n * c, (n + 1) * c)
        d = dot_nt(d_sp, w_sc[part, :]) + dot_nt(small, w_in[part, :])
        out[:, :, :, part] = d.astype(BF16).reshape(s_n, p_n, t_n, c)


def fast_grad(low_ref, hn, df, dlow, m16, wlat, wfa, out, gs):
    s_n, p_n, t_n, c = low_ref.shape
    shape = (s_n * p_n, t_n, c)
    low = flat(low_ref[...])
    small = hn[0].astype(F32)
    ends = [
        jnp.broadcast_to(small[s * 8 + p : s * 8 + p + 1, :], (t_n, c)) for s in range(s_n) for p in range(p_n)
    ]
    ends = jnp.concatenate(ends, axis=0).reshape(shape)
    n = low.shape[0]
    moved = pltpu.roll(low.astype(F32), n - 1, 0).reshape(shape)
    place = lax.broadcasted_iota(jnp.int32, shape, 1)
    following = flat(jnp.where(place == t_n - 1, ends, moved) * m16[2:3, :, 0:1]).astype(BF16)
    own = dot_nt(low, wlat[2 * LANES : 5 * LANES, :])
    late = dot_nt(following, wlat[0 : 2 * LANES, :])
    gs[pl.ds(0, n, stride=4), :] = own[:, 0:LANES]
    gs[pl.ds(1, n, stride=4), :] = own[:, LANES : 2 * LANES]
    gs[pl.ds(2, n, stride=4), :] = own[:, 2 * LANES :] + late[:, 0:LANES]
    gs[pl.ds(3, n, stride=4), :] = late[:, LANES:]
    back = dot(flat(dlow[...]), wfa[...])
    for s in range(s_n):
        cols = slice(s * LANES, (s + 1) * LANES)
        total = flat(df[:, :, cols]) + back[:, cols] + gs[s * n : (s + 1) * n, :]
        out[s] = total.astype(BF16).reshape(out.shape[1:])


def each(first, last, body):
    def step(k, carry):
        body(k)
        return carry
    lax.fori_loop(first, last, step, 0)


NEAR = 4


class Cube:
    def __init__(self, ch, far):
        self.ch, self.far = ch, far
        self.p, self.f = lax.axis_index("path"), lax.axis_index("frames")
        self.q, self.r = lax.rem(self.f, NEAR), lax.div(self.f, NEAR)
        self.sibling = (1 - self.p, self.f)

    def q_of(self, k):
        low = (self.q % 2 + k % 2) % 2
        return (self.q // 2 + k // 2) % 2 * 2 + low

    def r_of(self, k):
        return lax.rem(self.r + k, self.far)

    def plane(self, k):
        return (self.p, self.r * NEAR + self.q_of(k))

    def line(self, k):
        return (self.p, self.r_of(k) * NEAR + self.q)

    def at(self, path, q, r):
        return pl.ds(pl.multiple_of(((path * NEAR + q) * self.far + r) * self.ch, 16), self.ch)


def remote(src, dst, sem, index, device):
    return pltpu.make_async_remote_copy(
        src_ref=src, dst_ref=dst, send_sem=sem.at[(0, *index)], recv_sem=sem.at[(1, *index)],
        device_id=device, device_id_type=MESH)


def rows_for(sizes, n):
    unit = 16 * sizes[0] * sizes[1]
    return -(-n // unit) * unit


class Stream:
    def __init__(self, sizes, rows_n, width):
        self.sizes, self.rows_n, self.width = sizes, rows_n, width
        self.far = sizes[1] // NEAR
        self.ch = rows_n // (sizes[0] * sizes[1])
        self.chunk = (self.ch, width)
        self.near_shape = (self.far, *self.chunk)
        quad = pltpu.VMEM((NEAR, *self.near_shape), BF16)
        quad_sems, line_sems = pltpu.SemaphoreType.DMA((2, NEAR, self.far)), pltpu.SemaphoreType.DMA((2, self.far))
        self.near_scratch = [quad, quad, quad, pltpu.VMEM(self.chunk, F32), quad_sems, quad_sems]
        self.line_scratch = [pltpu.VMEM(self.near_shape, BF16), pltpu.VMEM(self.chunk, F32), line_sems]
        self.share_scratch = [line_sems, quad_sems, quad_sems, pltpu.SemaphoreType.DMA]


class Near:
    def __init__(self, stream, x, out, scratch):
        self.x, self.out, self.far, self.c = x, out, stream.far, Cube(stream.ch, stream.far)
        self.land_a, self.buf_b, self.land_b, self.acc, self.sem_a, self.sem_b = scratch

    def pair(self, k, m):
        c = self.c
        return remote(self.x.at[c.at(1 - c.p, c.q_of(k), c.r_of(m + 1))], self.land_a.at[k, m], self.sem_a, (k, m), c.sibling)

    def plane(self, k, m):
        return remote(self.buf_b.at[k, m], self.land_b.at[k, m], self.sem_b, (k, m), self.c.plane(k))

    def start(self):
        def one(m):
            each(1, NEAR, lambda k: self.pair(k, m).start())
            self.pair(0, m).start()

        each(0, self.far, one)

    def add_pair(self, first, last):
        c = self.c

        def one(k, m):
            self.pair(k, m).wait_recv()
            mine = self.x[c.at(c.p, c.q_of(k), c.r_of(m + 1)), :]
            self.buf_b[k, m] = (mine.astype(F32) + self.land_a[k, m].astype(F32)).astype(BF16)
            self.plane(k, m).start()

        each(first, last, lambda m: each(1, NEAR, lambda k: one(k, m)))

    def add_plane(self, first, last, then=None):
        c = self.c

        def one(m):
            self.pair(0, m).wait_recv()
            self.acc[...] = self.x[c.at(c.p, c.q, c.r_of(m + 1)), :].astype(F32) + self.land_a[0, m].astype(F32)

            def more(k):
                self.plane(k, m).wait_recv()
                self.acc[...] += self.land_b[k, m].astype(F32)

            each(1, NEAR, more)
            self.out[m] = self.acc[...].astype(BF16)
            if then is not None:
                then(m)

        each(first, last, one)

    def end(self):
        each(0, self.far, lambda m: each(0, NEAR, lambda k: self.pair(k, m).wait_send()))
        each(0, self.far, lambda m: each(1, NEAR, lambda k: self.plane(k, m).wait_send()))


class Line:
    def __init__(self, stream, near, scratch):
        self.near, self.far, self.c = near, stream.far, Cube(stream.ch, stream.far)
        self.land, self.acc, self.sem = scratch

    def line(self, m):
        return remote(self.near.at[m], self.land.at[m], self.sem, (m,), self.c.line(m + 1))

    def start(self, first, last):
        each(first, min(last, self.far - 1), lambda m: self.line(m).start())

    def total(self):
        self.acc[...] = self.near[self.far - 1].astype(F32)

        def one(m):
            self.line(m).wait_recv()
            self.acc[...] += self.land[m].astype(F32)

        each(0, self.far - 1, one)
        return self.acc[...].astype(BF16)

    def end(self):
        each(0, self.far - 1, lambda m: self.line(m).wait_send())


class Share:
    def __init__(self, stream, res, out, scratch):
        self.res, self.out, self.far, self.c = res, out, stream.far, Cube(stream.ch, stream.far)
        self.cut = stream.ch // 32 * 16
        self.sem_d, self.sem_e, self.sem_f, self.sem_own = scratch

    def own(self):
        return self.out.at[self.c.at(self.c.p, self.c.q, self.c.r)]

    def keep(self):
        return pltpu.make_async_copy(self.res, self.own(), self.sem_own)

    def line_back(self, k):
        return remote(self.res, self.own(), self.sem_d, (k,), self.c.line(k))

    def part(self, q, m):
        return self.out.at[self.c.at(self.c.p, q, self.c.r_of(self.far - m))]

    def plane_back(self, k, m, src=None):
        dst = self.part(self.c.q, m)
        return remote(dst if src is None else src, dst, self.sem_e, (k, m), self.c.plane(k))

    def pair_back(self, k, m, src=None):
        dst = self.part(self.c.q_of(k), m)
        return remote(dst if src is None else src, dst, self.sem_f, (k, m), self.c.sibling)

    def start_line(self):
        each(1, self.far, lambda k: self.line_back(k).start())

    def half(self, k, m):
        c, cut = self.c, self.cut
        start = ((c.p * NEAR + c.q_of(k)) * self.far + c.r_of(self.far - m)) * c.ch
        rows_n = cut if k == 1 else c.ch - cut
        part = self.out.at[pl.ds(pl.multiple_of(start + (0 if k == 1 else cut), 16), rows_n)]
        return remote(part, part, self.sem_e, (3 if k == 1 else 0, m), c.plane(3 - k))

    def start_plane(self):
        each(1, NEAR - 1, lambda k: self.plane_back(k, 0, self.res).start())
        self.pair_back(0, 0, self.res).start()
        self.keep().start()

    def relay(self, first, last):
        def one(m):
            self.line_back(m).wait_recv()
            each(1, NEAR - 1, lambda k: self.plane_back(k, m).start())
            self.pair_back(0, m).start()

        each(first, last, one)

    def hand_on(self, first, last):
        def one(m):
            for k in (1, 2):
                self.plane_back(k, m).wait_recv()
                self.half(k, m).start()
                self.pair_back(k, m).start()

        each(first, last, one)

    def hand_across(self, first, last):
        def one(m):
            for k in (1, 2):
                self.half(k, m).wait_recv()
            self.pair_back(3, m).start()

        each(first, last, one)

    def end(self):
        each(0, self.far, lambda m: each(0, NEAR, lambda k: self.pair_back(k, m).wait()))
        self.keep().wait()
        each(1, self.far, lambda k: self.line_back(k).wait_send())
        each(0, self.far, lambda m: each(1, NEAR - 1, lambda k: self.plane_back(k, m).wait_send()))

        def sent(m):
            for k in (1, 2):
                self.half(k, m).wait_send()

        each(0, self.far, sent)


def k_tail(cfg, *refs):
    st_a, st_b, ex7, ex8, side = cfg
    it = iter(refs)

    def take(n):
        return [next(it) for _ in range(n)]

    hbm = take(13)
    x_slow, lact_src, taps_src = take(3)
    gb, c1, c2, c3, q6, m16, m64, g_fout, g_fmid = take(9)
    low_out, dlow_out, lat_low_out, gf, gw_in, gw_lat, q7, q8, hn, res_a, near_b = take(11)
    local = take(13)
    gw_a, dsb, sb, spad, wsp, sa, x_fast, dfa, fa, w_in, w_sc, dsp, lat = local
    pad, gsp, gin, low, dlow, gw_b, near_a, ends, s1, s2, t1, t2, sems, out_sems = take(14)
    x_part, taps_part, gsi, glat, wsp_turned, x_sems, taps_sems, lact_sem = take(8)
    near1, line1, near2 = take(len(st_a.near_scratch)), take(len(st_a.line_scratch)), take(len(st_b.near_scratch))
    scr7 = take(len(ex7.local) + len(ex7.work))
    scr8 = take(len(ex8.local) + len(ex8.work))
    n_in = w_in.shape[0]
    srcs = list(hbm)
    for k in (9, 10):
        srcs[k] = hbm[k].at[pl.ds(hbm[k].shape[0] - n_in, n_in)]
    loads = [pltpu.make_async_copy(src, dst, sems.at[k]) for k, (src, dst) in enumerate(zip(srcs, local))]
    count = exchange_hello(ex8)
    for k in (1, 2, 0, 4, 3, 5, 6, 7, 8, 9, 10, 11, 12):
        loads[k].start()
    near = Near(st_a, gw_a, near_a, near1)
    line = Line(st_a, near_a, line1)
    near_two = Near(st_b, gw_b, near_b, near2)
    far = st_a.far
    t_n, c = pad.shape[2], pad.shape[3]
    wide = side * t_n
    per = side // STEPS
    fill = m16[0:1, :, 0:1]

    def waits(*names):
        for k in names:
            loads[k].wait()

    waits(1, 2)
    scale, p_row, q_row = rows(c3, 0, 4, 2), rows(q6, 0, 0, 2), rows(q6, 1, 0, 2)
    zero_ref(pad)

    def fill_pad(h):
        part = pl.ds(h * wide, wide)
        d = back_norm(
            scale, p_row, q_row, dsb[part].reshape(side, t_n, c), sb[part].reshape(side, t_n, c), fill
        )
        pad[h + 1, 1 : side + 1] = d.astype(BF16)

    each(0, side, fill_pad)
    waits(0, 4)
    for k in range(9):
        wsp_turned[k * c : (k + 1) * c, :] = wsp[k * c : (k + 1) * c, :].T
    pl.semaphore_wait(pltpu.get_barrier_semaphore(), count)
    near.start()
    waits(3, 5, 6, 7, 8)
    f_n = x_fast.shape[2]
    p_n = x_fast.shape[1] // STEPS

    def spatial(i):
        h0 = i * per
        turned = flat(pad[pl.ds(h0 + 1, per), 1 : side + 1]).T
        blocks = []
        for a in range(3):
            for b in range(3):
                k = 3 * a + b
                patch = flat(spad[pl.ds(h0 + a, per), b : b + side])
                cols = slice(k * c, (k + 1) * c)
                gsp[:, cols] = jnp.where(i == 0, 0.0, gsp[:, cols]) + dot(turned, patch)
                blocks.append(flat(pad[pl.ds(h0 + 2 - a, per), 2 - b : 2 - b + side]))
        acc = dot(jnp.concatenate(blocks, axis=1), wsp_turned[...])
        span = pl.ds(i * per * wide, per * wide)
        z = sa[span]
        back = acc * slope(z * rows(c2, 0, 1, 2) + rows(c2, 1, 1, 2))
        dsb[span] = back
        unit = z * rows(c2, 2, 1, 2) - rows(c2, 3, 1, 2)
        sum_add(i, back.reshape(per * side, t_n, c), s1)
        sum_add(i, (back * unit).reshape(per * side, t_n, c), s2)
        f_span = pl.ds(i * p_n, p_n)
        small = back_norm(
            rows(c1, 0, 0, 1), rows(q6, 0, 2, 1), rows(q6, 1, 2, 1), dfa[f_span], fa[f_span], m64[0:1]
        ).astype(BF16)
        dlow[f_span] = small
        packed = jnp.concatenate([flat(x_fast[s, f_span]) for s in range(x_fast.shape[0])], axis=1)
        add_to(i, gin, dot_tn(flat(small), packed))
        pl.when(i == 0)(lambda: near.add_pair(0, far // 2))
        pl.when(i == 1)(lambda: near.add_pair(far // 2, far))

    each(0, STEPS, spatial)
    stats = scr7[0]
    zero_ref(stats)
    put_rows(stats, 0, sum_end(s1))
    put_rows(stats, 2, sum_end(s2))
    stores = [pltpu.make_async_copy(dlow, dlow_out, out_sems.at[0])]
    stores[0].start()

    def late():
        for k in range(9):
            gw_b[k * c : (k + 1) * c, :] = gsp[:, k * c : (k + 1) * c].T.astype(BF16)
        if 9 * c < gw_b.shape[0]:
            gw_b[9 * c :, :] = jnp.zeros((gw_b.shape[0] - 9 * c, c), BF16)
        n = g_fout.shape[0]
        gf[0:n, 0:LANES] = fold_wide(gin, x_fast.shape[0])
        gf[0:n, LANES:] = g_fout[...]
        gf[n : 2 * n, 0:LANES] = g_fmid[0:n, :]
        gf[n : 2 * n, LANES:] = g_fmid[n : 2 * n, :]
        gf[2 * n :, 0:LANES] = g_fmid[2 * n :, :]
        gf[2 * n :, LANES:] = jnp.zeros((n, LANES), F32)

    n_pos = side * side
    lact = spad.reshape(-1, t_n, c).at[pl.ds(0, n_pos)]
    lat_low = pad.reshape(-1, t_n, c).at[pl.ds(0, n_pos)]
    lact_load = pltpu.make_async_copy(lact_src, lact, lact_sem)
    lact_load.start()
    block = per * wide

    def x_load(i):
        return pltpu.make_async_copy(x_slow.at[pl.ds(i * block, block)], x_part.at[i % 2], x_sems.at[i % 2])

    def taps_load(i):
        return pltpu.make_async_copy(taps_src.at[pl.ds(i * block, block)], taps_part.at[i % 2], taps_sems.at[i % 2])

    for i in range(2):
        x_load(i).start()
        taps_load(i).start()
    exchange_run(ex7, [gb, c2], [q7], scr7, late)
    near_two.start()
    near.add_plane(0, far - 1, lambda m: line.line(m).start())
    near.add_plane(far - 1, far)
    waits(9, 10, 11, 12)
    scale7, p7, q7_row = rows(c2, 0, 1, 2), rows(q7, 0, 0, 2), rows(q7, 1, 0, 2)

    def join(i):
        span = pl.ds(i * block, block)
        shape = (per * side, t_n, c)
        d = back_norm(scale7, p7, q7_row, dsb[span].reshape(shape), sa[span].reshape(shape), fill)
        small = flat(d).astype(BF16)
        low[span] = small
        d = dot_nt(dsp[span], w_sc[...]) + dot_nt(small, w_in[...])
        z = lat[span]
        back = d * slope(z * rows(c1, 0, 1, 2) + rows(c1, 1, 1, 2))
        sb[span] = back
        unit = z * rows(c1, 2, 1, 2) - rows(c1, 3, 1, 2)
        sum_add(i, back.reshape(shape), t1)
        sum_add(i, (back * unit).reshape(shape), t2)
        pl.when(i == 2)(lambda: near_two.add_pair(0, far))

    each(0, STEPS, join)
    stores.append(pltpu.make_async_copy(low, low_out, out_sems.at[1]))
    stores[1].start()
    stats = scr8[0]
    zero_ref(stats)
    put_rows(stats, 0, sum_end(t1))
    put_rows(stats, 2, sum_end(t2))

    def post(q, sent):
        d = back_norm(rows(c1, 0, 1, 2), rows(q, 0, 0, 2), rows(q, 1, 0, 2), ends[0], ends[1], m16[0, 0:1, 0:1])
        sent[...] = d.astype(BF16)

    def in_step(i):
        x_load(i).wait()
        joined = jnp.concatenate([x_part[i % 2], flat(lact[pl.ds(i * per * side, per * side)])], axis=1)
        add_to(i, gsi, dot(low[pl.ds(i * block, block)].T, joined))
        pl.when(i + 2 < STEPS)(lambda: x_load(i + 2).start())

    def in_grad():
        zero_ref(ends)
        for s in range(x_fast.shape[0]):
            for step in range(STEPS):
                for p in range(p_n):
                    at = ((s * STEPS + step) * p_n + p) * t_n
                    ends[0, step, s * 8 + p : s * 8 + p + 1, :] = sb[at : at + 1, :]
                    ends[1, step, s * 8 + p : s * 8 + p + 1, :] = lat[at : at + 1, :]
        lact_load.wait()
        each(0, STEPS, in_step)
        for n in range(gsi.shape[1] // c):
            gw_in[n * c : (n + 1) * c, :] = gsi[:, n * c : (n + 1) * c].T.astype(BF16)

    def lat_step(i):
        scale8, p8, q8_row = rows(c1, 0, 1, 2), rows(q8, 0, 0, 2), rows(q8, 1, 0, 2)
        span = pl.ds(i * block, block)
        shape = (per * side, t_n, c)
        d = back_norm(scale8, p8, q8_row, sb[span].reshape(shape), lat[span].reshape(shape), fill).astype(BF16)
        lat_low[pl.ds(i * per * side, per * side)] = d
        taps_load(i).wait()
        add_to(i, glat, dot_tn(flat(d), taps_part[i % 2]))
        pl.when(i + 2 < STEPS)(lambda: taps_load(i + 2).start())

    def lat_grad():
        each(0, STEPS, lat_step)
        stores.append(pltpu.make_async_copy(lat_low, lat_low_out, out_sems.at[2]))
        stores[2].start()
        for k in range(glat.shape[1] // LANES):
            gw_lat[k * LANES : (k + 1) * LANES, :] = glat[:, k * LANES : (k + 1) * LANES].T.astype(BF16)

    exchange_run(ex8, [gb, c1], [q8, hn], scr8, in_grad, post, lat_grad)
    res_a[...] = line.total()
    near_two.add_plane(0, far)
    for store in stores:
        store.wait()
    line.end()
    near.end()
    near_two.end()


def back_tail(st_a, st_b, ex7, ex8, hbm, more, small, side, t_n, c):
    vm, anywhere = pl.BlockSpec(memory_space=pltpu.VMEM), pl.BlockSpec(memory_space=pl.ANY)
    inner, f_n = hbm[7].shape[:2]
    n = side * side * t_n
    c_cat, c_taps = more[0].shape[1] + c, more[2].shape[1]
    part = n // STEPS
    outs = [((n, c), BF16), ((inner, f_n, LANES), BF16), (more[1].shape, BF16), (small[-1].shape[0:1] + (2 * LANES,), F32),
            ((c_cat, c), BF16), ((c_taps, c), BF16),
            *ex7.outs, *ex8.outs, (st_a.chunk, BF16), (st_b.near_shape, BF16)]
    local = [pltpu.VMEM((c,) + a.shape[1:] if k in (9, 10) else a.shape, a.dtype) for k, a in enumerate(hbm)]
    width = hbm[6].shape[0] * hbm[6].shape[3]
    scratch = [
        pltpu.VMEM((side + 2, side + 2, t_n, c), BF16), pltpu.VMEM((c, 9 * c), F32), pltpu.VMEM((LANES, width), F32),
        pltpu.VMEM((n, c), BF16), pltpu.VMEM((inner, f_n, LANES), BF16), pltpu.VMEM((st_b.rows_n, c), BF16),
        pltpu.VMEM(st_a.near_shape, BF16), pltpu.VMEM((2, *ex8.post), F32), *[pltpu.VMEM((t_n, c), F32)] * 4,
        pltpu.SemaphoreType.DMA((len(hbm),)), pltpu.SemaphoreType.DMA((3,)),
        pltpu.VMEM((2, part, c_cat - c), BF16), pltpu.VMEM((2, part, c_taps), BF16), pltpu.VMEM((c, c_cat), F32),
        pltpu.VMEM((c, c_taps), F32), pltpu.VMEM((9 * c, c), BF16), pltpu.SemaphoreType.DMA((2,)), pltpu.SemaphoreType.DMA((2,)), pltpu.SemaphoreType.DMA,
        *st_a.near_scratch, *st_a.line_scratch, *st_b.near_scratch, *ex7.local, *ex7.work, *ex8.local, *ex8.work,
    ]
    return pl.pallas_call(
        functools.partial(k_tail, (st_a, st_b, ex7, ex8, side)),
        out_shape=[jax.ShapeDtypeStruct(s, d) for s, d in outs],
        in_specs=[anywhere] * (len(hbm) + len(more)) + [vm] * len(small),
        out_specs=[anywhere] * 3 + [vm] * (len(outs) - 3),
        scratch_shapes=[*local, *scratch],
        compiler_params=pltpu.CompilerParams(collective_id=ex8.cid, has_side_effects=True, vmem_limit_bytes=VMEM_LIMIT),
        name="tail",
    )(*hbm, *more, *small)


def final_kernel(cfg, *refs):
    first, second, third, both, offsets, n_hbm, n_small = cfg
    it = iter(refs)

    def take(n):
        return [next(it) for _ in range(n)]

    hbm, small, (out_a, out_bc, gx_out, fast_out) = take(n_hbm), take(n_small), take(4)
    res_a, near_b, *parts, hn, m16, wlat, wfa = small
    loaded = take(n_hbm)
    low, dsp, w_in, w_sc, lat_low, df, dlow = loaded
    x, near_c, res, gx, fast_gx, gs, sems, gx_sems, fast_sems = take(9)
    share_a = Share(first, res_a, out_a, take(len(first.share_scratch)))
    line_b = Line(second, near_b, take(len(second.line_scratch)))
    near = Near(third, x, near_c, take(len(third.near_scratch)))
    line_c = Line(third, near_c, take(len(third.line_scratch)))
    share = Share(both, res, out_bc, take(len(both.share_scratch)))
    far, c = first.far, near.c
    barrier = pltpu.get_barrier_semaphore()
    loads = [pltpu.make_async_copy(a, b, sems.at[k]) for k, (a, b) in enumerate(zip(hbm, loaded))]

    def greet(device):
        pl.semaphore_signal(barrier, inc=1, device_id=device, device_id_type=MESH)

    greet(c.sibling)
    each(1, NEAR, lambda k: greet(c.plane(k)))
    each(1, far, lambda k: greet(c.line(k)))
    for load in loads:
        load.start()
    for ref, first_row, end in zip(parts, offsets, offsets[1:]):
        x[first_row:end, :] = ref[...].astype(BF16)
    if end < x.shape[0]:
        x[end:, :] = jnp.zeros((x.shape[0] - end, x.shape[1]), BF16)
    pl.semaphore_wait(barrier, NEAR + far - 1)

    near.start()
    line_b.start(0, far)
    share_a.start_line()
    p_n = dlow.shape[0] // STEPS

    def gx_store(i):
        part = pl.ds(i * p_n, p_n)
        return pltpu.make_async_copy(gx.at[:, part], gx_out.at[:, part], gx_sems.at[i])

    def slow_step(i):
        part = pl.ds(i * p_n, p_n)
        slow_grad(low.at[:, part], dsp.at[:, part], w_in, w_sc, gx.at[:, part])
        gx_store(i).start()

    def fast_store(i):
        part = pl.ds(i * p_n, p_n)
        return pltpu.make_async_copy(fast_gx.at[:, part], fast_out.at[:, part], fast_sems.at[i])

    def fast_step(i):
        part = pl.ds(i * p_n, p_n)
        fast_grad(lat_low.at[:, part], hn.at[pl.ds(i, 1)], df.at[part], dlow.at[part], m16, wlat, wfa,
                  fast_gx.at[:, part], gs)
        fast_store(i).start()

    near.add_pair(0, far)
    share_a.start_plane()
    for k in (0, 1, 2, 3):
        loads[k].wait()
    each(0, 1, slow_step)
    res[0 : second.ch, :] = line_b.total()
    share_a.relay(1, far)
    each(1, 4, slow_step)
    near.add_plane(0, far - 1, lambda m: line_c.line(m).start())
    near.add_plane(far - 1, far)
    share_a.hand_on(0, far // 2)
    each(4, STEPS, slow_step)
    res[second.ch :, :] = line_c.total()
    share.start_line()
    share.start_plane()
    for k in range(4, n_hbm):
        loads[k].wait()
    share_a.hand_on(far // 2, far)
    each(0, 2, fast_step)
    share.relay(1, far)
    share_a.hand_across(0, far)
    each(2, 4, fast_step)
    share.hand_on(0, far // 2)
    each(4, STEPS, fast_step)
    share.hand_on(far // 2, far)
    share.hand_across(0, far)
    share_a.end()
    share.end()
    line_b.end()
    line_c.end()
    near.end()
    each(0, STEPS, lambda i: gx_store(i).wait())
    each(0, STEPS, lambda i: fast_store(i).wait())


def final_sum(sizes, cid, first, second, hbm, small, gx, fast_gx, heights):
    width = first.width
    offsets = tuple(sum(heights[:k]) for k in range(len(heights) + 1))
    third = Stream(sizes, rows_for(sizes, offsets[-1]), width)
    both = Stream(sizes, second.rows_n + third.rows_n, width)
    vm, anywhere = pl.BlockSpec(memory_space=pltpu.VMEM), pl.BlockSpec(memory_space=pl.ANY)
    low, dlow = hbm[0], hbm[6]
    s_n, p_n, f_n = low.shape[0], low.shape[1] // STEPS, dlow.shape[1]
    out_a, out_bc, gx, fast_gx = pl.pallas_call(
        functools.partial(final_kernel, (first, second, third, both, offsets, len(hbm), len(small))),
        out_shape=[jax.ShapeDtypeStruct(s, BF16) for s in ((first.rows_n, width), (both.rows_n, width), gx, fast_gx)],
        in_specs=[anywhere] * len(hbm) + [vm] * len(small),
        out_specs=[anywhere] * 4,
        scratch_shapes=[
            *[pltpu.VMEM(a.shape, a.dtype) for a in hbm],
            pltpu.VMEM((third.rows_n, width), BF16), pltpu.VMEM(third.near_shape, BF16), pltpu.VMEM(both.chunk, BF16),
            pltpu.VMEM(gx, BF16), pltpu.VMEM(fast_gx, BF16), pltpu.VMEM((s_n * p_n * f_n, LANES), F32),
            pltpu.SemaphoreType.DMA((len(hbm),)), pltpu.SemaphoreType.DMA((STEPS,)), pltpu.SemaphoreType.DMA((STEPS,)),
            *first.share_scratch, *second.line_scratch, *third.near_scratch, *third.line_scratch, *both.share_scratch,
        ],
        compiler_params=pltpu.CompilerParams(collective_id=cid, has_side_effects=True, vmem_limit_bytes=VMEM_LIMIT),
        name="final_sum",
    )(*hbm, *small)
    return out_a, out_bc.reshape(-1, both.ch, width), gx, fast_gx


def k_unpack(pieces, cut, *refs):
    (src_a, src_b, q4, q5, q6, q7, q8), held, refs = refs[:7], refs[7:10], refs[10:]
    outs, (low_a, low_b, low_c, wide, line, *kept, sem_a, sem_b, sem_out, sem_held) = refs[:-12], refs[-12:]
    outs, given = outs[:-3], outs[-3:]

    def moves(srcs, dsts, way):
        return [
            pltpu.make_async_copy(a.at[pl.ds(k, 1)], b.at[pl.ds(k, 1)], sem_held.at[way, n, k])
            for n, (a, b) in enumerate(zip(srcs, dsts))
            for k in range(a.shape[0])
        ]

    passes_in, passes = moves(held, kept, 0), moves(kept, given, 1)
    outs, (gains_out, biases_out, in_out, mid_out, out_out) = outs[:-5], outs[-5:]
    lows = (low_a, low_b, low_c)
    flats = [low_a, low_b.reshape(-1, low_b.shape[-1]), low_c.reshape(-1, low_c.shape[-1])]
    starts = [sum(p[2] for p in pieces[:k]) for k in range(len(pieces))]

    def fetch_a(k):
        _, row, height, _, _ = pieces[k]
        return pltpu.make_async_copy(src_a.at[pl.ds(row, height)], low_a.at[pl.ds(row, height)], sem_a.at[k])

    def fetch_b(k):
        part = src_b.at[:, pl.ds(0, cut)] if k == 1 else src_b.at[:, pl.ds(cut, src_b.shape[1] - cut)]
        return pltpu.make_async_copy(part, lows[k], sem_b.at[k])

    def store(k):
        _, _, height, out, col = pieces[k]
        part = outs[out] if col is None else outs[out].at[:, pl.ds(col, wide.shape[1])]
        return pltpu.make_async_copy(wide.at[pl.ds(starts[k], height)], part, sem_out.at[k])

    for k, piece in enumerate(pieces):
        if piece[0] == 0:
            fetch_a(k).start()
    for k in (1, 2):
        fetch_b(k).start()
    for move in passes_in:
        move.start()
    seen = 0
    for k, (src, row, height, _, _) in enumerate(pieces):
        if src == 0:
            fetch_a(k).wait()
        elif src != seen:
            fetch_b(src).wait()
            seen = src
        wide[starts[k] : starts[k] + height, :] = flats[src][row : row + height, :].astype(F32)
        store(k).start()
    for move_in, move in zip(passes_in, passes):
        move_in.wait()
        move.start()
    lane = lax.broadcasted_iota(jnp.int32, (1, LANES), 1)
    left = lane < LANES // 2
    for slab, out in ((3, gains_out), (2, biases_out)):
        at = 0
        for q, first, count in ((q4, 0, 1), (q8, 0, 2), (q7, 0, 2), (q6, 0, 2), (q5, 0, 16)):
            line[at : at + count, :] = q[slab, first : first + count, :]
            at += count
        half = pltpu.roll(line[0:at, :], LANES // 2, 1)
        head = jnp.where(lane < LANES // 4, q6[slab, 2:3, :], q5[slab, 16:17, :])
        out[0:1, :] = jnp.where(left, head, half[0:1])
        out[1:at, :] = jnp.where(left, half[0 : at - 1], half[1:at])
        out[at : at + 1, :] = jnp.where(left, half[at - 1 : at], 0.0)
    a = in_out.shape[0]
    last = sum(p[2] for p in pieces if p[0] == 2)
    small = flats[2][last : last + 3 * a, :]
    in_out[...] = small[0:a, 0:LANES].astype(F32)
    out_out[...] = small[0:a, LANES:].astype(F32)
    eye = (lax.broadcasted_iota(jnp.int32, (a, a), 0) == lax.broadcasted_iota(jnp.int32, (a, a), 1)).astype(BF16)
    for k, (row, col) in enumerate(((a, 0), (a, LANES), (2 * a, 0))):
        mid_out[k] = dot_tn(small[row : row + a, col : col + LANES], eye)[0:a, :]
    for k in range(len(pieces)):
        store(k).wait()
    for move in passes:
        move.wait()


def unpack(src_a, src_b, cut, pieces, shapes, small_shapes, norm_sums, held):
    hbm, vm = pl.BlockSpec(memory_space=pl.ANY), pl.BlockSpec(memory_space=pltpu.VMEM)
    n, _, width = src_b.shape
    return pl.pallas_call(
        functools.partial(k_unpack, pieces, cut),
        out_shape=[jax.ShapeDtypeStruct(s, F32) for s in (*shapes, *small_shapes)]
        + [jax.ShapeDtypeStruct(a.shape, a.dtype) for a in held],
        in_specs=[hbm] * 2 + [vm] * len(norm_sums) + [hbm] * len(held),
        out_specs=[hbm] * len(shapes) + [vm] * len(small_shapes) + [hbm] * len(held),
        scratch_shapes=[
            pltpu.VMEM(src_a.shape, BF16),
            pltpu.VMEM((n, cut, width), BF16),
            pltpu.VMEM((n, src_b.shape[1] - cut, width), BF16),
            pltpu.VMEM((sum(p[2] for p in pieces), width), F32),
            pltpu.VMEM((24, LANES), F32),
            *[pltpu.VMEM(a.shape, a.dtype) for a in held],
            pltpu.SemaphoreType.DMA((len(pieces),)),
            pltpu.SemaphoreType.DMA((3,)),
            pltpu.SemaphoreType.DMA((len(pieces),)),
            pltpu.SemaphoreType.DMA((2, len(held), held[0].shape[0])),
        ],
        compiler_params=pltpu.CompilerParams(vmem_limit_bytes=VMEM_LIMIT),
        name="unpack",
    )(src_a, src_b, *norm_sums, *held)


def small_set_up(fill_ref, clip_ref, norm_ref, wfi_ref, wfm_ref, wfo_ref,
                 gb_ref, m16_ref, m64_ref, wfa_ref, wmid_ref, wback_ref, wout_ref, s_n, t_n):
    length = lax.axis_size("frames")
    total = lax.axis_size("path") * length
    me = lax.axis_index("path") * length + lax.axis_index("frames")
    lane = lax.broadcasted_iota(jnp.int32, (1, LANES), 1)
    for k in range(2):
        half = pltpu.roll(norm_ref[k], LANES // 2, 1)
        main = jnp.where(lane < LANES // 2, half[0:23], half[1:24])
        for j in range(2):
            v = jnp.where(lane // 32 == j, norm_ref[k, 0:1, :], 0.0)
            v = v + pltpu.roll(v, 64, 1)
            gb_ref[k, j : j + 1, :] = v + pltpu.roll(v, 32, 1)
        for j in range(4):
            gb_ref[k, 2 + j : 3 + j, :] = main[0:1]
        gb_ref[k, 6:28, :] = main[1:23]
        gb_ref[k, 28:32, :] = jnp.zeros((4, LANES), F32)

    def row(value):
        return jnp.full((1, LANES), value, F32)

    last = jnp.where(me < total - 1, 1.0, 0.0)
    link = [jnp.where(clip_ref[t] >= 1, 1.0, 0.0) for t in range(t_n)]
    for t in range(t_n):
        filled = row(fill_ref[t].astype(F32))
        after = row(link[t + 1] if t + 1 < t_n else last)
        m16_ref[0, t : t + 1, :] = filled
        m16_ref[1, t : t + 1, :] = row(link[t])
        m16_ref[2, t : t + 1, :] = after
        m64_ref[0, 4 * t : 4 * t + 4, :] = jnp.broadcast_to(filled, (4, LANES))
        m64_ref[1, 4 * t : 4 * t + 1, :] = row(link[t])
        m64_ref[1, 4 * t + 1 : 4 * t + 4, :] = jnp.ones((3, LANES), F32)
        m64_ref[2, 4 * t : 4 * t + 3, :] = jnp.ones((3, LANES), F32)
        m64_ref[2, 4 * t + 3 : 4 * t + 4, :] = after

    zero_ref(wfa_ref)
    zero_ref(wout_ref)
    a = wfi_ref.shape[0]
    for s in range(s_n):
        wfa_ref[s * a : (s + 1) * a, s * LANES : (s + 1) * LANES] = wfi_ref[...]
        wout_ref[s * a : (s + 1) * a, s * LANES : (s + 1) * LANES] = wfo_ref[...]
    tall = (LANES, a)
    spread = (lax.broadcasted_iota(jnp.int32, tall, 0) % a == lax.broadcasted_iota(jnp.int32, tall, 1)).astype(BF16)
    square = (LANES, LANES)
    diag = lax.broadcasted_iota(jnp.int32, square, 0) // a == lax.broadcasted_iota(jnp.int32, square, 1) // a
    for k in range(3):
        left = dot(spread, wfm_ref[k]).astype(BF16)
        wmid_ref[k * LANES : (k + 1) * LANES, :] = jnp.where(diag, dot_nt(left, spread), 0.0).astype(BF16)
        right = dot_nt(spread, wfm_ref[k]).astype(BF16)
        wback_ref[k * LANES : (k + 1) * LANES, :] = jnp.where(diag, dot_nt(right, spread), 0.0).astype(BF16)


def per_device(slow_input, fast_input, clip_offset, fill, w_fast_in, w_fast_mid, w_fast_out, w_lateral,
               w_slow_in, w_slow_mid, w_slow_out, w_shortcut, gains, biases, slow_cot, fast_cot):
    sizes = (lax.axis_size("path"), lax.axis_size("frames"))
    t_n, side, _, c_slow = slow_input.shape
    f_n, c_fast = fast_input.shape[0], fast_input.shape[3]
    in_fast, in_slow, c_lat = w_fast_in.shape[1], w_slow_in.shape[1], w_lateral.shape[2]
    pixels = side * side
    groups = LANES // in_fast
    inner = pixels // groups
    p_n = inner // STEPS

    def slow_view(a):
        return jnp.transpose(a, (1, 2, 0, 3)).reshape(groups, inner, t_n, a.shape[3])

    def fast_view(a):
        return jnp.transpose(a, (1, 2, 0, 3)).reshape(groups, inner, f_n, a.shape[3])

    def unview(a):
        return jnp.transpose(a.reshape(side, side, a.shape[2], a.shape[3]), (2, 0, 1, 3))

    x_slow, cot_slow = slow_view(slow_input), slow_view(slow_cot)
    x_fast, cot_fast = fast_view(fast_input), fast_view(fast_cot)

    norms = jnp.stack([gains, biases])
    norms = jnp.pad(norms, ((0, 0), (0, -norms.shape[1] % (8 * LANES)))).reshape(2, -1, LANES)
    wlat = w_lateral.reshape(-1, c_lat)
    wsp = w_slow_mid.reshape(-1, in_slow)

    sl = (groups, inner, t_n)
    fp = (inner, f_n)

    def slow_out(width, dtype):
        return out_blocked(sl + (width,), dtype, 1, p_n)

    def fast_out(width, dtype):
        return out_blocked(fp + (width,), dtype, 0, p_n)

    def sb_(a):
        return blocked(a, 1, p_n)

    def fb_(a):
        return blocked(a, 0, p_n)

    def stat(n):
        return out_whole((pad8(n), LANES), F32)

    def acc(rows_n, width, count):
        return [pltpu.VMEM((rows_n, width), F32)] * count

    small = (STEPS, 8, LANES)

    sems7 = pltpu.SemaphoreType.DMA((STEPS,))
    exs = [
        Exchange(sizes, 1, 7, fwd=(("lane4", 0, 1), ("plain", 6, 2)), up=small, down=small),
        Exchange(sizes, 1, 23, fwd=(("lane4", 1, 1), ("plain", 8, 2), ("plain", 20, 8))),
    ]
    kept = [
        (fp + (LANES,), F32), (sl + (c_lat,), F32), (sl + (5 * c_fast,), BF16), (sl + (c_lat,), BF16),
        (fp + (3 * LANES,), BF16), (sl + (in_slow,), F32), (sl + (c_slow,), F32), (fp + (LANES,), F32),
    ]
    ready = [((2, 32, LANES), F32), ((3, t_n, LANES), F32), ((3, f_n, LANES), F32), ((LANES, groups * c_fast), BF16),
             ((3 * LANES, LANES), BF16), ((3 * LANES, LANES), BF16), ((LANES, groups * c_fast), BF16)]
    ends = (STEPS, groups * 8, 2 * c_fast)
    fa, lat, taps, lact, ftap, sa, sp, fb, gb, m16, m64, wfa, wmid, wback, wout, c1, hp, hn, c2 = run_resident(
        functools.partial(k_front, exs), exs,
        [x_fast, wlat, x_slow, w_slow_in, w_shortcut],
        [fill, clip_offset, norms, w_fast_in.T, w_fast_mid, w_fast_out],
        kept, [*[(*k, True) for k in kept], *[(*k, False) for k in ready]],
        [pltpu.VMEM((groups * p_n * f_n, c_fast), F32), *acc(f_n, LANES, 2), *acc(t_n, c_lat, 2), *acc(t_n, in_slow, 2),
         *acc(t_n, c_slow, 2), *acc(f_n, LANES, 2), pltpu.SemaphoreType.DMA((8,)), sems7,
         pltpu.VMEM((pixels * t_n, c_fast), F32), pltpu.VMEM(ends, F32), pltpu.VMEM(ends, BF16), pltpu.VMEM(ends, BF16),
         pltpu.SemaphoreType.DMA((2,))],
        "front",
        scalars=2,
    )

    exs = [
        Exchange(sizes, 3, 13, fwd=(("row4", 2, 4), ("plain", 10, 2))),
        Exchange(sizes, 3, 25, fwd=(("plain", 12, 8),), bwd=(("row4", 0, 0, 2, 4, 0, 4),)),
    ]
    kept = [
        ((side + 2, side + 2, t_n, in_slow), BF16), ((pixels, t_n, in_slow), F32), (fp + (LANES,), BF16),
        ((pixels, t_n, in_slow), BF16), ((groups, inner, f_n, c_fast), BF16), (fp + (groups * c_fast,), F32),
    ]
    pad, sb, fact, sact, fast_y, df, c3, c4, q4 = run_resident(
        functools.partial(k_middle, exs), exs,
        [sa.reshape(side, side, t_n, in_slow), fb, wsp, w_slow_out, x_fast, cot_fast], [gb, c2, m16, m64, wout],
        kept, [(*k, True) for k in kept],
        [*acc(t_n, in_slow, 2), *acc(f_n, groups * c_fast, 2), *acc(t_n, c_slow, 2), *acc(f_n, groups * c_fast, 2),
         pltpu.SemaphoreType.DMA((4,)), sems7, sems7],
        "middle",
    )
    sb4, sact = sb.reshape(sl + (in_slow,)), sact.reshape(sl + (in_slow,))

    halo_pair = out_blocked((STEPS, 2, 8, LANES), F32, 0, 1)
    slow_y, dy, dfb, g_fout, up, down, st = call(
        k_out,
        [sb_(sact), sb_(sp), sb_(cot_slow), fb_(df), fb_(fact), fb_(fb), whole(c2), whole(c3), whole(c4), whole(q4),
         whole(m16), whole(m64), whole(w_slow_out), whole(wout)],
        [slow_out(c_slow, BF16), slow_out(c_slow, F32), fast_out(LANES, F32),
         out_whole((in_fast, c_fast), F32), halo_pair, halo_pair, stat(26)],
        [*acc(t_n, c_slow, 3), *acc(f_n, LANES, 2), *acc(LANES, groups * c_fast, 1)],
        "out",
    )
    pair = (STEPS, 2, 8, LANES)
    ex5 = Exchange(
        sizes, 6, 26,
        bwd=(("plain", 0, 0, 12, 8, 0, 8), ("plain", 1, 3, 20, 8, 0, 16), ("lane4", 1, 0, 1, 1, 24, 25)),
        up=pair, down=pair,
    )
    c_cat = w_slow_in.shape[0]
    width = in_slow
    stream_a = Stream(sizes, rows_for(sizes, c_cat * c_slow // width), width)
    stream_b = Stream(sizes, rows_for(sizes, 9 * in_slow), width)
    gw_short, gw_sout, dsp, dsb, dfa, g_fmid, q6, q5 = call(
        k_back_out,
        [sb_(x_slow), sb_(lact), sb_(dy), sb_(sp), sb_(sact), sb_(sb4), fb_(dfb), fb_(fb), fb_(fa), fb_(ftap), 1, 2,
         whole(c1), whole(c2), whole(c3), whole(c4), 0, whole(m16), whole(m64), whole(w_slow_out), whole(wback)],
        [out_whole((stream_a.rows_n, width), BF16), out_whole((c_slow, width), BF16), slow_out(c_slow, BF16),
         slow_out(in_slow, F32), fast_out(LANES, F32), out_whole((3 * in_fast, LANES), F32), STAT],
        [*acc(t_n, in_slow, 2), *acc(f_n, LANES, 2), *acc(c_cat, c_slow, 1), *acc(in_slow, c_slow, 1),
         *acc(LANES, 3 * LANES, 1)],
        "back_out",
        Exchange(sizes, 6, 6, bwd=(("plain", 0, 4, 10, 2, 0, 2), ("lane4", 1, 0, 0, 1, 4, 5))),
        [gb, c3, c1],
        ex5,
        [st, up, down, gb, c4, c2],
    )

    def rows2(a):
        return a.reshape(-1, a.shape[-1])

    dsa_low, dfa_low, lat_low, gw_fast, gw_in, gw_lat, q7, q8, hn, res_a, near_b = back_tail(
        stream_a, stream_b,
        Exchange(sizes, 7, 4, bwd=(("plain", 0, 1, 8, 2, 0, 2),)),
        Exchange(sizes, 7, 4, bwd=(("plain", 0, 1, 6, 2, 0, 2),), post=(STEPS, groups * 8, c_lat)),
        [gw_short, rows2(dsb), rows2(sb4), pad, wsp, rows2(sa), x_fast, dfa, fa, w_slow_in, w_shortcut, rows2(dsp), rows2(lat)],
        [rows2(x_slow), lact.reshape(pixels, t_n, c_lat), rows2(taps)],
        [gb, c1, c2, c3, q6, m16, m64, g_fout, g_fmid],
        side, t_n, in_slow,
    )
    heights = (gw_sout.shape[0], c_cat, 5 * c_fast, gw_fast.shape[0])
    sum_a, sum_bc, slow_gx, fast_gx = final_sum(
        sizes, 9, stream_a, stream_b,
        [dsa_low.reshape(sl + (in_slow,)), dsp, w_slow_in, w_shortcut, lat_low.reshape(sl + (c_lat,)), df, dfa_low],
        [res_a, near_b, gw_sout, gw_in, gw_lat, gw_fast, hn, m16, wlat, wfa],
        sl + (c_slow,), (groups, inner, f_n, c_fast), heights,
    )
    blocks = c_slow // in_slow
    pieces = [(0, n * c_cat, c_cat, 0, n * width) for n in range(blocks)]
    pieces.append((1, 0, 9 * in_slow, 2, None))
    at = 0
    for n in range(blocks):
        pieces.append((2, at, in_slow, 1, n * width))
        at += in_slow
    for out, tall in ((3, c_cat), (4, 5 * c_fast)):
        pieces.append((2, at, tall, out, None))
        at += tall
    norm_rows = -(-gains.shape[0] // LANES)
    g_short, g_sout, gw_mid, gw_in, gw_lat, gains_grad, biases_grad, g_fin, g_fmid, g_fout, *held = unpack(
        sum_a, sum_bc, stream_b.ch, tuple(pieces),
        [(c_cat, c_slow), (in_slow, c_slow), (9 * in_slow, width), (c_cat, in_slow), wlat.shape],
        [(norm_rows, LANES), (norm_rows, LANES), (in_fast, c_fast), w_fast_mid.shape, (in_fast, c_fast)],
        [q4, q5, q6, q7, q8],
        [slow_gx, fast_gx, fast_y],
    )
    slow_gx, fast_gx, fast_y = held
    grads = (
        g_fin.T,
        g_fmid,
        g_fout,
        gw_lat.reshape(w_lateral.shape),
        gw_in,
        gw_mid.reshape(w_slow_mid.shape),
        g_sout,
        g_short,
    )
    return (
        unview(slow_y),
        unview(fast_y),
        unview(slow_gx),
        unview(fast_gx),
        *grads,
        gains_grad.reshape(-1)[: gains.shape[0]],
        biases_grad.reshape(-1)[: biases.shape[0]],
    )


def solution(mesh):
    frames = P(("path", "frames"), None, None, None)
    in_specs = (frames, frames, P(AXES), P(AXES), *([P()] * 10), frames, frames)
    out_specs = (*([frames] * 4), *([P()] * 10))
    return jax.shard_map(per_device, mesh=mesh, in_specs=in_specs, out_specs=out_specs, check_vma=False)
```

```python
import functools

import jax
import jax.numpy as jnp
from jax import lax
from jax.experimental import pallas as pl
from jax.experimental.pallas import tpu as pltpu
from jax.sharding import PartitionSpec as P

norm_eps = 1e-05
F32 = jnp.float32
BF16 = jnp.bfloat16
MESH = pl.DeviceIdType.MESH
AXES = ("path", "frames")
STEPS = 7
LANES = 128
VMEM_LIMIT = 60 * 1024 * 1024


def dot(a, b):
    return jnp.dot(a, b, preferred_element_type=F32)


def dot_nt(a, b):
    return lax.dot_general(a, b, (((1,), (1,)), ((), ())), preferred_element_type=F32)


def dot_tn(a, b):
    return lax.dot_general(a, b, (((0,), (0,)), ((), ())), preferred_element_type=F32)


def sig(v):
    return 0.5 * jnp.tanh(0.5 * v) + 0.5


def slope(v):
    s = sig(v)
    return s + (v * s) * (1.0 - s)


def rows(ref, slab, first, count):
    parts = [ref[slab, first + j : first + j + 1, :] for j in range(count)]
    return parts[0] if count == 1 else jnp.concatenate(parts, axis=1)


def put_rows(ref, first, value):
    for j in range(value.shape[1] // LANES):
        ref[first + j : first + j + 1, :] = value[:, j * LANES : (j + 1) * LANES]


def zero_ref(ref):
    ref[...] = jnp.zeros(ref.shape, ref.dtype)


def spread_add(step, z, mean_ref, m2_ref, cols=slice(None)):
    count = z.shape[0]
    mean = jnp.sum(z, axis=0) * (1.0 / count)
    d = z - mean
    m2 = jnp.sum(d * d, axis=0)
    first = step == 0
    old_mean = jnp.where(first, 0.0, mean_ref[:, cols])
    old_m2 = jnp.where(first, 0.0, m2_ref[:, cols])
    done = jnp.full((1, z.shape[-1]), step, jnp.int32).astype(F32)
    share = 1.0 / (done + 1.0)
    delta = mean - old_mean
    mean_ref[:, cols] = old_mean + delta * share
    m2_ref[:, cols] = old_m2 + m2 + delta * delta * (done * share * count)


def spread_end(mean_ref, m2_ref, fill, positions):
    filled = jnp.sum(fill, axis=0, keepdims=True)
    mean = jnp.sum(fill * mean_ref[...], axis=0, keepdims=True) / jnp.maximum(filled, 1.0)
    d = mean_ref[...] - mean
    m2 = jnp.sum(fill * (m2_ref[...] + positions * (d * d)), axis=0, keepdims=True)
    return mean, m2


def sum_add(step, value, ref, cols=slice(None)):
    ref[:, cols] = jnp.where(step == 0, 0.0, ref[:, cols]) + jnp.sum(value, axis=0)


def sum_end(ref):
    return jnp.sum(ref[...], axis=0, keepdims=True)


def pad8(n):
    return -(-n // 8) * 8


def exchange_peers(cfg):
    paths, length = lax.axis_size("path"), lax.axis_size("frames")
    near = 4
    g1, g2 = paths * near, length // near
    me_p, me_f = lax.axis_index("path"), lax.axis_index("frames")
    me = me_p * length + me_f
    total = paths * length
    r1 = me_p * near + lax.rem(me_f, near)
    r2 = lax.div(me_f, near)

    def peer1(k):
        r = lax.rem(r1 + k, g1)
        return (lax.div(r, near), r2 * near + lax.rem(r, near))

    def peer2(k):
        r = lax.rem(r2 + k, g2)
        return (me_p, r * near + lax.rem(me_f, near))

    def split(index):
        return (lax.div(index, length), lax.rem(index, length))

    nxt, prv = split(lax.rem(me + 1, total)), split(lax.rem(me + total - 1, total))
    return g1, g2, r1, r2, peer1, peer2, nxt, prv


def exchange_hello(cfg):
    g1, g2, _, _, peer1, peer2, nxt, prv = exchange_peers(cfg)
    peers = [peer1(k) for k in range(1, g1)] + [peer2(k) for k in range(1, g2)]
    if cfg.greets:
        peers += [nxt, prv]
    for peer in peers:
        pl.semaphore_signal(pltpu.get_barrier_semaphore(), inc=1, device_id=peer, device_id_type=MESH)
    return len(peers)


def exchange_run(cfg, ins, outs, scratch, meanwhile=None, post=None, after=None, between=None):
    fwd, bwd = cfg.fwd, cfg.bwd
    nf = sum(c[2] for c in fwd)
    nb = max((c[6] + c[4] for c in bwd), default=0)
    n_row = 2 * nf + nb
    stats_ref, up_ref, down_ref = scratch[:3]
    gb_ref, *coef_refs = ins
    outs = list(outs)
    coef_out = outs.pop(0) if nf else None
    pq_out = outs.pop(0) if nb else None
    from_prev = outs.pop(0) if cfg.up else None
    from_next = outs.pop(0) if cfg.down else None
    slots1, slots2, mid, tot, send1, recv1, send2, recv2, up_land, up_sems, down_land, down_sems = scratch[3:15]
    g1, g2, r1, r2, peer1, peer2, nxt, prv = exchange_peers(cfg)

    halos = []
    copies = []
    for k in range(1, g1):
        copies.append(
            pltpu.make_async_remote_copy(
                src_ref=stats_ref,
                dst_ref=slots1.at[r1],
                send_sem=send1.at[k],
                recv_sem=recv1.at[k],
                device_id=peer1(k),
                device_id_type=MESH,
            )
        )
        copies[-1].start()
    for used, src, land, sems, peer in (
        (cfg.up, up_ref, up_land, up_sems, nxt),
        (cfg.down, down_ref, down_land, down_sems, prv),
    ):
        if used:
            halos.append(
                pltpu.make_async_remote_copy(
                    src_ref=src,
                    dst_ref=land,
                    send_sem=sems.at[0],
                    recv_sem=sems.at[1],
                    device_id=peer,
                    device_id_type=MESH,
                )
            )
            halos[-1].start()
    slots1[r1] = stats_ref[...]
    if meanwhile is not None:
        meanwhile()
    for c in copies:
        c.wait_recv()

    def combine(slots, count, out):
        if nf:
            n = slots[0, n_row : n_row + 1, :]
            for g in range(1, count):
                n = n + slots[g, n_row : n_row + 1, :]
            acc = slots[0, n_row : n_row + 1, :] * slots[0, 0:nf, :]
            for g in range(1, count):
                acc = acc + slots[g, n_row : n_row + 1, :] * slots[g, 0:nf, :]
            mean = acc / jnp.maximum(n, 1.0)
            m2 = None
            for g in range(count):
                d = slots[g, 0:nf, :] - mean
                part = slots[g, nf : 2 * nf, :] + slots[g, n_row : n_row + 1, :] * (d * d)
                m2 = part if m2 is None else m2 + part
            out[0:nf, :] = mean
            out[nf : 2 * nf, :] = m2
            out[n_row : n_row + 1, :] = n
        if nb:
            acc = slots[0, 2 * nf : n_row, :]
            for g in range(1, count):
                acc = acc + slots[g, 2 * nf : n_row, :]
            out[2 * nf : n_row, :] = acc

    zero_ref(mid)
    combine(slots1, g1, mid)
    copies2 = []
    for k in range(1, g2):
        copies2.append(
            pltpu.make_async_remote_copy(
                src_ref=mid,
                dst_ref=slots2.at[r2],
                send_sem=send2.at[k],
                recv_sem=recv2.at[k],
                device_id=peer2(k),
                device_id_type=MESH,
            )
        )
        copies2[-1].start()
    slots2[r2] = mid[...]
    if between is not None:
        between()
    for c in copies2:
        c.wait_recv()
    combine(slots2, g2, tot)

    def lanes4(v):
        w = v + pltpu.roll(v, 64, 1)
        return w + pltpu.roll(w, 32, 1)

    at = 0
    for kind, g_row, count in fwd:
        n = tot[n_row : n_row + 1, :]
        mean = tot[at : at + count, :]
        m2 = tot[nf + at : nf + at + count, :]
        if kind == "lane4":
            whole = lanes4(mean) * 0.25
            d = mean - whole
            var = lanes4(m2 + n * (d * d)) / (4.0 * n)
            mean = whole
        elif kind == "row4":
            whole = jnp.sum(mean, axis=0, keepdims=True) * 0.25
            d = mean - whole
            var = jnp.sum(m2 + n * (d * d), axis=0, keepdims=True) / (4.0 * n)
            var = jnp.broadcast_to(var, (count, LANES))
            mean = jnp.broadcast_to(whole, (count, LANES))
        else:
            var = m2 / n
        inv = lax.rsqrt(var + norm_eps)
        scale = inv * gb_ref[0, g_row : g_row + count, :]
        coef_out[0, at : at + count, :] = scale
        coef_out[1, at : at + count, :] = gb_ref[1, g_row : g_row + count, :] - mean * scale
        coef_out[2, at : at + count, :] = inv
        coef_out[3, at : at + count, :] = mean * inv
        coef_out[4, at : at + count, :] = jnp.broadcast_to(n, (count, LANES))
        at += count
    at = 0
    for kind, coef, row, _, count, db_at, dg_at in bwd:
        db = tot[2 * nf + db_at : 2 * nf + db_at + count, :]
        dg = tot[2 * nf + dg_at : 2 * nf + dg_at + count, :]
        c = coef_refs[coef]
        scale, inv = c[0, row : row + count, :], c[2, row : row + count, :]
        mi, n = c[3, row : row + count, :], c[4, row : row + count, :]
        if kind == "lane4":
            db, dg, n = lanes4(db), lanes4(dg), 4.0 * n
        elif kind == "row4":
            db = jnp.broadcast_to(jnp.sum(db, axis=0, keepdims=True), (count, LANES))
            dg = jnp.broadcast_to(jnp.sum(dg, axis=0, keepdims=True), (count, LANES))
            n = 4.0 * n
        pq_out[0, at : at + count, :] = scale / n * (db - mi * dg)
        pq_out[1, at : at + count, :] = scale / n * inv * dg
        pq_out[2, at : at + count, :] = db
        pq_out[3, at : at + count, :] = dg
        at += count

    if cfg.post:
        post_sent, post_land, post_sems = scratch[15:]
        post(pq_out, post_sent)
        late = pltpu.make_async_remote_copy(
            src_ref=post_sent,
            dst_ref=post_land,
            send_sem=post_sems.at[0],
            recv_sem=post_sems.at[1],
            device_id=prv,
            device_id_type=MESH,
        )
        late.start()
        if after is not None:
            after()
        late.wait()
        outs.pop(0)[...] = post_land[...]
    for c in halos:
        c.wait()
    if cfg.up:
        from_prev[...] = up_land[...]
    if cfg.down:
        from_next[...] = down_land[...]
    for c in copies:
        c.wait_send()
    for c in copies2:
        c.wait_send()


class Exchange:
    def __init__(self, sizes, cid, rows_n, fwd=(), bwd=(), up=None, down=None, post=None):
        self.cid, self.fwd, self.bwd, self.up, self.down, self.post = cid, fwd, bwd, up, down, post
        self.greets = bool(up or down or post)
        g1, g2, r = sizes[0] * 4, sizes[1] // 4, pad8(rows_n)
        self.outs = []
        nf, nn = sum(c[2] for c in fwd), sum(c[4] for c in bwd)
        if nf:
            self.outs.append(((5, nf, LANES), F32))
        if nn:
            self.outs.append(((4, nn, LANES), F32))
        self.outs += [(h, F32) for h in (up, down) if h]
        if post:
            self.outs.append((post, BF16))
        none = (8, LANES)
        self.stats = (r, LANES)
        self.work = [
            pltpu.VMEM((g1, r, LANES), F32),
            pltpu.VMEM((g2, r, LANES), F32),
            pltpu.VMEM((r, LANES), F32),
            pltpu.VMEM((r, LANES), F32),
            pltpu.SemaphoreType.DMA((g1,)),
            pltpu.SemaphoreType.DMA((g1,)),
            pltpu.SemaphoreType.DMA((g2,)),
            pltpu.SemaphoreType.DMA((g2,)),
            pltpu.VMEM(up or none, F32),
            pltpu.SemaphoreType.DMA((2,)),
            pltpu.VMEM(down or none, F32),
            pltpu.SemaphoreType.DMA((2,)),
        ]
        if post:
            self.work += [pltpu.VMEM(post, BF16), pltpu.VMEM(post, BF16), pltpu.SemaphoreType.DMA((2,))]
        self.local = [pltpu.VMEM(self.stats, F32), pltpu.VMEM(up or none, F32), pltpu.VMEM(down or none, F32)]


STAT, UP, DOWN = "stat", "up", "down"


def call(kernel, ins, outs, scratch=(), name=None, ex=None, ex_ins=(), pre=None, pre_ins=()):
    real = [o for o in outs if not isinstance(o, str)]
    given = ins
    ins = [a for a in given if not isinstance(a, int)]
    extra_in = [whole(a) for a in (*ex_ins, *pre_ins)]
    extra_out = [out_whole(s, d) for s, d in ex.outs] if ex else []
    local = [*ex.local, *ex.work] if ex else []
    n_local = len(local)
    if pre:
        extra_out.append(out_whole(*pre.outs[0]))
        local += [*pre.work, *[pltpu.VMEM(shape, d) for shape, d in pre.outs[1:]]]
    all_in, all_out = [*ins, *extra_in], [*real, *extra_out]
    sizes = [len(ins), len(extra_in), len(real), len(extra_out), len(scratch), len(local)]
    ends = [sum(sizes[: k + 1]) for k in range(len(sizes))]

    def body(*refs):
        k_in, x_in, k_out, x_out, k_scr, x_scr = (refs[e - n : e] for e, n in zip(ends, sizes))
        if ex is None:
            kernel(*k_in, *k_out, *k_scr)
            return
        i = pl.program_id(0)

        p_ins, p_outs, p_scr = x_in[len(ex_ins) :], [], x_scr[n_local:]
        x_in, x_scr = x_in[: len(ex_ins)], x_scr[:n_local]
        if pre:
            n = len(pre.work)
            p_outs = [x_out[-1], *p_scr[n:]]
            x_out = x_out[:-1]

        @pl.when(i == 0)
        def _():
            exchange_hello(pre or ex)
            if pre:
                pl.semaphore_wait(pltpu.get_barrier_semaphore(), len_peers(pre))
                exchange_run(pre, p_ins[3:], p_outs, [*p_ins[:3], *p_scr[:n]])

        if pre:
            it_in = iter(k_in)
            views = [p_outs[0], *[o.at[pl.ds(i, 1)] for o in p_outs[1:]]]
            k_in = [views[a] if isinstance(a, int) else next(it_in) for a in given]
        named = {STAT: x_scr[0]}
        if ex.up:
            named[UP] = x_scr[1].at[pl.ds(i, 1)]
        if ex.down:
            named[DOWN] = x_scr[2].at[pl.ds(i, 1)]
        it = iter(k_out)
        late = kernel(*k_in, *[named[o] if isinstance(o, str) else next(it) for o in outs], *k_scr)

        @pl.when(i == STEPS - 1)
        def _():
            if not pre:
                pl.semaphore_wait(pltpu.get_barrier_semaphore(), len_peers(ex))
            exchange_run(ex, x_in, x_out, x_scr, late)

    params = {"collective_id": ex.cid, "has_side_effects": True} if ex else {}
    return pl.pallas_call(
        body,
        grid=(STEPS,),
        in_specs=[pl.BlockSpec(b, m) for _, b, m in all_in],
        out_specs=[pl.BlockSpec(b, m) for _, _, b, m in all_out],
        out_shape=[jax.ShapeDtypeStruct(s, d) for s, d, _, _ in all_out],
        scratch_shapes=[*scratch, *local],
        compiler_params=pltpu.CompilerParams(
            dimension_semantics=("arbitrary",), vmem_limit_bytes=VMEM_LIMIT, **params
        ),
        name=name,
    )(*[a for a, _, _ in all_in])


def len_peers(ex):
    paths, length = lax.axis_size("path"), lax.axis_size("frames")
    return paths * 4 - 1 + length // 4 - 1 + (2 if ex.greets else 0)


def whole(array):
    zeros = (0,) * array.ndim
    return (array, array.shape, lambda i: zeros)


def blocked(array, axis, size):
    block = array.shape[:axis] + (size,) + array.shape[axis + 1 :]
    return (array, block, lambda i: tuple(i if d == axis else 0 for d in range(array.ndim)))


def out_whole(shape, dtype):
    zeros = (0,) * len(shape)
    return (shape, dtype, shape, lambda i: zeros)


def out_blocked(shape, dtype, axis, size):
    block = shape[:axis] + (size,) + shape[axis + 1 :]
    return (shape, dtype, block, lambda i: tuple(i if d == axis else 0 for d in range(len(shape))))


def flat(value):
    return value.reshape(-1, value.shape[-1])


def spread_rows(ref, index, count, height):
    return [jnp.broadcast_to(ref[(*index, slice(p, p + 1))], (height, ref.shape[-1])) for p in range(count)]


def k_first(i, x_ref, tail_ref, m16_ref, m64_ref, wfa_ref, wlat_ref,
            fa_ref, lat_ref, taps_ref, st_ref, up_ref, down_ref, xs, fm, fv, lm, lv):
    x = x_ref[...]
    s_n, p_n, f_n, _ = x.shape
    packed = jnp.concatenate([flat(x[s]) for s in range(s_n)], axis=1)
    fa = dot_nt(packed, wfa_ref[...])
    fa_ref[...] = fa.reshape(fa_ref.shape)
    zero_ref(up_ref)
    zero_ref(down_ref)
    for p in range(p_n):
        down_ref[0, p : p + 1, :] = fa[p * f_n : p * f_n + 1, :]
        up_ref[0, p : p + 1, :] = fa[p * f_n + f_n - 1 : p * f_n + f_n, :]
    spread_add(i, fa.reshape(p_n, f_n, LANES), fm, fv)

    xs[...] = flat(x).astype(F32)
    n = xs.shape[0] // 4
    quarter = [xs[pl.ds(k, n, stride=4), :] for k in range(4)]
    t_n = f_n // 4
    first = lax.broadcasted_iota(jnp.int32, (n // t_n, t_n, LANES), 1) == 0
    link = m16_ref[1:2]
    tail = tail_ref[0].astype(F32)
    taps = []
    for k in range(2):
        halo = jnp.concatenate(
            [
                jnp.broadcast_to(tail[s * 8 + p : s * 8 + p + 1, k * LANES : (k + 1) * LANES], (t_n, LANES))
                for s in range(s_n)
                for p in range(p_n)
            ],
            axis=0,
        )
        moved = pltpu.roll(quarter[2 + k], 1, 0).reshape(n // t_n, t_n, LANES)
        taps.append(flat(jnp.where(first, halo.reshape(moved.shape), moved) * link))
    taps = jnp.concatenate([*taps, *quarter[:3]], axis=1).astype(BF16)
    taps_ref[...] = taps.reshape(taps_ref.shape)
    lat = dot(taps, wlat_ref[...])
    lat_ref[...] = lat.reshape(lat_ref.shape)
    spread_add(i, lat.reshape(n // t_n, t_n, lat.shape[1]), lm, lv)

    @pl.when(i == STEPS - 1)
    def _():
        zero_ref(st_ref)
        fill = m16_ref[0, :, 0:1]
        mean, m2 = spread_end(fm, fv, m64_ref[0, :, 0:1], STEPS * p_n)
        put_rows(st_ref, 0, mean)
        put_rows(st_ref, 3, m2)
        mean, m2 = spread_end(lm, lv, fill, STEPS * p_n * s_n)
        put_rows(st_ref, 1, mean)
        put_rows(st_ref, 4, m2)
        put_rows(st_ref, 6, count_row(m16_ref, STEPS * p_n * s_n))


def count_row(m16_ref, positions):
    return jnp.sum(m16_ref[0], axis=0, keepdims=True) * float(positions)


def shifted(value, first_rows, last_rows, f_n):
    n = value.shape[0]
    shape = (n // f_n, f_n, value.shape[1])
    place = lax.broadcasted_iota(jnp.int32, shape, 1)
    before = jnp.where(place == 0, first_rows, pltpu.roll(value, 1, 0).reshape(shape))
    after = jnp.where(place == f_n - 1, last_rows, pltpu.roll(value, n - 1, 0).reshape(shape))
    return before, after


def k_join(i, x_ref, lat_ref, fa_ref, hp_ref, hn_ref, c1_ref, m16_ref, m64_ref, win_ref, wsc_ref, wmid_ref,
           lact_ref, ftap_ref, sa_ref, sp_ref, fb_ref, st_ref, am, av, pm, pv, bm, bv, begun=False):
    s_n, p_n, t_n, c_slow = x_ref.shape
    c_lat = lat_ref.shape[-1]
    v = flat(lat_ref[...]) * rows(c1_ref, 0, 1, 2) + rows(c1_ref, 1, 1, 2)
    lact = (v * sig(v)).astype(BF16)
    lact_ref[...] = lact.reshape(lact_ref.shape)
    joined = None if begun else jnp.concatenate([flat(x_ref[...]), lact], axis=1)
    wide = c_lat
    for n in range(1 + wsc_ref.shape[1] // wide):
        cols = slice((n - 1) * wide, n * wide)
        if begun:
            z = flat(sa_ref[...] if n == 0 else sp_ref[:, :, :, cols])
            z = z + dot(lact, win_ref[c_slow:, :] if n == 0 else wsc_ref[c_slow:, cols])
        else:
            z = dot(joined, win_ref[...] if n == 0 else wsc_ref[:, cols])
        z4 = z.reshape(s_n, p_n, t_n, wide)
        z3 = z.reshape(s_n * p_n, t_n, wide)
        if n == 0:
            sa_ref[...] = z4
            spread_add(i, z3, am, av)
        else:
            sp_ref[:, :, :, cols] = z4
            spread_add(i, z3, pm, pv, cols)

    f_n = fa_ref.shape[1]
    scale, shift = rows(c1_ref, 0, 0, 1), rows(c1_ref, 1, 0, 1)

    def act(z):
        w = z * scale + shift
        return (w * sig(w)).astype(BF16).astype(F32)

    fact = act(flat(fa_ref[...]))
    ends = []
    for ref in (hp_ref, hn_ref):
        small = act(ref[0])
        ends.append(
            jnp.concatenate(
                [jnp.broadcast_to(small[p : p + 1, :], (f_n, LANES)) for p in range(p_n)], axis=0
            ).reshape(p_n, f_n, LANES)
        )
    before, after = shifted(fact, ends[0], ends[1], f_n)
    ftap = jnp.concatenate(
        [flat(before * m64_ref[1:2]), fact, flat(after * m64_ref[2:3])], axis=1
    ).astype(BF16)
    ftap_ref[...] = ftap.reshape(ftap_ref.shape)
    fb = dot(ftap, wmid_ref[...])
    fb_ref[...] = fb.reshape(fb_ref.shape)
    spread_add(i, fb.reshape(p_n, f_n, LANES), bm, bv)

    @pl.when(i == STEPS - 1)
    def _():
        zero_ref(st_ref)
        fill = m16_ref[0, :, 0:1]
        positions = STEPS * p_n * s_n
        mean, m2 = spread_end(bm, bv, m64_ref[0, :, 0:1], STEPS * p_n)
        put_rows(st_ref, 0, mean)
        put_rows(st_ref, 11, m2)
        mean, m2 = spread_end(am, av, fill, positions)
        put_rows(st_ref, 1, mean)
        put_rows(st_ref, 12, m2)
        mean, m2 = spread_end(pm, pv, fill, positions)
        put_rows(st_ref, 3, mean)
        put_rows(st_ref, 14, m2)
        put_rows(st_ref, 22, count_row(m16_ref, positions))


def k_spatial(i, sa_ref, fb_ref, c2_ref, m16_ref, m64_ref, wsp_ref, wout_ref,
              pad_ref, sb_ref, fact_ref, st_ref, sm, sv, cm, cv):
    h_n, w_n, t_n, c = sa_ref.shape

    @pl.when(i == 0)
    def _():
        scale, shift = rows(c2_ref, 0, 1, 2), rows(c2_ref, 1, 1, 2)
        zero_ref(pad_ref)

        @pl.loop(0, h_n)
        def _(h):
            v = flat(sa_ref[h]) * scale + shift
            pad_ref[h + 1, 1 : w_n + 1] = (v * sig(v)).astype(BF16).reshape(w_n, t_n, c)

    per = h_n // STEPS
    h0 = i * per
    patches = [flat(pad_ref[pl.ds(h0 + a, per), b : b + w_n]) for a in range(3) for b in range(3)]
    acc = dot(jnp.concatenate(patches, axis=1), wsp_ref[...])
    sb_ref[...] = acc.reshape(sb_ref.shape)
    spread_add(i, acc.reshape(per * w_n, t_n, acc.shape[1]), sm, sv)

    p_n, f_n, _ = fb_ref.shape
    v = flat(fb_ref[...]) * rows(c2_ref, 0, 0, 1) + rows(c2_ref, 1, 0, 1)
    fact = (v * sig(v)).astype(BF16)
    fact_ref[...] = fact.reshape(fact_ref.shape)
    fc = dot(fact, wout_ref[...])
    spread_add(i, fc.reshape(p_n, f_n, fc.shape[1]), cm, cv)

    @pl.when(i == STEPS - 1)
    def _():
        zero_ref(st_ref)
        mean, m2 = spread_end(cm, cv, m64_ref[0, :, 0:1], STEPS * p_n)
        put_rows(st_ref, 0, mean)
        put_rows(st_ref, 6, m2)
        mean, m2 = spread_end(sm, sv, m16_ref[0, :, 0:1], h_n * w_n)
        put_rows(st_ref, 4, mean)
        put_rows(st_ref, 10, m2)
        put_rows(st_ref, 12, count_row(m16_ref, h_n * w_n))


def k_expand(i, sb_ref, fact_ref, x_ref, cot_ref, c3_ref, m16_ref, m64_ref, wso_ref, wout_ref,
             sact_ref, fout_ref, df_ref, st_ref, cm, cv, s1, s2):
    s_n, p_n, t_n = x_ref.shape[0], fact_ref.shape[0], sb_ref.shape[-2]
    v = flat(sb_ref[...]) * rows(c3_ref, 0, 4, 2) + rows(c3_ref, 1, 4, 2)
    sact = (v * sig(v)).astype(BF16)
    sact_ref[...] = sact.reshape(sact_ref.shape)
    wide = 256
    for n in range(wso_ref.shape[1] // wide):
        cols = slice(n * wide, (n + 1) * wide)
        z = dot(sact, wso_ref[:, cols])
        spread_add(i, z.reshape(s_n * p_n, t_n, wide), cm, cv, cols)

    f_n = fact_ref.shape[1]
    fc = dot(flat(fact_ref[...]), wout_ref[...])
    fill = m64_ref[0:1]
    for s in range(s_n):
        cols = slice(s * LANES, (s + 1) * LANES)
        z = fc[:, cols].reshape(p_n, f_n, LANES)
        unit = z * rows(c3_ref, 2, s, 1) - rows(c3_ref, 3, s, 1)
        pre = z * rows(c3_ref, 0, s, 1) + rows(c3_ref, 1, s, 1) + x_ref[s].astype(F32)
        g = sig(pre)
        y = pre * g
        fout_ref[s] = (y * fill).astype(BF16)
        d = cot_ref[s].astype(F32) * fill * (g + y * (1.0 - g))
        df_ref[:, :, cols] = d
        sum_add(i, d, s1, cols)
        sum_add(i, d * unit, s2, cols)

    @pl.when(i == STEPS - 1)
    def _():
        zero_ref(st_ref)
        positions = STEPS * p_n * s_n
        mean, m2 = spread_end(cm, cv, m16_ref[0, :, 0:1], positions)
        put_rows(st_ref, 0, mean)
        put_rows(st_ref, 8, m2)
        put_rows(st_ref, 16, sum_end(s1))
        put_rows(st_ref, 20, sum_end(s2))
        put_rows(st_ref, 24, count_row(m16_ref, positions))


def run_resident(kernel, ex_list, hbm, small, locals_, outs, scratch, name, scalars=0):
    vm, anywhere = pl.BlockSpec(memory_space=pltpu.VMEM), pl.BlockSpec(memory_space=pl.ANY)
    for ex in ex_list:
        outs = [*outs, *[(shape, dtype, False) for shape, dtype in ex.outs]]
    work = [w for ex in ex_list for w in (*ex.local, *ex.work)]
    sizes = [len(hbm), len(small), len(outs), len(hbm), len(locals_), len(scratch), 1]
    ends = [sum(sizes[: k + 1]) for k in range(len(sizes))]

    def body(*refs):
        h, sm, o, loaded, kept, scr, (sems,) = (refs[e - n : e] for e, n in zip(ends, sizes))
        rest, at = [], ends[-1]
        for ex in ex_list:
            n = len(ex.local) + len(ex.work)
            rest.append(refs[at : at + n])
            at += n
        loads = [pltpu.make_async_copy(a, b, sems.at[k]) for k, (a, b) in enumerate(zip(h, loaded))]
        greeter = max(ex_list, key=lambda ex: ex.greets)
        count = exchange_hello(greeter)
        for load in loads:
            load.start()
        kernel(loads, lambda: pl.semaphore_wait(pltpu.get_barrier_semaphore(), count), loaded, sm, kept, scr, o, rest)

    return pl.pallas_call(
        body,
        out_shape=[jax.ShapeDtypeStruct(shape, dtype) for shape, dtype, _ in outs],
        in_specs=[anywhere] * len(hbm) + [pl.BlockSpec(memory_space=pltpu.SMEM)] * scalars + [vm] * (len(small) - scalars),
        out_specs=[anywhere if stays else vm for _, _, stays in outs],
        scratch_shapes=[
            *[pltpu.VMEM(a.shape, a.dtype) for a in hbm], *[pltpu.VMEM(*k) for k in locals_], *scratch,
            pltpu.SemaphoreType.DMA((len(hbm),)), *work,
        ],
        compiler_params=pltpu.CompilerParams(
            collective_id=ex_list[0].cid, has_side_effects=True, vmem_limit_bytes=VMEM_LIMIT
        ),
        name=name,
    )(*hbm, *small)


def stores_of(pairs, sems):
    return [pltpu.make_async_copy(a, b, sems.at[k]) for k, (a, b) in enumerate(pairs)]


def k_front(exs, loads, met, loaded, small, kept, scratch, outs, work):
    x_fast, wlat, x_slow, w_in, w_sc = loaded
    fa, lat, taps, lact, ftap, sa, sp, fb = kept
    xs, fm, fv, lm, lv, am, av, pm, pv, bm, bv, sems, sp_sems, ends_f, sent, sent_low, tail_ref, tail_sems = scratch
    big, ready, (c1, hp, hn, c2) = outs[:8], outs[8:15], outs[15:]
    gb, m16, m64, wfa, wmid, wback, wout = ready
    p_n = fa.shape[0] // STEPS
    copies = dict(zip((0, 1, 2, 3, 4, 5, 7), stores_of([p for k, p in enumerate(zip(kept, big)) if k != 6], sems)))
    st1, up, down = work[0][:3]
    loads[0].wait()
    s_n, inner, f_n, ch = x_fast.shape
    t_n = lat.shape[2]
    ends_f[...] = flat(x_fast[:, :, f_n - t_n : f_n, :]).astype(F32)
    zero_ref(sent)
    for k in range(2):
        lines = ends_f[pl.ds(t_n - 2 + k, s_n * inner, stride=t_n), :]
        for s in range(s_n):
            for step in range(STEPS):
                at = s * inner + step * p_n
                sent[step, s * 8 : s * 8 + p_n, k * ch : (k + 1) * ch] = lines[at : at + p_n, :]
    sent_low[...] = sent[...].astype(BF16)
    met()
    nxt = exchange_peers(exs[0])[6]
    halo = pltpu.make_async_remote_copy(
        src_ref=sent_low, dst_ref=tail_ref, send_sem=tail_sems.at[0], recv_sem=tail_sems.at[1],
        device_id=nxt, device_id_type=MESH,
    )
    halo.start()
    small_set_up(*small, *ready, s_n, t_n)
    loads[1].wait()
    halo.wait()

    def first(i):
        part, one = pl.ds(i * p_n, p_n), pl.ds(i, 1)
        k_first(i, x_fast.at[:, part], tail_ref.at[one], m16, m64, wfa, wlat, fa.at[part], lat.at[:, part],
                taps.at[:, part], st1, up.at[one], down.at[one], xs, fm, fv, lm, lv)

    each(0, STEPS, first)
    for k in (0, 1, 2):
        copies[k].start()
    c_slow = x_slow.shape[-1]

    def begin(i):
        part = pl.ds(i * p_n, p_n)
        xs_part = flat(x_slow[:, part])
        wide = sa.shape[-1]
        sa[:, part] = dot(xs_part, w_in[0:c_slow, :]).reshape(s_n, p_n, t_n, wide)
        for n in range(sp.shape[-1] // wide):
            cols = slice(n * wide, (n + 1) * wide)
            sp[:, part, :, cols] = dot(xs_part, w_sc[0:c_slow, cols]).reshape(s_n, p_n, t_n, wide)

    def begin_some():
        for k in (2, 3, 4):
            loads[k].wait()
        each(0, 2, begin)

    exchange_run(exs[0], [gb], [c1, hp, hn], work[0], begin_some, between=lambda: each(2, 3, begin))

    def store_sp(i):
        part = pl.ds(i * p_n, p_n)
        return pltpu.make_async_copy(sp.at[:, part], big[6].at[:, part], sp_sems.at[i])

    def join(i, begun=False):
        part, one = pl.ds(i * p_n, p_n), pl.ds(i, 1)
        k_join(i, x_slow.at[:, part], lat.at[:, part], fa.at[part], hp.at[one], hn.at[one], c1, m16, m64, w_in, w_sc, wmid,
               lact.at[:, part], ftap.at[part], sa.at[:, part], sp.at[:, part], fb.at[part], work[1][0],
               am, av, pm, pv, bm, bv, begun)
        store_sp(i).start()

    each(0, 3, lambda i: join(i, True))
    each(3, STEPS, join)
    for k in (3, 4, 5, 7):
        copies[k].start()
    exchange_run(exs[1], [gb], [c2], work[1])
    each(0, STEPS, lambda i: store_sp(i).wait())
    for k in (0, 1, 2, 3, 4, 5, 7):
        copies[k].wait()


def k_middle(exs, loads, met, loaded, small, kept, scratch, outs, work):
    sa, fb, wsp, wso, x_fast, cot = loaded
    gb, c2, m16, m64, wout = small
    pad, sb, fact, sact, fast_y, df = kept
    sm, sv, cm, cv, em, ev, s1, s2, sems, y_sems, df_sems = scratch
    big, (c3, c4, q4) = outs[:6], outs[6:]
    p_n = fb.shape[0] // STEPS
    rows_n = sb.shape[0] // STEPS
    copies = stores_of(list(zip(kept, big))[:4], sems)
    for k in (0, 1, 2):
        loads[k].wait()

    def spatial(i):
        part, span = pl.ds(i * p_n, p_n), pl.ds(i * rows_n, rows_n)
        k_spatial(i, sa, fb.at[part], c2, m16, m64, wsp, wout, pad, sb.at[span], fact.at[part], work[0][0], sm, sv, cm, cv)

    each(0, STEPS, spatial)
    met()
    for k in (0, 1, 2):
        copies[k].start()
    exchange_run(exs[0], [gb], [c3], work[0])
    for k in (3, 4, 5):
        loads[k].wait()

    def y_store(i):
        part = pl.ds(i * p_n, p_n)
        return pltpu.make_async_copy(fast_y.at[:, part], big[4].at[:, part], y_sems.at[i])

    def df_store(i):
        part = pl.ds(i * p_n, p_n)
        return pltpu.make_async_copy(df.at[part], big[5].at[part], df_sems.at[i])

    def expand(i):
        part, span = pl.ds(i * p_n, p_n), pl.ds(i * rows_n, rows_n)
        k_expand(i, sb.at[span], fact.at[part], x_fast.at[:, part], cot.at[:, part], c3, m16, m64, wso, wout,
                 sact.at[span], fast_y.at[:, part], df.at[part], work[1][0], em, ev, s1, s2)
        y_store(i).start()
        df_store(i).start()

    each(0, STEPS, expand)
    copies[3].start()
    exchange_run(exs[1], [gb, c3], [c4, q4], work[1])
    each(0, STEPS, lambda i: y_store(i).wait())
    each(0, STEPS, lambda i: df_store(i).wait())
    for copy in copies:
        copy.wait()


def back_norm(scale, p, q, dy, z, fill):
    return scale * dy - fill * (p + z * q)


def k_out(sact_ref, sp_ref, cot_ref, df_ref, fact_ref, fb_ref, c2_ref, c3_ref, c4_ref, q4_ref,
          m16_ref, m64_ref, wso_ref, wout_ref,
          out_ref, dy_ref, dfb_ref, gout_ref, up_ref, down_ref, st_ref, s1, s2, s3, t1, t2, gout):
    i = pl.program_id(0)
    s_n, p_n, t_n, _ = sact_ref.shape
    sact = flat(sact_ref[...])
    fill = m16_ref[0:1, :, 0:1]
    wide = 256
    for n in range(wso_ref.shape[1] // wide):
        cols = slice(n * wide, (n + 1) * wide)
        shape = (s_n * p_n, t_n, wide)
        sc = dot(sact, wso_ref[:, cols]).reshape(shape)
        sp = sp_ref[:, :, :, cols].reshape(shape)
        u6 = sc * rows(c4_ref, 2, 2 * n, 2) - rows(c4_ref, 3, 2 * n, 2)
        u7 = sp * rows(c2_ref, 2, 3 + 2 * n, 2) - rows(c2_ref, 3, 3 + 2 * n, 2)
        pre = (
            sc * rows(c4_ref, 0, 2 * n, 2)
            + sp * rows(c2_ref, 0, 3 + 2 * n, 2)
            + (rows(c4_ref, 1, 2 * n, 2) + rows(c2_ref, 1, 3 + 2 * n, 2))
        )
        g = sig(pre)
        y = pre * g
        out_ref[:, :, :, cols] = (y * fill).astype(BF16).reshape(s_n, p_n, t_n, wide)
        d = cot_ref[:, :, :, cols].reshape(shape).astype(F32) * fill * (g + y * (1.0 - g))
        dy_ref[:, :, :, cols] = d.reshape(s_n, p_n, t_n, wide)
        sum_add(i, d, s1, cols)
        sum_add(i, d * u6, s2, cols)
        sum_add(i, d * u7, s3, cols)

    f_n = fact_ref.shape[1]
    fact = flat(fact_ref[...])
    fc = dot(fact, wout_ref[...])
    fill4 = m64_ref[0:1]
    parts = []
    for s in range(s_n):
        cols = slice(s * LANES, (s + 1) * LANES)
        d = back_norm(
            rows(c3_ref, 0, s, 1), rows(q4_ref, 0, s, 1), rows(q4_ref, 1, s, 1),
            df_ref[:, :, cols], fc[:, cols].reshape(p_n, f_n, LANES), fill4,
        )
        parts.append(flat(d).astype(BF16))
    dfc = jnp.concatenate(parts, axis=1)
    add_to(i, gout, dot_tn(fact, dfc))
    z = fb_ref[...]
    back = dot_nt(dfc, wout_ref[...]).reshape(p_n, f_n, LANES) * slope(
        z * rows(c2_ref, 0, 0, 1) + rows(c2_ref, 1, 0, 1)
    )
    dfb_ref[...] = back
    sum_add(i, back, t1)
    sum_add(i, back * (z * rows(c2_ref, 2, 0, 1) - rows(c2_ref, 3, 0, 1)), t2)
    for k, value in enumerate((back, z)):
        value = flat(value)
        for p in range(p_n):
            down_ref[0, k, p : p + 1, :] = value[p * f_n : p * f_n + 1, :]
            up_ref[0, k, p : p + 1, :] = value[p * f_n + f_n - 1 : p * f_n + f_n, :]
        down_ref[0, k, p_n : p_n + 1, :] = m64_ref[0, 0:1, :]
        up_ref[0, k, p_n : p_n + 1, :] = m64_ref[0, f_n - 1 : f_n, :]

    @pl.when(i == STEPS - 1)
    def _():
        zero_ref(st_ref)
        put_rows(st_ref, 0, sum_end(s1))
        put_rows(st_ref, 8, sum_end(s2))
        put_rows(st_ref, 16, sum_end(s3))
        put_rows(st_ref, 24, sum_end(t1))
        put_rows(st_ref, 25, sum_end(t2))
        gout_ref[...] = fold_wide(gout, s_n)


def add_to(step, ref, value):
    ref[...] = jnp.where(step == 0, 0.0, ref[...]) + value


def fold_wide(ref, count):
    a = ref.shape[0] // count
    return sum(ref[s * a : (s + 1) * a, s * LANES : (s + 1) * LANES] for s in range(count))


def fold_lanes(value, count):
    a = value.shape[0] // count
    parts = [value[s * a : (s + 1) * a, :] for s in range(count)]
    return sum(p if s == 0 else pltpu.roll(p, LANES - s * a, 1) for s, p in enumerate(parts))


def k_back_out(x_ref, lact_ref, dy_ref, sp_ref, sact_ref, sb_ref, dfb_ref, fb_ref, fa_ref, ftap_ref, hp_ref, hn_ref,
               c1_ref, c2_ref, c3_ref, c4_ref, q5_ref, m16_ref, m64_ref, wso_ref, wback_ref,
               gw_ref, gs_ref, dsp_ref, dsb_ref, dfa_ref, gmid_ref, st_ref, s1, s2, t1, t2, gsc, gso, gmid):
    i = pl.program_id(0)
    s_n, p_n, t_n, c = sb_ref.shape
    sact = flat(sact_ref[...])
    fill = m16_ref[0:1, :, 0:1]
    wide = 256
    dscs = []
    turned = jnp.concatenate([flat(x_ref[...]), flat(lact_ref[...])], axis=1).T
    sact_turned = sact.T
    for n in range(wso_ref.shape[1] // wide):
        cols = slice(n * wide, (n + 1) * wide)
        shape = (s_n * p_n, t_n, wide)
        d = dy_ref[:, :, :, cols].reshape(shape)
        sc = dot(sact, wso_ref[:, cols]).reshape(shape)
        dsc = back_norm(rows(c4_ref, 0, 2 * n, 2), rows(q5_ref, 0, 2 * n, 2), rows(q5_ref, 1, 2 * n, 2), d, sc, fill)
        dsc = flat(dsc.astype(BF16))
        old = jnp.where(i == 0, 0.0, gso[:, cols])
        gso[:, cols] = old + dot(sact_turned, dsc)
        sp = sp_ref[:, :, :, cols].reshape(shape)
        dsp = back_norm(
            rows(c2_ref, 0, 3 + 2 * n, 2), rows(q5_ref, 0, 8 + 2 * n, 2), rows(q5_ref, 1, 8 + 2 * n, 2), d, sp, fill
        )
        dsp = flat(dsp.astype(BF16))
        dsp_ref[:, :, :, cols] = dsp.reshape(s_n, p_n, t_n, wide)
        old = jnp.where(i == 0, 0.0, gsc[:, cols])
        gsc[:, cols] = old + dot(turned, dsp)
        dscs.append(dsc)
    z = sb_ref[...].reshape(s_n * p_n, t_n, c)
    back = dot_nt(jnp.concatenate(dscs, axis=1), wso_ref[...])
    back = back.reshape(z.shape) * slope(z * rows(c3_ref, 0, 4, 2) + rows(c3_ref, 1, 4, 2))
    dsb_ref[...] = back.reshape(dsb_ref.shape)
    sum_add(i, back, s1)
    sum_add(i, back * (z * rows(c3_ref, 2, 4, 2) - rows(c3_ref, 3, 4, 2)), s2)

    f_n = fb_ref.shape[1]
    scale, p_row, q_row = rows(c2_ref, 0, 0, 1), rows(q5_ref, 0, 16, 1), rows(q5_ref, 1, 16, 1)
    dfb = back_norm(scale, p_row, q_row, dfb_ref[...], fb_ref[...], m64_ref[0:1])
    dfb_low = flat(dfb).astype(BF16)
    add_to(i, gmid, dot_tn(dfb_low, flat(ftap_ref[...])))
    own = dfb_low.astype(F32)
    ends = []
    for ref in (hp_ref, hn_ref):
        small = back_norm(scale, p_row, q_row, ref[0, 0], ref[0, 1], ref[0, 0, p_n : p_n + 1, :])
        small = small.astype(BF16).astype(F32)
        ends.append(
            jnp.concatenate(
                [jnp.broadcast_to(small[p : p + 1, :], (f_n, LANES)) for p in range(p_n)], axis=0
            ).reshape(p_n, f_n, LANES)
        )
    before, after = shifted(own, ends[0], ends[1], f_n)
    taps = jnp.concatenate(
        [flat(after * m64_ref[2:3]), own, flat(before * m64_ref[1:2])], axis=1
    ).astype(BF16)
    z = fa_ref[...]
    back = dot(taps, wback_ref[...]).reshape(z.shape) * slope(
        z * rows(c1_ref, 0, 0, 1) + rows(c1_ref, 1, 0, 1)
    )
    dfa_ref[...] = back
    sum_add(i, back, t1)
    sum_add(i, back * (z * rows(c1_ref, 2, 0, 1) - rows(c1_ref, 3, 0, 1)), t2)

    @pl.when(i == STEPS - 1)
    def _():
        zero_ref(st_ref)
        put_rows(st_ref, 0, sum_end(s1))
        put_rows(st_ref, 2, sum_end(s2))
        put_rows(st_ref, 4, sum_end(t1))
        put_rows(st_ref, 5, sum_end(t2))

    def late():
        for k in range(3):
            gmid_ref[k * 32 : (k + 1) * 32, :] = fold_lanes(gmid[:, k * LANES : (k + 1) * LANES], s_n)
        tall, low_tall = gsc.shape[0], gso.shape[0]
        blocks = gsc.shape[1] // wide
        for n in range(blocks):
            cols = slice(n * wide, (n + 1) * wide)
            gw_ref[n * tall : (n + 1) * tall, :] = gsc[:, cols].astype(BF16)
            gs_ref[n * low_tall : (n + 1) * low_tall, :] = gso[:, cols].astype(BF16)
        if blocks * tall < gw_ref.shape[0]:
            gw_ref[blocks * tall :, :] = jnp.zeros((gw_ref.shape[0] - blocks * tall, wide), BF16)

    return late


def slow_grad(low, dsp, w_in, w_sc, out):
    s_n, p_n, t_n, c = low.shape
    small, d_sp = flat(low[...]), flat(dsp[...])
    for n in range(out.shape[-1] // c):
        part = slice(n * c, (n + 1) * c)
        d = dot_nt(d_sp, w_sc[part, :]) + dot_nt(small, w_in[part, :])
        out[:, :, :, part] = d.astype(BF16).reshape(s_n, p_n, t_n, c)


def fast_grad(low_ref, hn, df, dlow, m16, wlat, wfa, out, gs):
    s_n, p_n, t_n, c = low_ref.shape
    shape = (s_n * p_n, t_n, c)
    low = flat(low_ref[...])
    small = hn[0].astype(F32)
    ends = [
        jnp.broadcast_to(small[s * 8 + p : s * 8 + p + 1, :], (t_n, c)) for s in range(s_n) for p in range(p_n)
    ]
    ends = jnp.concatenate(ends, axis=0).reshape(shape)
    n = low.shape[0]
    moved = pltpu.roll(low.astype(F32), n - 1, 0).reshape(shape)
    place = lax.broadcasted_iota(jnp.int32, shape, 1)
    following = flat(jnp.where(place == t_n - 1, ends, moved) * m16[2:3, :, 0:1]).astype(BF16)
    own = dot_nt(low, wlat[2 * LANES : 5 * LANES, :])
    late = dot_nt(following, wlat[0 : 2 * LANES, :])
    gs[pl.ds(0, n, stride=4), :] = own[:, 0:LANES]
    gs[pl.ds(1, n, stride=4), :] = own[:, LANES : 2 * LANES]
    gs[pl.ds(2, n, stride=4), :] = own[:, 2 * LANES :] + late[:, 0:LANES]
    gs[pl.ds(3, n, stride=4), :] = late[:, LANES:]
    back = dot(flat(dlow[...]), wfa[...])
    for s in range(s_n):
        cols = slice(s * LANES, (s + 1) * LANES)
        total = flat(df[:, :, cols]) + back[:, cols] + gs[s * n : (s + 1) * n, :]
        out[s] = total.astype(BF16).reshape(out.shape[1:])


def each(first, last, body):
    def step(k, carry):
        body(k)
        return carry
    lax.fori_loop(first, last, step, 0)


NEAR = 4


class Cube:
    def __init__(self, ch, far):
        self.ch, self.far = ch, far
        self.p, self.f = lax.axis_index("path"), lax.axis_index("frames")
        self.q, self.r = lax.rem(self.f, NEAR), lax.div(self.f, NEAR)
        self.sibling = (1 - self.p, self.f)

    def q_of(self, k):
        low = (self.q % 2 + k % 2) % 2
        return (self.q // 2 + k // 2) % 2 * 2 + low

    def r_of(self, k):
        return lax.rem(self.r + k, self.far)

    def plane(self, k):
        return (self.p, self.r * NEAR + self.q_of(k))

    def line(self, k):
        return (self.p, self.r_of(k) * NEAR + self.q)

    def at(self, path, q, r):
        return pl.ds(pl.multiple_of(((path * NEAR + q) * self.far + r) * self.ch, 16), self.ch)


def remote(src, dst, sem, index, device):
    return pltpu.make_async_remote_copy(
        src_ref=src, dst_ref=dst, send_sem=sem.at[(0, *index)], recv_sem=sem.at[(1, *index)],
        device_id=device, device_id_type=MESH)


def rows_for(sizes, n):
    unit = 16 * sizes[0] * sizes[1]
    return -(-n // unit) * unit


class Stream:
    def __init__(self, sizes, rows_n, width):
        self.sizes, self.rows_n, self.width = sizes, rows_n, width
        self.far = sizes[1] // NEAR
        self.ch = rows_n // (sizes[0] * sizes[1])
        self.chunk = (self.ch, width)
        self.near_shape = (self.far, *self.chunk)
        quad = pltpu.VMEM((NEAR, *self.near_shape), BF16)
        quad_sems, line_sems = pltpu.SemaphoreType.DMA((2, NEAR, self.far)), pltpu.SemaphoreType.DMA((2, self.far))
        self.near_scratch = [quad, quad, quad, pltpu.VMEM(self.chunk, F32), quad_sems, quad_sems]
        self.line_scratch = [pltpu.VMEM(self.near_shape, BF16), pltpu.VMEM(self.chunk, F32), line_sems]
        self.share_scratch = [line_sems, quad_sems, quad_sems, pltpu.SemaphoreType.DMA]


class Near:
    def __init__(self, stream, x, out, scratch):
        self.x, self.out, self.far, self.c = x, out, stream.far, Cube(stream.ch, stream.far)
        self.land_a, self.buf_b, self.land_b, self.acc, self.sem_a, self.sem_b = scratch

    def pair(self, k, m):
        c = self.c
        return remote(self.x.at[c.at(1 - c.p, c.q_of(k), c.r_of(m + 1))], self.land_a.at[k, m], self.sem_a, (k, m), c.sibling)

    def plane(self, k, m):
        return remote(self.buf_b.at[k, m], self.land_b.at[k, m], self.sem_b, (k, m), self.c.plane(k))

    def start(self):
        def one(m):
            each(1, NEAR, lambda k: self.pair(k, m).start())
            self.pair(0, m).start()

        each(0, self.far, one)

    def add_pair(self, first, last):
        c = self.c

        def one(k, m):
            self.pair(k, m).wait_recv()
            mine = self.x[c.at(c.p, c.q_of(k), c.r_of(m + 1)), :]
            self.buf_b[k, m] = (mine.astype(F32) + self.land_a[k, m].astype(F32)).astype(BF16)
            self.plane(k, m).start()

        each(first, last, lambda m: each(1, NEAR, lambda k: one(k, m)))

    def add_plane(self, first, last, then=None):
        c = self.c

        def one(m):
            self.pair(0, m).wait_recv()
            self.acc[...] = self.x[c.at(c.p, c.q, c.r_of(m + 1)), :].astype(F32) + self.land_a[0, m].astype(F32)

            def more(k):
                self.plane(k, m).wait_recv()
                self.acc[...] += self.land_b[k, m].astype(F32)

            each(1, NEAR, more)
            self.out[m] = self.acc[...].astype(BF16)
            if then is not None:
                then(m)

        each(first, last, one)

    def end(self):
        each(0, self.far, lambda m: each(0, NEAR, lambda k: self.pair(k, m).wait_send()))
        each(0, self.far, lambda m: each(1, NEAR, lambda k: self.plane(k, m).wait_send()))


class Line:
    def __init__(self, stream, near, scratch):
        self.near, self.far, self.c = near, stream.far, Cube(stream.ch, stream.far)
        self.land, self.acc, self.sem = scratch

    def line(self, m):
        return remote(self.near.at[m], self.land.at[m], self.sem, (m,), self.c.line(m + 1))

    def start(self, first, last):
        each(first, min(last, self.far - 1), lambda m: self.line(m).start())

    def total(self):
        self.acc[...] = self.near[self.far - 1].astype(F32)

        def one(m):
            self.line(m).wait_recv()
            self.acc[...] += self.land[m].astype(F32)

        each(0, self.far - 1, one)
        return self.acc[...].astype(BF16)

    def end(self):
        each(0, self.far - 1, lambda m: self.line(m).wait_send())


class Share:
    def __init__(self, stream, res, out, scratch):
        self.res, self.out, self.far, self.c = res, out, stream.far, Cube(stream.ch, stream.far)
        self.cut = stream.ch // 32 * 16
        self.sem_d, self.sem_e, self.sem_f, self.sem_own = scratch

    def own(self):
        return self.out.at[self.c.at(self.c.p, self.c.q, self.c.r)]

    def keep(self):
        return pltpu.make_async_copy(self.res, self.own(), self.sem_own)

    def line_back(self, k):
        return remote(self.res, self.own(), self.sem_d, (k,), self.c.line(k))

    def part(self, q, m):
        return self.out.at[self.c.at(self.c.p, q, self.c.r_of(self.far - m))]

    def plane_back(self, k, m, src=None):
        dst = self.part(self.c.q, m)
        return remote(dst if src is None else src, dst, self.sem_e, (k, m), self.c.plane(k))

    def pair_back(self, k, m, src=None):
        dst = self.part(self.c.q_of(k), m)
        return remote(dst if src is None else src, dst, self.sem_f, (k, m), self.c.sibling)

    def start_line(self):
        each(1, self.far, lambda k: self.line_back(k).start())

    def half(self, k, m):
        c, cut = self.c, self.cut
        start = ((c.p * NEAR + c.q_of(k)) * self.far + c.r_of(self.far - m)) * c.ch
        rows_n = cut if k == 1 else c.ch - cut
        part = self.out.at[pl.ds(pl.multiple_of(start + (0 if k == 1 else cut), 16), rows_n)]
        return remote(part, part, self.sem_e, (3 if k == 1 else 0, m), c.plane(3 - k))

    def start_plane(self):
        each(1, NEAR - 1, lambda k: self.plane_back(k, 0, self.res).start())
        self.pair_back(0, 0, self.res).start()
        self.keep().start()

    def relay(self, first, last):
        def one(m):
            self.line_back(m).wait_recv()
            each(1, NEAR - 1, lambda k: self.plane_back(k, m).start())
            self.pair_back(0, m).start()

        each(first, last, one)

    def hand_on(self, first, last):
        def one(m):
            for k in (1, 2):
                self.plane_back(k, m).wait_recv()
                self.half(k, m).start()
                self.pair_back(k, m).start()

        each(first, last, one)

    def hand_across(self, first, last):
        def one(m):
            for k in (1, 2):
                self.half(k, m).wait_recv()
            self.pair_back(3, m).start()

        each(first, last, one)

    def end(self):
        each(0, self.far, lambda m: each(0, NEAR, lambda k: self.pair_back(k, m).wait()))
        self.keep().wait()
        each(1, self.far, lambda k: self.line_back(k).wait_send())
        each(0, self.far, lambda m: each(1, NEAR - 1, lambda k: self.plane_back(k, m).wait_send()))

        def sent(m):
            for k in (1, 2):
                self.half(k, m).wait_send()

        each(0, self.far, sent)


def k_tail(cfg, *refs):
    st_a, st_b, ex7, ex8, side = cfg
    it = iter(refs)

    def take(n):
        return [next(it) for _ in range(n)]

    hbm = take(13)
    x_slow, lact_src, taps_src = take(3)
    gb, c1, c2, c3, q6, m16, m64, g_fout, g_fmid = take(9)
    low_out, dlow_out, lat_low_out, gf, gw_in, gw_lat, q7, q8, hn, res_a, near_b = take(11)
    local = take(13)
    gw_a, dsb, sb, spad, wsp, sa, x_fast, dfa, fa, w_in, w_sc, dsp, lat = local
    pad, gsp, gin, low, dlow, gw_b, near_a, ends, s1, s2, t1, t2, sems, out_sems = take(14)
    x_part, taps_part, gsi, glat, wsp_turned, x_sems, taps_sems, lact_sem = take(8)
    near1, line1, near2 = take(len(st_a.near_scratch)), take(len(st_a.line_scratch)), take(len(st_b.near_scratch))
    scr7 = take(len(ex7.local) + len(ex7.work))
    scr8 = take(len(ex8.local) + len(ex8.work))
    n_in = w_in.shape[0]
    srcs = list(hbm)
    for k in (9, 10):
        srcs[k] = hbm[k].at[pl.ds(hbm[k].shape[0] - n_in, n_in)]
    loads = [pltpu.make_async_copy(src, dst, sems.at[k]) for k, (src, dst) in enumerate(zip(srcs, local))]
    count = exchange_hello(ex8)
    for k in (1, 2, 0, 4, 3, 5, 6, 7, 8, 9, 10, 11, 12):
        loads[k].start()
    near = Near(st_a, gw_a, near_a, near1)
    line = Line(st_a, near_a, line1)
    near_two = Near(st_b, gw_b, near_b, near2)
    far = st_a.far
    t_n, c = pad.shape[2], pad.shape[3]
    wide = side * t_n
    per = side // STEPS
    fill = m16[0:1, :, 0:1]

    def waits(*names):
        for k in names:
            loads[k].wait()

    waits(1, 2)
    scale, p_row, q_row = rows(c3, 0, 4, 2), rows(q6, 0, 0, 2), rows(q6, 1, 0, 2)
    zero_ref(pad)

    def fill_pad(h):
        part = pl.ds(h * wide, wide)
        d = back_norm(
            scale, p_row, q_row, dsb[part].reshape(side, t_n, c), sb[part].reshape(side, t_n, c), fill
        )
        pad[h + 1, 1 : side + 1] = d.astype(BF16)

    each(0, side, fill_pad)
    waits(0, 4)
    for k in range(9):
        wsp_turned[k * c : (k + 1) * c, :] = wsp[k * c : (k + 1) * c, :].T
    pl.semaphore_wait(pltpu.get_barrier_semaphore(), count)
    near.start()
    waits(3, 5, 6, 7, 8)
    f_n = x_fast.shape[2]
    p_n = x_fast.shape[1] // STEPS

    def spatial(i):
        h0 = i * per
        turned = flat(pad[pl.ds(h0 + 1, per), 1 : side + 1]).T
        blocks = []
        for a in range(3):
            for b in range(3):
                k = 3 * a + b
                patch = flat(spad[pl.ds(h0 + a, per), b : b + side])
                cols = slice(k * c, (k + 1) * c)
                gsp[:, cols] = jnp.where(i == 0, 0.0, gsp[:, cols]) + dot(turned, patch)
                blocks.append(flat(pad[pl.ds(h0 + 2 - a, per), 2 - b : 2 - b + side]))
        acc = dot(jnp.concatenate(blocks, axis=1), wsp_turned[...])
        span = pl.ds(i * per * wide, per * wide)
        z = sa[span]
        back = acc * slope(z * rows(c2, 0, 1, 2) + rows(c2, 1, 1, 2))
        dsb[span] = back
        unit = z * rows(c2, 2, 1, 2) - rows(c2, 3, 1, 2)
        sum_add(i, back.reshape(per * side, t_n, c), s1)
        sum_add(i, (back * unit).reshape(per * side, t_n, c), s2)
        f_span = pl.ds(i * p_n, p_n)
        small = back_norm(
            rows(c1, 0, 0, 1), rows(q6, 0, 2, 1), rows(q6, 1, 2, 1), dfa[f_span], fa[f_span], m64[0:1]
        ).astype(BF16)
        dlow[f_span] = small
        packed = jnp.concatenate([flat(x_fast[s, f_span]) for s in range(x_fast.shape[0])], axis=1)
        add_to(i, gin, dot_tn(flat(small), packed))
        pl.when(i == 0)(lambda: near.add_pair(0, far // 2))
        pl.when(i == 1)(lambda: near.add_pair(far // 2, far))

    each(0, STEPS, spatial)
    stats = scr7[0]
    zero_ref(stats)
    put_rows(stats, 0, sum_end(s1))
    put_rows(stats, 2, sum_end(s2))
    stores = [pltpu.make_async_copy(dlow, dlow_out, out_sems.at[0])]
    stores[0].start()

    def late():
        for k in range(9):
            gw_b[k * c : (k + 1) * c, :] = gsp[:, k * c : (k + 1) * c].T.astype(BF16)
        if 9 * c < gw_b.shape[0]:
            gw_b[9 * c :, :] = jnp.zeros((gw_b.shape[0] - 9 * c, c), BF16)
        n = g_fout.shape[0]
        gf[0:n, 0:LANES] = fold_wide(gin, x_fast.shape[0])
        gf[0:n, LANES:] = g_fout[...]
        gf[n : 2 * n, 0:LANES] = g_fmid[0:n, :]
        gf[n : 2 * n, LANES:] = g_fmid[n : 2 * n, :]
        gf[2 * n :, 0:LANES] = g_fmid[2 * n :, :]
        gf[2 * n :, LANES:] = jnp.zeros((n, LANES), F32)

    n_pos = side * side
    lact = spad.reshape(-1, t_n, c).at[pl.ds(0, n_pos)]
    lat_low = pad.reshape(-1, t_n, c).at[pl.ds(0, n_pos)]
    lact_load = pltpu.make_async_copy(lact_src, lact, lact_sem)
    lact_load.start()
    block = per * wide

    def x_load(i):
        return pltpu.make_async_copy(x_slow.at[pl.ds(i * block, block)], x_part.at[i % 2], x_sems.at[i % 2])

    def taps_load(i):
        return pltpu.make_async_copy(taps_src.at[pl.ds(i * block, block)], taps_part.at[i % 2], taps_sems.at[i % 2])

    for i in range(2):
        x_load(i).start()
        taps_load(i).start()
    exchange_run(ex7, [gb, c2], [q7], scr7, late)
    near_two.start()
    near.add_plane(0, far - 1, lambda m: line.line(m).start())
    near.add_plane(far - 1, far)
    waits(9, 10, 11, 12)
    scale7, p7, q7_row = rows(c2, 0, 1, 2), rows(q7, 0, 0, 2), rows(q7, 1, 0, 2)

    def join(i):
        span = pl.ds(i * block, block)
        shape = (per * side, t_n, c)
        d = back_norm(scale7, p7, q7_row, dsb[span].reshape(shape), sa[span].reshape(shape), fill)
        small = flat(d).astype(BF16)
        low[span] = small
        d = dot_nt(dsp[span], w_sc[...]) + dot_nt(small, w_in[...])
        z = lat[span]
        back = d * slope(z * rows(c1, 0, 1, 2) + rows(c1, 1, 1, 2))
        sb[span] = back
        unit = z * rows(c1, 2, 1, 2) - rows(c1, 3, 1, 2)
        sum_add(i, back.reshape(shape), t1)
        sum_add(i, (back * unit).reshape(shape), t2)
        pl.when(i == 2)(lambda: near_two.add_pair(0, far))

    each(0, STEPS, join)
    stores.append(pltpu.make_async_copy(low, low_out, out_sems.at[1]))
    stores[1].start()
    stats = scr8[0]
    zero_ref(stats)
    put_rows(stats, 0, sum_end(t1))
    put_rows(stats, 2, sum_end(t2))

    def post(q, sent):
        d = back_norm(rows(c1, 0, 1, 2), rows(q, 0, 0, 2), rows(q, 1, 0, 2), ends[0], ends[1], m16[0, 0:1, 0:1])
        sent[...] = d.astype(BF16)

    def in_step(i):
        x_load(i).wait()
        joined = jnp.concatenate([x_part[i % 2], flat(lact[pl.ds(i * per * side, per * side)])], axis=1)
        add_to(i, gsi, dot(low[pl.ds(i * block, block)].T, joined))
        pl.when(i + 2 < STEPS)(lambda: x_load(i + 2).start())

    def in_grad():
        zero_ref(ends)
        for s in range(x_fast.shape[0]):
            for step in range(STEPS):
                for p in range(p_n):
                    at = ((s * STEPS + step) * p_n + p) * t_n
                    ends[0, step, s * 8 + p : s * 8 + p + 1, :] = sb[at : at + 1, :]
                    ends[1, step, s * 8 + p : s * 8 + p + 1, :] = lat[at : at + 1, :]
        lact_load.wait()
        each(0, STEPS, in_step)
        for n in range(gsi.shape[1] // c):
            gw_in[n * c : (n + 1) * c, :] = gsi[:, n * c : (n + 1) * c].T.astype(BF16)

    def lat_step(i):
        scale8, p8, q8_row = rows(c1, 0, 1, 2), rows(q8, 0, 0, 2), rows(q8, 1, 0, 2)
        span = pl.ds(i * block, block)
        shape = (per * side, t_n, c)
        d = back_norm(scale8, p8, q8_row, sb[span].reshape(shape), lat[span].reshape(shape), fill).astype(BF16)
        lat_low[pl.ds(i * per * side, per * side)] = d
        taps_load(i).wait()
        add_to(i, glat, dot_tn(flat(d), taps_part[i % 2]))
        pl.when(i + 2 < STEPS)(lambda: taps_load(i + 2).start())

    def lat_grad():
        each(0, STEPS, lat_step)
        stores.append(pltpu.make_async_copy(lat_low, lat_low_out, out_sems.at[2]))
        stores[2].start()
        for k in range(glat.shape[1] // LANES):
            gw_lat[k * LANES : (k + 1) * LANES, :] = glat[:, k * LANES : (k + 1) * LANES].T.astype(BF16)

    exchange_run(ex8, [gb, c1], [q8, hn], scr8, in_grad, post, lat_grad)
    res_a[...] = line.total()
    near_two.add_plane(0, far)
    for store in stores:
        store.wait()
    line.end()
    near.end()
    near_two.end()


def back_tail(st_a, st_b, ex7, ex8, hbm, more, small, side, t_n, c):
    vm, anywhere = pl.BlockSpec(memory_space=pltpu.VMEM), pl.BlockSpec(memory_space=pl.ANY)
    inner, f_n = hbm[7].shape[:2]
    n = side * side * t_n
    c_cat, c_taps = more[0].shape[1] + c, more[2].shape[1]
    part = n // STEPS
    outs = [((n, c), BF16), ((inner, f_n, LANES), BF16), (more[1].shape, BF16), (small[-1].shape[0:1] + (2 * LANES,), F32),
            ((c_cat, c), BF16), ((c_taps, c), BF16),
            *ex7.outs, *ex8.outs, (st_a.chunk, BF16), (st_b.near_shape, BF16)]
    local = [pltpu.VMEM((c,) + a.shape[1:] if k in (9, 10) else a.shape, a.dtype) for k, a in enumerate(hbm)]
    width = hbm[6].shape[0] * hbm[6].shape[3]
    scratch = [
        pltpu.VMEM((side + 2, side + 2, t_n, c), BF16), pltpu.VMEM((c, 9 * c), F32), pltpu.VMEM((LANES, width), F32),
        pltpu.VMEM((n, c), BF16), pltpu.VMEM((inner, f_n, LANES), BF16), pltpu.VMEM((st_b.rows_n, c), BF16),
        pltpu.VMEM(st_a.near_shape, BF16), pltpu.VMEM((2, *ex8.post), F32), *[pltpu.VMEM((t_n, c), F32)] * 4,
        pltpu.SemaphoreType.DMA((len(hbm),)), pltpu.SemaphoreType.DMA((3,)),
        pltpu.VMEM((2, part, c_cat - c), BF16), pltpu.VMEM((2, part, c_taps), BF16), pltpu.VMEM((c, c_cat), F32),
        pltpu.VMEM((c, c_taps), F32), pltpu.VMEM((9 * c, c), BF16), pltpu.SemaphoreType.DMA((2,)), pltpu.SemaphoreType.DMA((2,)), pltpu.SemaphoreType.DMA,
        *st_a.near_scratch, *st_a.line_scratch, *st_b.near_scratch, *ex7.local, *ex7.work, *ex8.local, *ex8.work,
    ]
    return pl.pallas_call(
        functools.partial(k_tail, (st_a, st_b, ex7, ex8, side)),
        out_shape=[jax.ShapeDtypeStruct(s, d) for s, d in outs],
        in_specs=[anywhere] * (len(hbm) + len(more)) + [vm] * len(small),
        out_specs=[anywhere] * 3 + [vm] * (len(outs) - 3),
        scratch_shapes=[*local, *scratch],
        compiler_params=pltpu.CompilerParams(collective_id=ex8.cid, has_side_effects=True, vmem_limit_bytes=VMEM_LIMIT),
        name="tail",
    )(*hbm, *more, *small)


def final_kernel(cfg, *refs):
    first, second, third, both, offsets, n_hbm, n_small = cfg
    it = iter(refs)

    def take(n):
        return [next(it) for _ in range(n)]

    hbm, small, (out_a, out_bc, gx_out, fast_out) = take(n_hbm), take(n_small), take(4)
    res_a, near_b, *parts, hn, m16, wlat, wfa = small
    loaded = take(n_hbm)
    low, dsp, w_in, w_sc, lat_low, df, dlow = loaded
    x, near_c, res, gx, fast_gx, gs, sems, gx_sems, fast_sems = take(9)
    share_a = Share(first, res_a, out_a, take(len(first.share_scratch)))
    line_b = Line(second, near_b, take(len(second.line_scratch)))
    near = Near(third, x, near_c, take(len(third.near_scratch)))
    line_c = Line(third, near_c, take(len(third.line_scratch)))
    share = Share(both, res, out_bc, take(len(both.share_scratch)))
    far, c = first.far, near.c
    barrier = pltpu.get_barrier_semaphore()
    loads = [pltpu.make_async_copy(a, b, sems.at[k]) for k, (a, b) in enumerate(zip(hbm, loaded))]

    def greet(device):
        pl.semaphore_signal(barrier, inc=1, device_id=device, device_id_type=MESH)

    greet(c.sibling)
    each(1, NEAR, lambda k: greet(c.plane(k)))
    each(1, far, lambda k: greet(c.line(k)))
    for load in loads:
        load.start()
    for ref, first_row, end in zip(parts, offsets, offsets[1:]):
        x[first_row:end, :] = ref[...].astype(BF16)
    if end < x.shape[0]:
        x[end:, :] = jnp.zeros((x.shape[0] - end, x.shape[1]), BF16)
    pl.semaphore_wait(barrier, NEAR + far - 1)

    near.start()
    line_b.start(0, far)
    share_a.start_line()
    p_n = dlow.shape[0] // STEPS

    def gx_store(i):
        part = pl.ds(i * p_n, p_n)
        return pltpu.make_async_copy(gx.at[:, part], gx_out.at[:, part], gx_sems.at[i])

    def slow_step(i):
        part = pl.ds(i * p_n, p_n)
        slow_grad(low.at[:, part], dsp.at[:, part], w_in, w_sc, gx.at[:, part])
        gx_store(i).start()

    def fast_store(i):
        part = pl.ds(i * p_n, p_n)
        return pltpu.make_async_copy(fast_gx.at[:, part], fast_out.at[:, part], fast_sems.at[i])

    def fast_step(i):
        part = pl.ds(i * p_n, p_n)
        fast_grad(lat_low.at[:, part], hn.at[pl.ds(i, 1)], df.at[part], dlow.at[part], m16, wlat, wfa,
                  fast_gx.at[:, part], gs)
        fast_store(i).start()

    share_a.start_plane()
    near.add_pair(0, far)
    for k in (0, 1, 2, 3):
        loads[k].wait()
    each(0, 1, slow_step)
    res[0 : second.ch, :] = line_b.total()
    share_a.relay(1, far)
    share_a.hand_on(0, 1)
    each(1, 3, slow_step)
    near.add_plane(0, far - 1, lambda m: line_c.line(m).start())
    near.add_plane(far - 1, far)
    share_a.hand_on(1, far)
    each(3, 4, slow_step)
    res[second.ch :, :] = line_c.total()
    share.start_line()
    share.start_plane()
    each(4, STEPS, slow_step)
    for k in range(4, n_hbm):
        loads[k].wait()
    share.relay(1, far)
    share_a.hand_across(0, far)
    share.hand_on(0, 1)
    each(0, 3, fast_step)
    share.hand_on(1, far)
    each(3, STEPS, fast_step)
    share.hand_across(0, far)
    share_a.end()
    share.end()
    line_b.end()
    line_c.end()
    near.end()
    each(0, STEPS, lambda i: gx_store(i).wait())
    each(0, STEPS, lambda i: fast_store(i).wait())


def final_sum(sizes, cid, first, second, hbm, small, gx, fast_gx, heights):
    width = first.width
    offsets = tuple(sum(heights[:k]) for k in range(len(heights) + 1))
    third = Stream(sizes, rows_for(sizes, offsets[-1]), width)
    both = Stream(sizes, second.rows_n + third.rows_n, width)
    vm, anywhere = pl.BlockSpec(memory_space=pltpu.VMEM), pl.BlockSpec(memory_space=pl.ANY)
    low, dlow = hbm[0], hbm[6]
    s_n, p_n, f_n = low.shape[0], low.shape[1] // STEPS, dlow.shape[1]
    out_a, out_bc, gx, fast_gx = pl.pallas_call(
        functools.partial(final_kernel, (first, second, third, both, offsets, len(hbm), len(small))),
        out_shape=[jax.ShapeDtypeStruct(s, BF16) for s in ((first.rows_n, width), (both.rows_n, width), gx, fast_gx)],
        in_specs=[anywhere] * len(hbm) + [vm] * len(small),
        out_specs=[anywhere] * 4,
        scratch_shapes=[
            *[pltpu.VMEM(a.shape, a.dtype) for a in hbm],
            pltpu.VMEM((third.rows_n, width), BF16), pltpu.VMEM(third.near_shape, BF16), pltpu.VMEM(both.chunk, BF16),
            pltpu.VMEM(gx, BF16), pltpu.VMEM(fast_gx, BF16), pltpu.VMEM((s_n * p_n * f_n, LANES), F32),
            pltpu.SemaphoreType.DMA((len(hbm),)), pltpu.SemaphoreType.DMA((STEPS,)), pltpu.SemaphoreType.DMA((STEPS,)),
            *first.share_scratch, *second.line_scratch, *third.near_scratch, *third.line_scratch, *both.share_scratch,
        ],
        compiler_params=pltpu.CompilerParams(collective_id=cid, has_side_effects=True, vmem_limit_bytes=VMEM_LIMIT),
        name="final_sum",
    )(*hbm, *small)
    return out_a, out_bc.reshape(-1, both.ch, width), gx, fast_gx


def k_unpack(pieces, cut, *refs):
    (src_a, src_b, q4, q5, q6, q7, q8), held, refs = refs[:7], refs[7:10], refs[10:]
    outs, (low_a, low_b, low_c, wide, line, *kept, sem_a, sem_b, sem_out, sem_held) = refs[:-12], refs[-12:]
    outs, given = outs[:-3], outs[-3:]

    def moves(srcs, dsts, way):
        return [
            pltpu.make_async_copy(a.at[pl.ds(k, 1)], b.at[pl.ds(k, 1)], sem_held.at[way, n, k])
            for n, (a, b) in enumerate(zip(srcs, dsts))
            for k in range(a.shape[0])
        ]

    passes_in, passes = moves(held, kept, 0), moves(kept, given, 1)
    outs, (gains_out, biases_out, in_out, mid_out, out_out) = outs[:-5], outs[-5:]
    lows = (low_a, low_b, low_c)
    flats = [low_a, low_b.reshape(-1, low_b.shape[-1]), low_c.reshape(-1, low_c.shape[-1])]
    starts = [sum(p[2] for p in pieces[:k]) for k in range(len(pieces))]

    def fetch_a(k):
        _, row, height, _, _ = pieces[k]
        return pltpu.make_async_copy(src_a.at[pl.ds(row, height)], low_a.at[pl.ds(row, height)], sem_a.at[k])

    def fetch_b(k):
        part = src_b.at[:, pl.ds(0, cut)] if k == 1 else src_b.at[:, pl.ds(cut, src_b.shape[1] - cut)]
        return pltpu.make_async_copy(part, lows[k], sem_b.at[k])

    def store(k):
        _, _, height, out, col = pieces[k]
        part = outs[out] if col is None else outs[out].at[:, pl.ds(col, wide.shape[1])]
        return pltpu.make_async_copy(wide.at[pl.ds(starts[k], height)], part, sem_out.at[k])

    for k, piece in enumerate(pieces):
        if piece[0] == 0:
            fetch_a(k).start()
    for k in (1, 2):
        fetch_b(k).start()
    for move in passes_in:
        move.start()
    seen = 0
    for k, (src, row, height, _, _) in enumerate(pieces):
        if src == 0:
            fetch_a(k).wait()
        elif src != seen:
            fetch_b(src).wait()
            seen = src
        wide[starts[k] : starts[k] + height, :] = flats[src][row : row + height, :].astype(F32)
        store(k).start()
    for move_in, move in zip(passes_in, passes):
        move_in.wait()
        move.start()
    lane = lax.broadcasted_iota(jnp.int32, (1, LANES), 1)
    left = lane < LANES // 2
    for slab, out in ((3, gains_out), (2, biases_out)):
        at = 0
        for q, first, count in ((q4, 0, 1), (q8, 0, 2), (q7, 0, 2), (q6, 0, 2), (q5, 0, 16)):
            line[at : at + count, :] = q[slab, first : first + count, :]
            at += count
        half = pltpu.roll(line[0:at, :], LANES // 2, 1)
        head = jnp.where(lane < LANES // 4, q6[slab, 2:3, :], q5[slab, 16:17, :])
        out[0:1, :] = jnp.where(left, head, half[0:1])
        out[1:at, :] = jnp.where(left, half[0 : at - 1], half[1:at])
        out[at : at + 1, :] = jnp.where(left, half[at - 1 : at], 0.0)
    a = in_out.shape[0]
    last = sum(p[2] for p in pieces if p[0] == 2)
    small = flats[2][last : last + 3 * a, :]
    in_out[...] = small[0:a, 0:LANES].astype(F32)
    out_out[...] = small[0:a, LANES:].astype(F32)
    eye = (lax.broadcasted_iota(jnp.int32, (a, a), 0) == lax.broadcasted_iota(jnp.int32, (a, a), 1)).astype(BF16)
    for k, (row, col) in enumerate(((a, 0), (a, LANES), (2 * a, 0))):
        mid_out[k] = dot_tn(small[row : row + a, col : col + LANES], eye)[0:a, :]
    for k in range(len(pieces)):
        store(k).wait()
    for move in passes:
        move.wait()


def unpack(src_a, src_b, cut, pieces, shapes, small_shapes, norm_sums, held):
    hbm, vm = pl.BlockSpec(memory_space=pl.ANY), pl.BlockSpec(memory_space=pltpu.VMEM)
    n, _, width = src_b.shape
    return pl.pallas_call(
        functools.partial(k_unpack, pieces, cut),
        out_shape=[jax.ShapeDtypeStruct(s, F32) for s in (*shapes, *small_shapes)]
        + [jax.ShapeDtypeStruct(a.shape, a.dtype) for a in held],
        in_specs=[hbm] * 2 + [vm] * len(norm_sums) + [hbm] * len(held),
        out_specs=[hbm] * len(shapes) + [vm] * len(small_shapes) + [hbm] * len(held),
        scratch_shapes=[
            pltpu.VMEM(src_a.shape, BF16),
            pltpu.VMEM((n, cut, width), BF16),
            pltpu.VMEM((n, src_b.shape[1] - cut, width), BF16),
            pltpu.VMEM((sum(p[2] for p in pieces), width), F32),
            pltpu.VMEM((24, LANES), F32),
            *[pltpu.VMEM(a.shape, a.dtype) for a in held],
            pltpu.SemaphoreType.DMA((len(pieces),)),
            pltpu.SemaphoreType.DMA((3,)),
            pltpu.SemaphoreType.DMA((len(pieces),)),
            pltpu.SemaphoreType.DMA((2, len(held), held[0].shape[0])),
        ],
        compiler_params=pltpu.CompilerParams(vmem_limit_bytes=VMEM_LIMIT),
        name="unpack",
    )(src_a, src_b, *norm_sums, *held)


def small_set_up(fill_ref, clip_ref, norm_ref, wfi_ref, wfm_ref, wfo_ref,
                 gb_ref, m16_ref, m64_ref, wfa_ref, wmid_ref, wback_ref, wout_ref, s_n, t_n):
    length = lax.axis_size("frames")
    total = lax.axis_size("path") * length
    me = lax.axis_index("path") * length + lax.axis_index("frames")
    lane = lax.broadcasted_iota(jnp.int32, (1, LANES), 1)
    for k in range(2):
        half = pltpu.roll(norm_ref[k], LANES // 2, 1)
        main = jnp.where(lane < LANES // 2, half[0:23], half[1:24])
        for j in range(2):
            v = jnp.where(lane // 32 == j, norm_ref[k, 0:1, :], 0.0)
            v = v + pltpu.roll(v, 64, 1)
            gb_ref[k, j : j + 1, :] = v + pltpu.roll(v, 32, 1)
        for j in range(4):
            gb_ref[k, 2 + j : 3 + j, :] = main[0:1]
        gb_ref[k, 6:28, :] = main[1:23]
        gb_ref[k, 28:32, :] = jnp.zeros((4, LANES), F32)

    def row(value):
        return jnp.full((1, LANES), value, F32)

    last = jnp.where(me < total - 1, 1.0, 0.0)
    link = [jnp.where(clip_ref[t] >= 1, 1.0, 0.0) for t in range(t_n)]
    for t in range(t_n):
        filled = row(fill_ref[t].astype(F32))
        after = row(link[t + 1] if t + 1 < t_n else last)
        m16_ref[0, t : t + 1, :] = filled
        m16_ref[1, t : t + 1, :] = row(link[t])
        m16_ref[2, t : t + 1, :] = after
        m64_ref[0, 4 * t : 4 * t + 4, :] = jnp.broadcast_to(filled, (4, LANES))
        m64_ref[1, 4 * t : 4 * t + 1, :] = row(link[t])
        m64_ref[1, 4 * t + 1 : 4 * t + 4, :] = jnp.ones((3, LANES), F32)
        m64_ref[2, 4 * t : 4 * t + 3, :] = jnp.ones((3, LANES), F32)
        m64_ref[2, 4 * t + 3 : 4 * t + 4, :] = after

    zero_ref(wfa_ref)
    zero_ref(wout_ref)
    a = wfi_ref.shape[0]
    for s in range(s_n):
        wfa_ref[s * a : (s + 1) * a, s * LANES : (s + 1) * LANES] = wfi_ref[...]
        wout_ref[s * a : (s + 1) * a, s * LANES : (s + 1) * LANES] = wfo_ref[...]
    tall = (LANES, a)
    spread = (lax.broadcasted_iota(jnp.int32, tall, 0) % a == lax.broadcasted_iota(jnp.int32, tall, 1)).astype(BF16)
    square = (LANES, LANES)
    diag = lax.broadcasted_iota(jnp.int32, square, 0) // a == lax.broadcasted_iota(jnp.int32, square, 1) // a
    for k in range(3):
        left = dot(spread, wfm_ref[k]).astype(BF16)
        wmid_ref[k * LANES : (k + 1) * LANES, :] = jnp.where(diag, dot_nt(left, spread), 0.0).astype(BF16)
        right = dot_nt(spread, wfm_ref[k]).astype(BF16)
        wback_ref[k * LANES : (k + 1) * LANES, :] = jnp.where(diag, dot_nt(right, spread), 0.0).astype(BF16)


def per_device(slow_input, fast_input, clip_offset, fill, w_fast_in, w_fast_mid, w_fast_out, w_lateral,
               w_slow_in, w_slow_mid, w_slow_out, w_shortcut, gains, biases, slow_cot, fast_cot):
    sizes = (lax.axis_size("path"), lax.axis_size("frames"))
    t_n, side, _, c_slow = slow_input.shape
    f_n, c_fast = fast_input.shape[0], fast_input.shape[3]
    in_fast, in_slow, c_lat = w_fast_in.shape[1], w_slow_in.shape[1], w_lateral.shape[2]
    pixels = side * side
    groups = LANES // in_fast
    inner = pixels // groups
    p_n = inner // STEPS

    def slow_view(a):
        return jnp.transpose(a, (1, 2, 0, 3)).reshape(groups, inner, t_n, a.shape[3])

    def fast_view(a):
        return jnp.transpose(a, (1, 2, 0, 3)).reshape(groups, inner, f_n, a.shape[3])

    def unview(a):
        return jnp.transpose(a.reshape(side, side, a.shape[2], a.shape[3]), (2, 0, 1, 3))

    x_slow, cot_slow = slow_view(slow_input), slow_view(slow_cot)
    x_fast, cot_fast = fast_view(fast_input), fast_view(fast_cot)

    norms = jnp.stack([gains, biases])
    norms = jnp.pad(norms, ((0, 0), (0, -norms.shape[1] % (8 * LANES)))).reshape(2, -1, LANES)
    wlat = w_lateral.reshape(-1, c_lat)
    wsp = w_slow_mid.reshape(-1, in_slow)

    sl = (groups, inner, t_n)
    fp = (inner, f_n)

    def slow_out(width, dtype):
        return out_blocked(sl + (width,), dtype, 1, p_n)

    def fast_out(width, dtype):
        return out_blocked(fp + (width,), dtype, 0, p_n)

    def sb_(a):
        return blocked(a, 1, p_n)

    def fb_(a):
        return blocked(a, 0, p_n)

    def stat(n):
        return out_whole((pad8(n), LANES), F32)

    def acc(rows_n, width, count):
        return [pltpu.VMEM((rows_n, width), F32)] * count

    small = (STEPS, 8, LANES)

    sems7 = pltpu.SemaphoreType.DMA((STEPS,))
    exs = [
        Exchange(sizes, 1, 7, fwd=(("lane4", 0, 1), ("plain", 6, 2)), up=small, down=small),
        Exchange(sizes, 1, 23, fwd=(("lane4", 1, 1), ("plain", 8, 2), ("plain", 20, 8))),
    ]
    kept = [
        (fp + (LANES,), F32), (sl + (c_lat,), F32), (sl + (5 * c_fast,), BF16), (sl + (c_lat,), BF16),
        (fp + (3 * LANES,), BF16), (sl + (in_slow,), F32), (sl + (c_slow,), F32), (fp + (LANES,), F32),
    ]
    ready = [((2, 32, LANES), F32), ((3, t_n, LANES), F32), ((3, f_n, LANES), F32), ((LANES, groups * c_fast), BF16),
             ((3 * LANES, LANES), BF16), ((3 * LANES, LANES), BF16), ((LANES, groups * c_fast), BF16)]
    ends = (STEPS, groups * 8, 2 * c_fast)
    fa, lat, taps, lact, ftap, sa, sp, fb, gb, m16, m64, wfa, wmid, wback, wout, c1, hp, hn, c2 = run_resident(
        functools.partial(k_front, exs), exs,
        [x_fast, wlat, x_slow, w_slow_in, w_shortcut],
        [fill, clip_offset, norms, w_fast_in.T, w_fast_mid, w_fast_out],
        kept, [*[(*k, True) for k in kept], *[(*k, False) for k in ready]],
        [pltpu.VMEM((groups * p_n * f_n, c_fast), F32), *acc(f_n, LANES, 2), *acc(t_n, c_lat, 2), *acc(t_n, in_slow, 2),
         *acc(t_n, c_slow, 2), *acc(f_n, LANES, 2), pltpu.SemaphoreType.DMA((8,)), sems7,
         pltpu.VMEM((pixels * t_n, c_fast), F32), pltpu.VMEM(ends, F32), pltpu.VMEM(ends, BF16), pltpu.VMEM(ends, BF16),
         pltpu.SemaphoreType.DMA((2,))],
        "front",
        scalars=2,
    )

    exs = [
        Exchange(sizes, 3, 13, fwd=(("row4", 2, 4), ("plain", 10, 2))),
        Exchange(sizes, 3, 25, fwd=(("plain", 12, 8),), bwd=(("row4", 0, 0, 2, 4, 0, 4),)),
    ]
    kept = [
        ((side + 2, side + 2, t_n, in_slow), BF16), ((pixels, t_n, in_slow), F32), (fp + (LANES,), BF16),
        ((pixels, t_n, in_slow), BF16), ((groups, inner, f_n, c_fast), BF16), (fp + (groups * c_fast,), F32),
    ]
    pad, sb, fact, sact, fast_y, df, c3, c4, q4 = run_resident(
        functools.partial(k_middle, exs), exs,
        [sa.reshape(side, side, t_n, in_slow), fb, wsp, w_slow_out, x_fast, cot_fast], [gb, c2, m16, m64, wout],
        kept, [(*k, True) for k in kept],
        [*acc(t_n, in_slow, 2), *acc(f_n, groups * c_fast, 2), *acc(t_n, c_slow, 2), *acc(f_n, groups * c_fast, 2),
         pltpu.SemaphoreType.DMA((4,)), sems7, sems7],
        "middle",
    )
    sb4, sact = sb.reshape(sl + (in_slow,)), sact.reshape(sl + (in_slow,))

    halo_pair = out_blocked((STEPS, 2, 8, LANES), F32, 0, 1)
    slow_y, dy, dfb, g_fout, up, down, st = call(
        k_out,
        [sb_(sact), sb_(sp), sb_(cot_slow), fb_(df), fb_(fact), fb_(fb), whole(c2), whole(c3), whole(c4), whole(q4),
         whole(m16), whole(m64), whole(w_slow_out), whole(wout)],
        [slow_out(c_slow, BF16), slow_out(c_slow, F32), fast_out(LANES, F32),
         out_whole((in_fast, c_fast), F32), halo_pair, halo_pair, stat(26)],
        [*acc(t_n, c_slow, 3), *acc(f_n, LANES, 2), *acc(LANES, groups * c_fast, 1)],
        "out",
    )
    pair = (STEPS, 2, 8, LANES)
    ex5 = Exchange(
        sizes, 6, 26,
        bwd=(("plain", 0, 0, 12, 8, 0, 8), ("plain", 1, 3, 20, 8, 0, 16), ("lane4", 1, 0, 1, 1, 24, 25)),
        up=pair, down=pair,
    )
    c_cat = w_slow_in.shape[0]
    width = in_slow
    stream_a = Stream(sizes, rows_for(sizes, c_cat * c_slow // width), width)
    stream_b = Stream(sizes, rows_for(sizes, 9 * in_slow), width)
    gw_short, gw_sout, dsp, dsb, dfa, g_fmid, q6, q5 = call(
        k_back_out,
        [sb_(x_slow), sb_(lact), sb_(dy), sb_(sp), sb_(sact), sb_(sb4), fb_(dfb), fb_(fb), fb_(fa), fb_(ftap), 1, 2,
         whole(c1), whole(c2), whole(c3), whole(c4), 0, whole(m16), whole(m64), whole(w_slow_out), whole(wback)],
        [out_whole((stream_a.rows_n, width), BF16), out_whole((c_slow, width), BF16), slow_out(c_slow, BF16),
         slow_out(in_slow, F32), fast_out(LANES, F32), out_whole((3 * in_fast, LANES), F32), STAT],
        [*acc(t_n, in_slow, 2), *acc(f_n, LANES, 2), *acc(c_cat, c_slow, 1), *acc(in_slow, c_slow, 1),
         *acc(LANES, 3 * LANES, 1)],
        "back_out",
        Exchange(sizes, 6, 6, bwd=(("plain", 0, 4, 10, 2, 0, 2), ("lane4", 1, 0, 0, 1, 4, 5))),
        [gb, c3, c1],
        ex5,
        [st, up, down, gb, c4, c2],
    )

    def rows2(a):
        return a.reshape(-1, a.shape[-1])

    dsa_low, dfa_low, lat_low, gw_fast, gw_in, gw_lat, q7, q8, hn, res_a, near_b = back_tail(
        stream_a, stream_b,
        Exchange(sizes, 7, 4, bwd=(("plain", 0, 1, 8, 2, 0, 2),)),
        Exchange(sizes, 7, 4, bwd=(("plain", 0, 1, 6, 2, 0, 2),), post=(STEPS, groups * 8, c_lat)),
        [gw_short, rows2(dsb), rows2(sb4), pad, wsp, rows2(sa), x_fast, dfa, fa, w_slow_in, w_shortcut, rows2(dsp), rows2(lat)],
        [rows2(x_slow), lact.reshape(pixels, t_n, c_lat), rows2(taps)],
        [gb, c1, c2, c3, q6, m16, m64, g_fout, g_fmid],
        side, t_n, in_slow,
    )
    heights = (gw_sout.shape[0], c_cat, 5 * c_fast, gw_fast.shape[0])
    sum_a, sum_bc, slow_gx, fast_gx = final_sum(
        sizes, 9, stream_a, stream_b,
        [dsa_low.reshape(sl + (in_slow,)), dsp, w_slow_in, w_shortcut, lat_low.reshape(sl + (c_lat,)), df, dfa_low],
        [res_a, near_b, gw_sout, gw_in, gw_lat, gw_fast, hn, m16, wlat, wfa],
        sl + (c_slow,), (groups, inner, f_n, c_fast), heights,
    )
    blocks = c_slow // in_slow
    pieces = [(0, n * c_cat, c_cat, 0, n * width) for n in range(blocks)]
    pieces.append((1, 0, 9 * in_slow, 2, None))
    at = 0
    for n in range(blocks):
        pieces.append((2, at, in_slow, 1, n * width))
        at += in_slow
    for out, tall in ((3, c_cat), (4, 5 * c_fast)):
        pieces.append((2, at, tall, out, None))
        at += tall
    norm_rows = -(-gains.shape[0] // LANES)
    g_short, g_sout, gw_mid, gw_in, gw_lat, gains_grad, biases_grad, g_fin, g_fmid, g_fout, *held = unpack(
        sum_a, sum_bc, stream_b.ch, tuple(pieces),
        [(c_cat, c_slow), (in_slow, c_slow), (9 * in_slow, width), (c_cat, in_slow), wlat.shape],
        [(norm_rows, LANES), (norm_rows, LANES), (in_fast, c_fast), w_fast_mid.shape, (in_fast, c_fast)],
        [q4, q5, q6, q7, q8],
        [slow_gx, fast_gx, fast_y],
    )
    slow_gx, fast_gx, fast_y = held
    grads = (
        g_fin.T,
        g_fmid,
        g_fout,
        gw_lat.reshape(w_lateral.shape),
        gw_in,
        gw_mid.reshape(w_slow_mid.shape),
        g_sout,
        g_short,
    )
    return (
        unview(slow_y),
        unview(fast_y),
        unview(slow_gx),
        unview(fast_gx),
        *grads,
        gains_grad.reshape(-1)[: gains.shape[0]],
        biases_grad.reshape(-1)[: biases.shape[0]],
    )


def solution(mesh):
    frames = P(("path", "frames"), None, None, None)
    in_specs = (frames, frames, P(AXES), P(AXES), *([P()] * 10), frames, frames)
    out_specs = (*([frames] * 4), *([P()] * 10))
    return jax.shard_map(per_device, mesh=mesh, in_specs=in_specs, out_specs=out_specs, check_vma=False)
```

```python
import functools

import jax
import jax.numpy as jnp
from jax import lax
from jax.experimental import pallas as pl
from jax.experimental.pallas import tpu as pltpu
from jax.sharding import PartitionSpec as P

norm_eps = 1e-05
F32 = jnp.float32
BF16 = jnp.bfloat16
MESH = pl.DeviceIdType.MESH
AXES = ("path", "frames")
STEPS = 7
LANES = 128
VMEM_LIMIT = 60 * 1024 * 1024


def dot(a, b):
    return jnp.dot(a, b, preferred_element_type=F32)


def dot_nt(a, b):
    return lax.dot_general(a, b, (((1,), (1,)), ((), ())), preferred_element_type=F32)


def dot_tn(a, b):
    return lax.dot_general(a, b, (((0,), (0,)), ((), ())), preferred_element_type=F32)


def sig(v):
    return 0.5 * jnp.tanh(0.5 * v) + 0.5


def slope(v):
    s = sig(v)
    return s + (v * s) * (1.0 - s)


def rows(ref, slab, first, count):
    parts = [ref[slab, first + j : first + j + 1, :] for j in range(count)]
    return parts[0] if count == 1 else jnp.concatenate(parts, axis=1)


def put_rows(ref, first, value):
    for j in range(value.shape[1] // LANES):
        ref[first + j : first + j + 1, :] = value[:, j * LANES : (j + 1) * LANES]


def zero_ref(ref):
    ref[...] = jnp.zeros(ref.shape, ref.dtype)


def spread_add(step, z, mean_ref, m2_ref, cols=slice(None)):
    count = z.shape[0]
    mean = jnp.sum(z, axis=0) * (1.0 / count)
    d = z - mean
    m2 = jnp.sum(d * d, axis=0)
    first = step == 0
    old_mean = jnp.where(first, 0.0, mean_ref[:, cols])
    old_m2 = jnp.where(first, 0.0, m2_ref[:, cols])
    done = jnp.full((1, z.shape[-1]), step, jnp.int32).astype(F32)
    share = 1.0 / (done + 1.0)
    delta = mean - old_mean
    mean_ref[:, cols] = old_mean + delta * share
    m2_ref[:, cols] = old_m2 + m2 + delta * delta * (done * share * count)


def spread_end(mean_ref, m2_ref, fill, positions):
    filled = jnp.sum(fill, axis=0, keepdims=True)
    mean = jnp.sum(fill * mean_ref[...], axis=0, keepdims=True) / jnp.maximum(filled, 1.0)
    d = mean_ref[...] - mean
    m2 = jnp.sum(fill * (m2_ref[...] + positions * (d * d)), axis=0, keepdims=True)
    return mean, m2


def sum_add(step, value, ref, cols=slice(None)):
    ref[:, cols] = jnp.where(step == 0, 0.0, ref[:, cols]) + jnp.sum(value, axis=0)


def sum_end(ref):
    return jnp.sum(ref[...], axis=0, keepdims=True)


def pad8(n):
    return -(-n // 8) * 8


def exchange_peers(cfg):
    paths, length = lax.axis_size("path"), lax.axis_size("frames")
    near = 4
    g1, g2 = paths * near, length // near
    me_p, me_f = lax.axis_index("path"), lax.axis_index("frames")
    me = me_p * length + me_f
    total = paths * length
    r1 = me_p * near + lax.rem(me_f, near)
    r2 = lax.div(me_f, near)

    def peer1(k):
        r = lax.rem(r1 + k, g1)
        return (lax.div(r, near), r2 * near + lax.rem(r, near))

    def peer2(k):
        r = lax.rem(r2 + k, g2)
        return (me_p, r * near + lax.rem(me_f, near))

    def split(index):
        return (lax.div(index, length), lax.rem(index, length))

    nxt, prv = split(lax.rem(me + 1, total)), split(lax.rem(me + total - 1, total))
    return g1, g2, r1, r2, peer1, peer2, nxt, prv


def exchange_hello(cfg):
    g1, g2, _, _, peer1, peer2, nxt, prv = exchange_peers(cfg)
    peers = [peer1(k) for k in range(1, g1)] + [peer2(k) for k in range(1, g2)]
    if cfg.greets:
        peers += [nxt, prv]
    for peer in peers:
        pl.semaphore_signal(pltpu.get_barrier_semaphore(), inc=1, device_id=peer, device_id_type=MESH)
    return len(peers)


def exchange_run(cfg, ins, outs, scratch, meanwhile=None, post=None, after=None, between=None):
    fwd, bwd = cfg.fwd, cfg.bwd
    nf = sum(c[2] for c in fwd)
    nb = max((c[6] + c[4] for c in bwd), default=0)
    n_row = 2 * nf + nb
    stats_ref, up_ref, down_ref = scratch[:3]
    gb_ref, *coef_refs = ins
    outs = list(outs)
    coef_out = outs.pop(0) if nf else None
    pq_out = outs.pop(0) if nb else None
    from_prev = outs.pop(0) if cfg.up else None
    from_next = outs.pop(0) if cfg.down else None
    slots1, slots2, mid, tot, send1, recv1, send2, recv2, up_land, up_sems, down_land, down_sems = scratch[3:15]
    g1, g2, r1, r2, peer1, peer2, nxt, prv = exchange_peers(cfg)

    halos = []
    copies = []
    for k in range(1, g1):
        copies.append(
            pltpu.make_async_remote_copy(
                src_ref=stats_ref,
                dst_ref=slots1.at[r1],
                send_sem=send1.at[k],
                recv_sem=recv1.at[k],
                device_id=peer1(k),
                device_id_type=MESH,
            )
        )
        copies[-1].start()
    for used, src, land, sems, peer in (
        (cfg.up, up_ref, up_land, up_sems, nxt),
        (cfg.down, down_ref, down_land, down_sems, prv),
    ):
        if used:
            halos.append(
                pltpu.make_async_remote_copy(
                    src_ref=src,
                    dst_ref=land,
                    send_sem=sems.at[0],
                    recv_sem=sems.at[1],
                    device_id=peer,
                    device_id_type=MESH,
                )
            )
            halos[-1].start()
    slots1[r1] = stats_ref[...]
    if meanwhile is not None:
        meanwhile()
    for c in copies:
        c.wait_recv()

    def combine(slots, count, out):
        if nf:
            n = slots[0, n_row : n_row + 1, :]
            for g in range(1, count):
                n = n + slots[g, n_row : n_row + 1, :]
            acc = slots[0, n_row : n_row + 1, :] * slots[0, 0:nf, :]
            for g in range(1, count):
                acc = acc + slots[g, n_row : n_row + 1, :] * slots[g, 0:nf, :]
            mean = acc / jnp.maximum(n, 1.0)
            m2 = None
            for g in range(count):
                d = slots[g, 0:nf, :] - mean
                part = slots[g, nf : 2 * nf, :] + slots[g, n_row : n_row + 1, :] * (d * d)
                m2 = part if m2 is None else m2 + part
            out[0:nf, :] = mean
            out[nf : 2 * nf, :] = m2
            out[n_row : n_row + 1, :] = n
        if nb:
            acc = slots[0, 2 * nf : n_row, :]
            for g in range(1, count):
                acc = acc + slots[g, 2 * nf : n_row, :]
            out[2 * nf : n_row, :] = acc

    zero_ref(mid)
    combine(slots1, g1, mid)
    copies2 = []
    for k in range(1, g2):
        copies2.append(
            pltpu.make_async_remote_copy(
                src_ref=mid,
                dst_ref=slots2.at[r2],
                send_sem=send2.at[k],
                recv_sem=recv2.at[k],
                device_id=peer2(k),
                device_id_type=MESH,
            )
        )
        copies2[-1].start()
    slots2[r2] = mid[...]
    if between is not None:
        between()
    for c in copies2:
        c.wait_recv()
    combine(slots2, g2, tot)

    def lanes4(v):
        w = v + pltpu.roll(v, 64, 1)
        return w + pltpu.roll(w, 32, 1)

    at = 0
    for kind, g_row, count in fwd:
        n = tot[n_row : n_row + 1, :]
        mean = tot[at : at + count, :]
        m2 = tot[nf + at : nf + at + count, :]
        if kind == "lane4":
            whole = lanes4(mean) * 0.25
            d = mean - whole
            var = lanes4(m2 + n * (d * d)) / (4.0 * n)
            mean = whole
        elif kind == "row4":
            whole = jnp.sum(mean, axis=0, keepdims=True) * 0.25
            d = mean - whole
            var = jnp.sum(m2 + n * (d * d), axis=0, keepdims=True) / (4.0 * n)
            var = jnp.broadcast_to(var, (count, LANES))
            mean = jnp.broadcast_to(whole, (count, LANES))
        else:
            var = m2 / n
        inv = lax.rsqrt(var + norm_eps)
        scale = inv * gb_ref[0, g_row : g_row + count, :]
        coef_out[0, at : at + count, :] = scale
        coef_out[1, at : at + count, :] = gb_ref[1, g_row : g_row + count, :] - mean * scale
        coef_out[2, at : at + count, :] = inv
        coef_out[3, at : at + count, :] = mean * inv
        coef_out[4, at : at + count, :] = jnp.broadcast_to(n, (count, LANES))
        at += count
    at = 0
    for kind, coef, row, _, count, db_at, dg_at in bwd:
        db = tot[2 * nf + db_at : 2 * nf + db_at + count, :]
        dg = tot[2 * nf + dg_at : 2 * nf + dg_at + count, :]
        c = coef_refs[coef]
        scale, inv = c[0, row : row + count, :], c[2, row : row + count, :]
        mi, n = c[3, row : row + count, :], c[4, row : row + count, :]
        if kind == "lane4":
            db, dg, n = lanes4(db), lanes4(dg), 4.0 * n
        elif kind == "row4":
            db = jnp.broadcast_to(jnp.sum(db, axis=0, keepdims=True), (count, LANES))
            dg = jnp.broadcast_to(jnp.sum(dg, axis=0, keepdims=True), (count, LANES))
            n = 4.0 * n
        pq_out[0, at : at + count, :] = scale / n * (db - mi * dg)
        pq_out[1, at : at + count, :] = scale / n * inv * dg
        pq_out[2, at : at + count, :] = db
        pq_out[3, at : at + count, :] = dg
        at += count

    if cfg.post:
        post_sent, post_land, post_sems = scratch[15:]
        post(pq_out, post_sent)
        late = pltpu.make_async_remote_copy(
            src_ref=post_sent,
            dst_ref=post_land,
            send_sem=post_sems.at[0],
            recv_sem=post_sems.at[1],
            device_id=prv,
            device_id_type=MESH,
        )
        late.start()
        if after is not None:
            after()
        late.wait()
        outs.pop(0)[...] = post_land[...]
    for c in halos:
        c.wait()
    if cfg.up:
        from_prev[...] = up_land[...]
    if cfg.down:
        from_next[...] = down_land[...]
    for c in copies:
        c.wait_send()
    for c in copies2:
        c.wait_send()


class Exchange:
    def __init__(self, sizes, cid, rows_n, fwd=(), bwd=(), up=None, down=None, post=None):
        self.cid, self.fwd, self.bwd, self.up, self.down, self.post = cid, fwd, bwd, up, down, post
        self.greets = bool(up or down or post)
        g1, g2, r = sizes[0] * 4, sizes[1] // 4, pad8(rows_n)
        self.outs = []
        nf, nn = sum(c[2] for c in fwd), sum(c[4] for c in bwd)
        if nf:
            self.outs.append(((5, nf, LANES), F32))
        if nn:
            self.outs.append(((4, nn, LANES), F32))
        self.outs += [(h, F32) for h in (up, down) if h]
        if post:
            self.outs.append((post, BF16))
        none = (8, LANES)
        self.stats = (r, LANES)
        self.work = [
            pltpu.VMEM((g1, r, LANES), F32),
            pltpu.VMEM((g2, r, LANES), F32),
            pltpu.VMEM((r, LANES), F32),
            pltpu.VMEM((r, LANES), F32),
            pltpu.SemaphoreType.DMA((g1,)),
            pltpu.SemaphoreType.DMA((g1,)),
            pltpu.SemaphoreType.DMA((g2,)),
            pltpu.SemaphoreType.DMA((g2,)),
            pltpu.VMEM(up or none, F32),
            pltpu.SemaphoreType.DMA((2,)),
            pltpu.VMEM(down or none, F32),
            pltpu.SemaphoreType.DMA((2,)),
        ]
        if post:
            self.work += [pltpu.VMEM(post, BF16), pltpu.VMEM(post, BF16), pltpu.SemaphoreType.DMA((2,))]
        self.local = [pltpu.VMEM(self.stats, F32), pltpu.VMEM(up or none, F32), pltpu.VMEM(down or none, F32)]


STAT, UP, DOWN = "stat", "up", "down"


def call(kernel, ins, outs, scratch=(), name=None, ex=None, ex_ins=(), pre=None, pre_ins=()):
    real = [o for o in outs if not isinstance(o, str)]
    given = ins
    ins = [a for a in given if not isinstance(a, int)]
    extra_in = [whole(a) for a in (*ex_ins, *pre_ins)]
    extra_out = [out_whole(s, d) for s, d in ex.outs] if ex else []
    local = [*ex.local, *ex.work] if ex else []
    n_local = len(local)
    if pre:
        extra_out.append(out_whole(*pre.outs[0]))
        local += [*pre.work, *[pltpu.VMEM(shape, d) for shape, d in pre.outs[1:]]]
    all_in, all_out = [*ins, *extra_in], [*real, *extra_out]
    sizes = [len(ins), len(extra_in), len(real), len(extra_out), len(scratch), len(local)]
    ends = [sum(sizes[: k + 1]) for k in range(len(sizes))]

    def body(*refs):
        k_in, x_in, k_out, x_out, k_scr, x_scr = (refs[e - n : e] for e, n in zip(ends, sizes))
        if ex is None:
            kernel(*k_in, *k_out, *k_scr)
            return
        i = pl.program_id(0)

        p_ins, p_outs, p_scr = x_in[len(ex_ins) :], [], x_scr[n_local:]
        x_in, x_scr = x_in[: len(ex_ins)], x_scr[:n_local]
        if pre:
            n = len(pre.work)
            p_outs = [x_out[-1], *p_scr[n:]]
            x_out = x_out[:-1]

        @pl.when(i == 0)
        def _():
            exchange_hello(pre or ex)
            if pre:
                pl.semaphore_wait(pltpu.get_barrier_semaphore(), len_peers(pre))
                exchange_run(pre, p_ins[3:], p_outs, [*p_ins[:3], *p_scr[:n]])

        if pre:
            it_in = iter(k_in)
            views = [p_outs[0], *[o.at[pl.ds(i, 1)] for o in p_outs[1:]]]
            k_in = [views[a] if isinstance(a, int) else next(it_in) for a in given]
        named = {STAT: x_scr[0]}
        if ex.up:
            named[UP] = x_scr[1].at[pl.ds(i, 1)]
        if ex.down:
            named[DOWN] = x_scr[2].at[pl.ds(i, 1)]
        it = iter(k_out)
        late = kernel(*k_in, *[named[o] if isinstance(o, str) else next(it) for o in outs], *k_scr)

        @pl.when(i == STEPS - 1)
        def _():
            if not pre:
                pl.semaphore_wait(pltpu.get_barrier_semaphore(), len_peers(ex))
            exchange_run(ex, x_in, x_out, x_scr, late)

    params = {"collective_id": ex.cid, "has_side_effects": True} if ex else {}
    return pl.pallas_call(
        body,
        grid=(STEPS,),
        in_specs=[pl.BlockSpec(b, m) for _, b, m in all_in],
        out_specs=[pl.BlockSpec(b, m) for _, _, b, m in all_out],
        out_shape=[jax.ShapeDtypeStruct(s, d) for s, d, _, _ in all_out],
        scratch_shapes=[*scratch, *local],
        compiler_params=pltpu.CompilerParams(
            dimension_semantics=("arbitrary",), vmem_limit_bytes=VMEM_LIMIT, **params
        ),
        name=name,
    )(*[a for a, _, _ in all_in])


def len_peers(ex):
    paths, length = lax.axis_size("path"), lax.axis_size("frames")
    return paths * 4 - 1 + length // 4 - 1 + (2 if ex.greets else 0)


def whole(array):
    zeros = (0,) * array.ndim
    return (array, array.shape, lambda i: zeros)


def blocked(array, axis, size):
    block = array.shape[:axis] + (size,) + array.shape[axis + 1 :]
    return (array, block, lambda i: tuple(i if d == axis else 0 for d in range(array.ndim)))


def out_whole(shape, dtype):
    zeros = (0,) * len(shape)
    return (shape, dtype, shape, lambda i: zeros)


def out_blocked(shape, dtype, axis, size):
    block = shape[:axis] + (size,) + shape[axis + 1 :]
    return (shape, dtype, block, lambda i: tuple(i if d == axis else 0 for d in range(len(shape))))


def flat(value):
    return value.reshape(-1, value.shape[-1])


def spread_rows(ref, index, count, height):
    return [jnp.broadcast_to(ref[(*index, slice(p, p + 1))], (height, ref.shape[-1])) for p in range(count)]


def k_first(i, x_ref, tail_ref, m16_ref, m64_ref, wfa_ref, wlat_ref,
            fa_ref, lat_ref, taps_ref, st_ref, up_ref, down_ref, xs, fm, fv, lm, lv):
    x = x_ref[...]
    s_n, p_n, f_n, _ = x.shape
    packed = jnp.concatenate([flat(x[s]) for s in range(s_n)], axis=1)
    fa = dot_nt(packed, wfa_ref[...])
    fa_ref[...] = fa.reshape(fa_ref.shape)
    zero_ref(up_ref)
    zero_ref(down_ref)
    for p in range(p_n):
        down_ref[0, p : p + 1, :] = fa[p * f_n : p * f_n + 1, :]
        up_ref[0, p : p + 1, :] = fa[p * f_n + f_n - 1 : p * f_n + f_n, :]
    spread_add(i, fa.reshape(p_n, f_n, LANES), fm, fv)

    xs[...] = flat(x).astype(F32)
    n = xs.shape[0] // 4
    quarter = [xs[pl.ds(k, n, stride=4), :] for k in range(4)]
    t_n = f_n // 4
    first = lax.broadcasted_iota(jnp.int32, (n // t_n, t_n, LANES), 1) == 0
    link = m16_ref[1:2]
    tail = tail_ref[0].astype(F32)
    taps = []
    for k in range(2):
        halo = jnp.concatenate(
            [
                jnp.broadcast_to(tail[s * 8 + p : s * 8 + p + 1, k * LANES : (k + 1) * LANES], (t_n, LANES))
                for s in range(s_n)
                for p in range(p_n)
            ],
            axis=0,
        )
        moved = pltpu.roll(quarter[2 + k], 1, 0).reshape(n // t_n, t_n, LANES)
        taps.append(flat(jnp.where(first, halo.reshape(moved.shape), moved) * link))
    taps = jnp.concatenate([*taps, *quarter[:3]], axis=1).astype(BF16)
    taps_ref[...] = taps.reshape(taps_ref.shape)
    lat = dot(taps, wlat_ref[...])
    lat_ref[...] = lat.reshape(lat_ref.shape)
    spread_add(i, lat.reshape(n // t_n, t_n, lat.shape[1]), lm, lv)

    @pl.when(i == STEPS - 1)
    def _():
        zero_ref(st_ref)
        fill = m16_ref[0, :, 0:1]
        mean, m2 = spread_end(fm, fv, m64_ref[0, :, 0:1], STEPS * p_n)
        put_rows(st_ref, 0, mean)
        put_rows(st_ref, 3, m2)
        mean, m2 = spread_end(lm, lv, fill, STEPS * p_n * s_n)
        put_rows(st_ref, 1, mean)
        put_rows(st_ref, 4, m2)
        put_rows(st_ref, 6, count_row(m16_ref, STEPS * p_n * s_n))


def count_row(m16_ref, positions):
    return jnp.sum(m16_ref[0], axis=0, keepdims=True) * float(positions)


def shifted(value, first_rows, last_rows, f_n):
    n = value.shape[0]
    shape = (n // f_n, f_n, value.shape[1])
    place = lax.broadcasted_iota(jnp.int32, shape, 1)
    before = jnp.where(place == 0, first_rows, pltpu.roll(value, 1, 0).reshape(shape))
    after = jnp.where(place == f_n - 1, last_rows, pltpu.roll(value, n - 1, 0).reshape(shape))
    return before, after


def k_join(i, x_ref, lat_ref, fa_ref, hp_ref, hn_ref, c1_ref, m16_ref, m64_ref, win_ref, wsc_ref, wmid_ref,
           lact_ref, ftap_ref, sa_ref, sp_ref, fb_ref, st_ref, am, av, pm, pv, bm, bv, begun=False):
    s_n, p_n, t_n, c_slow = x_ref.shape
    c_lat = lat_ref.shape[-1]
    v = flat(lat_ref[...]) * rows(c1_ref, 0, 1, 2) + rows(c1_ref, 1, 1, 2)
    lact = (v * sig(v)).astype(BF16)
    lact_ref[...] = lact.reshape(lact_ref.shape)
    joined = None if begun else jnp.concatenate([flat(x_ref[...]), lact], axis=1)
    wide = c_lat
    for n in range(1 + wsc_ref.shape[1] // wide):
        cols = slice((n - 1) * wide, n * wide)
        if begun:
            z = flat(sa_ref[...] if n == 0 else sp_ref[:, :, :, cols])
            z = z + dot(lact, win_ref[c_slow:, :] if n == 0 else wsc_ref[c_slow:, cols])
        else:
            z = dot(joined, win_ref[...] if n == 0 else wsc_ref[:, cols])
        z4 = z.reshape(s_n, p_n, t_n, wide)
        z3 = z.reshape(s_n * p_n, t_n, wide)
        if n == 0:
            sa_ref[...] = z4
            spread_add(i, z3, am, av)
        else:
            sp_ref[:, :, :, cols] = z4
            spread_add(i, z3, pm, pv, cols)

    f_n = fa_ref.shape[1]
    scale, shift = rows(c1_ref, 0, 0, 1), rows(c1_ref, 1, 0, 1)

    def act(z):
        w = z * scale + shift
        return (w * sig(w)).astype(BF16).astype(F32)

    fact = act(flat(fa_ref[...]))
    ends = []
    for ref in (hp_ref, hn_ref):
        small = act(ref[0])
        ends.append(
            jnp.concatenate(
                [jnp.broadcast_to(small[p : p + 1, :], (f_n, LANES)) for p in range(p_n)], axis=0
            ).reshape(p_n, f_n, LANES)
        )
    before, after = shifted(fact, ends[0], ends[1], f_n)
    ftap = jnp.concatenate(
        [flat(before * m64_ref[1:2]), fact, flat(after * m64_ref[2:3])], axis=1
    ).astype(BF16)
    ftap_ref[...] = ftap.reshape(ftap_ref.shape)
    fb = dot(ftap, wmid_ref[...])
    fb_ref[...] = fb.reshape(fb_ref.shape)
    spread_add(i, fb.reshape(p_n, f_n, LANES), bm, bv)

    @pl.when(i == STEPS - 1)
    def _():
        zero_ref(st_ref)
        fill = m16_ref[0, :, 0:1]
        positions = STEPS * p_n * s_n
        mean, m2 = spread_end(bm, bv, m64_ref[0, :, 0:1], STEPS * p_n)
        put_rows(st_ref, 0, mean)
        put_rows(st_ref, 11, m2)
        mean, m2 = spread_end(am, av, fill, positions)
        put_rows(st_ref, 1, mean)
        put_rows(st_ref, 12, m2)
        mean, m2 = spread_end(pm, pv, fill, positions)
        put_rows(st_ref, 3, mean)
        put_rows(st_ref, 14, m2)
        put_rows(st_ref, 22, count_row(m16_ref, positions))


def k_spatial(i, sa_ref, fb_ref, c2_ref, m16_ref, m64_ref, wsp_ref, wout_ref,
              pad_ref, sb_ref, fact_ref, st_ref, sm, sv, cm, cv):
    h_n, w_n, t_n, c = sa_ref.shape

    @pl.when(i == 0)
    def _():
        scale, shift = rows(c2_ref, 0, 1, 2), rows(c2_ref, 1, 1, 2)
        zero_ref(pad_ref)

        @pl.loop(0, h_n)
        def _(h):
            v = flat(sa_ref[h]) * scale + shift
            pad_ref[h + 1, 1 : w_n + 1] = (v * sig(v)).astype(BF16).reshape(w_n, t_n, c)

    per = h_n // STEPS
    h0 = i * per
    patches = [flat(pad_ref[pl.ds(h0 + a, per), b : b + w_n]) for a in range(3) for b in range(3)]
    acc = dot(jnp.concatenate(patches, axis=1), wsp_ref[...])
    sb_ref[...] = acc.reshape(sb_ref.shape)
    spread_add(i, acc.reshape(per * w_n, t_n, acc.shape[1]), sm, sv)

    p_n, f_n, _ = fb_ref.shape
    v = flat(fb_ref[...]) * rows(c2_ref, 0, 0, 1) + rows(c2_ref, 1, 0, 1)
    fact = (v * sig(v)).astype(BF16)
    fact_ref[...] = fact.reshape(fact_ref.shape)
    fc = dot(fact, wout_ref[...])
    spread_add(i, fc.reshape(p_n, f_n, fc.shape[1]), cm, cv)

    @pl.when(i == STEPS - 1)
    def _():
        zero_ref(st_ref)
        mean, m2 = spread_end(cm, cv, m64_ref[0, :, 0:1], STEPS * p_n)
        put_rows(st_ref, 0, mean)
        put_rows(st_ref, 6, m2)
        mean, m2 = spread_end(sm, sv, m16_ref[0, :, 0:1], h_n * w_n)
        put_rows(st_ref, 4, mean)
        put_rows(st_ref, 10, m2)
        put_rows(st_ref, 12, count_row(m16_ref, h_n * w_n))


def k_expand(i, sb_ref, fact_ref, x_ref, cot_ref, c3_ref, m16_ref, m64_ref, wso_ref, wout_ref,
             sact_ref, fout_ref, df_ref, st_ref, cm, cv, s1, s2):
    s_n, p_n, t_n = x_ref.shape[0], fact_ref.shape[0], sb_ref.shape[-2]
    v = flat(sb_ref[...]) * rows(c3_ref, 0, 4, 2) + rows(c3_ref, 1, 4, 2)
    sact = (v * sig(v)).astype(BF16)
    sact_ref[...] = sact.reshape(sact_ref.shape)
    wide = 256
    for n in range(wso_ref.shape[1] // wide):
        cols = slice(n * wide, (n + 1) * wide)
        z = dot(sact, wso_ref[:, cols])
        spread_add(i, z.reshape(s_n * p_n, t_n, wide), cm, cv, cols)

    f_n = fact_ref.shape[1]
    fc = dot(flat(fact_ref[...]), wout_ref[...])
    fill = m64_ref[0:1]
    for s in range(s_n):
        cols = slice(s * LANES, (s + 1) * LANES)
        z = fc[:, cols].reshape(p_n, f_n, LANES)
        unit = z * rows(c3_ref, 2, s, 1) - rows(c3_ref, 3, s, 1)
        pre = z * rows(c3_ref, 0, s, 1) + rows(c3_ref, 1, s, 1) + x_ref[s].astype(F32)
        g = sig(pre)
        y = pre * g
        fout_ref[s] = (y * fill).astype(BF16)
        d = cot_ref[s].astype(F32) * fill * (g + y * (1.0 - g))
        df_ref[:, :, cols] = d
        sum_add(i, d, s1, cols)
        sum_add(i, d * unit, s2, cols)

    @pl.when(i == STEPS - 1)
    def _():
        zero_ref(st_ref)
        positions = STEPS * p_n * s_n
        mean, m2 = spread_end(cm, cv, m16_ref[0, :, 0:1], positions)
        put_rows(st_ref, 0, mean)
        put_rows(st_ref, 8, m2)
        put_rows(st_ref, 16, sum_end(s1))
        put_rows(st_ref, 20, sum_end(s2))
        put_rows(st_ref, 24, count_row(m16_ref, positions))


def run_resident(kernel, ex_list, hbm, small, locals_, outs, scratch, name, scalars=0):
    vm, anywhere = pl.BlockSpec(memory_space=pltpu.VMEM), pl.BlockSpec(memory_space=pl.ANY)
    for ex in ex_list:
        outs = [*outs, *[(shape, dtype, False) for shape, dtype in ex.outs]]
    work = [w for ex in ex_list for w in (*ex.local, *ex.work)]
    sizes = [len(hbm), len(small), len(outs), len(hbm), len(locals_), len(scratch), 1]
    ends = [sum(sizes[: k + 1]) for k in range(len(sizes))]

    def body(*refs):
        h, sm, o, loaded, kept, scr, (sems,) = (refs[e - n : e] for e, n in zip(ends, sizes))
        rest, at = [], ends[-1]
        for ex in ex_list:
            n = len(ex.local) + len(ex.work)
            rest.append(refs[at : at + n])
            at += n
        loads = [pltpu.make_async_copy(a, b, sems.at[k]) for k, (a, b) in enumerate(zip(h, loaded))]
        greeter = max(ex_list, key=lambda ex: ex.greets)
        count = exchange_hello(greeter)
        for load in loads:
            load.start()
        kernel(loads, lambda: pl.semaphore_wait(pltpu.get_barrier_semaphore(), count), loaded, sm, kept, scr, o, rest)

    return pl.pallas_call(
        body,
        out_shape=[jax.ShapeDtypeStruct(shape, dtype) for shape, dtype, _ in outs],
        in_specs=[anywhere] * len(hbm) + [pl.BlockSpec(memory_space=pltpu.SMEM)] * scalars + [vm] * (len(small) - scalars),
        out_specs=[anywhere if stays else vm for _, _, stays in outs],
        scratch_shapes=[
            *[pltpu.VMEM(a.shape, a.dtype) for a in hbm], *[pltpu.VMEM(*k) for k in locals_], *scratch,
            pltpu.SemaphoreType.DMA((len(hbm),)), *work,
        ],
        compiler_params=pltpu.CompilerParams(
            collective_id=ex_list[0].cid, has_side_effects=True, vmem_limit_bytes=VMEM_LIMIT
        ),
        name=name,
    )(*hbm, *small)


def stores_of(pairs, sems):
    return [pltpu.make_async_copy(a, b, sems.at[k]) for k, (a, b) in enumerate(pairs)]


def k_front(exs, loads, met, loaded, small, kept, scratch, outs, work):
    x_fast, wlat, x_slow, w_in, w_sc = loaded
    fa, lat, taps, lact, ftap, sa, sp, fb = kept
    xs, fm, fv, lm, lv, am, av, pm, pv, bm, bv, sems, sp_sems, ends_f, sent, sent_low, tail_ref, tail_sems = scratch
    big, ready, (c1, hp, hn, c2) = outs[:8], outs[8:15], outs[15:]
    gb, m16, m64, wfa, wmid, wback, wout = ready
    p_n = fa.shape[0] // STEPS
    copies = dict(zip((0, 1, 2, 3, 4, 5, 7), stores_of([p for k, p in enumerate(zip(kept, big)) if k != 6], sems)))
    st1, up, down = work[0][:3]
    loads[0].wait()
    s_n, inner, f_n, ch = x_fast.shape
    t_n = lat.shape[2]
    ends_f[...] = flat(x_fast[:, :, f_n - t_n : f_n, :]).astype(F32)
    zero_ref(sent)
    for k in range(2):
        lines = ends_f[pl.ds(t_n - 2 + k, s_n * inner, stride=t_n), :]
        for s in range(s_n):
            for step in range(STEPS):
                at = s * inner + step * p_n
                sent[step, s * 8 : s * 8 + p_n, k * ch : (k + 1) * ch] = lines[at : at + p_n, :]
    sent_low[...] = sent[...].astype(BF16)
    met()
    nxt = exchange_peers(exs[0])[6]
    halo = pltpu.make_async_remote_copy(
        src_ref=sent_low, dst_ref=tail_ref, send_sem=tail_sems.at[0], recv_sem=tail_sems.at[1],
        device_id=nxt, device_id_type=MESH,
    )
    halo.start()
    small_set_up(*small, *ready, s_n, t_n)
    loads[1].wait()
    halo.wait()

    def first(i):
        part, one = pl.ds(i * p_n, p_n), pl.ds(i, 1)
        k_first(i, x_fast.at[:, part], tail_ref.at[one], m16, m64, wfa, wlat, fa.at[part], lat.at[:, part],
                taps.at[:, part], st1, up.at[one], down.at[one], xs, fm, fv, lm, lv)

    each(0, STEPS, first)
    for k in (0, 1, 2):
        copies[k].start()
    c_slow = x_slow.shape[-1]

    def begin(i):
        part = pl.ds(i * p_n, p_n)
        xs_part = flat(x_slow[:, part])
        wide = sa.shape[-1]
        sa[:, part] = dot(xs_part, w_in[0:c_slow, :]).reshape(s_n, p_n, t_n, wide)
        for n in range(sp.shape[-1] // wide):
            cols = slice(n * wide, (n + 1) * wide)
            sp[:, part, :, cols] = dot(xs_part, w_sc[0:c_slow, cols]).reshape(s_n, p_n, t_n, wide)

    def begin_some():
        for k in (2, 3, 4):
            loads[k].wait()
        each(0, 2, begin)

    exchange_run(exs[0], [gb], [c1, hp, hn], work[0], begin_some, between=lambda: each(2, 4, begin))

    def store_sp(i):
        part = pl.ds(i * p_n, p_n)
        return pltpu.make_async_copy(sp.at[:, part], big[6].at[:, part], sp_sems.at[i])

    def join(i, begun=False):
        part, one = pl.ds(i * p_n, p_n), pl.ds(i, 1)
        k_join(i, x_slow.at[:, part], lat.at[:, part], fa.at[part], hp.at[one], hn.at[one], c1, m16, m64, w_in, w_sc, wmid,
               lact.at[:, part], ftap.at[part], sa.at[:, part], sp.at[:, part], fb.at[part], work[1][0],
               am, av, pm, pv, bm, bv, begun)
        store_sp(i).start()

    each(0, 4, lambda i: join(i, True))
    each(4, STEPS, join)
    for k in (3, 4, 5, 7):
        copies[k].start()
    exchange_run(exs[1], [gb], [c2], work[1])
    each(0, STEPS, lambda i: store_sp(i).wait())
    for k in (0, 1, 2, 3, 4, 5, 7):
        copies[k].wait()


def k_middle(exs, loads, met, loaded, small, kept, scratch, outs, work):
    sa, fb, wsp, wso, x_fast, cot = loaded
    gb, c2, m16, m64, wout = small
    pad, sb, fact, sact, fast_y, df = kept
    sm, sv, cm, cv, em, ev, s1, s2, sems, y_sems, df_sems = scratch
    big, (c3, c4, q4) = outs[:6], outs[6:]
    p_n = fb.shape[0] // STEPS
    rows_n = sb.shape[0] // STEPS
    copies = stores_of(list(zip(kept, big))[:4], sems)
    for k in (0, 1, 2):
        loads[k].wait()

    def spatial(i):
        part, span = pl.ds(i * p_n, p_n), pl.ds(i * rows_n, rows_n)
        k_spatial(i, sa, fb.at[part], c2, m16, m64, wsp, wout, pad, sb.at[span], fact.at[part], work[0][0], sm, sv, cm, cv)

    each(0, STEPS, spatial)
    met()
    for k in (0, 1, 2):
        copies[k].start()
    exchange_run(exs[0], [gb], [c3], work[0])
    for k in (3, 4, 5):
        loads[k].wait()

    def y_store(i):
        part = pl.ds(i * p_n, p_n)
        return pltpu.make_async_copy(fast_y.at[:, part], big[4].at[:, part], y_sems.at[i])

    def df_store(i):
        part = pl.ds(i * p_n, p_n)
        return pltpu.make_async_copy(df.at[part], big[5].at[part], df_sems.at[i])

    def expand(i):
        part, span = pl.ds(i * p_n, p_n), pl.ds(i * rows_n, rows_n)
        k_expand(i, sb.at[span], fact.at[part], x_fast.at[:, part], cot.at[:, part], c3, m16, m64, wso, wout,
                 sact.at[span], fast_y.at[:, part], df.at[part], work[1][0], em, ev, s1, s2)
        y_store(i).start()
        df_store(i).start()

    each(0, STEPS, expand)
    copies[3].start()
    exchange_run(exs[1], [gb, c3], [c4, q4], work[1])
    each(0, STEPS, lambda i: y_store(i).wait())
    each(0, STEPS, lambda i: df_store(i).wait())
    for copy in copies:
        copy.wait()


def back_norm(scale, p, q, dy, z, fill):
    return scale * dy - fill * (p + z * q)


def k_out(sact_ref, sp_ref, cot_ref, df_ref, fact_ref, fb_ref, c2_ref, c3_ref, c4_ref, q4_ref,
          m16_ref, m64_ref, wso_ref, wout_ref,
          out_ref, dy_ref, dfb_ref, gout_ref, up_ref, down_ref, st_ref, s1, s2, s3, t1, t2, gout):
    i = pl.program_id(0)
    s_n, p_n, t_n, _ = sact_ref.shape
    sact = flat(sact_ref[...])
    fill = m16_ref[0:1, :, 0:1]
    wide = 256
    for n in range(wso_ref.shape[1] // wide):
        cols = slice(n * wide, (n + 1) * wide)
        shape = (s_n * p_n, t_n, wide)
        sc = dot(sact, wso_ref[:, cols]).reshape(shape)
        sp = sp_ref[:, :, :, cols].reshape(shape)
        u6 = sc * rows(c4_ref, 2, 2 * n, 2) - rows(c4_ref, 3, 2 * n, 2)
        u7 = sp * rows(c2_ref, 2, 3 + 2 * n, 2) - rows(c2_ref, 3, 3 + 2 * n, 2)
        pre = (
            sc * rows(c4_ref, 0, 2 * n, 2)
            + sp * rows(c2_ref, 0, 3 + 2 * n, 2)
            + (rows(c4_ref, 1, 2 * n, 2) + rows(c2_ref, 1, 3 + 2 * n, 2))
        )
        g = sig(pre)
        y = pre * g
        out_ref[:, :, :, cols] = (y * fill).astype(BF16).reshape(s_n, p_n, t_n, wide)
        d = cot_ref[:, :, :, cols].reshape(shape).astype(F32) * fill * (g + y * (1.0 - g))
        dy_ref[:, :, :, cols] = d.reshape(s_n, p_n, t_n, wide)
        sum_add(i, d, s1, cols)
        sum_add(i, d * u6, s2, cols)
        sum_add(i, d * u7, s3, cols)

    f_n = fact_ref.shape[1]
    fact = flat(fact_ref[...])
    fc = dot(fact, wout_ref[...])
    fill4 = m64_ref[0:1]
    parts = []
    for s in range(s_n):
        cols = slice(s * LANES, (s + 1) * LANES)
        d = back_norm(
            rows(c3_ref, 0, s, 1), rows(q4_ref, 0, s, 1), rows(q4_ref, 1, s, 1),
            df_ref[:, :, cols], fc[:, cols].reshape(p_n, f_n, LANES), fill4,
        )
        parts.append(flat(d).astype(BF16))
    dfc = jnp.concatenate(parts, axis=1)
    add_to(i, gout, dot_tn(fact, dfc))
    z = fb_ref[...]
    back = dot_nt(dfc, wout_ref[...]).reshape(p_n, f_n, LANES) * slope(
        z * rows(c2_ref, 0, 0, 1) + rows(c2_ref, 1, 0, 1)
    )
    dfb_ref[...] = back
    sum_add(i, back, t1)
    sum_add(i, back * (z * rows(c2_ref, 2, 0, 1) - rows(c2_ref, 3, 0, 1)), t2)
    for k, value in enumerate((back, z)):
        value = flat(value)
        for p in range(p_n):
            down_ref[0, k, p : p + 1, :] = value[p * f_n : p * f_n + 1, :]
            up_ref[0, k, p : p + 1, :] = value[p * f_n + f_n - 1 : p * f_n + f_n, :]
        down_ref[0, k, p_n : p_n + 1, :] = m64_ref[0, 0:1, :]
        up_ref[0, k, p_n : p_n + 1, :] = m64_ref[0, f_n - 1 : f_n, :]

    @pl.when(i == STEPS - 1)
    def _():
        zero_ref(st_ref)
        put_rows(st_ref, 0, sum_end(s1))
        put_rows(st_ref, 8, sum_end(s2))
        put_rows(st_ref, 16, sum_end(s3))
        put_rows(st_ref, 24, sum_end(t1))
        put_rows(st_ref, 25, sum_end(t2))
        gout_ref[...] = fold_wide(gout, s_n)


def add_to(step, ref, value):
    ref[...] = jnp.where(step == 0, 0.0, ref[...]) + value


def fold_wide(ref, count):
    a = ref.shape[0] // count
    return sum(ref[s * a : (s + 1) * a, s * LANES : (s + 1) * LANES] for s in range(count))


def fold_lanes(value, count):
    a = value.shape[0] // count
    parts = [value[s * a : (s + 1) * a, :] for s in range(count)]
    return sum(p if s == 0 else pltpu.roll(p, LANES - s * a, 1) for s, p in enumerate(parts))


def k_back_out(x_ref, lact_ref, dy_ref, sp_ref, sact_ref, sb_ref, dfb_ref, fb_ref, fa_ref, ftap_ref, hp_ref, hn_ref,
               c1_ref, c2_ref, c3_ref, c4_ref, q5_ref, m16_ref, m64_ref, wso_ref, wback_ref,
               gw_ref, gs_ref, dsp_ref, dsb_ref, dfa_ref, gmid_ref, st_ref, s1, s2, t1, t2, gsc, gso, gmid):
    i = pl.program_id(0)
    s_n, p_n, t_n, c = sb_ref.shape
    sact = flat(sact_ref[...])
    fill = m16_ref[0:1, :, 0:1]
    wide = 256
    dscs = []
    turned = jnp.concatenate([flat(x_ref[...]), flat(lact_ref[...])], axis=1).T
    sact_turned = sact.T
    for n in range(wso_ref.shape[1] // wide):
        cols = slice(n * wide, (n + 1) * wide)
        shape = (s_n * p_n, t_n, wide)
        d = dy_ref[:, :, :, cols].reshape(shape)
        sc = dot(sact, wso_ref[:, cols]).reshape(shape)
        dsc = back_norm(rows(c4_ref, 0, 2 * n, 2), rows(q5_ref, 0, 2 * n, 2), rows(q5_ref, 1, 2 * n, 2), d, sc, fill)
        dsc = flat(dsc.astype(BF16))
        old = jnp.where(i == 0, 0.0, gso[:, cols])
        gso[:, cols] = old + dot(sact_turned, dsc)
        sp = sp_ref[:, :, :, cols].reshape(shape)
        dsp = back_norm(
            rows(c2_ref, 0, 3 + 2 * n, 2), rows(q5_ref, 0, 8 + 2 * n, 2), rows(q5_ref, 1, 8 + 2 * n, 2), d, sp, fill
        )
        dsp = flat(dsp.astype(BF16))
        dsp_ref[:, :, :, cols] = dsp.reshape(s_n, p_n, t_n, wide)
        old = jnp.where(i == 0, 0.0, gsc[:, cols])
        gsc[:, cols] = old + dot(turned, dsp)
        dscs.append(dsc)
    z = sb_ref[...].reshape(s_n * p_n, t_n, c)
    back = dot_nt(jnp.concatenate(dscs, axis=1), wso_ref[...])
    back = back.reshape(z.shape) * slope(z * rows(c3_ref, 0, 4, 2) + rows(c3_ref, 1, 4, 2))
    dsb_ref[...] = back.reshape(dsb_ref.shape)
    sum_add(i, back, s1)
    sum_add(i, back * (z * rows(c3_ref, 2, 4, 2) - rows(c3_ref, 3, 4, 2)), s2)

    f_n = fb_ref.shape[1]
    scale, p_row, q_row = rows(c2_ref, 0, 0, 1), rows(q5_ref, 0, 16, 1), rows(q5_ref, 1, 16, 1)
    dfb = back_norm(scale, p_row, q_row, dfb_ref[...], fb_ref[...], m64_ref[0:1])
    dfb_low = flat(dfb).astype(BF16)
    add_to(i, gmid, dot_tn(dfb_low, flat(ftap_ref[...])))
    own = dfb_low.astype(F32)
    ends = []
    for ref in (hp_ref, hn_ref):
        small = back_norm(scale, p_row, q_row, ref[0, 0], ref[0, 1], ref[0, 0, p_n : p_n + 1, :])
        small = small.astype(BF16).astype(F32)
        ends.append(
            jnp.concatenate(
                [jnp.broadcast_to(small[p : p + 1, :], (f_n, LANES)) for p in range(p_n)], axis=0
            ).reshape(p_n, f_n, LANES)
        )
    before, after = shifted(own, ends[0], ends[1], f_n)
    taps = jnp.concatenate(
        [flat(after * m64_ref[2:3]), own, flat(before * m64_ref[1:2])], axis=1
    ).astype(BF16)
    z = fa_ref[...]
    back = dot(taps, wback_ref[...]).reshape(z.shape) * slope(
        z * rows(c1_ref, 0, 0, 1) + rows(c1_ref, 1, 0, 1)
    )
    dfa_ref[...] = back
    sum_add(i, back, t1)
    sum_add(i, back * (z * rows(c1_ref, 2, 0, 1) - rows(c1_ref, 3, 0, 1)), t2)

    @pl.when(i == STEPS - 1)
    def _():
        zero_ref(st_ref)
        put_rows(st_ref, 0, sum_end(s1))
        put_rows(st_ref, 2, sum_end(s2))
        put_rows(st_ref, 4, sum_end(t1))
        put_rows(st_ref, 5, sum_end(t2))

    def late():
        for k in range(3):
            gmid_ref[k * 32 : (k + 1) * 32, :] = fold_lanes(gmid[:, k * LANES : (k + 1) * LANES], s_n)
        tall, low_tall = gsc.shape[0], gso.shape[0]
        blocks = gsc.shape[1] // wide
        for n in range(blocks):
            cols = slice(n * wide, (n + 1) * wide)
            gw_ref[n * tall : (n + 1) * tall, :] = gsc[:, cols].astype(BF16)
            gs_ref[n * low_tall : (n + 1) * low_tall, :] = gso[:, cols].astype(BF16)
        if blocks * tall < gw_ref.shape[0]:
            gw_ref[blocks * tall :, :] = jnp.zeros((gw_ref.shape[0] - blocks * tall, wide), BF16)

    return late


def slow_grad(low, dsp, w_in, w_sc, out):
    s_n, p_n, t_n, c = low.shape
    small, d_sp = flat(low[...]), flat(dsp[...])
    for n in range(out.shape[-1] // c):
        part = slice(n * c, (n + 1) * c)
        d = dot_nt(d_sp, w_sc[part, :]) + dot_nt(small, w_in[part, :])
        out[:, :, :, part] = d.astype(BF16).reshape(s_n, p_n, t_n, c)


def fast_grad(low_ref, hn, df, dlow, m16, wlat, wfa, out, gs):
    s_n, p_n, t_n, c = low_ref.shape
    shape = (s_n * p_n, t_n, c)
    low = flat(low_ref[...])
    small = hn[0].astype(F32)
    ends = [
        jnp.broadcast_to(small[s * 8 + p : s * 8 + p + 1, :], (t_n, c)) for s in range(s_n) for p in range(p_n)
    ]
    ends = jnp.concatenate(ends, axis=0).reshape(shape)
    n = low.shape[0]
    moved = pltpu.roll(low.astype(F32), n - 1, 0).reshape(shape)
    place = lax.broadcasted_iota(jnp.int32, shape, 1)
    following = flat(jnp.where(place == t_n - 1, ends, moved) * m16[2:3, :, 0:1]).astype(BF16)
    own = dot_nt(low, wlat[2 * LANES : 5 * LANES, :])
    late = dot_nt(following, wlat[0 : 2 * LANES, :])
    gs[pl.ds(0, n, stride=4), :] = own[:, 0:LANES]
    gs[pl.ds(1, n, stride=4), :] = own[:, LANES : 2 * LANES]
    gs[pl.ds(2, n, stride=4), :] = own[:, 2 * LANES :] + late[:, 0:LANES]
    gs[pl.ds(3, n, stride=4), :] = late[:, LANES:]
    back = dot(flat(dlow[...]), wfa[...])
    for s in range(s_n):
        cols = slice(s * LANES, (s + 1) * LANES)
        total = flat(df[:, :, cols]) + back[:, cols] + gs[s * n : (s + 1) * n, :]
        out[s] = total.astype(BF16).reshape(out.shape[1:])


def each(first, last, body):
    def step(k, carry):
        body(k)
        return carry
    lax.fori_loop(first, last, step, 0)


NEAR = 4


class Cube:
    def __init__(self, ch, far):
        self.ch, self.far = ch, far
        self.p, self.f = lax.axis_index("path"), lax.axis_index("frames")
        self.q, self.r = lax.rem(self.f, NEAR), lax.div(self.f, NEAR)
        self.sibling = (1 - self.p, self.f)

    def q_of(self, k):
        low = (self.q % 2 + k % 2) % 2
        return (self.q // 2 + k // 2) % 2 * 2 + low

    def r_of(self, k):
        return lax.rem(self.r + k, self.far)

    def plane(self, k):
        return (self.p, self.r * NEAR + self.q_of(k))

    def line(self, k):
        return (self.p, self.r_of(k) * NEAR + self.q)

    def at(self, path, q, r):
        return pl.ds(pl.multiple_of(((path * NEAR + q) * self.far + r) * self.ch, 16), self.ch)


def remote(src, dst, sem, index, device):
    return pltpu.make_async_remote_copy(
        src_ref=src, dst_ref=dst, send_sem=sem.at[(0, *index)], recv_sem=sem.at[(1, *index)],
        device_id=device, device_id_type=MESH)


def rows_for(sizes, n):
    unit = 16 * sizes[0] * sizes[1]
    return -(-n // unit) * unit


class Stream:
    def __init__(self, sizes, rows_n, width):
        self.sizes, self.rows_n, self.width = sizes, rows_n, width
        self.far = sizes[1] // NEAR
        self.ch = rows_n // (sizes[0] * sizes[1])
        self.chunk = (self.ch, width)
        self.near_shape = (self.far, *self.chunk)
        quad = pltpu.VMEM((NEAR, *self.near_shape), BF16)
        quad_sems, line_sems = pltpu.SemaphoreType.DMA((2, NEAR, self.far)), pltpu.SemaphoreType.DMA((2, self.far))
        self.near_scratch = [quad, quad, quad, pltpu.VMEM(self.chunk, F32), quad_sems, quad_sems]
        self.line_scratch = [pltpu.VMEM(self.near_shape, BF16), pltpu.VMEM(self.chunk, F32), line_sems]
        self.share_scratch = [line_sems, quad_sems, quad_sems, pltpu.SemaphoreType.DMA]


class Near:
    def __init__(self, stream, x, out, scratch):
        self.x, self.out, self.far, self.c = x, out, stream.far, Cube(stream.ch, stream.far)
        self.land_a, self.buf_b, self.land_b, self.acc, self.sem_a, self.sem_b = scratch

    def pair(self, k, m):
        c = self.c
        return remote(self.x.at[c.at(1 - c.p, c.q_of(k), c.r_of(m + 1))], self.land_a.at[k, m], self.sem_a, (k, m), c.sibling)

    def plane(self, k, m):
        return remote(self.buf_b.at[k, m], self.land_b.at[k, m], self.sem_b, (k, m), self.c.plane(k))

    def start(self):
        def one(m):
            each(1, NEAR, lambda k: self.pair(k, m).start())
            self.pair(0, m).start()

        each(0, self.far, one)

    def add_pair(self, first, last):
        c = self.c

        def one(k, m):
            self.pair(k, m).wait_recv()
            mine = self.x[c.at(c.p, c.q_of(k), c.r_of(m + 1)), :]
            self.buf_b[k, m] = (mine.astype(F32) + self.land_a[k, m].astype(F32)).astype(BF16)
            self.plane(k, m).start()

        each(first, last, lambda m: each(1, NEAR, lambda k: one(k, m)))

    def add_plane(self, first, last, then=None):
        c = self.c

        def one(m):
            self.pair(0, m).wait_recv()
            self.acc[...] = self.x[c.at(c.p, c.q, c.r_of(m + 1)), :].astype(F32) + self.land_a[0, m].astype(F32)

            def more(k):
                self.plane(k, m).wait_recv()
                self.acc[...] += self.land_b[k, m].astype(F32)

            each(1, NEAR, more)
            self.out[m] = self.acc[...].astype(BF16)
            if then is not None:
                then(m)

        each(first, last, one)

    def end(self):
        each(0, self.far, lambda m: each(0, NEAR, lambda k: self.pair(k, m).wait_send()))
        each(0, self.far, lambda m: each(1, NEAR, lambda k: self.plane(k, m).wait_send()))


class Line:
    def __init__(self, stream, near, scratch):
        self.near, self.far, self.c = near, stream.far, Cube(stream.ch, stream.far)
        self.land, self.acc, self.sem = scratch

    def line(self, m):
        return remote(self.near.at[m], self.land.at[m], self.sem, (m,), self.c.line(m + 1))

    def start(self, first, last):
        each(first, min(last, self.far - 1), lambda m: self.line(m).start())

    def total(self):
        self.acc[...] = self.near[self.far - 1].astype(F32)

        def one(m):
            self.line(m).wait_recv()
            self.acc[...] += self.land[m].astype(F32)

        each(0, self.far - 1, one)
        return self.acc[...].astype(BF16)

    def end(self):
        each(0, self.far - 1, lambda m: self.line(m).wait_send())


class Share:
    def __init__(self, stream, res, out, scratch):
        self.res, self.out, self.far, self.c = res, out, stream.far, Cube(stream.ch, stream.far)
        self.cut = stream.ch // 32 * 16
        self.sem_d, self.sem_e, self.sem_f, self.sem_own = scratch

    def own(self):
        return self.out.at[self.c.at(self.c.p, self.c.q, self.c.r)]

    def keep(self):
        return pltpu.make_async_copy(self.res, self.own(), self.sem_own)

    def line_back(self, k):
        return remote(self.res, self.own(), self.sem_d, (k,), self.c.line(k))

    def part(self, q, m):
        return self.out.at[self.c.at(self.c.p, q, self.c.r_of(self.far - m))]

    def plane_back(self, k, m, src=None):
        dst = self.part(self.c.q, m)
        return remote(dst if src is None else src, dst, self.sem_e, (k, m), self.c.plane(k))

    def pair_back(self, k, m, src=None):
        dst = self.part(self.c.q_of(k), m)
        return remote(dst if src is None else src, dst, self.sem_f, (k, m), self.c.sibling)

    def start_line(self):
        each(1, self.far, lambda k: self.line_back(k).start())

    def half(self, k, m):
        c, cut = self.c, self.cut
        start = ((c.p * NEAR + c.q_of(k)) * self.far + c.r_of(self.far - m)) * c.ch
        rows_n = cut if k == 1 else c.ch - cut
        part = self.out.at[pl.ds(pl.multiple_of(start + (0 if k == 1 else cut), 16), rows_n)]
        return remote(part, part, self.sem_e, (3 if k == 1 else 0, m), c.plane(3 - k))

    def start_plane(self):
        each(1, NEAR - 1, lambda k: self.plane_back(k, 0, self.res).start())
        self.pair_back(0, 0, self.res).start()
        self.keep().start()

    def relay(self, first, last):
        def one(m):
            self.line_back(m).wait_recv()
            each(1, NEAR - 1, lambda k: self.plane_back(k, m).start())
            self.pair_back(0, m).start()

        each(first, last, one)

    def hand_on(self, first, last):
        def one(m):
            for k in (1, 2):
                self.plane_back(k, m).wait_recv()
                self.half(k, m).start()
                self.pair_back(k, m).start()

        each(first, last, one)

    def hand_across(self, first, last):
        def one(m):
            for k in (1, 2):
                self.half(k, m).wait_recv()
            self.pair_back(3, m).start()

        each(first, last, one)

    def end(self):
        each(0, self.far, lambda m: each(0, NEAR, lambda k: self.pair_back(k, m).wait()))
        self.keep().wait()
        each(1, self.far, lambda k: self.line_back(k).wait_send())
        each(0, self.far, lambda m: each(1, NEAR - 1, lambda k: self.plane_back(k, m).wait_send()))

        def sent(m):
            for k in (1, 2):
                self.half(k, m).wait_send()

        each(0, self.far, sent)


def k_tail(cfg, *refs):
    st_a, st_b, ex7, ex8, side = cfg
    it = iter(refs)

    def take(n):
        return [next(it) for _ in range(n)]

    hbm = take(13)
    x_slow, lact_src, taps_src = take(3)
    gb, c1, c2, c3, q6, m16, m64, g_fout, g_fmid = take(9)
    low_out, dlow_out, lat_low_out, gf, gw_in, gw_lat, q7, q8, hn, res_a, near_b = take(11)
    local = take(13)
    gw_a, dsb, sb, spad, wsp, sa, x_fast, dfa, fa, w_in, w_sc, dsp, lat = local
    pad, gsp, gin, low, dlow, gw_b, near_a, ends, s1, s2, t1, t2, sems, out_sems = take(14)
    x_part, taps_part, gsi, glat, wsp_turned, x_sems, taps_sems, lact_sem = take(8)
    near1, line1, near2 = take(len(st_a.near_scratch)), take(len(st_a.line_scratch)), take(len(st_b.near_scratch))
    scr7 = take(len(ex7.local) + len(ex7.work))
    scr8 = take(len(ex8.local) + len(ex8.work))
    n_in = w_in.shape[0]
    srcs = list(hbm)
    for k in (9, 10):
        srcs[k] = hbm[k].at[pl.ds(hbm[k].shape[0] - n_in, n_in)]
    loads = [pltpu.make_async_copy(src, dst, sems.at[k]) for k, (src, dst) in enumerate(zip(srcs, local))]
    count = exchange_hello(ex8)
    for k in (1, 2, 0, 4, 3, 5, 6, 7, 8, 9, 10, 11, 12):
        loads[k].start()
    near = Near(st_a, gw_a, near_a, near1)
    line = Line(st_a, near_a, line1)
    near_two = Near(st_b, gw_b, near_b, near2)
    far = st_a.far
    t_n, c = pad.shape[2], pad.shape[3]
    wide = side * t_n
    per = side // STEPS
    fill = m16[0:1, :, 0:1]

    def waits(*names):
        for k in names:
            loads[k].wait()

    waits(1, 2)
    scale, p_row, q_row = rows(c3, 0, 4, 2), rows(q6, 0, 0, 2), rows(q6, 1, 0, 2)
    zero_ref(pad)

    def fill_pad(h):
        part = pl.ds(h * wide, wide)
        d = back_norm(
            scale, p_row, q_row, dsb[part].reshape(side, t_n, c), sb[part].reshape(side, t_n, c), fill
        )
        pad[h + 1, 1 : side + 1] = d.astype(BF16)

    each(0, side, fill_pad)
    waits(0, 4)
    for k in range(9):
        wsp_turned[k * c : (k + 1) * c, :] = wsp[k * c : (k + 1) * c, :].T
    pl.semaphore_wait(pltpu.get_barrier_semaphore(), count)
    near.start()
    waits(3, 5, 6, 7, 8)
    f_n = x_fast.shape[2]
    p_n = x_fast.shape[1] // STEPS

    def spatial(i):
        h0 = i * per
        turned = flat(pad[pl.ds(h0 + 1, per), 1 : side + 1]).T
        blocks = []
        for a in range(3):
            for b in range(3):
                k = 3 * a + b
                patch = flat(spad[pl.ds(h0 + a, per), b : b + side])
                cols = slice(k * c, (k + 1) * c)
                gsp[:, cols] = jnp.where(i == 0, 0.0, gsp[:, cols]) + dot(turned, patch)
                blocks.append(flat(pad[pl.ds(h0 + 2 - a, per), 2 - b : 2 - b + side]))
        acc = dot(jnp.concatenate(blocks, axis=1), wsp_turned[...])
        span = pl.ds(i * per * wide, per * wide)
        z = sa[span]
        back = acc * slope(z * rows(c2, 0, 1, 2) + rows(c2, 1, 1, 2))
        dsb[span] = back
        unit = z * rows(c2, 2, 1, 2) - rows(c2, 3, 1, 2)
        sum_add(i, back.reshape(per * side, t_n, c), s1)
        sum_add(i, (back * unit).reshape(per * side, t_n, c), s2)
        f_span = pl.ds(i * p_n, p_n)
        small = back_norm(
            rows(c1, 0, 0, 1), rows(q6, 0, 2, 1), rows(q6, 1, 2, 1), dfa[f_span], fa[f_span], m64[0:1]
        ).astype(BF16)
        dlow[f_span] = small
        packed = jnp.concatenate([flat(x_fast[s, f_span]) for s in range(x_fast.shape[0])], axis=1)
        add_to(i, gin, dot_tn(flat(small), packed))
        pl.when(i == 0)(lambda: near.add_pair(0, far // 2))
        pl.when(i == 1)(lambda: near.add_pair(far // 2, far))

    each(0, STEPS, spatial)
    stats = scr7[0]
    zero_ref(stats)
    put_rows(stats, 0, sum_end(s1))
    put_rows(stats, 2, sum_end(s2))
    stores = [pltpu.make_async_copy(dlow, dlow_out, out_sems.at[0])]
    stores[0].start()

    def late():
        for k in range(9):
            gw_b[k * c : (k + 1) * c, :] = gsp[:, k * c : (k + 1) * c].T.astype(BF16)
        if 9 * c < gw_b.shape[0]:
            gw_b[9 * c :, :] = jnp.zeros((gw_b.shape[0] - 9 * c, c), BF16)
        n = g_fout.shape[0]
        gf[0:n, 0:LANES] = fold_wide(gin, x_fast.shape[0])
        gf[0:n, LANES:] = g_fout[...]
        gf[n : 2 * n, 0:LANES] = g_fmid[0:n, :]
        gf[n : 2 * n, LANES:] = g_fmid[n : 2 * n, :]
        gf[2 * n :, 0:LANES] = g_fmid[2 * n :, :]
        gf[2 * n :, LANES:] = jnp.zeros((n, LANES), F32)

    n_pos = side * side
    lact = spad.reshape(-1, t_n, c).at[pl.ds(0, n_pos)]
    lat_low = pad.reshape(-1, t_n, c).at[pl.ds(0, n_pos)]
    lact_load = pltpu.make_async_copy(lact_src, lact, lact_sem)
    lact_load.start()
    block = per * wide

    def x_load(i):
        return pltpu.make_async_copy(x_slow.at[pl.ds(i * block, block)], x_part.at[i % 2], x_sems.at[i % 2])

    def taps_load(i):
        return pltpu.make_async_copy(taps_src.at[pl.ds(i * block, block)], taps_part.at[i % 2], taps_sems.at[i % 2])

    for i in range(2):
        x_load(i).start()
        taps_load(i).start()
    exchange_run(ex7, [gb, c2], [q7], scr7, late)
    near_two.start()
    near.add_plane(0, far - 1, lambda m: line.line(m).start())
    near.add_plane(far - 1, far)
    waits(9, 10, 11, 12)
    scale7, p7, q7_row = rows(c2, 0, 1, 2), rows(q7, 0, 0, 2), rows(q7, 1, 0, 2)

    def join(i):
        span = pl.ds(i * block, block)
        shape = (per * side, t_n, c)
        d = back_norm(scale7, p7, q7_row, dsb[span].reshape(shape), sa[span].reshape(shape), fill)
        small = flat(d).astype(BF16)
        low[span] = small
        d = dot_nt(dsp[span], w_sc[...]) + dot_nt(small, w_in[...])
        z = lat[span]
        back = d * slope(z * rows(c1, 0, 1, 2) + rows(c1, 1, 1, 2))
        sb[span] = back
        unit = z * rows(c1, 2, 1, 2) - rows(c1, 3, 1, 2)
        sum_add(i, back.reshape(shape), t1)
        sum_add(i, (back * unit).reshape(shape), t2)
        pl.when(i == 2)(lambda: near_two.add_pair(0, far))

    each(0, STEPS, join)
    stores.append(pltpu.make_async_copy(low, low_out, out_sems.at[1]))
    stores[1].start()
    stats = scr8[0]
    zero_ref(stats)
    put_rows(stats, 0, sum_end(t1))
    put_rows(stats, 2, sum_end(t2))

    def post(q, sent):
        d = back_norm(rows(c1, 0, 1, 2), rows(q, 0, 0, 2), rows(q, 1, 0, 2), ends[0], ends[1], m16[0, 0:1, 0:1])
        sent[...] = d.astype(BF16)

    def in_step(i):
        x_load(i).wait()
        joined = jnp.concatenate([x_part[i % 2], flat(lact[pl.ds(i * per * side, per * side)])], axis=1)
        add_to(i, gsi, dot(low[pl.ds(i * block, block)].T, joined))
        pl.when(i + 2 < STEPS)(lambda: x_load(i + 2).start())

    def in_grad():
        zero_ref(ends)
        for s in range(x_fast.shape[0]):
            for step in range(STEPS):
                for p in range(p_n):
                    at = ((s * STEPS + step) * p_n + p) * t_n
                    ends[0, step, s * 8 + p : s * 8 + p + 1, :] = sb[at : at + 1, :]
                    ends[1, step, s * 8 + p : s * 8 + p + 1, :] = lat[at : at + 1, :]
        lact_load.wait()
        each(0, 3, in_step)

    def in_grad_rest():
        each(3, STEPS, in_step)
        for n in range(gsi.shape[1] // c):
            gw_in[n * c : (n + 1) * c, :] = gsi[:, n * c : (n + 1) * c].T.astype(BF16)

    def lat_step(i):
        scale8, p8, q8_row = rows(c1, 0, 1, 2), rows(q8, 0, 0, 2), rows(q8, 1, 0, 2)
        span = pl.ds(i * block, block)
        shape = (per * side, t_n, c)
        d = back_norm(scale8, p8, q8_row, sb[span].reshape(shape), lat[span].reshape(shape), fill).astype(BF16)
        lat_low[pl.ds(i * per * side, per * side)] = d
        taps_load(i).wait()
        add_to(i, glat, dot_tn(flat(d), taps_part[i % 2]))
        pl.when(i + 2 < STEPS)(lambda: taps_load(i + 2).start())

    def lat_grad():
        each(0, STEPS, lat_step)
        stores.append(pltpu.make_async_copy(lat_low, lat_low_out, out_sems.at[2]))
        stores[2].start()
        for k in range(glat.shape[1] // LANES):
            gw_lat[k * LANES : (k + 1) * LANES, :] = glat[:, k * LANES : (k + 1) * LANES].T.astype(BF16)

    exchange_run(ex8, [gb, c1], [q8, hn], scr8, in_grad, post, lat_grad, in_grad_rest)
    res_a[...] = line.total()
    near_two.add_plane(0, far)
    for store in stores:
        store.wait()
    line.end()
    near.end()
    near_two.end()


def back_tail(st_a, st_b, ex7, ex8, hbm, more, small, side, t_n, c):
    vm, anywhere = pl.BlockSpec(memory_space=pltpu.VMEM), pl.BlockSpec(memory_space=pl.ANY)
    inner, f_n = hbm[7].shape[:2]
    n = side * side * t_n
    c_cat, c_taps = more[0].shape[1] + c, more[2].shape[1]
    part = n // STEPS
    outs = [((n, c), BF16), ((inner, f_n, LANES), BF16), (more[1].shape, BF16), (small[-1].shape[0:1] + (2 * LANES,), F32),
            ((c_cat, c), BF16), ((c_taps, c), BF16),
            *ex7.outs, *ex8.outs, (st_a.chunk, BF16), (st_b.near_shape, BF16)]
    local = [pltpu.VMEM((c,) + a.shape[1:] if k in (9, 10) else a.shape, a.dtype) for k, a in enumerate(hbm)]
    width = hbm[6].shape[0] * hbm[6].shape[3]
    scratch = [
        pltpu.VMEM((side + 2, side + 2, t_n, c), BF16), pltpu.VMEM((c, 9 * c), F32), pltpu.VMEM((LANES, width), F32),
        pltpu.VMEM((n, c), BF16), pltpu.VMEM((inner, f_n, LANES), BF16), pltpu.VMEM((st_b.rows_n, c), BF16),
        pltpu.VMEM(st_a.near_shape, BF16), pltpu.VMEM((2, *ex8.post), F32), *[pltpu.VMEM((t_n, c), F32)] * 4,
        pltpu.SemaphoreType.DMA((len(hbm),)), pltpu.SemaphoreType.DMA((3,)),
        pltpu.VMEM((2, part, c_cat - c), BF16), pltpu.VMEM((2, part, c_taps), BF16), pltpu.VMEM((c, c_cat), F32),
        pltpu.VMEM((c, c_taps), F32), pltpu.VMEM((9 * c, c), BF16), pltpu.SemaphoreType.DMA((2,)), pltpu.SemaphoreType.DMA((2,)), pltpu.SemaphoreType.DMA,
        *st_a.near_scratch, *st_a.line_scratch, *st_b.near_scratch, *ex7.local, *ex7.work, *ex8.local, *ex8.work,
    ]
    return pl.pallas_call(
        functools.partial(k_tail, (st_a, st_b, ex7, ex8, side)),
        out_shape=[jax.ShapeDtypeStruct(s, d) for s, d in outs],
        in_specs=[anywhere] * (len(hbm) + len(more)) + [vm] * len(small),
        out_specs=[anywhere] * 3 + [vm] * (len(outs) - 3),
        scratch_shapes=[*local, *scratch],
        compiler_params=pltpu.CompilerParams(collective_id=ex8.cid, has_side_effects=True, vmem_limit_bytes=VMEM_LIMIT),
        name="tail",
    )(*hbm, *more, *small)


def final_kernel(cfg, *refs):
    first, second, third, both, offsets, n_hbm, n_small = cfg
    it = iter(refs)

    def take(n):
        return [next(it) for _ in range(n)]

    hbm, small, (out_a, out_bc, gx_out, fast_out) = take(n_hbm), take(n_small), take(4)
    res_a, near_b, *parts, hn, m16, wlat, wfa = small
    loaded = take(n_hbm)
    low, dsp, w_in, w_sc, lat_low, df, dlow = loaded
    x, near_c, res, gx, fast_gx, gs, sems, gx_sems, fast_sems = take(9)
    share_a = Share(first, res_a, out_a, take(len(first.share_scratch)))
    line_b = Line(second, near_b, take(len(second.line_scratch)))
    near = Near(third, x, near_c, take(len(third.near_scratch)))
    line_c = Line(third, near_c, take(len(third.line_scratch)))
    share = Share(both, res, out_bc, take(len(both.share_scratch)))
    far, c = first.far, near.c
    barrier = pltpu.get_barrier_semaphore()
    loads = [pltpu.make_async_copy(a, b, sems.at[k]) for k, (a, b) in enumerate(zip(hbm, loaded))]

    def greet(device):
        pl.semaphore_signal(barrier, inc=1, device_id=device, device_id_type=MESH)

    greet(c.sibling)
    each(1, NEAR, lambda k: greet(c.plane(k)))
    each(1, far, lambda k: greet(c.line(k)))
    for load in loads:
        load.start()
    for ref, first_row, end in zip(parts, offsets, offsets[1:]):
        x[first_row:end, :] = ref[...].astype(BF16)
    if end < x.shape[0]:
        x[end:, :] = jnp.zeros((x.shape[0] - end, x.shape[1]), BF16)
    pl.semaphore_wait(barrier, NEAR + far - 1)

    near.start()
    line_b.start(0, far)
    share_a.start_line()
    p_n = dlow.shape[0] // STEPS

    def gx_store(i):
        part = pl.ds(i * p_n, p_n)
        return pltpu.make_async_copy(gx.at[:, part], gx_out.at[:, part], gx_sems.at[i])

    def slow_step(i):
        part = pl.ds(i * p_n, p_n)
        slow_grad(low.at[:, part], dsp.at[:, part], w_in, w_sc, gx.at[:, part])
        gx_store(i).start()

    def fast_store(i):
        part = pl.ds(i * p_n, p_n)
        return pltpu.make_async_copy(fast_gx.at[:, part], fast_out.at[:, part], fast_sems.at[i])

    def fast_step(i):
        part = pl.ds(i * p_n, p_n)
        fast_grad(lat_low.at[:, part], hn.at[pl.ds(i, 1)], df.at[part], dlow.at[part], m16, wlat, wfa,
                  fast_gx.at[:, part], gs)
        fast_store(i).start()

    share_a.start_plane()
    near.add_pair(0, far)
    for k in (0, 1, 2, 3):
        loads[k].wait()
    each(0, 1, slow_step)
    res[0 : second.ch, :] = line_b.total()
    share_a.relay(1, far)
    share_a.hand_on(0, 1)
    each(1, 3, slow_step)
    near.add_plane(0, far - 1, lambda m: line_c.line(m).start())
    near.add_plane(far - 1, far)
    share_a.hand_on(1, far)
    each(3, 4, slow_step)
    res[second.ch :, :] = line_c.total()
    share.start_line()
    share.start_plane()
    each(4, STEPS, slow_step)
    for k in range(4, n_hbm):
        loads[k].wait()
    share.relay(1, far)
    share_a.hand_across(0, far)
    share.hand_on(0, 1)
    each(0, 3, fast_step)
    share.hand_on(1, far)
    each(3, STEPS, fast_step)
    share.hand_across(0, far)
    share_a.end()
    share.end()
    line_b.end()
    line_c.end()
    near.end()
    each(0, STEPS, lambda i: gx_store(i).wait())
    each(0, STEPS, lambda i: fast_store(i).wait())


def final_sum(sizes, cid, first, second, hbm, small, gx, fast_gx, heights):
    width = first.width
    offsets = tuple(sum(heights[:k]) for k in range(len(heights) + 1))
    third = Stream(sizes, rows_for(sizes, offsets[-1]), width)
    both = Stream(sizes, second.rows_n + third.rows_n, width)
    vm, anywhere = pl.BlockSpec(memory_space=pltpu.VMEM), pl.BlockSpec(memory_space=pl.ANY)
    low, dlow = hbm[0], hbm[6]
    s_n, p_n, f_n = low.shape[0], low.shape[1] // STEPS, dlow.shape[1]
    out_a, out_bc, gx, fast_gx = pl.pallas_call(
        functools.partial(final_kernel, (first, second, third, both, offsets, len(hbm), len(small))),
        out_shape=[jax.ShapeDtypeStruct(s, BF16) for s in ((first.rows_n, width), (both.rows_n, width), gx, fast_gx)],
        in_specs=[anywhere] * len(hbm) + [vm] * len(small),
        out_specs=[anywhere] * 4,
        scratch_shapes=[
            *[pltpu.VMEM(a.shape, a.dtype) for a in hbm],
            pltpu.VMEM((third.rows_n, width), BF16), pltpu.VMEM(third.near_shape, BF16), pltpu.VMEM(both.chunk, BF16),
            pltpu.VMEM(gx, BF16), pltpu.VMEM(fast_gx, BF16), pltpu.VMEM((s_n * p_n * f_n, LANES), F32),
            pltpu.SemaphoreType.DMA((len(hbm),)), pltpu.SemaphoreType.DMA((STEPS,)), pltpu.SemaphoreType.DMA((STEPS,)),
            *first.share_scratch, *second.line_scratch, *third.near_scratch, *third.line_scratch, *both.share_scratch,
        ],
        compiler_params=pltpu.CompilerParams(collective_id=cid, has_side_effects=True, vmem_limit_bytes=VMEM_LIMIT),
        name="final_sum",
    )(*hbm, *small)
    return out_a, out_bc.reshape(-1, both.ch, width), gx, fast_gx


def k_unpack(pieces, cut, *refs):
    (src_a, src_b, q4, q5, q6, q7, q8), held, refs = refs[:7], refs[7:10], refs[10:]
    outs, (low_a, low_b, low_c, wide, line, *kept, sem_a, sem_b, sem_out, sem_held) = refs[:-12], refs[-12:]
    outs, given = outs[:-3], outs[-3:]

    def moves(srcs, dsts, way):
        return [
            pltpu.make_async_copy(a.at[pl.ds(k, 1)], b.at[pl.ds(k, 1)], sem_held.at[way, n, k])
            for n, (a, b) in enumerate(zip(srcs, dsts))
            for k in range(a.shape[0])
        ]

    passes_in, passes = moves(held, kept, 0), moves(kept, given, 1)
    outs, (gains_out, biases_out, in_out, mid_out, out_out) = outs[:-5], outs[-5:]
    lows = (low_a, low_b, low_c)
    flats = [low_a, low_b.reshape(-1, low_b.shape[-1]), low_c.reshape(-1, low_c.shape[-1])]
    starts = [sum(p[2] for p in pieces[:k]) for k in range(len(pieces))]

    def fetch_a(k):
        _, row, height, _, _ = pieces[k]
        return pltpu.make_async_copy(src_a.at[pl.ds(row, height)], low_a.at[pl.ds(row, height)], sem_a.at[k])

    def fetch_b(k):
        part = src_b.at[:, pl.ds(0, cut)] if k == 1 else src_b.at[:, pl.ds(cut, src_b.shape[1] - cut)]
        return pltpu.make_async_copy(part, lows[k], sem_b.at[k])

    def store(k):
        _, _, height, out, col = pieces[k]
        part = outs[out] if col is None else outs[out].at[:, pl.ds(col, wide.shape[1])]
        return pltpu.make_async_copy(wide.at[pl.ds(starts[k], height)], part, sem_out.at[k])

    for k, piece in enumerate(pieces):
        if piece[0] == 0:
            fetch_a(k).start()
    for k in (1, 2):
        fetch_b(k).start()
    for move in passes_in:
        move.start()
    seen = 0
    for k, (src, row, height, _, _) in enumerate(pieces):
        if src == 0:
            fetch_a(k).wait()
        elif src != seen:
            fetch_b(src).wait()
            seen = src
        wide[starts[k] : starts[k] + height, :] = flats[src][row : row + height, :].astype(F32)
        store(k).start()
    for move_in, move in zip(passes_in, passes):
        move_in.wait()
        move.start()
    lane = lax.broadcasted_iota(jnp.int32, (1, LANES), 1)
    left = lane < LANES // 2
    for slab, out in ((3, gains_out), (2, biases_out)):
        at = 0
        for q, first, count in ((q4, 0, 1), (q8, 0, 2), (q7, 0, 2), (q6, 0, 2), (q5, 0, 16)):
            line[at : at + count, :] = q[slab, first : first + count, :]
            at += count
        half = pltpu.roll(line[0:at, :], LANES // 2, 1)
        head = jnp.where(lane < LANES // 4, q6[slab, 2:3, :], q5[slab, 16:17, :])
        out[0:1, :] = jnp.where(left, head, half[0:1])
        out[1:at, :] = jnp.where(left, half[0 : at - 1], half[1:at])
        out[at : at + 1, :] = jnp.where(left, half[at - 1 : at], 0.0)
    a = in_out.shape[0]
    last = sum(p[2] for p in pieces if p[0] == 2)
    small = flats[2][last : last + 3 * a, :]
    in_out[...] = small[0:a, 0:LANES].astype(F32)
    out_out[...] = small[0:a, LANES:].astype(F32)
    eye = (lax.broadcasted_iota(jnp.int32, (a, a), 0) == lax.broadcasted_iota(jnp.int32, (a, a), 1)).astype(BF16)
    for k, (row, col) in enumerate(((a, 0), (a, LANES), (2 * a, 0))):
        mid_out[k] = dot_tn(small[row : row + a, col : col + LANES], eye)[0:a, :]
    for k in range(len(pieces)):
        store(k).wait()
    for move in passes:
        move.wait()


def unpack(src_a, src_b, cut, pieces, shapes, small_shapes, norm_sums, held):
    hbm, vm = pl.BlockSpec(memory_space=pl.ANY), pl.BlockSpec(memory_space=pltpu.VMEM)
    n, _, width = src_b.shape
    return pl.pallas_call(
        functools.partial(k_unpack, pieces, cut),
        out_shape=[jax.ShapeDtypeStruct(s, F32) for s in (*shapes, *small_shapes)]
        + [jax.ShapeDtypeStruct(a.shape, a.dtype) for a in held],
        in_specs=[hbm] * 2 + [vm] * len(norm_sums) + [hbm] * len(held),
        out_specs=[hbm] * len(shapes) + [vm] * len(small_shapes) + [hbm] * len(held),
        scratch_shapes=[
            pltpu.VMEM(src_a.shape, BF16),
            pltpu.VMEM((n, cut, width), BF16),
            pltpu.VMEM((n, src_b.shape[1] - cut, width), BF16),
            pltpu.VMEM((sum(p[2] for p in pieces), width), F32),
            pltpu.VMEM((24, LANES), F32),
            *[pltpu.VMEM(a.shape, a.dtype) for a in held],
            pltpu.SemaphoreType.DMA((len(pieces),)),
            pltpu.SemaphoreType.DMA((3,)),
            pltpu.SemaphoreType.DMA((len(pieces),)),
            pltpu.SemaphoreType.DMA((2, len(held), held[0].shape[0])),
        ],
        compiler_params=pltpu.CompilerParams(vmem_limit_bytes=VMEM_LIMIT),
        name="unpack",
    )(src_a, src_b, *norm_sums, *held)


def small_set_up(fill_ref, clip_ref, norm_ref, wfi_ref, wfm_ref, wfo_ref,
                 gb_ref, m16_ref, m64_ref, wfa_ref, wmid_ref, wback_ref, wout_ref, s_n, t_n):
    length = lax.axis_size("frames")
    total = lax.axis_size("path") * length
    me = lax.axis_index("path") * length + lax.axis_index("frames")
    lane = lax.broadcasted_iota(jnp.int32, (1, LANES), 1)
    for k in range(2):
        half = pltpu.roll(norm_ref[k], LANES // 2, 1)
        main = jnp.where(lane < LANES // 2, half[0:23], half[1:24])
        for j in range(2):
            v = jnp.where(lane // 32 == j, norm_ref[k, 0:1, :], 0.0)
            v = v + pltpu.roll(v, 64, 1)
            gb_ref[k, j : j + 1, :] = v + pltpu.roll(v, 32, 1)
        for j in range(4):
            gb_ref[k, 2 + j : 3 + j, :] = main[0:1]
        gb_ref[k, 6:28, :] = main[1:23]
        gb_ref[k, 28:32, :] = jnp.zeros((4, LANES), F32)

    def row(value):
        return jnp.full((1, LANES), value, F32)

    last = jnp.where(me < total - 1, 1.0, 0.0)
    link = [jnp.where(clip_ref[t] >= 1, 1.0, 0.0) for t in range(t_n)]
    for t in range(t_n):
        filled = row(fill_ref[t].astype(F32))
        after = row(link[t + 1] if t + 1 < t_n else last)
        m16_ref[0, t : t + 1, :] = filled
        m16_ref[1, t : t + 1, :] = row(link[t])
        m16_ref[2, t : t + 1, :] = after
        m64_ref[0, 4 * t : 4 * t + 4, :] = jnp.broadcast_to(filled, (4, LANES))
        m64_ref[1, 4 * t : 4 * t + 1, :] = row(link[t])
        m64_ref[1, 4 * t + 1 : 4 * t + 4, :] = jnp.ones((3, LANES), F32)
        m64_ref[2, 4 * t : 4 * t + 3, :] = jnp.ones((3, LANES), F32)
        m64_ref[2, 4 * t + 3 : 4 * t + 4, :] = after

    zero_ref(wfa_ref)
    zero_ref(wout_ref)
    a = wfi_ref.shape[0]
    for s in range(s_n):
        wfa_ref[s * a : (s + 1) * a, s * LANES : (s + 1) * LANES] = wfi_ref[...]
        wout_ref[s * a : (s + 1) * a, s * LANES : (s + 1) * LANES] = wfo_ref[...]
    tall = (LANES, a)
    spread = (lax.broadcasted_iota(jnp.int32, tall, 0) % a == lax.broadcasted_iota(jnp.int32, tall, 1)).astype(BF16)
    square = (LANES, LANES)
    diag = lax.broadcasted_iota(jnp.int32, square, 0) // a == lax.broadcasted_iota(jnp.int32, square, 1) // a
    for k in range(3):
        left = dot(spread, wfm_ref[k]).astype(BF16)
        wmid_ref[k * LANES : (k + 1) * LANES, :] = jnp.where(diag, dot_nt(left, spread), 0.0).astype(BF16)
        right = dot_nt(spread, wfm_ref[k]).astype(BF16)
        wback_ref[k * LANES : (k + 1) * LANES, :] = jnp.where(diag, dot_nt(right, spread), 0.0).astype(BF16)


def per_device(slow_input, fast_input, clip_offset, fill, w_fast_in, w_fast_mid, w_fast_out, w_lateral,
               w_slow_in, w_slow_mid, w_slow_out, w_shortcut, gains, biases, slow_cot, fast_cot):
    sizes = (lax.axis_size("path"), lax.axis_size("frames"))
    t_n, side, _, c_slow = slow_input.shape
    f_n, c_fast = fast_input.shape[0], fast_input.shape[3]
    in_fast, in_slow, c_lat = w_fast_in.shape[1], w_slow_in.shape[1], w_lateral.shape[2]
    pixels = side * side
    groups = LANES // in_fast
    inner = pixels // groups
    p_n = inner // STEPS

    def slow_view(a):
        return jnp.transpose(a, (1, 2, 0, 3)).reshape(groups, inner, t_n, a.shape[3])

    def fast_view(a):
        return jnp.transpose(a, (1, 2, 0, 3)).reshape(groups, inner, f_n, a.shape[3])

    def unview(a):
        return jnp.transpose(a.reshape(side, side, a.shape[2], a.shape[3]), (2, 0, 1, 3))

    x_slow, cot_slow = slow_view(slow_input), slow_view(slow_cot)
    x_fast, cot_fast = fast_view(fast_input), fast_view(fast_cot)

    norms = jnp.stack([gains, biases])
    norms = jnp.pad(norms, ((0, 0), (0, -norms.shape[1] % (8 * LANES)))).reshape(2, -1, LANES)
    wlat = w_lateral.reshape(-1, c_lat)
    wsp = w_slow_mid.reshape(-1, in_slow)

    sl = (groups, inner, t_n)
    fp = (inner, f_n)

    def slow_out(width, dtype):
        return out_blocked(sl + (width,), dtype, 1, p_n)

    def fast_out(width, dtype):
        return out_blocked(fp + (width,), dtype, 0, p_n)

    def sb_(a):
        return blocked(a, 1, p_n)

    def fb_(a):
        return blocked(a, 0, p_n)

    def stat(n):
        return out_whole((pad8(n), LANES), F32)

    def acc(rows_n, width, count):
        return [pltpu.VMEM((rows_n, width), F32)] * count

    small = (STEPS, 8, LANES)

    sems7 = pltpu.SemaphoreType.DMA((STEPS,))
    exs = [
        Exchange(sizes, 1, 7, fwd=(("lane4", 0, 1), ("plain", 6, 2)), up=small, down=small),
        Exchange(sizes, 1, 23, fwd=(("lane4", 1, 1), ("plain", 8, 2), ("plain", 20, 8))),
    ]
    kept = [
        (fp + (LANES,), F32), (sl + (c_lat,), F32), (sl + (5 * c_fast,), BF16), (sl + (c_lat,), BF16),
        (fp + (3 * LANES,), BF16), (sl + (in_slow,), F32), (sl + (c_slow,), F32), (fp + (LANES,), F32),
    ]
    ready = [((2, 32, LANES), F32), ((3, t_n, LANES), F32), ((3, f_n, LANES), F32), ((LANES, groups * c_fast), BF16),
             ((3 * LANES, LANES), BF16), ((3 * LANES, LANES), BF16), ((LANES, groups * c_fast), BF16)]
    ends = (STEPS, groups * 8, 2 * c_fast)
    fa, lat, taps, lact, ftap, sa, sp, fb, gb, m16, m64, wfa, wmid, wback, wout, c1, hp, hn, c2 = run_resident(
        functools.partial(k_front, exs), exs,
        [x_fast, wlat, x_slow, w_slow_in, w_shortcut],
        [fill, clip_offset, norms, w_fast_in.T, w_fast_mid, w_fast_out],
        kept, [*[(*k, True) for k in kept], *[(*k, False) for k in ready]],
        [pltpu.VMEM((groups * p_n * f_n, c_fast), F32), *acc(f_n, LANES, 2), *acc(t_n, c_lat, 2), *acc(t_n, in_slow, 2),
         *acc(t_n, c_slow, 2), *acc(f_n, LANES, 2), pltpu.SemaphoreType.DMA((8,)), sems7,
         pltpu.VMEM((pixels * t_n, c_fast), F32), pltpu.VMEM(ends, F32), pltpu.VMEM(ends, BF16), pltpu.VMEM(ends, BF16),
         pltpu.SemaphoreType.DMA((2,))],
        "front",
        scalars=2,
    )

    exs = [
        Exchange(sizes, 3, 13, fwd=(("row4", 2, 4), ("plain", 10, 2))),
        Exchange(sizes, 3, 25, fwd=(("plain", 12, 8),), bwd=(("row4", 0, 0, 2, 4, 0, 4),)),
    ]
    kept = [
        ((side + 2, side + 2, t_n, in_slow), BF16), ((pixels, t_n, in_slow), F32), (fp + (LANES,), BF16),
        ((pixels, t_n, in_slow), BF16), ((groups, inner, f_n, c_fast), BF16), (fp + (groups * c_fast,), F32),
    ]
    pad, sb, fact, sact, fast_y, df, c3, c4, q4 = run_resident(
        functools.partial(k_middle, exs), exs,
        [sa.reshape(side, side, t_n, in_slow), fb, wsp, w_slow_out, x_fast, cot_fast], [gb, c2, m16, m64, wout],
        kept, [(*k, True) for k in kept],
        [*acc(t_n, in_slow, 2), *acc(f_n, groups * c_fast, 2), *acc(t_n, c_slow, 2), *acc(f_n, groups * c_fast, 2),
         pltpu.SemaphoreType.DMA((4,)), sems7, sems7],
        "middle",
    )
    sb4, sact = sb.reshape(sl + (in_slow,)), sact.reshape(sl + (in_slow,))

    halo_pair = out_blocked((STEPS, 2, 8, LANES), F32, 0, 1)
    slow_y, dy, dfb, g_fout, up, down, st = call(
        k_out,
        [sb_(sact), sb_(sp), sb_(cot_slow), fb_(df), fb_(fact), fb_(fb), whole(c2), whole(c3), whole(c4), whole(q4),
         whole(m16), whole(m64), whole(w_slow_out), whole(wout)],
        [slow_out(c_slow, BF16), slow_out(c_slow, F32), fast_out(LANES, F32),
         out_whole((in_fast, c_fast), F32), halo_pair, halo_pair, stat(26)],
        [*acc(t_n, c_slow, 3), *acc(f_n, LANES, 2), *acc(LANES, groups * c_fast, 1)],
        "out",
    )
    pair = (STEPS, 2, 8, LANES)
    ex5 = Exchange(
        sizes, 6, 26,
        bwd=(("plain", 0, 0, 12, 8, 0, 8), ("plain", 1, 3, 20, 8, 0, 16), ("lane4", 1, 0, 1, 1, 24, 25)),
        up=pair, down=pair,
    )
    c_cat = w_slow_in.shape[0]
    width = in_slow
    stream_a = Stream(sizes, rows_for(sizes, c_cat * c_slow // width), width)
    stream_b = Stream(sizes, rows_for(sizes, 9 * in_slow), width)
    gw_short, gw_sout, dsp, dsb, dfa, g_fmid, q6, q5 = call(
        k_back_out,
        [sb_(x_slow), sb_(lact), sb_(dy), sb_(sp), sb_(sact), sb_(sb4), fb_(dfb), fb_(fb), fb_(fa), fb_(ftap), 1, 2,
         whole(c1), whole(c2), whole(c3), whole(c4), 0, whole(m16), whole(m64), whole(w_slow_out), whole(wback)],
        [out_whole((stream_a.rows_n, width), BF16), out_whole((c_slow, width), BF16), slow_out(c_slow, BF16),
         slow_out(in_slow, F32), fast_out(LANES, F32), out_whole((3 * in_fast, LANES), F32), STAT],
        [*acc(t_n, in_slow, 2), *acc(f_n, LANES, 2), *acc(c_cat, c_slow, 1), *acc(in_slow, c_slow, 1),
         *acc(LANES, 3 * LANES, 1)],
        "back_out",
        Exchange(sizes, 6, 6, bwd=(("plain", 0, 4, 10, 2, 0, 2), ("lane4", 1, 0, 0, 1, 4, 5))),
        [gb, c3, c1],
        ex5,
        [st, up, down, gb, c4, c2],
    )

    def rows2(a):
        return a.reshape(-1, a.shape[-1])

    dsa_low, dfa_low, lat_low, gw_fast, gw_in, gw_lat, q7, q8, hn, res_a, near_b = back_tail(
        stream_a, stream_b,
        Exchange(sizes, 7, 4, bwd=(("plain", 0, 1, 8, 2, 0, 2),)),
        Exchange(sizes, 7, 4, bwd=(("plain", 0, 1, 6, 2, 0, 2),), post=(STEPS, groups * 8, c_lat)),
        [gw_short, rows2(dsb), rows2(sb4), pad, wsp, rows2(sa), x_fast, dfa, fa, w_slow_in, w_shortcut, rows2(dsp), rows2(lat)],
        [rows2(x_slow), lact.reshape(pixels, t_n, c_lat), rows2(taps)],
        [gb, c1, c2, c3, q6, m16, m64, g_fout, g_fmid],
        side, t_n, in_slow,
    )
    heights = (gw_sout.shape[0], c_cat, 5 * c_fast, gw_fast.shape[0])
    sum_a, sum_bc, slow_gx, fast_gx = final_sum(
        sizes, 9, stream_a, stream_b,
        [dsa_low.reshape(sl + (in_slow,)), dsp, w_slow_in, w_shortcut, lat_low.reshape(sl + (c_lat,)), df, dfa_low],
        [res_a, near_b, gw_sout, gw_in, gw_lat, gw_fast, hn, m16, wlat, wfa],
        sl + (c_slow,), (groups, inner, f_n, c_fast), heights,
    )
    blocks = c_slow // in_slow
    pieces = [(0, n * c_cat, c_cat, 0, n * width) for n in range(blocks)]
    pieces.append((1, 0, 9 * in_slow, 2, None))
    at = 0
    for n in range(blocks):
        pieces.append((2, at, in_slow, 1, n * width))
        at += in_slow
    for out, tall in ((3, c_cat), (4, 5 * c_fast)):
        pieces.append((2, at, tall, out, None))
        at += tall
    norm_rows = -(-gains.shape[0] // LANES)
    g_short, g_sout, gw_mid, gw_in, gw_lat, gains_grad, biases_grad, g_fin, g_fmid, g_fout, *held = unpack(
        sum_a, sum_bc, stream_b.ch, tuple(pieces),
        [(c_cat, c_slow), (in_slow, c_slow), (9 * in_slow, width), (c_cat, in_slow), wlat.shape],
        [(norm_rows, LANES), (norm_rows, LANES), (in_fast, c_fast), w_fast_mid.shape, (in_fast, c_fast)],
        [q4, q5, q6, q7, q8],
        [slow_gx, fast_gx, fast_y],
    )
    slow_gx, fast_gx, fast_y = held
    grads = (
        g_fin.T,
        g_fmid,
        g_fout,
        gw_lat.reshape(w_lateral.shape),
        gw_in,
        gw_mid.reshape(w_slow_mid.shape),
        g_sout,
        g_short,
    )
    return (
        unview(slow_y),
        unview(fast_y),
        unview(slow_gx),
        unview(fast_gx),
        *grads,
        gains_grad.reshape(-1)[: gains.shape[0]],
        biases_grad.reshape(-1)[: biases.shape[0]],
    )


def solution(mesh):
    frames = P(("path", "frames"), None, None, None)
    in_specs = (frames, frames, P(AXES), P(AXES), *([P()] * 10), frames, frames)
    out_specs = (*([frames] * 4), *([P()] * 10))
    return jax.shard_map(per_device, mesh=mesh, in_specs=in_specs, out_specs=out_specs, check_vma=False)
```

```python
import functools

import jax
import jax.numpy as jnp
from jax import lax
from jax.experimental import pallas as pl
from jax.experimental.pallas import tpu as pltpu
from jax.sharding import PartitionSpec as P

norm_eps = 1e-05
F32 = jnp.float32
BF16 = jnp.bfloat16
MESH = pl.DeviceIdType.MESH
AXES = ("path", "frames")
STEPS = 7
LANES = 128
VMEM_LIMIT = 60 * 1024 * 1024


def dot(a, b):
    return jnp.dot(a, b, preferred_element_type=F32)


def dot_nt(a, b):
    return lax.dot_general(a, b, (((1,), (1,)), ((), ())), preferred_element_type=F32)


def dot_tn(a, b):
    return lax.dot_general(a, b, (((0,), (0,)), ((), ())), preferred_element_type=F32)


def sig(v):
    return 0.5 * jnp.tanh(0.5 * v) + 0.5


def slope(v):
    s = sig(v)
    return s + (v * s) * (1.0 - s)


def rows(ref, slab, first, count):
    parts = [ref[slab, first + j : first + j + 1, :] for j in range(count)]
    return parts[0] if count == 1 else jnp.concatenate(parts, axis=1)


def put_rows(ref, first, value):
    for j in range(value.shape[1] // LANES):
        ref[first + j : first + j + 1, :] = value[:, j * LANES : (j + 1) * LANES]


def zero_ref(ref):
    ref[...] = jnp.zeros(ref.shape, ref.dtype)


def spread_add(step, z, mean_ref, m2_ref, cols=slice(None)):
    count = z.shape[0]
    mean = jnp.sum(z, axis=0) * (1.0 / count)
    d = z - mean
    m2 = jnp.sum(d * d, axis=0)
    first = step == 0
    old_mean = jnp.where(first, 0.0, mean_ref[:, cols])
    old_m2 = jnp.where(first, 0.0, m2_ref[:, cols])
    done = jnp.full((1, z.shape[-1]), step, jnp.int32).astype(F32)
    share = 1.0 / (done + 1.0)
    delta = mean - old_mean
    mean_ref[:, cols] = old_mean + delta * share
    m2_ref[:, cols] = old_m2 + m2 + delta * delta * (done * share * count)


def spread_end(mean_ref, m2_ref, fill, positions):
    filled = jnp.sum(fill, axis=0, keepdims=True)
    mean = jnp.sum(fill * mean_ref[...], axis=0, keepdims=True) / jnp.maximum(filled, 1.0)
    d = mean_ref[...] - mean
    m2 = jnp.sum(fill * (m2_ref[...] + positions * (d * d)), axis=0, keepdims=True)
    return mean, m2


def sum_add(step, value, ref, cols=slice(None)):
    ref[:, cols] = jnp.where(step == 0, 0.0, ref[:, cols]) + jnp.sum(value, axis=0)


def sum_end(ref):
    return jnp.sum(ref[...], axis=0, keepdims=True)


def pad8(n):
    return -(-n // 8) * 8


def exchange_peers(cfg):
    paths, length = lax.axis_size("path"), lax.axis_size("frames")
    near = 4
    g1, g2 = paths * near, length // near
    me_p, me_f = lax.axis_index("path"), lax.axis_index("frames")
    me = me_p * length + me_f
    total = paths * length
    r1 = me_p * near + lax.rem(me_f, near)
    r2 = lax.div(me_f, near)

    def peer1(k):
        r = lax.rem(r1 + k, g1)
        return (lax.div(r, near), r2 * near + lax.rem(r, near))

    def peer2(k):
        r = lax.rem(r2 + k, g2)
        return (me_p, r * near + lax.rem(me_f, near))

    def split(index):
        return (lax.div(index, length), lax.rem(index, length))

    nxt, prv = split(lax.rem(me + 1, total)), split(lax.rem(me + total - 1, total))
    return g1, g2, r1, r2, peer1, peer2, nxt, prv


def exchange_hello(cfg):
    g1, g2, _, _, peer1, peer2, nxt, prv = exchange_peers(cfg)
    peers = [peer1(k) for k in range(1, g1)] + [peer2(k) for k in range(1, g2)]
    if cfg.greets:
        peers += [nxt, prv]
    for peer in peers:
        pl.semaphore_signal(pltpu.get_barrier_semaphore(), inc=1, device_id=peer, device_id_type=MESH)
    return len(peers)


def exchange_run(cfg, ins, outs, scratch, meanwhile=None, post=None, after=None, between=None):
    fwd, bwd = cfg.fwd, cfg.bwd
    nf = sum(c[2] for c in fwd)
    nb = max((c[6] + c[4] for c in bwd), default=0)
    n_row = 2 * nf + nb
    stats_ref, up_ref, down_ref = scratch[:3]
    gb_ref, *coef_refs = ins
    outs = list(outs)
    coef_out = outs.pop(0) if nf else None
    pq_out = outs.pop(0) if nb else None
    from_prev = outs.pop(0) if cfg.up else None
    from_next = outs.pop(0) if cfg.down else None
    slots1, slots2, mid, tot, send1, recv1, send2, recv2, up_land, up_sems, down_land, down_sems = scratch[3:15]
    g1, g2, r1, r2, peer1, peer2, nxt, prv = exchange_peers(cfg)

    halos = []
    copies = []
    for k in range(1, g1):
        copies.append(
            pltpu.make_async_remote_copy(
                src_ref=stats_ref,
                dst_ref=slots1.at[r1],
                send_sem=send1.at[k],
                recv_sem=recv1.at[k],
                device_id=peer1(k),
                device_id_type=MESH,
            )
        )
        copies[-1].start()
    for used, src, land, sems, peer in (
        (cfg.up, up_ref, up_land, up_sems, nxt),
        (cfg.down, down_ref, down_land, down_sems, prv),
    ):
        if used:
            halos.append(
                pltpu.make_async_remote_copy(
                    src_ref=src,
                    dst_ref=land,
                    send_sem=sems.at[0],
                    recv_sem=sems.at[1],
                    device_id=peer,
                    device_id_type=MESH,
                )
            )
            halos[-1].start()
    slots1[r1] = stats_ref[...]
    if meanwhile is not None:
        meanwhile()
    for c in copies:
        c.wait_recv()

    def combine(slots, count, out):
        if nf:
            n = slots[0, n_row : n_row + 1, :]
            for g in range(1, count):
                n = n + slots[g, n_row : n_row + 1, :]
            acc = slots[0, n_row : n_row + 1, :] * slots[0, 0:nf, :]
            for g in range(1, count):
                acc = acc + slots[g, n_row : n_row + 1, :] * slots[g, 0:nf, :]
            mean = acc / jnp.maximum(n, 1.0)
            m2 = None
            for g in range(count):
                d = slots[g, 0:nf, :] - mean
                part = slots[g, nf : 2 * nf, :] + slots[g, n_row : n_row + 1, :] * (d * d)
                m2 = part if m2 is None else m2 + part
            out[0:nf, :] = mean
            out[nf : 2 * nf, :] = m2
            out[n_row : n_row + 1, :] = n
        if nb:
            acc = slots[0, 2 * nf : n_row, :]
            for g in range(1, count):
                acc = acc + slots[g, 2 * nf : n_row, :]
            out[2 * nf : n_row, :] = acc

    zero_ref(mid)
    combine(slots1, g1, mid)
    copies2 = []
    for k in range(1, g2):
        copies2.append(
            pltpu.make_async_remote_copy(
                src_ref=mid,
                dst_ref=slots2.at[r2],
                send_sem=send2.at[k],
                recv_sem=recv2.at[k],
                device_id=peer2(k),
                device_id_type=MESH,
            )
        )
        copies2[-1].start()
    slots2[r2] = mid[...]
    if between is not None:
        between()
    for c in copies2:
        c.wait_recv()
    combine(slots2, g2, tot)

    def lanes4(v):
        w = v + pltpu.roll(v, 64, 1)
        return w + pltpu.roll(w, 32, 1)

    at = 0
    for kind, g_row, count in fwd:
        n = tot[n_row : n_row + 1, :]
        mean = tot[at : at + count, :]
        m2 = tot[nf + at : nf + at + count, :]
        if kind == "lane4":
            whole = lanes4(mean) * 0.25
            d = mean - whole
            var = lanes4(m2 + n * (d * d)) / (4.0 * n)
            mean = whole
        elif kind == "row4":
            whole = jnp.sum(mean, axis=0, keepdims=True) * 0.25
            d = mean - whole
            var = jnp.sum(m2 + n * (d * d), axis=0, keepdims=True) / (4.0 * n)
            var = jnp.broadcast_to(var, (count, LANES))
            mean = jnp.broadcast_to(whole, (count, LANES))
        else:
            var = m2 / n
        inv = lax.rsqrt(var + norm_eps)
        scale = inv * gb_ref[0, g_row : g_row + count, :]
        coef_out[0, at : at + count, :] = scale
        coef_out[1, at : at + count, :] = gb_ref[1, g_row : g_row + count, :] - mean * scale
        coef_out[2, at : at + count, :] = inv
        coef_out[3, at : at + count, :] = mean * inv
        coef_out[4, at : at + count, :] = jnp.broadcast_to(n, (count, LANES))
        at += count
    at = 0
    for kind, coef, row, _, count, db_at, dg_at in bwd:
        db = tot[2 * nf + db_at : 2 * nf + db_at + count, :]
        dg = tot[2 * nf + dg_at : 2 * nf + dg_at + count, :]
        c = coef_refs[coef]
        scale, inv = c[0, row : row + count, :], c[2, row : row + count, :]
        mi, n = c[3, row : row + count, :], c[4, row : row + count, :]
        if kind == "lane4":
            db, dg, n = lanes4(db), lanes4(dg), 4.0 * n
        elif kind == "row4":
            db = jnp.broadcast_to(jnp.sum(db, axis=0, keepdims=True), (count, LANES))
            dg = jnp.broadcast_to(jnp.sum(dg, axis=0, keepdims=True), (count, LANES))
            n = 4.0 * n
        pq_out[0, at : at + count, :] = scale / n * (db - mi * dg)
        pq_out[1, at : at + count, :] = scale / n * inv * dg
        pq_out[2, at : at + count, :] = db
        pq_out[3, at : at + count, :] = dg
        at += count

    if cfg.post:
        post_sent, post_land, post_sems = scratch[15:]
        post(pq_out, post_sent)
        late = pltpu.make_async_remote_copy(
            src_ref=post_sent,
            dst_ref=post_land,
            send_sem=post_sems.at[0],
            recv_sem=post_sems.at[1],
            device_id=prv,
            device_id_type=MESH,
        )
        late.start()
        if after is not None:
            after()
        late.wait()
        outs.pop(0)[...] = post_land[...]
    for c in halos:
        c.wait()
    if cfg.up:
        from_prev[...] = up_land[...]
    if cfg.down:
        from_next[...] = down_land[...]
    for c in copies:
        c.wait_send()
    for c in copies2:
        c.wait_send()


class Exchange:
    def __init__(self, sizes, cid, rows_n, fwd=(), bwd=(), up=None, down=None, post=None):
        self.cid, self.fwd, self.bwd, self.up, self.down, self.post = cid, fwd, bwd, up, down, post
        self.greets = bool(up or down or post)
        g1, g2, r = sizes[0] * 4, sizes[1] // 4, pad8(rows_n)
        self.outs = []
        nf, nn = sum(c[2] for c in fwd), sum(c[4] for c in bwd)
        if nf:
            self.outs.append(((5, nf, LANES), F32))
        if nn:
            self.outs.append(((4, nn, LANES), F32))
        self.outs += [(h, F32) for h in (up, down) if h]
        if post:
            self.outs.append((post, BF16))
        none = (8, LANES)
        self.stats = (r, LANES)
        self.work = [
            pltpu.VMEM((g1, r, LANES), F32),
            pltpu.VMEM((g2, r, LANES), F32),
            pltpu.VMEM((r, LANES), F32),
            pltpu.VMEM((r, LANES), F32),
            pltpu.SemaphoreType.DMA((g1,)),
            pltpu.SemaphoreType.DMA((g1,)),
            pltpu.SemaphoreType.DMA((g2,)),
            pltpu.SemaphoreType.DMA((g2,)),
            pltpu.VMEM(up or none, F32),
            pltpu.SemaphoreType.DMA((2,)),
            pltpu.VMEM(down or none, F32),
            pltpu.SemaphoreType.DMA((2,)),
        ]
        if post:
            self.work += [pltpu.VMEM(post, BF16), pltpu.VMEM(post, BF16), pltpu.SemaphoreType.DMA((2,))]
        self.local = [pltpu.VMEM(self.stats, F32), pltpu.VMEM(up or none, F32), pltpu.VMEM(down or none, F32)]


STAT, UP, DOWN = "stat", "up", "down"


def call(kernel, ins, outs, scratch=(), name=None, ex=None, ex_ins=(), pre=None, pre_ins=()):
    real = [o for o in outs if not isinstance(o, str)]
    given = ins
    ins = [a for a in given if not isinstance(a, int)]
    extra_in = [whole(a) for a in (*ex_ins, *pre_ins)]
    extra_out = [out_whole(s, d) for s, d in ex.outs] if ex else []
    local = [*ex.local, *ex.work] if ex else []
    n_local = len(local)
    if pre:
        extra_out.append(out_whole(*pre.outs[0]))
        local += [*pre.work, *[pltpu.VMEM(shape, d) for shape, d in pre.outs[1:]]]
    all_in, all_out = [*ins, *extra_in], [*real, *extra_out]
    sizes = [len(ins), len(extra_in), len(real), len(extra_out), len(scratch), len(local)]
    ends = [sum(sizes[: k + 1]) for k in range(len(sizes))]

    def body(*refs):
        k_in, x_in, k_out, x_out, k_scr, x_scr = (refs[e - n : e] for e, n in zip(ends, sizes))
        if ex is None:
            kernel(*k_in, *k_out, *k_scr)
            return
        i = pl.program_id(0)

        p_ins, p_outs, p_scr = x_in[len(ex_ins) :], [], x_scr[n_local:]
        x_in, x_scr = x_in[: len(ex_ins)], x_scr[:n_local]
        if pre:
            n = len(pre.work)
            p_outs = [x_out[-1], *p_scr[n:]]
            x_out = x_out[:-1]

        @pl.when(i == 0)
        def _():
            exchange_hello(pre or ex)
            if pre:
                pl.semaphore_wait(pltpu.get_barrier_semaphore(), len_peers(pre))
                exchange_run(pre, p_ins[3:], p_outs, [*p_ins[:3], *p_scr[:n]])

        if pre:
            it_in = iter(k_in)
            views = [p_outs[0], *[o.at[pl.ds(i, 1)] for o in p_outs[1:]]]
            k_in = [views[a] if isinstance(a, int) else next(it_in) for a in given]
        named = {STAT: x_scr[0]}
        if ex.up:
            named[UP] = x_scr[1].at[pl.ds(i, 1)]
        if ex.down:
            named[DOWN] = x_scr[2].at[pl.ds(i, 1)]
        it = iter(k_out)
        late = kernel(*k_in, *[named[o] if isinstance(o, str) else next(it) for o in outs], *k_scr)

        @pl.when(i == STEPS - 1)
        def _():
            if not pre:
                pl.semaphore_wait(pltpu.get_barrier_semaphore(), len_peers(ex))
            exchange_run(ex, x_in, x_out, x_scr, late)

    params = {"collective_id": ex.cid, "has_side_effects": True} if ex else {}
    return pl.pallas_call(
        body,
        grid=(STEPS,),
        in_specs=[pl.BlockSpec(b, m) for _, b, m in all_in],
        out_specs=[pl.BlockSpec(b, m) for _, _, b, m in all_out],
        out_shape=[jax.ShapeDtypeStruct(s, d) for s, d, _, _ in all_out],
        scratch_shapes=[*scratch, *local],
        compiler_params=pltpu.CompilerParams(
            dimension_semantics=("arbitrary",), vmem_limit_bytes=VMEM_LIMIT, **params
        ),
        name=name,
    )(*[a for a, _, _ in all_in])


def len_peers(ex):
    paths, length = lax.axis_size("path"), lax.axis_size("frames")
    return paths * 4 - 1 + length // 4 - 1 + (2 if ex.greets else 0)


def whole(array):
    zeros = (0,) * array.ndim
    return (array, array.shape, lambda i: zeros)


def blocked(array, axis, size):
    block = array.shape[:axis] + (size,) + array.shape[axis + 1 :]
    return (array, block, lambda i: tuple(i if d == axis else 0 for d in range(array.ndim)))


def out_whole(shape, dtype):
    zeros = (0,) * len(shape)
    return (shape, dtype, shape, lambda i: zeros)


def out_blocked(shape, dtype, axis, size):
    block = shape[:axis] + (size,) + shape[axis + 1 :]
    return (shape, dtype, block, lambda i: tuple(i if d == axis else 0 for d in range(len(shape))))


def flat(value):
    return value.reshape(-1, value.shape[-1])


def spread_rows(ref, index, count, height):
    return [jnp.broadcast_to(ref[(*index, slice(p, p + 1))], (height, ref.shape[-1])) for p in range(count)]


def k_first(i, x_ref, tail_ref, m16_ref, m64_ref, wfa_ref, wlat_ref,
            fa_ref, lat_ref, taps_ref, st_ref, up_ref, down_ref, xs, fm, fv, lm, lv):
    x = x_ref[...]
    s_n, p_n, f_n, _ = x.shape
    packed = jnp.concatenate([flat(x[s]) for s in range(s_n)], axis=1)
    fa = dot_nt(packed, wfa_ref[...])
    fa_ref[...] = fa.reshape(fa_ref.shape)
    zero_ref(up_ref)
    zero_ref(down_ref)
    for p in range(p_n):
        down_ref[0, p : p + 1, :] = fa[p * f_n : p * f_n + 1, :]
        up_ref[0, p : p + 1, :] = fa[p * f_n + f_n - 1 : p * f_n + f_n, :]
    spread_add(i, fa.reshape(p_n, f_n, LANES), fm, fv)

    xs[...] = flat(x).astype(F32)
    n = xs.shape[0] // 4
    quarter = [xs[pl.ds(k, n, stride=4), :] for k in range(4)]
    t_n = f_n // 4
    first = lax.broadcasted_iota(jnp.int32, (n // t_n, t_n, LANES), 1) == 0
    link = m16_ref[1:2]
    tail = tail_ref[0].astype(F32)
    taps = []
    for k in range(2):
        halo = jnp.concatenate(
            [
                jnp.broadcast_to(tail[s * 8 + p : s * 8 + p + 1, k * LANES : (k + 1) * LANES], (t_n, LANES))
                for s in range(s_n)
                for p in range(p_n)
            ],
            axis=0,
        )
        moved = pltpu.roll(quarter[2 + k], 1, 0).reshape(n // t_n, t_n, LANES)
        taps.append(flat(jnp.where(first, halo.reshape(moved.shape), moved) * link))
    taps = jnp.concatenate([*taps, *quarter[:3]], axis=1).astype(BF16)
    taps_ref[...] = taps.reshape(taps_ref.shape)
    lat = dot(taps, wlat_ref[...])
    lat_ref[...] = lat.reshape(lat_ref.shape)
    spread_add(i, lat.reshape(n // t_n, t_n, lat.shape[1]), lm, lv)

    @pl.when(i == STEPS - 1)
    def _():
        zero_ref(st_ref)
        fill = m16_ref[0, :, 0:1]
        mean, m2 = spread_end(fm, fv, m64_ref[0, :, 0:1], STEPS * p_n)
        put_rows(st_ref, 0, mean)
        put_rows(st_ref, 3, m2)
        mean, m2 = spread_end(lm, lv, fill, STEPS * p_n * s_n)
        put_rows(st_ref, 1, mean)
        put_rows(st_ref, 4, m2)
        put_rows(st_ref, 6, count_row(m16_ref, STEPS * p_n * s_n))


def count_row(m16_ref, positions):
    return jnp.sum(m16_ref[0], axis=0, keepdims=True) * float(positions)


def shifted(value, first_rows, last_rows, f_n):
    n = value.shape[0]
    shape = (n // f_n, f_n, value.shape[1])
    place = lax.broadcasted_iota(jnp.int32, shape, 1)
    before = jnp.where(place == 0, first_rows, pltpu.roll(value, 1, 0).reshape(shape))
    after = jnp.where(place == f_n - 1, last_rows, pltpu.roll(value, n - 1, 0).reshape(shape))
    return before, after


def k_join(i, x_ref, lat_ref, fa_ref, hp_ref, hn_ref, c1_ref, m16_ref, m64_ref, win_ref, wsc_ref, wmid_ref,
           lact_ref, ftap_ref, sa_ref, sp_ref, fb_ref, st_ref, am, av, pm, pv, bm, bv, begun=False):
    s_n, p_n, t_n, c_slow = x_ref.shape
    c_lat = lat_ref.shape[-1]
    v = flat(lat_ref[...]) * rows(c1_ref, 0, 1, 2) + rows(c1_ref, 1, 1, 2)
    lact = (v * sig(v)).astype(BF16)
    lact_ref[...] = lact.reshape(lact_ref.shape)
    joined = None if begun else jnp.concatenate([flat(x_ref[...]), lact], axis=1)
    wide = c_lat
    for n in range(1 + wsc_ref.shape[1] // wide):
        cols = slice((n - 1) * wide, n * wide)
        if begun:
            z = flat(sa_ref[...] if n == 0 else sp_ref[:, :, :, cols])
            z = z + dot(lact, win_ref[c_slow:, :] if n == 0 else wsc_ref[c_slow:, cols])
        else:
            z = dot(joined, win_ref[...] if n == 0 else wsc_ref[:, cols])
        z4 = z.reshape(s_n, p_n, t_n, wide)
        z3 = z.reshape(s_n * p_n, t_n, wide)
        if n == 0:
            sa_ref[...] = z4
            spread_add(i, z3, am, av)
        else:
            sp_ref[:, :, :, cols] = z4
            spread_add(i, z3, pm, pv, cols)

    f_n = fa_ref.shape[1]
    scale, shift = rows(c1_ref, 0, 0, 1), rows(c1_ref, 1, 0, 1)

    def act(z):
        w = z * scale + shift
        return (w * sig(w)).astype(BF16).astype(F32)

    fact = act(flat(fa_ref[...]))
    ends = []
    for ref in (hp_ref, hn_ref):
        small = act(ref[0])
        ends.append(
            jnp.concatenate(
                [jnp.broadcast_to(small[p : p + 1, :], (f_n, LANES)) for p in range(p_n)], axis=0
            ).reshape(p_n, f_n, LANES)
        )
    before, after = shifted(fact, ends[0], ends[1], f_n)
    ftap = jnp.concatenate(
        [flat(before * m64_ref[1:2]), fact, flat(after * m64_ref[2:3])], axis=1
    ).astype(BF16)
    ftap_ref[...] = ftap.reshape(ftap_ref.shape)
    fb = dot(ftap, wmid_ref[...])
    fb_ref[...] = fb.reshape(fb_ref.shape)
    spread_add(i, fb.reshape(p_n, f_n, LANES), bm, bv)

    @pl.when(i == STEPS - 1)
    def _():
        zero_ref(st_ref)
        fill = m16_ref[0, :, 0:1]
        positions = STEPS * p_n * s_n
        mean, m2 = spread_end(bm, bv, m64_ref[0, :, 0:1], STEPS * p_n)
        put_rows(st_ref, 0, mean)
        put_rows(st_ref, 11, m2)
        mean, m2 = spread_end(am, av, fill, positions)
        put_rows(st_ref, 1, mean)
        put_rows(st_ref, 12, m2)
        mean, m2 = spread_end(pm, pv, fill, positions)
        put_rows(st_ref, 3, mean)
        put_rows(st_ref, 14, m2)
        put_rows(st_ref, 22, count_row(m16_ref, positions))


def k_spatial(i, sa_ref, fb_ref, c2_ref, m16_ref, m64_ref, wsp_ref, wout_ref,
              pad_ref, sb_ref, fact_ref, st_ref, sm, sv, cm, cv):
    h_n, w_n, t_n, c = sa_ref.shape

    @pl.when(i == 0)
    def _():
        scale, shift = rows(c2_ref, 0, 1, 2), rows(c2_ref, 1, 1, 2)
        zero_ref(pad_ref)

        @pl.loop(0, h_n)
        def _(h):
            v = flat(sa_ref[h]) * scale + shift
            pad_ref[h + 1, 1 : w_n + 1] = (v * sig(v)).astype(BF16).reshape(w_n, t_n, c)

    per = h_n // STEPS
    h0 = i * per
    patches = [flat(pad_ref[pl.ds(h0 + a, per), b : b + w_n]) for a in range(3) for b in range(3)]
    acc = dot(jnp.concatenate(patches, axis=1), wsp_ref[...])
    sb_ref[...] = acc.reshape(sb_ref.shape)
    spread_add(i, acc.reshape(per * w_n, t_n, acc.shape[1]), sm, sv)

    p_n, f_n, _ = fb_ref.shape
    v = flat(fb_ref[...]) * rows(c2_ref, 0, 0, 1) + rows(c2_ref, 1, 0, 1)
    fact = (v * sig(v)).astype(BF16)
    fact_ref[...] = fact.reshape(fact_ref.shape)
    fc = dot(fact, wout_ref[...])
    spread_add(i, fc.reshape(p_n, f_n, fc.shape[1]), cm, cv)

    @pl.when(i == STEPS - 1)
    def _():
        zero_ref(st_ref)
        mean, m2 = spread_end(cm, cv, m64_ref[0, :, 0:1], STEPS * p_n)
        put_rows(st_ref, 0, mean)
        put_rows(st_ref, 6, m2)
        mean, m2 = spread_end(sm, sv, m16_ref[0, :, 0:1], h_n * w_n)
        put_rows(st_ref, 4, mean)
        put_rows(st_ref, 10, m2)
        put_rows(st_ref, 12, count_row(m16_ref, h_n * w_n))


def k_expand(i, sb_ref, fact_ref, x_ref, cot_ref, c3_ref, m16_ref, m64_ref, wso_ref, wout_ref,
             sact_ref, fout_ref, df_ref, st_ref, cm, cv, s1, s2):
    s_n, p_n, t_n = x_ref.shape[0], fact_ref.shape[0], sb_ref.shape[-2]
    v = flat(sb_ref[...]) * rows(c3_ref, 0, 4, 2) + rows(c3_ref, 1, 4, 2)
    sact = (v * sig(v)).astype(BF16)
    sact_ref[...] = sact.reshape(sact_ref.shape)
    wide = 256
    for n in range(wso_ref.shape[1] // wide):
        cols = slice(n * wide, (n + 1) * wide)
        z = dot(sact, wso_ref[:, cols])
        spread_add(i, z.reshape(s_n * p_n, t_n, wide), cm, cv, cols)

    f_n = fact_ref.shape[1]
    fc = dot(flat(fact_ref[...]), wout_ref[...])
    fill = m64_ref[0:1]
    for s in range(s_n):
        cols = slice(s * LANES, (s + 1) * LANES)
        z = fc[:, cols].reshape(p_n, f_n, LANES)
        unit = z * rows(c3_ref, 2, s, 1) - rows(c3_ref, 3, s, 1)
        pre = z * rows(c3_ref, 0, s, 1) + rows(c3_ref, 1, s, 1) + x_ref[s].astype(F32)
        g = sig(pre)
        y = pre * g
        fout_ref[s] = (y * fill).astype(BF16)
        d = cot_ref[s].astype(F32) * fill * (g + y * (1.0 - g))
        df_ref[:, :, cols] = d
        sum_add(i, d, s1, cols)
        sum_add(i, d * unit, s2, cols)

    @pl.when(i == STEPS - 1)
    def _():
        zero_ref(st_ref)
        positions = STEPS * p_n * s_n
        mean, m2 = spread_end(cm, cv, m16_ref[0, :, 0:1], positions)
        put_rows(st_ref, 0, mean)
        put_rows(st_ref, 8, m2)
        put_rows(st_ref, 16, sum_end(s1))
        put_rows(st_ref, 20, sum_end(s2))
        put_rows(st_ref, 24, count_row(m16_ref, positions))


def run_resident(kernel, ex_list, hbm, small, locals_, outs, scratch, name, scalars=0):
    vm, anywhere = pl.BlockSpec(memory_space=pltpu.VMEM), pl.BlockSpec(memory_space=pl.ANY)
    for ex in ex_list:
        outs = [*outs, *[(shape, dtype, False) for shape, dtype in ex.outs]]
    work = [w for ex in ex_list for w in (*ex.local, *ex.work)]
    sizes = [len(hbm), len(small), len(outs), len(hbm), len(locals_), len(scratch), 1]
    ends = [sum(sizes[: k + 1]) for k in range(len(sizes))]

    def body(*refs):
        h, sm, o, loaded, kept, scr, (sems,) = (refs[e - n : e] for e, n in zip(ends, sizes))
        rest, at = [], ends[-1]
        for ex in ex_list:
            n = len(ex.local) + len(ex.work)
            rest.append(refs[at : at + n])
            at += n
        loads = [pltpu.make_async_copy(a, b, sems.at[k]) for k, (a, b) in enumerate(zip(h, loaded))]
        greeter = max(ex_list, key=lambda ex: ex.greets)
        count = exchange_hello(greeter)
        for load in loads:
            load.start()
        kernel(loads, lambda: pl.semaphore_wait(pltpu.get_barrier_semaphore(), count), loaded, sm, kept, scr, o, rest)

    return pl.pallas_call(
        body,
        out_shape=[jax.ShapeDtypeStruct(shape, dtype) for shape, dtype, _ in outs],
        in_specs=[anywhere] * len(hbm) + [pl.BlockSpec(memory_space=pltpu.SMEM)] * scalars + [vm] * (len(small) - scalars),
        out_specs=[anywhere if stays else vm for _, _, stays in outs],
        scratch_shapes=[
            *[pltpu.VMEM(a.shape, a.dtype) for a in hbm], *[pltpu.VMEM(*k) for k in locals_], *scratch,
            pltpu.SemaphoreType.DMA((len(hbm),)), *work,
        ],
        compiler_params=pltpu.CompilerParams(
            collective_id=ex_list[0].cid, has_side_effects=True, vmem_limit_bytes=VMEM_LIMIT
        ),
        name=name,
    )(*hbm, *small)


def stores_of(pairs, sems):
    return [pltpu.make_async_copy(a, b, sems.at[k]) for k, (a, b) in enumerate(pairs)]


def k_front(exs, loads, met, loaded, small, kept, scratch, outs, work):
    x_fast, wlat, x_slow, w_in, w_sc = loaded
    fa, lat, taps, lact, ftap, sa, sp, fb = kept
    xs, fm, fv, lm, lv, am, av, pm, pv, bm, bv, sems, sp_sems, ends_f, sent, sent_low, tail_ref, tail_sems = scratch
    big, ready, (c1, hp, hn, c2) = outs[:8], outs[8:15], outs[15:]
    gb, m16, m64, wfa, wmid, wback, wout = ready
    p_n = fa.shape[0] // STEPS
    copies = dict(zip((0, 1, 2, 3, 4, 5, 7), stores_of([p for k, p in enumerate(zip(kept, big)) if k != 6], sems)))
    st1, up, down = work[0][:3]
    loads[0].wait()
    s_n, inner, f_n, ch = x_fast.shape
    t_n = lat.shape[2]
    ends_f[...] = flat(x_fast[:, :, f_n - t_n : f_n, :]).astype(F32)
    zero_ref(sent)
    for k in range(2):
        lines = ends_f[pl.ds(t_n - 2 + k, s_n * inner, stride=t_n), :]
        for s in range(s_n):
            for step in range(STEPS):
                at = s * inner + step * p_n
                sent[step, s * 8 : s * 8 + p_n, k * ch : (k + 1) * ch] = lines[at : at + p_n, :]
    sent_low[...] = sent[...].astype(BF16)
    met()
    nxt = exchange_peers(exs[0])[6]
    halo = pltpu.make_async_remote_copy(
        src_ref=sent_low, dst_ref=tail_ref, send_sem=tail_sems.at[0], recv_sem=tail_sems.at[1],
        device_id=nxt, device_id_type=MESH,
    )
    halo.start()
    small_set_up(*small, *ready, s_n, t_n)
    loads[1].wait()
    halo.wait()

    def first(i):
        part, one = pl.ds(i * p_n, p_n), pl.ds(i, 1)
        k_first(i, x_fast.at[:, part], tail_ref.at[one], m16, m64, wfa, wlat, fa.at[part], lat.at[:, part],
                taps.at[:, part], st1, up.at[one], down.at[one], xs, fm, fv, lm, lv)

    each(0, STEPS, first)
    for k in (0, 1, 2):
        copies[k].start()
    c_slow = x_slow.shape[-1]

    def begin(i):
        part = pl.ds(i * p_n, p_n)
        xs_part = flat(x_slow[:, part])
        wide = sa.shape[-1]
        sa[:, part] = dot(xs_part, w_in[0:c_slow, :]).reshape(s_n, p_n, t_n, wide)
        for n in range(sp.shape[-1] // wide):
            cols = slice(n * wide, (n + 1) * wide)
            sp[:, part, :, cols] = dot(xs_part, w_sc[0:c_slow, cols]).reshape(s_n, p_n, t_n, wide)

    def begin_some():
        for k in (2, 3, 4):
            loads[k].wait()
        each(0, 2, begin)

    exchange_run(exs[0], [gb], [c1, hp, hn], work[0], begin_some, between=lambda: each(2, 4, begin))

    def store_sp(i):
        part = pl.ds(i * p_n, p_n)
        return pltpu.make_async_copy(sp.at[:, part], big[6].at[:, part], sp_sems.at[i])

    def join(i, begun=False):
        part, one = pl.ds(i * p_n, p_n), pl.ds(i, 1)
        k_join(i, x_slow.at[:, part], lat.at[:, part], fa.at[part], hp.at[one], hn.at[one], c1, m16, m64, w_in, w_sc, wmid,
               lact.at[:, part], ftap.at[part], sa.at[:, part], sp.at[:, part], fb.at[part], work[1][0],
               am, av, pm, pv, bm, bv, begun)
        store_sp(i).start()

    each(0, 4, lambda i: join(i, True))
    each(4, STEPS, join)
    for k in (3, 4, 5, 7):
        copies[k].start()
    exchange_run(exs[1], [gb], [c2], work[1])
    each(0, STEPS, lambda i: store_sp(i).wait())
    for k in (0, 1, 2, 3, 4, 5, 7):
        copies[k].wait()


def k_middle(exs, loads, met, loaded, small, kept, scratch, outs, work):
    sa, fb, wsp, wso, x_fast, cot = loaded
    gb, c2, m16, m64, wout = small
    pad, sb, fact, sact, fast_y, df = kept
    sm, sv, cm, cv, em, ev, s1, s2, sems, y_sems, df_sems = scratch
    big, (c3, c4, q4) = outs[:6], outs[6:]
    p_n = fb.shape[0] // STEPS
    rows_n = sb.shape[0] // STEPS
    copies = stores_of(list(zip(kept, big))[:4], sems)
    for k in (0, 1, 2):
        loads[k].wait()

    def spatial(i):
        part, span = pl.ds(i * p_n, p_n), pl.ds(i * rows_n, rows_n)
        k_spatial(i, sa, fb.at[part], c2, m16, m64, wsp, wout, pad, sb.at[span], fact.at[part], work[0][0], sm, sv, cm, cv)

    each(0, STEPS, spatial)
    met()
    for k in (0, 1, 2):
        copies[k].start()
    exchange_run(exs[0], [gb], [c3], work[0])
    for k in (3, 4, 5):
        loads[k].wait()

    def y_store(i):
        part = pl.ds(i * p_n, p_n)
        return pltpu.make_async_copy(fast_y.at[:, part], big[4].at[:, part], y_sems.at[i])

    def df_store(i):
        part = pl.ds(i * p_n, p_n)
        return pltpu.make_async_copy(df.at[part], big[5].at[part], df_sems.at[i])

    def expand(i):
        part, span = pl.ds(i * p_n, p_n), pl.ds(i * rows_n, rows_n)
        k_expand(i, sb.at[span], fact.at[part], x_fast.at[:, part], cot.at[:, part], c3, m16, m64, wso, wout,
                 sact.at[span], fast_y.at[:, part], df.at[part], work[1][0], em, ev, s1, s2)
        y_store(i).start()
        df_store(i).start()

    each(0, STEPS, expand)
    copies[3].start()
    exchange_run(exs[1], [gb, c3], [c4, q4], work[1])
    each(0, STEPS, lambda i: y_store(i).wait())
    each(0, STEPS, lambda i: df_store(i).wait())
    for copy in copies:
        copy.wait()


def back_norm(scale, p, q, dy, z, fill):
    return scale * dy - fill * (p + z * q)


def k_out(sact_ref, sp_ref, cot_ref, df_ref, fact_ref, fb_ref, c2_ref, c3_ref, c4_ref, q4_ref,
          m16_ref, m64_ref, wso_ref, wout_ref,
          out_ref, dy_ref, dfb_ref, gout_ref, up_ref, down_ref, st_ref, s1, s2, s3, t1, t2, gout):
    i = pl.program_id(0)
    s_n, p_n, t_n, _ = sact_ref.shape
    sact = flat(sact_ref[...])
    fill = m16_ref[0:1, :, 0:1]
    wide = 256
    for n in range(wso_ref.shape[1] // wide):
        cols = slice(n * wide, (n + 1) * wide)
        shape = (s_n * p_n, t_n, wide)
        sc = dot(sact, wso_ref[:, cols]).reshape(shape)
        sp = sp_ref[:, :, :, cols].reshape(shape)
        u6 = sc * rows(c4_ref, 2, 2 * n, 2) - rows(c4_ref, 3, 2 * n, 2)
        u7 = sp * rows(c2_ref, 2, 3 + 2 * n, 2) - rows(c2_ref, 3, 3 + 2 * n, 2)
        pre = (
            sc * rows(c4_ref, 0, 2 * n, 2)
            + sp * rows(c2_ref, 0, 3 + 2 * n, 2)
            + (rows(c4_ref, 1, 2 * n, 2) + rows(c2_ref, 1, 3 + 2 * n, 2))
        )
        g = sig(pre)
        y = pre * g
        out_ref[:, :, :, cols] = (y * fill).astype(BF16).reshape(s_n, p_n, t_n, wide)
        d = cot_ref[:, :, :, cols].reshape(shape).astype(F32) * fill * (g + y * (1.0 - g))
        dy_ref[:, :, :, cols] = d.reshape(s_n, p_n, t_n, wide)
        sum_add(i, d, s1, cols)
        sum_add(i, d * u6, s2, cols)
        sum_add(i, d * u7, s3, cols)

    f_n = fact_ref.shape[1]
    fact = flat(fact_ref[...])
    fc = dot(fact, wout_ref[...])
    fill4 = m64_ref[0:1]
    parts = []
    for s in range(s_n):
        cols = slice(s * LANES, (s + 1) * LANES)
        d = back_norm(
            rows(c3_ref, 0, s, 1), rows(q4_ref, 0, s, 1), rows(q4_ref, 1, s, 1),
            df_ref[:, :, cols], fc[:, cols].reshape(p_n, f_n, LANES), fill4,
        )
        parts.append(flat(d).astype(BF16))
    dfc = jnp.concatenate(parts, axis=1)
    add_to(i, gout, dot_tn(fact, dfc))
    z = fb_ref[...]
    back = dot_nt(dfc, wout_ref[...]).reshape(p_n, f_n, LANES) * slope(
        z * rows(c2_ref, 0, 0, 1) + rows(c2_ref, 1, 0, 1)
    )
    dfb_ref[...] = back
    sum_add(i, back, t1)
    sum_add(i, back * (z * rows(c2_ref, 2, 0, 1) - rows(c2_ref, 3, 0, 1)), t2)
    for k, value in enumerate((back, z)):
        value = flat(value)
        for p in range(p_n):
            down_ref[0, k, p : p + 1, :] = value[p * f_n : p * f_n + 1, :]
            up_ref[0, k, p : p + 1, :] = value[p * f_n + f_n - 1 : p * f_n + f_n, :]
        down_ref[0, k, p_n : p_n + 1, :] = m64_ref[0, 0:1, :]
        up_ref[0, k, p_n : p_n + 1, :] = m64_ref[0, f_n - 1 : f_n, :]

    @pl.when(i == STEPS - 1)
    def _():
        zero_ref(st_ref)
        put_rows(st_ref, 0, sum_end(s1))
        put_rows(st_ref, 8, sum_end(s2))
        put_rows(st_ref, 16, sum_end(s3))
        put_rows(st_ref, 24, sum_end(t1))
        put_rows(st_ref, 25, sum_end(t2))
        gout_ref[...] = fold_wide(gout, s_n)


def add_to(step, ref, value):
    ref[...] = jnp.where(step == 0, 0.0, ref[...]) + value


def fold_wide(ref, count):
    a = ref.shape[0] // count
    return sum(ref[s * a : (s + 1) * a, s * LANES : (s + 1) * LANES] for s in range(count))


def fold_lanes(value, count):
    a = value.shape[0] // count
    parts = [value[s * a : (s + 1) * a, :] for s in range(count)]
    return sum(p if s == 0 else pltpu.roll(p, LANES - s * a, 1) for s, p in enumerate(parts))


def k_back_out(x_ref, lact_ref, dy_ref, sp_ref, sact_ref, sb_ref, dfb_ref, fb_ref, fa_ref, ftap_ref, hp_ref, hn_ref,
               c1_ref, c2_ref, c3_ref, c4_ref, q5_ref, m16_ref, m64_ref, wso_ref, wback_ref,
               gw_ref, gs_ref, dsp_ref, dsb_ref, dfa_ref, gmid_ref, st_ref, s1, s2, t1, t2, gsc, gso, gmid):
    i = pl.program_id(0)
    s_n, p_n, t_n, c = sb_ref.shape
    sact = flat(sact_ref[...])
    fill = m16_ref[0:1, :, 0:1]
    wide = 256
    dscs = []
    turned = jnp.concatenate([flat(x_ref[...]), flat(lact_ref[...])], axis=1).T
    sact_turned = sact.T
    for n in range(wso_ref.shape[1] // wide):
        cols = slice(n * wide, (n + 1) * wide)
        shape = (s_n * p_n, t_n, wide)
        d = dy_ref[:, :, :, cols].reshape(shape)
        sc = dot(sact, wso_ref[:, cols]).reshape(shape)
        dsc = back_norm(rows(c4_ref, 0, 2 * n, 2), rows(q5_ref, 0, 2 * n, 2), rows(q5_ref, 1, 2 * n, 2), d, sc, fill)
        dsc = flat(dsc.astype(BF16))
        old = jnp.where(i == 0, 0.0, gso[:, cols])
        gso[:, cols] = old + dot(sact_turned, dsc)
        sp = sp_ref[:, :, :, cols].reshape(shape)
        dsp = back_norm(
            rows(c2_ref, 0, 3 + 2 * n, 2), rows(q5_ref, 0, 8 + 2 * n, 2), rows(q5_ref, 1, 8 + 2 * n, 2), d, sp, fill
        )
        dsp = flat(dsp.astype(BF16))
        dsp_ref[:, :, :, cols] = dsp.reshape(s_n, p_n, t_n, wide)
        old = jnp.where(i == 0, 0.0, gsc[:, cols])
        gsc[:, cols] = old + dot(turned, dsp)
        dscs.append(dsc)
    z = sb_ref[...].reshape(s_n * p_n, t_n, c)
    back = dot_nt(jnp.concatenate(dscs, axis=1), wso_ref[...])
    back = back.reshape(z.shape) * slope(z * rows(c3_ref, 0, 4, 2) + rows(c3_ref, 1, 4, 2))
    dsb_ref[...] = back.reshape(dsb_ref.shape)
    sum_add(i, back, s1)
    sum_add(i, back * (z * rows(c3_ref, 2, 4, 2) - rows(c3_ref, 3, 4, 2)), s2)

    f_n = fb_ref.shape[1]
    scale, p_row, q_row = rows(c2_ref, 0, 0, 1), rows(q5_ref, 0, 16, 1), rows(q5_ref, 1, 16, 1)
    dfb = back_norm(scale, p_row, q_row, dfb_ref[...], fb_ref[...], m64_ref[0:1])
    dfb_low = flat(dfb).astype(BF16)
    add_to(i, gmid, dot_tn(dfb_low, flat(ftap_ref[...])))
    own = dfb_low.astype(F32)
    ends = []
    for ref in (hp_ref, hn_ref):
        small = back_norm(scale, p_row, q_row, ref[0, 0], ref[0, 1], ref[0, 0, p_n : p_n + 1, :])
        small = small.astype(BF16).astype(F32)
        ends.append(
            jnp.concatenate(
                [jnp.broadcast_to(small[p : p + 1, :], (f_n, LANES)) for p in range(p_n)], axis=0
            ).reshape(p_n, f_n, LANES)
        )
    before, after = shifted(own, ends[0], ends[1], f_n)
    taps = jnp.concatenate(
        [flat(after * m64_ref[2:3]), own, flat(before * m64_ref[1:2])], axis=1
    ).astype(BF16)
    z = fa_ref[...]
    back = dot(taps, wback_ref[...]).reshape(z.shape) * slope(
        z * rows(c1_ref, 0, 0, 1) + rows(c1_ref, 1, 0, 1)
    )
    dfa_ref[...] = back
    sum_add(i, back, t1)
    sum_add(i, back * (z * rows(c1_ref, 2, 0, 1) - rows(c1_ref, 3, 0, 1)), t2)

    @pl.when(i == STEPS - 1)
    def _():
        zero_ref(st_ref)
        put_rows(st_ref, 0, sum_end(s1))
        put_rows(st_ref, 2, sum_end(s2))
        put_rows(st_ref, 4, sum_end(t1))
        put_rows(st_ref, 5, sum_end(t2))

    def late():
        for k in range(3):
            gmid_ref[k * 32 : (k + 1) * 32, :] = fold_lanes(gmid[:, k * LANES : (k + 1) * LANES], s_n)
        tall, low_tall = gsc.shape[0], gso.shape[0]
        blocks = gsc.shape[1] // wide
        for n in range(blocks):
            cols = slice(n * wide, (n + 1) * wide)
            gw_ref[n * tall : (n + 1) * tall, :] = gsc[:, cols].astype(BF16)
            gs_ref[n * low_tall : (n + 1) * low_tall, :] = gso[:, cols].astype(BF16)
        if blocks * tall < gw_ref.shape[0]:
            gw_ref[blocks * tall :, :] = jnp.zeros((gw_ref.shape[0] - blocks * tall, wide), BF16)

    return late


def slow_grad(low, dsp, w_in, w_sc, out):
    s_n, p_n, t_n, c = low.shape
    small, d_sp = flat(low[...]), flat(dsp[...])
    for n in range(out.shape[-1] // c):
        part = slice(n * c, (n + 1) * c)
        d = dot_nt(d_sp, w_sc[part, :]) + dot_nt(small, w_in[part, :])
        out[:, :, :, part] = d.astype(BF16).reshape(s_n, p_n, t_n, c)


def fast_grad(low_ref, hn, df, dlow, m16, wlat, wfa, out, gs):
    s_n, p_n, t_n, c = low_ref.shape
    shape = (s_n * p_n, t_n, c)
    low = flat(low_ref[...])
    small = hn[0].astype(F32)
    ends = [
        jnp.broadcast_to(small[s * 8 + p : s * 8 + p + 1, :], (t_n, c)) for s in range(s_n) for p in range(p_n)
    ]
    ends = jnp.concatenate(ends, axis=0).reshape(shape)
    n = low.shape[0]
    moved = pltpu.roll(low.astype(F32), n - 1, 0).reshape(shape)
    place = lax.broadcasted_iota(jnp.int32, shape, 1)
    following = flat(jnp.where(place == t_n - 1, ends, moved) * m16[2:3, :, 0:1]).astype(BF16)
    own = dot_nt(low, wlat[2 * LANES : 5 * LANES, :])
    late = dot_nt(following, wlat[0 : 2 * LANES, :])
    gs[pl.ds(0, n, stride=4), :] = own[:, 0:LANES]
    gs[pl.ds(1, n, stride=4), :] = own[:, LANES : 2 * LANES]
    gs[pl.ds(2, n, stride=4), :] = own[:, 2 * LANES :] + late[:, 0:LANES]
    gs[pl.ds(3, n, stride=4), :] = late[:, LANES:]
    back = dot(flat(dlow[...]), wfa[...])
    for s in range(s_n):
        cols = slice(s * LANES, (s + 1) * LANES)
        total = flat(df[:, :, cols]) + back[:, cols] + gs[s * n : (s + 1) * n, :]
        out[s] = total.astype(BF16).reshape(out.shape[1:])


def each(first, last, body):
    def step(k, carry):
        body(k)
        return carry
    lax.fori_loop(first, last, step, 0)


NEAR = 4


class Cube:
    def __init__(self, ch, far):
        self.ch, self.far = ch, far
        self.p, self.f = lax.axis_index("path"), lax.axis_index("frames")
        self.q, self.r = lax.rem(self.f, NEAR), lax.div(self.f, NEAR)
        self.sibling = (1 - self.p, self.f)

    def q_of(self, k):
        low = (self.q % 2 + k % 2) % 2
        return (self.q // 2 + k // 2) % 2 * 2 + low

    def r_of(self, k):
        return lax.rem(self.r + k, self.far)

    def plane(self, k):
        return (self.p, self.r * NEAR + self.q_of(k))

    def line(self, k):
        return (self.p, self.r_of(k) * NEAR + self.q)

    def at(self, path, q, r):
        return pl.ds(pl.multiple_of(((path * NEAR + q) * self.far + r) * self.ch, 16), self.ch)


def remote(src, dst, sem, index, device):
    return pltpu.make_async_remote_copy(
        src_ref=src, dst_ref=dst, send_sem=sem.at[(0, *index)], recv_sem=sem.at[(1, *index)],
        device_id=device, device_id_type=MESH)


def rows_for(sizes, n):
    unit = 16 * sizes[0] * sizes[1]
    return -(-n // unit) * unit


class Stream:
    def __init__(self, sizes, rows_n, width):
        self.sizes, self.rows_n, self.width = sizes, rows_n, width
        self.far = sizes[1] // NEAR
        self.ch = rows_n // (sizes[0] * sizes[1])
        self.chunk = (self.ch, width)
        self.near_shape = (self.far, *self.chunk)
        quad = pltpu.VMEM((NEAR, *self.near_shape), BF16)
        quad_sems, line_sems = pltpu.SemaphoreType.DMA((2, NEAR, self.far)), pltpu.SemaphoreType.DMA((2, self.far))
        self.near_scratch = [quad, quad, quad, pltpu.VMEM(self.chunk, F32), quad_sems, quad_sems]
        self.line_scratch = [pltpu.VMEM(self.near_shape, BF16), pltpu.VMEM(self.chunk, F32), line_sems]
        self.share_scratch = [line_sems, quad_sems, quad_sems, pltpu.SemaphoreType.DMA]


class Near:
    def __init__(self, stream, x, out, scratch):
        self.x, self.out, self.far, self.c = x, out, stream.far, Cube(stream.ch, stream.far)
        self.land_a, self.buf_b, self.land_b, self.acc, self.sem_a, self.sem_b = scratch

    def pair(self, k, m):
        c = self.c
        return remote(self.x.at[c.at(1 - c.p, c.q_of(k), c.r_of(m + 1))], self.land_a.at[k, m], self.sem_a, (k, m), c.sibling)

    def plane(self, k, m):
        return remote(self.buf_b.at[k, m], self.land_b.at[k, m], self.sem_b, (k, m), self.c.plane(k))

    def start(self):
        def one(m):
            each(1, NEAR, lambda k: self.pair(k, m).start())
            self.pair(0, m).start()

        each(0, self.far, one)

    def add_pair(self, first, last):
        c = self.c

        def one(k, m):
            self.pair(k, m).wait_recv()
            mine = self.x[c.at(c.p, c.q_of(k), c.r_of(m + 1)), :]
            self.buf_b[k, m] = (mine.astype(F32) + self.land_a[k, m].astype(F32)).astype(BF16)
            self.plane(k, m).start()

        each(first, last, lambda m: each(1, NEAR, lambda k: one(k, m)))

    def add_plane(self, first, last, then=None):
        c = self.c

        def one(m):
            self.pair(0, m).wait_recv()
            self.acc[...] = self.x[c.at(c.p, c.q, c.r_of(m + 1)), :].astype(F32) + self.land_a[0, m].astype(F32)

            def more(k):
                self.plane(k, m).wait_recv()
                self.acc[...] += self.land_b[k, m].astype(F32)

            each(1, NEAR, more)
            self.out[m] = self.acc[...].astype(BF16)
            if then is not None:
                then(m)

        each(first, last, one)

    def end(self):
        each(0, self.far, lambda m: each(0, NEAR, lambda k: self.pair(k, m).wait_send()))
        each(0, self.far, lambda m: each(1, NEAR, lambda k: self.plane(k, m).wait_send()))


class Line:
    def __init__(self, stream, near, scratch):
        self.near, self.far, self.c = near, stream.far, Cube(stream.ch, stream.far)
        self.land, self.acc, self.sem = scratch

    def line(self, m):
        return remote(self.near.at[m], self.land.at[m], self.sem, (m,), self.c.line(m + 1))

    def start(self, first, last):
        each(first, min(last, self.far - 1), lambda m: self.line(m).start())

    def total(self):
        self.acc[...] = self.near[self.far - 1].astype(F32)

        def one(m):
            self.line(m).wait_recv()
            self.acc[...] += self.land[m].astype(F32)

        each(0, self.far - 1, one)
        return self.acc[...].astype(BF16)

    def end(self):
        each(0, self.far - 1, lambda m: self.line(m).wait_send())


class Share:
    def __init__(self, stream, res, out, scratch):
        self.res, self.out, self.far, self.c = res, out, stream.far, Cube(stream.ch, stream.far)
        self.cut = stream.ch // 32 * 16
        self.sem_d, self.sem_e, self.sem_f, self.sem_own = scratch

    def own(self):
        return self.out.at[self.c.at(self.c.p, self.c.q, self.c.r)]

    def keep(self):
        return pltpu.make_async_copy(self.res, self.own(), self.sem_own)

    def line_back(self, k):
        return remote(self.res, self.own(), self.sem_d, (k,), self.c.line(k))

    def part(self, q, m):
        return self.out.at[self.c.at(self.c.p, q, self.c.r_of(self.far - m))]

    def plane_back(self, k, m, src=None):
        dst = self.part(self.c.q, m)
        return remote(dst if src is None else src, dst, self.sem_e, (k, m), self.c.plane(k))

    def pair_back(self, k, m, src=None):
        dst = self.part(self.c.q_of(k), m)
        return remote(dst if src is None else src, dst, self.sem_f, (k, m), self.c.sibling)

    def start_line(self):
        each(1, self.far, lambda k: self.line_back(k).start())

    def half(self, k, m):
        c, cut = self.c, self.cut
        start = ((c.p * NEAR + c.q_of(k)) * self.far + c.r_of(self.far - m)) * c.ch
        rows_n = cut if k == 1 else c.ch - cut
        part = self.out.at[pl.ds(pl.multiple_of(start + (0 if k == 1 else cut), 16), rows_n)]
        return remote(part, part, self.sem_e, (3 if k == 1 else 0, m), c.plane(3 - k))

    def start_plane(self):
        each(1, NEAR - 1, lambda k: self.plane_back(k, 0, self.res).start())
        self.pair_back(0, 0, self.res).start()
        self.keep().start()

    def relay(self, first, last):
        def one(m):
            self.line_back(m).wait_recv()
            each(1, NEAR - 1, lambda k: self.plane_back(k, m).start())
            self.pair_back(0, m).start()

        each(first, last, one)

    def hand_on(self, first, last):
        def one(m):
            for k in (1, 2):
                self.plane_back(k, m).wait_recv()
                self.half(k, m).start()
                self.pair_back(k, m).start()

        each(first, last, one)

    def hand_across(self, first, last):
        def one(m):
            for k in (1, 2):
                self.half(k, m).wait_recv()
            self.pair_back(3, m).start()

        each(first, last, one)

    def end(self):
        each(0, self.far, lambda m: each(0, NEAR, lambda k: self.pair_back(k, m).wait()))
        self.keep().wait()
        each(1, self.far, lambda k: self.line_back(k).wait_send())
        each(0, self.far, lambda m: each(1, NEAR - 1, lambda k: self.plane_back(k, m).wait_send()))

        def sent(m):
            for k in (1, 2):
                self.half(k, m).wait_send()

        each(0, self.far, sent)


def k_tail(cfg, *refs):
    st_a, st_b, ex7, ex8, side = cfg
    it = iter(refs)

    def take(n):
        return [next(it) for _ in range(n)]

    hbm = take(13)
    x_slow, lact_src, taps_src = take(3)
    gb, c1, c2, c3, q6, m16, m64, g_fout, g_fmid = take(9)
    low_out, dlow_out, lat_low_out, gf, gw_in, gw_lat, q7, q8, hn, res_a, near_b = take(11)
    local = take(13)
    gw_a, dsb, sb, spad, wsp, sa, x_fast, dfa, fa, w_in, w_sc, dsp, lat = local
    pad, gsp, gin, low, dlow, gw_b, near_a, ends, s1, s2, t1, t2, sems, out_sems = take(14)
    x_part, taps_part, gsi, glat, wsp_turned, x_sems, taps_sems, lact_sem = take(8)
    near1, line1, near2 = take(len(st_a.near_scratch)), take(len(st_a.line_scratch)), take(len(st_b.near_scratch))
    scr7 = take(len(ex7.local) + len(ex7.work))
    scr8 = take(len(ex8.local) + len(ex8.work))
    n_in = w_in.shape[0]
    srcs = list(hbm)
    for k in (9, 10):
        srcs[k] = hbm[k].at[pl.ds(hbm[k].shape[0] - n_in, n_in)]
    loads = [pltpu.make_async_copy(src, dst, sems.at[k]) for k, (src, dst) in enumerate(zip(srcs, local))]
    count = exchange_hello(ex8)
    for k in (1, 2, 0, 4, 3, 5, 6, 7, 8, 9, 10, 11, 12):
        loads[k].start()
    near = Near(st_a, gw_a, near_a, near1)
    line = Line(st_a, near_a, line1)
    near_two = Near(st_b, gw_b, near_b, near2)
    far = st_a.far
    t_n, c = pad.shape[2], pad.shape[3]
    wide = side * t_n
    per = side // STEPS
    fill = m16[0:1, :, 0:1]

    def waits(*names):
        for k in names:
            loads[k].wait()

    waits(1, 2)
    scale, p_row, q_row = rows(c3, 0, 4, 2), rows(q6, 0, 0, 2), rows(q6, 1, 0, 2)
    zero_ref(pad)

    def fill_pad(h):
        part = pl.ds(h * wide, wide)
        d = back_norm(
            scale, p_row, q_row, dsb[part].reshape(side, t_n, c), sb[part].reshape(side, t_n, c), fill
        )
        pad[h + 1, 1 : side + 1] = d.astype(BF16)

    each(0, side, fill_pad)
    waits(0, 4)
    for k in range(9):
        wsp_turned[k * c : (k + 1) * c, :] = wsp[k * c : (k + 1) * c, :].T
    pl.semaphore_wait(pltpu.get_barrier_semaphore(), count)
    near.start()
    waits(3, 5, 6, 7, 8)
    f_n = x_fast.shape[2]
    p_n = x_fast.shape[1] // STEPS

    def spatial(i):
        h0 = i * per
        turned = flat(pad[pl.ds(h0 + 1, per), 1 : side + 1]).T
        blocks = []
        for a in range(3):
            for b in range(3):
                k = 3 * a + b
                patch = flat(spad[pl.ds(h0 + a, per), b : b + side])
                cols = slice(k * c, (k + 1) * c)
                gsp[:, cols] = jnp.where(i == 0, 0.0, gsp[:, cols]) + dot(turned, patch)
                blocks.append(flat(pad[pl.ds(h0 + 2 - a, per), 2 - b : 2 - b + side]))
        acc = dot(jnp.concatenate(blocks, axis=1), wsp_turned[...])
        span = pl.ds(i * per * wide, per * wide)
        z = sa[span]
        back = acc * slope(z * rows(c2, 0, 1, 2) + rows(c2, 1, 1, 2))
        dsb[span] = back
        unit = z * rows(c2, 2, 1, 2) - rows(c2, 3, 1, 2)
        sum_add(i, back.reshape(per * side, t_n, c), s1)
        sum_add(i, (back * unit).reshape(per * side, t_n, c), s2)
        f_span = pl.ds(i * p_n, p_n)
        small = back_norm(
            rows(c1, 0, 0, 1), rows(q6, 0, 2, 1), rows(q6, 1, 2, 1), dfa[f_span], fa[f_span], m64[0:1]
        ).astype(BF16)
        dlow[f_span] = small
        packed = jnp.concatenate([flat(x_fast[s, f_span]) for s in range(x_fast.shape[0])], axis=1)
        add_to(i, gin, dot_tn(flat(small), packed))
        pl.when(i == 0)(lambda: near.add_pair(0, far // 2))
        pl.when(i == 1)(lambda: near.add_pair(far // 2, far))

    each(0, STEPS, spatial)
    stats = scr7[0]
    zero_ref(stats)
    put_rows(stats, 0, sum_end(s1))
    put_rows(stats, 2, sum_end(s2))
    stores = [pltpu.make_async_copy(dlow, dlow_out, out_sems.at[0])]
    stores[0].start()

    def late():
        for k in range(9):
            gw_b[k * c : (k + 1) * c, :] = gsp[:, k * c : (k + 1) * c].T.astype(BF16)
        if 9 * c < gw_b.shape[0]:
            gw_b[9 * c :, :] = jnp.zeros((gw_b.shape[0] - 9 * c, c), BF16)
        n = g_fout.shape[0]
        gf[0:n, 0:LANES] = fold_wide(gin, x_fast.shape[0])
        gf[0:n, LANES:] = g_fout[...]
        gf[n : 2 * n, 0:LANES] = g_fmid[0:n, :]
        gf[n : 2 * n, LANES:] = g_fmid[n : 2 * n, :]
        gf[2 * n :, 0:LANES] = g_fmid[2 * n :, :]
        gf[2 * n :, LANES:] = jnp.zeros((n, LANES), F32)

    n_pos = side * side
    lact = spad.reshape(-1, t_n, c).at[pl.ds(0, n_pos)]
    lat_low = pad.reshape(-1, t_n, c).at[pl.ds(0, n_pos)]
    lact_load = pltpu.make_async_copy(lact_src, lact, lact_sem)
    lact_load.start()
    block = per * wide

    def x_load(i):
        return pltpu.make_async_copy(x_slow.at[pl.ds(i * block, block)], x_part.at[i % 2], x_sems.at[i % 2])

    def taps_load(i):
        return pltpu.make_async_copy(taps_src.at[pl.ds(i * block, block)], taps_part.at[i % 2], taps_sems.at[i % 2])

    for i in range(2):
        x_load(i).start()
        taps_load(i).start()
    def pull():
        near_two.start()
        near.add_plane(0, far // 2, lambda m: line.line(m).start())

    exchange_run(ex7, [gb, c2], [q7], scr7, late, between=pull)
    near.add_plane(far // 2, far - 1, lambda m: line.line(m).start())
    near.add_plane(far - 1, far)
    waits(9, 10, 11, 12)
    scale7, p7, q7_row = rows(c2, 0, 1, 2), rows(q7, 0, 0, 2), rows(q7, 1, 0, 2)

    def join(i):
        span = pl.ds(i * block, block)
        shape = (per * side, t_n, c)
        d = back_norm(scale7, p7, q7_row, dsb[span].reshape(shape), sa[span].reshape(shape), fill)
        small = flat(d).astype(BF16)
        low[span] = small
        d = dot_nt(dsp[span], w_sc[...]) + dot_nt(small, w_in[...])
        z = lat[span]
        back = d * slope(z * rows(c1, 0, 1, 2) + rows(c1, 1, 1, 2))
        sb[span] = back
        unit = z * rows(c1, 2, 1, 2) - rows(c1, 3, 1, 2)
        sum_add(i, back.reshape(shape), t1)
        sum_add(i, (back * unit).reshape(shape), t2)
        pl.when(i == 2)(lambda: near_two.add_pair(0, far))

    each(0, STEPS, join)
    stores.append(pltpu.make_async_copy(low, low_out, out_sems.at[1]))
    stores[1].start()
    stats = scr8[0]
    zero_ref(stats)
    put_rows(stats, 0, sum_end(t1))
    put_rows(stats, 2, sum_end(t2))

    def post(q, sent):
        d = back_norm(rows(c1, 0, 1, 2), rows(q, 0, 0, 2), rows(q, 1, 0, 2), ends[0], ends[1], m16[0, 0:1, 0:1])
        sent[...] = d.astype(BF16)

    def in_step(i):
        x_load(i).wait()
        joined = jnp.concatenate([x_part[i % 2], flat(lact[pl.ds(i * per * side, per * side)])], axis=1)
        add_to(i, gsi, dot(low[pl.ds(i * block, block)].T, joined))
        pl.when(i + 2 < STEPS)(lambda: x_load(i + 2).start())

    def in_grad():
        zero_ref(ends)
        for s in range(x_fast.shape[0]):
            for step in range(STEPS):
                for p in range(p_n):
                    at = ((s * STEPS + step) * p_n + p) * t_n
                    ends[0, step, s * 8 + p : s * 8 + p + 1, :] = sb[at : at + 1, :]
                    ends[1, step, s * 8 + p : s * 8 + p + 1, :] = lat[at : at + 1, :]
        lact_load.wait()
        each(0, 3, in_step)

    def in_grad_rest():
        each(3, STEPS, in_step)
        for n in range(gsi.shape[1] // c):
            gw_in[n * c : (n + 1) * c, :] = gsi[:, n * c : (n + 1) * c].T.astype(BF16)

    def lat_step(i):
        scale8, p8, q8_row = rows(c1, 0, 1, 2), rows(q8, 0, 0, 2), rows(q8, 1, 0, 2)
        span = pl.ds(i * block, block)
        shape = (per * side, t_n, c)
        d = back_norm(scale8, p8, q8_row, sb[span].reshape(shape), lat[span].reshape(shape), fill).astype(BF16)
        lat_low[pl.ds(i * per * side, per * side)] = d
        taps_load(i).wait()
        add_to(i, glat, dot_tn(flat(d), taps_part[i % 2]))
        pl.when(i + 2 < STEPS)(lambda: taps_load(i + 2).start())

    def lat_grad():
        each(0, STEPS, lat_step)
        stores.append(pltpu.make_async_copy(lat_low, lat_low_out, out_sems.at[2]))
        stores[2].start()
        for k in range(glat.shape[1] // LANES):
            gw_lat[k * LANES : (k + 1) * LANES, :] = glat[:, k * LANES : (k + 1) * LANES].T.astype(BF16)

    exchange_run(ex8, [gb, c1], [q8, hn], scr8, in_grad, post, lat_grad, in_grad_rest)
    res_a[...] = line.total()
    near_two.add_plane(0, far)
    for store in stores:
        store.wait()
    line.end()
    near.end()
    near_two.end()


def back_tail(st_a, st_b, ex7, ex8, hbm, more, small, side, t_n, c):
    vm, anywhere = pl.BlockSpec(memory_space=pltpu.VMEM), pl.BlockSpec(memory_space=pl.ANY)
    inner, f_n = hbm[7].shape[:2]
    n = side * side * t_n
    c_cat, c_taps = more[0].shape[1] + c, more[2].shape[1]
    part = n // STEPS
    outs = [((n, c), BF16), ((inner, f_n, LANES), BF16), (more[1].shape, BF16), (small[-1].shape[0:1] + (2 * LANES,), F32),
            ((c_cat, c), BF16), ((c_taps, c), BF16),
            *ex7.outs, *ex8.outs, (st_a.chunk, BF16), (st_b.near_shape, BF16)]
    local = [pltpu.VMEM((c,) + a.shape[1:] if k in (9, 10) else a.shape, a.dtype) for k, a in enumerate(hbm)]
    width = hbm[6].shape[0] * hbm[6].shape[3]
    scratch = [
        pltpu.VMEM((side + 2, side + 2, t_n, c), BF16), pltpu.VMEM((c, 9 * c), F32), pltpu.VMEM((LANES, width), F32),
        pltpu.VMEM((n, c), BF16), pltpu.VMEM((inner, f_n, LANES), BF16), pltpu.VMEM((st_b.rows_n, c), BF16),
        pltpu.VMEM(st_a.near_shape, BF16), pltpu.VMEM((2, *ex8.post), F32), *[pltpu.VMEM((t_n, c), F32)] * 4,
        pltpu.SemaphoreType.DMA((len(hbm),)), pltpu.SemaphoreType.DMA((3,)),
        pltpu.VMEM((2, part, c_cat - c), BF16), pltpu.VMEM((2, part, c_taps), BF16), pltpu.VMEM((c, c_cat), F32),
        pltpu.VMEM((c, c_taps), F32), pltpu.VMEM((9 * c, c), BF16), pltpu.SemaphoreType.DMA((2,)), pltpu.SemaphoreType.DMA((2,)), pltpu.SemaphoreType.DMA,
        *st_a.near_scratch, *st_a.line_scratch, *st_b.near_scratch, *ex7.local, *ex7.work, *ex8.local, *ex8.work,
    ]
    return pl.pallas_call(
        functools.partial(k_tail, (st_a, st_b, ex7, ex8, side)),
        out_shape=[jax.ShapeDtypeStruct(s, d) for s, d in outs],
        in_specs=[anywhere] * (len(hbm) + len(more)) + [vm] * len(small),
        out_specs=[anywhere] * 3 + [vm] * (len(outs) - 3),
        scratch_shapes=[*local, *scratch],
        compiler_params=pltpu.CompilerParams(collective_id=ex8.cid, has_side_effects=True, vmem_limit_bytes=VMEM_LIMIT),
        name="tail",
    )(*hbm, *more, *small)


def final_kernel(cfg, *refs):
    first, second, third, both, offsets, n_hbm, n_small = cfg
    it = iter(refs)

    def take(n):
        return [next(it) for _ in range(n)]

    hbm, small, (out_a, out_bc, gx_out, fast_out) = take(n_hbm), take(n_small), take(4)
    res_a, near_b, *parts, hn, m16, wlat, wfa = small
    loaded = take(n_hbm)
    low, dsp, w_in, w_sc, lat_low, df, dlow = loaded
    x, near_c, res, gx, fast_gx, gs, sems, gx_sems, fast_sems = take(9)
    share_a = Share(first, res_a, out_a, take(len(first.share_scratch)))
    line_b = Line(second, near_b, take(len(second.line_scratch)))
    near = Near(third, x, near_c, take(len(third.near_scratch)))
    line_c = Line(third, near_c, take(len(third.line_scratch)))
    share = Share(both, res, out_bc, take(len(both.share_scratch)))
    far, c = first.far, near.c
    barrier = pltpu.get_barrier_semaphore()
    loads = [pltpu.make_async_copy(a, b, sems.at[k]) for k, (a, b) in enumerate(zip(hbm, loaded))]

    def greet(device):
        pl.semaphore_signal(barrier, inc=1, device_id=device, device_id_type=MESH)

    greet(c.sibling)
    each(1, NEAR, lambda k: greet(c.plane(k)))
    each(1, far, lambda k: greet(c.line(k)))
    for load in loads:
        load.start()
    for ref, first_row, end in zip(parts, offsets, offsets[1:]):
        x[first_row:end, :] = ref[...].astype(BF16)
    if end < x.shape[0]:
        x[end:, :] = jnp.zeros((x.shape[0] - end, x.shape[1]), BF16)
    pl.semaphore_wait(barrier, NEAR + far - 1)

    near.start()
    line_b.start(0, far)
    share_a.start_line()
    p_n = dlow.shape[0] // STEPS

    def gx_store(i):
        part = pl.ds(i * p_n, p_n)
        return pltpu.make_async_copy(gx.at[:, part], gx_out.at[:, part], gx_sems.at[i])

    def slow_step(i):
        part = pl.ds(i * p_n, p_n)
        slow_grad(low.at[:, part], dsp.at[:, part], w_in, w_sc, gx.at[:, part])
        gx_store(i).start()

    def fast_store(i):
        part = pl.ds(i * p_n, p_n)
        return pltpu.make_async_copy(fast_gx.at[:, part], fast_out.at[:, part], fast_sems.at[i])

    def fast_step(i):
        part = pl.ds(i * p_n, p_n)
        fast_grad(lat_low.at[:, part], hn.at[pl.ds(i, 1)], df.at[part], dlow.at[part], m16, wlat, wfa,
                  fast_gx.at[:, part], gs)
        fast_store(i).start()

    share_a.start_plane()
    near.add_pair(0, far)
    for k in (0, 1, 2, 3):
        loads[k].wait()
    each(0, 1, slow_step)
    res[0 : second.ch, :] = line_b.total()
    share_a.relay(1, far)
    share_a.hand_on(0, 1)
    each(1, 3, slow_step)
    near.add_plane(0, far - 1, lambda m: line_c.line(m).start())
    near.add_plane(far - 1, far)
    share_a.hand_on(1, far)
    each(3, 4, slow_step)
    res[second.ch :, :] = line_c.total()
    share.start_line()
    share.start_plane()
    each(4, STEPS, slow_step)
    for k in range(4, n_hbm):
        loads[k].wait()
    share.relay(1, far)
    share_a.hand_across(0, far)
    share.hand_on(0, 1)
    each(0, 3, fast_step)
    share.hand_on(1, far)
    each(3, STEPS, fast_step)
    share.hand_across(0, far)
    share_a.end()
    share.end()
    line_b.end()
    line_c.end()
    near.end()
    each(0, STEPS, lambda i: gx_store(i).wait())
    each(0, STEPS, lambda i: fast_store(i).wait())


def final_sum(sizes, cid, first, second, hbm, small, gx, fast_gx, heights):
    width = first.width
    offsets = tuple(sum(heights[:k]) for k in range(len(heights) + 1))
    third = Stream(sizes, rows_for(sizes, offsets[-1]), width)
    both = Stream(sizes, second.rows_n + third.rows_n, width)
    vm, anywhere = pl.BlockSpec(memory_space=pltpu.VMEM), pl.BlockSpec(memory_space=pl.ANY)
    low, dlow = hbm[0], hbm[6]
    s_n, p_n, f_n = low.shape[0], low.shape[1] // STEPS, dlow.shape[1]
    out_a, out_bc, gx, fast_gx = pl.pallas_call(
        functools.partial(final_kernel, (first, second, third, both, offsets, len(hbm), len(small))),
        out_shape=[jax.ShapeDtypeStruct(s, BF16) for s in ((first.rows_n, width), (both.rows_n, width), gx, fast_gx)],
        in_specs=[anywhere] * len(hbm) + [vm] * len(small),
        out_specs=[anywhere] * 4,
        scratch_shapes=[
            *[pltpu.VMEM(a.shape, a.dtype) for a in hbm],
            pltpu.VMEM((third.rows_n, width), BF16), pltpu.VMEM(third.near_shape, BF16), pltpu.VMEM(both.chunk, BF16),
            pltpu.VMEM(gx, BF16), pltpu.VMEM(fast_gx, BF16), pltpu.VMEM((s_n * p_n * f_n, LANES), F32),
            pltpu.SemaphoreType.DMA((len(hbm),)), pltpu.SemaphoreType.DMA((STEPS,)), pltpu.SemaphoreType.DMA((STEPS,)),
            *first.share_scratch, *second.line_scratch, *third.near_scratch, *third.line_scratch, *both.share_scratch,
        ],
        compiler_params=pltpu.CompilerParams(collective_id=cid, has_side_effects=True, vmem_limit_bytes=VMEM_LIMIT),
        name="final_sum",
    )(*hbm, *small)
    return out_a, out_bc.reshape(-1, both.ch, width), gx, fast_gx


def k_unpack(pieces, cut, *refs):
    (src_a, src_b, q4, q5, q6, q7, q8), held, refs = refs[:7], refs[7:10], refs[10:]
    outs, (low_a, low_b, low_c, wide, line, *kept, sem_a, sem_b, sem_out, sem_held) = refs[:-12], refs[-12:]
    outs, given = outs[:-3], outs[-3:]

    def moves(srcs, dsts, way):
        return [
            pltpu.make_async_copy(a.at[pl.ds(k, 1)], b.at[pl.ds(k, 1)], sem_held.at[way, n, k])
            for n, (a, b) in enumerate(zip(srcs, dsts))
            for k in range(a.shape[0])
        ]

    passes_in, passes = moves(held, kept, 0), moves(kept, given, 1)
    outs, (gains_out, biases_out, in_out, mid_out, out_out) = outs[:-5], outs[-5:]
    lows = (low_a, low_b, low_c)
    flats = [low_a, low_b.reshape(-1, low_b.shape[-1]), low_c.reshape(-1, low_c.shape[-1])]
    starts = [sum(p[2] for p in pieces[:k]) for k in range(len(pieces))]

    def fetch_a(k):
        _, row, height, _, _ = pieces[k]
        return pltpu.make_async_copy(src_a.at[pl.ds(row, height)], low_a.at[pl.ds(row, height)], sem_a.at[k])

    def fetch_b(k):
        part = src_b.at[:, pl.ds(0, cut)] if k == 1 else src_b.at[:, pl.ds(cut, src_b.shape[1] - cut)]
        return pltpu.make_async_copy(part, lows[k], sem_b.at[k])

    def store(k):
        _, _, height, out, col = pieces[k]
        part = outs[out] if col is None else outs[out].at[:, pl.ds(col, wide.shape[1])]
        return pltpu.make_async_copy(wide.at[pl.ds(starts[k], height)], part, sem_out.at[k])

    for k, piece in enumerate(pieces):
        if piece[0] == 0:
            fetch_a(k).start()
    for k in (1, 2):
        fetch_b(k).start()
    for move in passes_in:
        move.start()
    seen = 0
    for k, (src, row, height, _, _) in enumerate(pieces):
        if src == 0:
            fetch_a(k).wait()
        elif src != seen:
            fetch_b(src).wait()
            seen = src
        wide[starts[k] : starts[k] + height, :] = flats[src][row : row + height, :].astype(F32)
        store(k).start()
    for move_in, move in zip(passes_in, passes):
        move_in.wait()
        move.start()
    lane = lax.broadcasted_iota(jnp.int32, (1, LANES), 1)
    left = lane < LANES // 2
    for slab, out in ((3, gains_out), (2, biases_out)):
        at = 0
        for q, first, count in ((q4, 0, 1), (q8, 0, 2), (q7, 0, 2), (q6, 0, 2), (q5, 0, 16)):
            line[at : at + count, :] = q[slab, first : first + count, :]
            at += count
        half = pltpu.roll(line[0:at, :], LANES // 2, 1)
        head = jnp.where(lane < LANES // 4, q6[slab, 2:3, :], q5[slab, 16:17, :])
        out[0:1, :] = jnp.where(left, head, half[0:1])
        out[1:at, :] = jnp.where(left, half[0 : at - 1], half[1:at])
        out[at : at + 1, :] = jnp.where(left, half[at - 1 : at], 0.0)
    a = in_out.shape[0]
    last = sum(p[2] for p in pieces if p[0] == 2)
    small = flats[2][last : last + 3 * a, :]
    in_out[...] = small[0:a, 0:LANES].astype(F32)
    out_out[...] = small[0:a, LANES:].astype(F32)
    eye = (lax.broadcasted_iota(jnp.int32, (a, a), 0) == lax.broadcasted_iota(jnp.int32, (a, a), 1)).astype(BF16)
    for k, (row, col) in enumerate(((a, 0), (a, LANES), (2 * a, 0))):
        mid_out[k] = dot_tn(small[row : row + a, col : col + LANES], eye)[0:a, :]
    for k in range(len(pieces)):
        store(k).wait()
    for move in passes:
        move.wait()


def unpack(src_a, src_b, cut, pieces, shapes, small_shapes, norm_sums, held):
    hbm, vm = pl.BlockSpec(memory_space=pl.ANY), pl.BlockSpec(memory_space=pltpu.VMEM)
    n, _, width = src_b.shape
    return pl.pallas_call(
        functools.partial(k_unpack, pieces, cut),
        out_shape=[jax.ShapeDtypeStruct(s, F32) for s in (*shapes, *small_shapes)]
        + [jax.ShapeDtypeStruct(a.shape, a.dtype) for a in held],
        in_specs=[hbm] * 2 + [vm] * len(norm_sums) + [hbm] * len(held),
        out_specs=[hbm] * len(shapes) + [vm] * len(small_shapes) + [hbm] * len(held),
        scratch_shapes=[
            pltpu.VMEM(src_a.shape, BF16),
            pltpu.VMEM((n, cut, width), BF16),
            pltpu.VMEM((n, src_b.shape[1] - cut, width), BF16),
            pltpu.VMEM((sum(p[2] for p in pieces), width), F32),
            pltpu.VMEM((24, LANES), F32),
            *[pltpu.VMEM(a.shape, a.dtype) for a in held],
            pltpu.SemaphoreType.DMA((len(pieces),)),
            pltpu.SemaphoreType.DMA((3,)),
            pltpu.SemaphoreType.DMA((len(pieces),)),
            pltpu.SemaphoreType.DMA((2, len(held), held[0].shape[0])),
        ],
        compiler_params=pltpu.CompilerParams(vmem_limit_bytes=VMEM_LIMIT),
        name="unpack",
    )(src_a, src_b, *norm_sums, *held)


def small_set_up(fill_ref, clip_ref, norm_ref, wfi_ref, wfm_ref, wfo_ref,
                 gb_ref, m16_ref, m64_ref, wfa_ref, wmid_ref, wback_ref, wout_ref, s_n, t_n):
    length = lax.axis_size("frames")
    total = lax.axis_size("path") * length
    me = lax.axis_index("path") * length + lax.axis_index("frames")
    lane = lax.broadcasted_iota(jnp.int32, (1, LANES), 1)
    for k in range(2):
        half = pltpu.roll(norm_ref[k], LANES // 2, 1)
        main = jnp.where(lane < LANES // 2, half[0:23], half[1:24])
        for j in range(2):
            v = jnp.where(lane // 32 == j, norm_ref[k, 0:1, :], 0.0)
            v = v + pltpu.roll(v, 64, 1)
            gb_ref[k, j : j + 1, :] = v + pltpu.roll(v, 32, 1)
        for j in range(4):
            gb_ref[k, 2 + j : 3 + j, :] = main[0:1]
        gb_ref[k, 6:28, :] = main[1:23]
        gb_ref[k, 28:32, :] = jnp.zeros((4, LANES), F32)

    def row(value):
        return jnp.full((1, LANES), value, F32)

    last = jnp.where(me < total - 1, 1.0, 0.0)
    link = [jnp.where(clip_ref[t] >= 1, 1.0, 0.0) for t in range(t_n)]
    for t in range(t_n):
        filled = row(fill_ref[t].astype(F32))
        after = row(link[t + 1] if t + 1 < t_n else last)
        m16_ref[0, t : t + 1, :] = filled
        m16_ref[1, t : t + 1, :] = row(link[t])
        m16_ref[2, t : t + 1, :] = after
        m64_ref[0, 4 * t : 4 * t + 4, :] = jnp.broadcast_to(filled, (4, LANES))
        m64_ref[1, 4 * t : 4 * t + 1, :] = row(link[t])
        m64_ref[1, 4 * t + 1 : 4 * t + 4, :] = jnp.ones((3, LANES), F32)
        m64_ref[2, 4 * t : 4 * t + 3, :] = jnp.ones((3, LANES), F32)
        m64_ref[2, 4 * t + 3 : 4 * t + 4, :] = after

    zero_ref(wfa_ref)
    zero_ref(wout_ref)
    a = wfi_ref.shape[0]
    for s in range(s_n):
        wfa_ref[s * a : (s + 1) * a, s * LANES : (s + 1) * LANES] = wfi_ref[...]
        wout_ref[s * a : (s + 1) * a, s * LANES : (s + 1) * LANES] = wfo_ref[...]
    tall = (LANES, a)
    spread = (lax.broadcasted_iota(jnp.int32, tall, 0) % a == lax.broadcasted_iota(jnp.int32, tall, 1)).astype(BF16)
    square = (LANES, LANES)
    diag = lax.broadcasted_iota(jnp.int32, square, 0) // a == lax.broadcasted_iota(jnp.int32, square, 1) // a
    for k in range(3):
        left = dot(spread, wfm_ref[k]).astype(BF16)
        wmid_ref[k * LANES : (k + 1) * LANES, :] = jnp.where(diag, dot_nt(left, spread), 0.0).astype(BF16)
        right = dot_nt(spread, wfm_ref[k]).astype(BF16)
        wback_ref[k * LANES : (k + 1) * LANES, :] = jnp.where(diag, dot_nt(right, spread), 0.0).astype(BF16)


def per_device(slow_input, fast_input, clip_offset, fill, w_fast_in, w_fast_mid, w_fast_out, w_lateral,
               w_slow_in, w_slow_mid, w_slow_out, w_shortcut, gains, biases, slow_cot, fast_cot):
    sizes = (lax.axis_size("path"), lax.axis_size("frames"))
    t_n, side, _, c_slow = slow_input.shape
    f_n, c_fast = fast_input.shape[0], fast_input.shape[3]
    in_fast, in_slow, c_lat = w_fast_in.shape[1], w_slow_in.shape[1], w_lateral.shape[2]
    pixels = side * side
    groups = LANES // in_fast
    inner = pixels // groups
    p_n = inner // STEPS

    def slow_view(a):
        return jnp.transpose(a, (1, 2, 0, 3)).reshape(groups, inner, t_n, a.shape[3])

    def fast_view(a):
        return jnp.transpose(a, (1, 2, 0, 3)).reshape(groups, inner, f_n, a.shape[3])

    def unview(a):
        return jnp.transpose(a.reshape(side, side, a.shape[2], a.shape[3]), (2, 0, 1, 3))

    x_slow, cot_slow = slow_view(slow_input), slow_view(slow_cot)
    x_fast, cot_fast = fast_view(fast_input), fast_view(fast_cot)

    norms = jnp.stack([gains, biases])
    norms = jnp.pad(norms, ((0, 0), (0, -norms.shape[1] % (8 * LANES)))).reshape(2, -1, LANES)
    wlat = w_lateral.reshape(-1, c_lat)
    wsp = w_slow_mid.reshape(-1, in_slow)

    sl = (groups, inner, t_n)
    fp = (inner, f_n)

    def slow_out(width, dtype):
        return out_blocked(sl + (width,), dtype, 1, p_n)

    def fast_out(width, dtype):
        return out_blocked(fp + (width,), dtype, 0, p_n)

    def sb_(a):
        return blocked(a, 1, p_n)

    def fb_(a):
        return blocked(a, 0, p_n)

    def stat(n):
        return out_whole((pad8(n), LANES), F32)

    def acc(rows_n, width, count):
        return [pltpu.VMEM((rows_n, width), F32)] * count

    small = (STEPS, 8, LANES)

    sems7 = pltpu.SemaphoreType.DMA((STEPS,))
    exs = [
        Exchange(sizes, 1, 7, fwd=(("lane4", 0, 1), ("plain", 6, 2)), up=small, down=small),
        Exchange(sizes, 1, 23, fwd=(("lane4", 1, 1), ("plain", 8, 2), ("plain", 20, 8))),
    ]
    kept = [
        (fp + (LANES,), F32), (sl + (c_lat,), F32), (sl + (5 * c_fast,), BF16), (sl + (c_lat,), BF16),
        (fp + (3 * LANES,), BF16), (sl + (in_slow,), F32), (sl + (c_slow,), F32), (fp + (LANES,), F32),
    ]
    ready = [((2, 32, LANES), F32), ((3, t_n, LANES), F32), ((3, f_n, LANES), F32), ((LANES, groups * c_fast), BF16),
             ((3 * LANES, LANES), BF16), ((3 * LANES, LANES), BF16), ((LANES, groups * c_fast), BF16)]
    ends = (STEPS, groups * 8, 2 * c_fast)
    fa, lat, taps, lact, ftap, sa, sp, fb, gb, m16, m64, wfa, wmid, wback, wout, c1, hp, hn, c2 = run_resident(
        functools.partial(k_front, exs), exs,
        [x_fast, wlat, x_slow, w_slow_in, w_shortcut],
        [fill, clip_offset, norms, w_fast_in.T, w_fast_mid, w_fast_out],
        kept, [*[(*k, True) for k in kept], *[(*k, False) for k in ready]],
        [pltpu.VMEM((groups * p_n * f_n, c_fast), F32), *acc(f_n, LANES, 2), *acc(t_n, c_lat, 2), *acc(t_n, in_slow, 2),
         *acc(t_n, c_slow, 2), *acc(f_n, LANES, 2), pltpu.SemaphoreType.DMA((8,)), sems7,
         pltpu.VMEM((pixels * t_n, c_fast), F32), pltpu.VMEM(ends, F32), pltpu.VMEM(ends, BF16), pltpu.VMEM(ends, BF16),
         pltpu.SemaphoreType.DMA((2,))],
        "front",
        scalars=2,
    )

    exs = [
        Exchange(sizes, 3, 13, fwd=(("row4", 2, 4), ("plain", 10, 2))),
        Exchange(sizes, 3, 25, fwd=(("plain", 12, 8),), bwd=(("row4", 0, 0, 2, 4, 0, 4),)),
    ]
    kept = [
        ((side + 2, side + 2, t_n, in_slow), BF16), ((pixels, t_n, in_slow), F32), (fp + (LANES,), BF16),
        ((pixels, t_n, in_slow), BF16), ((groups, inner, f_n, c_fast), BF16), (fp + (groups * c_fast,), F32),
    ]
    pad, sb, fact, sact, fast_y, df, c3, c4, q4 = run_resident(
        functools.partial(k_middle, exs), exs,
        [sa.reshape(side, side, t_n, in_slow), fb, wsp, w_slow_out, x_fast, cot_fast], [gb, c2, m16, m64, wout],
        kept, [(*k, True) for k in kept],
        [*acc(t_n, in_slow, 2), *acc(f_n, groups * c_fast, 2), *acc(t_n, c_slow, 2), *acc(f_n, groups * c_fast, 2),
         pltpu.SemaphoreType.DMA((4,)), sems7, sems7],
        "middle",
    )
    sb4, sact = sb.reshape(sl + (in_slow,)), sact.reshape(sl + (in_slow,))

    halo_pair = out_blocked((STEPS, 2, 8, LANES), F32, 0, 1)
    slow_y, dy, dfb, g_fout, up, down, st = call(
        k_out,
        [sb_(sact), sb_(sp), sb_(cot_slow), fb_(df), fb_(fact), fb_(fb), whole(c2), whole(c3), whole(c4), whole(q4),
         whole(m16), whole(m64), whole(w_slow_out), whole(wout)],
        [slow_out(c_slow, BF16), slow_out(c_slow, F32), fast_out(LANES, F32),
         out_whole((in_fast, c_fast), F32), halo_pair, halo_pair, stat(26)],
        [*acc(t_n, c_slow, 3), *acc(f_n, LANES, 2), *acc(LANES, groups * c_fast, 1)],
        "out",
    )
    pair = (STEPS, 2, 8, LANES)
    ex5 = Exchange(
        sizes, 6, 26,
        bwd=(("plain", 0, 0, 12, 8, 0, 8), ("plain", 1, 3, 20, 8, 0, 16), ("lane4", 1, 0, 1, 1, 24, 25)),
        up=pair, down=pair,
    )
    c_cat = w_slow_in.shape[0]
    width = in_slow
    stream_a = Stream(sizes, rows_for(sizes, c_cat * c_slow // width), width)
    stream_b = Stream(sizes, rows_for(sizes, 9 * in_slow), width)
    gw_short, gw_sout, dsp, dsb, dfa, g_fmid, q6, q5 = call(
        k_back_out,
        [sb_(x_slow), sb_(lact), sb_(dy), sb_(sp), sb_(sact), sb_(sb4), fb_(dfb), fb_(fb), fb_(fa), fb_(ftap), 1, 2,
         whole(c1), whole(c2), whole(c3), whole(c4), 0, whole(m16), whole(m64), whole(w_slow_out), whole(wback)],
        [out_whole((stream_a.rows_n, width), BF16), out_whole((c_slow, width), BF16), slow_out(c_slow, BF16),
         slow_out(in_slow, F32), fast_out(LANES, F32), out_whole((3 * in_fast, LANES), F32), STAT],
        [*acc(t_n, in_slow, 2), *acc(f_n, LANES, 2), *acc(c_cat, c_slow, 1), *acc(in_slow, c_slow, 1),
         *acc(LANES, 3 * LANES, 1)],
        "back_out",
        Exchange(sizes, 6, 6, bwd=(("plain", 0, 4, 10, 2, 0, 2), ("lane4", 1, 0, 0, 1, 4, 5))),
        [gb, c3, c1],
        ex5,
        [st, up, down, gb, c4, c2],
    )

    def rows2(a):
        return a.reshape(-1, a.shape[-1])

    dsa_low, dfa_low, lat_low, gw_fast, gw_in, gw_lat, q7, q8, hn, res_a, near_b = back_tail(
        stream_a, stream_b,
        Exchange(sizes, 7, 4, bwd=(("plain", 0, 1, 8, 2, 0, 2),)),
        Exchange(sizes, 7, 4, bwd=(("plain", 0, 1, 6, 2, 0, 2),), post=(STEPS, groups * 8, c_lat)),
        [gw_short, rows2(dsb), rows2(sb4), pad, wsp, rows2(sa), x_fast, dfa, fa, w_slow_in, w_shortcut, rows2(dsp), rows2(lat)],
        [rows2(x_slow), lact.reshape(pixels, t_n, c_lat), rows2(taps)],
        [gb, c1, c2, c3, q6, m16, m64, g_fout, g_fmid],
        side, t_n, in_slow,
    )
    heights = (gw_sout.shape[0], c_cat, 5 * c_fast, gw_fast.shape[0])
    sum_a, sum_bc, slow_gx, fast_gx = final_sum(
        sizes, 9, stream_a, stream_b,
        [dsa_low.reshape(sl + (in_slow,)), dsp, w_slow_in, w_shortcut, lat_low.reshape(sl + (c_lat,)), df, dfa_low],
        [res_a, near_b, gw_sout, gw_in, gw_lat, gw_fast, hn, m16, wlat, wfa],
        sl + (c_slow,), (groups, inner, f_n, c_fast), heights,
    )
    blocks = c_slow // in_slow
    pieces = [(0, n * c_cat, c_cat, 0, n * width) for n in range(blocks)]
    pieces.append((1, 0, 9 * in_slow, 2, None))
    at = 0
    for n in range(blocks):
        pieces.append((2, at, in_slow, 1, n * width))
        at += in_slow
    for out, tall in ((3, c_cat), (4, 5 * c_fast)):
        pieces.append((2, at, tall, out, None))
        at += tall
    norm_rows = -(-gains.shape[0] // LANES)
    g_short, g_sout, gw_mid, gw_in, gw_lat, gains_grad, biases_grad, g_fin, g_fmid, g_fout, *held = unpack(
        sum_a, sum_bc, stream_b.ch, tuple(pieces),
        [(c_cat, c_slow), (in_slow, c_slow), (9 * in_slow, width), (c_cat, in_slow), wlat.shape],
        [(norm_rows, LANES), (norm_rows, LANES), (in_fast, c_fast), w_fast_mid.shape, (in_fast, c_fast)],
        [q4, q5, q6, q7, q8],
        [slow_gx, fast_gx, fast_y],
    )
    slow_gx, fast_gx, fast_y = held
    grads = (
        g_fin.T,
        g_fmid,
        g_fout,
        gw_lat.reshape(w_lateral.shape),
        gw_in,
        gw_mid.reshape(w_slow_mid.shape),
        g_sout,
        g_short,
    )
    return (
        unview(slow_y),
        unview(fast_y),
        unview(slow_gx),
        unview(fast_gx),
        *grads,
        gains_grad.reshape(-1)[: gains.shape[0]],
        biases_grad.reshape(-1)[: biases.shape[0]],
    )


def solution(mesh):
    frames = P(("path", "frames"), None, None, None)
    in_specs = (frames, frames, P(AXES), P(AXES), *([P()] * 10), frames, frames)
    out_specs = (*([frames] * 4), *([P()] * 10))
    return jax.shard_map(per_device, mesh=mesh, in_specs=in_specs, out_specs=out_specs, check_vma=False)
```

```python
import functools

import jax
import jax.numpy as jnp
from jax import lax
from jax.experimental import pallas as pl
from jax.experimental.pallas import tpu as pltpu
from jax.sharding import PartitionSpec as P

norm_eps = 1e-05
F32 = jnp.float32
BF16 = jnp.bfloat16
MESH = pl.DeviceIdType.MESH
AXES = ("path", "frames")
STEPS = 7
LANES = 128
VMEM_LIMIT = 60 * 1024 * 1024


def dot(a, b):
    return jnp.dot(a, b, preferred_element_type=F32)


def dot_nt(a, b):
    return lax.dot_general(a, b, (((1,), (1,)), ((), ())), preferred_element_type=F32)


def dot_tn(a, b):
    return lax.dot_general(a, b, (((0,), (0,)), ((), ())), preferred_element_type=F32)


def sig(v):
    return 0.5 * jnp.tanh(0.5 * v) + 0.5


def slope(v):
    s = sig(v)
    return s + (v * s) * (1.0 - s)


def rows(ref, slab, first, count):
    parts = [ref[slab, first + j : first + j + 1, :] for j in range(count)]
    return parts[0] if count == 1 else jnp.concatenate(parts, axis=1)


def put_rows(ref, first, value):
    for j in range(value.shape[1] // LANES):
        ref[first + j : first + j + 1, :] = value[:, j * LANES : (j + 1) * LANES]


def zero_ref(ref):
    ref[...] = jnp.zeros(ref.shape, ref.dtype)


def spread_add(step, z, mean_ref, m2_ref, cols=slice(None)):
    count = z.shape[0]
    mean = jnp.sum(z, axis=0) * (1.0 / count)
    d = z - mean
    m2 = jnp.sum(d * d, axis=0)
    first = step == 0
    old_mean = jnp.where(first, 0.0, mean_ref[:, cols])
    old_m2 = jnp.where(first, 0.0, m2_ref[:, cols])
    done = jnp.full((1, z.shape[-1]), step, jnp.int32).astype(F32)
    share = 1.0 / (done + 1.0)
    delta = mean - old_mean
    mean_ref[:, cols] = old_mean + delta * share
    m2_ref[:, cols] = old_m2 + m2 + delta * delta * (done * share * count)


def spread_end(mean_ref, m2_ref, fill, positions):
    filled = jnp.sum(fill, axis=0, keepdims=True)
    mean = jnp.sum(fill * mean_ref[...], axis=0, keepdims=True) / jnp.maximum(filled, 1.0)
    d = mean_ref[...] - mean
    m2 = jnp.sum(fill * (m2_ref[...] + positions * (d * d)), axis=0, keepdims=True)
    return mean, m2


def sum_add(step, value, ref, cols=slice(None)):
    ref[:, cols] = jnp.where(step == 0, 0.0, ref[:, cols]) + jnp.sum(value, axis=0)


def sum_end(ref):
    return jnp.sum(ref[...], axis=0, keepdims=True)


def pad8(n):
    return -(-n // 8) * 8


def exchange_peers(cfg):
    paths, length = lax.axis_size("path"), lax.axis_size("frames")
    near = 4
    g1, g2 = paths * near, length // near
    me_p, me_f = lax.axis_index("path"), lax.axis_index("frames")
    me = me_p * length + me_f
    total = paths * length
    r1 = me_p * near + lax.rem(me_f, near)
    r2 = lax.div(me_f, near)

    def peer1(k):
        r = lax.rem(r1 + k, g1)
        return (lax.div(r, near), r2 * near + lax.rem(r, near))

    def peer2(k):
        r = lax.rem(r2 + k, g2)
        return (me_p, r * near + lax.rem(me_f, near))

    def split(index):
        return (lax.div(index, length), lax.rem(index, length))

    nxt, prv = split(lax.rem(me + 1, total)), split(lax.rem(me + total - 1, total))
    return g1, g2, r1, r2, peer1, peer2, nxt, prv


def exchange_hello(cfg):
    g1, g2, _, _, peer1, peer2, nxt, prv = exchange_peers(cfg)
    peers = [peer1(k) for k in range(1, g1)] + [peer2(k) for k in range(1, g2)]
    if cfg.greets:
        peers += [nxt, prv]
    for peer in peers:
        pl.semaphore_signal(pltpu.get_barrier_semaphore(), inc=1, device_id=peer, device_id_type=MESH)
    return len(peers)


def exchange_run(cfg, ins, outs, scratch, meanwhile=None, post=None, after=None, between=None):
    fwd, bwd = cfg.fwd, cfg.bwd
    nf = sum(c[2] for c in fwd)
    nb = max((c[6] + c[4] for c in bwd), default=0)
    n_row = 2 * nf + nb
    stats_ref, up_ref, down_ref = scratch[:3]
    gb_ref, *coef_refs = ins
    outs = list(outs)
    coef_out = outs.pop(0) if nf else None
    pq_out = outs.pop(0) if nb else None
    from_prev = outs.pop(0) if cfg.up else None
    from_next = outs.pop(0) if cfg.down else None
    slots1, slots2, mid, tot, send1, recv1, send2, recv2, up_land, up_sems, down_land, down_sems = scratch[3:15]
    g1, g2, r1, r2, peer1, peer2, nxt, prv = exchange_peers(cfg)

    halos = []
    copies = []
    for k in range(1, g1):
        copies.append(
            pltpu.make_async_remote_copy(
                src_ref=stats_ref,
                dst_ref=slots1.at[r1],
                send_sem=send1.at[k],
                recv_sem=recv1.at[k],
                device_id=peer1(k),
                device_id_type=MESH,
            )
        )
        copies[-1].start()
    for used, src, land, sems, peer in (
        (cfg.up, up_ref, up_land, up_sems, nxt),
        (cfg.down, down_ref, down_land, down_sems, prv),
    ):
        if used:
            halos.append(
                pltpu.make_async_remote_copy(
                    src_ref=src,
                    dst_ref=land,
                    send_sem=sems.at[0],
                    recv_sem=sems.at[1],
                    device_id=peer,
                    device_id_type=MESH,
                )
            )
            halos[-1].start()
    slots1[r1] = stats_ref[...]
    if meanwhile is not None:
        meanwhile()
    for c in copies:
        c.wait_recv()

    def combine(slots, count, out):
        if nf:
            n = slots[0, n_row : n_row + 1, :]
            for g in range(1, count):
                n = n + slots[g, n_row : n_row + 1, :]
            acc = slots[0, n_row : n_row + 1, :] * slots[0, 0:nf, :]
            for g in range(1, count):
                acc = acc + slots[g, n_row : n_row + 1, :] * slots[g, 0:nf, :]
            mean = acc / jnp.maximum(n, 1.0)
            m2 = None
            for g in range(count):
                d = slots[g, 0:nf, :] - mean
                part = slots[g, nf : 2 * nf, :] + slots[g, n_row : n_row + 1, :] * (d * d)
                m2 = part if m2 is None else m2 + part
            out[0:nf, :] = mean
            out[nf : 2 * nf, :] = m2
            out[n_row : n_row + 1, :] = n
        if nb:
            acc = slots[0, 2 * nf : n_row, :]
            for g in range(1, count):
                acc = acc + slots[g, 2 * nf : n_row, :]
            out[2 * nf : n_row, :] = acc

    zero_ref(mid)
    combine(slots1, g1, mid)
    copies2 = []
    for k in range(1, g2):
        copies2.append(
            pltpu.make_async_remote_copy(
                src_ref=mid,
                dst_ref=slots2.at[r2],
                send_sem=send2.at[k],
                recv_sem=recv2.at[k],
                device_id=peer2(k),
                device_id_type=MESH,
            )
        )
        copies2[-1].start()
    slots2[r2] = mid[...]
    if between is not None:
        between()
    for c in copies2:
        c.wait_recv()
    combine(slots2, g2, tot)

    def lanes4(v):
        w = v + pltpu.roll(v, 64, 1)
        return w + pltpu.roll(w, 32, 1)

    at = 0
    for kind, g_row, count in fwd:
        n = tot[n_row : n_row + 1, :]
        mean = tot[at : at + count, :]
        m2 = tot[nf + at : nf + at + count, :]
        if kind == "lane4":
            whole = lanes4(mean) * 0.25
            d = mean - whole
            var = lanes4(m2 + n * (d * d)) / (4.0 * n)
            mean = whole
        elif kind == "row4":
            whole = jnp.sum(mean, axis=0, keepdims=True) * 0.25
            d = mean - whole
            var = jnp.sum(m2 + n * (d * d), axis=0, keepdims=True) / (4.0 * n)
            var = jnp.broadcast_to(var, (count, LANES))
            mean = jnp.broadcast_to(whole, (count, LANES))
        else:
            var = m2 / n
        inv = lax.rsqrt(var + norm_eps)
        scale = inv * gb_ref[0, g_row : g_row + count, :]
        coef_out[0, at : at + count, :] = scale
        coef_out[1, at : at + count, :] = gb_ref[1, g_row : g_row + count, :] - mean * scale
        coef_out[2, at : at + count, :] = inv
        coef_out[3, at : at + count, :] = mean * inv
        coef_out[4, at : at + count, :] = jnp.broadcast_to(n, (count, LANES))
        at += count
    at = 0
    for kind, coef, row, _, count, db_at, dg_at in bwd:
        db = tot[2 * nf + db_at : 2 * nf + db_at + count, :]
        dg = tot[2 * nf + dg_at : 2 * nf + dg_at + count, :]
        c = coef_refs[coef]
        scale, inv = c[0, row : row + count, :], c[2, row : row + count, :]
        mi, n = c[3, row : row + count, :], c[4, row : row + count, :]
        if kind == "lane4":
            db, dg, n = lanes4(db), lanes4(dg), 4.0 * n
        elif kind == "row4":
            db = jnp.broadcast_to(jnp.sum(db, axis=0, keepdims=True), (count, LANES))
            dg = jnp.broadcast_to(jnp.sum(dg, axis=0, keepdims=True), (count, LANES))
            n = 4.0 * n
        pq_out[0, at : at + count, :] = scale / n * (db - mi * dg)
        pq_out[1, at : at + count, :] = scale / n * inv * dg
        pq_out[2, at : at + count, :] = db
        pq_out[3, at : at + count, :] = dg
        at += count

    if cfg.post:
        post_sent, post_land, post_sems = scratch[15:]
        post(pq_out, post_sent)
        late = pltpu.make_async_remote_copy(
            src_ref=post_sent,
            dst_ref=post_land,
            send_sem=post_sems.at[0],
            recv_sem=post_sems.at[1],
            device_id=prv,
            device_id_type=MESH,
        )
        late.start()
        if after is not None:
            after()
        late.wait()
        outs.pop(0)[...] = post_land[...]
    for c in halos:
        c.wait()
    if cfg.up:
        from_prev[...] = up_land[...]
    if cfg.down:
        from_next[...] = down_land[...]
    for c in copies:
        c.wait_send()
    for c in copies2:
        c.wait_send()


class Exchange:
    def __init__(self, sizes, cid, rows_n, fwd=(), bwd=(), up=None, down=None, post=None):
        self.cid, self.fwd, self.bwd, self.up, self.down, self.post = cid, fwd, bwd, up, down, post
        self.greets = bool(up or down or post)
        g1, g2, r = sizes[0] * 4, sizes[1] // 4, pad8(rows_n)
        self.outs = []
        nf, nn = sum(c[2] for c in fwd), sum(c[4] for c in bwd)
        if nf:
            self.outs.append(((5, nf, LANES), F32))
        if nn:
            self.outs.append(((4, nn, LANES), F32))
        self.outs += [(h, F32) for h in (up, down) if h]
        if post:
            self.outs.append((post, BF16))
        none = (8, LANES)
        self.stats = (r, LANES)
        self.work = [
            pltpu.VMEM((g1, r, LANES), F32),
            pltpu.VMEM((g2, r, LANES), F32),
            pltpu.VMEM((r, LANES), F32),
            pltpu.VMEM((r, LANES), F32),
            pltpu.SemaphoreType.DMA((g1,)),
            pltpu.SemaphoreType.DMA((g1,)),
            pltpu.SemaphoreType.DMA((g2,)),
            pltpu.SemaphoreType.DMA((g2,)),
            pltpu.VMEM(up or none, F32),
            pltpu.SemaphoreType.DMA((2,)),
            pltpu.VMEM(down or none, F32),
            pltpu.SemaphoreType.DMA((2,)),
        ]
        if post:
            self.work += [pltpu.VMEM(post, BF16), pltpu.VMEM(post, BF16), pltpu.SemaphoreType.DMA((2,))]
        self.local = [pltpu.VMEM(self.stats, F32), pltpu.VMEM(up or none, F32), pltpu.VMEM(down or none, F32)]


STAT, UP, DOWN = "stat", "up", "down"


def call(kernel, ins, outs, scratch=(), name=None, ex=None, ex_ins=(), pre=None, pre_ins=()):
    real = [o for o in outs if not isinstance(o, str)]
    given = ins
    ins = [a for a in given if not isinstance(a, int)]
    extra_in = [whole(a) for a in (*ex_ins, *pre_ins)]
    extra_out = [out_whole(s, d) for s, d in ex.outs] if ex else []
    local = [*ex.local, *ex.work] if ex else []
    n_local = len(local)
    if pre:
        extra_out.append(out_whole(*pre.outs[0]))
        local += [*pre.work, *[pltpu.VMEM(shape, d) for shape, d in pre.outs[1:]]]
    all_in, all_out = [*ins, *extra_in], [*real, *extra_out]
    sizes = [len(ins), len(extra_in), len(real), len(extra_out), len(scratch), len(local)]
    ends = [sum(sizes[: k + 1]) for k in range(len(sizes))]

    def body(*refs):
        k_in, x_in, k_out, x_out, k_scr, x_scr = (refs[e - n : e] for e, n in zip(ends, sizes))
        if ex is None:
            kernel(*k_in, *k_out, *k_scr)
            return
        i = pl.program_id(0)

        p_ins, p_outs, p_scr = x_in[len(ex_ins) :], [], x_scr[n_local:]
        x_in, x_scr = x_in[: len(ex_ins)], x_scr[:n_local]
        if pre:
            n = len(pre.work)
            p_outs = [x_out[-1], *p_scr[n:]]
            x_out = x_out[:-1]

        @pl.when(i == 0)
        def _():
            exchange_hello(pre or ex)
            if pre:
                pl.semaphore_wait(pltpu.get_barrier_semaphore(), len_peers(pre))
                exchange_run(pre, p_ins[3:], p_outs, [*p_ins[:3], *p_scr[:n]])

        if pre:
            it_in = iter(k_in)
            views = [p_outs[0], *[o.at[pl.ds(i, 1)] for o in p_outs[1:]]]
            k_in = [views[a] if isinstance(a, int) else next(it_in) for a in given]
        named = {STAT: x_scr[0]}
        if ex.up:
            named[UP] = x_scr[1].at[pl.ds(i, 1)]
        if ex.down:
            named[DOWN] = x_scr[2].at[pl.ds(i, 1)]
        it = iter(k_out)
        late = kernel(*k_in, *[named[o] if isinstance(o, str) else next(it) for o in outs], *k_scr)

        @pl.when(i == STEPS - 1)
        def _():
            if not pre:
                pl.semaphore_wait(pltpu.get_barrier_semaphore(), len_peers(ex))
            exchange_run(ex, x_in, x_out, x_scr, late)

    params = {"collective_id": ex.cid, "has_side_effects": True} if ex else {}
    return pl.pallas_call(
        body,
        grid=(STEPS,),
        in_specs=[pl.BlockSpec(b, m) for _, b, m in all_in],
        out_specs=[pl.BlockSpec(b, m) for _, _, b, m in all_out],
        out_shape=[jax.ShapeDtypeStruct(s, d) for s, d, _, _ in all_out],
        scratch_shapes=[*scratch, *local],
        compiler_params=pltpu.CompilerParams(
            dimension_semantics=("arbitrary",), vmem_limit_bytes=VMEM_LIMIT, **params
        ),
        name=name,
    )(*[a for a, _, _ in all_in])


def len_peers(ex):
    paths, length = lax.axis_size("path"), lax.axis_size("frames")
    return paths * 4 - 1 + length // 4 - 1 + (2 if ex.greets else 0)


def whole(array):
    zeros = (0,) * array.ndim
    return (array, array.shape, lambda i: zeros)


def blocked(array, axis, size):
    block = array.shape[:axis] + (size,) + array.shape[axis + 1 :]
    return (array, block, lambda i: tuple(i if d == axis else 0 for d in range(array.ndim)))


def out_whole(shape, dtype):
    zeros = (0,) * len(shape)
    return (shape, dtype, shape, lambda i: zeros)


def out_blocked(shape, dtype, axis, size):
    block = shape[:axis] + (size,) + shape[axis + 1 :]
    return (shape, dtype, block, lambda i: tuple(i if d == axis else 0 for d in range(len(shape))))


def flat(value):
    return value.reshape(-1, value.shape[-1])


def spread_rows(ref, index, count, height):
    return [jnp.broadcast_to(ref[(*index, slice(p, p + 1))], (height, ref.shape[-1])) for p in range(count)]


def k_first(i, x_ref, tail_ref, m16_ref, m64_ref, wfa_ref, wlat_ref,
            fa_ref, lat_ref, taps_ref, st_ref, up_ref, down_ref, xs, fm, fv, lm, lv):
    x = x_ref[...]
    s_n, p_n, f_n, _ = x.shape
    packed = jnp.concatenate([flat(x[s]) for s in range(s_n)], axis=1)
    fa = dot_nt(packed, wfa_ref[...])
    fa_ref[...] = fa.reshape(fa_ref.shape)
    zero_ref(up_ref)
    zero_ref(down_ref)
    for p in range(p_n):
        down_ref[0, p : p + 1, :] = fa[p * f_n : p * f_n + 1, :]
        up_ref[0, p : p + 1, :] = fa[p * f_n + f_n - 1 : p * f_n + f_n, :]
    spread_add(i, fa.reshape(p_n, f_n, LANES), fm, fv)

    xs[...] = flat(x).astype(F32)
    n = xs.shape[0] // 4
    quarter = [xs[pl.ds(k, n, stride=4), :] for k in range(4)]
    t_n = f_n // 4
    first = lax.broadcasted_iota(jnp.int32, (n // t_n, t_n, LANES), 1) == 0
    link = m16_ref[1:2]
    tail = tail_ref[0].astype(F32)
    taps = []
    for k in range(2):
        halo = jnp.concatenate(
            [
                jnp.broadcast_to(tail[s * 8 + p : s * 8 + p + 1, k * LANES : (k + 1) * LANES], (t_n, LANES))
                for s in range(s_n)
                for p in range(p_n)
            ],
            axis=0,
        )
        moved = pltpu.roll(quarter[2 + k], 1, 0).reshape(n // t_n, t_n, LANES)
        taps.append(flat(jnp.where(first, halo.reshape(moved.shape), moved) * link))
    taps = jnp.concatenate([*taps, *quarter[:3]], axis=1).astype(BF16)
    taps_ref[...] = taps.reshape(taps_ref.shape)
    lat = dot(taps, wlat_ref[...])
    lat_ref[...] = lat.reshape(lat_ref.shape)
    spread_add(i, lat.reshape(n // t_n, t_n, lat.shape[1]), lm, lv)

    @pl.when(i == STEPS - 1)
    def _():
        zero_ref(st_ref)
        fill = m16_ref[0, :, 0:1]
        mean, m2 = spread_end(fm, fv, m64_ref[0, :, 0:1], STEPS * p_n)
        put_rows(st_ref, 0, mean)
        put_rows(st_ref, 3, m2)
        mean, m2 = spread_end(lm, lv, fill, STEPS * p_n * s_n)
        put_rows(st_ref, 1, mean)
        put_rows(st_ref, 4, m2)
        put_rows(st_ref, 6, count_row(m16_ref, STEPS * p_n * s_n))


def count_row(m16_ref, positions):
    return jnp.sum(m16_ref[0], axis=0, keepdims=True) * float(positions)


def shifted(value, first_rows, last_rows, f_n):
    n = value.shape[0]
    shape = (n // f_n, f_n, value.shape[1])
    place = lax.broadcasted_iota(jnp.int32, shape, 1)
    before = jnp.where(place == 0, first_rows, pltpu.roll(value, 1, 0).reshape(shape))
    after = jnp.where(place == f_n - 1, last_rows, pltpu.roll(value, n - 1, 0).reshape(shape))
    return before, after


def k_join(i, x_ref, lat_ref, fa_ref, hp_ref, hn_ref, c1_ref, m16_ref, m64_ref, win_ref, wsc_ref, wmid_ref,
           lact_ref, ftap_ref, sa_ref, sp_ref, fb_ref, st_ref, am, av, pm, pv, bm, bv, begun=False):
    s_n, p_n, t_n, c_slow = x_ref.shape
    c_lat = lat_ref.shape[-1]
    v = flat(lat_ref[...]) * rows(c1_ref, 0, 1, 2) + rows(c1_ref, 1, 1, 2)
    lact = (v * sig(v)).astype(BF16)
    lact_ref[...] = lact.reshape(lact_ref.shape)
    joined = None if begun else jnp.concatenate([flat(x_ref[...]), lact], axis=1)
    wide = c_lat
    for n in range(1 + wsc_ref.shape[1] // wide):
        cols = slice((n - 1) * wide, n * wide)
        if begun:
            z = flat(sa_ref[...] if n == 0 else sp_ref[:, :, :, cols])
            z = z + dot(lact, win_ref[c_slow:, :] if n == 0 else wsc_ref[c_slow:, cols])
        else:
            z = dot(joined, win_ref[...] if n == 0 else wsc_ref[:, cols])
        z4 = z.reshape(s_n, p_n, t_n, wide)
        z3 = z.reshape(s_n * p_n, t_n, wide)
        if n == 0:
            sa_ref[...] = z4
            spread_add(i, z3, am, av)
        else:
            sp_ref[:, :, :, cols] = z4
            spread_add(i, z3, pm, pv, cols)

    f_n = fa_ref.shape[1]
    scale, shift = rows(c1_ref, 0, 0, 1), rows(c1_ref, 1, 0, 1)

    def act(z):
        w = z * scale + shift
        return (w * sig(w)).astype(BF16).astype(F32)

    fact = act(flat(fa_ref[...]))
    ends = []
    for ref in (hp_ref, hn_ref):
        small = act(ref[0])
        ends.append(
            jnp.concatenate(
                [jnp.broadcast_to(small[p : p + 1, :], (f_n, LANES)) for p in range(p_n)], axis=0
            ).reshape(p_n, f_n, LANES)
        )
    before, after = shifted(fact, ends[0], ends[1], f_n)
    ftap = jnp.concatenate(
        [flat(before * m64_ref[1:2]), fact, flat(after * m64_ref[2:3])], axis=1
    ).astype(BF16)
    ftap_ref[...] = ftap.reshape(ftap_ref.shape)
    fb = dot(ftap, wmid_ref[...])
    fb_ref[...] = fb.reshape(fb_ref.shape)
    spread_add(i, fb.reshape(p_n, f_n, LANES), bm, bv)

    @pl.when(i == STEPS - 1)
    def _():
        zero_ref(st_ref)
        fill = m16_ref[0, :, 0:1]
        positions = STEPS * p_n * s_n
        mean, m2 = spread_end(bm, bv, m64_ref[0, :, 0:1], STEPS * p_n)
        put_rows(st_ref, 0, mean)
        put_rows(st_ref, 11, m2)
        mean, m2 = spread_end(am, av, fill, positions)
        put_rows(st_ref, 1, mean)
        put_rows(st_ref, 12, m2)
        mean, m2 = spread_end(pm, pv, fill, positions)
        put_rows(st_ref, 3, mean)
        put_rows(st_ref, 14, m2)
        put_rows(st_ref, 22, count_row(m16_ref, positions))


def k_spatial(i, sa_ref, fb_ref, c2_ref, m16_ref, m64_ref, wsp_ref, wout_ref,
              pad_ref, sb_ref, fact_ref, st_ref, sm, sv, cm, cv):
    h_n, w_n, t_n, c = sa_ref.shape

    @pl.when(i == 0)
    def _():
        scale, shift = rows(c2_ref, 0, 1, 2), rows(c2_ref, 1, 1, 2)
        zero_ref(pad_ref)

        @pl.loop(0, h_n)
        def _(h):
            v = flat(sa_ref[h]) * scale + shift
            pad_ref[h + 1, 1 : w_n + 1] = (v * sig(v)).astype(BF16).reshape(w_n, t_n, c)

    per = h_n // STEPS
    h0 = i * per
    patches = [flat(pad_ref[pl.ds(h0 + a, per), b : b + w_n]) for a in range(3) for b in range(3)]
    acc = dot(jnp.concatenate(patches, axis=1), wsp_ref[...])
    sb_ref[...] = acc.reshape(sb_ref.shape)
    spread_add(i, acc.reshape(per * w_n, t_n, acc.shape[1]), sm, sv)

    p_n, f_n, _ = fb_ref.shape
    v = flat(fb_ref[...]) * rows(c2_ref, 0, 0, 1) + rows(c2_ref, 1, 0, 1)
    fact = (v * sig(v)).astype(BF16)
    fact_ref[...] = fact.reshape(fact_ref.shape)
    fc = dot(fact, wout_ref[...])
    spread_add(i, fc.reshape(p_n, f_n, fc.shape[1]), cm, cv)

    @pl.when(i == STEPS - 1)
    def _():
        zero_ref(st_ref)
        mean, m2 = spread_end(cm, cv, m64_ref[0, :, 0:1], STEPS * p_n)
        put_rows(st_ref, 0, mean)
        put_rows(st_ref, 6, m2)
        mean, m2 = spread_end(sm, sv, m16_ref[0, :, 0:1], h_n * w_n)
        put_rows(st_ref, 4, mean)
        put_rows(st_ref, 10, m2)
        put_rows(st_ref, 12, count_row(m16_ref, h_n * w_n))


def k_expand(i, sb_ref, fact_ref, x_ref, cot_ref, c3_ref, m16_ref, m64_ref, wso_ref, wout_ref,
             sact_ref, fout_ref, df_ref, st_ref, cm, cv, s1, s2):
    s_n, p_n, t_n = x_ref.shape[0], fact_ref.shape[0], sb_ref.shape[-2]
    v = flat(sb_ref[...]) * rows(c3_ref, 0, 4, 2) + rows(c3_ref, 1, 4, 2)
    sact = (v * sig(v)).astype(BF16)
    sact_ref[...] = sact.reshape(sact_ref.shape)
    wide = 256
    for n in range(wso_ref.shape[1] // wide):
        cols = slice(n * wide, (n + 1) * wide)
        z = dot(sact, wso_ref[:, cols])
        spread_add(i, z.reshape(s_n * p_n, t_n, wide), cm, cv, cols)

    f_n = fact_ref.shape[1]
    fc = dot(flat(fact_ref[...]), wout_ref[...])
    fill = m64_ref[0:1]
    for s in range(s_n):
        cols = slice(s * LANES, (s + 1) * LANES)
        z = fc[:, cols].reshape(p_n, f_n, LANES)
        unit = z * rows(c3_ref, 2, s, 1) - rows(c3_ref, 3, s, 1)
        pre = z * rows(c3_ref, 0, s, 1) + rows(c3_ref, 1, s, 1) + x_ref[s].astype(F32)
        g = sig(pre)
        y = pre * g
        fout_ref[s] = (y * fill).astype(BF16)
        d = cot_ref[s].astype(F32) * fill * (g + y * (1.0 - g))
        df_ref[:, :, cols] = d
        sum_add(i, d, s1, cols)
        sum_add(i, d * unit, s2, cols)

    @pl.when(i == STEPS - 1)
    def _():
        zero_ref(st_ref)
        positions = STEPS * p_n * s_n
        mean, m2 = spread_end(cm, cv, m16_ref[0, :, 0:1], positions)
        put_rows(st_ref, 0, mean)
        put_rows(st_ref, 8, m2)
        put_rows(st_ref, 16, sum_end(s1))
        put_rows(st_ref, 20, sum_end(s2))
        put_rows(st_ref, 24, count_row(m16_ref, positions))


def run_resident(kernel, ex_list, hbm, small, locals_, outs, scratch, name, scalars=0):
    vm, anywhere = pl.BlockSpec(memory_space=pltpu.VMEM), pl.BlockSpec(memory_space=pl.ANY)
    for ex in ex_list:
        outs = [*outs, *[(shape, dtype, False) for shape, dtype in ex.outs]]
    work = [w for ex in ex_list for w in (*ex.local, *ex.work)]
    sizes = [len(hbm), len(small), len(outs), len(hbm), len(locals_), len(scratch), 1]
    ends = [sum(sizes[: k + 1]) for k in range(len(sizes))]

    def body(*refs):
        h, sm, o, loaded, kept, scr, (sems,) = (refs[e - n : e] for e, n in zip(ends, sizes))
        rest, at = [], ends[-1]
        for ex in ex_list:
            n = len(ex.local) + len(ex.work)
            rest.append(refs[at : at + n])
            at += n
        loads = [pltpu.make_async_copy(a, b, sems.at[k]) for k, (a, b) in enumerate(zip(h, loaded))]
        greeter = max(ex_list, key=lambda ex: ex.greets)
        count = exchange_hello(greeter)
        for load in loads:
            load.start()
        kernel(loads, lambda: pl.semaphore_wait(pltpu.get_barrier_semaphore(), count), loaded, sm, kept, scr, o, rest)

    return pl.pallas_call(
        body,
        out_shape=[jax.ShapeDtypeStruct(shape, dtype) for shape, dtype, _ in outs],
        in_specs=[anywhere] * len(hbm) + [pl.BlockSpec(memory_space=pltpu.SMEM)] * scalars + [vm] * (len(small) - scalars),
        out_specs=[anywhere if stays else vm for _, _, stays in outs],
        scratch_shapes=[
            *[pltpu.VMEM(a.shape, a.dtype) for a in hbm], *[pltpu.VMEM(*k) for k in locals_], *scratch,
            pltpu.SemaphoreType.DMA((len(hbm),)), *work,
        ],
        compiler_params=pltpu.CompilerParams(
            collective_id=ex_list[0].cid, has_side_effects=True, vmem_limit_bytes=VMEM_LIMIT
        ),
        name=name,
    )(*hbm, *small)


def stores_of(pairs, sems):
    return [pltpu.make_async_copy(a, b, sems.at[k]) for k, (a, b) in enumerate(pairs)]


def k_front(exs, loads, met, loaded, small, kept, scratch, outs, work):
    x_fast, wlat, x_slow, w_in, w_sc = loaded
    fa, lat, taps, lact, ftap, sa, sp, fb = kept
    xs, fm, fv, lm, lv, am, av, pm, pv, bm, bv, sems, sp_sems, ends_f, sent, sent_low, tail_ref, tail_sems = scratch
    big, ready, (c1, hp, hn, c2) = outs[:8], outs[8:15], outs[15:]
    gb, m16, m64, wfa, wmid, wback, wout = ready
    p_n = fa.shape[0] // STEPS
    copies = dict(zip((0, 1, 2, 3, 4, 5, 7), stores_of([p for k, p in enumerate(zip(kept, big)) if k != 6], sems)))
    st1, up, down = work[0][:3]
    loads[0].wait()
    s_n, inner, f_n, ch = x_fast.shape
    t_n = lat.shape[2]
    ends_f[...] = flat(x_fast[:, :, f_n - t_n : f_n, :]).astype(F32)
    zero_ref(sent)
    for k in range(2):
        lines = ends_f[pl.ds(t_n - 2 + k, s_n * inner, stride=t_n), :]
        for s in range(s_n):
            for step in range(STEPS):
                at = s * inner + step * p_n
                sent[step, s * 8 : s * 8 + p_n, k * ch : (k + 1) * ch] = lines[at : at + p_n, :]
    sent_low[...] = sent[...].astype(BF16)
    met()
    nxt = exchange_peers(exs[0])[6]
    halo = pltpu.make_async_remote_copy(
        src_ref=sent_low, dst_ref=tail_ref, send_sem=tail_sems.at[0], recv_sem=tail_sems.at[1],
        device_id=nxt, device_id_type=MESH,
    )
    halo.start()
    small_set_up(*small, *ready, s_n, t_n)
    loads[1].wait()
    halo.wait()

    def first(i):
        part, one = pl.ds(i * p_n, p_n), pl.ds(i, 1)
        k_first(i, x_fast.at[:, part], tail_ref.at[one], m16, m64, wfa, wlat, fa.at[part], lat.at[:, part],
                taps.at[:, part], st1, up.at[one], down.at[one], xs, fm, fv, lm, lv)

    each(0, STEPS, first)
    for k in (0, 1, 2):
        copies[k].start()
    c_slow = x_slow.shape[-1]

    def begin(i):
        part = pl.ds(i * p_n, p_n)
        xs_part = flat(x_slow[:, part])
        wide = sa.shape[-1]
        sa[:, part] = dot(xs_part, w_in[0:c_slow, :]).reshape(s_n, p_n, t_n, wide)
        for n in range(sp.shape[-1] // wide):
            cols = slice(n * wide, (n + 1) * wide)
            sp[:, part, :, cols] = dot(xs_part, w_sc[0:c_slow, cols]).reshape(s_n, p_n, t_n, wide)

    def begin_some():
        for k in (2, 3, 4):
            loads[k].wait()
        each(0, 2, begin)

    exchange_run(exs[0], [gb], [c1, hp, hn], work[0], begin_some, between=lambda: each(2, 5, begin))

    def store_sp(i):
        part = pl.ds(i * p_n, p_n)
        return pltpu.make_async_copy(sp.at[:, part], big[6].at[:, part], sp_sems.at[i])

    def join(i, begun=False):
        part, one = pl.ds(i * p_n, p_n), pl.ds(i, 1)
        k_join(i, x_slow.at[:, part], lat.at[:, part], fa.at[part], hp.at[one], hn.at[one], c1, m16, m64, w_in, w_sc, wmid,
               lact.at[:, part], ftap.at[part], sa.at[:, part], sp.at[:, part], fb.at[part], work[1][0],
               am, av, pm, pv, bm, bv, begun)
        store_sp(i).start()

    each(0, 5, lambda i: join(i, True))
    each(5, STEPS, join)
    for k in (3, 4, 5, 7):
        copies[k].start()
    exchange_run(exs[1], [gb], [c2], work[1])
    each(0, STEPS, lambda i: store_sp(i).wait())
    for k in (0, 1, 2, 3, 4, 5, 7):
        copies[k].wait()


def k_middle(exs, loads, met, loaded, small, kept, scratch, outs, work):
    sa, fb, wsp, wso, x_fast, cot = loaded
    gb, c2, m16, m64, wout = small
    pad, sb, fact, sact, fast_y, df = kept
    sm, sv, cm, cv, em, ev, s1, s2, sems, y_sems, df_sems = scratch
    big, (c3, c4, q4) = outs[:6], outs[6:]
    p_n = fb.shape[0] // STEPS
    rows_n = sb.shape[0] // STEPS
    copies = stores_of(list(zip(kept, big))[:4], sems)
    for k in (0, 1, 2):
        loads[k].wait()

    def spatial(i):
        part, span = pl.ds(i * p_n, p_n), pl.ds(i * rows_n, rows_n)
        k_spatial(i, sa, fb.at[part], c2, m16, m64, wsp, wout, pad, sb.at[span], fact.at[part], work[0][0], sm, sv, cm, cv)

    each(0, STEPS, spatial)
    met()
    for k in (0, 1, 2):
        copies[k].start()
    exchange_run(exs[0], [gb], [c3], work[0])
    for k in (3, 4, 5):
        loads[k].wait()

    def y_store(i):
        part = pl.ds(i * p_n, p_n)
        return pltpu.make_async_copy(fast_y.at[:, part], big[4].at[:, part], y_sems.at[i])

    def df_store(i):
        part = pl.ds(i * p_n, p_n)
        return pltpu.make_async_copy(df.at[part], big[5].at[part], df_sems.at[i])

    def expand(i):
        part, span = pl.ds(i * p_n, p_n), pl.ds(i * rows_n, rows_n)
        k_expand(i, sb.at[span], fact.at[part], x_fast.at[:, part], cot.at[:, part], c3, m16, m64, wso, wout,
                 sact.at[span], fast_y.at[:, part], df.at[part], work[1][0], em, ev, s1, s2)
        y_store(i).start()
        df_store(i).start()

    each(0, STEPS, expand)
    copies[3].start()
    exchange_run(exs[1], [gb, c3], [c4, q4], work[1])
    each(0, STEPS, lambda i: y_store(i).wait())
    each(0, STEPS, lambda i: df_store(i).wait())
    for copy in copies:
        copy.wait()


def back_norm(scale, p, q, dy, z, fill):
    return scale * dy - fill * (p + z * q)


def k_out(sact_ref, sp_ref, cot_ref, df_ref, fact_ref, fb_ref, c2_ref, c3_ref, c4_ref, q4_ref,
          m16_ref, m64_ref, wso_ref, wout_ref,
          out_ref, dy_ref, dfb_ref, gout_ref, up_ref, down_ref, st_ref, s1, s2, s3, t1, t2, gout):
    i = pl.program_id(0)
    s_n, p_n, t_n, _ = sact_ref.shape
    sact = flat(sact_ref[...])
    fill = m16_ref[0:1, :, 0:1]
    wide = 256
    for n in range(wso_ref.shape[1] // wide):
        cols = slice(n * wide, (n + 1) * wide)
        shape = (s_n * p_n, t_n, wide)
        sc = dot(sact, wso_ref[:, cols]).reshape(shape)
        sp = sp_ref[:, :, :, cols].reshape(shape)
        u6 = sc * rows(c4_ref, 2, 2 * n, 2) - rows(c4_ref, 3, 2 * n, 2)
        u7 = sp * rows(c2_ref, 2, 3 + 2 * n, 2) - rows(c2_ref, 3, 3 + 2 * n, 2)
        pre = (
            sc * rows(c4_ref, 0, 2 * n, 2)
            + sp * rows(c2_ref, 0, 3 + 2 * n, 2)
            + (rows(c4_ref, 1, 2 * n, 2) + rows(c2_ref, 1, 3 + 2 * n, 2))
        )
        g = sig(pre)
        y = pre * g
        out_ref[:, :, :, cols] = (y * fill).astype(BF16).reshape(s_n, p_n, t_n, wide)
        d = cot_ref[:, :, :, cols].reshape(shape).astype(F32) * fill * (g + y * (1.0 - g))
        dy_ref[:, :, :, cols] = d.reshape(s_n, p_n, t_n, wide)
        sum_add(i, d, s1, cols)
        sum_add(i, d * u6, s2, cols)
        sum_add(i, d * u7, s3, cols)

    f_n = fact_ref.shape[1]
    fact = flat(fact_ref[...])
    fc = dot(fact, wout_ref[...])
    fill4 = m64_ref[0:1]
    parts = []
    for s in range(s_n):
        cols = slice(s * LANES, (s + 1) * LANES)
        d = back_norm(
            rows(c3_ref, 0, s, 1), rows(q4_ref, 0, s, 1), rows(q4_ref, 1, s, 1),
            df_ref[:, :, cols], fc[:, cols].reshape(p_n, f_n, LANES), fill4,
        )
        parts.append(flat(d).astype(BF16))
    dfc = jnp.concatenate(parts, axis=1)
    add_to(i, gout, dot_tn(fact, dfc))
    z = fb_ref[...]
    back = dot_nt(dfc, wout_ref[...]).reshape(p_n, f_n, LANES) * slope(
        z * rows(c2_ref, 0, 0, 1) + rows(c2_ref, 1, 0, 1)
    )
    dfb_ref[...] = back
    sum_add(i, back, t1)
    sum_add(i, back * (z * rows(c2_ref, 2, 0, 1) - rows(c2_ref, 3, 0, 1)), t2)
    for k, value in enumerate((back, z)):
        value = flat(value)
        for p in range(p_n):
            down_ref[0, k, p : p + 1, :] = value[p * f_n : p * f_n + 1, :]
            up_ref[0, k, p : p + 1, :] = value[p * f_n + f_n - 1 : p * f_n + f_n, :]
        down_ref[0, k, p_n : p_n + 1, :] = m64_ref[0, 0:1, :]
        up_ref[0, k, p_n : p_n + 1, :] = m64_ref[0, f_n - 1 : f_n, :]

    @pl.when(i == STEPS - 1)
    def _():
        zero_ref(st_ref)
        put_rows(st_ref, 0, sum_end(s1))
        put_rows(st_ref, 8, sum_end(s2))
        put_rows(st_ref, 16, sum_end(s3))
        put_rows(st_ref, 24, sum_end(t1))
        put_rows(st_ref, 25, sum_end(t2))
        gout_ref[...] = fold_wide(gout, s_n)


def add_to(step, ref, value):
    ref[...] = jnp.where(step == 0, 0.0, ref[...]) + value


def fold_wide(ref, count):
    a = ref.shape[0] // count
    return sum(ref[s * a : (s + 1) * a, s * LANES : (s + 1) * LANES] for s in range(count))


def fold_lanes(value, count):
    a = value.shape[0] // count
    parts = [value[s * a : (s + 1) * a, :] for s in range(count)]
    return sum(p if s == 0 else pltpu.roll(p, LANES - s * a, 1) for s, p in enumerate(parts))


def k_back_out(x_ref, lact_ref, dy_ref, sp_ref, sact_ref, sb_ref, dfb_ref, fb_ref, fa_ref, ftap_ref, hp_ref, hn_ref,
               c1_ref, c2_ref, c3_ref, c4_ref, q5_ref, m16_ref, m64_ref, wso_ref, wback_ref,
               gw_ref, gs_ref, dsp_ref, dsb_ref, dfa_ref, gmid_ref, st_ref, s1, s2, t1, t2, gsc, gso, gmid):
    i = pl.program_id(0)
    s_n, p_n, t_n, c = sb_ref.shape
    sact = flat(sact_ref[...])
    fill = m16_ref[0:1, :, 0:1]
    wide = 256
    dscs = []
    turned = jnp.concatenate([flat(x_ref[...]), flat(lact_ref[...])], axis=1).T
    sact_turned = sact.T
    for n in range(wso_ref.shape[1] // wide):
        cols = slice(n * wide, (n + 1) * wide)
        shape = (s_n * p_n, t_n, wide)
        d = dy_ref[:, :, :, cols].reshape(shape)
        sc = dot(sact, wso_ref[:, cols]).reshape(shape)
        dsc = back_norm(rows(c4_ref, 0, 2 * n, 2), rows(q5_ref, 0, 2 * n, 2), rows(q5_ref, 1, 2 * n, 2), d, sc, fill)
        dsc = flat(dsc.astype(BF16))
        old = jnp.where(i == 0, 0.0, gso[:, cols])
        gso[:, cols] = old + dot(sact_turned, dsc)
        sp = sp_ref[:, :, :, cols].reshape(shape)
        dsp = back_norm(
            rows(c2_ref, 0, 3 + 2 * n, 2), rows(q5_ref, 0, 8 + 2 * n, 2), rows(q5_ref, 1, 8 + 2 * n, 2), d, sp, fill
        )
        dsp = flat(dsp.astype(BF16))
        dsp_ref[:, :, :, cols] = dsp.reshape(s_n, p_n, t_n, wide)
        old = jnp.where(i == 0, 0.0, gsc[:, cols])
        gsc[:, cols] = old + dot(turned, dsp)
        dscs.append(dsc)
    z = sb_ref[...].reshape(s_n * p_n, t_n, c)
    back = dot_nt(jnp.concatenate(dscs, axis=1), wso_ref[...])
    back = back.reshape(z.shape) * slope(z * rows(c3_ref, 0, 4, 2) + rows(c3_ref, 1, 4, 2))
    dsb_ref[...] = back.reshape(dsb_ref.shape)
    sum_add(i, back, s1)
    sum_add(i, back * (z * rows(c3_ref, 2, 4, 2) - rows(c3_ref, 3, 4, 2)), s2)

    f_n = fb_ref.shape[1]
    scale, p_row, q_row = rows(c2_ref, 0, 0, 1), rows(q5_ref, 0, 16, 1), rows(q5_ref, 1, 16, 1)
    dfb = back_norm(scale, p_row, q_row, dfb_ref[...], fb_ref[...], m64_ref[0:1])
    dfb_low = flat(dfb).astype(BF16)
    add_to(i, gmid, dot_tn(dfb_low, flat(ftap_ref[...])))
    own = dfb_low.astype(F32)
    ends = []
    for ref in (hp_ref, hn_ref):
        small = back_norm(scale, p_row, q_row, ref[0, 0], ref[0, 1], ref[0, 0, p_n : p_n + 1, :])
        small = small.astype(BF16).astype(F32)
        ends.append(
            jnp.concatenate(
                [jnp.broadcast_to(small[p : p + 1, :], (f_n, LANES)) for p in range(p_n)], axis=0
            ).reshape(p_n, f_n, LANES)
        )
    before, after = shifted(own, ends[0], ends[1], f_n)
    taps = jnp.concatenate(
        [flat(after * m64_ref[2:3]), own, flat(before * m64_ref[1:2])], axis=1
    ).astype(BF16)
    z = fa_ref[...]
    back = dot(taps, wback_ref[...]).reshape(z.shape) * slope(
        z * rows(c1_ref, 0, 0, 1) + rows(c1_ref, 1, 0, 1)
    )
    dfa_ref[...] = back
    sum_add(i, back, t1)
    sum_add(i, back * (z * rows(c1_ref, 2, 0, 1) - rows(c1_ref, 3, 0, 1)), t2)

    @pl.when(i == STEPS - 1)
    def _():
        zero_ref(st_ref)
        put_rows(st_ref, 0, sum_end(s1))
        put_rows(st_ref, 2, sum_end(s2))
        put_rows(st_ref, 4, sum_end(t1))
        put_rows(st_ref, 5, sum_end(t2))

    def late():
        for k in range(3):
            gmid_ref[k * 32 : (k + 1) * 32, :] = fold_lanes(gmid[:, k * LANES : (k + 1) * LANES], s_n)
        tall, low_tall = gsc.shape[0], gso.shape[0]
        blocks = gsc.shape[1] // wide
        for n in range(blocks):
            cols = slice(n * wide, (n + 1) * wide)
            gw_ref[n * tall : (n + 1) * tall, :] = gsc[:, cols].astype(BF16)
            gs_ref[n * low_tall : (n + 1) * low_tall, :] = gso[:, cols].astype(BF16)
        if blocks * tall < gw_ref.shape[0]:
            gw_ref[blocks * tall :, :] = jnp.zeros((gw_ref.shape[0] - blocks * tall, wide), BF16)

    return late


def slow_grad(low, dsp, w_in, w_sc, out):
    s_n, p_n, t_n, c = low.shape
    small, d_sp = flat(low[...]), flat(dsp[...])
    for n in range(out.shape[-1] // c):
        part = slice(n * c, (n + 1) * c)
        d = dot_nt(d_sp, w_sc[part, :]) + dot_nt(small, w_in[part, :])
        out[:, :, :, part] = d.astype(BF16).reshape(s_n, p_n, t_n, c)


def fast_grad(low_ref, hn, df, dlow, m16, wlat, wfa, out, gs):
    s_n, p_n, t_n, c = low_ref.shape
    shape = (s_n * p_n, t_n, c)
    low = flat(low_ref[...])
    small = hn[0].astype(F32)
    ends = [
        jnp.broadcast_to(small[s * 8 + p : s * 8 + p + 1, :], (t_n, c)) for s in range(s_n) for p in range(p_n)
    ]
    ends = jnp.concatenate(ends, axis=0).reshape(shape)
    n = low.shape[0]
    moved = pltpu.roll(low.astype(F32), n - 1, 0).reshape(shape)
    place = lax.broadcasted_iota(jnp.int32, shape, 1)
    following = flat(jnp.where(place == t_n - 1, ends, moved) * m16[2:3, :, 0:1]).astype(BF16)
    own = dot_nt(low, wlat[2 * LANES : 5 * LANES, :])
    late = dot_nt(following, wlat[0 : 2 * LANES, :])
    gs[pl.ds(0, n, stride=4), :] = own[:, 0:LANES]
    gs[pl.ds(1, n, stride=4), :] = own[:, LANES : 2 * LANES]
    gs[pl.ds(2, n, stride=4), :] = own[:, 2 * LANES :] + late[:, 0:LANES]
    gs[pl.ds(3, n, stride=4), :] = late[:, LANES:]
    back = dot(flat(dlow[...]), wfa[...])
    for s in range(s_n):
        cols = slice(s * LANES, (s + 1) * LANES)
        total = flat(df[:, :, cols]) + back[:, cols] + gs[s * n : (s + 1) * n, :]
        out[s] = total.astype(BF16).reshape(out.shape[1:])


def each(first, last, body):
    def step(k, carry):
        body(k)
        return carry
    lax.fori_loop(first, last, step, 0)


NEAR = 4


class Cube:
    def __init__(self, ch, far):
        self.ch, self.far = ch, far
        self.p, self.f = lax.axis_index("path"), lax.axis_index("frames")
        self.q, self.r = lax.rem(self.f, NEAR), lax.div(self.f, NEAR)
        self.sibling = (1 - self.p, self.f)

    def q_of(self, k):
        low = (self.q % 2 + k % 2) % 2
        return (self.q // 2 + k // 2) % 2 * 2 + low

    def r_of(self, k):
        return lax.rem(self.r + k, self.far)

    def plane(self, k):
        return (self.p, self.r * NEAR + self.q_of(k))

    def line(self, k):
        return (self.p, self.r_of(k) * NEAR + self.q)

    def at(self, path, q, r):
        return pl.ds(pl.multiple_of(((path * NEAR + q) * self.far + r) * self.ch, 16), self.ch)


def remote(src, dst, sem, index, device):
    return pltpu.make_async_remote_copy(
        src_ref=src, dst_ref=dst, send_sem=sem.at[(0, *index)], recv_sem=sem.at[(1, *index)],
        device_id=device, device_id_type=MESH)


def rows_for(sizes, n):
    unit = 16 * sizes[0] * sizes[1]
    return -(-n // unit) * unit


class Stream:
    def __init__(self, sizes, rows_n, width):
        self.sizes, self.rows_n, self.width = sizes, rows_n, width
        self.far = sizes[1] // NEAR
        self.ch = rows_n // (sizes[0] * sizes[1])
        self.chunk = (self.ch, width)
        self.near_shape = (self.far, *self.chunk)
        quad = pltpu.VMEM((NEAR, *self.near_shape), BF16)
        quad_sems, line_sems = pltpu.SemaphoreType.DMA((2, NEAR, self.far)), pltpu.SemaphoreType.DMA((2, self.far))
        self.near_scratch = [quad, quad, quad, pltpu.VMEM(self.chunk, F32), quad_sems, quad_sems]
        self.line_scratch = [pltpu.VMEM(self.near_shape, BF16), pltpu.VMEM(self.chunk, F32), line_sems]
        self.share_scratch = [line_sems, quad_sems, quad_sems, pltpu.SemaphoreType.DMA]


class Near:
    def __init__(self, stream, x, out, scratch):
        self.x, self.out, self.far, self.c = x, out, stream.far, Cube(stream.ch, stream.far)
        self.land_a, self.buf_b, self.land_b, self.acc, self.sem_a, self.sem_b = scratch

    def pair(self, k, m):
        c = self.c
        return remote(self.x.at[c.at(1 - c.p, c.q_of(k), c.r_of(m + 1))], self.land_a.at[k, m], self.sem_a, (k, m), c.sibling)

    def plane(self, k, m):
        return remote(self.buf_b.at[k, m], self.land_b.at[k, m], self.sem_b, (k, m), self.c.plane(k))

    def start(self):
        def one(m):
            each(1, NEAR, lambda k: self.pair(k, m).start())
            self.pair(0, m).start()

        each(0, self.far, one)

    def add_pair(self, first, last):
        c = self.c

        def one(k, m):
            self.pair(k, m).wait_recv()
            mine = self.x[c.at(c.p, c.q_of(k), c.r_of(m + 1)), :]
            self.buf_b[k, m] = (mine.astype(F32) + self.land_a[k, m].astype(F32)).astype(BF16)
            self.plane(k, m).start()

        each(first, last, lambda m: each(1, NEAR, lambda k: one(k, m)))

    def add_plane(self, first, last, then=None):
        c = self.c

        def one(m):
            self.pair(0, m).wait_recv()
            self.acc[...] = self.x[c.at(c.p, c.q, c.r_of(m + 1)), :].astype(F32) + self.land_a[0, m].astype(F32)

            def more(k):
                self.plane(k, m).wait_recv()
                self.acc[...] += self.land_b[k, m].astype(F32)

            each(1, NEAR, more)
            self.out[m] = self.acc[...].astype(BF16)
            if then is not None:
                then(m)

        each(first, last, one)

    def end(self):
        each(0, self.far, lambda m: each(0, NEAR, lambda k: self.pair(k, m).wait_send()))
        each(0, self.far, lambda m: each(1, NEAR, lambda k: self.plane(k, m).wait_send()))


class Line:
    def __init__(self, stream, near, scratch):
        self.near, self.far, self.c = near, stream.far, Cube(stream.ch, stream.far)
        self.land, self.acc, self.sem = scratch

    def line(self, m):
        return remote(self.near.at[m], self.land.at[m], self.sem, (m,), self.c.line(m + 1))

    def start(self, first, last):
        each(first, min(last, self.far - 1), lambda m: self.line(m).start())

    def total(self):
        self.acc[...] = self.near[self.far - 1].astype(F32)

        def one(m):
            self.line(m).wait_recv()
            self.acc[...] += self.land[m].astype(F32)

        each(0, self.far - 1, one)
        return self.acc[...].astype(BF16)

    def end(self):
        each(0, self.far - 1, lambda m: self.line(m).wait_send())


class Share:
    def __init__(self, stream, res, out, scratch):
        self.res, self.out, self.far, self.c = res, out, stream.far, Cube(stream.ch, stream.far)
        self.cut = stream.ch // 32 * 16
        self.sem_d, self.sem_e, self.sem_f, self.sem_own = scratch

    def own(self):
        return self.out.at[self.c.at(self.c.p, self.c.q, self.c.r)]

    def keep(self):
        return pltpu.make_async_copy(self.res, self.own(), self.sem_own)

    def line_back(self, k):
        return remote(self.res, self.own(), self.sem_d, (k,), self.c.line(k))

    def part(self, q, m):
        return self.out.at[self.c.at(self.c.p, q, self.c.r_of(self.far - m))]

    def plane_back(self, k, m, src=None):
        dst = self.part(self.c.q, m)
        return remote(dst if src is None else src, dst, self.sem_e, (k, m), self.c.plane(k))

    def pair_back(self, k, m, src=None):
        dst = self.part(self.c.q_of(k), m)
        return remote(dst if src is None else src, dst, self.sem_f, (k, m), self.c.sibling)

    def start_line(self):
        each(1, self.far, lambda k: self.line_back(k).start())

    def half(self, k, m):
        c, cut = self.c, self.cut
        start = ((c.p * NEAR + c.q_of(k)) * self.far + c.r_of(self.far - m)) * c.ch
        rows_n = cut if k == 1 else c.ch - cut
        part = self.out.at[pl.ds(pl.multiple_of(start + (0 if k == 1 else cut), 16), rows_n)]
        return remote(part, part, self.sem_e, (3 if k == 1 else 0, m), c.plane(3 - k))

    def start_plane(self):
        each(1, NEAR - 1, lambda k: self.plane_back(k, 0, self.res).start())
        self.pair_back(0, 0, self.res).start()
        self.keep().start()

    def relay(self, first, last):
        def one(m):
            self.line_back(m).wait_recv()
            each(1, NEAR - 1, lambda k: self.plane_back(k, m).start())
            self.pair_back(0, m).start()

        each(first, last, one)

    def hand_on(self, first, last):
        def one(m):
            for k in (1, 2):
                self.plane_back(k, m).wait_recv()
                self.half(k, m).start()
                self.pair_back(k, m).start()

        each(first, last, one)

    def hand_across(self, first, last):
        def one(m):
            for k in (1, 2):
                self.half(k, m).wait_recv()
            self.pair_back(3, m).start()

        each(first, last, one)

    def end(self):
        each(0, self.far, lambda m: each(0, NEAR, lambda k: self.pair_back(k, m).wait()))
        self.keep().wait()
        each(1, self.far, lambda k: self.line_back(k).wait_send())
        each(0, self.far, lambda m: each(1, NEAR - 1, lambda k: self.plane_back(k, m).wait_send()))

        def sent(m):
            for k in (1, 2):
                self.half(k, m).wait_send()

        each(0, self.far, sent)


def k_tail(cfg, *refs):
    st_a, st_b, ex7, ex8, side = cfg
    it = iter(refs)

    def take(n):
        return [next(it) for _ in range(n)]

    hbm = take(13)
    x_slow, lact_src, taps_src = take(3)
    gb, c1, c2, c3, q6, m16, m64, g_fout, g_fmid = take(9)
    low_out, dlow_out, lat_low_out, gf, gw_in, gw_lat, q7, q8, hn, res_a, near_b = take(11)
    local = take(13)
    gw_a, dsb, sb, spad, wsp, sa, x_fast, dfa, fa, w_in, w_sc, dsp, lat = local
    pad, gsp, gin, low, dlow, gw_b, near_a, ends, s1, s2, t1, t2, sems, out_sems = take(14)
    x_part, taps_part, gsi, glat, wsp_turned, x_sems, taps_sems, lact_sem = take(8)
    near1, line1, near2 = take(len(st_a.near_scratch)), take(len(st_a.line_scratch)), take(len(st_b.near_scratch))
    scr7 = take(len(ex7.local) + len(ex7.work))
    scr8 = take(len(ex8.local) + len(ex8.work))
    n_in = w_in.shape[0]
    srcs = list(hbm)
    for k in (9, 10):
        srcs[k] = hbm[k].at[pl.ds(hbm[k].shape[0] - n_in, n_in)]
    loads = [pltpu.make_async_copy(src, dst, sems.at[k]) for k, (src, dst) in enumerate(zip(srcs, local))]
    count = exchange_hello(ex8)
    for k in (1, 2, 0, 4, 3, 5, 6, 7, 8, 9, 10, 11, 12):
        loads[k].start()
    near = Near(st_a, gw_a, near_a, near1)
    line = Line(st_a, near_a, line1)
    near_two = Near(st_b, gw_b, near_b, near2)
    far = st_a.far
    t_n, c = pad.shape[2], pad.shape[3]
    wide = side * t_n
    per = side // STEPS
    fill = m16[0:1, :, 0:1]

    def waits(*names):
        for k in names:
            loads[k].wait()

    waits(1, 2)
    scale, p_row, q_row = rows(c3, 0, 4, 2), rows(q6, 0, 0, 2), rows(q6, 1, 0, 2)
    zero_ref(pad)

    def fill_pad(h):
        part = pl.ds(h * wide, wide)
        d = back_norm(
            scale, p_row, q_row, dsb[part].reshape(side, t_n, c), sb[part].reshape(side, t_n, c), fill
        )
        pad[h + 1, 1 : side + 1] = d.astype(BF16)

    each(0, side, fill_pad)
    waits(0, 4)
    for k in range(9):
        wsp_turned[k * c : (k + 1) * c, :] = wsp[k * c : (k + 1) * c, :].T
    pl.semaphore_wait(pltpu.get_barrier_semaphore(), count)
    near.start()
    waits(3, 5, 6, 7, 8)
    f_n = x_fast.shape[2]
    p_n = x_fast.shape[1] // STEPS

    def spatial(i):
        h0 = i * per
        turned = flat(pad[pl.ds(h0 + 1, per), 1 : side + 1]).T
        blocks = []
        for a in range(3):
            for b in range(3):
                k = 3 * a + b
                patch = flat(spad[pl.ds(h0 + a, per), b : b + side])
                cols = slice(k * c, (k + 1) * c)
                gsp[:, cols] = jnp.where(i == 0, 0.0, gsp[:, cols]) + dot(turned, patch)
                blocks.append(flat(pad[pl.ds(h0 + 2 - a, per), 2 - b : 2 - b + side]))
        acc = dot(jnp.concatenate(blocks, axis=1), wsp_turned[...])
        span = pl.ds(i * per * wide, per * wide)
        z = sa[span]
        back = acc * slope(z * rows(c2, 0, 1, 2) + rows(c2, 1, 1, 2))
        dsb[span] = back
        unit = z * rows(c2, 2, 1, 2) - rows(c2, 3, 1, 2)
        sum_add(i, back.reshape(per * side, t_n, c), s1)
        sum_add(i, (back * unit).reshape(per * side, t_n, c), s2)
        f_span = pl.ds(i * p_n, p_n)
        small = back_norm(
            rows(c1, 0, 0, 1), rows(q6, 0, 2, 1), rows(q6, 1, 2, 1), dfa[f_span], fa[f_span], m64[0:1]
        ).astype(BF16)
        dlow[f_span] = small
        packed = jnp.concatenate([flat(x_fast[s, f_span]) for s in range(x_fast.shape[0])], axis=1)
        add_to(i, gin, dot_tn(flat(small), packed))
        pl.when(i == 0)(lambda: near.add_pair(0, far // 2))
        pl.when(i == 1)(lambda: near.add_pair(far // 2, far))

    each(0, STEPS, spatial)
    stats = scr7[0]
    zero_ref(stats)
    put_rows(stats, 0, sum_end(s1))
    put_rows(stats, 2, sum_end(s2))
    stores = [pltpu.make_async_copy(dlow, dlow_out, out_sems.at[0])]
    stores[0].start()

    def late():
        for k in range(9):
            gw_b[k * c : (k + 1) * c, :] = gsp[:, k * c : (k + 1) * c].T.astype(BF16)
        if 9 * c < gw_b.shape[0]:
            gw_b[9 * c :, :] = jnp.zeros((gw_b.shape[0] - 9 * c, c), BF16)
        n = g_fout.shape[0]
        gf[0:n, 0:LANES] = fold_wide(gin, x_fast.shape[0])
        gf[0:n, LANES:] = g_fout[...]
        gf[n : 2 * n, 0:LANES] = g_fmid[0:n, :]
        gf[n : 2 * n, LANES:] = g_fmid[n : 2 * n, :]
        gf[2 * n :, 0:LANES] = g_fmid[2 * n :, :]
        gf[2 * n :, LANES:] = jnp.zeros((n, LANES), F32)

    n_pos = side * side
    lact = spad.reshape(-1, t_n, c).at[pl.ds(0, n_pos)]
    lat_low = pad.reshape(-1, t_n, c).at[pl.ds(0, n_pos)]
    lact_load = pltpu.make_async_copy(lact_src, lact, lact_sem)
    lact_load.start()
    block = per * wide

    def x_load(i):
        return pltpu.make_async_copy(x_slow.at[pl.ds(i * block, block)], x_part.at[i % 2], x_sems.at[i % 2])

    def taps_load(i):
        return pltpu.make_async_copy(taps_src.at[pl.ds(i * block, block)], taps_part.at[i % 2], taps_sems.at[i % 2])

    for i in range(2):
        x_load(i).start()
        taps_load(i).start()
    def pull():
        near_two.start()
        near.add_plane(0, far // 2, lambda m: line.line(m).start())

    exchange_run(ex7, [gb, c2], [q7], scr7, late, between=pull)
    near.add_plane(far // 2, far - 1, lambda m: line.line(m).start())
    near.add_plane(far - 1, far)
    waits(9, 10, 11, 12)
    scale7, p7, q7_row = rows(c2, 0, 1, 2), rows(q7, 0, 0, 2), rows(q7, 1, 0, 2)

    def join(i):
        span = pl.ds(i * block, block)
        shape = (per * side, t_n, c)
        d = back_norm(scale7, p7, q7_row, dsb[span].reshape(shape), sa[span].reshape(shape), fill)
        small = flat(d).astype(BF16)
        low[span] = small
        d = dot_nt(dsp[span], w_sc[...]) + dot_nt(small, w_in[...])
        z = lat[span]
        back = d * slope(z * rows(c1, 0, 1, 2) + rows(c1, 1, 1, 2))
        sb[span] = back
        unit = z * rows(c1, 2, 1, 2) - rows(c1, 3, 1, 2)
        sum_add(i, back.reshape(shape), t1)
        sum_add(i, (back * unit).reshape(shape), t2)
        pl.when(i == 2)(lambda: near_two.add_pair(0, far))

    each(0, STEPS, join)
    stores.append(pltpu.make_async_copy(low, low_out, out_sems.at[1]))
    stores[1].start()
    stats = scr8[0]
    zero_ref(stats)
    put_rows(stats, 0, sum_end(t1))
    put_rows(stats, 2, sum_end(t2))

    def post(q, sent):
        d = back_norm(rows(c1, 0, 1, 2), rows(q, 0, 0, 2), rows(q, 1, 0, 2), ends[0], ends[1], m16[0, 0:1, 0:1])
        sent[...] = d.astype(BF16)

    def in_step(i):
        x_load(i).wait()
        joined = jnp.concatenate([x_part[i % 2], flat(lact[pl.ds(i * per * side, per * side)])], axis=1)
        add_to(i, gsi, dot(low[pl.ds(i * block, block)].T, joined))
        pl.when(i + 2 < STEPS)(lambda: x_load(i + 2).start())

    def in_grad():
        zero_ref(ends)
        for s in range(x_fast.shape[0]):
            for step in range(STEPS):
                for p in range(p_n):
                    at = ((s * STEPS + step) * p_n + p) * t_n
                    ends[0, step, s * 8 + p : s * 8 + p + 1, :] = sb[at : at + 1, :]
                    ends[1, step, s * 8 + p : s * 8 + p + 1, :] = lat[at : at + 1, :]
        lact_load.wait()
        each(0, 3, in_step)

    def in_grad_rest():
        each(3, STEPS, in_step)
        for n in range(gsi.shape[1] // c):
            gw_in[n * c : (n + 1) * c, :] = gsi[:, n * c : (n + 1) * c].T.astype(BF16)

    def lat_step(i):
        scale8, p8, q8_row = rows(c1, 0, 1, 2), rows(q8, 0, 0, 2), rows(q8, 1, 0, 2)
        span = pl.ds(i * block, block)
        shape = (per * side, t_n, c)
        d = back_norm(scale8, p8, q8_row, sb[span].reshape(shape), lat[span].reshape(shape), fill).astype(BF16)
        lat_low[pl.ds(i * per * side, per * side)] = d
        taps_load(i).wait()
        add_to(i, glat, dot_tn(flat(d), taps_part[i % 2]))
        pl.when(i + 2 < STEPS)(lambda: taps_load(i + 2).start())

    def lat_grad():
        each(0, STEPS, lat_step)
        stores.append(pltpu.make_async_copy(lat_low, lat_low_out, out_sems.at[2]))
        stores[2].start()
        for k in range(glat.shape[1] // LANES):
            gw_lat[k * LANES : (k + 1) * LANES, :] = glat[:, k * LANES : (k + 1) * LANES].T.astype(BF16)

    exchange_run(ex8, [gb, c1], [q8, hn], scr8, in_grad, post, lat_grad, in_grad_rest)
    res_a[...] = line.total()
    near_two.add_plane(0, far)
    for store in stores:
        store.wait()
    line.end()
    near.end()
    near_two.end()


def back_tail(st_a, st_b, ex7, ex8, hbm, more, small, side, t_n, c):
    vm, anywhere = pl.BlockSpec(memory_space=pltpu.VMEM), pl.BlockSpec(memory_space=pl.ANY)
    inner, f_n = hbm[7].shape[:2]
    n = side * side * t_n
    c_cat, c_taps = more[0].shape[1] + c, more[2].shape[1]
    part = n // STEPS
    outs = [((n, c), BF16), ((inner, f_n, LANES), BF16), (more[1].shape, BF16), (small[-1].shape[0:1] + (2 * LANES,), F32),
            ((c_cat, c), BF16), ((c_taps, c), BF16),
            *ex7.outs, *ex8.outs, (st_a.chunk, BF16), (st_b.near_shape, BF16)]
    local = [pltpu.VMEM((c,) + a.shape[1:] if k in (9, 10) else a.shape, a.dtype) for k, a in enumerate(hbm)]
    width = hbm[6].shape[0] * hbm[6].shape[3]
    scratch = [
        pltpu.VMEM((side + 2, side + 2, t_n, c), BF16), pltpu.VMEM((c, 9 * c), F32), pltpu.VMEM((LANES, width), F32),
        pltpu.VMEM((n, c), BF16), pltpu.VMEM((inner, f_n, LANES), BF16), pltpu.VMEM((st_b.rows_n, c), BF16),
        pltpu.VMEM(st_a.near_shape, BF16), pltpu.VMEM((2, *ex8.post), F32), *[pltpu.VMEM((t_n, c), F32)] * 4,
        pltpu.SemaphoreType.DMA((len(hbm),)), pltpu.SemaphoreType.DMA((3,)),
        pltpu.VMEM((2, part, c_cat - c), BF16), pltpu.VMEM((2, part, c_taps), BF16), pltpu.VMEM((c, c_cat), F32),
        pltpu.VMEM((c, c_taps), F32), pltpu.VMEM((9 * c, c), BF16), pltpu.SemaphoreType.DMA((2,)), pltpu.SemaphoreType.DMA((2,)), pltpu.SemaphoreType.DMA,
        *st_a.near_scratch, *st_a.line_scratch, *st_b.near_scratch, *ex7.local, *ex7.work, *ex8.local, *ex8.work,
    ]
    return pl.pallas_call(
        functools.partial(k_tail, (st_a, st_b, ex7, ex8, side)),
        out_shape=[jax.ShapeDtypeStruct(s, d) for s, d in outs],
        in_specs=[anywhere] * (len(hbm) + len(more)) + [vm] * len(small),
        out_specs=[anywhere] * 3 + [vm] * (len(outs) - 3),
        scratch_shapes=[*local, *scratch],
        compiler_params=pltpu.CompilerParams(collective_id=ex8.cid, has_side_effects=True, vmem_limit_bytes=VMEM_LIMIT),
        name="tail",
    )(*hbm, *more, *small)


def final_kernel(cfg, *refs):
    first, second, third, both, offsets, n_hbm, n_small = cfg
    it = iter(refs)

    def take(n):
        return [next(it) for _ in range(n)]

    hbm, small, (out_a, out_bc, gx_out, fast_out) = take(n_hbm), take(n_small), take(4)
    res_a, near_b, *parts, hn, m16, wlat, wfa = small
    loaded = take(n_hbm)
    low, dsp, w_in, w_sc, lat_low, df, dlow = loaded
    x, near_c, res, gx, fast_gx, gs, sems, gx_sems, fast_sems = take(9)
    share_a = Share(first, res_a, out_a, take(len(first.share_scratch)))
    line_b = Line(second, near_b, take(len(second.line_scratch)))
    near = Near(third, x, near_c, take(len(third.near_scratch)))
    line_c = Line(third, near_c, take(len(third.line_scratch)))
    share = Share(both, res, out_bc, take(len(both.share_scratch)))
    far, c = first.far, near.c
    barrier = pltpu.get_barrier_semaphore()
    loads = [pltpu.make_async_copy(a, b, sems.at[k]) for k, (a, b) in enumerate(zip(hbm, loaded))]

    def greet(device):
        pl.semaphore_signal(barrier, inc=1, device_id=device, device_id_type=MESH)

    greet(c.sibling)
    each(1, NEAR, lambda k: greet(c.plane(k)))
    each(1, far, lambda k: greet(c.line(k)))
    for load in loads:
        load.start()
    for ref, first_row, end in zip(parts, offsets, offsets[1:]):
        x[first_row:end, :] = ref[...].astype(BF16)
    if end < x.shape[0]:
        x[end:, :] = jnp.zeros((x.shape[0] - end, x.shape[1]), BF16)
    pl.semaphore_wait(barrier, NEAR + far - 1)

    near.start()
    line_b.start(0, far)
    share_a.start_line()
    p_n = dlow.shape[0] // STEPS

    def gx_store(i):
        part = pl.ds(i * p_n, p_n)
        return pltpu.make_async_copy(gx.at[:, part], gx_out.at[:, part], gx_sems.at[i])

    def slow_step(i):
        part = pl.ds(i * p_n, p_n)
        slow_grad(low.at[:, part], dsp.at[:, part], w_in, w_sc, gx.at[:, part])
        gx_store(i).start()

    def fast_store(i):
        part = pl.ds(i * p_n, p_n)
        return pltpu.make_async_copy(fast_gx.at[:, part], fast_out.at[:, part], fast_sems.at[i])

    def fast_step(i):
        part = pl.ds(i * p_n, p_n)
        fast_grad(lat_low.at[:, part], hn.at[pl.ds(i, 1)], df.at[part], dlow.at[part], m16, wlat, wfa,
                  fast_gx.at[:, part], gs)
        fast_store(i).start()

    share_a.start_plane()
    near.add_pair(0, far)
    for k in (0, 1, 2, 3):
        loads[k].wait()
    each(0, 1, slow_step)
    res[0 : second.ch, :] = line_b.total()
    share_a.relay(1, far)
    share_a.hand_on(0, 1)
    each(1, 3, slow_step)
    near.add_plane(0, far - 1, lambda m: line_c.line(m).start())
    near.add_plane(far - 1, far)
    share_a.hand_on(1, far)
    each(3, 4, slow_step)
    res[second.ch :, :] = line_c.total()
    share.start_line()
    share.start_plane()
    each(4, STEPS, slow_step)
    for k in range(4, n_hbm):
        loads[k].wait()
    share.relay(1, far)
    share_a.hand_across(0, far)
    share.hand_on(0, 1)
    each(0, 3, fast_step)
    share.hand_on(1, far)
    each(3, STEPS, fast_step)
    share.hand_across(0, far)
    share_a.end()
    share.end()
    line_b.end()
    line_c.end()
    near.end()
    each(0, STEPS, lambda i: gx_store(i).wait())
    each(0, STEPS, lambda i: fast_store(i).wait())


def final_sum(sizes, cid, first, second, hbm, small, gx, fast_gx, heights):
    width = first.width
    offsets = tuple(sum(heights[:k]) for k in range(len(heights) + 1))
    third = Stream(sizes, rows_for(sizes, offsets[-1]), width)
    both = Stream(sizes, second.rows_n + third.rows_n, width)
    vm, anywhere = pl.BlockSpec(memory_space=pltpu.VMEM), pl.BlockSpec(memory_space=pl.ANY)
    low, dlow = hbm[0], hbm[6]
    s_n, p_n, f_n = low.shape[0], low.shape[1] // STEPS, dlow.shape[1]
    out_a, out_bc, gx, fast_gx = pl.pallas_call(
        functools.partial(final_kernel, (first, second, third, both, offsets, len(hbm), len(small))),
        out_shape=[jax.ShapeDtypeStruct(s, BF16) for s in ((first.rows_n, width), (both.rows_n, width), gx, fast_gx)],
        in_specs=[anywhere] * len(hbm) + [vm] * len(small),
        out_specs=[anywhere] * 4,
        scratch_shapes=[
            *[pltpu.VMEM(a.shape, a.dtype) for a in hbm],
            pltpu.VMEM((third.rows_n, width), BF16), pltpu.VMEM(third.near_shape, BF16), pltpu.VMEM(both.chunk, BF16),
            pltpu.VMEM(gx, BF16), pltpu.VMEM(fast_gx, BF16), pltpu.VMEM((s_n * p_n * f_n, LANES), F32),
            pltpu.SemaphoreType.DMA((len(hbm),)), pltpu.SemaphoreType.DMA((STEPS,)), pltpu.SemaphoreType.DMA((STEPS,)),
            *first.share_scratch, *second.line_scratch, *third.near_scratch, *third.line_scratch, *both.share_scratch,
        ],
        compiler_params=pltpu.CompilerParams(collective_id=cid, has_side_effects=True, vmem_limit_bytes=VMEM_LIMIT),
        name="final_sum",
    )(*hbm, *small)
    return out_a, out_bc.reshape(-1, both.ch, width), gx, fast_gx


def k_unpack(pieces, cut, *refs):
    (src_a, src_b, q4, q5, q6, q7, q8), held, refs = refs[:7], refs[7:10], refs[10:]
    outs, (low_a, low_b, low_c, wide, line, *kept, sem_a, sem_b, sem_out, sem_held) = refs[:-12], refs[-12:]
    outs, given = outs[:-3], outs[-3:]

    def moves(srcs, dsts, way):
        return [
            pltpu.make_async_copy(a.at[pl.ds(k, 1)], b.at[pl.ds(k, 1)], sem_held.at[way, n, k])
            for n, (a, b) in enumerate(zip(srcs, dsts))
            for k in range(a.shape[0])
        ]

    passes_in, passes = moves(held, kept, 0), moves(kept, given, 1)
    outs, (gains_out, biases_out, in_out, mid_out, out_out) = outs[:-5], outs[-5:]
    lows = (low_a, low_b, low_c)
    flats = [low_a, low_b.reshape(-1, low_b.shape[-1]), low_c.reshape(-1, low_c.shape[-1])]
    starts = [sum(p[2] for p in pieces[:k]) for k in range(len(pieces))]

    def fetch_a(k):
        _, row, height, _, _ = pieces[k]
        return pltpu.make_async_copy(src_a.at[pl.ds(row, height)], low_a.at[pl.ds(row, height)], sem_a.at[k])

    def fetch_b(k):
        part = src_b.at[:, pl.ds(0, cut)] if k == 1 else src_b.at[:, pl.ds(cut, src_b.shape[1] - cut)]
        return pltpu.make_async_copy(part, lows[k], sem_b.at[k])

    def store(k):
        _, _, height, out, col = pieces[k]
        part = outs[out] if col is None else outs[out].at[:, pl.ds(col, wide.shape[1])]
        return pltpu.make_async_copy(wide.at[pl.ds(starts[k], height)], part, sem_out.at[k])

    for k, piece in enumerate(pieces):
        if piece[0] == 0:
            fetch_a(k).start()
    for k in (1, 2):
        fetch_b(k).start()
    for move in passes_in:
        move.start()
    seen = 0
    for k, (src, row, height, _, _) in enumerate(pieces):
        if src == 0:
            fetch_a(k).wait()
        elif src != seen:
            fetch_b(src).wait()
            seen = src
        wide[starts[k] : starts[k] + height, :] = flats[src][row : row + height, :].astype(F32)
        store(k).start()
    for move_in, move in zip(passes_in, passes):
        move_in.wait()
        move.start()
    lane = lax.broadcasted_iota(jnp.int32, (1, LANES), 1)
    left = lane < LANES // 2
    for slab, out in ((3, gains_out), (2, biases_out)):
        at = 0
        for q, first, count in ((q4, 0, 1), (q8, 0, 2), (q7, 0, 2), (q6, 0, 2), (q5, 0, 16)):
            line[at : at + count, :] = q[slab, first : first + count, :]
            at += count
        half = pltpu.roll(line[0:at, :], LANES // 2, 1)
        head = jnp.where(lane < LANES // 4, q6[slab, 2:3, :], q5[slab, 16:17, :])
        out[0:1, :] = jnp.where(left, head, half[0:1])
        out[1:at, :] = jnp.where(left, half[0 : at - 1], half[1:at])
        out[at : at + 1, :] = jnp.where(left, half[at - 1 : at], 0.0)
    a = in_out.shape[0]
    last = sum(p[2] for p in pieces if p[0] == 2)
    small = flats[2][last : last + 3 * a, :]
    in_out[...] = small[0:a, 0:LANES].astype(F32)
    out_out[...] = small[0:a, LANES:].astype(F32)
    eye = (lax.broadcasted_iota(jnp.int32, (a, a), 0) == lax.broadcasted_iota(jnp.int32, (a, a), 1)).astype(BF16)
    for k, (row, col) in enumerate(((a, 0), (a, LANES), (2 * a, 0))):
        mid_out[k] = dot_tn(small[row : row + a, col : col + LANES], eye)[0:a, :]
    for k in range(len(pieces)):
        store(k).wait()
    for move in passes:
        move.wait()


def unpack(src_a, src_b, cut, pieces, shapes, small_shapes, norm_sums, held):
    hbm, vm = pl.BlockSpec(memory_space=pl.ANY), pl.BlockSpec(memory_space=pltpu.VMEM)
    n, _, width = src_b.shape
    return pl.pallas_call(
        functools.partial(k_unpack, pieces, cut),
        out_shape=[jax.ShapeDtypeStruct(s, F32) for s in (*shapes, *small_shapes)]
        + [jax.ShapeDtypeStruct(a.shape, a.dtype) for a in held],
        in_specs=[hbm] * 2 + [vm] * len(norm_sums) + [hbm] * len(held),
        out_specs=[hbm] * len(shapes) + [vm] * len(small_shapes) + [hbm] * len(held),
        scratch_shapes=[
            pltpu.VMEM(src_a.shape, BF16),
            pltpu.VMEM((n, cut, width), BF16),
            pltpu.VMEM((n, src_b.shape[1] - cut, width), BF16),
            pltpu.VMEM((sum(p[2] for p in pieces), width), F32),
            pltpu.VMEM((24, LANES), F32),
            *[pltpu.VMEM(a.shape, a.dtype) for a in held],
            pltpu.SemaphoreType.DMA((len(pieces),)),
            pltpu.SemaphoreType.DMA((3,)),
            pltpu.SemaphoreType.DMA((len(pieces),)),
            pltpu.SemaphoreType.DMA((2, len(held), held[0].shape[0])),
        ],
        compiler_params=pltpu.CompilerParams(vmem_limit_bytes=VMEM_LIMIT),
        name="unpack",
    )(src_a, src_b, *norm_sums, *held)


def small_set_up(fill_ref, clip_ref, norm_ref, wfi_ref, wfm_ref, wfo_ref,
                 gb_ref, m16_ref, m64_ref, wfa_ref, wmid_ref, wback_ref, wout_ref, s_n, t_n):
    length = lax.axis_size("frames")
    total = lax.axis_size("path") * length
    me = lax.axis_index("path") * length + lax.axis_index("frames")
    lane = lax.broadcasted_iota(jnp.int32, (1, LANES), 1)
    for k in range(2):
        half = pltpu.roll(norm_ref[k], LANES // 2, 1)
        main = jnp.where(lane < LANES // 2, half[0:23], half[1:24])
        for j in range(2):
            v = jnp.where(lane // 32 == j, norm_ref[k, 0:1, :], 0.0)
            v = v + pltpu.roll(v, 64, 1)
            gb_ref[k, j : j + 1, :] = v + pltpu.roll(v, 32, 1)
        for j in range(4):
            gb_ref[k, 2 + j : 3 + j, :] = main[0:1]
        gb_ref[k, 6:28, :] = main[1:23]
        gb_ref[k, 28:32, :] = jnp.zeros((4, LANES), F32)

    def row(value):
        return jnp.full((1, LANES), value, F32)

    last = jnp.where(me < total - 1, 1.0, 0.0)
    link = [jnp.where(clip_ref[t] >= 1, 1.0, 0.0) for t in range(t_n)]
    for t in range(t_n):
        filled = row(fill_ref[t].astype(F32))
        after = row(link[t + 1] if t + 1 < t_n else last)
        m16_ref[0, t : t + 1, :] = filled
        m16_ref[1, t : t + 1, :] = row(link[t])
        m16_ref[2, t : t + 1, :] = after
        m64_ref[0, 4 * t : 4 * t + 4, :] = jnp.broadcast_to(filled, (4, LANES))
        m64_ref[1, 4 * t : 4 * t + 1, :] = row(link[t])
        m64_ref[1, 4 * t + 1 : 4 * t + 4, :] = jnp.ones((3, LANES), F32)
        m64_ref[2, 4 * t : 4 * t + 3, :] = jnp.ones((3, LANES), F32)
        m64_ref[2, 4 * t + 3 : 4 * t + 4, :] = after

    zero_ref(wfa_ref)
    zero_ref(wout_ref)
    a = wfi_ref.shape[0]
    for s in range(s_n):
        wfa_ref[s * a : (s + 1) * a, s * LANES : (s + 1) * LANES] = wfi_ref[...]
        wout_ref[s * a : (s + 1) * a, s * LANES : (s + 1) * LANES] = wfo_ref[...]
    tall = (LANES, a)
    spread = (lax.broadcasted_iota(jnp.int32, tall, 0) % a == lax.broadcasted_iota(jnp.int32, tall, 1)).astype(BF16)
    square = (LANES, LANES)
    diag = lax.broadcasted_iota(jnp.int32, square, 0) // a == lax.broadcasted_iota(jnp.int32, square, 1) // a
    for k in range(3):
        left = dot(spread, wfm_ref[k]).astype(BF16)
        wmid_ref[k * LANES : (k + 1) * LANES, :] = jnp.where(diag, dot_nt(left, spread), 0.0).astype(BF16)
        right = dot_nt(spread, wfm_ref[k]).astype(BF16)
        wback_ref[k * LANES : (k + 1) * LANES, :] = jnp.where(diag, dot_nt(right, spread), 0.0).astype(BF16)


def per_device(slow_input, fast_input, clip_offset, fill, w_fast_in, w_fast_mid, w_fast_out, w_lateral,
               w_slow_in, w_slow_mid, w_slow_out, w_shortcut, gains, biases, slow_cot, fast_cot):
    sizes = (lax.axis_size("path"), lax.axis_size("frames"))
    t_n, side, _, c_slow = slow_input.shape
    f_n, c_fast = fast_input.shape[0], fast_input.shape[3]
    in_fast, in_slow, c_lat = w_fast_in.shape[1], w_slow_in.shape[1], w_lateral.shape[2]
    pixels = side * side
    groups = LANES // in_fast
    inner = pixels // groups
    p_n = inner // STEPS

    def slow_view(a):
        return jnp.transpose(a, (1, 2, 0, 3)).reshape(groups, inner, t_n, a.shape[3])

    def fast_view(a):
        return jnp.transpose(a, (1, 2, 0, 3)).reshape(groups, inner, f_n, a.shape[3])

    def unview(a):
        return jnp.transpose(a.reshape(side, side, a.shape[2], a.shape[3]), (2, 0, 1, 3))

    x_slow, cot_slow = slow_view(slow_input), slow_view(slow_cot)
    x_fast, cot_fast = fast_view(fast_input), fast_view(fast_cot)

    norms = jnp.stack([gains, biases])
    norms = jnp.pad(norms, ((0, 0), (0, -norms.shape[1] % (8 * LANES)))).reshape(2, -1, LANES)
    wlat = w_lateral.reshape(-1, c_lat)
    wsp = w_slow_mid.reshape(-1, in_slow)

    sl = (groups, inner, t_n)
    fp = (inner, f_n)

    def slow_out(width, dtype):
        return out_blocked(sl + (width,), dtype, 1, p_n)

    def fast_out(width, dtype):
        return out_blocked(fp + (width,), dtype, 0, p_n)

    def sb_(a):
        return blocked(a, 1, p_n)

    def fb_(a):
        return blocked(a, 0, p_n)

    def stat(n):
        return out_whole((pad8(n), LANES), F32)

    def acc(rows_n, width, count):
        return [pltpu.VMEM((rows_n, width), F32)] * count

    small = (STEPS, 8, LANES)

    sems7 = pltpu.SemaphoreType.DMA((STEPS,))
    exs = [
        Exchange(sizes, 1, 7, fwd=(("lane4", 0, 1), ("plain", 6, 2)), up=small, down=small),
        Exchange(sizes, 1, 23, fwd=(("lane4", 1, 1), ("plain", 8, 2), ("plain", 20, 8))),
    ]
    kept = [
        (fp + (LANES,), F32), (sl + (c_lat,), F32), (sl + (5 * c_fast,), BF16), (sl + (c_lat,), BF16),
        (fp + (3 * LANES,), BF16), (sl + (in_slow,), F32), (sl + (c_slow,), F32), (fp + (LANES,), F32),
    ]
    ready = [((2, 32, LANES), F32), ((3, t_n, LANES), F32), ((3, f_n, LANES), F32), ((LANES, groups * c_fast), BF16),
             ((3 * LANES, LANES), BF16), ((3 * LANES, LANES), BF16), ((LANES, groups * c_fast), BF16)]
    ends = (STEPS, groups * 8, 2 * c_fast)
    fa, lat, taps, lact, ftap, sa, sp, fb, gb, m16, m64, wfa, wmid, wback, wout, c1, hp, hn, c2 = run_resident(
        functools.partial(k_front, exs), exs,
        [x_fast, wlat, x_slow, w_slow_in, w_shortcut],
        [fill, clip_offset, norms, w_fast_in.T, w_fast_mid, w_fast_out],
        kept, [*[(*k, True) for k in kept], *[(*k, False) for k in ready]],
        [pltpu.VMEM((groups * p_n * f_n, c_fast), F32), *acc(f_n, LANES, 2), *acc(t_n, c_lat, 2), *acc(t_n, in_slow, 2),
         *acc(t_n, c_slow, 2), *acc(f_n, LANES, 2), pltpu.SemaphoreType.DMA((8,)), sems7,
         pltpu.VMEM((pixels * t_n, c_fast), F32), pltpu.VMEM(ends, F32), pltpu.VMEM(ends, BF16), pltpu.VMEM(ends, BF16),
         pltpu.SemaphoreType.DMA((2,))],
        "front",
        scalars=2,
    )

    exs = [
        Exchange(sizes, 3, 13, fwd=(("row4", 2, 4), ("plain", 10, 2))),
        Exchange(sizes, 3, 25, fwd=(("plain", 12, 8),), bwd=(("row4", 0, 0, 2, 4, 0, 4),)),
    ]
    kept = [
        ((side + 2, side + 2, t_n, in_slow), BF16), ((pixels, t_n, in_slow), F32), (fp + (LANES,), BF16),
        ((pixels, t_n, in_slow), BF16), ((groups, inner, f_n, c_fast), BF16), (fp + (groups * c_fast,), F32),
    ]
    pad, sb, fact, sact, fast_y, df, c3, c4, q4 = run_resident(
        functools.partial(k_middle, exs), exs,
        [sa.reshape(side, side, t_n, in_slow), fb, wsp, w_slow_out, x_fast, cot_fast], [gb, c2, m16, m64, wout],
        kept, [(*k, True) for k in kept],
        [*acc(t_n, in_slow, 2), *acc(f_n, groups * c_fast, 2), *acc(t_n, c_slow, 2), *acc(f_n, groups * c_fast, 2),
         pltpu.SemaphoreType.DMA((4,)), sems7, sems7],
        "middle",
    )
    sb4, sact = sb.reshape(sl + (in_slow,)), sact.reshape(sl + (in_slow,))

    halo_pair = out_blocked((STEPS, 2, 8, LANES), F32, 0, 1)
    slow_y, dy, dfb, g_fout, up, down, st = call(
        k_out,
        [sb_(sact), sb_(sp), sb_(cot_slow), fb_(df), fb_(fact), fb_(fb), whole(c2), whole(c3), whole(c4), whole(q4),
         whole(m16), whole(m64), whole(w_slow_out), whole(wout)],
        [slow_out(c_slow, BF16), slow_out(c_slow, F32), fast_out(LANES, F32),
         out_whole((in_fast, c_fast), F32), halo_pair, halo_pair, stat(26)],
        [*acc(t_n, c_slow, 3), *acc(f_n, LANES, 2), *acc(LANES, groups * c_fast, 1)],
        "out",
    )
    pair = (STEPS, 2, 8, LANES)
    ex5 = Exchange(
        sizes, 6, 26,
        bwd=(("plain", 0, 0, 12, 8, 0, 8), ("plain", 1, 3, 20, 8, 0, 16), ("lane4", 1, 0, 1, 1, 24, 25)),
        up=pair, down=pair,
    )
    c_cat = w_slow_in.shape[0]
    width = in_slow
    stream_a = Stream(sizes, rows_for(sizes, c_cat * c_slow // width), width)
    stream_b = Stream(sizes, rows_for(sizes, 9 * in_slow), width)
    gw_short, gw_sout, dsp, dsb, dfa, g_fmid, q6, q5 = call(
        k_back_out,
        [sb_(x_slow), sb_(lact), sb_(dy), sb_(sp), sb_(sact), sb_(sb4), fb_(dfb), fb_(fb), fb_(fa), fb_(ftap), 1, 2,
         whole(c1), whole(c2), whole(c3), whole(c4), 0, whole(m16), whole(m64), whole(w_slow_out), whole(wback)],
        [out_whole((stream_a.rows_n, width), BF16), out_whole((c_slow, width), BF16), slow_out(c_slow, BF16),
         slow_out(in_slow, F32), fast_out(LANES, F32), out_whole((3 * in_fast, LANES), F32), STAT],
        [*acc(t_n, in_slow, 2), *acc(f_n, LANES, 2), *acc(c_cat, c_slow, 1), *acc(in_slow, c_slow, 1),
         *acc(LANES, 3 * LANES, 1)],
        "back_out",
        Exchange(sizes, 6, 6, bwd=(("plain", 0, 4, 10, 2, 0, 2), ("lane4", 1, 0, 0, 1, 4, 5))),
        [gb, c3, c1],
        ex5,
        [st, up, down, gb, c4, c2],
    )

    def rows2(a):
        return a.reshape(-1, a.shape[-1])

    dsa_low, dfa_low, lat_low, gw_fast, gw_in, gw_lat, q7, q8, hn, res_a, near_b = back_tail(
        stream_a, stream_b,
        Exchange(sizes, 7, 4, bwd=(("plain", 0, 1, 8, 2, 0, 2),)),
        Exchange(sizes, 7, 4, bwd=(("plain", 0, 1, 6, 2, 0, 2),), post=(STEPS, groups * 8, c_lat)),
        [gw_short, rows2(dsb), rows2(sb4), pad, wsp, rows2(sa), x_fast, dfa, fa, w_slow_in, w_shortcut, rows2(dsp), rows2(lat)],
        [rows2(x_slow), lact.reshape(pixels, t_n, c_lat), rows2(taps)],
        [gb, c1, c2, c3, q6, m16, m64, g_fout, g_fmid],
        side, t_n, in_slow,
    )
    heights = (gw_sout.shape[0], c_cat, 5 * c_fast, gw_fast.shape[0])
    sum_a, sum_bc, slow_gx, fast_gx = final_sum(
        sizes, 9, stream_a, stream_b,
        [dsa_low.reshape(sl + (in_slow,)), dsp, w_slow_in, w_shortcut, lat_low.reshape(sl + (c_lat,)), df, dfa_low],
        [res_a, near_b, gw_sout, gw_in, gw_lat, gw_fast, hn, m16, wlat, wfa],
        sl + (c_slow,), (groups, inner, f_n, c_fast), heights,
    )
    blocks = c_slow // in_slow
    pieces = [(0, n * c_cat, c_cat, 0, n * width) for n in range(blocks)]
    pieces.append((1, 0, 9 * in_slow, 2, None))
    at = 0
    for n in range(blocks):
        pieces.append((2, at, in_slow, 1, n * width))
        at += in_slow
    for out, tall in ((3, c_cat), (4, 5 * c_fast)):
        pieces.append((2, at, tall, out, None))
        at += tall
    norm_rows = -(-gains.shape[0] // LANES)
    g_short, g_sout, gw_mid, gw_in, gw_lat, gains_grad, biases_grad, g_fin, g_fmid, g_fout, *held = unpack(
        sum_a, sum_bc, stream_b.ch, tuple(pieces),
        [(c_cat, c_slow), (in_slow, c_slow), (9 * in_slow, width), (c_cat, in_slow), wlat.shape],
        [(norm_rows, LANES), (norm_rows, LANES), (in_fast, c_fast), w_fast_mid.shape, (in_fast, c_fast)],
        [q4, q5, q6, q7, q8],
        [slow_gx, fast_gx, fast_y],
    )
    slow_gx, fast_gx, fast_y = held
    grads = (
        g_fin.T,
        g_fmid,
        g_fout,
        gw_lat.reshape(w_lateral.shape),
        gw_in,
        gw_mid.reshape(w_slow_mid.shape),
        g_sout,
        g_short,
    )
    return (
        unview(slow_y),
        unview(fast_y),
        unview(slow_gx),
        unview(fast_gx),
        *grads,
        gains_grad.reshape(-1)[: gains.shape[0]],
        biases_grad.reshape(-1)[: biases.shape[0]],
    )


def solution(mesh):
    frames = P(("path", "frames"), None, None, None)
    in_specs = (frames, frames, P(AXES), P(AXES), *([P()] * 10), frames, frames)
    out_specs = (*([frames] * 4), *([P()] * 10))
    return jax.shard_map(per_device, mesh=mesh, in_specs=in_specs, out_specs=out_specs, check_vma=False)
```
